32 devices in a mesh: gx: 4 (over y, core), gy: 8 (over z, x).
Axes of the slice: x: 2, y: 2, z: 4, core: 2. Of those that a mesh axis runs over, the one named last changes fastest.
Arguments:
- initial: float32 [3, 24, 24, 384], P(None, 'gx', 'gy'), may hold values from -2.5 to 2.5
- forcing: float32 [3, 24, 24, 384], P(None, 'gx', 'gy'), may hold values from -600 to 600
- modulus: float32 [8, 8, 128], P('gx', 'gy'), may hold values from 0.5 to 2
- solid_list: int32 [4, 8, 192], P('gx', 'gy'), may hold values from 0 to 256, as said below
Outputs:
- displacement: float32 [3, 24, 24, 384], P(None, 'gx', 'gy')
- coarse_iterate: float32 [3, 8, 8, 128], P(None, 'gx', 'gy')
The draws below stay inside these ranges and needn't reach their ends.
Inputs may be any that keep to these rules, and one draw needn't show every extreme that they name: `solid_list`: each device's row lists distinct local element numbers below 256 first, then padding entries equal to 256; at least 64 entries of a row are live, and in every draw some device's row is live throughout.
All inputs are finite; a program needn't handle non-finite values.
Results may differ from the reference program's by a relative error of at most 0.0003.
Values sent between devices are 32-bit elements; how exact they have to be, the bound alone decides.
No kernel may reach another device: no remote copies, remote signals or barrier semaphores. Data moves between devices by JAX's collectives and lax.ppermute only.
A program may use at most 64 MiB of HBM per device.

```python
import math
import jax
import jax.numpy as jnp
import numpy as np
from jax import lax

EX = 2
EY = 1
EZ = 128
CHEB = 3
CAP = 192
ELEMENTS_ALONG_X = 8
ELEMENTS_ALONG_Y = 8
ELEMENTS_ALONG_Z = 128
NNX = 24
NNY = 24
NNZ = 384
N_GX = 4
N_GY = 8


def draw_solid_list(key, part):
    key = jax.random.fold_in(key, 7)
    count_key, pick_key, order_key = jax.random.split(key, 3)
    devices = N_GX * N_GY
    elements = EX * EY * EZ
    counts = jax.random.randint(count_key, (devices,), elements // 4, CAP + 1)
    busiest = jax.random.randint(pick_key, (), 0, devices)
    counts = jnp.where(jnp.arange(devices) == busiest, CAP, counts)
    device_keys = jax.random.split(order_key, devices)

    def shuffle(device_key):
        return jax.random.permutation(device_key, elements)
    orders = jax.vmap(shuffle)(device_keys)[:, :CAP]
    positions = jnp.arange(CAP)[None, :]
    listed = jnp.where(positions < counts[:, None], orders, elements)
    return listed.reshape(N_GX, N_GY, CAP).astype(jnp.int32)


def steps_of(key, dims, shards, low, high):
    loudness, own = 1.0, jax.random.fold_in(key, 6)
    for dim, shards_of in shards:
        draws = jnp.exp(jax.random.uniform(jax.random.fold_in(own, dim), (shards_of,), jnp.float32, low / len(shards), high / len(shards)))
        loudness = loudness * jnp.repeat(draws, dims[dim] // shards_of).reshape([-1 if axis == dim else 1 for axis in range(len(dims))])
    return loudness


def scatter_about(stream_key, shape, width, limit, shards=(), kind=jnp.bfloat16):
    gain = steps_of(stream_key, shape, shards, -0.22, 0.18) if shards else 1.0
    entries = jax.random.normal(stream_key, shape, jnp.float32) * width * gain
    return jnp.minimum(jnp.maximum(entries, -limit), limit).astype(kind)


def setup_inputs(seed: int = 0) -> dict:
    key_list = jax.random.split(jax.random.key(seed), 5)
    initial = scatter_about(key_list[0], (3, NNX, NNY, NNZ), 0.3, 2.5, ((1, 4), (2, 8)), jnp.float32)
    forcing = scatter_about(key_list[1], (3, NNX, NNY, NNZ), 100.0, 600.0, ((1, 4), (2, 8)), jnp.float32)
    modulus = jnp.clip(jnp.exp(math.log(2.0) - 1.3862944 * jax.random.uniform(key_list[2], (ELEMENTS_ALONG_X, ELEMENTS_ALONG_Y, ELEMENTS_ALONG_Z), jnp.float32) ** steps_of(key_list[2], (ELEMENTS_ALONG_X, ELEMENTS_ALONG_Y, ELEMENTS_ALONG_Z), ((0, 4), (1, 8)), -0.2, 0.2)), 0.5, 2.0)
    solid_list = draw_solid_list(jax.random.fold_in(key_list[4], 71), 0)
    return dict(initial=initial, forcing=forcing, modulus=modulus, solid_list=solid_list)


element_span = 20.0
lame_ratio = 4.0
rest_ratio = 1.25
modulus_top = 2.0
spectrum_floor = 0.05
interval_centre = (1.0 + spectrum_floor) / 2.0
interval_radius = (1.0 - spectrum_floor) / 2.0
interval_ratio = interval_centre / interval_radius
inner_anchors = (0.5 - 0.5 / math.sqrt(5.0), 0.5 + 0.5 / math.sqrt(5.0))

def gauss_rule(point_count):
    if point_count == 2:
        offset = 1.0 / math.sqrt(3.0)
        points = [-offset, offset]
        weights = [1.0, 1.0]
    else:
        inner = math.sqrt(3.0 / 7.0 - 2.0 / 7.0 * math.sqrt(6.0 / 5.0))
        outer = math.sqrt(3.0 / 7.0 + 2.0 / 7.0 * math.sqrt(6.0 / 5.0))
        heavy = (18.0 + math.sqrt(30.0)) / 36.0
        light = (18.0 - math.sqrt(30.0)) / 36.0
        points = [-outer, -inner, inner, outer]
        weights = [light, heavy, heavy, light]
    return (np.array(points), np.array(weights))

def lagrange_tables(anchors, samples):
    values = np.zeros((len(samples), len(anchors)))
    slopes = np.zeros((len(samples), len(anchors)))
    for sample_index, sample in enumerate(samples):
        for anchor_index, anchor in enumerate(anchors):
            others = [location for location_index, location in enumerate(anchors) if location_index != anchor_index]
            product = 1.0
            for location in others:
                product = product * (sample - location) / (anchor - location)
            values[sample_index, anchor_index] = product
            derivative = 0.0
            for skipped in range(len(others)):
                summand = 1.0 / (anchor - others[skipped])
                for kept_index in range(len(others)):
                    if kept_index != skipped:
                        summand = summand * (sample - others[kept_index]) / (anchor - others[kept_index])
                derivative = derivative + summand
            slopes[sample_index, anchor_index] = derivative
    return (values, slopes)

def outer_three(first, second, third):
    return first[:, None, None, :, None, None] * second[None, :, None, None, :, None] * third[None, None, :, None, None, :]

def build_tables(anchors, point_count):
    raw_points, raw_weights = gauss_rule(point_count)
    samples = (raw_points + 1.0) / 2.0
    weights = raw_weights / 2.0
    basis_values, slopes = lagrange_tables(anchors, samples)
    quad_total = point_count ** 3
    nodal_count = len(anchors) ** 3
    derivative_one = outer_three(slopes, basis_values, basis_values).reshape(quad_total, nodal_count)
    derivative_two = outer_three(basis_values, slopes, basis_values).reshape(quad_total, nodal_count)
    derivative_three = outer_three(basis_values, basis_values, slopes).reshape(quad_total, nodal_count)
    stacked = np.stack([derivative_one, derivative_two, derivative_three]) / element_span
    volume = (weights[:, None, None] * weights[None, :, None] * weights[None, None, :]).reshape(-1) * element_span ** 3
    forward = stacked.reshape(3 * quad_total, nodal_count)
    backward = (stacked * volume[None, :, None]).reshape(3 * quad_total, nodal_count).T
    weighted = stacked * volume[None, :, None]
    laplace = weighted[0].T @ stacked[0] + weighted[1].T @ stacked[1] + weighted[2].T @ stacked[2]
    matrix = np.zeros((nodal_count, 3, nodal_count, 3))
    for first in range(3):
        for second in range(3):
            block = weighted[second].T @ stacked[first] + (lame_ratio - 1.0) * (weighted[first].T @ stacked[second])
            if first == second:
                block = block + laplace
            matrix[:, first, :, second] = block
    matrix = matrix.reshape(3 * nodal_count, 3 * nodal_count)
    vector = 1.5 + np.cos(1.3 * np.arange(3 * nodal_count))
    for repeat in range(200):
        vector = matrix @ vector
        vector = vector / np.sqrt(vector @ vector)
    largest = vector @ (matrix @ vector)
    return (jnp.asarray(forward, jnp.float32), jnp.asarray(backward, jnp.float32), float(4.0 * modulus_top * 1.1 * largest))

def element_force(values_at_nodes, stiffness, tables):
    forward, backward = (tables[0], tables[1])
    count_nodes = values_at_nodes.shape[0]
    elements = values_at_nodes.shape[2]
    quad_points = forward.shape[0] // 3
    gradient = jnp.dot(forward, values_at_nodes.reshape(count_nodes, 3 * elements), precision=lax.Precision.HIGHEST)
    gradient = gradient.reshape(3, quad_points, 3, elements)
    deform = [[gradient[column, :, row_at, :] + (1.0 if row_at == column else 0.0) for column in range(3)] for row_at in range(3)]
    cofactors = [[deform[(row_at + 1) % 3][(column + 1) % 3] * deform[(row_at + 2) % 3][(column + 2) % 3] - deform[(row_at + 1) % 3][(column + 2) % 3] * deform[(row_at + 2) % 3][(column + 1) % 3] for column in range(3)] for row_at in range(3)]
    jacobian = deform[0][0] * cofactors[0][0] + deform[0][1] * cofactors[0][1] + deform[0][2] * cofactors[0][2]
    pressure = lame_ratio * (jacobian - rest_ratio)
    element_scale = stiffness[None, :]
    stress = jnp.stack([jnp.stack([element_scale * (deform[row_at][column] + pressure * cofactors[row_at][column]) for row_at in range(3)], 1) for column in range(3)], 0)
    element_loading = jnp.dot(backward, stress.reshape(3 * quad_points, 3 * elements), precision=lax.Precision.HIGHEST)
    return element_loading.reshape(count_nodes, 3, elements)

def same_layer(boundary):
    return boundary

def nothing(boundary):
    return jnp.zeros_like(boundary)

def split_nodes(values, axis_index, factor, neighbour):
    blocks = values.shape[axis_index] // factor
    gathered_groups = values.reshape(values.shape[:axis_index] + (blocks, factor) + values.shape[axis_index + 1:])
    above_layer = neighbour(lax.slice_in_dim(values, 0, 1, axis=axis_index))
    following = jnp.concatenate([lax.slice_in_dim(values, factor, blocks * factor, factor, axis_index), above_layer], axis_index)
    return jnp.concatenate([gathered_groups, jnp.expand_dims(following, axis_index + 1)], axis_index + 1)

def join_nodes(element_shares, axis_index, factor, neighbour):
    blocks = element_shares.shape[axis_index]
    closing = lax.index_in_dim(element_shares, factor, axis_index + 1, keepdims=False)
    outflow = lax.slice_in_dim(closing, blocks - 1, blocks, axis=axis_index)
    carried = jnp.concatenate([neighbour(outflow), lax.slice_in_dim(closing, 0, blocks - 1, axis=axis_index)], axis_index)
    leading = lax.index_in_dim(element_shares, 0, axis_index + 1, keepdims=False) + carried
    pieces = [leading] + [lax.index_in_dim(element_shares, other, axis_index + 1, keepdims=False) for other in range(1, factor)]
    stacked = jnp.stack(pieces, axis_index + 1)
    return stacked.reshape(element_shares.shape[:axis_index] + (blocks * factor,) + element_shares.shape[axis_index + 2:])

def restrict_dim(values, axis_index, neighbour):
    blocks = values.shape[axis_index] // 3
    gathered_groups = values.reshape(values.shape[:axis_index] + (blocks, 3) + values.shape[axis_index + 1:])
    node_zero = lax.index_in_dim(gathered_groups, 0, axis_index + 1, keepdims=False)
    node_one = lax.index_in_dim(gathered_groups, 1, axis_index + 1, keepdims=False)
    node_two = lax.index_in_dim(gathered_groups, 2, axis_index + 1, keepdims=False)
    staying = node_zero + (1.0 - inner_anchors[0]) * node_one + (1.0 - inner_anchors[1]) * node_two
    moving = inner_anchors[0] * node_one + inner_anchors[1] * node_two
    outflow = lax.slice_in_dim(moving, blocks - 1, blocks, axis=axis_index)
    carried = jnp.concatenate([neighbour(outflow), lax.slice_in_dim(moving, 0, blocks - 1, axis=axis_index)], axis_index)
    return staying + carried

def prolong_dim(values, axis_index, neighbour):
    blocks = values.shape[axis_index]
    above_layer = neighbour(lax.slice_in_dim(values, 0, 1, axis=axis_index))
    following = jnp.concatenate([lax.slice_in_dim(values, 1, blocks, axis=axis_index), above_layer], axis_index)
    pieces = [values, (1.0 - inner_anchors[0]) * values + inner_anchors[0] * following, (1.0 - inner_anchors[1]) * values + inner_anchors[1] * following]
    stacked = jnp.stack(pieces, axis_index + 1)
    return stacked.reshape(values.shape[:axis_index] + (blocks * 3,) + values.shape[axis_index + 1:])

def smooth(iterate, target, operator, keep_mask, upper_bound):
    scaled_residual = (target - operator(iterate)) * keep_mask / upper_bound
    ratio_now = 1.0 / interval_ratio
    update = scaled_residual / interval_centre
    for sweep_index in range(CHEB):
        iterate = iterate + update
        if sweep_index + 1 < CHEB:
            scaled_residual = (target - operator(iterate)) * keep_mask / upper_bound
            ratio_next = 1.0 / (2.0 * interval_ratio - ratio_now)
            update = ratio_next * ratio_now * update + 2.0 * ratio_next / interval_radius * scaled_residual
            ratio_now = ratio_next
    return iterate

def solid_mask(solid_list):
    per_device = EX * EY * EZ

    def mark_one(listing):
        return jnp.zeros((per_device + 1,), jnp.float32).at[listing].set(1.0)[:per_device]
    flagged_nodes = jax.vmap(mark_one)(solid_list.reshape(-1, CAP)).reshape(N_GX, N_GY, EX, EY, EZ)
    return flagged_nodes.transpose(0, 2, 1, 3, 4).reshape(ELEMENTS_ALONG_X, ELEMENTS_ALONG_Y, ELEMENTS_ALONG_Z)

def fine_force(values, stiffness, tables):
    padded = jnp.concatenate([values, jnp.zeros((3, 1, NNY, NNZ), values.dtype)], 1)

    def layer_force(position):
        node_rows = lax.dynamic_slice_in_dim(padded, 3 * position, 4, 1)
        gathered_groups = split_nodes(node_rows, 2, 3, same_layer)
        gathered_groups = split_nodes(gathered_groups, 4, 3, same_layer)
        values_at_nodes = gathered_groups.transpose(1, 3, 5, 0, 2, 4).reshape(64, 3, ELEMENTS_ALONG_Y * ELEMENTS_ALONG_Z)
        layer_stiffness = lax.dynamic_index_in_dim(stiffness, position, 0, keepdims=False).reshape(-1)
        element_loading = element_force(values_at_nodes, layer_stiffness, tables)
        element_shares = element_loading.reshape(4, 4, 4, 3, ELEMENTS_ALONG_Y, ELEMENTS_ALONG_Z).transpose(3, 0, 4, 1, 5, 2)
        element_shares = join_nodes(element_shares, 4, 3, same_layer)
        return join_nodes(element_shares, 2, 3, same_layer)
    layered = lax.map(layer_force, jnp.arange(ELEMENTS_ALONG_X, dtype=jnp.int32))
    return join_nodes(layered.transpose(1, 0, 2, 3, 4), 1, 3, nothing)

def coarse_force(values, stiffness, tables):
    gathered_groups = split_nodes(values, 1, 1, nothing)
    gathered_groups = split_nodes(gathered_groups, 3, 1, same_layer)
    gathered_groups = split_nodes(gathered_groups, 5, 1, same_layer)
    values_at_nodes = gathered_groups.transpose(2, 4, 6, 0, 1, 3, 5).reshape(8, 3, -1)
    element_loading = element_force(values_at_nodes, stiffness.reshape(-1), tables)
    element_shares = element_loading.reshape((2, 2, 2, 3) + stiffness.shape).transpose(3, 4, 0, 5, 1, 6, 2)
    element_shares = join_nodes(element_shares, 5, 1, same_layer)
    element_shares = join_nodes(element_shares, 3, 1, same_layer)
    return join_nodes(element_shares, 1, 1, nothing)

def reference(initial, forcing, modulus, solid_list):
    cubic_tables = build_tables([0.0, inner_anchors[0], inner_anchors[1], 1.0], 4)
    linear_tables = build_tables([0.0, 1.0], 2)
    stiffness = modulus * solid_mask(solid_list)
    keep_fine = (jnp.arange(NNX) > 0).astype(jnp.float32).reshape(1, NNX, 1, 1)
    keep_coarse = (jnp.arange(ELEMENTS_ALONG_X) > 0).astype(jnp.float32).reshape(1, ELEMENTS_ALONG_X, 1, 1)

    def fine_apply(values):
        return fine_force(values, stiffness, cubic_tables)

    def coarse_apply(values):
        return coarse_force(values, stiffness, linear_tables)
    iterate = smooth(initial * keep_fine, forcing, fine_apply, keep_fine, cubic_tables[2])
    residual = (forcing - fine_apply(iterate)) * keep_fine
    coarse_start = iterate[:, ::3, ::3, ::3]
    restricted = restrict_dim(residual, 3, same_layer)
    restricted = restrict_dim(restricted, 2, same_layer)
    restricted = restrict_dim(restricted, 1, nothing)
    coarse_target = restricted + coarse_apply(coarse_start)
    coarse_end = smooth(coarse_start, coarse_target, coarse_apply, keep_coarse, linear_tables[2])
    correction = prolong_dim(coarse_end - coarse_start, 1, nothing)
    correction = prolong_dim(correction, 2, same_layer)
    correction = prolong_dim(correction, 3, same_layer)
    iterate = iterate + correction
    iterate = smooth(iterate, forcing, fine_apply, keep_fine, cubic_tables[2])
    return (iterate, coarse_end)
```

```python
import math

import jax
import jax.numpy as jnp
import numpy as np
from jax import lax
from jax.experimental import pallas as pl
from jax.experimental.pallas import tpu as pltpu
from jax.sharding import PartitionSpec as P

CHEB = 3
EZ = 128

element_span = 20.0
lame_ratio = 4.0
rest_ratio = 1.25
modulus_top = 2.0
spectrum_floor = 0.05
interval_centre = (1.0 + spectrum_floor) / 2.0
interval_radius = (1.0 - spectrum_floor) / 2.0
interval_ratio = interval_centre / interval_radius
inner_anchors = (0.5 - 0.5 / math.sqrt(5.0), 0.5 + 0.5 / math.sqrt(5.0))

BEFORE = 10
PAIRS = 12
PAIR_SLOTS = 16
OWN = BEFORE // 2
FIELD_COLUMNS = 3 * PAIRS * 32

SLOTS = [
    (0, 0, 0), (1, 0, 0), (2, 0, 0), (0, 1, 0), (0, 2, 0), (0, 0, 1), (0, 0, 2), None,
    (0, 1, 1), (0, 1, 2), (0, 2, 1), (0, 2, 2), (1, 0, 1), (1, 0, 2), (2, 0, 1), (2, 0, 2),
    (1, 1, 0), (1, 2, 0), (2, 1, 0), (2, 2, 0), (1, 1, 1), (1, 1, 2), (1, 2, 1), (1, 2, 2),
    (2, 1, 1), (2, 1, 2), (2, 2, 1), (2, 2, 2), None, None, None, None,
]
STIFF_SLOT = 7
GROUPS = [
    ((0, 0, 0), 0), ((0, 0, 0), 1), ((0, 0, 0), 2), ((0, 0, 0), 3),
    ((1, 0, 0), 0), ((1, 0, 0), 1),
    ((0, 1, 0), 0), ((0, 1, 0), 1),
    ((0, 0, 1), 0), ((0, 0, 1), 2),
    ((1, 1, 0), 0), ((1, 0, 1), 0), ((0, 1, 1), 0), ((1, 1, 1), 0),
]
ROWS = 8 * len(GROUPS)
CORNERS = [(a, b, c) for a in range(2) for b in range(2) for c in range(2)]


def gauss_rule(point_count):
    if point_count == 2:
        offset = 1.0 / math.sqrt(3.0)
        points = [-offset, offset]
        weights = [1.0, 1.0]
    else:
        inner = math.sqrt(3.0 / 7.0 - 2.0 / 7.0 * math.sqrt(6.0 / 5.0))
        outer = math.sqrt(3.0 / 7.0 + 2.0 / 7.0 * math.sqrt(6.0 / 5.0))
        heavy = (18.0 + math.sqrt(30.0)) / 36.0
        light = (18.0 - math.sqrt(30.0)) / 36.0
        points = [-outer, -inner, inner, outer]
        weights = [light, heavy, heavy, light]
    return (np.array(points), np.array(weights))


def lagrange_tables(anchors, samples):
    values = np.zeros((len(samples), len(anchors)))
    slopes = np.zeros((len(samples), len(anchors)))
    for sample_index, sample in enumerate(samples):
        for anchor_index, anchor in enumerate(anchors):
            others = [
                location
                for location_index, location in enumerate(anchors)
                if location_index != anchor_index
            ]
            product = 1.0
            for location in others:
                product = product * (sample - location) / (anchor - location)
            values[sample_index, anchor_index] = product
            derivative = 0.0
            for skipped in range(len(others)):
                summand = 1.0 / (anchor - others[skipped])
                for kept_index in range(len(others)):
                    if kept_index != skipped:
                        summand = (
                            summand * (sample - others[kept_index]) / (anchor - others[kept_index])
                        )
                derivative = derivative + summand
            slopes[sample_index, anchor_index] = derivative
    return (values, slopes)


def outer_three(first, second, third):
    return (
        first[:, None, None, :, None, None]
        * second[None, :, None, None, :, None]
        * third[None, None, :, None, None, :]
    )


def build_tables(anchors, point_count):
    raw_points, raw_weights = gauss_rule(point_count)
    samples = (raw_points + 1.0) / 2.0
    weights = raw_weights / 2.0
    basis_values, slopes = lagrange_tables(anchors, samples)
    quad_total = point_count**3
    nodal_count = len(anchors) ** 3
    derivative_one = outer_three(slopes, basis_values, basis_values).reshape(
        quad_total, nodal_count
    )
    derivative_two = outer_three(basis_values, slopes, basis_values).reshape(
        quad_total, nodal_count
    )
    derivative_three = outer_three(basis_values, basis_values, slopes).reshape(
        quad_total, nodal_count
    )
    stacked = np.stack([derivative_one, derivative_two, derivative_three]) / element_span
    volume = (weights[:, None, None] * weights[None, :, None] * weights[None, None, :]).reshape(
        -1
    ) * element_span**3
    forward = stacked.reshape(3 * quad_total, nodal_count)
    backward = (stacked * volume[None, :, None]).reshape(3 * quad_total, nodal_count).T
    weighted = stacked * volume[None, :, None]
    laplace = weighted[0].T @ stacked[0] + weighted[1].T @ stacked[1] + weighted[2].T @ stacked[2]
    matrix = np.zeros((nodal_count, 3, nodal_count, 3))
    for first in range(3):
        for second in range(3):
            block = weighted[second].T @ stacked[first] + (lame_ratio - 1.0) * (
                weighted[first].T @ stacked[second]
            )
            if first == second:
                block = block + laplace
            matrix[:, first, :, second] = block
    matrix = matrix.reshape(3 * nodal_count, 3 * nodal_count)
    vector = 1.5 + np.cos(1.3 * np.arange(3 * nodal_count))
    for repeat in range(200):
        vector = matrix @ vector
        vector = vector / np.sqrt(vector @ vector)
    largest = vector @ (matrix @ vector)
    return (forward, backward, float(4.0 * modulus_top * 1.1 * largest))


def row_nodes():
    nodes = []
    for shift, group in GROUPS:
        for slot in SLOTS[8 * group : 8 * group + 8]:
            if slot is None or any(s and n for s, n in zip(shift, slot)):
                nodes.append(None)
            else:
                a, b, c = (3 * s + n for s, n in zip(shift, slot))
                nodes.append(16 * a + 4 * b + c)
    return nodes


def halves(matrix):
    whole = np.asarray(matrix, np.float32)
    high = whole.astype(jnp.bfloat16)
    low = (whole - high.astype(np.float32)).astype(jnp.bfloat16)
    return high, low


def element_tables():
    forward, backward, bound = build_tables([0.0, inner_anchors[0], inner_anchors[1], 1.0], 4)
    spread = np.zeros((forward.shape[0], ROWS))
    collect = np.zeros((ROWS, backward.shape[1]))
    for row, node in enumerate(row_nodes()):
        if node is not None:
            spread[:, row] = forward[:, node]
            collect[row, :] = backward[node, :]
    spread_high, spread_low = halves(spread)
    collect_high, collect_low = halves(collect)
    return (
        np.concatenate([spread_high, spread_high, spread_low], 1),
        np.concatenate([collect_high, collect_high, collect_low], 1),
        bound,
    )


def transfer_table():
    table = np.zeros((8, 32))
    reach = (0.0, inner_anchors[0], inner_anchors[1])
    for row, corner in enumerate(CORNERS):
        for column, slot in enumerate(SLOTS):
            if slot is not None:
                weight = 1.0
                for side, node in zip(corner, slot):
                    weight = weight * (reach[node] if side else 1.0 - reach[node])
                table[row, column] = weight
    return table.astype(np.float32)


def chebyshev_steps():
    steps = [(0.0, 1.0 / interval_centre)]
    ratio_now = 1.0 / interval_ratio
    for sweep in range(1, CHEB):
        ratio_next = 1.0 / (2.0 * interval_ratio - ratio_now)
        steps.append((ratio_next * ratio_now, 2.0 * ratio_next / interval_radius))
        ratio_now = ratio_next
    return steps


def stack_row(field, component, layer, b):
    return field * 54 + component * 18 + layer * 3 + b


def pack_table():
    table = np.zeros((3, 128, 2, 2, 3, 4, 32), np.float32)
    for field in range(2):
        for x in range(2):
            for component in range(3):
                for column, slot in enumerate(SLOTS):
                    if slot is not None:
                        a, b, c = slot
                        row = stack_row(field, component, 3 * x + a, b)
                        table[c, row, field, x, component, :, column] = 1.0
            table[0, 108 + x, 0, x, 0, :, STIFF_SLOT] = 1.0
    return table.reshape(384, 12 * 128).astype(jnp.bfloat16)


def unpack_table():
    table = np.zeros((2, 128, 3, 128), np.float32)
    for x in range(2):
        for component in range(3):
            for column, slot in enumerate(SLOTS):
                if slot is not None:
                    a, b, c = slot
                    row = stack_row(0, component, 3 * x + a, b)
                    table[x, component * 32 + column, c, row] = 1.0
            table[x, 96 + component, 0, 54 + 2 * component + x] = 1.0
    return table.reshape(256, 384).astype(jnp.bfloat16)


def exact_pick(values, table):
    high = values.astype(jnp.bfloat16)
    rest = values - high.astype(jnp.float32)
    middle = rest.astype(jnp.bfloat16)
    low = (rest - middle.astype(jnp.float32)).astype(jnp.bfloat16)
    parts = [
        jnp.dot(part, table, preferred_element_type=jnp.float32) for part in (high, middle, low)
    ]
    return parts[0] + (parts[1] + parts[2])


def pack_kernel(initial, forcing, modulus, listing, table, out, rows, turned, places):
    devices = out.shape[0]
    own_layers = EZ // devices
    rows[108:128, :] = jnp.zeros((20, 384), jnp.float32)
    for field, source in enumerate((initial, forcing)):
        for component in range(3):
            for layer in range(6):
                at = stack_row(field, component, layer, 0)
                rows[at : at + 3, :] = source[component, layer]
    for part in range(3):
        span = slice(128 * part, 128 * part + 128)
        turned[span, :] = rows[:, span].T
    listed = listing[0].astype(jnp.float32)
    listed = jnp.concatenate([listed, jnp.full((1, 64), 256.0, jnp.float32)], 1)
    listed = jnp.broadcast_to(listed, (128, 256)).T
    lanes = lax.broadcasted_iota(jnp.int32, (256, 128), 1).astype(jnp.float32)
    row_at = lax.broadcasted_iota(jnp.int32, (128, 128), 0)
    stiff = jnp.zeros((128, 128), jnp.float32)
    for x in range(2):
        hit = jnp.max(jnp.where(listed == lanes + 128.0 * x, 1.0, 0.0), axis=0, keepdims=True)
        stiff = jnp.where(row_at == 108 + x, hit * modulus[x], stiff)
    picked = [turned[pl.ds(c, 128, stride=3), :] for c in range(3)]
    picked[0] = picked[0] + stiff.T
    wide = exact_pick(jnp.concatenate(picked, 1), table[...])
    group = lax.broadcasted_iota(jnp.int32, (128, 128), 1) // 32
    for block in range(12):
        here = wide[:, 128 * block : 128 * block + 128]
        shifted = here
        for ahead in range(1, 4):
            shifted = jnp.where(group == ahead, pltpu.roll(here, 128 - 2 * ahead, 0), shifted)
        places[block, 16:144, :] = shifted
        places[block, 0:16, :] = shifted[112:128]
        places[block, 144:160, :] = shifted[0:16]
    for field in range(2):
        for x in range(2):
            for component in range(3):
                block = (field * 2 + x) * 3 + component
                for parity in range(2):
                    for chunk in range(PAIRS // 4):
                        first = 16 - BEFORE + 8 * chunk + parity
                        at = component * 32 * PAIRS + 128 * chunk
                        out[:, field * 4 + x * 2 + parity, at : at + 128] = places[
                            block, pl.ds(first, devices, stride=own_layers), :
                        ]


def unpack_kernel(arrived, table, out, coarse_out, layers, turned):
    devices = arrived.shape[0]
    own_layers = EZ // devices
    for x in range(2):
        for layer in range(own_layers):
            row = (layer // 2) * 4 + x * 2 + layer % 2
            layers[x, pl.ds(layer, devices, stride=own_layers), :] = arrived[:, row, :]
    wide = exact_pick(jnp.concatenate([layers[0], layers[1]], 1), table[...])
    for c in range(3):
        turned[pl.ds(c, 128, stride=3), :] = wide[:, 128 * c : 128 * c + 128]
    for part in range(3):
        span = slice(128 * part, 128 * part + 128)
        back = turned[span, :].T
        for component in range(3):
            for layer in range(6):
                at = stack_row(0, component, layer, 0)
                out[component, layer, :, span] = back[at : at + 3, :]
    back = wide[:, 0:128].T
    for component in range(3):
        for x in range(2):
            at = 54 + 2 * component + x
            coarse_out[component, x] = back[at : at + 1, :]


def cofactor_rows(deform):
    return [
        [
            deform[(row_at + 1) % 3][(column + 1) % 3] * deform[(row_at + 2) % 3][(column + 2) % 3]
            - deform[(row_at + 1) % 3][(column + 2) % 3]
            * deform[(row_at + 2) % 3][(column + 1) % 3]
            for column in range(3)
        ]
        for row_at in range(3)
    ]


def point_stress(deform, stiffness, stiffness_four):
    cofactors = cofactor_rows(deform)
    jacobian = (
        deform[0][0] * cofactors[0][0]
        + deform[0][1] * cofactors[0][1]
        + deform[0][2] * cofactors[0][2]
    )
    pressure = stiffness_four * (jacobian - rest_ratio)
    return [
        [stiffness * deform[i][d] + pressure * cofactors[i][d] for d in range(3)] for i in range(3)
    ]


def split_rows(values):
    high = values.astype(jnp.bfloat16)
    low = (values - high.astype(jnp.float32)).astype(jnp.bfloat16)
    return jnp.concatenate([high, low, high], 0)


def make_cycle_kernel(width, across, own_layers, fine_bound, coarse_bound):
    steps = chebyshev_steps()
    y_step = 2 * across

    def cycle_kernel(
        arrived, spread, collect, transfer, transfer_back, out, u, f, d, shares, raised
    ):
        def lane_of(rows):
            return lax.broadcasted_iota(jnp.int32, (rows, width), 1)

        def masks(rows):
            lane = lane_of(rows)
            x = (lane // 2) % across
            return x == 0, x == across - 1, lane % 2 == 0

        def next_x(v, top):
            return jnp.where(top, 0.0, pltpu.roll(v, width - 2, 1))

        def next_y(v):
            return pltpu.roll(v, width - y_step, 1)

        def onto_x(v, bottom):
            return jnp.where(bottom, 0.0, pltpu.roll(v, 2, 1))

        def onto_y(v):
            return pltpu.roll(v, y_step, 1)

        bottom8, top8, even8 = masks(8)
        bottom16, top16, even16 = masks(16)
        row32 = lax.broadcasted_iota(jnp.int32, (32, width), 0)
        on_face = (row32 == 0) | ((row32 >= 3) & (row32 <= 6)) | ((row32 >= 8) & (row32 <= 11))
        keep = jnp.where(on_face & masks(32)[0], 0.0, 1.0)

        u[:, PAIRS:, :, :] = jnp.zeros((3, PAIR_SLOTS - PAIRS, 32, width), jnp.float32)
        lower = lax.broadcasted_iota(jnp.int32, (width // 8, 8, 128), 1) < 4
        for component in range(3):
            for chunk in range(PAIRS // 4):
                at = component * 32 * PAIRS + 128 * chunk
                first = arrived[:, 0, :, at : at + 128]
                second = arrived[:, 1, :, at : at + 128]
                value = jnp.where(lower, first, pltpu.roll(second, 4, 1))
                load = jnp.where(lower, pltpu.roll(first, 4, 1), second)
                value = value.reshape(width, 128).T
                load = load.reshape(width, 128).T
                for q in range(4):
                    u[component, 4 * chunk + q] = value[32 * q : 32 * q + 32] * keep
                    f[component, 4 * chunk + q] = load[32 * q : 32 * q + 32]

        def gather(component, pair):
            here = u[component, pair]
            ahead = u[component, pair + 1]
            g0, g1, g2 = here[0:8], here[8:16], here[16:24]
            z0 = jnp.where(
                even8, pltpu.roll(g0, width - 1, 1), pltpu.roll(ahead[0:8], 1, 1)
            )
            z2 = jnp.where(
                even8, pltpu.roll(g2, width - 1, 1), pltpu.roll(ahead[16:24], 1, 1)
            )
            y0, y1 = next_y(g0), next_y(g1)
            yz = next_y(z0)
            return jnp.concatenate(
                [
                    here,
                    next_x(g0, top8),
                    next_x(g1, top8),
                    y0,
                    y1,
                    z0,
                    z2,
                    next_x(y0, top8),
                    next_x(z0, top8),
                    yz,
                    next_x(yz, top8),
                ],
                0,
            )

        def scatter(part, behind):
            g = [part[8 * n : 8 * n + 8] for n in range(len(GROUPS))]
            yz = g[12] + onto_x(g[13], bottom8)
            z0 = g[8] + onto_x(g[11], bottom8) + onto_y(yz)
            y0 = g[6] + onto_x(g[10], bottom8)
            z2 = g[9]
            own0 = g[0] + onto_x(g[4], bottom8) + onto_y(y0)
            own1 = g[1] + onto_x(g[5], bottom8) + onto_y(g[7])
            own0 = own0 + jnp.where(even8, behind[0], pltpu.roll(z0, 1, 1))
            own2 = g[2] + jnp.where(even8, behind[1], pltpu.roll(z2, 1, 1))
            moved = (pltpu.roll(z0, width - 1, 1), pltpu.roll(z2, width - 1, 1))
            return jnp.concatenate([own0, own1, own2, g[3]], 0), moved

        def apply(first, count, finish):
            def step(index, carry):
                pair = first + 2 * index
                blocks = [gather(i, pair + q) for i in range(3) for q in range(2)]
                gradient = jnp.dot(
                    spread[...],
                    split_rows(jnp.concatenate(blocks, 1)),
                    preferred_element_type=jnp.float32,
                )
                stiffness = jnp.concatenate(
                    [u[0, pair + q, STIFF_SLOT : STIFF_SLOT + 1, :] for q in range(2)], 1
                )
                deform = [
                    [
                        gradient[64 * e : 64 * e + 64, 2 * width * i : 2 * width * (i + 1)]
                        + (1.0 if i == e else 0.0)
                        for e in range(3)
                    ]
                    for i in range(3)
                ]
                stress = point_stress(deform, stiffness, lame_ratio * stiffness)
                stress = jnp.concatenate(
                    [jnp.concatenate([stress[i][e] for i in range(3)], 1) for e in range(3)], 0
                )
                force = jnp.dot(
                    collect[...], split_rows(stress), preferred_element_type=jnp.float32
                )
                carry = list(carry)
                totals = [[], []]
                for q in range(2):
                    for i in range(3):
                        at = (2 * i + q) * width
                        total, carry[i] = scatter(force[:, at : at + width], carry[i])
                        totals[q].append(total)
                for q in range(2):
                    finish(pair + q, totals[q])
                return tuple(carry)

            none = jnp.zeros((8, width), jnp.float32)
            lax.fori_loop(0, (count + 1) // 2, step, tuple((none, none) for i in range(3)))

        def smooth(starts):
            for (first, count), (held, added) in zip(starts, steps):

                def finish(pair, forces, held=held, added=added):
                    for i in range(3):
                        z = (added / fine_bound) * keep * (f[i, pair] - forces[i])
                        move = held * d[i, pair] + z if held else z
                        d[i, pair] = move
                        u[i, pair] = u[i, pair] + move

                apply(first, count, finish)

        reach = [BEFORE - 9, BEFORE - 8, BEFORE - 7, BEFORE - 6, BEFORE - 3, BEFORE - 2, BEFORE - 1]
        ends = [BEFORE + own_layers + n for n in (8, 7, 6, 5, 2, 1, 0)]
        spans = [(lo // 2, (hi + 1) // 2 - lo // 2) for lo, hi in zip(reach, ends)]

        smooth(spans[0:3])

        shares[...] = jnp.zeros(shares.shape, jnp.float32)

        def restrict(pair, forces):
            rest = jnp.concatenate([keep * (f[i, pair] - forces[i]) for i in range(3)], 1)
            corner = jnp.dot(
                transfer[...],
                rest,
                preferred_element_type=jnp.float32,
                precision=lax.Precision.HIGHEST,
            )
            for i in range(3):
                shares[i, pair] = corner[:, width * i : width * (i + 1)]

        apply(spans[3][0], spans[3][1], restrict)

        def next_z(v):
            return jnp.where(
                even16,
                pltpu.roll(v, width - 1, 1),
                pltpu.roll(pltpu.roll(v, 1, 1), PAIR_SLOTS - 1, 0),
            )

        def onto_z(v):
            return jnp.where(
                even16, pltpu.roll(pltpu.roll(v, width - 1, 1), 1, 0), pltpu.roll(v, 1, 1)
            )

        def corners_of(v):
            found = {}
            found[0, 0, 0] = v
            found[0, 0, 1] = next_z(v)
            for c in range(2):
                found[0, 1, c] = next_y(found[0, 0, c])
            for b in range(2):
                for c in range(2):
                    found[1, b, c] = next_x(found[0, b, c], top16)
            return found

        def assemble(part):
            line = {
                (a, b): part[a, b, 0] + onto_z(part[a, b, 1]) for a in range(2) for b in range(2)
            }
            face = [line[a, 0] + onto_y(line[a, 1]) for a in range(2)]
            return face[0] + onto_x(face[1], bottom16)

        samples = [0.5 - 0.5 / math.sqrt(3.0), 0.5 + 0.5 / math.sqrt(3.0)]
        two = range(2)

        def at_points(low, high):
            change = high - low
            return [low + s * change for s in samples], change * (1.0 / element_span)

        def coarse_force(values, stiffness):
            grads = []
            for i in range(3):
                v = corners_of(values[i])
                vz, sz = {}, {}
                for a in two:
                    for b in two:
                        vz[a, b], sz[a, b] = at_points(v[a, b, 0], v[a, b, 1])
                vv, vs, sv = {}, {}, {}
                for a in two:
                    for k in two:
                        vv[a, k], vs[a, k] = at_points(vz[a, 0][k], vz[a, 1][k])
                    sv[a], unused = at_points(sz[a, 0], sz[a, 1])
                dx, dy, dz = {}, {}, {}
                for k in two:
                    for j in two:
                        dx[j, k] = (vv[1, k][j] - vv[0, k][j]) * (1.0 / element_span)
                    line, unused = at_points(vs[0, k], vs[1, k])
                    for h in two:
                        dy[h, k] = line[h]
                for j in two:
                    line, unused = at_points(sv[0][j], sv[1][j])
                    for h in two:
                        dz[h, j] = line[h]
                grads.append((dx, dy, dz))
            weight = element_span**2 / 8.0
            scaled = weight * stiffness
            scaled_four = lame_ratio * scaled
            sums = [({}, {}, {}) for i in range(3)]

            def add(table, key, value):
                table[key] = table[key] + value if key in table else value

            for h in two:
                for j in two:
                    for k in two:
                        deform = [
                            [grads[i][0][j, k], grads[i][1][h, k], grads[i][2][h, j]]
                            for i in range(3)
                        ]
                        for i in range(3):
                            deform[i][i] = deform[i][i] + 1.0
                        stress = point_stress(deform, scaled, scaled_four)
                        for i in range(3):
                            add(sums[i][0], (j, k), stress[i][0])
                            add(sums[i][1], (h, k), stress[i][1])
                            add(sums[i][2], (h, j), stress[i][2])

            def ends_of(first, second):
                high = samples[0] * first + samples[1] * second
                return [first + second - high, high]

            forces = []
            for i in range(3):
                part = {}
                qx, qy, qz = sums[i]
                along_z = [ends_of(qx[j, 0], qx[j, 1]) for j in two]
                for c in two:
                    line = ends_of(along_z[0][c], along_z[1][c])
                    for b in two:
                        part[0, b, c] = -line[b]
                        part[1, b, c] = line[b]
                along_z = [ends_of(qy[h, 0], qy[h, 1]) for h in two]
                for c in two:
                    line = ends_of(along_z[0][c], along_z[1][c])
                    for a in two:
                        part[a, 0, c] = part[a, 0, c] - line[a]
                        part[a, 1, c] = part[a, 1, c] + line[a]
                along_y = [ends_of(qz[h, 0], qz[h, 1]) for h in two]
                for b in two:
                    line = ends_of(along_y[0][b], along_y[1][b])
                    for a in two:
                        part[a, b, 0] = part[a, b, 0] - line[a]
                        part[a, b, 1] = part[a, b, 1] + line[a]
                forces.append(assemble(part))
            return forces

        stiffness = u[0, :, STIFF_SLOT, :]
        keep_coarse = jnp.where(bottom16, 0.0, 1.0)
        start = [u[i, :, 0, :] for i in range(3)]
        restricted = [
            assemble({corner: shares[i, :, n, :] for n, corner in enumerate(CORNERS)})
            for i in range(3)
        ]
        before = coarse_force(start, stiffness)
        move = [(steps[0][1] / coarse_bound) * keep_coarse * restricted[i] for i in range(3)]
        level = [start[i] + move[i] for i in range(3)]
        for held, added in steps[1:]:
            force = coarse_force(level, stiffness)
            for i in range(3):
                z = keep_coarse * (restricted[i] + before[i] - force[i])
                move[i] = held * move[i] + (added / coarse_bound) * z
                level[i] = level[i] + move[i]

        for i in range(3):
            change = corners_of(level[i] - start[i])
            for n, corner in enumerate(CORNERS):
                raised[i, :, n, :] = change[corner]
        for pair in range(spans[4][0], spans[4][0] + spans[4][1] + 2):
            lift = jnp.dot(
                transfer_back[...],
                jnp.concatenate([raised[i, pair] for i in range(3)], 1),
                preferred_element_type=jnp.float32,
                precision=lax.Precision.HIGHEST,
            )
            for i in range(3):
                u[i, pair] = u[i, pair] + lift[:, width * i : width * (i + 1)]

        smooth(spans[4:7])

        sides = []
        blank = jnp.zeros((29, width), jnp.float32)
        for q in range(2):
            ends_here = jnp.concatenate(
                [u[i, OWN + q] for i in range(3)]
                + [level[i][OWN + q : OWN + q + 1] for i in range(3)]
                + [blank],
                0,
            )
            sides.append(ends_here.T.reshape(width // 8, 8, 128))
        out[:, 0] = jnp.where(lower, sides[0], pltpu.roll(sides[1], 4, 1))
        out[:, 1] = jnp.where(lower, pltpu.roll(sides[0], 4, 1), sides[1])

    return cycle_kernel


def solution(mesh):
    rows_of, columns_of = mesh.shape["gx"], mesh.shape["gy"]
    devices = rows_of * columns_of
    own_layers = EZ // devices
    width = 4 * devices
    spread, collect, fine_bound = element_tables()
    coarse_bound = build_tables([0.0, 1.0], 2)[2]
    transfer = transfer_table()
    limit = pltpu.CompilerParams(vmem_limit_bytes=48 * 1024 * 1024)
    f32 = jnp.float32

    pack = pl.pallas_call(
        pack_kernel,
        out_shape=jax.ShapeDtypeStruct((devices, 8, FIELD_COLUMNS), f32),
        scratch_shapes=[
            pltpu.VMEM((128, 384), f32),
            pltpu.VMEM((384, 128), f32),
            pltpu.VMEM((12, 160, 128), f32),
        ],
        compiler_params=limit,
    )
    cycle = pl.pallas_call(
        make_cycle_kernel(width, 2 * rows_of, own_layers, fine_bound, coarse_bound),
        out_shape=jax.ShapeDtypeStruct((devices // 2, 2, 8, 128), f32),
        scratch_shapes=[
            pltpu.VMEM((3, PAIR_SLOTS, 32, width), f32),
            pltpu.VMEM((3, PAIR_SLOTS, 32, width), f32),
            pltpu.VMEM((3, PAIR_SLOTS, 32, width), f32),
            pltpu.VMEM((3, PAIR_SLOTS, 8, width), f32),
            pltpu.VMEM((3, PAIR_SLOTS, 8, width), f32),
        ],
        compiler_params=limit,
    )
    unpack = pl.pallas_call(
        unpack_kernel,
        out_shape=(
            jax.ShapeDtypeStruct((3, 6, 3, 384), f32),
            jax.ShapeDtypeStruct((3, 2, 1, EZ), f32),
        ),
        scratch_shapes=[pltpu.VMEM((2, 128, 128), f32), pltpu.VMEM((384, 128), f32)],
        compiler_params=limit,
    )
    everyone = ("gy", "gx")

    def body(initial, forcing, modulus, solid_list):
        sent = pack(initial, forcing, modulus, solid_list, jnp.asarray(pack_table()))
        arrived = lax.all_to_all(sent, everyone, 0, 0, tiled=True)
        result = cycle(
            arrived.reshape(devices // 2, 2, 8, FIELD_COLUMNS),
            jnp.asarray(spread),
            jnp.asarray(collect),
            jnp.asarray(transfer),
            jnp.asarray(transfer.T.copy()),
        )
        back = lax.all_to_all(result.reshape(devices, 8, 128), everyone, 0, 0, tiled=True)
        return unpack(back, jnp.asarray(unpack_table()))

    placed = (
        P(None, "gx", "gy", None),
        P(None, "gx", "gy", None),
        P("gx", "gy", None),
        P("gx", "gy", None),
    )
    return jax.shard_map(
        body,
        mesh=mesh,
        in_specs=placed,
        out_specs=(P(None, "gx", "gy", None), P(None, "gx", "gy", None)),
        check_vma=False,
    )
```

```python
import math

import jax
import jax.numpy as jnp
import numpy as np
from jax import lax
from jax.experimental import pallas as pl
from jax.experimental.pallas import tpu as pltpu
from jax.sharding import PartitionSpec as P

CHEB = 3
EZ = 128

element_span = 20.0
lame_ratio = 4.0
rest_ratio = 1.25
modulus_top = 2.0
spectrum_floor = 0.05
interval_centre = (1.0 + spectrum_floor) / 2.0
interval_radius = (1.0 - spectrum_floor) / 2.0
interval_ratio = interval_centre / interval_radius
inner_anchors = (0.5 - 0.5 / math.sqrt(5.0), 0.5 + 0.5 / math.sqrt(5.0))

BEFORE = 4
PAIRS = 6
BEFORE_B = 6
PAIRS_B = 8
BLOCK = 84
SENT = 512

SLOTS = [
    (0, 0, 0), (1, 0, 0), (2, 0, 0), (0, 1, 0), (0, 2, 0), (0, 0, 1), (0, 0, 2), None,
    (0, 1, 1), (0, 1, 2), (0, 2, 1), (0, 2, 2), (1, 0, 1), (1, 0, 2), (2, 0, 1), (2, 0, 2),
    (1, 1, 0), (1, 2, 0), (2, 1, 0), (2, 2, 0), (1, 1, 1), (1, 1, 2), (1, 2, 1), (1, 2, 2),
    None, None, None, None, (2, 1, 1), (2, 1, 2), (2, 2, 1), (2, 2, 2),
]
TWIN = 7
RESTRICTED_SLOT = 24
STIFF_SLOT = 25
OWN_SHIFT, SHIFT_X, SHIFT_Y, SHIFT_Z = (0, 0, 0), (1, 0, 0), (0, 1, 0), (0, 0, 1)
ELEMENT_ROWS = (
    [(slot, OWN_SHIFT) for slot in range(24)]
    + [(slot, SHIFT_Z) for slot in range(16, 20)]
    + [(slot, OWN_SHIFT) for slot in range(28, 32)]
    + [(slot, SHIFT_X) for slot in range(7)] + [None]
    + [(slot, SHIFT_Y) for slot in range(7)] + [(0, (0, 1, 1))]
    + [(slot, SHIFT_Z) for slot in range(7)] + [(0, (1, 0, 1))]
    + [(slot, SHIFT_X) for slot in range(8, 12)] + [(slot, SHIFT_Y) for slot in range(12, 16)]
    + [(0, (1, 1, 1)), (1, (0, 1, 1)), (2, (0, 1, 1)), (3, (1, 0, 1)), (4, (1, 0, 1))]
    + [(5, (1, 1, 0)), (6, (1, 1, 0)), (0, (1, 1, 0))]
)
ROWS = len(ELEMENT_ROWS)
DEPTH = 80
CORNERS = [(a, b, c) for a in range(2) for b in range(2) for c in range(2)]


def gauss_rule(point_count):
    if point_count == 2:
        offset = 1.0 / math.sqrt(3.0)
        points = [-offset, offset]
        weights = [1.0, 1.0]
    else:
        inner = math.sqrt(3.0 / 7.0 - 2.0 / 7.0 * math.sqrt(6.0 / 5.0))
        outer = math.sqrt(3.0 / 7.0 + 2.0 / 7.0 * math.sqrt(6.0 / 5.0))
        heavy = (18.0 + math.sqrt(30.0)) / 36.0
        light = (18.0 - math.sqrt(30.0)) / 36.0
        points = [-outer, -inner, inner, outer]
        weights = [light, heavy, heavy, light]
    return (np.array(points), np.array(weights))


def lagrange_tables(anchors, samples):
    values = np.zeros((len(samples), len(anchors)))
    slopes = np.zeros((len(samples), len(anchors)))
    for sample_index, sample in enumerate(samples):
        for anchor_index, anchor in enumerate(anchors):
            others = [
                location
                for location_index, location in enumerate(anchors)
                if location_index != anchor_index
            ]
            product = 1.0
            for location in others:
                product = product * (sample - location) / (anchor - location)
            values[sample_index, anchor_index] = product
            derivative = 0.0
            for skipped in range(len(others)):
                summand = 1.0 / (anchor - others[skipped])
                for kept_index in range(len(others)):
                    if kept_index != skipped:
                        summand = (
                            summand * (sample - others[kept_index]) / (anchor - others[kept_index])
                        )
                derivative = derivative + summand
            slopes[sample_index, anchor_index] = derivative
    return (values, slopes)


def outer_three(first, second, third):
    return (
        first[:, None, None, :, None, None]
        * second[None, :, None, None, :, None]
        * third[None, None, :, None, None, :]
    )


def build_tables(anchors, point_count):
    raw_points, raw_weights = gauss_rule(point_count)
    samples = (raw_points + 1.0) / 2.0
    weights = raw_weights / 2.0
    basis_values, slopes = lagrange_tables(anchors, samples)
    quad_total = point_count**3
    nodal_count = len(anchors) ** 3
    derivative_one = outer_three(slopes, basis_values, basis_values).reshape(
        quad_total, nodal_count
    )
    derivative_two = outer_three(basis_values, slopes, basis_values).reshape(
        quad_total, nodal_count
    )
    derivative_three = outer_three(basis_values, basis_values, slopes).reshape(
        quad_total, nodal_count
    )
    stacked = np.stack([derivative_one, derivative_two, derivative_three]) / element_span
    volume = (weights[:, None, None] * weights[None, :, None] * weights[None, None, :]).reshape(
        -1
    ) * element_span**3
    forward = stacked.reshape(3 * quad_total, nodal_count)
    backward = (stacked * volume[None, :, None]).reshape(3 * quad_total, nodal_count).T
    weighted = stacked * volume[None, :, None]
    laplace = weighted[0].T @ stacked[0] + weighted[1].T @ stacked[1] + weighted[2].T @ stacked[2]
    matrix = np.zeros((nodal_count, 3, nodal_count, 3))
    for first in range(3):
        for second in range(3):
            block = weighted[second].T @ stacked[first] + (lame_ratio - 1.0) * (
                weighted[first].T @ stacked[second]
            )
            if first == second:
                block = block + laplace
            matrix[:, first, :, second] = block
    matrix = matrix.reshape(3 * nodal_count, 3 * nodal_count)
    vector = 1.5 + np.cos(1.3 * np.arange(3 * nodal_count))
    for repeat in range(200):
        vector = matrix @ vector
        vector = vector / np.sqrt(vector @ vector)
    largest = vector @ (matrix @ vector)
    return (forward, backward, float(4.0 * modulus_top * 1.1 * largest))


def row_nodes():
    nodes = []
    for entry in ELEMENT_ROWS:
        slot = SLOTS[entry[0]] if entry else None
        if slot is None or any(s and n for s, n in zip(entry[1], slot)):
            nodes.append(None)
        else:
            a, b, c = (3 * s + n for s, n in zip(entry[1], slot))
            nodes.append(16 * a + 4 * b + c)
    return nodes


def halves(matrix):
    whole = np.asarray(matrix, np.float32)
    high = whole.astype(jnp.bfloat16)
    low = (whole - high.astype(np.float32)).astype(jnp.bfloat16)
    return high, low


def element_tables():
    forward, backward, bound = build_tables([0.0, inner_anchors[0], inner_anchors[1], 1.0], 4)
    spread = np.zeros((forward.shape[0], DEPTH))
    collect = np.zeros((ROWS, backward.shape[1]))
    for row, node in enumerate(row_nodes()):
        if node is not None:
            spread[:, row] = forward[:, node]
            collect[row, :] = backward[node, :]
    spread_high, spread_low = halves(spread)
    collect_high, collect_low = halves(collect)
    return (
        np.concatenate([spread_high, spread_high, spread_low], 1),
        np.concatenate([collect_high, collect_low], 0),
        bound,
    )


def transfer_table():
    table = np.zeros((8, 32))
    reach = (0.0, inner_anchors[0], inner_anchors[1])
    for row, corner in enumerate(CORNERS):
        for column, slot in enumerate(SLOTS):
            if slot is not None:
                weight = 1.0
                for side, node in zip(corner, slot):
                    weight = weight * (reach[node] if side else 1.0 - reach[node])
                table[row, column] = weight
    back = table.T.copy()
    back[TWIN] = back[0]
    return table.astype(np.float32), back.astype(np.float32)


def chebyshev_steps():
    steps = [(0.0, 1.0 / interval_centre)]
    ratio_now = 1.0 / interval_ratio
    for sweep in range(1, CHEB):
        ratio_next = 1.0 / (2.0 * interval_ratio - ratio_now)
        steps.append((ratio_next * ratio_now, 2.0 * ratio_next / interval_radius))
        ratio_now = ratio_next
    return steps


def stack_row(field, component, layer, b):
    return field * 54 + component * 18 + layer * 3 + b


def block_column(component, slot):
    return 72 + 4 * component + slot - 28 if slot >= 24 else 24 * component + slot


def pack_table():
    table = np.zeros((3, 128, 2, 2, 128), np.float32)
    for field in range(2):
        for x in range(2):
            for component in range(3):
                for column, slot in enumerate(SLOTS):
                    if slot is not None:
                        a, b, c = slot
                        row = stack_row(field, component, 3 * x + a, b)
                        table[c, row, field, x, block_column(component, column)] = 1.0
            table[0, 108 + x, 0, x, TWIN] = 1.0
    return table.reshape(384, 512).astype(jnp.bfloat16)


def unpack_table():
    table = np.zeros((2, 128, 3, 128), np.float32)
    for x in range(2):
        for component in range(3):
            for column, slot in enumerate(SLOTS):
                if slot is not None:
                    a, b, c = slot
                    row = stack_row(0, component, 3 * x + a, b)
                    table[x, component * 32 + column, c, row] = 1.0
            table[x, 96 + component, 0, 54 + 2 * component + x] = 1.0
    return table.reshape(256, 384).astype(jnp.bfloat16)


def exact_pick(values, table):
    high = values.astype(jnp.bfloat16)
    rest = values - high.astype(jnp.float32)
    middle = rest.astype(jnp.bfloat16)
    low = (rest - middle.astype(jnp.float32)).astype(jnp.bfloat16)
    count = values.shape[0]
    parts = jnp.dot(
        jnp.concatenate([high, middle, low], 0), table, preferred_element_type=jnp.float32
    )
    return parts[:count] + (parts[count : 2 * count] + parts[2 * count :])


def pack_kernel(
    initial_at, forcing_at, modulus_at, listing_at, table_at, out,
    initial, forcing, modulus, listing, table, rows, turned, places, ready,
):
    devices = out.shape[0]
    own_layers = EZ // devices
    sources = (listing_at, modulus_at, initial_at, forcing_at, table_at)
    copies = [
        pltpu.make_async_copy(source, here, ready.at[n])
        for n, (source, here) in enumerate(
            zip(sources, (listing, modulus, initial, forcing, table))
        )
    ]
    for copy in copies:
        copy.start()
    rows[108:128, :] = jnp.zeros((20, 384), jnp.float32)
    copies[0].wait()
    copies[1].wait()
    listed = listing[0].astype(jnp.float32)
    listed = jnp.concatenate([listed, jnp.full((1, 64), 256.0, jnp.float32)], 1)
    listed = jnp.broadcast_to(listed, (128, 256)).T
    lanes = lax.broadcasted_iota(jnp.int32, (256, 128), 1).astype(jnp.float32)
    row_at = lax.broadcasted_iota(jnp.int32, (128, 128), 0)
    stiff = jnp.zeros((128, 128), jnp.float32)
    for x in range(2):
        hit = jnp.max(jnp.where(listed == lanes + 128.0 * x, 1.0, 0.0), axis=0, keepdims=True)
        stiff = jnp.where(row_at == 108 + x, hit * modulus[x], stiff)
    copies[2].wait()
    copies[3].wait()
    for field, source in enumerate((initial, forcing)):
        for component in range(3):
            for layer in range(6):
                at = stack_row(field, component, layer, 0)
                rows[at : at + 3, :] = source[component, layer]
    for part in range(3):
        span = slice(128 * part, 128 * part + 128)
        turned[span, :] = rows[:, span].T
    picked = [turned[pl.ds(c, 128, stride=3), :] for c in range(3)]
    picked[0] = picked[0] + stiff.T
    copies[4].wait()
    wide = exact_pick(jnp.concatenate(picked, 1), table[...])
    lane = lax.broadcasted_iota(jnp.int32, (128, 128), 1)
    for block in range(4):
        here = wide[:, 128 * block : 128 * block + 128]
        tiles = [None] * (SENT // 128)
        for pair in range(PAIRS):
            first = BLOCK * pair
            moved = here if pair == 0 else pltpu.roll(here, 128 - 2 * pair, 0)
            if first % 128:
                moved = pltpu.roll(moved, first % 128, 1)
            for tile in range(first // 128, (first + BLOCK - 1) // 128 + 1):
                before = tiles[tile]
                if before is None:
                    tiles[tile] = moved
                else:
                    tiles[tile] = jnp.where(lane >= first - 128 * tile, moved, before)
        for tile in range(SENT // 128):
            at = 4 * block + tile
            places[at, 16:144, :] = tiles[tile]
            places[at, 0:16, :] = tiles[tile][112:128]
            places[at, 144:160, :] = tiles[tile][0:16]
    for block in range(4):
        for parity in range(2):
            for tile in range(SENT // 128):
                out[:, 2 * block + parity, 128 * tile : 128 * tile + 128] = places[
                    4 * block + tile, pl.ds(16 - BEFORE + parity, devices, stride=own_layers), :
                ]


def unpack_kernel(arrived, table, out, coarse_out, layers, turned):
    devices = arrived.shape[0]
    own_layers = EZ // devices
    for x in range(2):
        for layer in range(own_layers):
            row = (layer // 2) * 4 + x * 2 + layer % 2
            layers[x, pl.ds(layer, devices, stride=own_layers), :] = arrived[:, row, :]
    wide = exact_pick(jnp.concatenate([layers[0], layers[1]], 1), table[...])
    for c in range(3):
        turned[pl.ds(c, 128, stride=3), :] = wide[:, 128 * c : 128 * c + 128]
    for part in range(3):
        span = slice(128 * part, 128 * part + 128)
        back = turned[span, :].T
        for component in range(3):
            for layer in range(6):
                at = stack_row(0, component, layer, 0)
                out[component, layer, :, span] = back[at : at + 3, :]
    back = wide[:, 0:128].T
    for component in range(3):
        for x in range(2):
            at = 54 + 2 * component + x
            coarse_out[component, x] = back[at : at + 1, :]


def cofactor_rows(deform):
    return [
        [
            deform[(row_at + 1) % 3][(column + 1) % 3] * deform[(row_at + 2) % 3][(column + 2) % 3]
            - deform[(row_at + 1) % 3][(column + 2) % 3]
            * deform[(row_at + 2) % 3][(column + 1) % 3]
            for column in range(3)
        ]
        for row_at in range(3)
    ]


def point_stress(deform, stiffness, stiffness_four):
    cofactors = cofactor_rows(deform)
    jacobian = (
        deform[0][0] * cofactors[0][0]
        + deform[0][1] * cofactors[0][1]
        + deform[0][2] * cofactors[0][2]
    )
    pressure = stiffness_four * (jacobian - rest_ratio)
    return [
        [stiffness * deform[i][d] + pressure * cofactors[i][d] for d in range(3)] for i in range(3)
    ]


coarse_samples = [0.5 - 0.5 / math.sqrt(3.0), 0.5 + 0.5 / math.sqrt(3.0)]
two = range(2)


def at_points(low, high):
    change = high - low
    return [low + s * change for s in coarse_samples], change * (1.0 / element_span)


def ends_of(first, second):
    high = coarse_samples[0] * first + coarse_samples[1] * second
    return [first + second - high, high]


def high_low(values):
    high = values.astype(jnp.bfloat16)
    return high, (values - high.astype(jnp.float32)).astype(jnp.bfloat16)


class Slab:
    def __init__(self, width, across):
        self.width = width
        self.y_step = 2 * across
        lane = lax.broadcasted_iota(jnp.int32, (8, width), 1)
        x = (lane // 2) % across
        self.bottom, self.top, self.even = x == 0, x == across - 1, lane % 2 == 0
        self.row = lax.broadcasted_iota(jnp.int32, (8, width), 0)
        row = lax.broadcasted_iota(jnp.int32, (32, width), 0)
        lane = lax.broadcasted_iota(jnp.int32, (32, width), 1)
        on_face = (row == 0) | ((row >= 3) & (row <= 11))
        self.keep = jnp.where(on_face & ((lane // 2) % across == 0), 0.0, 1.0)

    def lanes(self, v, step):
        return pltpu.roll(v, step % self.width, 1)

    def next_x(self, v):
        return jnp.where(self.top, 0.0, self.lanes(v, -2))

    def next_y(self, v):
        return self.lanes(v, -self.y_step)

    def next_z(self, v, ahead):
        return jnp.where(self.even, self.lanes(v, -1), self.lanes(ahead, 1))

    def onto_x(self, v):
        return jnp.where(self.bottom, 0.0, self.lanes(v, 2))

    def onto_y(self, v):
        return self.lanes(v, self.y_step)

    def gather(self, here, ahead):
        row = self.row
        g0, g1, g2, g3 = here[0:8], here[8:16], here[16:24], here[24:32]
        z0 = self.next_z(g0, ahead[0:8])
        z2 = self.next_z(g2, ahead[16:24])
        y0 = self.next_y(g0)
        yz, xz, xy = self.next_y(z0), self.next_x(z0), self.next_x(y0)
        edges = jnp.where(row <= 2, yz, jnp.where(row <= 4, xz, xy))
        return jnp.concatenate(
            [
                g0,
                g1,
                g2,
                jnp.where(row < 4, z2, g3),
                self.next_x(g0),
                jnp.where(row == 7, yz, y0),
                jnp.where(row == 7, xz, z0),
                jnp.where(row < 4, self.next_x(g1), self.next_y(g1)),
                jnp.where(row == 0, self.next_x(yz), edges),
                jnp.zeros_like(g0),
            ],
            0,
        )

    def scatter(self, part, behind):
        row = self.row
        g0, g1, g2, g3, x0, y0, z0, sides, edges = (part[8 * n : 8 * n + 8] for n in range(9))
        edges_x = self.onto_x(edges)
        yz = jnp.where(row == 0, edges_x, jnp.where(row == 7, y0, edges))
        yz = jnp.where((row <= 2) | (row == 7), yz, 0.0)
        z0 = jnp.where(row == 7, self.onto_x(z0), z0)
        z0 = z0 + jnp.where((row == 3) | (row == 4), edges_x, 0.0) + self.onto_y(yz)
        y0 = jnp.where(row == 7, edges_x, y0 + jnp.where(row >= 5, edges_x, 0.0))
        z2 = g3
        own0 = g0 + self.onto_x(x0) + self.onto_y(y0)
        own0 = own0 + jnp.where(self.even, behind[0], self.lanes(z0, 1))
        own1 = g1 + jnp.where(row < 4, self.onto_x(sides), self.onto_y(sides))
        share2 = jnp.where(self.even, behind[1], self.lanes(z2, 1))
        own2 = g2 + jnp.where(row < 4, share2, 0.0)
        own3 = jnp.where(row < 4, 0.0, g3)
        own0 = own0 + jnp.where(row == 0, pltpu.roll(own0, 1, 0), 0.0)
        own0 = jnp.where(row == 7, pltpu.roll(own0, 7, 0), own0)
        moved = (self.lanes(z0, -1), self.lanes(z2, -1))
        return jnp.concatenate([own0, own1, own2, own3], 0), moved

    def apply(self, u, stiff, spread, collect, first, count, finish):
        width = self.width

        def step(index, carry):
            pair = first + 2 * index
            blocks = [
                self.gather(u[i, pair + q], u[i, pair + q + 1])
                for i in range(3)
                for q in range(2)
            ]
            high, low = high_low(jnp.concatenate(blocks, 1))
            gradient = jnp.dot(
                spread[...],
                jnp.concatenate([high, low, high], 0),
                preferred_element_type=jnp.float32,
            )
            stiffness = jnp.concatenate([stiff[pl.ds(pair + q, 1), :] for q in range(2)], 1)
            deform = [
                [
                    gradient[64 * e : 64 * e + 64, 2 * width * i : 2 * width * (i + 1)]
                    + (1.0 if i == e else 0.0)
                    for e in range(3)
                ]
                for i in range(3)
            ]
            stress = point_stress(deform, stiffness, lame_ratio * stiffness)
            stress = jnp.concatenate(
                [jnp.concatenate([stress[i][e] for i in range(3)], 1) for e in range(3)], 0
            )
            high, low = high_low(stress)
            force = jnp.dot(collect[...], high, preferred_element_type=jnp.float32)
            force = force[0:ROWS] + (
                force[ROWS:] + jnp.dot(collect[0:ROWS], low, preferred_element_type=jnp.float32)
            )
            carry = list(carry)
            totals = [[], []]
            for q in range(2):
                for i in range(3):
                    at = (2 * i + q) * width
                    total, carry[i] = self.scatter(force[:, at : at + width], carry[i])
                    totals[q].append(total)
            for q in range(2):
                finish(pair + q, totals[q])
            return tuple(carry)

        none = jnp.zeros((8, width), jnp.float32)
        lax.fori_loop(0, (count + 1) // 2, step, tuple((none, none) for i in range(3)))

    def smooth(self, u, f, f_shift, d, stiff, spread, collect, spans, bound):
        for (first, count), (held, added) in zip(spans, chebyshev_steps()):

            def finish(pair, forces, held=held, added=added):
                for i in range(3):
                    z = (added / bound) * self.keep * (f[i, pair + f_shift] - forces[i])
                    move = held * d[i, pair] + z if held else z
                    d[i, pair] = move
                    u[i, pair] = u[i, pair] + move

            self.apply(u, stiff, spread, collect, first, count, finish)

    def coarse_next_z(self, v):
        return self.next_z(v, pltpu.roll(v, 7, 0))

    def coarse_onto_z(self, v):
        return jnp.where(self.even, pltpu.roll(self.lanes(v, -1), 1, 0), self.lanes(v, 1))

    def corners_of(self, v):
        found = {(0, 0, 0): v, (0, 0, 1): self.coarse_next_z(v)}
        for c in range(2):
            found[0, 1, c] = self.next_y(found[0, 0, c])
        for b in range(2):
            for c in range(2):
                found[1, b, c] = self.next_x(found[0, b, c])
        return found

    def assemble(self, part):
        line = {
            (a, b): part[a, b, 0] + self.coarse_onto_z(part[a, b, 1])
            for a in range(2)
            for b in range(2)
        }
        face = [line[a, 0] + self.onto_y(line[a, 1]) for a in range(2)]
        return face[0] + self.onto_x(face[1])

    def coarse_force(self, values, stiffness):
        grads = []
        for i in range(3):
            v = self.corners_of(values[i])
            vz, sz = {}, {}
            for a in two:
                for b in two:
                    vz[a, b], sz[a, b] = at_points(v[a, b, 0], v[a, b, 1])
            vv, vs, sv = {}, {}, {}
            for a in two:
                for k in two:
                    vv[a, k], vs[a, k] = at_points(vz[a, 0][k], vz[a, 1][k])
                sv[a], unused = at_points(sz[a, 0], sz[a, 1])
            dx, dy, dz = {}, {}, {}
            for k in two:
                for j in two:
                    dx[j, k] = (vv[1, k][j] - vv[0, k][j]) * (1.0 / element_span)
                line, unused = at_points(vs[0, k], vs[1, k])
                for h in two:
                    dy[h, k] = line[h]
            for j in two:
                line, unused = at_points(sv[0][j], sv[1][j])
                for h in two:
                    dz[h, j] = line[h]
            grads.append((dx, dy, dz))
        weight = element_span**2 / 8.0
        scaled = weight * stiffness
        scaled_four = lame_ratio * scaled
        sums = [({}, {}, {}) for i in range(3)]

        def add(table, key, value):
            table[key] = table[key] + value if key in table else value

        for h in two:
            for j in two:
                for k in two:
                    deform = [
                        [grads[i][0][j, k], grads[i][1][h, k], grads[i][2][h, j]]
                        for i in range(3)
                    ]
                    for i in range(3):
                        deform[i][i] = deform[i][i] + 1.0
                    stress = point_stress(deform, scaled, scaled_four)
                    for i in range(3):
                        add(sums[i][0], (j, k), stress[i][0])
                        add(sums[i][1], (h, k), stress[i][1])
                        add(sums[i][2], (h, j), stress[i][2])

        forces = []
        for i in range(3):
            part = {}
            qx, qy, qz = sums[i]
            along_z = [ends_of(qx[j, 0], qx[j, 1]) for j in two]
            for c in two:
                line = ends_of(along_z[0][c], along_z[1][c])
                for b in two:
                    part[0, b, c] = -line[b]
                    part[1, b, c] = line[b]
            along_z = [ends_of(qy[h, 0], qy[h, 1]) for h in two]
            for c in two:
                line = ends_of(along_z[0][c], along_z[1][c])
                for a in two:
                    part[a, 0, c] = part[a, 0, c] - line[a]
                    part[a, 1, c] = part[a, 1, c] + line[a]
            along_y = [ends_of(qz[h, 0], qz[h, 1]) for h in two]
            for b in two:
                line = ends_of(along_y[0][b], along_y[1][b])
                for a in two:
                    part[a, b, 0] = part[a, b, 0] - line[a]
                    part[a, b, 1] = part[a, b, 1] + line[a]
            forces.append(self.assemble(part))
        return forces


def make_first_kernel(width, across, own_layers, fine_bound):
    own = BEFORE // 2
    own_pairs = (own_layers + 1) // 2
    spans = []
    for n in (4, 3, 2, 1):
        low, high = BEFORE - n, BEFORE + own_layers + n - 1
        spans.append((low // 2, (high + 1) // 2 - low // 2))

    def first_kernel(
        arrived, spread, collect, transfer, message, edge, f, u, d, stiff, shares, turned
    ):
        slab = Slab(width, across)
        row = slab.row
        u[...] = jnp.zeros(u.shape, jnp.float32)
        f[...] = jnp.zeros(f.shape, jnp.float32)
        shares[...] = jnp.zeros(shares.shape, jnp.float32)
        stiff[...] = jnp.zeros(stiff.shape, jnp.float32)
        lower = lax.broadcasted_iota(jnp.int32, (width // 8, 8, 128), 1) < 4
        for tile in range(SENT // 128):
            span = slice(128 * tile, 128 * tile + 128)
            first, second = arrived[:, 0, :, span], arrived[:, 1, :, span]
            value = jnp.where(lower, first, pltpu.roll(second, 4, 1))
            load = jnp.where(lower, pltpu.roll(first, 4, 1), second)
            turned[0, span, :] = value.reshape(width, 128).T
            turned[1, span, :] = load.reshape(width, 128).T
        for field, target in enumerate((u, f)):
            for pair in range(PAIRS):
                base = BLOCK * pair
                for i in range(3):
                    parts = [
                        turned[field, base + 24 * i + 8 * n : base + 24 * i + 8 * n + 8, :]
                        for n in range(3)
                    ]
                    inner = turned[field, base + 68 + 4 * i : base + 76 + 4 * i, :]
                    if field == 0 and i == 0:
                        stiff[pair : pair + 1, :] = parts[0][TWIN : TWIN + 1]
                    parts[0] = jnp.where(row == TWIN, pltpu.roll(parts[0], TWIN, 0), parts[0])
                    parts.append(jnp.where(row < 4, 0.0, inner))
                    whole = jnp.concatenate(parts, 0)
                    target[i, pair] = whole * slab.keep if field == 0 else whole

        slab.smooth(u, f, 0, d, stiff, spread, collect, spans[0:3], fine_bound)

        def restrict(pair, forces):
            rest = jnp.concatenate([slab.keep * (f[i, pair] - forces[i]) for i in range(3)], 1)
            corner = jnp.dot(
                transfer[...],
                rest,
                preferred_element_type=jnp.float32,
                precision=lax.Precision.HIGHEST,
            )
            for i in range(3):
                shares[i, pair] = corner[:, width * i : width * (i + 1)]

        slab.apply(u, stiff, spread, collect, *spans[3], restrict)

        restricted = [
            slab.assemble({corner: shares[i, :, n, :] for n, corner in enumerate(CORNERS)})
            for i in range(3)
        ]
        for q in range(own_pairs):
            hard = stiff[own + q : own + q + 1, :]
            for i in range(3):
                message[i, q] = u[i, own + q]
                message[i, q, RESTRICTED_SLOT : RESTRICTED_SLOT + 1, :] = restricted[i][
                    own + q : own + q + 1
                ]
                edge[q, i : i + 1, :] = u[i, own + q, 0:1, :]
                edge[q, 3 + i : 4 + i, :] = restricted[i][own + q : own + q + 1]
            message[0, q, STIFF_SLOT : STIFF_SLOT + 1, :] = hard
            edge[q, 6:8, :] = jnp.broadcast_to(hard, (2, width))

    return first_kernel


def full_reach(own_layers):
    return -(-3 // own_layers)


def coarse_reach(own_layers):
    return -(-5 // own_layers)


def make_second_kernel(width, across, own_layers, fine_bound, coarse_bound):
    own = BEFORE_B // 2
    own_pairs = (own_layers + 1) // 2
    shift = (BEFORE - BEFORE_B) // 2
    near, far = full_reach(own_layers), coarse_reach(own_layers)
    steps = chebyshev_steps()
    spans = []
    for n in (3, 2, 1):
        low, high = BEFORE_B - n, BEFORE_B + own_layers + n - 1
        spans.append((low // 2, (high + 1) // 2 - low // 2))

    def second_kernel(*refs):
        messages = dict(zip(range(-near, near + 1), refs[: 2 * near + 1]))
        refs = refs[2 * near + 1 :]
        outer = [n for n in range(-far, far + 1) if abs(n) > near]
        edges = dict(zip(outer, refs[: len(outer)]))
        f, spread, collect, transfer_back, out, u, d, stiff, coarse, raised = refs[len(outer) :]
        slab = Slab(width, across)

        def pair_of(pair, fetch):
            found = []
            for parity in range(2):
                layer = 2 * pair - BEFORE_B + parity
                device = layer // own_layers
                layer = layer - device * own_layers
                found.append((device, layer // 2, layer % 2))
            values = [fetch(device, q) for device, q, parity in found]
            if found[0][:2] == found[1][:2] or (values[0] is None and values[1] is None):
                return values[0]
            for parity in range(2):
                if values[parity] is None:
                    values[parity] = jnp.zeros_like(values[1 - parity])
                elif found[parity][2] != parity:
                    values[parity] = slab.lanes(values[parity], 2 * parity - 1)
            lane = lax.broadcasted_iota(jnp.int32, values[0].shape, 1)
            return jnp.where(lane % 2 == 0, values[0], values[1])

        u[...] = jnp.zeros(u.shape, jnp.float32)
        coarse[...] = jnp.zeros(coarse.shape, jnp.float32)
        d[...] = jnp.zeros(d.shape, jnp.float32)
        for pair in range(PAIRS_B):
            for i in range(3):
                whole = pair_of(pair, lambda n, q: messages[n][i, q] if n in messages else None)
                if whole is not None:
                    u[i, pair] = whole
            for n in range(7):

                def fetch(device, q, n=n):
                    if device in messages:
                        i, slot = ((n, 0), (n - 3, RESTRICTED_SLOT), (0, STIFF_SLOT))[n // 3]
                        return messages[device][i, q, slot : slot + 1, :]
                    return edges[device][q, n : n + 1, :] if device in edges else None

                line = pair_of(pair, fetch)
                if line is not None:
                    coarse[n, pair : pair + 1, :] = line
        stiff[...] = coarse[6]

        stiffness = coarse[6]
        keep_coarse = jnp.where(slab.bottom, 0.0, 1.0)
        start = [coarse[i] for i in range(3)]
        restricted = [coarse[3 + i] for i in range(3)]
        before = slab.coarse_force(start, stiffness)
        move = [(steps[0][1] / coarse_bound) * keep_coarse * restricted[i] for i in range(3)]
        level = [start[i] + move[i] for i in range(3)]
        for held, added in steps[1:]:
            force = slab.coarse_force(level, stiffness)
            for i in range(3):
                z = keep_coarse * (restricted[i] + before[i] - force[i])
                move[i] = held * move[i] + (added / coarse_bound) * z
                level[i] = level[i] + move[i]

        for i in range(3):
            change = slab.corners_of(level[i] - start[i])
            for n, corner in enumerate(CORNERS):
                raised[i, :, n, :] = change[corner]
        for pair in range(spans[0][0], min(spans[0][0] + spans[0][1] + 1, PAIRS_B)):
            lift = jnp.dot(
                transfer_back[...],
                jnp.concatenate([raised[i, pair] for i in range(3)], 1),
                preferred_element_type=jnp.float32,
                precision=lax.Precision.HIGHEST,
            )
            for i in range(3):
                u[i, pair] = u[i, pair] + lift[:, width * i : width * (i + 1)]

        slab.smooth(u, f, shift, d, stiff, spread, collect, spans, fine_bound)

        lower = lax.broadcasted_iota(jnp.int32, (width // 8, 8, 128), 1) < 4
        sides = []
        blank = jnp.zeros((29, width), jnp.float32)
        for q in range(2):
            ends_here = jnp.concatenate(
                [u[i, own + q] for i in range(3)]
                + [level[i][own + q : own + q + 1] for i in range(3)]
                + [blank],
                0,
            )
            sides.append(ends_here.T.reshape(width // 8, 8, 128))
        out[:, 0] = jnp.where(lower, sides[0], pltpu.roll(sides[1], 4, 1))
        out[:, 1] = jnp.where(lower, pltpu.roll(sides[0], 4, 1), sides[1])

    return second_kernel


def solution(mesh):
    rows_of, columns_of = mesh.shape["gx"], mesh.shape["gy"]
    devices = rows_of * columns_of
    own_layers = EZ // devices
    own_pairs = (own_layers + 1) // 2
    width = 4 * devices
    across = 2 * rows_of
    near, far = full_reach(own_layers), coarse_reach(own_layers)
    spread, collect, fine_bound = element_tables()
    coarse_bound = build_tables([0.0, 1.0], 2)[2]
    transfer, transfer_back = transfer_table()
    wide = pltpu.CompilerParams(vmem_limit_bytes=60 * 1024 * 1024)
    limit = pltpu.CompilerParams(vmem_limit_bytes=48 * 1024 * 1024)
    f32 = jnp.float32

    pack = pl.pallas_call(
        pack_kernel,
        out_shape=jax.ShapeDtypeStruct((devices, 8, SENT), f32),
        in_specs=[pl.BlockSpec(memory_space=pl.ANY)] * 5,
        out_specs=pl.BlockSpec(memory_space=pltpu.VMEM),
        scratch_shapes=[
            pltpu.VMEM((3, 6, 3, 384), f32),
            pltpu.VMEM((3, 6, 3, 384), f32),
            pltpu.VMEM((2, 1, EZ), f32),
            pltpu.VMEM((1, 1, 192), jnp.int32),
            pltpu.VMEM((384, 512), jnp.bfloat16),
            pltpu.VMEM((128, 384), f32),
            pltpu.VMEM((384, 128), f32),
            pltpu.VMEM((16, 160, 128), f32),
            pltpu.SemaphoreType.DMA((5,)),
        ],
        compiler_params=wide,
    )
    first = pl.pallas_call(
        make_first_kernel(width, across, own_layers, fine_bound),
        out_shape=(
            jax.ShapeDtypeStruct((3, own_pairs, 32, width), f32),
            jax.ShapeDtypeStruct((own_pairs, 8, width), f32),
            jax.ShapeDtypeStruct((3, PAIRS, 32, width), f32),
        ),
        scratch_shapes=[
            pltpu.VMEM((3, 8, 32, width), f32),
            pltpu.VMEM((3, 8, 32, width), f32),
            pltpu.VMEM((8, width), f32),
            pltpu.VMEM((3, 8, 8, width), f32),
            pltpu.VMEM((2, SENT, width), f32),
        ],
        compiler_params=limit,
    )
    second = pl.pallas_call(
        make_second_kernel(width, across, own_layers, fine_bound, coarse_bound),
        out_shape=jax.ShapeDtypeStruct((devices // 2, 2, 8, 128), f32),
        scratch_shapes=[
            pltpu.VMEM((3, PAIRS_B + 2, 32, width), f32),
            pltpu.VMEM((3, PAIRS_B, 32, width), f32),
            pltpu.VMEM((PAIRS_B, width), f32),
            pltpu.VMEM((7, PAIRS_B, width), f32),
            pltpu.VMEM((3, PAIRS_B, 8, width), f32),
        ],
        compiler_params=limit,
    )
    unpack = pl.pallas_call(
        unpack_kernel,
        out_shape=(
            jax.ShapeDtypeStruct((3, 6, 3, 384), f32),
            jax.ShapeDtypeStruct((3, 2, 1, EZ), f32),
        ),
        scratch_shapes=[pltpu.VMEM((2, 128, 128), f32), pltpu.VMEM((384, 128), f32)],
        compiler_params=limit,
    )
    everyone = ("gy", "gx")

    def from_device(block, distance):
        place = [k % rows_of * columns_of + k // rows_of for k in range(devices)]
        route = [(place[(k + distance) % devices], place[k]) for k in range(devices)]
        return lax.ppermute(block, ("gx", "gy"), route)

    def body(initial, forcing, modulus, solid_list):
        sent = pack(initial, forcing, modulus, solid_list, jnp.asarray(pack_table()))
        arrived = lax.all_to_all(sent, everyone, 0, 0, tiled=True)
        message, edge, load = first(
            arrived.reshape(devices // 2, 2, 8, SENT),
            jnp.asarray(spread),
            jnp.asarray(collect),
            jnp.asarray(transfer),
        )
        messages = [
            from_device(message, n) if n else message for n in range(-near, near + 1)
        ]
        edges = [from_device(edge, n) for n in range(-far, far + 1) if abs(n) > near]
        result = second(
            *messages,
            *edges,
            load,
            jnp.asarray(spread),
            jnp.asarray(collect),
            jnp.asarray(transfer_back),
        )
        back = lax.all_to_all(result.reshape(devices, 8, 128), everyone, 0, 0, tiled=True)
        return unpack(back, jnp.asarray(unpack_table()))

    placed = (
        P(None, "gx", "gy", None),
        P(None, "gx", "gy", None),
        P("gx", "gy", None),
        P("gx", "gy", None),
    )
    return jax.shard_map(
        body,
        mesh=mesh,
        in_specs=placed,
        out_specs=(P(None, "gx", "gy", None), P(None, "gx", "gy", None)),
        check_vma=False,
    )
```

```python
import math

import jax
import jax.numpy as jnp
import numpy as np
from jax import lax
from jax.experimental import pallas as pl
from jax.experimental.pallas import tpu as pltpu
from jax.sharding import PartitionSpec as P

CHEB = 3
EZ = 128

element_span = 20.0
lame_ratio = 4.0
rest_ratio = 1.25
modulus_top = 2.0
spectrum_floor = 0.05
interval_centre = (1.0 + spectrum_floor) / 2.0
interval_radius = (1.0 - spectrum_floor) / 2.0
interval_ratio = interval_centre / interval_radius
inner_anchors = (0.5 - 0.5 / math.sqrt(5.0), 0.5 + 0.5 / math.sqrt(5.0))

BEFORE = 4
PAIRS = 6
BEFORE_B = 6
PAIRS_B = 8
BLOCK = 84
SENT = 512

SLOTS = [
    (0, 0, 0), (1, 0, 0), (2, 0, 0), (0, 1, 0), (0, 2, 0), (0, 0, 1), (0, 0, 2), None,
    (0, 1, 1), (0, 1, 2), (0, 2, 1), (0, 2, 2), (1, 0, 1), (1, 0, 2), (2, 0, 1), (2, 0, 2),
    (1, 1, 0), (1, 2, 0), (2, 1, 0), (2, 2, 0), (1, 1, 1), (1, 1, 2), (1, 2, 1), (1, 2, 2),
    None, None, None, None, (2, 1, 1), (2, 1, 2), (2, 2, 1), (2, 2, 2),
]
TWIN = 7
RESTRICTED_SLOT = 24
STIFF_SLOT = 25
OWN_SHIFT, SHIFT_X, SHIFT_Y, SHIFT_Z = (0, 0, 0), (1, 0, 0), (0, 1, 0), (0, 0, 1)
ELEMENT_ROWS = (
    [(slot, OWN_SHIFT) for slot in range(24)]
    + [(slot, SHIFT_Z) for slot in range(16, 20)]
    + [(slot, OWN_SHIFT) for slot in range(28, 32)]
    + [(slot, SHIFT_X) for slot in range(7)] + [None]
    + [(slot, SHIFT_Y) for slot in range(7)] + [(0, (0, 1, 1))]
    + [(slot, SHIFT_Z) for slot in range(7)] + [(0, (1, 0, 1))]
    + [(slot, SHIFT_X) for slot in range(8, 12)] + [(slot, SHIFT_Y) for slot in range(12, 16)]
    + [(0, (1, 1, 1)), (1, (0, 1, 1)), (2, (0, 1, 1)), (3, (1, 0, 1)), (4, (1, 0, 1))]
    + [(5, (1, 1, 0)), (6, (1, 1, 0)), (0, (1, 1, 0))]
)
ROWS = len(ELEMENT_ROWS)
DEPTH = 80
CORNERS = [(a, b, c) for a in range(2) for b in range(2) for c in range(2)]


def gauss_rule(point_count):
    if point_count == 2:
        offset = 1.0 / math.sqrt(3.0)
        points = [-offset, offset]
        weights = [1.0, 1.0]
    else:
        inner = math.sqrt(3.0 / 7.0 - 2.0 / 7.0 * math.sqrt(6.0 / 5.0))
        outer = math.sqrt(3.0 / 7.0 + 2.0 / 7.0 * math.sqrt(6.0 / 5.0))
        heavy = (18.0 + math.sqrt(30.0)) / 36.0
        light = (18.0 - math.sqrt(30.0)) / 36.0
        points = [-outer, -inner, inner, outer]
        weights = [light, heavy, heavy, light]
    return (np.array(points), np.array(weights))


def lagrange_tables(anchors, samples):
    values = np.zeros((len(samples), len(anchors)))
    slopes = np.zeros((len(samples), len(anchors)))
    for sample_index, sample in enumerate(samples):
        for anchor_index, anchor in enumerate(anchors):
            others = [
                location
                for location_index, location in enumerate(anchors)
                if location_index != anchor_index
            ]
            product = 1.0
            for location in others:
                product = product * (sample - location) / (anchor - location)
            values[sample_index, anchor_index] = product
            derivative = 0.0
            for skipped in range(len(others)):
                summand = 1.0 / (anchor - others[skipped])
                for kept_index in range(len(others)):
                    if kept_index != skipped:
                        summand = (
                            summand * (sample - others[kept_index]) / (anchor - others[kept_index])
                        )
                derivative = derivative + summand
            slopes[sample_index, anchor_index] = derivative
    return (values, slopes)


def outer_three(first, second, third):
    return (
        first[:, None, None, :, None, None]
        * second[None, :, None, None, :, None]
        * third[None, None, :, None, None, :]
    )


def build_tables(anchors, point_count):
    raw_points, raw_weights = gauss_rule(point_count)
    samples = (raw_points + 1.0) / 2.0
    weights = raw_weights / 2.0
    basis_values, slopes = lagrange_tables(anchors, samples)
    quad_total = point_count**3
    nodal_count = len(anchors) ** 3
    derivative_one = outer_three(slopes, basis_values, basis_values).reshape(
        quad_total, nodal_count
    )
    derivative_two = outer_three(basis_values, slopes, basis_values).reshape(
        quad_total, nodal_count
    )
    derivative_three = outer_three(basis_values, basis_values, slopes).reshape(
        quad_total, nodal_count
    )
    stacked = np.stack([derivative_one, derivative_two, derivative_three]) / element_span
    volume = (weights[:, None, None] * weights[None, :, None] * weights[None, None, :]).reshape(
        -1
    ) * element_span**3
    forward = stacked.reshape(3 * quad_total, nodal_count)
    backward = (stacked * volume[None, :, None]).reshape(3 * quad_total, nodal_count).T
    weighted = stacked * volume[None, :, None]
    laplace = weighted[0].T @ stacked[0] + weighted[1].T @ stacked[1] + weighted[2].T @ stacked[2]
    matrix = np.zeros((nodal_count, 3, nodal_count, 3))
    for first in range(3):
        for second in range(3):
            block = weighted[second].T @ stacked[first] + (lame_ratio - 1.0) * (
                weighted[first].T @ stacked[second]
            )
            if first == second:
                block = block + laplace
            matrix[:, first, :, second] = block
    matrix = matrix.reshape(3 * nodal_count, 3 * nodal_count)
    vector = 1.5 + np.cos(1.3 * np.arange(3 * nodal_count))
    for repeat in range(200):
        vector = matrix @ vector
        vector = vector / np.sqrt(vector @ vector)
    largest = vector @ (matrix @ vector)
    return (forward, backward, float(4.0 * modulus_top * 1.1 * largest))


def row_nodes():
    nodes = []
    for entry in ELEMENT_ROWS:
        slot = SLOTS[entry[0]] if entry else None
        if slot is None or any(s and n for s, n in zip(entry[1], slot)):
            nodes.append(None)
        else:
            a, b, c = (3 * s + n for s, n in zip(entry[1], slot))
            nodes.append(16 * a + 4 * b + c)
    return nodes


def halves(matrix):
    whole = np.asarray(matrix, np.float32)
    high = whole.astype(jnp.bfloat16)
    low = (whole - high.astype(np.float32)).astype(jnp.bfloat16)
    return high, low


def element_tables():
    forward, backward, bound = build_tables([0.0, inner_anchors[0], inner_anchors[1], 1.0], 4)
    spread = np.zeros((forward.shape[0], DEPTH))
    collect = np.zeros((ROWS, backward.shape[1]))
    for row, node in enumerate(row_nodes()):
        if node is not None:
            spread[:, row] = forward[:, node]
            collect[row, :] = backward[node, :]
    spread_high, spread_low = halves(spread)
    collect_high, collect_low = halves(collect)
    return (
        np.concatenate([spread_high, spread_high, spread_low], 1),
        np.concatenate([collect_high, collect_low], 0),
        bound,
    )


def transfer_table():
    table = np.zeros((8, 32))
    reach = (0.0, inner_anchors[0], inner_anchors[1])
    for row, corner in enumerate(CORNERS):
        for column, slot in enumerate(SLOTS):
            if slot is not None:
                weight = 1.0
                for side, node in zip(corner, slot):
                    weight = weight * (reach[node] if side else 1.0 - reach[node])
                table[row, column] = weight
    back = table.T.copy()
    back[TWIN] = back[0]
    return table.T.astype(np.float32), back.astype(np.float32)


def chebyshev_steps():
    steps = [(0.0, 1.0 / interval_centre)]
    ratio_now = 1.0 / interval_ratio
    for sweep in range(1, CHEB):
        ratio_next = 1.0 / (2.0 * interval_ratio - ratio_now)
        steps.append((ratio_next * ratio_now, 2.0 * ratio_next / interval_radius))
        ratio_now = ratio_next
    return steps


def stack_row(field, component, layer, b):
    return field * 54 + component * 18 + layer * 3 + b


def block_column(component, slot):
    return 72 + 4 * component + slot - 28 if slot >= 24 else 24 * component + slot


def pack_table():
    table = np.zeros((3, 128, 2, 2, 128), np.float32)
    for field in range(2):
        for x in range(2):
            for component in range(3):
                for column, slot in enumerate(SLOTS):
                    if slot is not None:
                        a, b, c = slot
                        row = stack_row(field, component, 3 * x + a, b)
                        table[c, row, field, x, block_column(component, column)] = 1.0
            table[0, 108 + x, 0, x, TWIN] = 1.0
    return table.reshape(384, 512).astype(jnp.bfloat16)


def unpack_table():
    table = np.zeros((2, 128, 3, 128), np.float32)
    for x in range(2):
        for component in range(3):
            for column, slot in enumerate(SLOTS):
                if slot is not None:
                    a, b, c = slot
                    row = stack_row(0, component, 3 * x + a, b)
                    table[x, component * 32 + column, c, row] = 1.0
            table[x, 96 + component, 0, 54 + 2 * component + x] = 1.0
    return table.reshape(256, 384).astype(jnp.bfloat16)


def exact_pick(values, table):
    high = values.astype(jnp.bfloat16)
    rest = values - high.astype(jnp.float32)
    middle = rest.astype(jnp.bfloat16)
    low = (rest - middle.astype(jnp.float32)).astype(jnp.bfloat16)
    count = values.shape[0]
    parts = jnp.dot(
        jnp.concatenate([high, middle, low], 0), table, preferred_element_type=jnp.float32
    )
    return parts[:count] + (parts[count : 2 * count] + parts[2 * count :])


def pack_kernel(
    initial_at, forcing_at, modulus_at, listing_at, table_at, out,
    initial, forcing, modulus, listing, table, rows, turned, places, ready,
):
    devices = out.shape[0]
    own_layers = EZ // devices
    sources = (listing_at, modulus_at, initial_at, forcing_at, table_at)
    copies = [
        pltpu.make_async_copy(source, here, ready.at[n])
        for n, (source, here) in enumerate(
            zip(sources, (listing, modulus, initial, forcing, table))
        )
    ]
    for copy in copies:
        copy.start()
    rows[108:128, :] = jnp.zeros((20, 384), jnp.float32)
    copies[0].wait()
    copies[1].wait()
    listed = listing[0].astype(jnp.float32)
    listed = jnp.concatenate([listed, jnp.full((1, 64), 256.0, jnp.float32)], 1)
    listed = jnp.broadcast_to(listed, (128, 256)).T
    lanes = lax.broadcasted_iota(jnp.int32, (256, 128), 1).astype(jnp.float32)
    row_at = lax.broadcasted_iota(jnp.int32, (128, 128), 0)
    stiff = jnp.zeros((128, 128), jnp.float32)
    for x in range(2):
        hit = jnp.max(jnp.where(listed == lanes + 128.0 * x, 1.0, 0.0), axis=0, keepdims=True)
        stiff = jnp.where(row_at == 108 + x, hit * modulus[x], stiff)
    copies[2].wait()
    copies[3].wait()
    for field, source in enumerate((initial, forcing)):
        for component in range(3):
            for layer in range(6):
                at = stack_row(field, component, layer, 0)
                rows[at : at + 3, :] = source[component, layer]
    for part in range(3):
        span = slice(128 * part, 128 * part + 128)
        turned[span, :] = rows[:, span].T
    picked = [turned[pl.ds(c, 128, stride=3), :] for c in range(3)]
    picked[0] = picked[0] + stiff.T
    copies[4].wait()
    wide = exact_pick(jnp.concatenate(picked, 1), table[...])
    lane = lax.broadcasted_iota(jnp.int32, (128, 128), 1)
    for block in range(4):
        here = wide[:, 128 * block : 128 * block + 128]
        tiles = [None] * (SENT // 128)
        for pair in range(PAIRS):
            first = BLOCK * pair
            moved = here if pair == 0 else pltpu.roll(here, 128 - 2 * pair, 0)
            if first % 128:
                moved = pltpu.roll(moved, first % 128, 1)
            for tile in range(first // 128, (first + BLOCK - 1) // 128 + 1):
                before = tiles[tile]
                if before is None:
                    tiles[tile] = moved
                else:
                    tiles[tile] = jnp.where(lane >= first - 128 * tile, moved, before)
        for tile in range(SENT // 128):
            at = 4 * block + tile
            places[at, 16:144, :] = tiles[tile]
            places[at, 0:16, :] = tiles[tile][112:128]
            places[at, 144:160, :] = tiles[tile][0:16]
    for block in range(4):
        for parity in range(2):
            for tile in range(SENT // 128):
                out[:, 2 * block + parity, 128 * tile : 128 * tile + 128] = places[
                    4 * block + tile, pl.ds(16 - BEFORE + parity, devices, stride=own_layers), :
                ]


def unpack_kernel(arrived, table, out, coarse_out, layers, turned):
    devices = arrived.shape[0]
    own_layers = EZ // devices
    for x in range(2):
        for layer in range(own_layers):
            row = (layer // 2) * 4 + x * 2 + layer % 2
            layers[x, pl.ds(layer, devices, stride=own_layers), :] = arrived[:, row, :]
    wide = exact_pick(jnp.concatenate([layers[0], layers[1]], 1), table[...])
    for c in range(3):
        turned[pl.ds(c, 128, stride=3), :] = wide[:, 128 * c : 128 * c + 128]
    for part in range(3):
        span = slice(128 * part, 128 * part + 128)
        back = turned[span, :].T
        for component in range(3):
            for layer in range(6):
                at = stack_row(0, component, layer, 0)
                out[component, layer, :, span] = back[at : at + 3, :]
    back = wide[:, 0:128].T
    for component in range(3):
        for x in range(2):
            at = 54 + 2 * component + x
            coarse_out[component, x] = back[at : at + 1, :]


def cofactor_rows(deform):
    return [
        [
            deform[(row_at + 1) % 3][(column + 1) % 3] * deform[(row_at + 2) % 3][(column + 2) % 3]
            - deform[(row_at + 1) % 3][(column + 2) % 3]
            * deform[(row_at + 2) % 3][(column + 1) % 3]
            for column in range(3)
        ]
        for row_at in range(3)
    ]


def point_stress(deform, stiffness, stiffness_four):
    cofactors = cofactor_rows(deform)
    jacobian = (
        deform[0][0] * cofactors[0][0]
        + deform[0][1] * cofactors[0][1]
        + deform[0][2] * cofactors[0][2]
    )
    pressure = stiffness_four * (jacobian - rest_ratio)
    return [
        [stiffness * deform[i][d] + pressure * cofactors[i][d] for d in range(3)] for i in range(3)
    ]


coarse_samples = [0.5 - 0.5 / math.sqrt(3.0), 0.5 + 0.5 / math.sqrt(3.0)]
two = range(2)


def at_points(low, high):
    change = high - low
    return [low + s * change for s in coarse_samples], change * (1.0 / element_span)


def ends_of(first, second):
    high = coarse_samples[0] * first + coarse_samples[1] * second
    return [first + second - high, high]


def high_low(values):
    high = values.astype(jnp.bfloat16)
    return high, (values - high.astype(jnp.float32)).astype(jnp.bfloat16)


class Slab:
    def __init__(self, width, across):
        self.width = width
        self.y_step = 2 * across
        lane = lax.broadcasted_iota(jnp.int32, (8, width), 1)
        x = (lane // 2) % across
        self.bottom, self.top, self.even = x == 0, x == across - 1, lane % 2 == 0
        self.row = lax.broadcasted_iota(jnp.int32, (8, width), 0)
        row = lax.broadcasted_iota(jnp.int32, (32, width), 0)
        lane = lax.broadcasted_iota(jnp.int32, (32, width), 1)
        on_face = (row == 0) | ((row >= 3) & (row <= 11))
        self.keep = jnp.where(on_face & ((lane // 2) % across == 0), 0.0, 1.0)

    def lanes(self, v, step):
        return pltpu.roll(v, step % self.width, 1)

    def next_x(self, v):
        return jnp.where(self.top, 0.0, self.lanes(v, -2))

    def next_y(self, v):
        return self.lanes(v, -self.y_step)

    def next_z(self, v, ahead):
        return jnp.where(self.even, self.lanes(v, -1), self.lanes(ahead, 1))

    def onto_x(self, v):
        return jnp.where(self.bottom, 0.0, self.lanes(v, 2))

    def onto_y(self, v):
        return self.lanes(v, self.y_step)

    def gather(self, here, ahead):
        row = self.row
        g0, g1, g2, g3 = here[0:8], here[8:16], here[16:24], here[24:32]
        z0 = self.next_z(g0, ahead[0:8])
        z2 = self.next_z(g2, ahead[16:24])
        y0 = self.next_y(g0)
        yz, xz, xy = self.next_y(z0), self.next_x(z0), self.next_x(y0)
        edges = jnp.where(row <= 2, yz, jnp.where(row <= 4, xz, xy))
        return jnp.concatenate(
            [
                g0,
                g1,
                g2,
                jnp.where(row < 4, z2, g3),
                self.next_x(g0),
                jnp.where(row == 7, yz, y0),
                jnp.where(row == 7, xz, z0),
                jnp.where(row < 4, self.next_x(g1), self.next_y(g1)),
                jnp.where(row == 0, self.next_x(yz), edges),
                jnp.zeros_like(g0),
            ],
            0,
        )

    def scatter(self, part, behind):
        row = self.row
        g0, g1, g2, g3, x0, y0, z0, sides, edges = (part[8 * n : 8 * n + 8] for n in range(9))
        edges_x = self.onto_x(edges)
        yz = jnp.where(row == 0, edges_x, jnp.where(row == 7, y0, edges))
        yz = jnp.where((row <= 2) | (row == 7), yz, 0.0)
        z0 = jnp.where(row == 7, self.onto_x(z0), z0)
        z0 = z0 + jnp.where((row == 3) | (row == 4), edges_x, 0.0) + self.onto_y(yz)
        y0 = jnp.where(row == 7, edges_x, y0 + jnp.where(row >= 5, edges_x, 0.0))
        z2 = g3
        own0 = g0 + self.onto_x(x0) + self.onto_y(y0)
        own0 = own0 + jnp.where(self.even, behind[0], self.lanes(z0, 1))
        own1 = g1 + jnp.where(row < 4, self.onto_x(sides), self.onto_y(sides))
        share2 = jnp.where(self.even, behind[1], self.lanes(z2, 1))
        own2 = g2 + jnp.where(row < 4, share2, 0.0)
        own3 = jnp.where(row < 4, 0.0, g3)
        own0 = own0 + jnp.where(row == 0, pltpu.roll(own0, 1, 0), 0.0)
        own0 = jnp.where(row == 7, pltpu.roll(own0, 7, 0), own0)
        moved = (self.lanes(z0, -1), self.lanes(z2, -1))
        return jnp.concatenate([own0, own1, own2, own3], 0), moved

    def apply(self, u, stiff, spread, collect, first, count, finish):
        width = self.width

        def step(index, carry):
            pair = first + 2 * index
            blocks = [
                self.gather(u[i, pair + q], u[i, pair + q + 1])
                for i in range(3)
                for q in range(2)
            ]
            high, low = high_low(jnp.concatenate(blocks, 1))
            gradient = jnp.dot(
                spread[...],
                jnp.concatenate([high, low, high], 0),
                preferred_element_type=jnp.float32,
            )
            stiffness = jnp.concatenate([stiff[pl.ds(pair + q, 1), :] for q in range(2)], 1)
            deform = [
                [
                    gradient[64 * e : 64 * e + 64, 2 * width * i : 2 * width * (i + 1)]
                    + (1.0 if i == e else 0.0)
                    for e in range(3)
                ]
                for i in range(3)
            ]
            stress = point_stress(deform, stiffness, lame_ratio * stiffness)
            stress = jnp.concatenate(
                [jnp.concatenate([stress[i][e] for i in range(3)], 1) for e in range(3)], 0
            )
            high, low = high_low(stress)
            force = jnp.dot(collect[...], high, preferred_element_type=jnp.float32)
            force = force[0:ROWS] + (
                force[ROWS:] + jnp.dot(collect[0:ROWS], low, preferred_element_type=jnp.float32)
            )
            carry = list(carry)
            totals = [[], []]
            for q in range(2):
                for i in range(3):
                    at = (2 * i + q) * width
                    total, carry[i] = self.scatter(force[:, at : at + width], carry[i])
                    totals[q].append(total)
            for q in range(2):
                finish(pair + q, totals[q])
            return tuple(carry)

        none = jnp.zeros((8, width), jnp.float32)
        lax.fori_loop(0, (count + 1) // 2, step, tuple((none, none) for i in range(3)))

    def smooth(self, u, f, f_shift, d, stiff, spread, collect, spans, bound):
        for (first, count), (held, added) in zip(spans, chebyshev_steps()):

            def finish(pair, forces, held=held, added=added):
                for i in range(3):
                    z = (added / bound) * self.keep * (f[i, pair + f_shift] - forces[i])
                    move = held * d[i, pair] + z if held else z
                    d[i, pair] = move
                    u[i, pair] = u[i, pair] + move

            self.apply(u, stiff, spread, collect, first, count, finish)

    def coarse_next_z(self, v):
        return self.next_z(v, pltpu.roll(v, 7, 0))

    def coarse_onto_z(self, v):
        return jnp.where(self.even, pltpu.roll(self.lanes(v, -1), 1, 0), self.lanes(v, 1))

    def corners_of(self, v):
        found = {(0, 0, 0): v, (0, 0, 1): self.coarse_next_z(v)}
        for c in range(2):
            found[0, 1, c] = self.next_y(found[0, 0, c])
        for b in range(2):
            for c in range(2):
                found[1, b, c] = self.next_x(found[0, b, c])
        return found

    def assemble(self, part):
        line = {
            (a, b): part[a, b, 0] + self.coarse_onto_z(part[a, b, 1])
            for a in range(2)
            for b in range(2)
        }
        face = [line[a, 0] + self.onto_y(line[a, 1]) for a in range(2)]
        return face[0] + self.onto_x(face[1])

    def coarse_force(self, values, stiffness):
        grads = []
        for i in range(3):
            v = self.corners_of(values[i])
            vz, sz = {}, {}
            for a in two:
                for b in two:
                    vz[a, b], sz[a, b] = at_points(v[a, b, 0], v[a, b, 1])
            vv, vs, sv = {}, {}, {}
            for a in two:
                for k in two:
                    vv[a, k], vs[a, k] = at_points(vz[a, 0][k], vz[a, 1][k])
                sv[a], unused = at_points(sz[a, 0], sz[a, 1])
            dx, dy, dz = {}, {}, {}
            for k in two:
                for j in two:
                    dx[j, k] = (vv[1, k][j] - vv[0, k][j]) * (1.0 / element_span)
                line, unused = at_points(vs[0, k], vs[1, k])
                for h in two:
                    dy[h, k] = line[h]
            for j in two:
                line, unused = at_points(sv[0][j], sv[1][j])
                for h in two:
                    dz[h, j] = line[h]
            grads.append((dx, dy, dz))
        weight = element_span**2 / 8.0
        scaled = weight * stiffness
        scaled_four = lame_ratio * scaled
        sums = [({}, {}, {}) for i in range(3)]

        def add(table, key, value):
            table[key] = table[key] + value if key in table else value

        for h in two:
            for j in two:
                for k in two:
                    deform = [
                        [grads[i][0][j, k], grads[i][1][h, k], grads[i][2][h, j]]
                        for i in range(3)
                    ]
                    for i in range(3):
                        deform[i][i] = deform[i][i] + 1.0
                    stress = point_stress(deform, scaled, scaled_four)
                    for i in range(3):
                        add(sums[i][0], (j, k), stress[i][0])
                        add(sums[i][1], (h, k), stress[i][1])
                        add(sums[i][2], (h, j), stress[i][2])

        forces = []
        for i in range(3):
            part = {}
            qx, qy, qz = sums[i]
            along_z = [ends_of(qx[j, 0], qx[j, 1]) for j in two]
            for c in two:
                line = ends_of(along_z[0][c], along_z[1][c])
                for b in two:
                    part[0, b, c] = -line[b]
                    part[1, b, c] = line[b]
            along_z = [ends_of(qy[h, 0], qy[h, 1]) for h in two]
            for c in two:
                line = ends_of(along_z[0][c], along_z[1][c])
                for a in two:
                    part[a, 0, c] = part[a, 0, c] - line[a]
                    part[a, 1, c] = part[a, 1, c] + line[a]
            along_y = [ends_of(qz[h, 0], qz[h, 1]) for h in two]
            for b in two:
                line = ends_of(along_y[0][b], along_y[1][b])
                for a in two:
                    part[a, b, 0] = part[a, b, 0] - line[a]
                    part[a, b, 1] = part[a, b, 1] + line[a]
            forces.append(self.assemble(part))
        return forces


def make_first_kernel(width, across, own_layers, fine_bound):
    own = BEFORE // 2
    own_pairs = (own_layers + 1) // 2
    spans = []
    for n in (4, 3, 2, 1):
        low, high = BEFORE - n, BEFORE + own_layers + n - 1
        spans.append((low // 2, (high + 1) // 2 - low // 2))

    def first_kernel(
        arrived, spread, collect, transfer, message, edge, f, u, d, stiff, shares, turned
    ):
        slab = Slab(width, across)
        row = slab.row
        u[...] = jnp.zeros(u.shape, jnp.float32)
        f[...] = jnp.zeros(f.shape, jnp.float32)
        shares[...] = jnp.zeros(shares.shape, jnp.float32)
        stiff[...] = jnp.zeros(stiff.shape, jnp.float32)
        lower = lax.broadcasted_iota(jnp.int32, (width // 8, 8, 128), 1) < 4
        for tile in range(SENT // 128):
            span = slice(128 * tile, 128 * tile + 128)
            first, second = arrived[:, 0, :, span], arrived[:, 1, :, span]
            value = jnp.where(lower, first, pltpu.roll(second, 4, 1))
            load = jnp.where(lower, pltpu.roll(first, 4, 1), second)
            turned[0, span, :] = value.reshape(width, 128).T
            turned[1, span, :] = load.reshape(width, 128).T
        for field, target in enumerate((u, f)):
            for pair in range(PAIRS):
                base = BLOCK * pair
                for i in range(3):
                    parts = [
                        turned[field, base + 24 * i + 8 * n : base + 24 * i + 8 * n + 8, :]
                        for n in range(3)
                    ]
                    inner = turned[field, base + 68 + 4 * i : base + 76 + 4 * i, :]
                    if field == 0 and i == 0:
                        stiff[pair : pair + 1, :] = parts[0][TWIN : TWIN + 1]
                    parts[0] = jnp.where(row == TWIN, pltpu.roll(parts[0], TWIN, 0), parts[0])
                    parts.append(jnp.where(row < 4, 0.0, inner))
                    whole = jnp.concatenate(parts, 0)
                    target[i, pair] = whole * slab.keep if field == 0 else whole

        slab.smooth(u, f, 0, d, stiff, spread, collect, spans[0:3], fine_bound)

        weights = [jnp.broadcast_to(transfer[:, n : n + 1], (32, width)) for n in range(8)]

        def restrict(pair, forces):
            for i in range(3):
                rest = slab.keep * (f[i, pair] - forces[i])
                for n in range(8):
                    part = rest * weights[n]
                    part = (part[0:8] + part[8:16]) + (part[16:24] + part[24:32])
                    shares[i, n, pl.ds(pair, 1), :] = jnp.sum(part, axis=0, keepdims=True)

        slab.apply(u, stiff, spread, collect, *spans[3], restrict)

        restricted = [
            slab.assemble({corner: shares[i, n] for n, corner in enumerate(CORNERS)})
            for i in range(3)
        ]
        for q in range(own_pairs):
            hard = stiff[own + q : own + q + 1, :]
            for i in range(3):
                message[i, q] = u[i, own + q]
                message[i, q, RESTRICTED_SLOT : RESTRICTED_SLOT + 1, :] = restricted[i][
                    own + q : own + q + 1
                ]
                edge[q, i : i + 1, :] = u[i, own + q, 0:1, :]
                edge[q, 3 + i : 4 + i, :] = restricted[i][own + q : own + q + 1]
            message[0, q, STIFF_SLOT : STIFF_SLOT + 1, :] = hard
            edge[q, 6:8, :] = jnp.broadcast_to(hard, (2, width))

    return first_kernel


def full_reach(own_layers):
    return -(-3 // own_layers)


def coarse_reach(own_layers):
    return -(-5 // own_layers)


def make_second_kernel(width, across, own_layers, fine_bound, coarse_bound):
    own = BEFORE_B // 2
    own_pairs = (own_layers + 1) // 2
    shift = (BEFORE - BEFORE_B) // 2
    near, far = full_reach(own_layers), coarse_reach(own_layers)
    steps = chebyshev_steps()
    spans = []
    for n in (3, 2, 1):
        low, high = BEFORE_B - n, BEFORE_B + own_layers + n - 1
        spans.append((low // 2, (high + 1) // 2 - low // 2))

    def second_kernel(*refs):
        messages = dict(zip(range(-near, near + 1), refs[: 2 * near + 1]))
        refs = refs[2 * near + 1 :]
        outer = [n for n in range(-far, far + 1) if abs(n) > near]
        edges = dict(zip(outer, refs[: len(outer)]))
        f, spread, collect, transfer_back, out, u, d, stiff, coarse = refs[len(outer) :]
        slab = Slab(width, across)

        def pair_of(pair, fetch):
            found = []
            for parity in range(2):
                layer = 2 * pair - BEFORE_B + parity
                device = layer // own_layers
                layer = layer - device * own_layers
                found.append((device, layer // 2, layer % 2))
            values = [fetch(device, q) for device, q, parity in found]
            if found[0][:2] == found[1][:2] or (values[0] is None and values[1] is None):
                return values[0]
            for parity in range(2):
                if values[parity] is None:
                    values[parity] = jnp.zeros_like(values[1 - parity])
                elif found[parity][2] != parity:
                    values[parity] = slab.lanes(values[parity], 2 * parity - 1)
            lane = lax.broadcasted_iota(jnp.int32, values[0].shape, 1)
            return jnp.where(lane % 2 == 0, values[0], values[1])

        u[...] = jnp.zeros(u.shape, jnp.float32)
        coarse[...] = jnp.zeros(coarse.shape, jnp.float32)
        d[...] = jnp.zeros(d.shape, jnp.float32)
        for pair in range(PAIRS_B):
            for i in range(3):
                whole = pair_of(pair, lambda n, q: messages[n][i, q] if n in messages else None)
                if whole is not None:
                    u[i, pair] = whole
            for n in range(7):

                def fetch(device, q, n=n):
                    if device in messages:
                        i, slot = ((n, 0), (n - 3, RESTRICTED_SLOT), (0, STIFF_SLOT))[n // 3]
                        return messages[device][i, q, slot : slot + 1, :]
                    return edges[device][q, n : n + 1, :] if device in edges else None

                line = pair_of(pair, fetch)
                if line is not None:
                    coarse[n, pair : pair + 1, :] = line
        stiff[...] = coarse[6]

        stiffness = coarse[6]
        keep_coarse = jnp.where(slab.bottom, 0.0, 1.0)
        start = [coarse[i] for i in range(3)]
        restricted = [coarse[3 + i] for i in range(3)]
        before = slab.coarse_force(start, stiffness)
        move = [(steps[0][1] / coarse_bound) * keep_coarse * restricted[i] for i in range(3)]
        level = [start[i] + move[i] for i in range(3)]
        for held, added in steps[1:]:
            force = slab.coarse_force(level, stiffness)
            for i in range(3):
                z = keep_coarse * (restricted[i] + before[i] - force[i])
                move[i] = held * move[i] + (added / coarse_bound) * z
                level[i] = level[i] + move[i]

        weights = [jnp.broadcast_to(transfer_back[:, n : n + 1], (32, width)) for n in range(8)]
        for i in range(3):
            change = slab.corners_of(level[i] - start[i])
            for pair in range(spans[0][0], min(spans[0][0] + spans[0][1] + 1, PAIRS_B)):
                lift = u[i, pair]
                for n, corner in enumerate(CORNERS):
                    lift = lift + weights[n] * change[corner][pair : pair + 1]
                u[i, pair] = lift

        slab.smooth(u, f, shift, d, stiff, spread, collect, spans, fine_bound)

        lower = lax.broadcasted_iota(jnp.int32, (width // 8, 8, 128), 1) < 4
        sides = []
        blank = jnp.zeros((29, width), jnp.float32)
        for q in range(2):
            ends_here = jnp.concatenate(
                [u[i, own + q] for i in range(3)]
                + [level[i][own + q : own + q + 1] for i in range(3)]
                + [blank],
                0,
            )
            sides.append(ends_here.T.reshape(width // 8, 8, 128))
        out[:, 0] = jnp.where(lower, sides[0], pltpu.roll(sides[1], 4, 1))
        out[:, 1] = jnp.where(lower, pltpu.roll(sides[0], 4, 1), sides[1])

    return second_kernel


def solution(mesh):
    rows_of, columns_of = mesh.shape["gx"], mesh.shape["gy"]
    devices = rows_of * columns_of
    own_layers = EZ // devices
    own_pairs = (own_layers + 1) // 2
    width = 4 * devices
    across = 2 * rows_of
    near, far = full_reach(own_layers), coarse_reach(own_layers)
    spread, collect, fine_bound = element_tables()
    coarse_bound = build_tables([0.0, 1.0], 2)[2]
    transfer, transfer_back = transfer_table()
    wide = pltpu.CompilerParams(vmem_limit_bytes=60 * 1024 * 1024)
    limit = pltpu.CompilerParams(vmem_limit_bytes=48 * 1024 * 1024)
    f32 = jnp.float32

    pack = pl.pallas_call(
        pack_kernel,
        out_shape=jax.ShapeDtypeStruct((devices, 8, SENT), f32),
        in_specs=[pl.BlockSpec(memory_space=pl.ANY)] * 5,
        out_specs=pl.BlockSpec(memory_space=pltpu.VMEM),
        scratch_shapes=[
            pltpu.VMEM((3, 6, 3, 384), f32),
            pltpu.VMEM((3, 6, 3, 384), f32),
            pltpu.VMEM((2, 1, EZ), f32),
            pltpu.VMEM((1, 1, 192), jnp.int32),
            pltpu.VMEM((384, 512), jnp.bfloat16),
            pltpu.VMEM((128, 384), f32),
            pltpu.VMEM((384, 128), f32),
            pltpu.VMEM((16, 160, 128), f32),
            pltpu.SemaphoreType.DMA((5,)),
        ],
        compiler_params=wide,
    )
    first = pl.pallas_call(
        make_first_kernel(width, across, own_layers, fine_bound),
        out_shape=(
            jax.ShapeDtypeStruct((3, own_pairs, 32, width), f32),
            jax.ShapeDtypeStruct((own_pairs, 8, width), f32),
            jax.ShapeDtypeStruct((3, PAIRS, 32, width), f32),
        ),
        scratch_shapes=[
            pltpu.VMEM((3, 8, 32, width), f32),
            pltpu.VMEM((3, 8, 32, width), f32),
            pltpu.VMEM((8, width), f32),
            pltpu.VMEM((3, 8, 8, width), f32),
            pltpu.VMEM((2, SENT, width), f32),
        ],
        compiler_params=limit,
    )
    second = pl.pallas_call(
        make_second_kernel(width, across, own_layers, fine_bound, coarse_bound),
        out_shape=jax.ShapeDtypeStruct((devices // 2, 2, 8, 128), f32),
        scratch_shapes=[
            pltpu.VMEM((3, PAIRS_B + 2, 32, width), f32),
            pltpu.VMEM((3, PAIRS_B, 32, width), f32),
            pltpu.VMEM((PAIRS_B, width), f32),
            pltpu.VMEM((7, PAIRS_B, width), f32),
        ],
        compiler_params=limit,
    )
    unpack = pl.pallas_call(
        unpack_kernel,
        out_shape=(
            jax.ShapeDtypeStruct((3, 6, 3, 384), f32),
            jax.ShapeDtypeStruct((3, 2, 1, EZ), f32),
        ),
        scratch_shapes=[pltpu.VMEM((2, 128, 128), f32), pltpu.VMEM((384, 128), f32)],
        compiler_params=limit,
    )
    everyone = ("gy", "gx")

    def from_device(block, distance):
        place = [k % rows_of * columns_of + k // rows_of for k in range(devices)]
        route = [(place[(k + distance) % devices], place[k]) for k in range(devices)]
        return lax.ppermute(block, ("gx", "gy"), route)

    def body(initial, forcing, modulus, solid_list):
        sent = pack(initial, forcing, modulus, solid_list, jnp.asarray(pack_table()))
        arrived = lax.all_to_all(sent, everyone, 0, 0, tiled=True)
        message, edge, load = first(
            arrived.reshape(devices // 2, 2, 8, SENT),
            jnp.asarray(spread),
            jnp.asarray(collect),
            jnp.asarray(transfer),
        )
        messages = [
            from_device(message, n) if n else message for n in range(-near, near + 1)
        ]
        edges = [from_device(edge, n) for n in range(-far, far + 1) if abs(n) > near]
        result = second(
            *messages,
            *edges,
            load,
            jnp.asarray(spread),
            jnp.asarray(collect),
            jnp.asarray(transfer_back),
        )
        back = lax.all_to_all(result.reshape(devices, 8, 128), everyone, 0, 0, tiled=True)
        return unpack(back, jnp.asarray(unpack_table()))

    placed = (
        P(None, "gx", "gy", None),
        P(None, "gx", "gy", None),
        P("gx", "gy", None),
        P("gx", "gy", None),
    )
    return jax.shard_map(
        body,
        mesh=mesh,
        in_specs=placed,
        out_specs=(P(None, "gx", "gy", None), P(None, "gx", "gy", None)),
        check_vma=False,
    )
```

```python
import functools
import math

import jax
import jax.numpy as jnp
import numpy as np
from jax import lax
from jax.experimental import pallas as pl
from jax.experimental.pallas import tpu as pltpu
from jax.sharding import PartitionSpec as P

CHEB = 3
EZ = 128

element_span = 20.0
lame_ratio = 4.0
rest_ratio = 1.25
modulus_top = 2.0
spectrum_floor = 0.05
interval_centre = (1.0 + spectrum_floor) / 2.0
interval_radius = (1.0 - spectrum_floor) / 2.0
interval_ratio = interval_centre / interval_radius
inner_anchors = (0.5 - 0.5 / math.sqrt(5.0), 0.5 + 0.5 / math.sqrt(5.0))

BEFORE = 4
PAIRS = 6
BEFORE_B = 6
PAIRS_B = 8
BLOCK = 84
SENT = 512

SLOTS = [
    (0, 0, 0), (1, 0, 0), (2, 0, 0), (0, 1, 0), (0, 2, 0), (0, 0, 1), (0, 0, 2), None,
    (0, 1, 1), (0, 1, 2), (0, 2, 1), (0, 2, 2), (1, 0, 1), (1, 0, 2), (2, 0, 1), (2, 0, 2),
    (1, 1, 0), (1, 2, 0), (2, 1, 0), (2, 2, 0), (1, 1, 1), (1, 1, 2), (1, 2, 1), (1, 2, 2),
    None, None, None, None, (2, 1, 1), (2, 1, 2), (2, 2, 1), (2, 2, 2),
]
TWIN = 7
RESTRICTED_SLOT = 24
STIFF_SLOT = 25
OWN_SHIFT, SHIFT_X, SHIFT_Y, SHIFT_Z = (0, 0, 0), (1, 0, 0), (0, 1, 0), (0, 0, 1)
ELEMENT_ROWS = (
    [(slot, OWN_SHIFT) for slot in range(24)]
    + [(slot, SHIFT_Z) for slot in range(16, 20)]
    + [(slot, OWN_SHIFT) for slot in range(28, 32)]
    + [(slot, SHIFT_X) for slot in range(7)] + [None]
    + [(slot, SHIFT_Y) for slot in range(7)] + [(0, (0, 1, 1))]
    + [(slot, SHIFT_Z) for slot in range(7)] + [(0, (1, 0, 1))]
    + [(slot, SHIFT_X) for slot in range(8, 12)] + [(slot, SHIFT_Y) for slot in range(12, 16)]
    + [(0, (1, 1, 1)), (1, (0, 1, 1)), (2, (0, 1, 1)), (3, (1, 0, 1)), (4, (1, 0, 1))]
    + [(5, (1, 1, 0)), (6, (1, 1, 0)), (0, (1, 1, 0))]
)
ROWS = len(ELEMENT_ROWS)
DEPTH = 80
CORNERS = [(a, b, c) for a in range(2) for b in range(2) for c in range(2)]


def gauss_rule(point_count):
    if point_count == 2:
        offset = 1.0 / math.sqrt(3.0)
        points = [-offset, offset]
        weights = [1.0, 1.0]
    else:
        inner = math.sqrt(3.0 / 7.0 - 2.0 / 7.0 * math.sqrt(6.0 / 5.0))
        outer = math.sqrt(3.0 / 7.0 + 2.0 / 7.0 * math.sqrt(6.0 / 5.0))
        heavy = (18.0 + math.sqrt(30.0)) / 36.0
        light = (18.0 - math.sqrt(30.0)) / 36.0
        points = [-outer, -inner, inner, outer]
        weights = [light, heavy, heavy, light]
    return (np.array(points), np.array(weights))


def lagrange_tables(anchors, samples):
    values = np.zeros((len(samples), len(anchors)))
    slopes = np.zeros((len(samples), len(anchors)))
    for sample_index, sample in enumerate(samples):
        for anchor_index, anchor in enumerate(anchors):
            others = [
                location
                for location_index, location in enumerate(anchors)
                if location_index != anchor_index
            ]
            product = 1.0
            for location in others:
                product = product * (sample - location) / (anchor - location)
            values[sample_index, anchor_index] = product
            derivative = 0.0
            for skipped in range(len(others)):
                summand = 1.0 / (anchor - others[skipped])
                for kept_index in range(len(others)):
                    if kept_index != skipped:
                        summand = (
                            summand * (sample - others[kept_index]) / (anchor - others[kept_index])
                        )
                derivative = derivative + summand
            slopes[sample_index, anchor_index] = derivative
    return (values, slopes)


def outer_three(first, second, third):
    return (
        first[:, None, None, :, None, None]
        * second[None, :, None, None, :, None]
        * third[None, None, :, None, None, :]
    )


def build_tables(anchors, point_count):
    raw_points, raw_weights = gauss_rule(point_count)
    samples = (raw_points + 1.0) / 2.0
    weights = raw_weights / 2.0
    basis_values, slopes = lagrange_tables(anchors, samples)
    quad_total = point_count**3
    nodal_count = len(anchors) ** 3
    derivative_one = outer_three(slopes, basis_values, basis_values).reshape(
        quad_total, nodal_count
    )
    derivative_two = outer_three(basis_values, slopes, basis_values).reshape(
        quad_total, nodal_count
    )
    derivative_three = outer_three(basis_values, basis_values, slopes).reshape(
        quad_total, nodal_count
    )
    stacked = np.stack([derivative_one, derivative_two, derivative_three]) / element_span
    volume = (weights[:, None, None] * weights[None, :, None] * weights[None, None, :]).reshape(
        -1
    ) * element_span**3
    forward = stacked.reshape(3 * quad_total, nodal_count)
    backward = (stacked * volume[None, :, None]).reshape(3 * quad_total, nodal_count).T
    weighted = stacked * volume[None, :, None]
    laplace = weighted[0].T @ stacked[0] + weighted[1].T @ stacked[1] + weighted[2].T @ stacked[2]
    matrix = np.zeros((nodal_count, 3, nodal_count, 3))
    for first in range(3):
        for second in range(3):
            block = weighted[second].T @ stacked[first] + (lame_ratio - 1.0) * (
                weighted[first].T @ stacked[second]
            )
            if first == second:
                block = block + laplace
            matrix[:, first, :, second] = block
    matrix = matrix.reshape(3 * nodal_count, 3 * nodal_count)
    vector = 1.5 + np.cos(1.3 * np.arange(3 * nodal_count))
    for repeat in range(200):
        vector = matrix @ vector
        vector = vector / np.sqrt(vector @ vector)
    largest = vector @ (matrix @ vector)
    return (forward, backward, float(4.0 * modulus_top * 1.1 * largest))


def row_nodes():
    nodes = []
    for entry in ELEMENT_ROWS:
        slot = SLOTS[entry[0]] if entry else None
        if slot is None or any(s and n for s, n in zip(entry[1], slot)):
            nodes.append(None)
        else:
            a, b, c = (3 * s + n for s, n in zip(entry[1], slot))
            nodes.append(16 * a + 4 * b + c)
    return nodes


def halves(matrix):
    whole = np.asarray(matrix, np.float32)
    high = whole.astype(jnp.bfloat16)
    low = (whole - high.astype(np.float32)).astype(jnp.bfloat16)
    return high, low


def element_tables():
    forward, backward, bound = build_tables([0.0, inner_anchors[0], inner_anchors[1], 1.0], 4)
    spread = np.zeros((forward.shape[0], DEPTH))
    collect = np.zeros((ROWS, backward.shape[1]))
    for row, node in enumerate(row_nodes()):
        if node is not None:
            spread[:, row] = forward[:, node]
            collect[row, :] = backward[node, :]
    spread_high, spread_low = halves(spread)
    collect_high, collect_low = halves(collect)
    return (
        np.concatenate([spread_high, spread_high, spread_low], 1),
        np.concatenate([collect_high, collect_low], 0),
        bound,
    )


def transfer_table():
    table = np.zeros((8, 32))
    reach = (0.0, inner_anchors[0], inner_anchors[1])
    for row, corner in enumerate(CORNERS):
        for column, slot in enumerate(SLOTS):
            if slot is not None:
                weight = 1.0
                for side, node in zip(corner, slot):
                    weight = weight * (reach[node] if side else 1.0 - reach[node])
                table[row, column] = weight
    back = table.T.copy()
    back[TWIN] = back[0]
    return table.T.astype(np.float32), back.astype(np.float32)


def chebyshev_steps():
    steps = [(0.0, 1.0 / interval_centre)]
    ratio_now = 1.0 / interval_ratio
    for sweep in range(1, CHEB):
        ratio_next = 1.0 / (2.0 * interval_ratio - ratio_now)
        steps.append((ratio_next * ratio_now, 2.0 * ratio_next / interval_radius))
        ratio_now = ratio_next
    return steps


def stack_row(field, component, layer, b):
    return field * 54 + component * 18 + layer * 3 + b


def block_column(component, slot):
    return 72 + 4 * component + slot - 28 if slot >= 24 else 24 * component + slot


def pack_table():
    table = np.zeros((3, 128, 2, 2, 128), np.float32)
    for field in range(2):
        for x in range(2):
            for component in range(3):
                for column, slot in enumerate(SLOTS):
                    if slot is not None:
                        a, b, c = slot
                        row = stack_row(field, component, 3 * x + a, b)
                        table[c, row, field, x, block_column(component, column)] = 1.0
            table[0, 108 + x, 0, x, TWIN] = 1.0
    return table.reshape(384, 512).astype(jnp.bfloat16)


def unpack_table():
    table = np.zeros((2, 128, 3, 128), np.float32)
    for x in range(2):
        for component in range(3):
            for column, slot in enumerate(SLOTS):
                if slot is not None:
                    a, b, c = slot
                    row = stack_row(0, component, 3 * x + a, b)
                    table[x, component * 32 + column, c, row] = 1.0
            table[x, 96 + component, 0, 54 + 2 * component + x] = 1.0
    return table.reshape(256, 384).astype(jnp.bfloat16)


def exact_pick(values, table):
    high = values.astype(jnp.bfloat16)
    rest = values - high.astype(jnp.float32)
    middle = rest.astype(jnp.bfloat16)
    low = (rest - middle.astype(jnp.float32)).astype(jnp.bfloat16)
    count = values.shape[0]
    parts = jnp.dot(
        jnp.concatenate([high, middle, low], 0), table, preferred_element_type=jnp.float32
    )
    return parts[:count] + (parts[count : 2 * count] + parts[2 * count :])


def ring_order(rows_of, columns_of):
    if (rows_of, columns_of) != (4, 8):
        return list(range(rows_of * columns_of))
    order = []
    for z in range(4):
        for x in range(2):
            for y in range(2):
                chip = (z, 7 - z, 15 - z, 8 + z)[2 * x + y]
                order += [2 * chip, 2 * chip + 1]
    return order


def region_shift(own_layers):
    return 2 if own_layers == 4 else 0


def pack_kernel(
    order,
    initial_at, forcing_at, modulus_at, listing_at, table_at, out,
    initial, forcing, modulus, listing, table, rows, turned, places, ready,
):
    devices = out.shape[0]
    own_layers = EZ // devices
    sources = (listing_at, modulus_at, initial_at, forcing_at, table_at)
    copies = [
        pltpu.make_async_copy(source, here, ready.at[n])
        for n, (source, here) in enumerate(
            zip(sources, (listing, modulus, initial, forcing, table))
        )
    ]
    for copy in copies:
        copy.start()
    rows[108:128, :] = jnp.zeros((20, 384), jnp.float32)
    copies[0].wait()
    copies[1].wait()
    listed = listing[0].astype(jnp.float32)
    listed = jnp.concatenate([listed, jnp.full((1, 64), 256.0, jnp.float32)], 1)
    listed = jnp.broadcast_to(listed, (128, 256)).T
    lanes = lax.broadcasted_iota(jnp.int32, (256, 128), 1).astype(jnp.float32)
    row_at = lax.broadcasted_iota(jnp.int32, (128, 128), 0)
    stiff = jnp.zeros((128, 128), jnp.float32)
    for x in range(2):
        hit = jnp.max(jnp.where(listed == lanes + 128.0 * x, 1.0, 0.0), axis=0, keepdims=True)
        stiff = jnp.where(row_at == 108 + x, hit * modulus[x], stiff)
    copies[2].wait()
    copies[3].wait()
    for field, source in enumerate((initial, forcing)):
        for component in range(3):
            for layer in range(6):
                at = stack_row(field, component, layer, 0)
                rows[at : at + 3, :] = source[component, layer]
    for part in range(3):
        span = slice(128 * part, 128 * part + 128)
        turned[span, :] = rows[:, span].T
    picked = [turned[pl.ds(c, 128, stride=3), :] for c in range(3)]
    picked[0] = picked[0] + stiff.T
    copies[4].wait()
    wide = exact_pick(jnp.concatenate(picked, 1), table[...])
    lane = lax.broadcasted_iota(jnp.int32, (128, 128), 1)
    for block in range(4):
        here = wide[:, 128 * block : 128 * block + 128]
        tiles = [None] * (SENT // 128)
        for pair in range(PAIRS):
            first = BLOCK * pair
            moved = here if pair == 0 else pltpu.roll(here, 128 - 2 * pair, 0)
            if first % 128:
                moved = pltpu.roll(moved, first % 128, 1)
            for tile in range(first // 128, (first + BLOCK - 1) // 128 + 1):
                before = tiles[tile]
                if before is None:
                    tiles[tile] = moved
                else:
                    tiles[tile] = jnp.where(lane >= first - 128 * tile, moved, before)
        for tile in range(SENT // 128):
            at = 4 * block + tile
            places[at, 16:144, :] = tiles[tile]
            places[at, 0:16, :] = tiles[tile][112:128]
            places[at, 144:160, :] = tiles[tile][0:16]
    for block in range(4):
        for parity in range(2):
            for tile in range(SENT // 128):
                at, span = 4 * block + tile, slice(128 * tile, 128 * tile + 128)
                first = 16 - BEFORE + parity
                if order == sorted(order):
                    out[:, 2 * block + parity, span] = places[
                        at, pl.ds(first, devices, stride=own_layers), :
                    ]
                    continue
                for device, k in enumerate(order):
                    row = first + own_layers * k
                    out[device, 2 * block + parity : 2 * block + parity + 1, span] = places[
                        at, row : row + 1, :
                    ]


def unpack_kernel(order, arrived, table, out, coarse_out, layers, turned):
    devices = arrived.shape[0]
    own_layers = EZ // devices
    for x in range(2):
        for layer in range(own_layers):
            row = (layer // 2) * 4 + x * 2 + layer % 2
            if order == sorted(order):
                layers[x, pl.ds(layer, devices, stride=own_layers), :] = arrived[:, row, :]
                continue
            for device, k in enumerate(order):
                at = (region_shift(own_layers) + own_layers * k + layer) % EZ
                layers[x, at : at + 1, :] = arrived[device, row : row + 1, :]
    wide = exact_pick(jnp.concatenate([layers[0], layers[1]], 1), table[...])
    for c in range(3):
        turned[pl.ds(c, 128, stride=3), :] = wide[:, 128 * c : 128 * c + 128]
    for part in range(3):
        span = slice(128 * part, 128 * part + 128)
        back = turned[span, :].T
        for component in range(3):
            for layer in range(6):
                at = stack_row(0, component, layer, 0)
                out[component, layer, :, span] = back[at : at + 3, :]
    back = wide[:, 0:128].T
    for component in range(3):
        for x in range(2):
            at = 54 + 2 * component + x
            coarse_out[component, x] = back[at : at + 1, :]


def cofactor_rows(deform):
    return [
        [
            deform[(row_at + 1) % 3][(column + 1) % 3] * deform[(row_at + 2) % 3][(column + 2) % 3]
            - deform[(row_at + 1) % 3][(column + 2) % 3]
            * deform[(row_at + 2) % 3][(column + 1) % 3]
            for column in range(3)
        ]
        for row_at in range(3)
    ]


def point_stress(deform, stiffness, stiffness_four):
    cofactors = cofactor_rows(deform)
    jacobian = (
        deform[0][0] * cofactors[0][0]
        + deform[0][1] * cofactors[0][1]
        + deform[0][2] * cofactors[0][2]
    )
    pressure = stiffness_four * (jacobian - rest_ratio)
    return [
        [stiffness * deform[i][d] + pressure * cofactors[i][d] for d in range(3)] for i in range(3)
    ]


coarse_samples = [0.5 - 0.5 / math.sqrt(3.0), 0.5 + 0.5 / math.sqrt(3.0)]
two = range(2)


def at_points(low, high):
    change = high - low
    return [low + s * change for s in coarse_samples], change * (1.0 / element_span)


def ends_of(first, second):
    high = coarse_samples[0] * first + coarse_samples[1] * second
    return [first + second - high, high]


def high_low(values):
    high = values.astype(jnp.bfloat16)
    return high, (values - high.astype(jnp.float32)).astype(jnp.bfloat16)


class Slab:
    def __init__(self, width, across):
        self.width = width
        self.y_step = 2 * across
        lane = lax.broadcasted_iota(jnp.int32, (8, width), 1)
        x = (lane // 2) % across
        self.bottom, self.top, self.even = x == 0, x == across - 1, lane % 2 == 0
        self.row = lax.broadcasted_iota(jnp.int32, (8, width), 0)
        row = lax.broadcasted_iota(jnp.int32, (32, width), 0)
        lane = lax.broadcasted_iota(jnp.int32, (32, width), 1)
        on_face = (row == 0) | ((row >= 3) & (row <= 11))
        self.keep = jnp.where(on_face & ((lane // 2) % across == 0), 0.0, 1.0)

    def lanes(self, v, step):
        return pltpu.roll(v, step % self.width, 1)

    def next_x(self, v):
        return jnp.where(self.top, 0.0, self.lanes(v, -2))

    def next_y(self, v):
        return self.lanes(v, -self.y_step)

    def next_z(self, v, ahead):
        return jnp.where(self.even, self.lanes(v, -1), self.lanes(ahead, 1))

    def onto_x(self, v):
        return jnp.where(self.bottom, 0.0, self.lanes(v, 2))

    def onto_y(self, v):
        return self.lanes(v, self.y_step)

    def gather(self, here, ahead):
        row = self.row
        g0, g1, g2, g3 = here[0:8], here[8:16], here[16:24], here[24:32]
        z0 = self.next_z(g0, ahead[0:8])
        z2 = self.next_z(g2, ahead[16:24])
        y0 = self.next_y(g0)
        yz, xz, xy = self.next_y(z0), self.next_x(z0), self.next_x(y0)
        edges = jnp.where(row <= 2, yz, jnp.where(row <= 4, xz, xy))
        return jnp.concatenate(
            [
                g0,
                g1,
                g2,
                jnp.where(row < 4, z2, g3),
                self.next_x(g0),
                jnp.where(row == 7, yz, y0),
                jnp.where(row == 7, xz, z0),
                jnp.where(row < 4, self.next_x(g1), self.next_y(g1)),
                jnp.where(row == 0, self.next_x(yz), edges),
                jnp.zeros_like(g0),
            ],
            0,
        )

    def scatter(self, part, behind):
        row = self.row
        g0, g1, g2, g3, x0, y0, z0, sides, edges = (part[8 * n : 8 * n + 8] for n in range(9))
        edges_x = self.onto_x(edges)
        yz = jnp.where(row == 0, edges_x, jnp.where(row == 7, y0, edges))
        yz = jnp.where((row <= 2) | (row == 7), yz, 0.0)
        z0 = jnp.where(row == 7, self.onto_x(z0), z0)
        z0 = z0 + jnp.where((row == 3) | (row == 4), edges_x, 0.0) + self.onto_y(yz)
        y0 = jnp.where(row == 7, edges_x, y0 + jnp.where(row >= 5, edges_x, 0.0))
        z2 = g3
        own0 = g0 + self.onto_x(x0) + self.onto_y(y0)
        own0 = own0 + jnp.where(self.even, behind[0], self.lanes(z0, 1))
        own1 = g1 + jnp.where(row < 4, self.onto_x(sides), self.onto_y(sides))
        share2 = jnp.where(self.even, behind[1], self.lanes(z2, 1))
        own2 = g2 + jnp.where(row < 4, share2, 0.0)
        own3 = jnp.where(row < 4, 0.0, g3)
        own0 = own0 + jnp.where(row == 0, pltpu.roll(own0, 1, 0), 0.0)
        own0 = jnp.where(row == 7, pltpu.roll(own0, 7, 0), own0)
        moved = (self.lanes(z0, -1), self.lanes(z2, -1))
        return jnp.concatenate([own0, own1, own2, own3], 0), moved

    def apply(self, u, stiff, spread, collect, first, count, finish):
        width = self.width

        def step(index, carry):
            pair = first + 2 * index
            blocks = [
                self.gather(u[i, pair + q], u[i, pair + q + 1])
                for i in range(3)
                for q in range(2)
            ]
            high, low = high_low(jnp.concatenate(blocks, 1))
            gradient = jnp.dot(
                spread[...],
                jnp.concatenate([high, low, high], 0),
                preferred_element_type=jnp.float32,
            )
            stiffness = jnp.concatenate([stiff[pl.ds(pair + q, 1), :] for q in range(2)], 1)
            deform = [
                [
                    gradient[64 * e : 64 * e + 64, 2 * width * i : 2 * width * (i + 1)]
                    + (1.0 if i == e else 0.0)
                    for e in range(3)
                ]
                for i in range(3)
            ]
            stress = point_stress(deform, stiffness, lame_ratio * stiffness)
            stress = jnp.concatenate(
                [jnp.concatenate([stress[i][e] for i in range(3)], 1) for e in range(3)], 0
            )
            high, low = high_low(stress)
            force = jnp.dot(collect[...], high, preferred_element_type=jnp.float32)
            force = force[0:ROWS] + (
                force[ROWS:] + jnp.dot(collect[0:ROWS], low, preferred_element_type=jnp.float32)
            )
            carry = list(carry)
            totals = [[], []]
            for q in range(2):
                for i in range(3):
                    at = (2 * i + q) * width
                    total, carry[i] = self.scatter(force[:, at : at + width], carry[i])
                    totals[q].append(total)
            for q in range(2):
                finish(pair + q, totals[q])
            return tuple(carry)

        none = jnp.zeros((8, width), jnp.float32)
        lax.fori_loop(0, (count + 1) // 2, step, tuple((none, none) for i in range(3)))

    def smooth(self, u, f, f_shift, d, stiff, spread, collect, spans, bound):
        for (first, count), (held, added) in zip(spans, chebyshev_steps()):

            def finish(pair, forces, held=held, added=added):
                for i in range(3):
                    z = (added / bound) * self.keep * (f[i, pair + f_shift] - forces[i])
                    move = held * d[i, pair] + z if held else z
                    d[i, pair] = move
                    u[i, pair] = u[i, pair] + move

            self.apply(u, stiff, spread, collect, first, count, finish)

    def coarse_next_z(self, v):
        return self.next_z(v, pltpu.roll(v, 7, 0))

    def coarse_onto_z(self, v):
        return jnp.where(self.even, pltpu.roll(self.lanes(v, -1), 1, 0), self.lanes(v, 1))

    def corners_of(self, v):
        found = {(0, 0, 0): v, (0, 0, 1): self.coarse_next_z(v)}
        for c in range(2):
            found[0, 1, c] = self.next_y(found[0, 0, c])
        for b in range(2):
            for c in range(2):
                found[1, b, c] = self.next_x(found[0, b, c])
        return found

    def assemble(self, part):
        line = {
            (a, b): part[a, b, 0] + self.coarse_onto_z(part[a, b, 1])
            for a in range(2)
            for b in range(2)
        }
        face = [line[a, 0] + self.onto_y(line[a, 1]) for a in range(2)]
        return face[0] + self.onto_x(face[1])

    def coarse_force(self, values, stiffness):
        grads = []
        for i in range(3):
            v = self.corners_of(values[i])
            vz, sz = {}, {}
            for a in two:
                for b in two:
                    vz[a, b], sz[a, b] = at_points(v[a, b, 0], v[a, b, 1])
            vv, vs, sv = {}, {}, {}
            for a in two:
                for k in two:
                    vv[a, k], vs[a, k] = at_points(vz[a, 0][k], vz[a, 1][k])
                sv[a], unused = at_points(sz[a, 0], sz[a, 1])
            dx, dy, dz = {}, {}, {}
            for k in two:
                for j in two:
                    dx[j, k] = (vv[1, k][j] - vv[0, k][j]) * (1.0 / element_span)
                line, unused = at_points(vs[0, k], vs[1, k])
                for h in two:
                    dy[h, k] = line[h]
            for j in two:
                line, unused = at_points(sv[0][j], sv[1][j])
                for h in two:
                    dz[h, j] = line[h]
            grads.append((dx, dy, dz))
        weight = element_span**2 / 8.0
        scaled = weight * stiffness
        scaled_four = lame_ratio * scaled
        sums = [({}, {}, {}) for i in range(3)]

        def add(table, key, value):
            table[key] = table[key] + value if key in table else value

        for h in two:
            for j in two:
                for k in two:
                    deform = [
                        [grads[i][0][j, k], grads[i][1][h, k], grads[i][2][h, j]]
                        for i in range(3)
                    ]
                    for i in range(3):
                        deform[i][i] = deform[i][i] + 1.0
                    stress = point_stress(deform, scaled, scaled_four)
                    for i in range(3):
                        add(sums[i][0], (j, k), stress[i][0])
                        add(sums[i][1], (h, k), stress[i][1])
                        add(sums[i][2], (h, j), stress[i][2])

        forces = []
        for i in range(3):
            part = {}
            qx, qy, qz = sums[i]
            along_z = [ends_of(qx[j, 0], qx[j, 1]) for j in two]
            for c in two:
                line = ends_of(along_z[0][c], along_z[1][c])
                for b in two:
                    part[0, b, c] = -line[b]
                    part[1, b, c] = line[b]
            along_z = [ends_of(qy[h, 0], qy[h, 1]) for h in two]
            for c in two:
                line = ends_of(along_z[0][c], along_z[1][c])
                for a in two:
                    part[a, 0, c] = part[a, 0, c] - line[a]
                    part[a, 1, c] = part[a, 1, c] + line[a]
            along_y = [ends_of(qz[h, 0], qz[h, 1]) for h in two]
            for b in two:
                line = ends_of(along_y[0][b], along_y[1][b])
                for a in two:
                    part[a, b, 0] = part[a, b, 0] - line[a]
                    part[a, b, 1] = part[a, b, 1] + line[a]
            forces.append(self.assemble(part))
        return forces


def make_first_kernel(width, across, own_layers, fine_bound):
    own = BEFORE // 2
    own_pairs = (own_layers + 1) // 2
    spans = []
    for n in (4, 3, 2, 1):
        low, high = BEFORE - n, BEFORE + own_layers + n - 1
        spans.append((low // 2, (high + 1) // 2 - low // 2))

    def first_kernel(
        arrived, spread, collect, transfer, message, edge, f, u, d, stiff, shares, turned
    ):
        slab = Slab(width, across)
        row = slab.row
        u[...] = jnp.zeros(u.shape, jnp.float32)
        f[...] = jnp.zeros(f.shape, jnp.float32)
        shares[...] = jnp.zeros(shares.shape, jnp.float32)
        stiff[...] = jnp.zeros(stiff.shape, jnp.float32)
        lower = lax.broadcasted_iota(jnp.int32, (width // 8, 8, 128), 1) < 4
        for tile in range(SENT // 128):
            span = slice(128 * tile, 128 * tile + 128)
            first, second = arrived[:, 0, :, span], arrived[:, 1, :, span]
            value = jnp.where(lower, first, pltpu.roll(second, 4, 1))
            load = jnp.where(lower, pltpu.roll(first, 4, 1), second)
            turned[0, span, :] = value.reshape(width, 128).T
            turned[1, span, :] = load.reshape(width, 128).T
        for field, target in enumerate((u, f)):
            for pair in range(PAIRS):
                base = BLOCK * pair
                for i in range(3):
                    parts = [
                        turned[field, base + 24 * i + 8 * n : base + 24 * i + 8 * n + 8, :]
                        for n in range(3)
                    ]
                    inner = turned[field, base + 68 + 4 * i : base + 76 + 4 * i, :]
                    if field == 0 and i == 0:
                        stiff[pair : pair + 1, :] = parts[0][TWIN : TWIN + 1]
                    parts[0] = jnp.where(row == TWIN, pltpu.roll(parts[0], TWIN, 0), parts[0])
                    parts.append(jnp.where(row < 4, 0.0, inner))
                    whole = jnp.concatenate(parts, 0)
                    target[i, pair] = whole * slab.keep if field == 0 else whole

        slab.smooth(u, f, 0, d, stiff, spread, collect, spans[0:3], fine_bound)

        weights = [jnp.broadcast_to(transfer[:, n : n + 1], (32, width)) for n in range(8)]

        def restrict(pair, forces):
            for i in range(3):
                rest = slab.keep * (f[i, pair] - forces[i])
                for n in range(8):
                    part = rest * weights[n]
                    part = (part[0:8] + part[8:16]) + (part[16:24] + part[24:32])
                    shares[i, n, pl.ds(pair, 1), :] = jnp.sum(part, axis=0, keepdims=True)

        slab.apply(u, stiff, spread, collect, *spans[3], restrict)

        restricted = [
            slab.assemble({corner: shares[i, n] for n, corner in enumerate(CORNERS)})
            for i in range(3)
        ]
        for q in range(own_pairs):
            hard = stiff[own + q : own + q + 1, :]
            for i in range(3):
                message[i, q] = u[i, own + q]
                message[i, q, RESTRICTED_SLOT : RESTRICTED_SLOT + 1, :] = restricted[i][
                    own + q : own + q + 1
                ]
                edge[q, i : i + 1, :] = u[i, own + q, 0:1, :]
                edge[q, 3 + i : 4 + i, :] = restricted[i][own + q : own + q + 1]
            message[0, q, STIFF_SLOT : STIFF_SLOT + 1, :] = hard
            edge[q, 6:8, :] = jnp.broadcast_to(hard, (2, width))

    return first_kernel


def sources_of(own_layers):
    shift = region_shift(own_layers)
    whole = range((shift - 3) // own_layers, (shift + own_layers + 2) // own_layers + 1)
    coarse = range((shift - 5) // own_layers, (shift + own_layers + 4) // own_layers + 1)
    return list(whole), [n for n in coarse if n not in whole]


def make_second_kernel(width, across, own_layers, fine_bound, coarse_bound):
    own = BEFORE_B // 2
    own_pairs = (own_layers + 1) // 2
    first_layer = region_shift(own_layers) - BEFORE_B
    shift = (BEFORE + first_layer) // 2
    whole, outer = sources_of(own_layers)
    steps = chebyshev_steps()
    spans = []
    for n in (3, 2, 1):
        low, high = BEFORE_B - n, BEFORE_B + own_layers + n - 1
        spans.append((low // 2, (high + 1) // 2 - low // 2))

    def second_kernel(*refs):
        messages = dict(zip(whole, refs))
        refs = refs[len(whole) :]
        edges = dict(zip(outer, refs))
        f, spread, collect, transfer_back, out, u, d, stiff, coarse = refs[len(outer) :]
        slab = Slab(width, across)

        def pair_of(pair, fetch):
            found = []
            for parity in range(2):
                layer = 2 * pair + first_layer + parity
                device = layer // own_layers
                layer = layer - device * own_layers
                found.append((device, layer // 2, layer % 2))
            values = [fetch(device, q) for device, q, parity in found]
            if found[0][:2] == found[1][:2] or (values[0] is None and values[1] is None):
                return values[0]
            for parity in range(2):
                if values[parity] is None:
                    values[parity] = jnp.zeros_like(values[1 - parity])
                elif found[parity][2] != parity:
                    values[parity] = slab.lanes(values[parity], 2 * parity - 1)
            lane = lax.broadcasted_iota(jnp.int32, values[0].shape, 1)
            return jnp.where(lane % 2 == 0, values[0], values[1])

        u[...] = jnp.zeros(u.shape, jnp.float32)
        coarse[...] = jnp.zeros(coarse.shape, jnp.float32)
        d[...] = jnp.zeros(d.shape, jnp.float32)
        for pair in range(PAIRS_B):
            for i in range(3):
                block = pair_of(pair, lambda n, q: messages[n][i, q] if n in messages else None)
                if block is not None:
                    u[i, pair] = block
            for n in range(7):

                def fetch(device, q, n=n):
                    if device in messages:
                        i, slot = ((n, 0), (n - 3, RESTRICTED_SLOT), (0, STIFF_SLOT))[n // 3]
                        return messages[device][i, q, slot : slot + 1, :]
                    return edges[device][q, n : n + 1, :] if device in edges else None

                line = pair_of(pair, fetch)
                if line is not None:
                    coarse[n, pair : pair + 1, :] = line
        stiff[...] = coarse[6]

        stiffness = coarse[6]
        keep_coarse = jnp.where(slab.bottom, 0.0, 1.0)
        start = [coarse[i] for i in range(3)]
        restricted = [coarse[3 + i] for i in range(3)]
        before = slab.coarse_force(start, stiffness)
        move = [(steps[0][1] / coarse_bound) * keep_coarse * restricted[i] for i in range(3)]
        level = [start[i] + move[i] for i in range(3)]
        for held, added in steps[1:]:
            force = slab.coarse_force(level, stiffness)
            for i in range(3):
                z = keep_coarse * (restricted[i] + before[i] - force[i])
                move[i] = held * move[i] + (added / coarse_bound) * z
                level[i] = level[i] + move[i]

        weights = [jnp.broadcast_to(transfer_back[:, n : n + 1], (32, width)) for n in range(8)]
        for i in range(3):
            change = slab.corners_of(level[i] - start[i])
            for pair in range(spans[0][0], min(spans[0][0] + spans[0][1] + 1, PAIRS_B)):
                lift = u[i, pair]
                for n, corner in enumerate(CORNERS):
                    lift = lift + weights[n] * change[corner][pair : pair + 1]
                u[i, pair] = lift

        slab.smooth(u, f, shift, d, stiff, spread, collect, spans, fine_bound)

        lower = lax.broadcasted_iota(jnp.int32, (width // 8, 8, 128), 1) < 4
        sides = []
        blank = jnp.zeros((29, width), jnp.float32)
        for q in range(2):
            ends_here = jnp.concatenate(
                [u[i, own + q] for i in range(3)]
                + [level[i][own + q : own + q + 1] for i in range(3)]
                + [blank],
                0,
            )
            sides.append(ends_here.T.reshape(width // 8, 8, 128))
        out[:, 0] = jnp.where(lower, sides[0], pltpu.roll(sides[1], 4, 1))
        out[:, 1] = jnp.where(lower, pltpu.roll(sides[0], 4, 1), sides[1])

    return second_kernel


def solution(mesh):
    rows_of, columns_of = mesh.shape["gx"], mesh.shape["gy"]
    devices = rows_of * columns_of
    order = ring_order(rows_of, columns_of)
    own_layers = EZ // devices
    own_pairs = (own_layers + 1) // 2
    width = 4 * devices
    across = 2 * rows_of
    whole, outer = sources_of(own_layers)
    spread, collect, fine_bound = element_tables()
    coarse_bound = build_tables([0.0, 1.0], 2)[2]
    transfer, transfer_back = transfer_table()
    wide = pltpu.CompilerParams(vmem_limit_bytes=60 * 1024 * 1024)
    limit = pltpu.CompilerParams(vmem_limit_bytes=48 * 1024 * 1024)
    f32 = jnp.float32

    pack = pl.pallas_call(
        functools.partial(pack_kernel, order),
        out_shape=jax.ShapeDtypeStruct((devices, 8, SENT), f32),
        in_specs=[pl.BlockSpec(memory_space=pl.ANY)] * 5,
        out_specs=pl.BlockSpec(memory_space=pltpu.VMEM),
        scratch_shapes=[
            pltpu.VMEM((3, 6, 3, 384), f32),
            pltpu.VMEM((3, 6, 3, 384), f32),
            pltpu.VMEM((2, 1, EZ), f32),
            pltpu.VMEM((1, 1, 192), jnp.int32),
            pltpu.VMEM((384, 512), jnp.bfloat16),
            pltpu.VMEM((128, 384), f32),
            pltpu.VMEM((384, 128), f32),
            pltpu.VMEM((16, 160, 128), f32),
            pltpu.SemaphoreType.DMA((5,)),
        ],
        compiler_params=wide,
    )
    first = pl.pallas_call(
        make_first_kernel(width, across, own_layers, fine_bound),
        out_shape=(
            jax.ShapeDtypeStruct((3, own_pairs, 32, width), f32),
            jax.ShapeDtypeStruct((own_pairs, 8, width), f32),
            jax.ShapeDtypeStruct((3, PAIRS_B, 32, width), f32),
        ),
        scratch_shapes=[
            pltpu.VMEM((3, 8, 32, width), f32),
            pltpu.VMEM((3, 8, 32, width), f32),
            pltpu.VMEM((8, width), f32),
            pltpu.VMEM((3, 8, 8, width), f32),
            pltpu.VMEM((2, SENT, width), f32),
        ],
        compiler_params=limit,
    )
    second = pl.pallas_call(
        make_second_kernel(width, across, own_layers, fine_bound, coarse_bound),
        out_shape=jax.ShapeDtypeStruct((devices // 2, 2, 8, 128), f32),
        scratch_shapes=[
            pltpu.VMEM((3, PAIRS_B + 2, 32, width), f32),
            pltpu.VMEM((3, PAIRS_B, 32, width), f32),
            pltpu.VMEM((PAIRS_B, width), f32),
            pltpu.VMEM((7, PAIRS_B, width), f32),
        ],
        compiler_params=limit,
    )
    unpack = pl.pallas_call(
        functools.partial(unpack_kernel, order),
        out_shape=(
            jax.ShapeDtypeStruct((3, 6, 3, 384), f32),
            jax.ShapeDtypeStruct((3, 2, 1, EZ), f32),
        ),
        scratch_shapes=[pltpu.VMEM((2, 128, 128), f32), pltpu.VMEM((384, 128), f32)],
        compiler_params=limit,
    )
    everyone = ("gy", "gx")

    def from_device(block, distance):
        place = {k: m % rows_of * columns_of + m // rows_of for m, k in enumerate(order)}
        route = [(place[(k + distance) % devices], place[k]) for k in range(devices)]
        return lax.ppermute(block, ("gx", "gy"), route)

    def body(initial, forcing, modulus, solid_list):
        sent = pack(initial, forcing, modulus, solid_list, jnp.asarray(pack_table()))
        arrived = lax.all_to_all(sent, everyone, 0, 0, tiled=True)
        message, edge, load = first(
            arrived.reshape(devices // 2, 2, 8, SENT),
            jnp.asarray(spread),
            jnp.asarray(collect),
            jnp.asarray(transfer),
        )
        messages = [from_device(message, n) if n else message for n in whole]
        edges = [from_device(edge, n) for n in outer]
        result = second(
            *messages,
            *edges,
            load,
            jnp.asarray(spread),
            jnp.asarray(collect),
            jnp.asarray(transfer_back),
        )
        back = lax.all_to_all(result.reshape(devices, 8, 128), everyone, 0, 0, tiled=True)
        return unpack(back, jnp.asarray(unpack_table()))

    placed = (
        P(None, "gx", "gy", None),
        P(None, "gx", "gy", None),
        P("gx", "gy", None),
        P("gx", "gy", None),
    )
    return jax.shard_map(
        body,
        mesh=mesh,
        in_specs=placed,
        out_specs=(P(None, "gx", "gy", None), P(None, "gx", "gy", None)),
        check_vma=False,
    )
```

```python
import functools
import math

import jax
import jax.numpy as jnp
import numpy as np
from jax import lax
from jax.experimental import pallas as pl
from jax.experimental.pallas import tpu as pltpu
from jax.sharding import PartitionSpec as P

CHEB = 3
EZ = 128

element_span = 20.0
lame_ratio = 4.0
rest_ratio = 1.25
modulus_top = 2.0
spectrum_floor = 0.05
interval_centre = (1.0 + spectrum_floor) / 2.0
interval_radius = (1.0 - spectrum_floor) / 2.0
interval_ratio = interval_centre / interval_radius
inner_anchors = (0.5 - 0.5 / math.sqrt(5.0), 0.5 + 0.5 / math.sqrt(5.0))

BEFORE = 4
PAIRS = 6
BEFORE_B = 6
PAIRS_B = 8
BLOCK = 84
SENT = 512

SLOTS = [
    (0, 0, 0), (1, 0, 0), (2, 0, 0), (0, 1, 0), (0, 2, 0), (0, 0, 1), (0, 0, 2), None,
    (0, 1, 1), (0, 1, 2), (0, 2, 1), (0, 2, 2), (1, 0, 1), (1, 0, 2), (2, 0, 1), (2, 0, 2),
    (1, 1, 0), (1, 2, 0), (2, 1, 0), (2, 2, 0), (1, 1, 1), (1, 1, 2), (1, 2, 1), (1, 2, 2),
    None, None, None, None, (2, 1, 1), (2, 1, 2), (2, 2, 1), (2, 2, 2),
]
TWIN = 7
RESTRICTED_SLOT = 24
STIFF_SLOT = 25
OWN_SHIFT, SHIFT_X, SHIFT_Y, SHIFT_Z = (0, 0, 0), (1, 0, 0), (0, 1, 0), (0, 0, 1)
ELEMENT_ROWS = (
    [(slot, OWN_SHIFT) for slot in range(24)]
    + [(slot, SHIFT_Z) for slot in range(16, 20)]
    + [(slot, OWN_SHIFT) for slot in range(28, 32)]
    + [(slot, SHIFT_X) for slot in range(7)] + [None]
    + [(slot, SHIFT_Y) for slot in range(7)] + [(0, (0, 1, 1))]
    + [(slot, SHIFT_Z) for slot in range(7)] + [(0, (1, 0, 1))]
    + [(slot, SHIFT_X) for slot in range(8, 12)] + [(slot, SHIFT_Y) for slot in range(12, 16)]
    + [(0, (1, 1, 1)), (1, (0, 1, 1)), (2, (0, 1, 1)), (3, (1, 0, 1)), (4, (1, 0, 1))]
    + [(5, (1, 1, 0)), (6, (1, 1, 0)), (0, (1, 1, 0))]
)
ROWS = len(ELEMENT_ROWS)
DEPTH = 80
CORNERS = [(a, b, c) for a in range(2) for b in range(2) for c in range(2)]


def gauss_rule(point_count):
    if point_count == 2:
        offset = 1.0 / math.sqrt(3.0)
        points = [-offset, offset]
        weights = [1.0, 1.0]
    else:
        inner = math.sqrt(3.0 / 7.0 - 2.0 / 7.0 * math.sqrt(6.0 / 5.0))
        outer = math.sqrt(3.0 / 7.0 + 2.0 / 7.0 * math.sqrt(6.0 / 5.0))
        heavy = (18.0 + math.sqrt(30.0)) / 36.0
        light = (18.0 - math.sqrt(30.0)) / 36.0
        points = [-outer, -inner, inner, outer]
        weights = [light, heavy, heavy, light]
    return (np.array(points), np.array(weights))


def lagrange_tables(anchors, samples):
    values = np.zeros((len(samples), len(anchors)))
    slopes = np.zeros((len(samples), len(anchors)))
    for sample_index, sample in enumerate(samples):
        for anchor_index, anchor in enumerate(anchors):
            others = [
                location
                for location_index, location in enumerate(anchors)
                if location_index != anchor_index
            ]
            product = 1.0
            for location in others:
                product = product * (sample - location) / (anchor - location)
            values[sample_index, anchor_index] = product
            derivative = 0.0
            for skipped in range(len(others)):
                summand = 1.0 / (anchor - others[skipped])
                for kept_index in range(len(others)):
                    if kept_index != skipped:
                        summand = (
                            summand * (sample - others[kept_index]) / (anchor - others[kept_index])
                        )
                derivative = derivative + summand
            slopes[sample_index, anchor_index] = derivative
    return (values, slopes)


def outer_three(first, second, third):
    return (
        first[:, None, None, :, None, None]
        * second[None, :, None, None, :, None]
        * third[None, None, :, None, None, :]
    )


def build_tables(anchors, point_count):
    raw_points, raw_weights = gauss_rule(point_count)
    samples = (raw_points + 1.0) / 2.0
    weights = raw_weights / 2.0
    basis_values, slopes = lagrange_tables(anchors, samples)
    quad_total = point_count**3
    nodal_count = len(anchors) ** 3
    derivative_one = outer_three(slopes, basis_values, basis_values).reshape(
        quad_total, nodal_count
    )
    derivative_two = outer_three(basis_values, slopes, basis_values).reshape(
        quad_total, nodal_count
    )
    derivative_three = outer_three(basis_values, basis_values, slopes).reshape(
        quad_total, nodal_count
    )
    stacked = np.stack([derivative_one, derivative_two, derivative_three]) / element_span
    volume = (weights[:, None, None] * weights[None, :, None] * weights[None, None, :]).reshape(
        -1
    ) * element_span**3
    forward = stacked.reshape(3 * quad_total, nodal_count)
    backward = (stacked * volume[None, :, None]).reshape(3 * quad_total, nodal_count).T
    weighted = stacked * volume[None, :, None]
    laplace = weighted[0].T @ stacked[0] + weighted[1].T @ stacked[1] + weighted[2].T @ stacked[2]
    matrix = np.zeros((nodal_count, 3, nodal_count, 3))
    for first in range(3):
        for second in range(3):
            block = weighted[second].T @ stacked[first] + (lame_ratio - 1.0) * (
                weighted[first].T @ stacked[second]
            )
            if first == second:
                block = block + laplace
            matrix[:, first, :, second] = block
    matrix = matrix.reshape(3 * nodal_count, 3 * nodal_count)
    vector = 1.5 + np.cos(1.3 * np.arange(3 * nodal_count))
    for repeat in range(200):
        vector = matrix @ vector
        vector = vector / np.sqrt(vector @ vector)
    largest = vector @ (matrix @ vector)
    return (forward, backward, float(4.0 * modulus_top * 1.1 * largest))


def row_nodes():
    nodes = []
    for entry in ELEMENT_ROWS:
        slot = SLOTS[entry[0]] if entry else None
        if slot is None or any(s and n for s, n in zip(entry[1], slot)):
            nodes.append(None)
        else:
            a, b, c = (3 * s + n for s, n in zip(entry[1], slot))
            nodes.append(16 * a + 4 * b + c)
    return nodes


def halves(matrix):
    whole = np.asarray(matrix, np.float32)
    high = whole.astype(jnp.bfloat16)
    low = (whole - high.astype(np.float32)).astype(jnp.bfloat16)
    return high, low


def element_tables():
    forward, backward, bound = build_tables([0.0, inner_anchors[0], inner_anchors[1], 1.0], 4)
    spread = np.zeros((forward.shape[0], DEPTH))
    collect = np.zeros((ROWS, backward.shape[1]))
    for row, node in enumerate(row_nodes()):
        if node is not None:
            spread[:, row] = forward[:, node]
            collect[row, :] = backward[node, :]
    spread_high, spread_low = halves(spread)
    collect_high, collect_low = halves(collect)
    return (
        np.concatenate([spread_high, spread_high, spread_low], 1),
        np.concatenate([collect_high, collect_low], 0),
        bound,
    )


def transfer_table():
    table = np.zeros((8, 32))
    reach = (0.0, inner_anchors[0], inner_anchors[1])
    for row, corner in enumerate(CORNERS):
        for column, slot in enumerate(SLOTS):
            if slot is not None:
                weight = 1.0
                for side, node in zip(corner, slot):
                    weight = weight * (reach[node] if side else 1.0 - reach[node])
                table[row, column] = weight
    back = table.T.copy()
    back[TWIN] = back[0]
    return table.T.astype(np.float32), back.astype(np.float32)


def chebyshev_steps():
    steps = [(0.0, 1.0 / interval_centre)]
    ratio_now = 1.0 / interval_ratio
    for sweep in range(1, CHEB):
        ratio_next = 1.0 / (2.0 * interval_ratio - ratio_now)
        steps.append((ratio_next * ratio_now, 2.0 * ratio_next / interval_radius))
        ratio_now = ratio_next
    return steps


def stack_row(field, component, layer, b):
    return field * 54 + component * 18 + layer * 3 + b


def block_column(component, slot):
    return 72 + 4 * component + slot - 28 if slot >= 24 else 24 * component + slot


def pack_table():
    table = np.zeros((3, 128, 2, 2, 128), np.float32)
    for field in range(2):
        for x in range(2):
            for component in range(3):
                for column, slot in enumerate(SLOTS):
                    if slot is not None:
                        a, b, c = slot
                        row = stack_row(field, component, 3 * x + a, b)
                        table[c, row, field, x, block_column(component, column)] = 1.0
            table[0, 108 + x, 0, x, TWIN] = 1.0
    return table.reshape(384, 512).astype(jnp.bfloat16)


def unpack_table():
    table = np.zeros((2, 128, 3, 128), np.float32)
    for x in range(2):
        for component in range(3):
            for column, slot in enumerate(SLOTS):
                if slot is not None:
                    a, b, c = slot
                    row = stack_row(0, component, 3 * x + a, b)
                    table[x, component * 32 + column, c, row] = 1.0
            table[x, 96 + component, 0, 54 + 2 * component + x] = 1.0
    return table.reshape(256, 384).astype(jnp.bfloat16)


def exact_pick(values, table):
    high = values.astype(jnp.bfloat16)
    rest = values - high.astype(jnp.float32)
    middle = rest.astype(jnp.bfloat16)
    low = (rest - middle.astype(jnp.float32)).astype(jnp.bfloat16)
    count = values.shape[0]
    parts = jnp.dot(
        jnp.concatenate([high, middle, low], 0), table, preferred_element_type=jnp.float32
    )
    return parts[:count] + (parts[count : 2 * count] + parts[2 * count :])


def ring_order(rows_of, columns_of):
    if (rows_of, columns_of) != (4, 8):
        return list(range(rows_of * columns_of))
    order = []
    for z in range(4):
        for x in range(2):
            for y in range(2):
                chip = (z, 7 - z, 15 - z, 8 + z)[2 * x + y]
                order += [2 * chip, 2 * chip + 1]
    return order


def region_shift(own_layers):
    return 2 if own_layers == 4 else 0


def pack_kernel(
    order,
    initial_at, forcing_at, modulus_at, listing_at, table_at, out,
    initial, forcing, modulus, listing, table, rows, turned, places, ready,
):
    devices = out.shape[0]
    own_layers = EZ // devices
    sources = (listing_at, modulus_at, initial_at, forcing_at, table_at)
    copies = [
        pltpu.make_async_copy(source, here, ready.at[n])
        for n, (source, here) in enumerate(
            zip(sources, (listing, modulus, initial, forcing, table))
        )
    ]
    for copy in copies:
        copy.start()
    rows[108:128, :] = jnp.zeros((20, 384), jnp.float32)
    copies[0].wait()
    copies[1].wait()
    listed = listing[0].astype(jnp.float32)
    listed = jnp.concatenate([listed, jnp.full((1, 64), 256.0, jnp.float32)], 1)
    listed = jnp.broadcast_to(listed, (128, 256)).T
    lanes = lax.broadcasted_iota(jnp.int32, (256, 128), 1).astype(jnp.float32)
    row_at = lax.broadcasted_iota(jnp.int32, (128, 128), 0)
    stiff = jnp.zeros((128, 128), jnp.float32)
    for x in range(2):
        hit = jnp.max(jnp.where(listed == lanes + 128.0 * x, 1.0, 0.0), axis=0, keepdims=True)
        stiff = jnp.where(row_at == 108 + x, hit * modulus[x], stiff)
    copies[2].wait()
    copies[3].wait()
    for field, source in enumerate((initial, forcing)):
        for component in range(3):
            for layer in range(6):
                at = stack_row(field, component, layer, 0)
                rows[at : at + 3, :] = source[component, layer]
    for part in range(3):
        span = slice(128 * part, 128 * part + 128)
        turned[span, :] = rows[:, span].T
    picked = [turned[pl.ds(c, 128, stride=3), :] for c in range(3)]
    picked[0] = picked[0] + stiff.T
    copies[4].wait()
    wide = exact_pick(jnp.concatenate(picked, 1), table[...])
    lane = lax.broadcasted_iota(jnp.int32, (128, 128), 1)
    for block in range(4):
        here = wide[:, 128 * block : 128 * block + 128]
        tiles = [None] * (SENT // 128)
        for pair in range(PAIRS):
            first = BLOCK * pair
            moved = here if pair == 0 else pltpu.roll(here, 128 - 2 * pair, 0)
            if first % 128:
                moved = pltpu.roll(moved, first % 128, 1)
            for tile in range(first // 128, (first + BLOCK - 1) // 128 + 1):
                before = tiles[tile]
                if before is None:
                    tiles[tile] = moved
                else:
                    tiles[tile] = jnp.where(lane >= first - 128 * tile, moved, before)
        for tile in range(SENT // 128):
            at = 4 * block + tile
            places[at, 16:144, :] = tiles[tile]
            places[at, 0:16, :] = tiles[tile][112:128]
            places[at, 144:160, :] = tiles[tile][0:16]
    for block in range(4):
        for parity in range(2):
            for tile in range(SENT // 128):
                at, span = 4 * block + tile, slice(128 * tile, 128 * tile + 128)
                first = 16 - BEFORE + parity
                if order == sorted(order):
                    out[:, 2 * block + parity, span] = places[
                        at, pl.ds(first, devices, stride=own_layers), :
                    ]
                    continue
                for device, k in enumerate(order):
                    row = first + own_layers * k
                    out[device, 2 * block + parity : 2 * block + parity + 1, span] = places[
                        at, row : row + 1, :
                    ]


def unpack_kernel(order, arrived, table, out, coarse_out, layers, turned):
    devices = arrived.shape[0]
    own_layers = EZ // devices
    for x in range(2):
        for layer in range(own_layers):
            row = (layer // 2) * 4 + x * 2 + layer % 2
            if order == sorted(order):
                layers[x, pl.ds(layer, devices, stride=own_layers), :] = arrived[:, row, :]
                continue
            for device, k in enumerate(order):
                at = (region_shift(own_layers) + own_layers * k + layer) % EZ
                layers[x, at : at + 1, :] = arrived[device, row : row + 1, :]
    wide = exact_pick(jnp.concatenate([layers[0], layers[1]], 1), table[...])
    for c in range(3):
        turned[pl.ds(c, 128, stride=3), :] = wide[:, 128 * c : 128 * c + 128]
    for part in range(3):
        span = slice(128 * part, 128 * part + 128)
        back = turned[span, :].T
        for component in range(3):
            for layer in range(6):
                at = stack_row(0, component, layer, 0)
                out[component, layer, :, span] = back[at : at + 3, :]
    back = wide[:, 0:128].T
    for component in range(3):
        for x in range(2):
            at = 54 + 2 * component + x
            coarse_out[component, x] = back[at : at + 1, :]


def cofactor_rows(deform):
    return [
        [
            deform[(row_at + 1) % 3][(column + 1) % 3] * deform[(row_at + 2) % 3][(column + 2) % 3]
            - deform[(row_at + 1) % 3][(column + 2) % 3]
            * deform[(row_at + 2) % 3][(column + 1) % 3]
            for column in range(3)
        ]
        for row_at in range(3)
    ]


def point_stress(deform, stiffness, stiffness_four):
    cofactors = cofactor_rows(deform)
    jacobian = (
        deform[0][0] * cofactors[0][0]
        + deform[0][1] * cofactors[0][1]
        + deform[0][2] * cofactors[0][2]
    )
    pressure = stiffness_four * (jacobian - rest_ratio)
    return [
        [stiffness * deform[i][d] + pressure * cofactors[i][d] for d in range(3)] for i in range(3)
    ]


coarse_samples = [0.5 - 0.5 / math.sqrt(3.0), 0.5 + 0.5 / math.sqrt(3.0)]
two = range(2)


def at_points(low, high):
    change = high - low
    return [low + s * change for s in coarse_samples], change * (1.0 / element_span)


def ends_of(first, second):
    high = coarse_samples[0] * first + coarse_samples[1] * second
    return [first + second - high, high]


def high_low(values):
    high = values.astype(jnp.bfloat16)
    return high, (values - high.astype(jnp.float32)).astype(jnp.bfloat16)


class Slab:
    def __init__(self, width, across):
        self.width = width
        self.y_step = 2 * across
        lane = lax.broadcasted_iota(jnp.int32, (8, width), 1)
        x = (lane // 2) % across
        self.bottom, self.top, self.even = x == 0, x == across - 1, lane % 2 == 0
        self.row = lax.broadcasted_iota(jnp.int32, (8, width), 0)
        row = lax.broadcasted_iota(jnp.int32, (32, width), 0)
        lane = lax.broadcasted_iota(jnp.int32, (32, width), 1)
        on_face = (row == 0) | ((row >= 3) & (row <= 11))
        self.keep = jnp.where(on_face & ((lane // 2) % across == 0), 0.0, 1.0)

    def lanes(self, v, step):
        return pltpu.roll(v, step % self.width, 1)

    def next_x(self, v):
        return jnp.where(self.top, 0.0, self.lanes(v, -2))

    def next_y(self, v):
        return self.lanes(v, -self.y_step)

    def next_z(self, v, ahead):
        return jnp.where(self.even, self.lanes(v, -1), self.lanes(ahead, 1))

    def onto_x(self, v):
        return jnp.where(self.bottom, 0.0, self.lanes(v, 2))

    def onto_y(self, v):
        return self.lanes(v, self.y_step)

    def gather(self, here, ahead):
        row = self.row
        g0, g1, g2, g3 = here[0:8], here[8:16], here[16:24], here[24:32]
        z0 = self.next_z(g0, ahead[0:8])
        z2 = self.next_z(g2, ahead[16:24])
        y0 = self.next_y(g0)
        yz, xz, xy = self.next_y(z0), self.next_x(z0), self.next_x(y0)
        edges = jnp.where(row <= 2, yz, jnp.where(row <= 4, xz, xy))
        return jnp.concatenate(
            [
                g0,
                g1,
                g2,
                jnp.where(row < 4, z2, g3),
                self.next_x(g0),
                jnp.where(row == 7, yz, y0),
                jnp.where(row == 7, xz, z0),
                jnp.where(row < 4, self.next_x(g1), self.next_y(g1)),
                jnp.where(row == 0, self.next_x(yz), edges),
                jnp.zeros_like(g0),
            ],
            0,
        )

    def scatter(self, part, behind):
        row = self.row
        g0, g1, g2, g3, x0, y0, z0, sides, edges = (part[8 * n : 8 * n + 8] for n in range(9))
        edges_x = self.onto_x(edges)
        yz = jnp.where(row == 0, edges_x, jnp.where(row == 7, y0, edges))
        yz = jnp.where((row <= 2) | (row == 7), yz, 0.0)
        z0 = jnp.where(row == 7, self.onto_x(z0), z0)
        z0 = z0 + jnp.where((row == 3) | (row == 4), edges_x, 0.0) + self.onto_y(yz)
        y0 = jnp.where(row == 7, edges_x, y0 + jnp.where(row >= 5, edges_x, 0.0))
        z2 = g3
        own0 = g0 + self.onto_x(x0) + self.onto_y(y0)
        own0 = own0 + jnp.where(self.even, behind[0], self.lanes(z0, 1))
        own1 = g1 + jnp.where(row < 4, self.onto_x(sides), self.onto_y(sides))
        share2 = jnp.where(self.even, behind[1], self.lanes(z2, 1))
        own2 = g2 + jnp.where(row < 4, share2, 0.0)
        own3 = jnp.where(row < 4, 0.0, g3)
        own0 = own0 + jnp.where(row == 0, pltpu.roll(own0, 1, 0), 0.0)
        own0 = jnp.where(row == 7, pltpu.roll(own0, 7, 0), own0)
        moved = (self.lanes(z0, -1), self.lanes(z2, -1))
        return jnp.concatenate([own0, own1, own2, own3], 0), moved

    def gradient(self, u, spread, pair):
        blocks = [
            self.gather(u[i, pair + q], u[i, pair + q + 1]) for i in range(3) for q in range(2)
        ]
        high, low = high_low(jnp.concatenate(blocks, 1))
        return jnp.dot(
            spread[...],
            jnp.concatenate([high, low, high], 0),
            preferred_element_type=jnp.float32,
        )

    def force(self, gradient, stiff, collect, pair):
        width = 2 * self.width
        stiffness = jnp.concatenate([stiff[pair + q : pair + q + 1, :] for q in range(2)], 1)
        deform = [
            [
                gradient[64 * e : 64 * e + 64, width * i : width * (i + 1)]
                + (1.0 if i == e else 0.0)
                for e in range(3)
            ]
            for i in range(3)
        ]
        stress = point_stress(deform, stiffness, lame_ratio * stiffness)
        stress = jnp.concatenate(
            [jnp.concatenate([stress[i][e] for i in range(3)], 1) for e in range(3)], 0
        )
        high, low = high_low(stress)
        force = jnp.dot(collect[...], high, preferred_element_type=jnp.float32)
        return force[0:ROWS] + (
            force[ROWS:] + jnp.dot(collect[0:ROWS], low, preferred_element_type=jnp.float32)
        )

    def apply(self, u, stiff, spread, collect, first, count, finish):
        width = self.width
        none = jnp.zeros((8, width), jnp.float32)
        carry = [(none, none) for i in range(3)]
        last = first + 2 * ((count + 1) // 2)
        ahead = self.gradient(u, spread, first)
        for pair in range(first, last, 2):
            gradient = ahead
            if pair + 2 < last:
                ahead = self.gradient(u, spread, pair + 2)
            force = self.force(gradient, stiff, collect, pair)
            totals = [[], []]
            for q in range(2):
                for i in range(3):
                    at = (2 * i + q) * width
                    total, carry[i] = self.scatter(force[:, at : at + width], carry[i])
                    totals[q].append(total)
            for q in range(2):
                finish(pair + q, totals[q])

    def smooth(self, u, f, f_shift, d, stiff, spread, collect, spans, bound):
        for (first, count), (held, added) in zip(spans, chebyshev_steps()):

            def finish(pair, forces, held=held, added=added):
                for i in range(3):
                    z = (added / bound) * self.keep * (f[i, pair + f_shift] - forces[i])
                    move = held * d[i, pair] + z if held else z
                    d[i, pair] = move
                    u[i, pair] = u[i, pair] + move

            self.apply(u, stiff, spread, collect, first, count, finish)

    def coarse_next_z(self, v):
        return self.next_z(v, pltpu.roll(v, 7, 0))

    def coarse_onto_z(self, v):
        return jnp.where(self.even, pltpu.roll(self.lanes(v, -1), 1, 0), self.lanes(v, 1))

    def corners_of(self, v):
        found = {(0, 0, 0): v, (0, 0, 1): self.coarse_next_z(v)}
        for c in range(2):
            found[0, 1, c] = self.next_y(found[0, 0, c])
        for b in range(2):
            for c in range(2):
                found[1, b, c] = self.next_x(found[0, b, c])
        return found

    def assemble(self, part):
        line = {
            (a, b): part[a, b, 0] + self.coarse_onto_z(part[a, b, 1])
            for a in range(2)
            for b in range(2)
        }
        face = [line[a, 0] + self.onto_y(line[a, 1]) for a in range(2)]
        return face[0] + self.onto_x(face[1])

    def coarse_force(self, values, stiffness):
        grads = []
        for i in range(3):
            v = self.corners_of(values[i])
            vz, sz = {}, {}
            for a in two:
                for b in two:
                    vz[a, b], sz[a, b] = at_points(v[a, b, 0], v[a, b, 1])
            vv, vs, sv = {}, {}, {}
            for a in two:
                for k in two:
                    vv[a, k], vs[a, k] = at_points(vz[a, 0][k], vz[a, 1][k])
                sv[a], unused = at_points(sz[a, 0], sz[a, 1])
            dx, dy, dz = {}, {}, {}
            for k in two:
                for j in two:
                    dx[j, k] = (vv[1, k][j] - vv[0, k][j]) * (1.0 / element_span)
                line, unused = at_points(vs[0, k], vs[1, k])
                for h in two:
                    dy[h, k] = line[h]
            for j in two:
                line, unused = at_points(sv[0][j], sv[1][j])
                for h in two:
                    dz[h, j] = line[h]
            grads.append((dx, dy, dz))
        weight = element_span**2 / 8.0
        scaled = weight * stiffness
        scaled_four = lame_ratio * scaled
        sums = [({}, {}, {}) for i in range(3)]

        def add(table, key, value):
            table[key] = table[key] + value if key in table else value

        for h in two:
            for j in two:
                for k in two:
                    deform = [
                        [grads[i][0][j, k], grads[i][1][h, k], grads[i][2][h, j]]
                        for i in range(3)
                    ]
                    for i in range(3):
                        deform[i][i] = deform[i][i] + 1.0
                    stress = point_stress(deform, scaled, scaled_four)
                    for i in range(3):
                        add(sums[i][0], (j, k), stress[i][0])
                        add(sums[i][1], (h, k), stress[i][1])
                        add(sums[i][2], (h, j), stress[i][2])

        forces = []
        for i in range(3):
            part = {}
            qx, qy, qz = sums[i]
            along_z = [ends_of(qx[j, 0], qx[j, 1]) for j in two]
            for c in two:
                line = ends_of(along_z[0][c], along_z[1][c])
                for b in two:
                    part[0, b, c] = -line[b]
                    part[1, b, c] = line[b]
            along_z = [ends_of(qy[h, 0], qy[h, 1]) for h in two]
            for c in two:
                line = ends_of(along_z[0][c], along_z[1][c])
                for a in two:
                    part[a, 0, c] = part[a, 0, c] - line[a]
                    part[a, 1, c] = part[a, 1, c] + line[a]
            along_y = [ends_of(qz[h, 0], qz[h, 1]) for h in two]
            for b in two:
                line = ends_of(along_y[0][b], along_y[1][b])
                for a in two:
                    part[a, b, 0] = part[a, b, 0] - line[a]
                    part[a, b, 1] = part[a, b, 1] + line[a]
            forces.append(self.assemble(part))
        return forces


def make_first_kernel(width, across, own_layers, fine_bound):
    own = BEFORE // 2
    own_pairs = (own_layers + 1) // 2
    spans = []
    for n in (4, 3, 2, 1):
        low, high = BEFORE - n, BEFORE + own_layers + n - 1
        spans.append((low // 2, (high + 1) // 2 - low // 2))

    def first_kernel(
        arrived, spread, collect, transfer, message, edge, f, u, d, stiff, shares, turned
    ):
        slab = Slab(width, across)
        row = slab.row
        u[...] = jnp.zeros(u.shape, jnp.float32)
        f[...] = jnp.zeros(f.shape, jnp.float32)
        shares[...] = jnp.zeros(shares.shape, jnp.float32)
        stiff[...] = jnp.zeros(stiff.shape, jnp.float32)
        lower = lax.broadcasted_iota(jnp.int32, (width // 8, 8, 128), 1) < 4
        for tile in range(SENT // 128):
            span = slice(128 * tile, 128 * tile + 128)
            first, second = arrived[:, 0, :, span], arrived[:, 1, :, span]
            value = jnp.where(lower, first, pltpu.roll(second, 4, 1))
            load = jnp.where(lower, pltpu.roll(first, 4, 1), second)
            turned[0, span, :] = value.reshape(width, 128).T
            turned[1, span, :] = load.reshape(width, 128).T
        for field, target in enumerate((u, f)):
            for pair in range(PAIRS):
                base = BLOCK * pair
                for i in range(3):
                    parts = [
                        turned[field, base + 24 * i + 8 * n : base + 24 * i + 8 * n + 8, :]
                        for n in range(3)
                    ]
                    inner = turned[field, base + 68 + 4 * i : base + 76 + 4 * i, :]
                    if field == 0 and i == 0:
                        stiff[pair : pair + 1, :] = parts[0][TWIN : TWIN + 1]
                    parts[0] = jnp.where(row == TWIN, pltpu.roll(parts[0], TWIN, 0), parts[0])
                    parts.append(jnp.where(row < 4, 0.0, inner))
                    whole = jnp.concatenate(parts, 0)
                    target[i, pair] = whole * slab.keep if field == 0 else whole

        slab.smooth(u, f, 0, d, stiff, spread, collect, spans[0:3], fine_bound)

        weights = [jnp.broadcast_to(transfer[:, n : n + 1], (32, width)) for n in range(8)]

        def restrict(pair, forces):
            for i in range(3):
                rest = slab.keep * (f[i, pair] - forces[i])
                for n in range(8):
                    part = rest * weights[n]
                    part = (part[0:8] + part[8:16]) + (part[16:24] + part[24:32])
                    shares[i, n, pl.ds(pair, 1), :] = jnp.sum(part, axis=0, keepdims=True)

        slab.apply(u, stiff, spread, collect, *spans[3], restrict)

        restricted = [
            slab.assemble({corner: shares[i, n] for n, corner in enumerate(CORNERS)})
            for i in range(3)
        ]
        for q in range(own_pairs):
            hard = stiff[own + q : own + q + 1, :]
            for i in range(3):
                message[i, q] = u[i, own + q]
                message[i, q, RESTRICTED_SLOT : RESTRICTED_SLOT + 1, :] = restricted[i][
                    own + q : own + q + 1
                ]
                edge[q, i : i + 1, :] = u[i, own + q, 0:1, :]
                edge[q, 3 + i : 4 + i, :] = restricted[i][own + q : own + q + 1]
            message[0, q, STIFF_SLOT : STIFF_SLOT + 1, :] = hard
            edge[q, 6:8, :] = jnp.broadcast_to(hard, (2, width))

    return first_kernel


def sources_of(own_layers):
    shift = region_shift(own_layers)
    whole = range((shift - 3) // own_layers, (shift + own_layers + 2) // own_layers + 1)
    coarse = range((shift - 5) // own_layers, (shift + own_layers + 4) // own_layers + 1)
    return list(whole), [n for n in coarse if n not in whole]


def make_second_kernel(width, across, own_layers, fine_bound, coarse_bound):
    own = BEFORE_B // 2
    own_pairs = (own_layers + 1) // 2
    first_layer = region_shift(own_layers) - BEFORE_B
    shift = (BEFORE + first_layer) // 2
    whole, outer = sources_of(own_layers)
    steps = chebyshev_steps()
    spans = []
    for n in (3, 2, 1):
        low, high = BEFORE_B - n, BEFORE_B + own_layers + n - 1
        spans.append((low // 2, (high + 1) // 2 - low // 2))

    def second_kernel(*refs):
        messages = dict(zip(whole, refs))
        refs = refs[len(whole) :]
        edges = dict(zip(outer, refs))
        f, spread, collect, transfer_back, out, u, d, stiff, coarse = refs[len(outer) :]
        slab = Slab(width, across)

        def pair_of(pair, fetch):
            found = []
            for parity in range(2):
                layer = 2 * pair + first_layer + parity
                device = layer // own_layers
                layer = layer - device * own_layers
                found.append((device, layer // 2, layer % 2))
            values = [fetch(device, q) for device, q, parity in found]
            if found[0][:2] == found[1][:2] or (values[0] is None and values[1] is None):
                return values[0]
            for parity in range(2):
                if values[parity] is None:
                    values[parity] = jnp.zeros_like(values[1 - parity])
                elif found[parity][2] != parity:
                    values[parity] = slab.lanes(values[parity], 2 * parity - 1)
            lane = lax.broadcasted_iota(jnp.int32, values[0].shape, 1)
            return jnp.where(lane % 2 == 0, values[0], values[1])

        u[...] = jnp.zeros(u.shape, jnp.float32)
        coarse[...] = jnp.zeros(coarse.shape, jnp.float32)
        d[...] = jnp.zeros(d.shape, jnp.float32)
        for pair in range(PAIRS_B):
            for i in range(3):
                block = pair_of(pair, lambda n, q: messages[n][i, q] if n in messages else None)
                if block is not None:
                    u[i, pair] = block
            for n in range(7):

                def fetch(device, q, n=n):
                    if device in messages:
                        i, slot = ((n, 0), (n - 3, RESTRICTED_SLOT), (0, STIFF_SLOT))[n // 3]
                        return messages[device][i, q, slot : slot + 1, :]
                    return edges[device][q, n : n + 1, :] if device in edges else None

                line = pair_of(pair, fetch)
                if line is not None:
                    coarse[n, pair : pair + 1, :] = line
        stiff[...] = coarse[6]

        stiffness = coarse[6]
        keep_coarse = jnp.where(slab.bottom, 0.0, 1.0)
        start = [coarse[i] for i in range(3)]
        restricted = [coarse[3 + i] for i in range(3)]
        before = slab.coarse_force(start, stiffness)
        move = [(steps[0][1] / coarse_bound) * keep_coarse * restricted[i] for i in range(3)]
        level = [start[i] + move[i] for i in range(3)]
        for held, added in steps[1:]:
            force = slab.coarse_force(level, stiffness)
            for i in range(3):
                z = keep_coarse * (restricted[i] + before[i] - force[i])
                move[i] = held * move[i] + (added / coarse_bound) * z
                level[i] = level[i] + move[i]

        weights = [jnp.broadcast_to(transfer_back[:, n : n + 1], (32, width)) for n in range(8)]
        for i in range(3):
            change = slab.corners_of(level[i] - start[i])
            for pair in range(spans[0][0], min(spans[0][0] + spans[0][1] + 1, PAIRS_B)):
                lift = u[i, pair]
                for n, corner in enumerate(CORNERS):
                    lift = lift + weights[n] * change[corner][pair : pair + 1]
                u[i, pair] = lift

        slab.smooth(u, f, shift, d, stiff, spread, collect, spans, fine_bound)

        lower = lax.broadcasted_iota(jnp.int32, (width // 8, 8, 128), 1) < 4
        sides = []
        blank = jnp.zeros((29, width), jnp.float32)
        for q in range(2):
            ends_here = jnp.concatenate(
                [u[i, own + q] for i in range(3)]
                + [level[i][own + q : own + q + 1] for i in range(3)]
                + [blank],
                0,
            )
            sides.append(ends_here.T.reshape(width // 8, 8, 128))
        out[:, 0] = jnp.where(lower, sides[0], pltpu.roll(sides[1], 4, 1))
        out[:, 1] = jnp.where(lower, pltpu.roll(sides[0], 4, 1), sides[1])

    return second_kernel


def solution(mesh):
    rows_of, columns_of = mesh.shape["gx"], mesh.shape["gy"]
    devices = rows_of * columns_of
    order = ring_order(rows_of, columns_of)
    own_layers = EZ // devices
    own_pairs = (own_layers + 1) // 2
    width = 4 * devices
    across = 2 * rows_of
    whole, outer = sources_of(own_layers)
    spread, collect, fine_bound = element_tables()
    coarse_bound = build_tables([0.0, 1.0], 2)[2]
    transfer, transfer_back = transfer_table()
    wide = pltpu.CompilerParams(vmem_limit_bytes=60 * 1024 * 1024)
    limit = pltpu.CompilerParams(vmem_limit_bytes=48 * 1024 * 1024)
    f32 = jnp.float32

    pack = pl.pallas_call(
        functools.partial(pack_kernel, order),
        out_shape=jax.ShapeDtypeStruct((devices, 8, SENT), f32),
        in_specs=[pl.BlockSpec(memory_space=pl.ANY)] * 5,
        out_specs=pl.BlockSpec(memory_space=pltpu.VMEM),
        scratch_shapes=[
            pltpu.VMEM((3, 6, 3, 384), f32),
            pltpu.VMEM((3, 6, 3, 384), f32),
            pltpu.VMEM((2, 1, EZ), f32),
            pltpu.VMEM((1, 1, 192), jnp.int32),
            pltpu.VMEM((384, 512), jnp.bfloat16),
            pltpu.VMEM((128, 384), f32),
            pltpu.VMEM((384, 128), f32),
            pltpu.VMEM((16, 160, 128), f32),
            pltpu.SemaphoreType.DMA((5,)),
        ],
        compiler_params=wide,
    )
    first = pl.pallas_call(
        make_first_kernel(width, across, own_layers, fine_bound),
        out_shape=(
            jax.ShapeDtypeStruct((3, own_pairs, 32, width), f32),
            jax.ShapeDtypeStruct((own_pairs, 8, width), f32),
            jax.ShapeDtypeStruct((3, PAIRS_B, 32, width), f32),
        ),
        scratch_shapes=[
            pltpu.VMEM((3, 8, 32, width), f32),
            pltpu.VMEM((3, 8, 32, width), f32),
            pltpu.VMEM((8, width), f32),
            pltpu.VMEM((3, 8, 8, width), f32),
            pltpu.VMEM((2, SENT, width), f32),
        ],
        compiler_params=limit,
    )
    second = pl.pallas_call(
        make_second_kernel(width, across, own_layers, fine_bound, coarse_bound),
        out_shape=jax.ShapeDtypeStruct((devices // 2, 2, 8, 128), f32),
        scratch_shapes=[
            pltpu.VMEM((3, PAIRS_B + 2, 32, width), f32),
            pltpu.VMEM((3, PAIRS_B, 32, width), f32),
            pltpu.VMEM((PAIRS_B, width), f32),
            pltpu.VMEM((7, PAIRS_B, width), f32),
        ],
        compiler_params=limit,
    )
    unpack = pl.pallas_call(
        functools.partial(unpack_kernel, order),
        out_shape=(
            jax.ShapeDtypeStruct((3, 6, 3, 384), f32),
            jax.ShapeDtypeStruct((3, 2, 1, EZ), f32),
        ),
        scratch_shapes=[pltpu.VMEM((2, 128, 128), f32), pltpu.VMEM((384, 128), f32)],
        compiler_params=limit,
    )
    everyone = ("gy", "gx")

    def from_device(block, distance):
        place = {k: m % rows_of * columns_of + m // rows_of for m, k in enumerate(order)}
        route = [(place[(k + distance) % devices], place[k]) for k in range(devices)]
        return lax.ppermute(block, ("gx", "gy"), route)

    def body(initial, forcing, modulus, solid_list):
        sent = pack(initial, forcing, modulus, solid_list, jnp.asarray(pack_table()))
        arrived = lax.all_to_all(sent, everyone, 0, 0, tiled=True)
        message, edge, load = first(
            arrived.reshape(devices // 2, 2, 8, SENT),
            jnp.asarray(spread),
            jnp.asarray(collect),
            jnp.asarray(transfer),
        )
        messages = [from_device(message, n) if n else message for n in whole]
        edges = [from_device(edge, n) for n in outer]
        result = second(
            *messages,
            *edges,
            load,
            jnp.asarray(spread),
            jnp.asarray(collect),
            jnp.asarray(transfer_back),
        )
        back = lax.all_to_all(result.reshape(devices, 8, 128), everyone, 0, 0, tiled=True)
        return unpack(back, jnp.asarray(unpack_table()))

    placed = (
        P(None, "gx", "gy", None),
        P(None, "gx", "gy", None),
        P("gx", "gy", None),
        P("gx", "gy", None),
    )
    return jax.shard_map(
        body,
        mesh=mesh,
        in_specs=placed,
        out_specs=(P(None, "gx", "gy", None), P(None, "gx", "gy", None)),
        check_vma=False,
    )
```

```python
import functools
import math

import jax
import jax.numpy as jnp
import numpy as np
from jax import lax
from jax.experimental import pallas as pl
from jax.experimental.pallas import tpu as pltpu
from jax.sharding import PartitionSpec as P

CHEB = 3
EZ = 128

element_span = 20.0
lame_ratio = 4.0
rest_ratio = 1.25
modulus_top = 2.0
spectrum_floor = 0.05
interval_centre = (1.0 + spectrum_floor) / 2.0
interval_radius = (1.0 - spectrum_floor) / 2.0
interval_ratio = interval_centre / interval_radius
inner_anchors = (0.5 - 0.5 / math.sqrt(5.0), 0.5 + 0.5 / math.sqrt(5.0))

BEFORE = 4
PAIRS = 6
BEFORE_B = 6
PAIRS_B = 8
BLOCK = 84
SENT = 384

SLOTS = [
    (0, 0, 0), (1, 0, 0), (2, 0, 0), (0, 1, 0), (0, 2, 0), (0, 0, 1), (0, 0, 2), None,
    (0, 1, 1), (0, 1, 2), (0, 2, 1), (0, 2, 2), (1, 0, 1), (1, 0, 2), (2, 0, 1), (2, 0, 2),
    (1, 1, 0), (1, 2, 0), (2, 1, 0), (2, 2, 0), (1, 1, 1), (1, 1, 2), (1, 2, 1), (1, 2, 2),
    None, None, None, None, (2, 1, 1), (2, 1, 2), (2, 2, 1), (2, 2, 2),
]
TWIN = 7
RESTRICTED_SLOT = 24
STIFF_SLOT = 25
OWN_SHIFT, SHIFT_X, SHIFT_Y, SHIFT_Z = (0, 0, 0), (1, 0, 0), (0, 1, 0), (0, 0, 1)
ELEMENT_ROWS = (
    [(slot, OWN_SHIFT) for slot in range(24)]
    + [(slot, SHIFT_Z) for slot in range(16, 20)]
    + [(slot, OWN_SHIFT) for slot in range(28, 32)]
    + [(slot, SHIFT_X) for slot in range(7)] + [None]
    + [(slot, SHIFT_Y) for slot in range(7)] + [(0, (0, 1, 1))]
    + [(slot, SHIFT_Z) for slot in range(7)] + [(0, (1, 0, 1))]
    + [(slot, SHIFT_X) for slot in range(8, 12)] + [(slot, SHIFT_Y) for slot in range(12, 16)]
    + [(0, (1, 1, 1)), (1, (0, 1, 1)), (2, (0, 1, 1)), (3, (1, 0, 1)), (4, (1, 0, 1))]
    + [(5, (1, 1, 0)), (6, (1, 1, 0)), (0, (1, 1, 0))]
)
ROWS = len(ELEMENT_ROWS)
DEPTH = 80
CORNERS = [(a, b, c) for a in range(2) for b in range(2) for c in range(2)]


def gauss_rule(point_count):
    if point_count == 2:
        offset = 1.0 / math.sqrt(3.0)
        points = [-offset, offset]
        weights = [1.0, 1.0]
    else:
        inner = math.sqrt(3.0 / 7.0 - 2.0 / 7.0 * math.sqrt(6.0 / 5.0))
        outer = math.sqrt(3.0 / 7.0 + 2.0 / 7.0 * math.sqrt(6.0 / 5.0))
        heavy = (18.0 + math.sqrt(30.0)) / 36.0
        light = (18.0 - math.sqrt(30.0)) / 36.0
        points = [-outer, -inner, inner, outer]
        weights = [light, heavy, heavy, light]
    return (np.array(points), np.array(weights))


def lagrange_tables(anchors, samples):
    values = np.zeros((len(samples), len(anchors)))
    slopes = np.zeros((len(samples), len(anchors)))
    for sample_index, sample in enumerate(samples):
        for anchor_index, anchor in enumerate(anchors):
            others = [
                location
                for location_index, location in enumerate(anchors)
                if location_index != anchor_index
            ]
            product = 1.0
            for location in others:
                product = product * (sample - location) / (anchor - location)
            values[sample_index, anchor_index] = product
            derivative = 0.0
            for skipped in range(len(others)):
                summand = 1.0 / (anchor - others[skipped])
                for kept_index in range(len(others)):
                    if kept_index != skipped:
                        summand = (
                            summand * (sample - others[kept_index]) / (anchor - others[kept_index])
                        )
                derivative = derivative + summand
            slopes[sample_index, anchor_index] = derivative
    return (values, slopes)


def outer_three(first, second, third):
    return (
        first[:, None, None, :, None, None]
        * second[None, :, None, None, :, None]
        * third[None, None, :, None, None, :]
    )


def build_tables(anchors, point_count):
    raw_points, raw_weights = gauss_rule(point_count)
    samples = (raw_points + 1.0) / 2.0
    weights = raw_weights / 2.0
    basis_values, slopes = lagrange_tables(anchors, samples)
    quad_total = point_count**3
    nodal_count = len(anchors) ** 3
    derivative_one = outer_three(slopes, basis_values, basis_values).reshape(
        quad_total, nodal_count
    )
    derivative_two = outer_three(basis_values, slopes, basis_values).reshape(
        quad_total, nodal_count
    )
    derivative_three = outer_three(basis_values, basis_values, slopes).reshape(
        quad_total, nodal_count
    )
    stacked = np.stack([derivative_one, derivative_two, derivative_three]) / element_span
    volume = (weights[:, None, None] * weights[None, :, None] * weights[None, None, :]).reshape(
        -1
    ) * element_span**3
    forward = stacked.reshape(3 * quad_total, nodal_count)
    backward = (stacked * volume[None, :, None]).reshape(3 * quad_total, nodal_count).T
    weighted = stacked * volume[None, :, None]
    laplace = weighted[0].T @ stacked[0] + weighted[1].T @ stacked[1] + weighted[2].T @ stacked[2]
    matrix = np.zeros((nodal_count, 3, nodal_count, 3))
    for first in range(3):
        for second in range(3):
            block = weighted[second].T @ stacked[first] + (lame_ratio - 1.0) * (
                weighted[first].T @ stacked[second]
            )
            if first == second:
                block = block + laplace
            matrix[:, first, :, second] = block
    matrix = matrix.reshape(3 * nodal_count, 3 * nodal_count)
    vector = 1.5 + np.cos(1.3 * np.arange(3 * nodal_count))
    for repeat in range(200):
        vector = matrix @ vector
        vector = vector / np.sqrt(vector @ vector)
    largest = vector @ (matrix @ vector)
    return (forward, backward, float(4.0 * modulus_top * 1.1 * largest))


def row_nodes():
    nodes = []
    for entry in ELEMENT_ROWS:
        slot = SLOTS[entry[0]] if entry else None
        if slot is None or any(s and n for s, n in zip(entry[1], slot)):
            nodes.append(None)
        else:
            a, b, c = (3 * s + n for s, n in zip(entry[1], slot))
            nodes.append(16 * a + 4 * b + c)
    return nodes


def halves(matrix):
    whole = np.asarray(matrix, np.float32)
    high = whole.astype(jnp.bfloat16)
    low = (whole - high.astype(np.float32)).astype(jnp.bfloat16)
    return high, low


def element_tables():
    forward, backward, bound = build_tables([0.0, inner_anchors[0], inner_anchors[1], 1.0], 4)
    spread = np.zeros((forward.shape[0], DEPTH))
    collect = np.zeros((ROWS, backward.shape[1]))
    for row, node in enumerate(row_nodes()):
        if node is not None:
            spread[:, row] = forward[:, node]
            collect[row, :] = backward[node, :]
    spread_high, spread_low = halves(spread)
    collect_high, collect_low = halves(collect)
    return (
        np.concatenate([spread_high, spread_high, spread_low], 1),
        np.concatenate([collect_high, collect_low], 0),
        bound,
    )


def transfer_table():
    table = np.zeros((8, 32))
    reach = (0.0, inner_anchors[0], inner_anchors[1])
    for row, corner in enumerate(CORNERS):
        for column, slot in enumerate(SLOTS):
            if slot is not None:
                weight = 1.0
                for side, node in zip(corner, slot):
                    weight = weight * (reach[node] if side else 1.0 - reach[node])
                table[row, column] = weight
    back = table.T.copy()
    back[TWIN] = back[0]
    return table.T.astype(np.float32), back.astype(np.float32)


def chebyshev_steps():
    steps = [(0.0, 1.0 / interval_centre)]
    ratio_now = 1.0 / interval_ratio
    for sweep in range(1, CHEB):
        ratio_next = 1.0 / (2.0 * interval_ratio - ratio_now)
        steps.append((ratio_next * ratio_now, 2.0 * ratio_next / interval_radius))
        ratio_now = ratio_next
    return steps


def stack_row(field, component, layer, b):
    return field * 54 + component * 18 + layer * 3 + b


def block_column(component, slot):
    return 72 + 4 * component + slot - 28 if slot >= 24 else 24 * component + slot


def pack_table():
    table = np.zeros((3, 128, 2, 2, 128), np.float32)
    for field in range(2):
        for x in range(2):
            for component in range(3):
                for column, slot in enumerate(SLOTS):
                    if slot is not None:
                        a, b, c = slot
                        row = stack_row(field, component, 3 * x + a, b)
                        table[c, row, field, x, block_column(component, column)] = 1.0
            table[0, 108 + x, 0, x, TWIN] = 1.0
    return table.reshape(384, 512).astype(jnp.bfloat16)


def unpack_table():
    table = np.zeros((2, 128, 3, 128), np.float32)
    for x in range(2):
        for component in range(3):
            for column, slot in enumerate(SLOTS):
                if slot is not None:
                    a, b, c = slot
                    row = stack_row(0, component, 3 * x + a, b)
                    table[x, component * 32 + column, c, row] = 1.0
            table[x, 96 + component, 0, 54 + 2 * component + x] = 1.0
    return table.reshape(256, 384).astype(jnp.bfloat16)


def exact_pick(values, table):
    high = values.astype(jnp.bfloat16)
    rest = values - high.astype(jnp.float32)
    middle = rest.astype(jnp.bfloat16)
    low = (rest - middle.astype(jnp.float32)).astype(jnp.bfloat16)
    count = values.shape[0]
    parts = jnp.dot(
        jnp.concatenate([high, middle, low], 0), table, preferred_element_type=jnp.float32
    )
    return parts[:count] + (parts[count : 2 * count] + parts[2 * count :])


def ring_order(rows_of, columns_of):
    if (rows_of, columns_of) != (4, 8):
        return list(range(rows_of * columns_of))
    order = []
    for z in range(4):
        for x in range(2):
            for y in range(2):
                chip = (z, 7 - z, 15 - z, 8 + z)[2 * x + y]
                order += [2 * chip, 2 * chip + 1]
    return order


def region_shift(own_layers):
    return 2 if own_layers == 4 else 0


def pack_kernel(
    order,
    initial_at, forcing_at, modulus_at, listing_at, table_at, out,
    initial, forcing, modulus, listing, table, rows, turned, places, ready,
):
    own_layers = EZ // len(order)
    sources = (listing_at, modulus_at, initial_at, forcing_at, table_at)
    copies = [
        pltpu.make_async_copy(source, here, ready.at[n])
        for n, (source, here) in enumerate(
            zip(sources, (listing, modulus, initial, forcing, table))
        )
    ]
    for copy in copies:
        copy.start()
    rows[108:128, :] = jnp.zeros((20, 384), jnp.float32)
    copies[0].wait()
    copies[1].wait()
    listed = listing[0].astype(jnp.float32)
    listed = jnp.concatenate([listed, jnp.full((1, 64), 256.0, jnp.float32)], 1)
    listed = jnp.broadcast_to(listed, (128, 256)).T
    lanes = lax.broadcasted_iota(jnp.int32, (256, 128), 1).astype(jnp.float32)
    row_at = lax.broadcasted_iota(jnp.int32, (128, 128), 0)
    stiff = jnp.zeros((128, 128), jnp.float32)
    for x in range(2):
        hit = jnp.max(jnp.where(listed == lanes + 128.0 * x, 1.0, 0.0), axis=0, keepdims=True)
        stiff = jnp.where(row_at == 108 + x, hit * modulus[x], stiff)
    copies[2].wait()
    copies[3].wait()
    for field, source in enumerate((initial, forcing)):
        for component in range(3):
            for layer in range(6):
                at = stack_row(field, component, layer, 0)
                rows[at : at + 3, :] = source[component, layer]
    for part in range(3):
        span = slice(128 * part, 128 * part + 128)
        turned[span, :] = rows[:, span].T
    picked = [turned[pl.ds(c, 128, stride=3), :] for c in range(3)]
    picked[0] = picked[0] + stiff.T
    copies[4].wait()
    wide = exact_pick(jnp.concatenate(picked, 1), table[...])
    lane = lax.broadcasted_iota(jnp.int32, (128, 128), 1)
    for x in range(2):
        tiles = [None] * (SENT // 128)
        for n in range(4):
            pair, field = n // 2, n % 2
            moved = wide[:, 128 * (2 * field + x) : 128 * (2 * field + x) + 128]
            first = BLOCK * n
            if pair:
                moved = pltpu.roll(moved, 128 - 2 * pair, 0)
            if first % 128:
                moved = pltpu.roll(moved, first % 128, 1)
            for tile in range(first // 128, (first + BLOCK - 1) // 128 + 1):
                before = tiles[tile]
                if before is None:
                    tiles[tile] = moved
                else:
                    tiles[tile] = jnp.where(lane >= first - 128 * tile, moved, before)
        for tile in range(SENT // 128):
            places[3 * x + tile, 0:128, :] = tiles[tile]
            places[3 * x + tile, 128:136, :] = jnp.zeros((8, 128), jnp.float32)
    for device, k in enumerate(order):
        for tile in range(SENT // 128):
            for x in range(2):
                at = 12 * device + 4 * tile + 2 * x
                out[at : at + 2, :] = places[
                    3 * x + tile, own_layers * k : own_layers * k + 2, :
                ]


def unpack_kernel(order, arrived, table, out, coarse_out, layers, turned):
    devices = arrived.shape[0]
    own_layers = EZ // devices
    for x in range(2):
        for layer in range(own_layers):
            row = (layer // 2) * 4 + x * 2 + layer % 2
            if order == sorted(order):
                layers[x, pl.ds(layer, devices, stride=own_layers), :] = arrived[:, row, :]
                continue
            for device, k in enumerate(order):
                at = (region_shift(own_layers) + own_layers * k + layer) % EZ
                layers[x, at : at + 1, :] = arrived[device, row : row + 1, :]
    wide = exact_pick(jnp.concatenate([layers[0], layers[1]], 1), table[...])
    for c in range(3):
        turned[pl.ds(c, 128, stride=3), :] = wide[:, 128 * c : 128 * c + 128]
    for part in range(3):
        span = slice(128 * part, 128 * part + 128)
        back = turned[span, :].T
        for component in range(3):
            for layer in range(6):
                at = stack_row(0, component, layer, 0)
                out[component, layer, :, span] = back[at : at + 3, :]
    back = wide[:, 0:128].T
    for component in range(3):
        for x in range(2):
            at = 54 + 2 * component + x
            coarse_out[component, x] = back[at : at + 1, :]


def cofactor_rows(deform):
    return [
        [
            deform[(row_at + 1) % 3][(column + 1) % 3] * deform[(row_at + 2) % 3][(column + 2) % 3]
            - deform[(row_at + 1) % 3][(column + 2) % 3]
            * deform[(row_at + 2) % 3][(column + 1) % 3]
            for column in range(3)
        ]
        for row_at in range(3)
    ]


def point_stress(deform, stiffness, stiffness_four):
    cofactors = cofactor_rows(deform)
    jacobian = (
        deform[0][0] * cofactors[0][0]
        + deform[0][1] * cofactors[0][1]
        + deform[0][2] * cofactors[0][2]
    )
    pressure = stiffness_four * (jacobian - rest_ratio)
    return [
        [stiffness * deform[i][d] + pressure * cofactors[i][d] for d in range(3)] for i in range(3)
    ]


coarse_samples = [0.5 - 0.5 / math.sqrt(3.0), 0.5 + 0.5 / math.sqrt(3.0)]
two = range(2)


def at_points(low, high):
    change = high - low
    return [low + s * change for s in coarse_samples], change * (1.0 / element_span)


def ends_of(first, second):
    high = coarse_samples[0] * first + coarse_samples[1] * second
    return [first + second - high, high]


def high_low(values):
    high = values.astype(jnp.bfloat16)
    return high, (values - high.astype(jnp.float32)).astype(jnp.bfloat16)


class Slab:
    def __init__(self, width, across):
        self.width = width
        self.y_step = 2 * across
        lane = lax.broadcasted_iota(jnp.int32, (8, width), 1)
        x = (lane // 2) % across
        self.bottom, self.top, self.even = x == 0, x == across - 1, lane % 2 == 0
        self.row = lax.broadcasted_iota(jnp.int32, (8, width), 0)
        row = lax.broadcasted_iota(jnp.int32, (32, width), 0)
        lane = lax.broadcasted_iota(jnp.int32, (32, width), 1)
        on_face = (row == 0) | ((row >= 3) & (row <= 11))
        self.keep = jnp.where(on_face & ((lane // 2) % across == 0), 0.0, 1.0)

    def lanes(self, v, step):
        return pltpu.roll(v, step % self.width, 1)

    def next_x(self, v):
        return jnp.where(self.top, 0.0, self.lanes(v, -2))

    def next_y(self, v):
        return self.lanes(v, -self.y_step)

    def next_z(self, v, ahead):
        return jnp.where(self.even, self.lanes(v, -1), self.lanes(ahead, 1))

    def onto_x(self, v):
        return jnp.where(self.bottom, 0.0, self.lanes(v, 2))

    def onto_y(self, v):
        return self.lanes(v, self.y_step)

    def gather(self, here, ahead):
        row = self.row
        g0, g1, g2, g3 = here[0:8], here[8:16], here[16:24], here[24:32]
        z0 = self.next_z(g0, ahead[0:8])
        z2 = self.next_z(g2, ahead[16:24])
        y0 = self.next_y(g0)
        yz, xz, xy = self.next_y(z0), self.next_x(z0), self.next_x(y0)
        edges = jnp.where(row <= 2, yz, jnp.where(row <= 4, xz, xy))
        return jnp.concatenate(
            [
                g0,
                g1,
                g2,
                jnp.where(row < 4, z2, g3),
                self.next_x(g0),
                jnp.where(row == 7, yz, y0),
                jnp.where(row == 7, xz, z0),
                jnp.where(row < 4, self.next_x(g1), self.next_y(g1)),
                jnp.where(row == 0, self.next_x(yz), edges),
                jnp.zeros_like(g0),
            ],
            0,
        )

    def scatter(self, part, behind):
        row = self.row
        g0, g1, g2, g3, x0, y0, z0, sides, edges = (part[8 * n : 8 * n + 8] for n in range(9))
        edges_x = self.onto_x(edges)
        yz = jnp.where(row == 0, edges_x, jnp.where(row == 7, y0, edges))
        yz = jnp.where((row <= 2) | (row == 7), yz, 0.0)
        z0 = jnp.where(row == 7, self.onto_x(z0), z0)
        z0 = z0 + jnp.where((row == 3) | (row == 4), edges_x, 0.0) + self.onto_y(yz)
        y0 = jnp.where(row == 7, edges_x, y0 + jnp.where(row >= 5, edges_x, 0.0))
        z2 = g3
        own0 = g0 + self.onto_x(x0) + self.onto_y(y0)
        own0 = own0 + jnp.where(self.even, behind[0], self.lanes(z0, 1))
        own1 = g1 + jnp.where(row < 4, self.onto_x(sides), self.onto_y(sides))
        share2 = jnp.where(self.even, behind[1], self.lanes(z2, 1))
        own2 = g2 + jnp.where(row < 4, share2, 0.0)
        own3 = jnp.where(row < 4, 0.0, g3)
        own0 = own0 + jnp.where(row == 0, pltpu.roll(own0, 1, 0), 0.0)
        own0 = jnp.where(row == 7, pltpu.roll(own0, 7, 0), own0)
        moved = (self.lanes(z0, -1), self.lanes(z2, -1))
        return jnp.concatenate([own0, own1, own2, own3], 0), moved

    def gradient(self, u, spread, pair):
        blocks = [
            self.gather(u[i, pair + q], u[i, pair + q + 1]) for i in range(3) for q in range(2)
        ]
        high, low = high_low(jnp.concatenate(blocks, 1))
        return jnp.dot(
            spread[...],
            jnp.concatenate([high, low, high], 0),
            preferred_element_type=jnp.float32,
        )

    def force(self, gradient, stiff, collect, pair):
        width = 2 * self.width
        stiffness = jnp.concatenate([stiff[pair + q : pair + q + 1, :] for q in range(2)], 1)
        deform = [
            [
                gradient[64 * e : 64 * e + 64, width * i : width * (i + 1)]
                + (1.0 if i == e else 0.0)
                for e in range(3)
            ]
            for i in range(3)
        ]
        stress = point_stress(deform, stiffness, lame_ratio * stiffness)
        stress = jnp.concatenate(
            [jnp.concatenate([stress[i][e] for i in range(3)], 1) for e in range(3)], 0
        )
        high, low = high_low(stress)
        force = jnp.dot(collect[...], high, preferred_element_type=jnp.float32)
        return force[0:ROWS] + (
            force[ROWS:] + jnp.dot(collect[0:ROWS], low, preferred_element_type=jnp.float32)
        )

    def apply(self, u, stiff, spread, collect, first, count, finish):
        width = self.width
        none = jnp.zeros((8, width), jnp.float32)
        carry = [(none, none) for i in range(3)]
        last = first + 2 * ((count + 1) // 2)
        ahead = self.gradient(u, spread, first)
        for pair in range(first, last, 2):
            gradient = ahead
            if pair + 2 < last:
                ahead = self.gradient(u, spread, pair + 2)
            force = self.force(gradient, stiff, collect, pair)
            totals = [[], []]
            for q in range(2):
                for i in range(3):
                    at = (2 * i + q) * width
                    total, carry[i] = self.scatter(force[:, at : at + width], carry[i])
                    totals[q].append(total)
            for q in range(2):
                finish(pair + q, totals[q])

    def smooth(self, u, f, f_shift, d, stiff, spread, collect, spans, bound):
        for (first, count), (held, added) in zip(spans, chebyshev_steps()):

            def finish(pair, forces, held=held, added=added):
                for i in range(3):
                    z = (added / bound) * self.keep * (f[i, pair + f_shift] - forces[i])
                    move = held * d[i, pair] + z if held else z
                    d[i, pair] = move
                    u[i, pair] = u[i, pair] + move

            self.apply(u, stiff, spread, collect, first, count, finish)

    def coarse_next_z(self, v):
        return self.next_z(v, pltpu.roll(v, 7, 0))

    def coarse_onto_z(self, v):
        return jnp.where(self.even, pltpu.roll(self.lanes(v, -1), 1, 0), self.lanes(v, 1))

    def corners_of(self, v):
        found = {(0, 0, 0): v, (0, 0, 1): self.coarse_next_z(v)}
        for c in range(2):
            found[0, 1, c] = self.next_y(found[0, 0, c])
        for b in range(2):
            for c in range(2):
                found[1, b, c] = self.next_x(found[0, b, c])
        return found

    def assemble(self, part):
        line = {
            (a, b): part[a, b, 0] + self.coarse_onto_z(part[a, b, 1])
            for a in range(2)
            for b in range(2)
        }
        face = [line[a, 0] + self.onto_y(line[a, 1]) for a in range(2)]
        return face[0] + self.onto_x(face[1])

    def coarse_force(self, values, stiffness):
        grads = []
        for i in range(3):
            v = self.corners_of(values[i])
            vz, sz = {}, {}
            for a in two:
                for b in two:
                    vz[a, b], sz[a, b] = at_points(v[a, b, 0], v[a, b, 1])
            vv, vs, sv = {}, {}, {}
            for a in two:
                for k in two:
                    vv[a, k], vs[a, k] = at_points(vz[a, 0][k], vz[a, 1][k])
                sv[a], unused = at_points(sz[a, 0], sz[a, 1])
            dx, dy, dz = {}, {}, {}
            for k in two:
                for j in two:
                    dx[j, k] = (vv[1, k][j] - vv[0, k][j]) * (1.0 / element_span)
                line, unused = at_points(vs[0, k], vs[1, k])
                for h in two:
                    dy[h, k] = line[h]
            for j in two:
                line, unused = at_points(sv[0][j], sv[1][j])
                for h in two:
                    dz[h, j] = line[h]
            grads.append((dx, dy, dz))
        weight = element_span**2 / 8.0
        scaled = weight * stiffness
        scaled_four = lame_ratio * scaled
        sums = [({}, {}, {}) for i in range(3)]

        def add(table, key, value):
            table[key] = table[key] + value if key in table else value

        for h in two:
            for j in two:
                for k in two:
                    deform = [
                        [grads[i][0][j, k], grads[i][1][h, k], grads[i][2][h, j]]
                        for i in range(3)
                    ]
                    for i in range(3):
                        deform[i][i] = deform[i][i] + 1.0
                    stress = point_stress(deform, scaled, scaled_four)
                    for i in range(3):
                        add(sums[i][0], (j, k), stress[i][0])
                        add(sums[i][1], (h, k), stress[i][1])
                        add(sums[i][2], (h, j), stress[i][2])

        forces = []
        for i in range(3):
            part = {}
            qx, qy, qz = sums[i]
            along_z = [ends_of(qx[j, 0], qx[j, 1]) for j in two]
            for c in two:
                line = ends_of(along_z[0][c], along_z[1][c])
                for b in two:
                    part[0, b, c] = -line[b]
                    part[1, b, c] = line[b]
            along_z = [ends_of(qy[h, 0], qy[h, 1]) for h in two]
            for c in two:
                line = ends_of(along_z[0][c], along_z[1][c])
                for a in two:
                    part[a, 0, c] = part[a, 0, c] - line[a]
                    part[a, 1, c] = part[a, 1, c] + line[a]
            along_y = [ends_of(qz[h, 0], qz[h, 1]) for h in two]
            for b in two:
                line = ends_of(along_y[0][b], along_y[1][b])
                for a in two:
                    part[a, b, 0] = part[a, b, 0] - line[a]
                    part[a, b, 1] = part[a, b, 1] + line[a]
            forces.append(self.assemble(part))
        return forces


def window_pair(slab, first_layer, own_layers, fetch):
    found = []
    for parity in range(2):
        layer = first_layer + parity
        device = layer // own_layers
        layer = layer - device * own_layers
        found.append((device, layer // 2, layer % 2))
    values = [fetch(device, q) for device, q, parity in found]
    if found[0][:2] == found[1][:2] or (values[0] is None and values[1] is None):
        return values[0]
    for parity in range(2):
        if values[parity] is None:
            values[parity] = jnp.zeros_like(values[1 - parity])
        elif found[parity][2] != parity:
            values[parity] = slab.lanes(values[parity], 2 * parity - 1)
    lane = lax.broadcasted_iota(jnp.int32, values[0].shape, 1)
    return jnp.where(lane % 2 == 0, values[0], values[1])


def first_sources(own_layers):
    return list(range(-BEFORE // own_layers, (own_layers + BEFORE - 1) // own_layers + 1))


def make_first_kernel(width, across, own_layers, fine_bound):
    own = BEFORE // 2
    own_pairs = (own_layers + 1) // 2
    spans = []
    for n in (4, 3, 2, 1):
        low, high = BEFORE - n, BEFORE + own_layers + n - 1
        spans.append((low // 2, (high + 1) // 2 - low // 2))

    sources = first_sources(own_layers)

    def first_kernel(*refs):
        arrived = refs[: len(sources)]
        refs = refs[len(sources) :]
        spread, collect, transfer, message, edge, f, u, d, stiff, shares, mixed, turned = refs
        slab = Slab(width, across)
        row = slab.row
        u[...] = jnp.zeros(u.shape, jnp.float32)
        f[...] = jnp.zeros(f.shape, jnp.float32)
        shares[...] = jnp.zeros(shares.shape, jnp.float32)
        stiff[...] = jnp.zeros(stiff.shape, jnp.float32)
        for n in range(len(sources)):
            for tile in range(SENT // 128):
                at = n * (SENT // 128) + tile
                for m in range(width // 4):
                    first = 12 * m + 4 * tile
                    mixed[at, 4 * m : 4 * m + 4, :] = arrived[n][first : first + 4, :]
                turned[n, 128 * tile : 128 * tile + 128, :] = mixed[at].T
        for field, target in enumerate((u, f)):
            for pair in range(PAIRS):

                def rows(start, field=field, pair=pair):
                    def fetch(device, q):
                        if device not in sources:
                            return None
                        at = BLOCK * (2 * q + field) + start
                        return turned[device - sources[0], at : at + 8, :]

                    value = window_pair(slab, 2 * pair - BEFORE, own_layers, fetch)
                    return jnp.zeros((8, width), jnp.float32) if value is None else value

                for i in range(3):
                    parts = [rows(24 * i + 8 * n) for n in range(3)]
                    if field == 0 and i == 0:
                        stiff[pair : pair + 1, :] = parts[0][TWIN : TWIN + 1]
                    parts[0] = jnp.where(row == TWIN, pltpu.roll(parts[0], TWIN, 0), parts[0])
                    parts.append(jnp.where(row < 4, 0.0, rows(68 + 4 * i)))
                    whole = jnp.concatenate(parts, 0)
                    target[i, pair] = whole * slab.keep if field == 0 else whole

        slab.smooth(u, f, 0, d, stiff, spread, collect, spans[0:3], fine_bound)

        weights = [jnp.broadcast_to(transfer[:, n : n + 1], (32, width)) for n in range(8)]

        def restrict(pair, forces):
            for i in range(3):
                rest = slab.keep * (f[i, pair] - forces[i])
                for n in range(8):
                    part = rest * weights[n]
                    part = (part[0:8] + part[8:16]) + (part[16:24] + part[24:32])
                    shares[i, n, pl.ds(pair, 1), :] = jnp.sum(part, axis=0, keepdims=True)

        slab.apply(u, stiff, spread, collect, *spans[3], restrict)

        restricted = [
            slab.assemble({corner: shares[i, n] for n, corner in enumerate(CORNERS)})
            for i in range(3)
        ]
        for q in range(own_pairs):
            hard = stiff[own + q : own + q + 1, :]
            for i in range(3):
                message[i, q] = u[i, own + q]
                message[i, q, RESTRICTED_SLOT : RESTRICTED_SLOT + 1, :] = restricted[i][
                    own + q : own + q + 1
                ]
                edge[q, i : i + 1, :] = u[i, own + q, 0:1, :]
                edge[q, 3 + i : 4 + i, :] = restricted[i][own + q : own + q + 1]
            message[0, q, STIFF_SLOT : STIFF_SLOT + 1, :] = hard
            edge[q, 6:8, :] = jnp.broadcast_to(hard, (2, width))

    return first_kernel


def sources_of(own_layers):
    shift = region_shift(own_layers)
    whole = range((shift - 3) // own_layers, (shift + own_layers + 2) // own_layers + 1)
    coarse = range((shift - 5) // own_layers, (shift + own_layers + 4) // own_layers + 1)
    return list(whole), [n for n in coarse if n not in whole]


def make_second_kernel(width, across, own_layers, fine_bound, coarse_bound):
    own = BEFORE_B // 2
    own_pairs = (own_layers + 1) // 2
    first_layer = region_shift(own_layers) - BEFORE_B
    shift = (BEFORE + first_layer) // 2
    whole, outer = sources_of(own_layers)
    steps = chebyshev_steps()
    spans = []
    for n in (3, 2, 1):
        low, high = BEFORE_B - n, BEFORE_B + own_layers + n - 1
        spans.append((low // 2, (high + 1) // 2 - low // 2))

    def second_kernel(*refs):
        messages = dict(zip(whole, refs))
        refs = refs[len(whole) :]
        edges = dict(zip(outer, refs))
        f, spread, collect, transfer_back, out, u, d, stiff, coarse = refs[len(outer) :]
        slab = Slab(width, across)

        def pair_of(pair, fetch):
            return window_pair(slab, first_layer + 2 * pair, own_layers, fetch)

        u[...] = jnp.zeros(u.shape, jnp.float32)
        coarse[...] = jnp.zeros(coarse.shape, jnp.float32)
        d[...] = jnp.zeros(d.shape, jnp.float32)
        for pair in range(PAIRS_B):
            for i in range(3):
                block = pair_of(pair, lambda n, q: messages[n][i, q] if n in messages else None)
                if block is not None:
                    u[i, pair] = block
            for n in range(7):

                def fetch(device, q, n=n):
                    if device in messages:
                        i, slot = ((n, 0), (n - 3, RESTRICTED_SLOT), (0, STIFF_SLOT))[n // 3]
                        return messages[device][i, q, slot : slot + 1, :]
                    return edges[device][q, n : n + 1, :] if device in edges else None

                line = pair_of(pair, fetch)
                if line is not None:
                    coarse[n, pair : pair + 1, :] = line
        stiff[...] = coarse[6]

        stiffness = coarse[6]
        keep_coarse = jnp.where(slab.bottom, 0.0, 1.0)
        start = [coarse[i] for i in range(3)]
        restricted = [coarse[3 + i] for i in range(3)]
        before = slab.coarse_force(start, stiffness)
        move = [(steps[0][1] / coarse_bound) * keep_coarse * restricted[i] for i in range(3)]
        level = [start[i] + move[i] for i in range(3)]
        for held, added in steps[1:]:
            force = slab.coarse_force(level, stiffness)
            for i in range(3):
                z = keep_coarse * (restricted[i] + before[i] - force[i])
                move[i] = held * move[i] + (added / coarse_bound) * z
                level[i] = level[i] + move[i]

        weights = [jnp.broadcast_to(transfer_back[:, n : n + 1], (32, width)) for n in range(8)]
        for i in range(3):
            change = slab.corners_of(level[i] - start[i])
            for pair in range(spans[0][0], min(spans[0][0] + spans[0][1] + 1, PAIRS_B)):
                lift = u[i, pair]
                for n, corner in enumerate(CORNERS):
                    lift = lift + weights[n] * change[corner][pair : pair + 1]
                u[i, pair] = lift

        slab.smooth(u, f, shift, d, stiff, spread, collect, spans, fine_bound)

        lower = lax.broadcasted_iota(jnp.int32, (width // 8, 8, 128), 1) < 4
        sides = []
        blank = jnp.zeros((29, width), jnp.float32)
        for q in range(2):
            ends_here = jnp.concatenate(
                [u[i, own + q] for i in range(3)]
                + [level[i][own + q : own + q + 1] for i in range(3)]
                + [blank],
                0,
            )
            sides.append(ends_here.T.reshape(width // 8, 8, 128))
        out[:, 0] = jnp.where(lower, sides[0], pltpu.roll(sides[1], 4, 1))
        out[:, 1] = jnp.where(lower, pltpu.roll(sides[0], 4, 1), sides[1])

    return second_kernel


def solution(mesh):
    rows_of, columns_of = mesh.shape["gx"], mesh.shape["gy"]
    devices = rows_of * columns_of
    order = ring_order(rows_of, columns_of)
    own_layers = EZ // devices
    own_pairs = (own_layers + 1) // 2
    width = 4 * devices
    across = 2 * rows_of
    near = first_sources(own_layers)
    whole, outer = sources_of(own_layers)
    spread, collect, fine_bound = element_tables()
    coarse_bound = build_tables([0.0, 1.0], 2)[2]
    transfer, transfer_back = transfer_table()
    wide = pltpu.CompilerParams(vmem_limit_bytes=60 * 1024 * 1024)
    limit = pltpu.CompilerParams(vmem_limit_bytes=48 * 1024 * 1024)
    f32 = jnp.float32

    pack = pl.pallas_call(
        functools.partial(pack_kernel, order),
        out_shape=jax.ShapeDtypeStruct((devices * 12, 128), f32),
        in_specs=[pl.BlockSpec(memory_space=pl.ANY)] * 5,
        out_specs=pl.BlockSpec(memory_space=pltpu.VMEM),
        scratch_shapes=[
            pltpu.VMEM((3, 6, 3, 384), f32),
            pltpu.VMEM((3, 6, 3, 384), f32),
            pltpu.VMEM((2, 1, EZ), f32),
            pltpu.VMEM((1, 1, 192), jnp.int32),
            pltpu.VMEM((384, 512), jnp.bfloat16),
            pltpu.VMEM((128, 384), f32),
            pltpu.VMEM((384, 128), f32),
            pltpu.VMEM((6, 136, 128), f32),
            pltpu.SemaphoreType.DMA((5,)),
        ],
        compiler_params=wide,
    )
    first = pl.pallas_call(
        make_first_kernel(width, across, own_layers, fine_bound),
        out_shape=(
            jax.ShapeDtypeStruct((3, own_pairs, 32, width), f32),
            jax.ShapeDtypeStruct((own_pairs, 8, width), f32),
            jax.ShapeDtypeStruct((3, PAIRS_B, 32, width), f32),
        ),
        scratch_shapes=[
            pltpu.VMEM((3, 8, 32, width), f32),
            pltpu.VMEM((3, 8, 32, width), f32),
            pltpu.VMEM((8, width), f32),
            pltpu.VMEM((3, 8, 8, width), f32),
            pltpu.VMEM((len(near) * (SENT // 128), width, 128), f32),
            pltpu.VMEM((len(near), SENT, width), f32),
        ],
        compiler_params=limit,
    )
    second = pl.pallas_call(
        make_second_kernel(width, across, own_layers, fine_bound, coarse_bound),
        out_shape=jax.ShapeDtypeStruct((devices // 2, 2, 8, 128), f32),
        scratch_shapes=[
            pltpu.VMEM((3, PAIRS_B + 2, 32, width), f32),
            pltpu.VMEM((3, PAIRS_B, 32, width), f32),
            pltpu.VMEM((PAIRS_B, width), f32),
            pltpu.VMEM((7, PAIRS_B, width), f32),
        ],
        compiler_params=limit,
    )
    unpack = pl.pallas_call(
        functools.partial(unpack_kernel, order),
        out_shape=(
            jax.ShapeDtypeStruct((3, 6, 3, 384), f32),
            jax.ShapeDtypeStruct((3, 2, 1, EZ), f32),
        ),
        scratch_shapes=[pltpu.VMEM((2, 128, 128), f32), pltpu.VMEM((384, 128), f32)],
        compiler_params=limit,
    )
    everyone = ("gy", "gx")

    def from_device(block, distance):
        place = {k: m % rows_of * columns_of + m // rows_of for m, k in enumerate(order)}
        route = [(place[(k + distance) % devices], place[k]) for k in range(devices)]
        return lax.ppermute(block, ("gx", "gy"), route)

    def body(initial, forcing, modulus, solid_list):
        sent = pack(initial, forcing, modulus, solid_list, jnp.asarray(pack_table()))
        sent = sent.reshape(devices, SENT // 128, 4, 128)
        arrived = lax.all_to_all(sent, everyone, 0, 0, tiled=True).reshape(devices * 12, 128)
        message, edge, load = first(
            *[from_device(arrived, n) if n else arrived for n in near],
            jnp.asarray(spread),
            jnp.asarray(collect),
            jnp.asarray(transfer),
        )
        messages = [from_device(message, n) if n else message for n in whole]
        edges = [from_device(edge, n) for n in outer]
        result = second(
            *messages,
            *edges,
            load,
            jnp.asarray(spread),
            jnp.asarray(collect),
            jnp.asarray(transfer_back),
        )
        back = lax.all_to_all(result.reshape(devices, 8, 128), everyone, 0, 0, tiled=True)
        return unpack(back, jnp.asarray(unpack_table()))

    placed = (
        P(None, "gx", "gy", None),
        P(None, "gx", "gy", None),
        P("gx", "gy", None),
        P("gx", "gy", None),
    )
    return jax.shard_map(
        body,
        mesh=mesh,
        in_specs=placed,
        out_specs=(P(None, "gx", "gy", None), P(None, "gx", "gy", None)),
        check_vma=False,
    )
```

```python
import functools
import math

import jax
import jax.numpy as jnp
import numpy as np
from jax import lax
from jax.experimental import pallas as pl
from jax.experimental.pallas import tpu as pltpu
from jax.sharding import PartitionSpec as P

CHEB = 3
EZ = 128

element_span = 20.0
lame_ratio = 4.0
rest_ratio = 1.25
modulus_top = 2.0
spectrum_floor = 0.05
interval_centre = (1.0 + spectrum_floor) / 2.0
interval_radius = (1.0 - spectrum_floor) / 2.0
interval_ratio = interval_centre / interval_radius
inner_anchors = (0.5 - 0.5 / math.sqrt(5.0), 0.5 + 0.5 / math.sqrt(5.0))

BEFORE = 4
PAIRS = 6
BEFORE_B = 6
PAIRS_B = 8
BLOCK = 84
SENT = 384

SLOTS = [
    (0, 0, 0), (1, 0, 0), (2, 0, 0), (0, 1, 0), (0, 2, 0), (0, 0, 1), (0, 0, 2), None,
    (0, 1, 1), (0, 1, 2), (0, 2, 1), (0, 2, 2), (1, 0, 1), (1, 0, 2), (2, 0, 1), (2, 0, 2),
    (1, 1, 0), (1, 2, 0), (2, 1, 0), (2, 2, 0), (1, 1, 1), (1, 1, 2), (1, 2, 1), (1, 2, 2),
    None, None, None, None, (2, 1, 1), (2, 1, 2), (2, 2, 1), (2, 2, 2),
]
TWIN = 7
RESTRICTED_SLOT = 24
STIFF_SLOT = 25
OWN_SHIFT, SHIFT_X, SHIFT_Y, SHIFT_Z = (0, 0, 0), (1, 0, 0), (0, 1, 0), (0, 0, 1)
ELEMENT_ROWS = (
    [(slot, OWN_SHIFT) for slot in range(24)]
    + [(slot, SHIFT_Z) for slot in range(16, 20)]
    + [(slot, OWN_SHIFT) for slot in range(28, 32)]
    + [(slot, SHIFT_X) for slot in range(7)] + [None]
    + [(slot, SHIFT_Y) for slot in range(7)] + [(0, (0, 1, 1))]
    + [(slot, SHIFT_Z) for slot in range(7)] + [(0, (1, 0, 1))]
    + [(slot, SHIFT_X) for slot in range(8, 12)] + [(slot, SHIFT_Y) for slot in range(12, 16)]
    + [(0, (1, 1, 1)), (1, (0, 1, 1)), (2, (0, 1, 1)), (3, (1, 0, 1)), (4, (1, 0, 1))]
    + [(5, (1, 1, 0)), (6, (1, 1, 0)), (0, (1, 1, 0))]
)
ROWS = len(ELEMENT_ROWS)
DEPTH = 80
CORNERS = [(a, b, c) for a in range(2) for b in range(2) for c in range(2)]


def gauss_rule(point_count):
    if point_count == 2:
        offset = 1.0 / math.sqrt(3.0)
        points = [-offset, offset]
        weights = [1.0, 1.0]
    else:
        inner = math.sqrt(3.0 / 7.0 - 2.0 / 7.0 * math.sqrt(6.0 / 5.0))
        outer = math.sqrt(3.0 / 7.0 + 2.0 / 7.0 * math.sqrt(6.0 / 5.0))
        heavy = (18.0 + math.sqrt(30.0)) / 36.0
        light = (18.0 - math.sqrt(30.0)) / 36.0
        points = [-outer, -inner, inner, outer]
        weights = [light, heavy, heavy, light]
    return (np.array(points), np.array(weights))


def lagrange_tables(anchors, samples):
    values = np.zeros((len(samples), len(anchors)))
    slopes = np.zeros((len(samples), len(anchors)))
    for sample_index, sample in enumerate(samples):
        for anchor_index, anchor in enumerate(anchors):
            others = [
                location
                for location_index, location in enumerate(anchors)
                if location_index != anchor_index
            ]
            product = 1.0
            for location in others:
                product = product * (sample - location) / (anchor - location)
            values[sample_index, anchor_index] = product
            derivative = 0.0
            for skipped in range(len(others)):
                summand = 1.0 / (anchor - others[skipped])
                for kept_index in range(len(others)):
                    if kept_index != skipped:
                        summand = (
                            summand * (sample - others[kept_index]) / (anchor - others[kept_index])
                        )
                derivative = derivative + summand
            slopes[sample_index, anchor_index] = derivative
    return (values, slopes)


def outer_three(first, second, third):
    return (
        first[:, None, None, :, None, None]
        * second[None, :, None, None, :, None]
        * third[None, None, :, None, None, :]
    )


def build_tables(anchors, point_count):
    raw_points, raw_weights = gauss_rule(point_count)
    samples = (raw_points + 1.0) / 2.0
    weights = raw_weights / 2.0
    basis_values, slopes = lagrange_tables(anchors, samples)
    quad_total = point_count**3
    nodal_count = len(anchors) ** 3
    derivative_one = outer_three(slopes, basis_values, basis_values).reshape(
        quad_total, nodal_count
    )
    derivative_two = outer_three(basis_values, slopes, basis_values).reshape(
        quad_total, nodal_count
    )
    derivative_three = outer_three(basis_values, basis_values, slopes).reshape(
        quad_total, nodal_count
    )
    stacked = np.stack([derivative_one, derivative_two, derivative_three]) / element_span
    volume = (weights[:, None, None] * weights[None, :, None] * weights[None, None, :]).reshape(
        -1
    ) * element_span**3
    forward = stacked.reshape(3 * quad_total, nodal_count)
    backward = (stacked * volume[None, :, None]).reshape(3 * quad_total, nodal_count).T
    weighted = stacked * volume[None, :, None]
    laplace = weighted[0].T @ stacked[0] + weighted[1].T @ stacked[1] + weighted[2].T @ stacked[2]
    matrix = np.zeros((nodal_count, 3, nodal_count, 3))
    for first in range(3):
        for second in range(3):
            block = weighted[second].T @ stacked[first] + (lame_ratio - 1.0) * (
                weighted[first].T @ stacked[second]
            )
            if first == second:
                block = block + laplace
            matrix[:, first, :, second] = block
    matrix = matrix.reshape(3 * nodal_count, 3 * nodal_count)
    vector = 1.5 + np.cos(1.3 * np.arange(3 * nodal_count))
    for repeat in range(200):
        vector = matrix @ vector
        vector = vector / np.sqrt(vector @ vector)
    largest = vector @ (matrix @ vector)
    return (forward, backward, float(4.0 * modulus_top * 1.1 * largest))


def row_nodes():
    nodes = []
    for entry in ELEMENT_ROWS:
        slot = SLOTS[entry[0]] if entry else None
        if slot is None or any(s and n for s, n in zip(entry[1], slot)):
            nodes.append(None)
        else:
            a, b, c = (3 * s + n for s, n in zip(entry[1], slot))
            nodes.append(16 * a + 4 * b + c)
    return nodes


def halves(matrix):
    whole = np.asarray(matrix, np.float32)
    high = whole.astype(jnp.bfloat16)
    low = (whole - high.astype(np.float32)).astype(jnp.bfloat16)
    return high, low


def element_tables():
    forward, backward, bound = build_tables([0.0, inner_anchors[0], inner_anchors[1], 1.0], 4)
    spread = np.zeros((forward.shape[0], DEPTH))
    collect = np.zeros((ROWS, backward.shape[1]))
    for row, node in enumerate(row_nodes()):
        if node is not None:
            spread[:, row] = forward[:, node]
            collect[row, :] = backward[node, :]
    spread_high, spread_low = halves(spread)
    collect_high, collect_low = halves(collect)
    return (
        np.concatenate([spread_high, spread_high, spread_low], 1),
        np.concatenate([collect_high, collect_low], 0),
        bound,
    )


def transfer_table():
    table = np.zeros((8, 32))
    reach = (0.0, inner_anchors[0], inner_anchors[1])
    for row, corner in enumerate(CORNERS):
        for column, slot in enumerate(SLOTS):
            if slot is not None:
                weight = 1.0
                for side, node in zip(corner, slot):
                    weight = weight * (reach[node] if side else 1.0 - reach[node])
                table[row, column] = weight
    back = table.T.copy()
    back[TWIN] = back[0]
    return table.T.astype(np.float32), back.astype(np.float32)


def chebyshev_steps():
    steps = [(0.0, 1.0 / interval_centre)]
    ratio_now = 1.0 / interval_ratio
    for sweep in range(1, CHEB):
        ratio_next = 1.0 / (2.0 * interval_ratio - ratio_now)
        steps.append((ratio_next * ratio_now, 2.0 * ratio_next / interval_radius))
        ratio_now = ratio_next
    return steps


def stack_row(field, component, layer, b):
    return field * 54 + component * 18 + layer * 3 + b


def block_column(component, slot):
    return 72 + 4 * component + slot - 28 if slot >= 24 else 24 * component + slot


def pack_table():
    table = np.zeros((3, 128, 2, 2, 128), np.float32)
    for field in range(2):
        for x in range(2):
            for component in range(3):
                for column, slot in enumerate(SLOTS):
                    if slot is not None:
                        a, b, c = slot
                        row = stack_row(field, component, 3 * x + a, b)
                        table[c, row, field, x, block_column(component, column)] = 1.0
            table[0, 108 + x, 0, x, TWIN] = 1.0
    return table.reshape(384, 512).astype(jnp.bfloat16)


def unpack_table():
    table = np.zeros((2, 128, 3, 128), np.float32)
    for x in range(2):
        for component in range(3):
            for column, slot in enumerate(SLOTS):
                if slot is not None:
                    a, b, c = slot
                    row = stack_row(0, component, 3 * x + a, b)
                    table[x, component * 32 + column, c, row] = 1.0
            table[x, 96 + component, 0, 54 + 2 * component + x] = 1.0
    return table.reshape(256, 384).astype(jnp.bfloat16)


def pick(values, table):
    count = values.shape[0]
    parts = jnp.dot(
        jnp.concatenate(high_low(values), 0), table, preferred_element_type=jnp.float32
    )
    return parts[:count] + parts[count:]


def ring_order(rows_of, columns_of):
    if (rows_of, columns_of) != (4, 8):
        return list(range(rows_of * columns_of))
    order = []
    for z in range(4):
        for x in range(2):
            for y in range(2):
                chip = (z, 7 - z, 15 - z, 8 + z)[2 * x + y]
                order += [2 * chip, 2 * chip + 1]
    return order


def pack_kernel(
    order,
    initial_at, forcing_at, modulus_at, listing_at, table_at, out,
    initial, forcing, modulus, listing, table, rows, turned, places, ready,
):
    own_layers = EZ // len(order)
    sources = (listing_at, modulus_at, initial_at, forcing_at, table_at)
    copies = [
        pltpu.make_async_copy(source, here, ready.at[n])
        for n, (source, here) in enumerate(
            zip(sources, (listing, modulus, initial, forcing, table))
        )
    ]
    for copy in copies:
        copy.start()
    rows[108:128, :] = jnp.zeros((20, 384), jnp.float32)
    copies[0].wait()
    copies[1].wait()
    listed = listing[0].astype(jnp.float32)
    listed = jnp.concatenate([listed, jnp.full((1, 64), 256.0, jnp.float32)], 1)
    listed = jnp.broadcast_to(listed, (128, 256)).T
    lanes = lax.broadcasted_iota(jnp.int32, (256, 128), 1).astype(jnp.float32)
    row_at = lax.broadcasted_iota(jnp.int32, (128, 128), 0)
    stiff = jnp.zeros((128, 128), jnp.float32)
    for x in range(2):
        hit = jnp.max(jnp.where(listed == lanes + 128.0 * x, 1.0, 0.0), axis=0, keepdims=True)
        stiff = jnp.where(row_at == 108 + x, hit * modulus[x], stiff)
    copies[2].wait()
    copies[3].wait()
    for field, source in enumerate((initial, forcing)):
        for component in range(3):
            for layer in range(6):
                at = stack_row(field, component, layer, 0)
                rows[at : at + 3, :] = source[component, layer]
    for part in range(3):
        span = slice(128 * part, 128 * part + 128)
        turned[span, :] = rows[:, span].T
    picked = [turned[pl.ds(c, 128, stride=3), :] for c in range(3)]
    picked[0] = picked[0] + stiff.T
    copies[4].wait()
    wide = pick(jnp.concatenate(picked, 1), table[...])
    lane = lax.broadcasted_iota(jnp.int32, (128, 128), 1)
    for x in range(2):
        tiles = [None] * (SENT // 128)
        for n in range(4):
            pair, field = n // 2, n % 2
            moved = wide[:, 128 * (2 * field + x) : 128 * (2 * field + x) + 128]
            first = BLOCK * n
            if pair:
                moved = pltpu.roll(moved, 128 - 2 * pair, 0)
            if first % 128:
                moved = pltpu.roll(moved, first % 128, 1)
            for tile in range(first // 128, (first + BLOCK - 1) // 128 + 1):
                before = tiles[tile]
                if before is None:
                    tiles[tile] = moved
                else:
                    tiles[tile] = jnp.where(lane >= first - 128 * tile, moved, before)
        for tile in range(SENT // 128):
            places[3 * x + tile, 0:128, :] = tiles[tile]
            places[3 * x + tile, 128:136, :] = jnp.zeros((8, 128), jnp.float32)
    for device, k in enumerate(order):
        for tile in range(SENT // 128):
            for x in range(2):
                at = 12 * device + 4 * tile + 2 * x
                out[at : at + 2, :] = places[
                    3 * x + tile, own_layers * k : own_layers * k + 2, :
                ]


def unpack_kernel(order, arrived, table, out, coarse_out, layers, turned):
    devices = arrived.shape[0]
    own_layers = EZ // devices
    for x in range(2):
        for layer in range(own_layers):
            row = (layer // 2) * 4 + x * 2 + layer % 2
            if order == sorted(order):
                layers[x, pl.ds(layer, devices, stride=own_layers), :] = arrived[:, row, :]
                continue
            for device, k in enumerate(order):
                at = own_layers * k + layer
                layers[x, at : at + 1, :] = arrived[device, row : row + 1, :]
    wide = pick(jnp.concatenate([layers[0], layers[1]], 1), table[...])
    for c in range(3):
        turned[pl.ds(c, 128, stride=3), :] = wide[:, 128 * c : 128 * c + 128]
    for part in range(3):
        span = slice(128 * part, 128 * part + 128)
        back = turned[span, :].T
        for component in range(3):
            for layer in range(6):
                at = stack_row(0, component, layer, 0)
                out[component, layer, :, span] = back[at : at + 3, :]
    back = wide[:, 0:128].T
    for component in range(3):
        for x in range(2):
            at = 54 + 2 * component + x
            coarse_out[component, x] = back[at : at + 1, :]


def cofactor_rows(deform):
    return [
        [
            deform[(row_at + 1) % 3][(column + 1) % 3] * deform[(row_at + 2) % 3][(column + 2) % 3]
            - deform[(row_at + 1) % 3][(column + 2) % 3]
            * deform[(row_at + 2) % 3][(column + 1) % 3]
            for column in range(3)
        ]
        for row_at in range(3)
    ]


def point_stress(deform, stiffness, stiffness_four):
    cofactors = cofactor_rows(deform)
    jacobian = (
        deform[0][0] * cofactors[0][0]
        + deform[0][1] * cofactors[0][1]
        + deform[0][2] * cofactors[0][2]
    )
    pressure = stiffness_four * (jacobian - rest_ratio)
    return [
        [stiffness * deform[i][d] + pressure * cofactors[i][d] for d in range(3)] for i in range(3)
    ]


coarse_samples = [0.5 - 0.5 / math.sqrt(3.0), 0.5 + 0.5 / math.sqrt(3.0)]
two = range(2)


def at_points(low, high):
    change = high - low
    return [low + s * change for s in coarse_samples], change * (1.0 / element_span)


def ends_of(first, second):
    high = coarse_samples[0] * first + coarse_samples[1] * second
    return [first + second - high, high]


def high_low(values):
    high = values.astype(jnp.bfloat16)
    return high, (values - high.astype(jnp.float32)).astype(jnp.bfloat16)


class Slab:
    def __init__(self, width, across):
        self.width = width
        self.y_step = 2 * across
        lane = lax.broadcasted_iota(jnp.int32, (8, width), 1)
        x = (lane // 2) % across
        self.bottom, self.top, self.even = x == 0, x == across - 1, lane % 2 == 0
        self.row = lax.broadcasted_iota(jnp.int32, (8, width), 0)
        row = lax.broadcasted_iota(jnp.int32, (32, width), 0)
        lane = lax.broadcasted_iota(jnp.int32, (32, width), 1)
        on_face = (row == 0) | ((row >= 3) & (row <= 11))
        self.keep = jnp.where(on_face & ((lane // 2) % across == 0), 0.0, 1.0)

    def lanes(self, v, step):
        return pltpu.roll(v, step % self.width, 1)

    def next_x(self, v):
        return jnp.where(self.top, 0.0, self.lanes(v, -2))

    def next_y(self, v):
        return self.lanes(v, -self.y_step)

    def next_z(self, v, ahead):
        return jnp.where(self.even, self.lanes(v, -1), self.lanes(ahead, 1))

    def onto_x(self, v):
        return jnp.where(self.bottom, 0.0, self.lanes(v, 2))

    def onto_y(self, v):
        return self.lanes(v, self.y_step)

    def gather(self, here, ahead):
        row = self.row
        g0, g1, g2, g3 = here[0:8], here[8:16], here[16:24], here[24:32]
        z0 = self.next_z(g0, ahead[0:8])
        z2 = self.next_z(g2, ahead[16:24])
        y0 = self.next_y(g0)
        yz, xz, xy = self.next_y(z0), self.next_x(z0), self.next_x(y0)
        edges = jnp.where(row <= 2, yz, jnp.where(row <= 4, xz, xy))
        return jnp.concatenate(
            [
                g0,
                g1,
                g2,
                jnp.where(row < 4, z2, g3),
                self.next_x(g0),
                jnp.where(row == 7, yz, y0),
                jnp.where(row == 7, xz, z0),
                jnp.where(row < 4, self.next_x(g1), self.next_y(g1)),
                jnp.where(row == 0, self.next_x(yz), edges),
                jnp.zeros_like(g0),
            ],
            0,
        )

    def scatter(self, part, behind):
        row = self.row
        g0, g1, g2, g3, x0, y0, z0, sides, edges = (part[8 * n : 8 * n + 8] for n in range(9))
        edges_x = self.onto_x(edges)
        yz = jnp.where(row == 0, edges_x, jnp.where(row == 7, y0, edges))
        yz = jnp.where((row <= 2) | (row == 7), yz, 0.0)
        z0 = jnp.where(row == 7, self.onto_x(z0), z0)
        z0 = z0 + jnp.where((row == 3) | (row == 4), edges_x, 0.0) + self.onto_y(yz)
        y0 = jnp.where(row == 7, edges_x, y0 + jnp.where(row >= 5, edges_x, 0.0))
        z2 = g3
        own0 = g0 + self.onto_x(x0) + self.onto_y(y0)
        own0 = own0 + jnp.where(self.even, behind[0], self.lanes(z0, 1))
        own1 = g1 + jnp.where(row < 4, self.onto_x(sides), self.onto_y(sides))
        share2 = jnp.where(self.even, behind[1], self.lanes(z2, 1))
        own2 = g2 + jnp.where(row < 4, share2, 0.0)
        own3 = jnp.where(row < 4, 0.0, g3)
        own0 = own0 + jnp.where(row == 0, pltpu.roll(own0, 1, 0), 0.0)
        own0 = jnp.where(row == 7, pltpu.roll(own0, 7, 0), own0)
        moved = (self.lanes(z0, -1), self.lanes(z2, -1))
        return jnp.concatenate([own0, own1, own2, own3], 0), moved

    def gradient(self, u, spread, pairs):
        blocks = [self.gather(u[i, pair], u[i, pair + 1]) for i in range(3) for pair in pairs]
        high, low = high_low(jnp.concatenate(blocks, 1))
        return jnp.dot(
            spread[...],
            jnp.concatenate([high, low, high], 0),
            preferred_element_type=jnp.float32,
        )

    def force(self, gradient, stiff, collect, pairs):
        width = len(pairs) * self.width
        stiffness = jnp.concatenate([stiff[pair : pair + 1, :] for pair in pairs], 1)
        deform = [
            [
                gradient[64 * e : 64 * e + 64, width * i : width * (i + 1)]
                + (1.0 if i == e else 0.0)
                for e in range(3)
            ]
            for i in range(3)
        ]
        stress = point_stress(deform, stiffness, lame_ratio * stiffness)
        stress = jnp.concatenate(
            [jnp.concatenate([stress[i][e] for i in range(3)], 1) for e in range(3)], 0
        )
        high, low = high_low(stress)
        force = jnp.dot(collect[...], high, preferred_element_type=jnp.float32)
        return force[0:ROWS] + (
            force[ROWS:] + jnp.dot(collect[0:ROWS], low, preferred_element_type=jnp.float32)
        )

    def apply(self, u, stiff, spread, collect, first, count, finish):
        width = self.width
        none = jnp.zeros((8, width), jnp.float32)
        carry = [(none, none) for i in range(3)]
        last = first + count
        steps = [list(range(at, min(at + 2, last))) for at in range(first, last, 2)]
        ahead = self.gradient(u, spread, steps[0])
        for n, pairs in enumerate(steps):
            gradient = ahead
            if n + 1 < len(steps):
                ahead = self.gradient(u, spread, steps[n + 1])
            force = self.force(gradient, stiff, collect, pairs)
            totals = [[] for pair in pairs]
            for q in range(len(pairs)):
                for i in range(3):
                    at = (len(pairs) * i + q) * width
                    total, carry[i] = self.scatter(force[:, at : at + width], carry[i])
                    totals[q].append(total)
            for pair, total in zip(pairs, totals):
                finish(pair, total)

    def smooth(self, u, f, f_shift, d, stiff, spread, collect, spans, bound):
        for (first, count), (held, added) in zip(spans, chebyshev_steps()):

            def finish(pair, forces, held=held, added=added):
                for i in range(3):
                    z = (added / bound) * self.keep * (f[i, pair + f_shift] - forces[i])
                    move = held * d[i, pair] + z if held else z
                    d[i, pair] = move
                    u[i, pair] = u[i, pair] + move

            self.apply(u, stiff, spread, collect, first, count, finish)

    def coarse_next_z(self, v):
        return self.next_z(v, pltpu.roll(v, 7, 0))

    def coarse_onto_z(self, v):
        return jnp.where(self.even, pltpu.roll(self.lanes(v, -1), 1, 0), self.lanes(v, 1))

    def corners_of(self, v):
        found = {(0, 0, 0): v, (0, 0, 1): self.coarse_next_z(v)}
        for c in range(2):
            found[0, 1, c] = self.next_y(found[0, 0, c])
        for b in range(2):
            for c in range(2):
                found[1, b, c] = self.next_x(found[0, b, c])
        return found

    def assemble(self, part):
        line = {
            (a, b): part[a, b, 0] + self.coarse_onto_z(part[a, b, 1])
            for a in range(2)
            for b in range(2)
        }
        face = [line[a, 0] + self.onto_y(line[a, 1]) for a in range(2)]
        return face[0] + self.onto_x(face[1])

    def coarse_force(self, values, stiffness):
        grads = []
        for i in range(3):
            v = self.corners_of(values[i])
            vz, sz = {}, {}
            for a in two:
                for b in two:
                    vz[a, b], sz[a, b] = at_points(v[a, b, 0], v[a, b, 1])
            vv, vs, sv = {}, {}, {}
            for a in two:
                for k in two:
                    vv[a, k], vs[a, k] = at_points(vz[a, 0][k], vz[a, 1][k])
                sv[a], unused = at_points(sz[a, 0], sz[a, 1])
            dx, dy, dz = {}, {}, {}
            for k in two:
                for j in two:
                    dx[j, k] = (vv[1, k][j] - vv[0, k][j]) * (1.0 / element_span)
                line, unused = at_points(vs[0, k], vs[1, k])
                for h in two:
                    dy[h, k] = line[h]
            for j in two:
                line, unused = at_points(sv[0][j], sv[1][j])
                for h in two:
                    dz[h, j] = line[h]
            grads.append((dx, dy, dz))
        weight = element_span**2 / 8.0
        scaled = weight * stiffness
        scaled_four = lame_ratio * scaled
        sums = [({}, {}, {}) for i in range(3)]

        def add(table, key, value):
            table[key] = table[key] + value if key in table else value

        for h in two:
            for j in two:
                for k in two:
                    deform = [
                        [grads[i][0][j, k], grads[i][1][h, k], grads[i][2][h, j]]
                        for i in range(3)
                    ]
                    for i in range(3):
                        deform[i][i] = deform[i][i] + 1.0
                    stress = point_stress(deform, scaled, scaled_four)
                    for i in range(3):
                        add(sums[i][0], (j, k), stress[i][0])
                        add(sums[i][1], (h, k), stress[i][1])
                        add(sums[i][2], (h, j), stress[i][2])

        forces = []
        for i in range(3):
            part = {}
            qx, qy, qz = sums[i]
            along_z = [ends_of(qx[j, 0], qx[j, 1]) for j in two]
            for c in two:
                line = ends_of(along_z[0][c], along_z[1][c])
                for b in two:
                    part[0, b, c] = -line[b]
                    part[1, b, c] = line[b]
            along_z = [ends_of(qy[h, 0], qy[h, 1]) for h in two]
            for c in two:
                line = ends_of(along_z[0][c], along_z[1][c])
                for a in two:
                    part[a, 0, c] = part[a, 0, c] - line[a]
                    part[a, 1, c] = part[a, 1, c] + line[a]
            along_y = [ends_of(qz[h, 0], qz[h, 1]) for h in two]
            for b in two:
                line = ends_of(along_y[0][b], along_y[1][b])
                for a in two:
                    part[a, b, 0] = part[a, b, 0] - line[a]
                    part[a, b, 1] = part[a, b, 1] + line[a]
            forces.append(self.assemble(part))
        return forces


def window_pair(slab, first_layer, own_layers, fetch):
    found = []
    for parity in range(2):
        layer = first_layer + parity
        device = layer // own_layers
        layer = layer - device * own_layers
        found.append((device, layer // 2, layer % 2))
    values = [fetch(device, q) for device, q, parity in found]
    if found[0][:2] == found[1][:2] or (values[0] is None and values[1] is None):
        return values[0]
    for parity in range(2):
        if values[parity] is None:
            values[parity] = jnp.zeros_like(values[1 - parity])
        elif found[parity][2] != parity:
            values[parity] = slab.lanes(values[parity], 2 * parity - 1)
    lane = lax.broadcasted_iota(jnp.int32, values[0].shape, 1)
    return jnp.where(lane % 2 == 0, values[0], values[1])


def first_sources(own_layers):
    return list(range(-BEFORE // own_layers, (own_layers + BEFORE - 1) // own_layers + 1))


def make_first_kernel(width, across, own_layers, fine_bound):
    own = BEFORE // 2
    own_pairs = (own_layers + 1) // 2
    spans = []
    for n in (4, 3, 2, 1):
        low, high = BEFORE - n, BEFORE + own_layers + n - 1
        spans.append((low // 2, (high + 1) // 2 - low // 2))

    sources = first_sources(own_layers)

    def first_kernel(*refs):
        arrived = refs[: len(sources)]
        refs = refs[len(sources) :]
        spread, collect, transfer, message, edge, f, u, d, stiff, shares, mixed, turned = refs
        slab = Slab(width, across)
        row = slab.row
        u[...] = jnp.zeros(u.shape, jnp.float32)
        f[...] = jnp.zeros(f.shape, jnp.float32)
        shares[...] = jnp.zeros(shares.shape, jnp.float32)
        stiff[...] = jnp.zeros(stiff.shape, jnp.float32)
        for n in range(len(sources)):
            for tile in range(SENT // 128):
                at = n * (SENT // 128) + tile
                for m in range(width // 4):
                    first = 12 * m + 4 * tile
                    mixed[at, 4 * m : 4 * m + 4, :] = arrived[n][first : first + 4, :]
                turned[n, 128 * tile : 128 * tile + 128, :] = mixed[at].T
        for field, target in enumerate((u, f)):
            for pair in range(PAIRS):

                def rows(start, field=field, pair=pair):
                    def fetch(device, q):
                        if device not in sources:
                            return None
                        at = BLOCK * (2 * q + field) + start
                        return turned[device - sources[0], at : at + 8, :]

                    value = window_pair(slab, 2 * pair - BEFORE, own_layers, fetch)
                    return jnp.zeros((8, width), jnp.float32) if value is None else value

                for i in range(3):
                    parts = [rows(24 * i + 8 * n) for n in range(3)]
                    if field == 0 and i == 0:
                        stiff[pair : pair + 1, :] = parts[0][TWIN : TWIN + 1]
                    parts[0] = jnp.where(row == TWIN, pltpu.roll(parts[0], TWIN, 0), parts[0])
                    parts.append(jnp.where(row < 4, 0.0, rows(68 + 4 * i)))
                    whole = jnp.concatenate(parts, 0)
                    target[i, pair] = whole * slab.keep if field == 0 else whole

        slab.smooth(u, f, 0, d, stiff, spread, collect, spans[0:3], fine_bound)

        weights = [jnp.broadcast_to(transfer[:, n : n + 1], (32, width)) for n in range(8)]

        def restrict(pair, forces):
            for i in range(3):
                rest = slab.keep * (f[i, pair] - forces[i])
                for n in range(8):
                    part = rest * weights[n]
                    part = (part[0:8] + part[8:16]) + (part[16:24] + part[24:32])
                    shares[i, n, pl.ds(pair, 1), :] = jnp.sum(part, axis=0, keepdims=True)

        slab.apply(u, stiff, spread, collect, *spans[3], restrict)

        restricted = [
            slab.assemble({corner: shares[i, n] for n, corner in enumerate(CORNERS)})
            for i in range(3)
        ]
        for q in range(own_pairs):
            hard = stiff[own + q : own + q + 1, :]
            for i in range(3):
                message[i, q] = u[i, own + q]
                message[i, q, RESTRICTED_SLOT : RESTRICTED_SLOT + 1, :] = restricted[i][
                    own + q : own + q + 1
                ]
                edge[q, i : i + 1, :] = u[i, own + q, 0:1, :]
                edge[q, 3 + i : 4 + i, :] = restricted[i][own + q : own + q + 1]
            message[0, q, STIFF_SLOT : STIFF_SLOT + 1, :] = hard
            edge[q, 6:8, :] = jnp.broadcast_to(hard, (2, width))

    return first_kernel


def sources_of(own_layers):
    whole = range(-3 // own_layers, (own_layers + 2) // own_layers + 1)
    coarse = range(-5 // own_layers, (own_layers + 4) // own_layers + 1)
    return list(whole), [n for n in coarse if n not in whole]


def make_second_kernel(width, across, own_layers, fine_bound, coarse_bound):
    own = BEFORE_B // 2
    own_pairs = (own_layers + 1) // 2
    shift = (BEFORE - BEFORE_B) // 2
    whole, outer = sources_of(own_layers)
    steps = chebyshev_steps()
    spans = []
    for n in (3, 2, 1):
        low, high = BEFORE_B - n, BEFORE_B + own_layers + n - 1
        spans.append((low // 2, (high + 1) // 2 - low // 2))

    def second_kernel(*refs):
        messages = dict(zip(whole, refs))
        refs = refs[len(whole) :]
        edges = dict(zip(outer, refs))
        f, spread, collect, transfer_back, out, u, d, stiff, coarse = refs[len(outer) :]
        slab = Slab(width, across)

        def pair_of(pair, fetch):
            return window_pair(slab, 2 * pair - BEFORE_B, own_layers, fetch)

        u[...] = jnp.zeros(u.shape, jnp.float32)
        coarse[...] = jnp.zeros(coarse.shape, jnp.float32)
        d[...] = jnp.zeros(d.shape, jnp.float32)
        for pair in range(PAIRS_B):
            for i in range(3):
                block = pair_of(pair, lambda n, q: messages[n][i, q] if n in messages else None)
                if block is not None:
                    u[i, pair] = block
            for n in range(7):

                def fetch(device, q, n=n):
                    if device in messages:
                        i, slot = ((n, 0), (n - 3, RESTRICTED_SLOT), (0, STIFF_SLOT))[n // 3]
                        return messages[device][i, q, slot : slot + 1, :]
                    return edges[device][q, n : n + 1, :] if device in edges else None

                line = pair_of(pair, fetch)
                if line is not None:
                    coarse[n, pair : pair + 1, :] = line
        stiff[...] = coarse[6]

        stiffness = coarse[6]
        keep_coarse = jnp.where(slab.bottom, 0.0, 1.0)
        start = [coarse[i] for i in range(3)]
        restricted = [coarse[3 + i] for i in range(3)]
        before = slab.coarse_force(start, stiffness)
        move = [(steps[0][1] / coarse_bound) * keep_coarse * restricted[i] for i in range(3)]
        level = [start[i] + move[i] for i in range(3)]
        for held, added in steps[1:]:
            force = slab.coarse_force(level, stiffness)
            for i in range(3):
                z = keep_coarse * (restricted[i] + before[i] - force[i])
                move[i] = held * move[i] + (added / coarse_bound) * z
                level[i] = level[i] + move[i]

        weights = [jnp.broadcast_to(transfer_back[:, n : n + 1], (32, width)) for n in range(8)]
        for i in range(3):
            change = slab.corners_of(level[i] - start[i])
            for pair in range(spans[0][0], min(spans[0][0] + spans[0][1] + 1, PAIRS_B)):
                lift = u[i, pair]
                for n, corner in enumerate(CORNERS):
                    lift = lift + weights[n] * change[corner][pair : pair + 1]
                u[i, pair] = lift

        slab.smooth(u, f, shift, d, stiff, spread, collect, spans, fine_bound)

        lower = lax.broadcasted_iota(jnp.int32, (width // 8, 8, 128), 1) < 4
        sides = []
        blank = jnp.zeros((29, width), jnp.float32)
        for q in range(2):
            ends_here = jnp.concatenate(
                [u[i, own + q] for i in range(3)]
                + [level[i][own + q : own + q + 1] for i in range(3)]
                + [blank],
                0,
            )
            sides.append(ends_here.T.reshape(width // 8, 8, 128))
        out[:, 0] = jnp.where(lower, sides[0], pltpu.roll(sides[1], 4, 1))
        out[:, 1] = jnp.where(lower, pltpu.roll(sides[0], 4, 1), sides[1])

    return second_kernel


def solution(mesh):
    rows_of, columns_of = mesh.shape["gx"], mesh.shape["gy"]
    devices = rows_of * columns_of
    order = ring_order(rows_of, columns_of)
    own_layers = EZ // devices
    own_pairs = (own_layers + 1) // 2
    width = 4 * devices
    across = 2 * rows_of
    near = first_sources(own_layers)
    whole, outer = sources_of(own_layers)
    spread, collect, fine_bound = element_tables()
    coarse_bound = build_tables([0.0, 1.0], 2)[2]
    transfer, transfer_back = transfer_table()
    wide = pltpu.CompilerParams(vmem_limit_bytes=60 * 1024 * 1024)
    limit = pltpu.CompilerParams(vmem_limit_bytes=48 * 1024 * 1024)
    f32 = jnp.float32

    pack = pl.pallas_call(
        functools.partial(pack_kernel, order),
        out_shape=jax.ShapeDtypeStruct((devices * 12, 128), f32),
        in_specs=[pl.BlockSpec(memory_space=pl.ANY)] * 5,
        out_specs=pl.BlockSpec(memory_space=pltpu.VMEM),
        scratch_shapes=[
            pltpu.VMEM((3, 6, 3, 384), f32),
            pltpu.VMEM((3, 6, 3, 384), f32),
            pltpu.VMEM((2, 1, EZ), f32),
            pltpu.VMEM((1, 1, 192), jnp.int32),
            pltpu.VMEM((384, 512), jnp.bfloat16),
            pltpu.VMEM((128, 384), f32),
            pltpu.VMEM((384, 128), f32),
            pltpu.VMEM((6, 136, 128), f32),
            pltpu.SemaphoreType.DMA((5,)),
        ],
        compiler_params=wide,
    )
    first = pl.pallas_call(
        make_first_kernel(width, across, own_layers, fine_bound),
        out_shape=(
            jax.ShapeDtypeStruct((3, own_pairs, 32, width), f32),
            jax.ShapeDtypeStruct((own_pairs, 8, width), f32),
            jax.ShapeDtypeStruct((3, PAIRS, 32, width), f32),
        ),
        scratch_shapes=[
            pltpu.VMEM((3, 8, 32, width), f32),
            pltpu.VMEM((3, 8, 32, width), f32),
            pltpu.VMEM((8, width), f32),
            pltpu.VMEM((3, 8, 8, width), f32),
            pltpu.VMEM((len(near) * (SENT // 128), width, 128), f32),
            pltpu.VMEM((len(near), SENT, width), f32),
        ],
        compiler_params=limit,
    )
    second = pl.pallas_call(
        make_second_kernel(width, across, own_layers, fine_bound, coarse_bound),
        out_shape=jax.ShapeDtypeStruct((devices // 2, 2, 8, 128), f32),
        scratch_shapes=[
            pltpu.VMEM((3, PAIRS_B + 2, 32, width), f32),
            pltpu.VMEM((3, PAIRS_B, 32, width), f32),
            pltpu.VMEM((PAIRS_B, width), f32),
            pltpu.VMEM((7, PAIRS_B, width), f32),
        ],
        compiler_params=limit,
    )
    unpack = pl.pallas_call(
        functools.partial(unpack_kernel, order),
        out_shape=(
            jax.ShapeDtypeStruct((3, 6, 3, 384), f32),
            jax.ShapeDtypeStruct((3, 2, 1, EZ), f32),
        ),
        scratch_shapes=[pltpu.VMEM((2, 128, 128), f32), pltpu.VMEM((384, 128), f32)],
        compiler_params=limit,
    )
    everyone = ("gy", "gx")

    def from_device(block, distance):
        place = {k: m % rows_of * columns_of + m // rows_of for m, k in enumerate(order)}
        route = [(place[(k + distance) % devices], place[k]) for k in range(devices)]
        return lax.ppermute(block, ("gx", "gy"), route)

    def body(initial, forcing, modulus, solid_list):
        sent = pack(initial, forcing, modulus, solid_list, jnp.asarray(pack_table()))
        sent = sent.reshape(devices, SENT // 128, 4, 128)
        arrived = lax.all_to_all(sent, everyone, 0, 0, tiled=True).reshape(devices * 12, 128)
        message, edge, load = first(
            *[from_device(arrived, n) if n else arrived for n in near],
            jnp.asarray(spread),
            jnp.asarray(collect),
            jnp.asarray(transfer),
        )
        messages = [from_device(message, n) if n else message for n in whole]
        edges = [from_device(edge, n) for n in outer]
        result = second(
            *messages,
            *edges,
            load,
            jnp.asarray(spread),
            jnp.asarray(collect),
            jnp.asarray(transfer_back),
        )
        back = lax.all_to_all(result.reshape(devices, 8, 128), everyone, 0, 0, tiled=True)
        return unpack(back, jnp.asarray(unpack_table()))

    placed = (
        P(None, "gx", "gy", None),
        P(None, "gx", "gy", None),
        P("gx", "gy", None),
        P("gx", "gy", None),
    )
    return jax.shard_map(
        body,
        mesh=mesh,
        in_specs=placed,
        out_specs=(P(None, "gx", "gy", None), P(None, "gx", "gy", None)),
        check_vma=False,
    )
```

```python
import functools
import math

import jax
import jax.numpy as jnp
import numpy as np
from jax import lax
from jax.experimental import pallas as pl
from jax.experimental.pallas import tpu as pltpu
from jax.sharding import PartitionSpec as P

CHEB = 3
EZ = 128

element_span = 20.0
lame_ratio = 4.0
rest_ratio = 1.25
modulus_top = 2.0
spectrum_floor = 0.05
interval_centre = (1.0 + spectrum_floor) / 2.0
interval_radius = (1.0 - spectrum_floor) / 2.0
interval_ratio = interval_centre / interval_radius
inner_anchors = (0.5 - 0.5 / math.sqrt(5.0), 0.5 + 0.5 / math.sqrt(5.0))

BEFORE = 4
PAIRS = 6
BEFORE_B = 6
PAIRS_B = 8
BLOCK = 84
SENT = 384

SLOTS = [
    (0, 0, 0), (1, 0, 0), (2, 0, 0), (0, 1, 0), (0, 2, 0), (0, 0, 1), (0, 0, 2), None,
    (0, 1, 1), (0, 1, 2), (0, 2, 1), (0, 2, 2), (1, 0, 1), (1, 0, 2), (2, 0, 1), (2, 0, 2),
    (1, 1, 0), (1, 2, 0), (2, 1, 0), (2, 2, 0), (1, 1, 1), (1, 1, 2), (1, 2, 1), (1, 2, 2),
    None, None, None, None, (2, 1, 1), (2, 1, 2), (2, 2, 1), (2, 2, 2),
]
TWIN = 7
RESTRICTED_SLOT = 24
STIFF_SLOT = 25
OWN_SHIFT, SHIFT_X, SHIFT_Y, SHIFT_Z = (0, 0, 0), (1, 0, 0), (0, 1, 0), (0, 0, 1)
ELEMENT_ROWS = (
    [(slot, OWN_SHIFT) for slot in range(24)]
    + [(slot, SHIFT_Z) for slot in range(16, 20)]
    + [(slot, OWN_SHIFT) for slot in range(28, 32)]
    + [(slot, SHIFT_X) for slot in range(7)] + [None]
    + [(slot, SHIFT_Y) for slot in range(7)] + [(0, (0, 1, 1))]
    + [(slot, SHIFT_Z) for slot in range(7)] + [(0, (1, 0, 1))]
    + [(slot, SHIFT_X) for slot in range(8, 12)] + [(slot, SHIFT_Y) for slot in range(12, 16)]
    + [(0, (1, 1, 1)), (1, (0, 1, 1)), (2, (0, 1, 1)), (3, (1, 0, 1)), (4, (1, 0, 1))]
    + [(5, (1, 1, 0)), (6, (1, 1, 0)), (0, (1, 1, 0))]
)
ROWS = len(ELEMENT_ROWS)
DEPTH = 80
CORNERS = [(a, b, c) for a in range(2) for b in range(2) for c in range(2)]


def gauss_rule(point_count):
    if point_count == 2:
        offset = 1.0 / math.sqrt(3.0)
        points = [-offset, offset]
        weights = [1.0, 1.0]
    else:
        inner = math.sqrt(3.0 / 7.0 - 2.0 / 7.0 * math.sqrt(6.0 / 5.0))
        outer = math.sqrt(3.0 / 7.0 + 2.0 / 7.0 * math.sqrt(6.0 / 5.0))
        heavy = (18.0 + math.sqrt(30.0)) / 36.0
        light = (18.0 - math.sqrt(30.0)) / 36.0
        points = [-outer, -inner, inner, outer]
        weights = [light, heavy, heavy, light]
    return (np.array(points), np.array(weights))


def lagrange_tables(anchors, samples):
    values = np.zeros((len(samples), len(anchors)))
    slopes = np.zeros((len(samples), len(anchors)))
    for sample_index, sample in enumerate(samples):
        for anchor_index, anchor in enumerate(anchors):
            others = [
                location
                for location_index, location in enumerate(anchors)
                if location_index != anchor_index
            ]
            product = 1.0
            for location in others:
                product = product * (sample - location) / (anchor - location)
            values[sample_index, anchor_index] = product
            derivative = 0.0
            for skipped in range(len(others)):
                summand = 1.0 / (anchor - others[skipped])
                for kept_index in range(len(others)):
                    if kept_index != skipped:
                        summand = (
                            summand * (sample - others[kept_index]) / (anchor - others[kept_index])
                        )
                derivative = derivative + summand
            slopes[sample_index, anchor_index] = derivative
    return (values, slopes)


def outer_three(first, second, third):
    return (
        first[:, None, None, :, None, None]
        * second[None, :, None, None, :, None]
        * third[None, None, :, None, None, :]
    )


def build_tables(anchors, point_count):
    raw_points, raw_weights = gauss_rule(point_count)
    samples = (raw_points + 1.0) / 2.0
    weights = raw_weights / 2.0
    basis_values, slopes = lagrange_tables(anchors, samples)
    quad_total = point_count**3
    nodal_count = len(anchors) ** 3
    derivative_one = outer_three(slopes, basis_values, basis_values).reshape(
        quad_total, nodal_count
    )
    derivative_two = outer_three(basis_values, slopes, basis_values).reshape(
        quad_total, nodal_count
    )
    derivative_three = outer_three(basis_values, basis_values, slopes).reshape(
        quad_total, nodal_count
    )
    stacked = np.stack([derivative_one, derivative_two, derivative_three]) / element_span
    volume = (weights[:, None, None] * weights[None, :, None] * weights[None, None, :]).reshape(
        -1
    ) * element_span**3
    forward = stacked.reshape(3 * quad_total, nodal_count)
    backward = (stacked * volume[None, :, None]).reshape(3 * quad_total, nodal_count).T
    weighted = stacked * volume[None, :, None]
    laplace = weighted[0].T @ stacked[0] + weighted[1].T @ stacked[1] + weighted[2].T @ stacked[2]
    matrix = np.zeros((nodal_count, 3, nodal_count, 3))
    for first in range(3):
        for second in range(3):
            block = weighted[second].T @ stacked[first] + (lame_ratio - 1.0) * (
                weighted[first].T @ stacked[second]
            )
            if first == second:
                block = block + laplace
            matrix[:, first, :, second] = block
    matrix = matrix.reshape(3 * nodal_count, 3 * nodal_count)
    vector = 1.5 + np.cos(1.3 * np.arange(3 * nodal_count))
    for repeat in range(200):
        vector = matrix @ vector
        vector = vector / np.sqrt(vector @ vector)
    largest = vector @ (matrix @ vector)
    return (forward, backward, float(4.0 * modulus_top * 1.1 * largest))


def row_nodes():
    nodes = []
    for entry in ELEMENT_ROWS:
        slot = SLOTS[entry[0]] if entry else None
        if slot is None or any(s and n for s, n in zip(entry[1], slot)):
            nodes.append(None)
        else:
            a, b, c = (3 * s + n for s, n in zip(entry[1], slot))
            nodes.append(16 * a + 4 * b + c)
    return nodes


def halves(matrix):
    whole = np.asarray(matrix, np.float32)
    high = whole.astype(jnp.bfloat16)
    low = (whole - high.astype(np.float32)).astype(jnp.bfloat16)
    return high, low


def element_tables():
    forward, backward, bound = build_tables([0.0, inner_anchors[0], inner_anchors[1], 1.0], 4)
    spread = np.zeros((forward.shape[0], DEPTH))
    collect = np.zeros((ROWS, backward.shape[1]))
    for row, node in enumerate(row_nodes()):
        if node is not None:
            spread[:, row] = forward[:, node]
            collect[row, :] = backward[node, :]
    spread_high, spread_low = halves(spread)
    collect_high, collect_low = halves(collect)
    return (
        np.concatenate([spread_high, spread_high, spread_low], 1),
        np.concatenate([collect_high, collect_low], 0),
        bound,
    )


def transfer_table():
    table = np.zeros((8, 32))
    reach = (0.0, inner_anchors[0], inner_anchors[1])
    for row, corner in enumerate(CORNERS):
        for column, slot in enumerate(SLOTS):
            if slot is not None:
                weight = 1.0
                for side, node in zip(corner, slot):
                    weight = weight * (reach[node] if side else 1.0 - reach[node])
                table[row, column] = weight
    back = table.T.copy()
    back[TWIN] = back[0]
    return table.T.astype(np.float32), back.astype(np.float32)


def chebyshev_steps():
    steps = [(0.0, 1.0 / interval_centre)]
    ratio_now = 1.0 / interval_ratio
    for sweep in range(1, CHEB):
        ratio_next = 1.0 / (2.0 * interval_ratio - ratio_now)
        steps.append((ratio_next * ratio_now, 2.0 * ratio_next / interval_radius))
        ratio_now = ratio_next
    return steps


def stack_row(field, component, layer, b):
    return field * 54 + component * 18 + layer * 3 + b


def block_column(component, slot):
    return 72 + 4 * component + slot - 28 if slot >= 24 else 24 * component + slot


def pack_table():
    table = np.zeros((3, 128, 2, 2, 128), np.float32)
    for field in range(2):
        for x in range(2):
            for component in range(3):
                for column, slot in enumerate(SLOTS):
                    if slot is not None:
                        a, b, c = slot
                        row = stack_row(field, component, 3 * x + a, b)
                        table[c, row, field, x, block_column(component, column)] = 1.0
            table[0, 108 + x, 0, x, TWIN] = 1.0
    return table.reshape(384, 512).astype(jnp.bfloat16)


def unpack_table():
    table = np.zeros((2, 128, 4, 128), np.float32)
    for x in range(2):
        for component in range(3):
            for column, slot in enumerate(SLOTS):
                if slot is not None:
                    a, b, c = slot
                    row = stack_row(0, component, 3 * x + a, b)
                    table[x, component * 32 + column, c, row] = 1.0
                    if column < 5:
                        table[x, 96 + 8 * component + column, 3, row] = 1.0
                    if column == 0:
                        table[x, 96 + 8 * component + TWIN, 3, row] = 1.0
                    if 16 <= column < 20:
                        table[x, component * 32 + column + 8, 3, row] = 1.0
            table[x, 120 + component, 0, 54 + 2 * component + x] = 1.0
    return table.reshape(256, 512).astype(jnp.bfloat16)


def pick(values, table):
    count = values.shape[0]
    parts = jnp.dot(
        jnp.concatenate(high_low(values), 0), table, preferred_element_type=jnp.float32
    )
    return parts[:count] + parts[count:]


def ring_order(rows_of, columns_of):
    if (rows_of, columns_of) != (4, 8):
        return list(range(rows_of * columns_of))
    order = []
    for z in range(4):
        for x in range(2):
            for y in range(2):
                chip = (z, 7 - z, 15 - z, 8 + z)[2 * x + y]
                order += [2 * chip, 2 * chip + 1]
    return order


def pack_kernel(
    order,
    initial_at, forcing_at, modulus_at, listing_at, table_at, out,
    initial, forcing, modulus, listing, table, rows, turned, places, ready,
):
    own_layers = EZ // len(order)
    sources = (listing_at, modulus_at, initial_at, forcing_at, table_at)
    copies = [
        pltpu.make_async_copy(source, here, ready.at[n])
        for n, (source, here) in enumerate(
            zip(sources, (listing, modulus, initial, forcing, table))
        )
    ]
    for copy in copies:
        copy.start()
    rows[108:128, :] = jnp.zeros((20, 384), jnp.float32)
    copies[0].wait()
    copies[1].wait()
    listed = listing[0].astype(jnp.float32)
    listed = jnp.concatenate([listed, jnp.full((1, 64), 256.0, jnp.float32)], 1)
    listed = jnp.broadcast_to(listed, (128, 256)).T
    lanes = lax.broadcasted_iota(jnp.int32, (256, 128), 1).astype(jnp.float32)
    row_at = lax.broadcasted_iota(jnp.int32, (128, 128), 0)
    stiff = jnp.zeros((128, 128), jnp.float32)
    for x in range(2):
        hit = jnp.max(jnp.where(listed == lanes + 128.0 * x, 1.0, 0.0), axis=0, keepdims=True)
        stiff = jnp.where(row_at == 108 + x, hit * modulus[x], stiff)
    copies[2].wait()
    copies[3].wait()
    for field, source in enumerate((initial, forcing)):
        for component in range(3):
            for layer in range(6):
                at = stack_row(field, component, layer, 0)
                rows[at : at + 3, :] = source[component, layer]
    for part in range(3):
        span = slice(128 * part, 128 * part + 128)
        turned[span, :] = rows[:, span].T
    picked = [turned[pl.ds(c, 128, stride=3), :] for c in range(3)]
    picked[0] = picked[0] + stiff.T
    copies[4].wait()
    wide = pick(jnp.concatenate(picked, 1), table[...])
    lane = lax.broadcasted_iota(jnp.int32, (128, 128), 1)
    for x in range(2):
        tiles = [None] * (SENT // 128)
        for n in range(4):
            pair, field = n // 2, n % 2
            moved = wide[:, 128 * (2 * field + x) : 128 * (2 * field + x) + 128]
            first = BLOCK * n
            if pair:
                moved = pltpu.roll(moved, 128 - 2 * pair, 0)
            if first % 128:
                moved = pltpu.roll(moved, first % 128, 1)
            for tile in range(first // 128, (first + BLOCK - 1) // 128 + 1):
                before = tiles[tile]
                if before is None:
                    tiles[tile] = moved
                else:
                    tiles[tile] = jnp.where(lane >= first - 128 * tile, moved, before)
        for tile in range(SENT // 128):
            places[3 * x + tile, 0:128, :] = tiles[tile]
            places[3 * x + tile, 128:136, :] = jnp.zeros((8, 128), jnp.float32)
    for device, k in enumerate(order):
        for tile in range(SENT // 128):
            for x in range(2):
                at = 12 * device + 4 * tile + 2 * x
                out[at : at + 2, :] = places[
                    3 * x + tile, own_layers * k : own_layers * k + 2, :
                ]


def unpack_kernel(order, arrived, table, out, coarse_out, layers, turned):
    devices = arrived.shape[0]
    own_layers = EZ // devices
    for x in range(2):
        for layer in range(own_layers):
            row = (layer // 2) * 4 + x * 2 + layer % 2
            if order == sorted(order):
                layers[x, pl.ds(layer, devices, stride=own_layers), :] = arrived[:, row, :]
                continue
            for device, k in enumerate(order):
                at = own_layers * k + layer
                layers[x, at : at + 1, :] = arrived[device, row : row + 1, :]
    wide = pick(jnp.concatenate([layers[0], layers[1]], 1), table[...])
    shares = pltpu.roll(wide[:, 384:512], own_layers, 0)
    turned[pl.ds(0, 128, stride=3), :] = wide[:, 0:128] + shares
    for c in range(1, 3):
        turned[pl.ds(c, 128, stride=3), :] = wide[:, 128 * c : 128 * c + 128]
    for part in range(3):
        span = slice(128 * part, 128 * part + 128)
        back = turned[span, :].T
        for component in range(3):
            for layer in range(6):
                at = stack_row(0, component, layer, 0)
                out[component, layer, :, span] = back[at : at + 3, :]
    back = wide[:, 0:128].T
    for component in range(3):
        for x in range(2):
            at = 54 + 2 * component + x
            coarse_out[component, x] = back[at : at + 1, :]


def cofactor_rows(deform):
    return [
        [
            deform[(row_at + 1) % 3][(column + 1) % 3] * deform[(row_at + 2) % 3][(column + 2) % 3]
            - deform[(row_at + 1) % 3][(column + 2) % 3]
            * deform[(row_at + 2) % 3][(column + 1) % 3]
            for column in range(3)
        ]
        for row_at in range(3)
    ]


def point_stress(deform, stiffness, stiffness_four):
    cofactors = cofactor_rows(deform)
    jacobian = (
        deform[0][0] * cofactors[0][0]
        + deform[0][1] * cofactors[0][1]
        + deform[0][2] * cofactors[0][2]
    )
    pressure = stiffness_four * (jacobian - rest_ratio)
    return [
        [stiffness * deform[i][d] + pressure * cofactors[i][d] for d in range(3)] for i in range(3)
    ]


coarse_samples = [0.5 - 0.5 / math.sqrt(3.0), 0.5 + 0.5 / math.sqrt(3.0)]
two = range(2)


def at_points(low, high):
    change = high - low
    return [low + s * change for s in coarse_samples], change * (1.0 / element_span)


def ends_of(first, second):
    high = coarse_samples[0] * first + coarse_samples[1] * second
    return [first + second - high, high]


def high_low(values):
    high = values.astype(jnp.bfloat16)
    return high, (values - high.astype(jnp.float32)).astype(jnp.bfloat16)


class Slab:
    def __init__(self, width, across):
        self.width = width
        self.y_step = 2 * across
        lane = lax.broadcasted_iota(jnp.int32, (8, width), 1)
        x = (lane // 2) % across
        self.bottom, self.top, self.even = x == 0, x == across - 1, lane % 2 == 0
        self.row = lax.broadcasted_iota(jnp.int32, (8, width), 0)
        row = lax.broadcasted_iota(jnp.int32, (32, width), 0)
        lane = lax.broadcasted_iota(jnp.int32, (32, width), 1)
        on_face = (row == 0) | ((row >= 3) & (row <= 11))
        self.keep = jnp.where(on_face & ((lane // 2) % across == 0), 0.0, 1.0)

    def lanes(self, v, step):
        return pltpu.roll(v, step % self.width, 1)

    def next_x(self, v):
        return jnp.where(self.top, 0.0, self.lanes(v, -2))

    def next_y(self, v):
        return self.lanes(v, -self.y_step)

    def next_z(self, v, ahead):
        return jnp.where(self.even, self.lanes(v, -1), self.lanes(ahead, 1))

    def onto_x(self, v):
        return jnp.where(self.bottom, 0.0, self.lanes(v, 2))

    def onto_y(self, v):
        return self.lanes(v, self.y_step)

    def gather(self, here, ahead):
        row = self.row
        g0, g1, g2, g3 = here[0:8], here[8:16], here[16:24], here[24:32]
        z0 = self.next_z(g0, ahead[0:8])
        z2 = self.next_z(g2, ahead[16:24])
        y0 = self.next_y(g0)
        yz, xz, xy = self.next_y(z0), self.next_x(z0), self.next_x(y0)
        edges = jnp.where(row <= 2, yz, jnp.where(row <= 4, xz, xy))
        return jnp.concatenate(
            [
                g0,
                g1,
                g2,
                jnp.where(row < 4, z2, g3),
                self.next_x(g0),
                jnp.where(row == 7, yz, y0),
                jnp.where(row == 7, xz, z0),
                jnp.where(row < 4, self.next_x(g1), self.next_y(g1)),
                jnp.where(row == 0, self.next_x(yz), edges),
                jnp.zeros_like(g0),
            ],
            0,
        )

    def scatter(self, part, behind):
        row = self.row
        g0, g1, g2, g3, x0, y0, z0, sides, edges = (part[8 * n : 8 * n + 8] for n in range(9))
        edges_x = self.onto_x(edges)
        yz = jnp.where(row == 0, edges_x, jnp.where(row == 7, y0, edges))
        yz = jnp.where((row <= 2) | (row == 7), yz, 0.0)
        z0 = jnp.where(row == 7, self.onto_x(z0), z0)
        z0 = z0 + jnp.where((row == 3) | (row == 4), edges_x, 0.0) + self.onto_y(yz)
        y0 = jnp.where(row == 7, edges_x, y0 + jnp.where(row >= 5, edges_x, 0.0))
        z2 = g3
        own0 = g0 + self.onto_x(x0) + self.onto_y(y0)
        own0 = own0 + jnp.where(self.even, behind[0], self.lanes(z0, 1))
        own1 = g1 + jnp.where(row < 4, self.onto_x(sides), self.onto_y(sides))
        share2 = jnp.where(self.even, behind[1], self.lanes(z2, 1))
        own2 = g2 + jnp.where(row < 4, share2, 0.0)
        own3 = jnp.where(row < 4, 0.0, g3)
        own0 = own0 + jnp.where(row == 0, pltpu.roll(own0, 1, 0), 0.0)
        own0 = jnp.where(row == 7, pltpu.roll(own0, 7, 0), own0)
        moved = (self.lanes(z0, -1), self.lanes(z2, -1))
        return jnp.concatenate([own0, own1, own2, own3], 0), moved

    def gradient(self, u, spread, pairs):
        blocks = [self.gather(u[i, pair], u[i, pair + 1]) for i in range(3) for pair in pairs]
        high, low = high_low(jnp.concatenate(blocks, 1))
        return jnp.dot(
            spread[...],
            jnp.concatenate([high, low, high], 0),
            preferred_element_type=jnp.float32,
        )

    def force(self, gradient, stiff, collect, pairs):
        width = len(pairs) * self.width
        stiffness = jnp.concatenate([stiff[pair : pair + 1, :] for pair in pairs], 1)
        deform = [
            [
                gradient[64 * e : 64 * e + 64, width * i : width * (i + 1)]
                + (1.0 if i == e else 0.0)
                for e in range(3)
            ]
            for i in range(3)
        ]
        stress = point_stress(deform, stiffness, lame_ratio * stiffness)
        stress = jnp.concatenate(
            [jnp.concatenate([stress[i][e] for i in range(3)], 1) for e in range(3)], 0
        )
        high, low = high_low(stress)
        force = jnp.dot(collect[...], high, preferred_element_type=jnp.float32)
        return force[0:ROWS] + (
            force[ROWS:] + jnp.dot(collect[0:ROWS], low, preferred_element_type=jnp.float32)
        )

    def apply(self, u, stiff, spread, collect, first, count, finish):
        width = self.width
        none = jnp.zeros((8, width), jnp.float32)
        carry = [(none, none) for i in range(3)]
        last = first + count
        steps = [list(range(at, min(at + 2, last))) for at in range(first, last, 2)]
        ahead = self.gradient(u, spread, steps[0])
        for n, pairs in enumerate(steps):
            gradient = ahead
            if n + 1 < len(steps):
                ahead = self.gradient(u, spread, steps[n + 1])
            force = self.force(gradient, stiff, collect, pairs)
            totals = [[] for pair in pairs]
            for q in range(len(pairs)):
                for i in range(3):
                    at = (len(pairs) * i + q) * width
                    total, carry[i] = self.scatter(force[:, at : at + width], carry[i])
                    totals[q].append(total)
            for pair, total in zip(pairs, totals):
                finish(pair, total)
        return carry

    def smooth(self, u, f, f_shift, d, stiff, spread, collect, spans, bound):
        for (first, count), (held, added) in zip(spans, chebyshev_steps()):

            def finish(pair, forces, held=held, added=added):
                for i in range(3):
                    z = (added / bound) * self.keep * (f[i, pair + f_shift] - forces[i])
                    move = held * d[i, pair] + z if held else z
                    d[i, pair] = move
                    u[i, pair] = u[i, pair] + move

            rest = self.apply(u, stiff, spread, collect, first, count, finish)
        owed = []
        for low, high in rest:
            low = jnp.where(self.even, low, 0.0) * self.keep[0:8]
            high = jnp.where(self.even, high, 0.0) * self.keep[16:24]
            owed.append((-(added / bound) * low, -(added / bound) * high))
        return owed

    def coarse_next_z(self, v):
        return self.next_z(v, pltpu.roll(v, 7, 0))

    def coarse_onto_z(self, v):
        return jnp.where(self.even, pltpu.roll(self.lanes(v, -1), 1, 0), self.lanes(v, 1))

    def corners_of(self, v):
        found = {(0, 0, 0): v, (0, 0, 1): self.coarse_next_z(v)}
        for c in range(2):
            found[0, 1, c] = self.next_y(found[0, 0, c])
        for b in range(2):
            for c in range(2):
                found[1, b, c] = self.next_x(found[0, b, c])
        return found

    def assemble(self, part):
        line = {
            (a, b): part[a, b, 0] + self.coarse_onto_z(part[a, b, 1])
            for a in range(2)
            for b in range(2)
        }
        face = [line[a, 0] + self.onto_y(line[a, 1]) for a in range(2)]
        return face[0] + self.onto_x(face[1])

    def coarse_force(self, values, stiffness):
        grads = []
        for i in range(3):
            v = self.corners_of(values[i])
            vz, sz = {}, {}
            for a in two:
                for b in two:
                    vz[a, b], sz[a, b] = at_points(v[a, b, 0], v[a, b, 1])
            vv, vs, sv = {}, {}, {}
            for a in two:
                for k in two:
                    vv[a, k], vs[a, k] = at_points(vz[a, 0][k], vz[a, 1][k])
                sv[a], unused = at_points(sz[a, 0], sz[a, 1])
            dx, dy, dz = {}, {}, {}
            for k in two:
                for j in two:
                    dx[j, k] = (vv[1, k][j] - vv[0, k][j]) * (1.0 / element_span)
                line, unused = at_points(vs[0, k], vs[1, k])
                for h in two:
                    dy[h, k] = line[h]
            for j in two:
                line, unused = at_points(sv[0][j], sv[1][j])
                for h in two:
                    dz[h, j] = line[h]
            grads.append((dx, dy, dz))
        weight = element_span**2 / 8.0
        scaled = weight * stiffness
        scaled_four = lame_ratio * scaled
        sums = [({}, {}, {}) for i in range(3)]

        def add(table, key, value):
            table[key] = table[key] + value if key in table else value

        for h in two:
            for j in two:
                for k in two:
                    deform = [
                        [grads[i][0][j, k], grads[i][1][h, k], grads[i][2][h, j]]
                        for i in range(3)
                    ]
                    for i in range(3):
                        deform[i][i] = deform[i][i] + 1.0
                    stress = point_stress(deform, scaled, scaled_four)
                    for i in range(3):
                        add(sums[i][0], (j, k), stress[i][0])
                        add(sums[i][1], (h, k), stress[i][1])
                        add(sums[i][2], (h, j), stress[i][2])

        forces = []
        for i in range(3):
            part = {}
            qx, qy, qz = sums[i]
            along_z = [ends_of(qx[j, 0], qx[j, 1]) for j in two]
            for c in two:
                line = ends_of(along_z[0][c], along_z[1][c])
                for b in two:
                    part[0, b, c] = -line[b]
                    part[1, b, c] = line[b]
            along_z = [ends_of(qy[h, 0], qy[h, 1]) for h in two]
            for c in two:
                line = ends_of(along_z[0][c], along_z[1][c])
                for a in two:
                    part[a, 0, c] = part[a, 0, c] - line[a]
                    part[a, 1, c] = part[a, 1, c] + line[a]
            along_y = [ends_of(qz[h, 0], qz[h, 1]) for h in two]
            for b in two:
                line = ends_of(along_y[0][b], along_y[1][b])
                for a in two:
                    part[a, b, 0] = part[a, b, 0] - line[a]
                    part[a, b, 1] = part[a, b, 1] + line[a]
            forces.append(self.assemble(part))
        return forces


def window_pair(slab, first_layer, own_layers, fetch):
    found = []
    for parity in range(2):
        layer = first_layer + parity
        device = layer // own_layers
        layer = layer - device * own_layers
        found.append((device, layer // 2, layer % 2))
    values = [fetch(device, q) for device, q, parity in found]
    if found[0][:2] == found[1][:2] or (values[0] is None and values[1] is None):
        return values[0]
    for parity in range(2):
        if values[parity] is None:
            values[parity] = jnp.zeros_like(values[1 - parity])
        elif found[parity][2] != parity:
            values[parity] = slab.lanes(values[parity], 2 * parity - 1)
    lane = lax.broadcasted_iota(jnp.int32, values[0].shape, 1)
    return jnp.where(lane % 2 == 0, values[0], values[1])


def first_sources(own_layers):
    return list(range(-BEFORE // own_layers, (own_layers + BEFORE - 1) // own_layers + 1))


def make_first_kernel(width, across, own_layers, fine_bound):
    own = BEFORE // 2
    own_pairs = (own_layers + 1) // 2
    spans = []
    for n in (4, 3, 2, 1):
        low, high = BEFORE - n, BEFORE + own_layers + n - 1
        spans.append((low // 2, (high + 1) // 2 - low // 2))

    sources = first_sources(own_layers)

    def first_kernel(*refs):
        arrived = refs[: len(sources)]
        refs = refs[len(sources) :]
        spread, collect, transfer, message, edge, f, u, d, stiff, shares, mixed, turned = refs
        slab = Slab(width, across)
        row = slab.row
        u[...] = jnp.zeros(u.shape, jnp.float32)
        f[...] = jnp.zeros(f.shape, jnp.float32)
        shares[...] = jnp.zeros(shares.shape, jnp.float32)
        stiff[...] = jnp.zeros(stiff.shape, jnp.float32)
        for n in range(len(sources)):
            for tile in range(SENT // 128):
                at = n * (SENT // 128) + tile
                for m in range(width // 4):
                    first = 12 * m + 4 * tile
                    mixed[at, 4 * m : 4 * m + 4, :] = arrived[n][first : first + 4, :]
                turned[n, 128 * tile : 128 * tile + 128, :] = mixed[at].T
        for field, target in enumerate((u, f)):
            for pair in range(PAIRS):

                def rows(start, field=field, pair=pair):
                    def fetch(device, q):
                        if device not in sources:
                            return None
                        at = BLOCK * (2 * q + field) + start
                        return turned[device - sources[0], at : at + 8, :]

                    value = window_pair(slab, 2 * pair - BEFORE, own_layers, fetch)
                    return jnp.zeros((8, width), jnp.float32) if value is None else value

                for i in range(3):
                    parts = [rows(24 * i + 8 * n) for n in range(3)]
                    if field == 0 and i == 0:
                        stiff[pair : pair + 1, :] = parts[0][TWIN : TWIN + 1]
                    parts[0] = jnp.where(row == TWIN, pltpu.roll(parts[0], TWIN, 0), parts[0])
                    parts.append(jnp.where(row < 4, 0.0, rows(68 + 4 * i)))
                    whole = jnp.concatenate(parts, 0)
                    target[i, pair] = whole * slab.keep if field == 0 else whole

        slab.smooth(u, f, 0, d, stiff, spread, collect, spans[0:3], fine_bound)

        weights = [jnp.broadcast_to(transfer[:, n : n + 1], (32, width)) for n in range(8)]

        def restrict(pair, forces):
            for i in range(3):
                rest = slab.keep * (f[i, pair] - forces[i])
                for n in range(8):
                    part = rest * weights[n]
                    part = (part[0:8] + part[8:16]) + (part[16:24] + part[24:32])
                    shares[i, n, pl.ds(pair, 1), :] = jnp.sum(part, axis=0, keepdims=True)

        slab.apply(u, stiff, spread, collect, *spans[3], restrict)

        restricted = [
            slab.assemble({corner: shares[i, n] for n, corner in enumerate(CORNERS)})
            for i in range(3)
        ]
        for q in range(own_pairs):
            hard = stiff[own + q : own + q + 1, :]
            for i in range(3):
                message[i, q] = u[i, own + q]
                message[i, q, RESTRICTED_SLOT : RESTRICTED_SLOT + 1, :] = restricted[i][
                    own + q : own + q + 1
                ]
                edge[q, i : i + 1, :] = u[i, own + q, 0:1, :]
                edge[q, 3 + i : 4 + i, :] = restricted[i][own + q : own + q + 1]
            message[0, q, STIFF_SLOT : STIFF_SLOT + 1, :] = hard
            edge[q, 6:8, :] = jnp.broadcast_to(hard, (2, width))

    return first_kernel


def shares_sent(own_layers):
    return own_layers % 2 == 0


def sources_of(own_layers):
    below = 2 if shares_sent(own_layers) else 3
    whole = range(-below // own_layers, (own_layers + 2) // own_layers + 1)
    coarse = range(-(below + 2) // own_layers, (own_layers + 4) // own_layers + 1)
    return list(whole), [n for n in coarse if n not in whole]


def make_second_kernel(width, across, own_layers, fine_bound, coarse_bound):
    own = BEFORE_B // 2
    own_pairs = (own_layers + 1) // 2
    shift = (BEFORE - BEFORE_B) // 2
    whole, outer = sources_of(own_layers)
    steps = chebyshev_steps()
    spans = []
    for n in (3, 2, 1):
        low, high = BEFORE_B - n + shares_sent(own_layers), BEFORE_B + own_layers + n - 1
        spans.append((low // 2, (high + 1) // 2 - low // 2))

    def second_kernel(*refs):
        messages = dict(zip(whole, refs))
        refs = refs[len(whole) :]
        edges = dict(zip(outer, refs))
        f, spread, collect, transfer_back, out, u, d, stiff, coarse = refs[len(outer) :]
        slab = Slab(width, across)

        def pair_of(pair, fetch):
            return window_pair(slab, 2 * pair - BEFORE_B, own_layers, fetch)

        u[...] = jnp.zeros(u.shape, jnp.float32)
        coarse[...] = jnp.zeros(coarse.shape, jnp.float32)
        d[...] = jnp.zeros(d.shape, jnp.float32)
        for pair in range(PAIRS_B):
            for i in range(3):
                block = pair_of(pair, lambda n, q: messages[n][i, q] if n in messages else None)
                if block is not None:
                    u[i, pair] = block
            for n in range(7):

                def fetch(device, q, n=n):
                    if device in messages:
                        i, slot = ((n, 0), (n - 3, RESTRICTED_SLOT), (0, STIFF_SLOT))[n // 3]
                        return messages[device][i, q, slot : slot + 1, :]
                    return edges[device][q, n : n + 1, :] if device in edges else None

                line = pair_of(pair, fetch)
                if line is not None:
                    coarse[n, pair : pair + 1, :] = line
        stiff[...] = coarse[6]

        stiffness = coarse[6]
        keep_coarse = jnp.where(slab.bottom, 0.0, 1.0)
        start = [coarse[i] for i in range(3)]
        restricted = [coarse[3 + i] for i in range(3)]
        before = slab.coarse_force(start, stiffness)
        move = [(steps[0][1] / coarse_bound) * keep_coarse * restricted[i] for i in range(3)]
        level = [start[i] + move[i] for i in range(3)]
        for held, added in steps[1:]:
            force = slab.coarse_force(level, stiffness)
            for i in range(3):
                z = keep_coarse * (restricted[i] + before[i] - force[i])
                move[i] = held * move[i] + (added / coarse_bound) * z
                level[i] = level[i] + move[i]

        weights = [jnp.broadcast_to(transfer_back[:, n : n + 1], (32, width)) for n in range(8)]
        for i in range(3):
            change = slab.corners_of(level[i] - start[i])
            for pair in range(spans[0][0], min(spans[0][0] + spans[0][1] + 1, PAIRS_B)):
                lift = u[i, pair]
                for n, corner in enumerate(CORNERS):
                    lift = lift + weights[n] * change[corner][pair : pair + 1]
                u[i, pair] = lift

        owed = slab.smooth(u, f, shift, d, stiff, spread, collect, spans, fine_bound)

        lower = lax.broadcasted_iota(jnp.int32, (width // 8, 8, 128), 1) < 4
        nothing = jnp.zeros((8, width), jnp.float32)
        sides = []
        for q in range(2):
            if q or not shares_sent(own_layers):
                owed = [(nothing, nothing)] * 3
            rows = []
            for i in range(3):
                value = u[i, own + q]
                rows += [value[0:24], jnp.where(slab.row < 4, owed[i][1], value[24:32])]
            rows += [owed[i][0] for i in range(3)]
            rows += [level[i][own + q : own + q + 1] for i in range(3)] + [nothing[0:5]]
            sides.append(jnp.concatenate(rows, 0).T.reshape(width // 8, 8, 128))
        out[:, 0] = jnp.where(lower, sides[0], pltpu.roll(sides[1], 4, 1))
        out[:, 1] = jnp.where(lower, pltpu.roll(sides[0], 4, 1), sides[1])

    return second_kernel


def solution(mesh):
    rows_of, columns_of = mesh.shape["gx"], mesh.shape["gy"]
    devices = rows_of * columns_of
    order = ring_order(rows_of, columns_of)
    own_layers = EZ // devices
    own_pairs = (own_layers + 1) // 2
    width = 4 * devices
    across = 2 * rows_of
    near = first_sources(own_layers)
    whole, outer = sources_of(own_layers)
    spread, collect, fine_bound = element_tables()
    coarse_bound = build_tables([0.0, 1.0], 2)[2]
    transfer, transfer_back = transfer_table()
    wide = pltpu.CompilerParams(vmem_limit_bytes=60 * 1024 * 1024)
    limit = pltpu.CompilerParams(vmem_limit_bytes=48 * 1024 * 1024)
    f32 = jnp.float32

    pack = pl.pallas_call(
        functools.partial(pack_kernel, order),
        out_shape=jax.ShapeDtypeStruct((devices * 12, 128), f32),
        in_specs=[pl.BlockSpec(memory_space=pl.ANY)] * 5,
        out_specs=pl.BlockSpec(memory_space=pltpu.VMEM),
        scratch_shapes=[
            pltpu.VMEM((3, 6, 3, 384), f32),
            pltpu.VMEM((3, 6, 3, 384), f32),
            pltpu.VMEM((2, 1, EZ), f32),
            pltpu.VMEM((1, 1, 192), jnp.int32),
            pltpu.VMEM((384, 512), jnp.bfloat16),
            pltpu.VMEM((128, 384), f32),
            pltpu.VMEM((384, 128), f32),
            pltpu.VMEM((6, 136, 128), f32),
            pltpu.SemaphoreType.DMA((5,)),
        ],
        compiler_params=wide,
    )
    first = pl.pallas_call(
        make_first_kernel(width, across, own_layers, fine_bound),
        out_shape=(
            jax.ShapeDtypeStruct((3, own_pairs, 32, width), f32),
            jax.ShapeDtypeStruct((own_pairs, 8, width), f32),
            jax.ShapeDtypeStruct((3, PAIRS, 32, width), f32),
        ),
        scratch_shapes=[
            pltpu.VMEM((3, 8, 32, width), f32),
            pltpu.VMEM((3, 8, 32, width), f32),
            pltpu.VMEM((8, width), f32),
            pltpu.VMEM((3, 8, 8, width), f32),
            pltpu.VMEM((len(near) * (SENT // 128), width, 128), f32),
            pltpu.VMEM((len(near), SENT, width), f32),
        ],
        compiler_params=limit,
    )
    second = pl.pallas_call(
        make_second_kernel(width, across, own_layers, fine_bound, coarse_bound),
        out_shape=jax.ShapeDtypeStruct((devices // 2, 2, 8, 128), f32),
        scratch_shapes=[
            pltpu.VMEM((3, PAIRS_B + 2, 32, width), f32),
            pltpu.VMEM((3, PAIRS_B, 32, width), f32),
            pltpu.VMEM((PAIRS_B, width), f32),
            pltpu.VMEM((7, PAIRS_B, width), f32),
        ],
        compiler_params=limit,
    )
    unpack = pl.pallas_call(
        functools.partial(unpack_kernel, order),
        out_shape=(
            jax.ShapeDtypeStruct((3, 6, 3, 384), f32),
            jax.ShapeDtypeStruct((3, 2, 1, EZ), f32),
        ),
        scratch_shapes=[pltpu.VMEM((2, 128, 128), f32), pltpu.VMEM((384, 128), f32)],
        compiler_params=limit,
    )
    everyone = ("gy", "gx")

    def from_device(block, distance):
        place = {k: m % rows_of * columns_of + m // rows_of for m, k in enumerate(order)}
        route = [(place[(k + distance) % devices], place[k]) for k in range(devices)]
        return lax.ppermute(block, ("gx", "gy"), route)

    def body(initial, forcing, modulus, solid_list):
        sent = pack(initial, forcing, modulus, solid_list, jnp.asarray(pack_table()))
        sent = sent.reshape(devices, SENT // 128, 4, 128)
        arrived = lax.all_to_all(sent, everyone, 0, 0, tiled=True).reshape(devices * 12, 128)
        message, edge, load = first(
            *[from_device(arrived, n) if n else arrived for n in near],
            jnp.asarray(spread),
            jnp.asarray(collect),
            jnp.asarray(transfer),
        )
        messages = [from_device(message, n) if n else message for n in whole]
        edges = [from_device(edge, n) for n in outer]
        result = second(
            *messages,
            *edges,
            load,
            jnp.asarray(spread),
            jnp.asarray(collect),
            jnp.asarray(transfer_back),
        )
        back = lax.all_to_all(result.reshape(devices, 8, 128), everyone, 0, 0, tiled=True)
        return unpack(back, jnp.asarray(unpack_table()))

    placed = (
        P(None, "gx", "gy", None),
        P(None, "gx", "gy", None),
        P("gx", "gy", None),
        P("gx", "gy", None),
    )
    return jax.shard_map(
        body,
        mesh=mesh,
        in_specs=placed,
        out_specs=(P(None, "gx", "gy", None), P(None, "gx", "gy", None)),
        check_vma=False,
    )
```

```python
import functools
import math

import jax
import jax.numpy as jnp
import numpy as np
from jax import lax
from jax.experimental import pallas as pl
from jax.experimental.pallas import tpu as pltpu
from jax.sharding import PartitionSpec as P

CHEB = 3
EZ = 128

element_span = 20.0
lame_ratio = 4.0
rest_ratio = 1.25
modulus_top = 2.0
spectrum_floor = 0.05
interval_centre = (1.0 + spectrum_floor) / 2.0
interval_radius = (1.0 - spectrum_floor) / 2.0
interval_ratio = interval_centre / interval_radius
inner_anchors = (0.5 - 0.5 / math.sqrt(5.0), 0.5 + 0.5 / math.sqrt(5.0))

BEFORE = 4
PAIRS = 6
BEFORE_B = 6
PAIRS_B = 8
BLOCK = 84
SENT = 384

SLOTS = [
    (0, 0, 0), (1, 0, 0), (2, 0, 0), (0, 1, 0), (0, 2, 0), (0, 0, 1), (0, 0, 2), None,
    (0, 1, 1), (0, 1, 2), (0, 2, 1), (0, 2, 2), (1, 0, 1), (1, 0, 2), (2, 0, 1), (2, 0, 2),
    (1, 1, 0), (1, 2, 0), (2, 1, 0), (2, 2, 0), (1, 1, 1), (1, 1, 2), (1, 2, 1), (1, 2, 2),
    None, None, None, None, (2, 1, 1), (2, 1, 2), (2, 2, 1), (2, 2, 2),
]
TWIN = 7
RESTRICTED_SLOT = 24
STIFF_SLOT = 25
OWN_SHIFT, SHIFT_X, SHIFT_Y, SHIFT_Z = (0, 0, 0), (1, 0, 0), (0, 1, 0), (0, 0, 1)
ELEMENT_ROWS = (
    [(slot, OWN_SHIFT) for slot in range(24)]
    + [(slot, SHIFT_Z) for slot in range(16, 20)]
    + [(slot, OWN_SHIFT) for slot in range(28, 32)]
    + [(slot, SHIFT_X) for slot in range(7)] + [None]
    + [(slot, SHIFT_Y) for slot in range(7)] + [(0, (0, 1, 1))]
    + [(slot, SHIFT_Z) for slot in range(7)] + [(0, (1, 0, 1))]
    + [(slot, SHIFT_X) for slot in range(8, 12)] + [(slot, SHIFT_Y) for slot in range(12, 16)]
    + [(0, (1, 1, 1)), (1, (0, 1, 1)), (2, (0, 1, 1)), (3, (1, 0, 1)), (4, (1, 0, 1))]
    + [(5, (1, 1, 0)), (6, (1, 1, 0)), (0, (1, 1, 0))]
)
ROWS = len(ELEMENT_ROWS)
DEPTH = 80
CORNERS = [(a, b, c) for a in range(2) for b in range(2) for c in range(2)]


def gauss_rule(point_count):
    if point_count == 2:
        offset = 1.0 / math.sqrt(3.0)
        points = [-offset, offset]
        weights = [1.0, 1.0]
    else:
        inner = math.sqrt(3.0 / 7.0 - 2.0 / 7.0 * math.sqrt(6.0 / 5.0))
        outer = math.sqrt(3.0 / 7.0 + 2.0 / 7.0 * math.sqrt(6.0 / 5.0))
        heavy = (18.0 + math.sqrt(30.0)) / 36.0
        light = (18.0 - math.sqrt(30.0)) / 36.0
        points = [-outer, -inner, inner, outer]
        weights = [light, heavy, heavy, light]
    return (np.array(points), np.array(weights))


def lagrange_tables(anchors, samples):
    values = np.zeros((len(samples), len(anchors)))
    slopes = np.zeros((len(samples), len(anchors)))
    for sample_index, sample in enumerate(samples):
        for anchor_index, anchor in enumerate(anchors):
            others = [
                location
                for location_index, location in enumerate(anchors)
                if location_index != anchor_index
            ]
            product = 1.0
            for location in others:
                product = product * (sample - location) / (anchor - location)
            values[sample_index, anchor_index] = product
            derivative = 0.0
            for skipped in range(len(others)):
                summand = 1.0 / (anchor - others[skipped])
                for kept_index in range(len(others)):
                    if kept_index != skipped:
                        summand = (
                            summand * (sample - others[kept_index]) / (anchor - others[kept_index])
                        )
                derivative = derivative + summand
            slopes[sample_index, anchor_index] = derivative
    return (values, slopes)


def outer_three(first, second, third):
    return (
        first[:, None, None, :, None, None]
        * second[None, :, None, None, :, None]
        * third[None, None, :, None, None, :]
    )


def build_tables(anchors, point_count):
    raw_points, raw_weights = gauss_rule(point_count)
    samples = (raw_points + 1.0) / 2.0
    weights = raw_weights / 2.0
    basis_values, slopes = lagrange_tables(anchors, samples)
    quad_total = point_count**3
    nodal_count = len(anchors) ** 3
    derivative_one = outer_three(slopes, basis_values, basis_values).reshape(
        quad_total, nodal_count
    )
    derivative_two = outer_three(basis_values, slopes, basis_values).reshape(
        quad_total, nodal_count
    )
    derivative_three = outer_three(basis_values, basis_values, slopes).reshape(
        quad_total, nodal_count
    )
    stacked = np.stack([derivative_one, derivative_two, derivative_three]) / element_span
    volume = (weights[:, None, None] * weights[None, :, None] * weights[None, None, :]).reshape(
        -1
    ) * element_span**3
    forward = stacked.reshape(3 * quad_total, nodal_count)
    backward = (stacked * volume[None, :, None]).reshape(3 * quad_total, nodal_count).T
    weighted = stacked * volume[None, :, None]
    laplace = weighted[0].T @ stacked[0] + weighted[1].T @ stacked[1] + weighted[2].T @ stacked[2]
    matrix = np.zeros((nodal_count, 3, nodal_count, 3))
    for first in range(3):
        for second in range(3):
            block = weighted[second].T @ stacked[first] + (lame_ratio - 1.0) * (
                weighted[first].T @ stacked[second]
            )
            if first == second:
                block = block + laplace
            matrix[:, first, :, second] = block
    matrix = matrix.reshape(3 * nodal_count, 3 * nodal_count)
    vector = 1.5 + np.cos(1.3 * np.arange(3 * nodal_count))
    for repeat in range(200):
        vector = matrix @ vector
        vector = vector / np.sqrt(vector @ vector)
    largest = vector @ (matrix @ vector)
    return (forward, backward, float(4.0 * modulus_top * 1.1 * largest))


def row_nodes():
    nodes = []
    for entry in ELEMENT_ROWS:
        slot = SLOTS[entry[0]] if entry else None
        if slot is None or any(s and n for s, n in zip(entry[1], slot)):
            nodes.append(None)
        else:
            a, b, c = (3 * s + n for s, n in zip(entry[1], slot))
            nodes.append(16 * a + 4 * b + c)
    return nodes


def halves(matrix):
    whole = np.asarray(matrix, np.float32)
    high = whole.astype(jnp.bfloat16)
    low = (whole - high.astype(np.float32)).astype(jnp.bfloat16)
    return high, low


def element_tables():
    forward, backward, bound = build_tables([0.0, inner_anchors[0], inner_anchors[1], 1.0], 4)
    spread = np.zeros((forward.shape[0], DEPTH))
    collect = np.zeros((ROWS, backward.shape[1]))
    for row, node in enumerate(row_nodes()):
        if node is not None:
            spread[:, row] = forward[:, node]
            collect[row, :] = backward[node, :]
    spread_high, spread_low = halves(spread)
    collect_high, collect_low = halves(collect)
    return (
        np.concatenate([spread_high, spread_high, spread_low], 1),
        np.concatenate([collect_high, collect_low], 0),
        bound,
    )


def transfer_table():
    table = np.zeros((8, 32))
    reach = (0.0, inner_anchors[0], inner_anchors[1])
    for row, corner in enumerate(CORNERS):
        for column, slot in enumerate(SLOTS):
            if slot is not None:
                weight = 1.0
                for side, node in zip(corner, slot):
                    weight = weight * (reach[node] if side else 1.0 - reach[node])
                table[row, column] = weight
    back = table.T.copy()
    back[TWIN] = back[0]
    return table.T.astype(np.float32), back.astype(np.float32)


def chebyshev_steps():
    steps = [(0.0, 1.0 / interval_centre)]
    ratio_now = 1.0 / interval_ratio
    for sweep in range(1, CHEB):
        ratio_next = 1.0 / (2.0 * interval_ratio - ratio_now)
        steps.append((ratio_next * ratio_now, 2.0 * ratio_next / interval_radius))
        ratio_now = ratio_next
    return steps


def stack_row(field, component, layer, b):
    return field * 54 + component * 18 + layer * 3 + b


def block_column(component, slot):
    return 72 + 4 * component + slot - 28 if slot >= 24 else 24 * component + slot


def pack_table():
    table = np.zeros((3, 128, 2, 2, 128), np.float32)
    for field in range(2):
        for x in range(2):
            for component in range(3):
                for column, slot in enumerate(SLOTS):
                    if slot is not None:
                        a, b, c = slot
                        row = stack_row(field, component, 3 * x + a, b)
                        table[c, row, field, x, block_column(component, column)] = 1.0
            table[0, 108 + x, 0, x, TWIN] = 1.0
    return table.reshape(384, 512).astype(jnp.bfloat16)


def unpack_table():
    table = np.zeros((2, 128, 4, 128), np.float32)
    for x in range(2):
        for component in range(3):
            for column, slot in enumerate(SLOTS):
                if slot is not None:
                    a, b, c = slot
                    row = stack_row(0, component, 3 * x + a, b)
                    table[x, component * 32 + column, c, row] = 1.0
                    if column < 5:
                        table[x, 96 + 8 * component + column, 3, row] = 1.0
                    if column == 0:
                        table[x, 96 + 8 * component + TWIN, 3, row] = 1.0
                    if 16 <= column < 20:
                        table[x, component * 32 + column + 8, 3, row] = 1.0
            table[x, 120 + component, 0, 54 + 2 * component + x] = 1.0
    return table.reshape(256, 512).astype(jnp.bfloat16)


def pick(values, table):
    count = values.shape[0]
    parts = jnp.dot(
        jnp.concatenate(high_low(values), 0), table, preferred_element_type=jnp.float32
    )
    return parts[:count] + parts[count:]


def ring_order(rows_of, columns_of):
    if (rows_of, columns_of) != (4, 8):
        return list(range(rows_of * columns_of))
    order = []
    for z in range(4):
        for x in range(2):
            for y in range(2):
                chip = (z, 7 - z, 15 - z, 8 + z)[2 * x + y]
                order += [2 * chip, 2 * chip + 1]
    return order


def pack_kernel(
    order,
    initial_at, forcing_at, modulus_at, listing_at, table_at, out,
    initial, forcing, modulus, listing, table, rows, turned, places, ready,
):
    own_layers = EZ // len(order)
    sources = (listing_at, modulus_at, initial_at, forcing_at, table_at)
    copies = [
        pltpu.make_async_copy(source, here, ready.at[n])
        for n, (source, here) in enumerate(
            zip(sources, (listing, modulus, initial, forcing, table))
        )
    ]
    for copy in copies:
        copy.start()
    rows[108:128, :] = jnp.zeros((20, 384), jnp.float32)
    copies[0].wait()
    copies[1].wait()
    listed = listing[0].astype(jnp.float32)
    listed = jnp.concatenate([listed, jnp.full((1, 64), 256.0, jnp.float32)], 1)
    listed = jnp.broadcast_to(listed, (128, 256)).T
    lanes = lax.broadcasted_iota(jnp.int32, (256, 128), 1).astype(jnp.float32)
    row_at = lax.broadcasted_iota(jnp.int32, (128, 128), 0)
    stiff = jnp.zeros((128, 128), jnp.float32)
    for x in range(2):
        hit = jnp.max(jnp.where(listed == lanes + 128.0 * x, 1.0, 0.0), axis=0, keepdims=True)
        stiff = jnp.where(row_at == 108 + x, hit * modulus[x], stiff)
    copies[2].wait()
    copies[3].wait()
    for field, source in enumerate((initial, forcing)):
        for component in range(3):
            for layer in range(6):
                at = stack_row(field, component, layer, 0)
                rows[at : at + 3, :] = source[component, layer]
    for part in range(3):
        span = slice(128 * part, 128 * part + 128)
        turned[span, :] = rows[:, span].T
    picked = [turned[pl.ds(c, 128, stride=3), :] for c in range(3)]
    picked[0] = picked[0] + stiff.T
    copies[4].wait()
    wide = pick(jnp.concatenate(picked, 1), table[...])
    lane = lax.broadcasted_iota(jnp.int32, (128, 128), 1)
    for x in range(2):
        tiles = [None] * (SENT // 128)
        for n in range(4):
            pair, field = n // 2, n % 2
            moved = wide[:, 128 * (2 * field + x) : 128 * (2 * field + x) + 128]
            first = BLOCK * n
            if pair:
                moved = pltpu.roll(moved, 128 - 2 * pair, 0)
            if first % 128:
                moved = pltpu.roll(moved, first % 128, 1)
            for tile in range(first // 128, (first + BLOCK - 1) // 128 + 1):
                before = tiles[tile]
                if before is None:
                    tiles[tile] = moved
                else:
                    tiles[tile] = jnp.where(lane >= first - 128 * tile, moved, before)
        for tile in range(SENT // 128):
            places[3 * x + tile, 0:128, :] = tiles[tile]
            places[3 * x + tile, 128:136, :] = jnp.zeros((8, 128), jnp.float32)
    for device, k in enumerate(order):
        for tile in range(SENT // 128):
            for x in range(2):
                at = 12 * device + 4 * tile + 2 * x
                out[at : at + 2, :] = places[
                    3 * x + tile, own_layers * k : own_layers * k + 2, :
                ]


def unpack_kernel(order, arrived, table, out, coarse_out, layers, turned):
    devices = arrived.shape[0]
    own_layers = EZ // devices
    for x in range(2):
        for layer in range(own_layers):
            row = (layer // 2) * 4 + x * 2 + layer % 2
            if order == sorted(order):
                layers[x, pl.ds(layer, devices, stride=own_layers), :] = arrived[:, row, :]
                continue
            for device, k in enumerate(order):
                at = own_layers * k + layer
                layers[x, at : at + 1, :] = arrived[device, row : row + 1, :]
    wide = pick(jnp.concatenate([layers[0], layers[1]], 1), table[...])
    shares = pltpu.roll(wide[:, 384:512], own_layers, 0)
    turned[pl.ds(0, 128, stride=3), :] = wide[:, 0:128] + shares
    for c in range(1, 3):
        turned[pl.ds(c, 128, stride=3), :] = wide[:, 128 * c : 128 * c + 128]
    for part in range(3):
        span = slice(128 * part, 128 * part + 128)
        back = turned[span, :].T
        for component in range(3):
            for layer in range(6):
                at = stack_row(0, component, layer, 0)
                out[component, layer, :, span] = back[at : at + 3, :]
    back = wide[:, 0:128].T
    for component in range(3):
        for x in range(2):
            at = 54 + 2 * component + x
            coarse_out[component, x] = back[at : at + 1, :]


def cofactor_rows(deform):
    return [
        [
            deform[(row_at + 1) % 3][(column + 1) % 3] * deform[(row_at + 2) % 3][(column + 2) % 3]
            - deform[(row_at + 1) % 3][(column + 2) % 3]
            * deform[(row_at + 2) % 3][(column + 1) % 3]
            for column in range(3)
        ]
        for row_at in range(3)
    ]


def point_stress(deform, stiffness, stiffness_four):
    cofactors = cofactor_rows(deform)
    jacobian = (
        deform[0][0] * cofactors[0][0]
        + deform[0][1] * cofactors[0][1]
        + deform[0][2] * cofactors[0][2]
    )
    pressure = stiffness_four * (jacobian - rest_ratio)
    return [
        [stiffness * deform[i][d] + pressure * cofactors[i][d] for d in range(3)] for i in range(3)
    ]


coarse_samples = [0.5 - 0.5 / math.sqrt(3.0), 0.5 + 0.5 / math.sqrt(3.0)]
two = range(2)


def at_points(low, high):
    change = high - low
    return [low + s * change for s in coarse_samples], change * (1.0 / element_span)


def ends_of(first, second):
    high = coarse_samples[0] * first + coarse_samples[1] * second
    return [first + second - high, high]


def high_low(values):
    high = values.astype(jnp.bfloat16)
    return high, (values - high.astype(jnp.float32)).astype(jnp.bfloat16)


def reads(pairs):
    return set(range(pairs[0], pairs[-1] + 2))


def plan_steps(spans):
    plan = []
    for first, count in spans:
        pairs = list(range(first, first + count))
        plan.append([pairs[n : n + 2] for n in range(0, count, 2)])
    for now, later in zip(plan, plan[1:]):
        if reads(later[0]) & set(now[-1]) and len(now[-1]) == 2:
            now[-1:] = [now[-1][:1], now[-1][1:]]
        if reads(later[0]) & set(now[-1]) and len(later[0]) == 2:
            later[:1] = [later[0][:1], later[0][1:]]
    return plan


class Slab:
    def __init__(self, width, across):
        self.width = width
        self.y_step = 2 * across
        lane = lax.broadcasted_iota(jnp.int32, (8, width), 1)
        x = (lane // 2) % across
        self.bottom, self.top, self.even = x == 0, x == across - 1, lane % 2 == 0
        self.row = lax.broadcasted_iota(jnp.int32, (8, width), 0)
        row = lax.broadcasted_iota(jnp.int32, (32, width), 0)
        lane = lax.broadcasted_iota(jnp.int32, (32, width), 1)
        on_face = (row == 0) | ((row >= 3) & (row <= 11))
        self.keep = jnp.where(on_face & ((lane // 2) % across == 0), 0.0, 1.0)

    def lanes(self, v, step):
        return pltpu.roll(v, step % self.width, 1)

    def from_next(self, v, x, y):
        if x or y:
            v = self.lanes(v, -2 * x - self.y_step * y)
        return jnp.where(self.top, 0.0, v) if x else v

    def from_next_z(self, v, ahead, x, y):
        step = -2 * x - self.y_step * y
        v = jnp.where(self.even, self.lanes(v, step - 1), self.lanes(ahead, step + 1))
        return jnp.where(self.top, 0.0, v) if x else v

    def onto_next(self, v, x, y, z=0):
        if x or y or z:
            v = self.lanes(v, 2 * x + self.y_step * y + z)
        return jnp.where(self.bottom, 0.0, v) if x else v

    def gather(self, here, ahead):
        row = self.row
        g0, g1, g2, g3 = here[0:8], here[8:16], here[16:24], here[24:32]
        a0 = ahead[0:8]
        z0, xz = self.from_next_z(g0, a0, 0, 0), self.from_next_z(g0, a0, 1, 0)
        yz, xyz = self.from_next_z(g0, a0, 0, 1), self.from_next_z(g0, a0, 1, 1)
        z2 = self.from_next_z(g2, ahead[16:24], 0, 0)
        edges = jnp.where(row <= 4, xz, self.from_next(g0, 1, 1))
        edges = jnp.where(row == 0, xyz, jnp.where(row <= 2, yz, edges))
        return jnp.concatenate(
            [
                g0,
                g1,
                g2,
                jnp.where(row < 4, z2, g3),
                self.from_next(g0, 1, 0),
                jnp.where(row == 7, yz, self.from_next(g0, 0, 1)),
                jnp.where(row == 7, xz, z0),
                jnp.where(row < 4, self.from_next(g1, 1, 0), self.from_next(g1, 0, 1)),
                edges,
                jnp.zeros_like(g0),
            ],
            0,
        )

    def scatter(self, part, behind):
        row = self.row
        g0, g1, g2, g3, x0, y0, z0, sides, edges = (part[8 * n : 8 * n + 8] for n in range(9))
        last = row == 7
        for_z = jnp.where(last, 0.0, z0)
        for_xz = jnp.where(last, z0, jnp.where((row == 3) | (row == 4), edges, 0.0))
        for_yz = jnp.where(last, y0, jnp.where((row == 1) | (row == 2), edges, 0.0))
        for_xyz = jnp.where(row == 0, edges, 0.0)
        for_xy = jnp.where(row >= 5, edges, 0.0)

        def above(z):
            return (
                self.onto_next(for_z, 0, 0, z)
                + self.onto_next(for_yz, 0, 1, z)
                + self.onto_next(for_xz, 1, 0, z)
                + self.onto_next(for_xyz, 1, 1, z)
            )

        own0 = g0 + self.onto_next(x0, 1, 0) + self.onto_next(jnp.where(last, 0.0, y0), 0, 1)
        own0 = own0 + self.onto_next(for_xy, 1, 1)
        own0 = own0 + jnp.where(self.even, behind[0], above(1))
        own1 = g1 + jnp.where(row < 4, self.onto_next(sides, 1, 0), self.onto_next(sides, 0, 1))
        share2 = jnp.where(self.even, behind[1], self.onto_next(g3, 0, 0, 1))
        own2 = g2 + jnp.where(row < 4, share2, 0.0)
        own3 = jnp.where(row < 4, 0.0, g3)
        twins = jnp.where(last, pltpu.roll(own0, 7, 0), 0.0)
        own0 = own0 + jnp.where(row == 0, pltpu.roll(own0, 1, 0), twins)
        moved = (above(-1), self.onto_next(g3, 0, 0, -1))
        return jnp.concatenate([own0, own1, own2, own3], 0), moved

    def gradient(self, u, spread, pairs):
        blocks = [self.gather(u[i, pair], u[i, pair + 1]) for i in range(3) for pair in pairs]
        high, low = high_low(jnp.concatenate(blocks, 1))
        return jnp.dot(
            spread[...],
            jnp.concatenate([high, low, high], 0),
            preferred_element_type=jnp.float32,
        )

    def force(self, gradient, stiff, collect, pairs):
        width = len(pairs) * self.width
        stiffness = jnp.concatenate([stiff[pair : pair + 1, :] for pair in pairs], 1)
        deform = [
            [
                gradient[64 * e : 64 * e + 64, width * i : width * (i + 1)]
                + (1.0 if i == e else 0.0)
                for e in range(3)
            ]
            for i in range(3)
        ]
        stress = point_stress(deform, stiffness, lame_ratio * stiffness)
        stress = jnp.concatenate(
            [jnp.concatenate([stress[i][e] for i in range(3)], 1) for e in range(3)], 0
        )
        high, low = high_low(stress)
        force = jnp.dot(collect[...], high, preferred_element_type=jnp.float32)
        return force[0:ROWS] + (
            force[ROWS:] + jnp.dot(collect[0:ROWS], low, preferred_element_type=jnp.float32)
        )

    def run(self, u, stiff, spread, collect, jobs):
        plan = plan_steps([job[:2] for job in jobs])
        steps = [(pairs, n) for n, chunks in enumerate(plan) for pairs in chunks]
        none = jnp.zeros((8, self.width), jnp.float32)
        ahead, carry, job = None, None, None
        for at, (pairs, n) in enumerate(steps):
            gradient = self.gradient(u, spread, pairs) if ahead is None else ahead
            ahead = None
            if at + 1 < len(steps):
                later, later_job = steps[at + 1]
                if later_job == n or not reads(later) & set(pairs):
                    ahead = self.gradient(u, spread, later)
            if job != n:
                carry, job = [(none, none) for i in range(3)], n
            force = self.force(gradient, stiff, collect, pairs)
            totals = [[] for pair in pairs]
            for q in range(len(pairs)):
                for i in range(3):
                    lane = (len(pairs) * i + q) * self.width
                    total, carry[i] = self.scatter(force[:, lane : lane + self.width], carry[i])
                    totals[q].append(total)
            for pair, total in zip(pairs, totals):
                jobs[n][2](pair, total)
        return carry

    def smoothing(self, u, f, f_shift, d, spans, bound):
        jobs = []
        for (first, count), (held, added) in zip(spans, chebyshev_steps()):

            def finish(pair, forces, held=held, added=added):
                for i in range(3):
                    z = (added / bound) * self.keep * (f[i, pair + f_shift] - forces[i])
                    move = held * d[i, pair] + z if held else z
                    d[i, pair] = move
                    u[i, pair] = u[i, pair] + move

            jobs.append((first, count, finish))
        return jobs

    def owed(self, carry, bound):
        scale = -chebyshev_steps()[-1][1] / bound
        return [
            (
                scale * jnp.where(self.even, low, 0.0) * self.keep[0:8],
                scale * jnp.where(self.even, high, 0.0) * self.keep[16:24],
            )
            for low, high in carry
        ]

    def corners_of(self, v):
        ahead = pltpu.roll(v, 7, 0)
        found = {}
        for a in range(2):
            for b in range(2):
                found[a, b, 0] = self.from_next(v, a, b)
                found[a, b, 1] = self.from_next_z(v, ahead, a, b)
        return found

    def assemble(self, part):
        here, odd, even = 0.0, 0.0, 0.0
        for a in range(2):
            for b in range(2):
                here = here + self.onto_next(part[a, b, 0], a, b)
                odd = odd + self.onto_next(part[a, b, 1], a, b, 1)
                even = even + self.onto_next(part[a, b, 1], a, b, -1)
        return here + jnp.where(self.even, pltpu.roll(even, 1, 0), odd)

    def coarse_force(self, values, stiffness):
        grads = []
        for i in range(3):
            v = self.corners_of(values[i])
            vz, sz = {}, {}
            for a in two:
                for b in two:
                    vz[a, b], sz[a, b] = at_points(v[a, b, 0], v[a, b, 1])
            vv, vs, sv = {}, {}, {}
            for a in two:
                for k in two:
                    vv[a, k], vs[a, k] = at_points(vz[a, 0][k], vz[a, 1][k])
                sv[a], unused = at_points(sz[a, 0], sz[a, 1])
            dx, dy, dz = {}, {}, {}
            for k in two:
                for j in two:
                    dx[j, k] = (vv[1, k][j] - vv[0, k][j]) * (1.0 / element_span)
                line, unused = at_points(vs[0, k], vs[1, k])
                for h in two:
                    dy[h, k] = line[h]
            for j in two:
                line, unused = at_points(sv[0][j], sv[1][j])
                for h in two:
                    dz[h, j] = line[h]
            grads.append((dx, dy, dz))
        weight = element_span**2 / 8.0
        scaled = weight * stiffness
        scaled_four = lame_ratio * scaled
        sums = [({}, {}, {}) for i in range(3)]

        def add(table, key, value):
            table[key] = table[key] + value if key in table else value

        for h in two:
            for j in two:
                for k in two:
                    deform = [
                        [grads[i][0][j, k], grads[i][1][h, k], grads[i][2][h, j]]
                        for i in range(3)
                    ]
                    for i in range(3):
                        deform[i][i] = deform[i][i] + 1.0
                    stress = point_stress(deform, scaled, scaled_four)
                    for i in range(3):
                        add(sums[i][0], (j, k), stress[i][0])
                        add(sums[i][1], (h, k), stress[i][1])
                        add(sums[i][2], (h, j), stress[i][2])

        forces = []
        for i in range(3):
            part = {}
            qx, qy, qz = sums[i]
            along_z = [ends_of(qx[j, 0], qx[j, 1]) for j in two]
            for c in two:
                line = ends_of(along_z[0][c], along_z[1][c])
                for b in two:
                    part[0, b, c] = -line[b]
                    part[1, b, c] = line[b]
            along_z = [ends_of(qy[h, 0], qy[h, 1]) for h in two]
            for c in two:
                line = ends_of(along_z[0][c], along_z[1][c])
                for a in two:
                    part[a, 0, c] = part[a, 0, c] - line[a]
                    part[a, 1, c] = part[a, 1, c] + line[a]
            along_y = [ends_of(qz[h, 0], qz[h, 1]) for h in two]
            for b in two:
                line = ends_of(along_y[0][b], along_y[1][b])
                for a in two:
                    part[a, b, 0] = part[a, b, 0] - line[a]
                    part[a, b, 1] = part[a, b, 1] + line[a]
            forces.append(self.assemble(part))
        return forces


def window_pair(slab, first_layer, own_layers, fetch):
    found = []
    for parity in range(2):
        layer = first_layer + parity
        device = layer // own_layers
        layer = layer - device * own_layers
        found.append((device, layer // 2, layer % 2))
    values = [fetch(device, q) for device, q, parity in found]
    if found[0][:2] == found[1][:2] or (values[0] is None and values[1] is None):
        return values[0]
    for parity in range(2):
        if values[parity] is None:
            values[parity] = jnp.zeros_like(values[1 - parity])
        elif found[parity][2] != parity:
            values[parity] = slab.lanes(values[parity], 2 * parity - 1)
    lane = lax.broadcasted_iota(jnp.int32, values[0].shape, 1)
    return jnp.where(lane % 2 == 0, values[0], values[1])


def first_sources(own_layers):
    return list(range(-BEFORE // own_layers, (own_layers + BEFORE - 1) // own_layers + 1))


def make_first_kernel(width, across, own_layers, fine_bound):
    own = BEFORE // 2
    own_pairs = (own_layers + 1) // 2
    spans = []
    for n in (4, 3, 2, 1):
        low, high = BEFORE - n, BEFORE + own_layers + n - 1
        spans.append((low // 2, (high + 1) // 2 - low // 2))

    sources = first_sources(own_layers)

    def first_kernel(*refs):
        arrived = refs[: len(sources)]
        refs = refs[len(sources) :]
        spread, collect, transfer, message, edge, f, u, d, stiff, shares, mixed, turned = refs
        slab = Slab(width, across)
        row = slab.row
        u[...] = jnp.zeros(u.shape, jnp.float32)
        f[...] = jnp.zeros(f.shape, jnp.float32)
        shares[...] = jnp.zeros(shares.shape, jnp.float32)
        stiff[...] = jnp.zeros(stiff.shape, jnp.float32)
        for n in range(len(sources)):
            for tile in range(SENT // 128):
                at = n * (SENT // 128) + tile
                for m in range(width // 4):
                    first = 12 * m + 4 * tile
                    mixed[at, 4 * m : 4 * m + 4, :] = arrived[n][first : first + 4, :]
                turned[n, 128 * tile : 128 * tile + 128, :] = mixed[at].T
        for field, target in enumerate((u, f)):
            for pair in range(PAIRS):

                def rows(start, field=field, pair=pair):
                    def fetch(device, q):
                        if device not in sources:
                            return None
                        at = BLOCK * (2 * q + field) + start
                        return turned[device - sources[0], at : at + 8, :]

                    value = window_pair(slab, 2 * pair - BEFORE, own_layers, fetch)
                    return jnp.zeros((8, width), jnp.float32) if value is None else value

                for i in range(3):
                    parts = [rows(24 * i + 8 * n) for n in range(3)]
                    if field == 0 and i == 0:
                        stiff[pair : pair + 1, :] = parts[0][TWIN : TWIN + 1]
                    parts[0] = jnp.where(row == TWIN, pltpu.roll(parts[0], TWIN, 0), parts[0])
                    parts.append(jnp.where(row < 4, 0.0, rows(68 + 4 * i)))
                    whole = jnp.concatenate(parts, 0)
                    target[i, pair] = whole * slab.keep if field == 0 else whole

        weights = [jnp.broadcast_to(transfer[:, n : n + 1], (32, width)) for n in range(8)]

        def restrict(pair, forces):
            for i in range(3):
                rest = slab.keep * (f[i, pair] - forces[i])
                for n in range(8):
                    part = rest * weights[n]
                    part = (part[0:8] + part[8:16]) + (part[16:24] + part[24:32])
                    shares[i, n, pl.ds(pair, 1), :] = jnp.sum(part, axis=0, keepdims=True)

        jobs = slab.smoothing(u, f, 0, d, spans[0:3], fine_bound)
        slab.run(u, stiff, spread, collect, jobs + [(*spans[3], restrict)])

        restricted = [
            slab.assemble({corner: shares[i, n] for n, corner in enumerate(CORNERS)})
            for i in range(3)
        ]
        for q in range(own_pairs):
            hard = stiff[own + q : own + q + 1, :]
            for i in range(3):
                message[i, q] = u[i, own + q]
                message[i, q, RESTRICTED_SLOT : RESTRICTED_SLOT + 1, :] = restricted[i][
                    own + q : own + q + 1
                ]
                edge[q, i : i + 1, :] = u[i, own + q, 0:1, :]
                edge[q, 3 + i : 4 + i, :] = restricted[i][own + q : own + q + 1]
            message[0, q, STIFF_SLOT : STIFF_SLOT + 1, :] = hard
            edge[q, 6:8, :] = jnp.broadcast_to(hard, (2, width))

    return first_kernel


def shares_sent(own_layers):
    return own_layers % 2 == 0


def sources_of(own_layers):
    below = 2 if shares_sent(own_layers) else 3
    whole = range(-below // own_layers, (own_layers + 2) // own_layers + 1)
    coarse = range(-(below + 2) // own_layers, (own_layers + 4) // own_layers + 1)
    return list(whole), [n for n in coarse if n not in whole]


def make_second_kernel(width, across, own_layers, fine_bound, coarse_bound):
    own = BEFORE_B // 2
    own_pairs = (own_layers + 1) // 2
    shift = (BEFORE - BEFORE_B) // 2
    whole, outer = sources_of(own_layers)
    steps = chebyshev_steps()
    spans = []
    for n in (3, 2, 1):
        low, high = BEFORE_B - n + shares_sent(own_layers), BEFORE_B + own_layers + n - 1
        spans.append((low // 2, (high + 1) // 2 - low // 2))

    def second_kernel(*refs):
        messages = dict(zip(whole, refs))
        refs = refs[len(whole) :]
        edges = dict(zip(outer, refs))
        f, spread, collect, transfer_back, out, u, d, stiff, coarse = refs[len(outer) :]
        slab = Slab(width, across)

        def pair_of(pair, fetch):
            return window_pair(slab, 2 * pair - BEFORE_B, own_layers, fetch)

        u[...] = jnp.zeros(u.shape, jnp.float32)
        coarse[...] = jnp.zeros(coarse.shape, jnp.float32)
        d[...] = jnp.zeros(d.shape, jnp.float32)
        for pair in range(PAIRS_B):
            for i in range(3):
                block = pair_of(pair, lambda n, q: messages[n][i, q] if n in messages else None)
                if block is not None:
                    u[i, pair] = block
            for n in range(7):

                def fetch(device, q, n=n):
                    if device in messages:
                        i, slot = ((n, 0), (n - 3, RESTRICTED_SLOT), (0, STIFF_SLOT))[n // 3]
                        return messages[device][i, q, slot : slot + 1, :]
                    return edges[device][q, n : n + 1, :] if device in edges else None

                line = pair_of(pair, fetch)
                if line is not None:
                    coarse[n, pair : pair + 1, :] = line
        stiff[...] = coarse[6]

        stiffness = coarse[6]
        keep_coarse = jnp.where(slab.bottom, 0.0, 1.0)
        start = [coarse[i] for i in range(3)]
        restricted = [coarse[3 + i] for i in range(3)]
        before = slab.coarse_force(start, stiffness)
        move = [(steps[0][1] / coarse_bound) * keep_coarse * restricted[i] for i in range(3)]
        level = [start[i] + move[i] for i in range(3)]
        for held, added in steps[1:]:
            force = slab.coarse_force(level, stiffness)
            for i in range(3):
                z = keep_coarse * (restricted[i] + before[i] - force[i])
                move[i] = held * move[i] + (added / coarse_bound) * z
                level[i] = level[i] + move[i]

        weights = [jnp.broadcast_to(transfer_back[:, n : n + 1], (32, width)) for n in range(8)]
        for i in range(3):
            change = slab.corners_of(level[i] - start[i])
            for pair in range(spans[0][0], min(spans[0][0] + spans[0][1] + 1, PAIRS_B)):
                lift = u[i, pair]
                for n, corner in enumerate(CORNERS):
                    lift = lift + weights[n] * change[corner][pair : pair + 1]
                u[i, pair] = lift

        jobs = slab.smoothing(u, f, shift, d, spans, fine_bound)
        owed = slab.owed(slab.run(u, stiff, spread, collect, jobs), fine_bound)

        lower = lax.broadcasted_iota(jnp.int32, (width // 8, 8, 128), 1) < 4
        nothing = jnp.zeros((8, width), jnp.float32)
        sides = []
        for q in range(2):
            if q or not shares_sent(own_layers):
                owed = [(nothing, nothing)] * 3
            rows = []
            for i in range(3):
                value = u[i, own + q]
                rows += [value[0:24], jnp.where(slab.row < 4, owed[i][1], value[24:32])]
            rows += [owed[i][0] for i in range(3)]
            rows += [level[i][own + q : own + q + 1] for i in range(3)] + [nothing[0:5]]
            sides.append(jnp.concatenate(rows, 0).T.reshape(width // 8, 8, 128))
        out[:, 0] = jnp.where(lower, sides[0], pltpu.roll(sides[1], 4, 1))
        out[:, 1] = jnp.where(lower, pltpu.roll(sides[0], 4, 1), sides[1])

    return second_kernel


def solution(mesh):
    rows_of, columns_of = mesh.shape["gx"], mesh.shape["gy"]
    devices = rows_of * columns_of
    order = ring_order(rows_of, columns_of)
    own_layers = EZ // devices
    own_pairs = (own_layers + 1) // 2
    width = 4 * devices
    across = 2 * rows_of
    near = first_sources(own_layers)
    whole, outer = sources_of(own_layers)
    spread, collect, fine_bound = element_tables()
    coarse_bound = build_tables([0.0, 1.0], 2)[2]
    transfer, transfer_back = transfer_table()
    wide = pltpu.CompilerParams(vmem_limit_bytes=60 * 1024 * 1024)
    limit = pltpu.CompilerParams(vmem_limit_bytes=48 * 1024 * 1024)
    f32 = jnp.float32

    pack = pl.pallas_call(
        functools.partial(pack_kernel, order),
        out_shape=jax.ShapeDtypeStruct((devices * 12, 128), f32),
        in_specs=[pl.BlockSpec(memory_space=pl.ANY)] * 5,
        out_specs=pl.BlockSpec(memory_space=pltpu.VMEM),
        scratch_shapes=[
            pltpu.VMEM((3, 6, 3, 384), f32),
            pltpu.VMEM((3, 6, 3, 384), f32),
            pltpu.VMEM((2, 1, EZ), f32),
            pltpu.VMEM((1, 1, 192), jnp.int32),
            pltpu.VMEM((384, 512), jnp.bfloat16),
            pltpu.VMEM((128, 384), f32),
            pltpu.VMEM((384, 128), f32),
            pltpu.VMEM((6, 136, 128), f32),
            pltpu.SemaphoreType.DMA((5,)),
        ],
        compiler_params=wide,
    )
    first = pl.pallas_call(
        make_first_kernel(width, across, own_layers, fine_bound),
        out_shape=(
            jax.ShapeDtypeStruct((3, own_pairs, 32, width), f32),
            jax.ShapeDtypeStruct((own_pairs, 8, width), f32),
            jax.ShapeDtypeStruct((3, PAIRS, 32, width), f32),
        ),
        scratch_shapes=[
            pltpu.VMEM((3, 8, 32, width), f32),
            pltpu.VMEM((3, 8, 32, width), f32),
            pltpu.VMEM((8, width), f32),
            pltpu.VMEM((3, 8, 8, width), f32),
            pltpu.VMEM((len(near) * (SENT // 128), width, 128), f32),
            pltpu.VMEM((len(near), SENT, width), f32),
        ],
        compiler_params=limit,
    )
    second = pl.pallas_call(
        make_second_kernel(width, across, own_layers, fine_bound, coarse_bound),
        out_shape=jax.ShapeDtypeStruct((devices // 2, 2, 8, 128), f32),
        scratch_shapes=[
            pltpu.VMEM((3, PAIRS_B + 2, 32, width), f32),
            pltpu.VMEM((3, PAIRS_B, 32, width), f32),
            pltpu.VMEM((PAIRS_B, width), f32),
            pltpu.VMEM((7, PAIRS_B, width), f32),
        ],
        compiler_params=limit,
    )
    unpack = pl.pallas_call(
        functools.partial(unpack_kernel, order),
        out_shape=(
            jax.ShapeDtypeStruct((3, 6, 3, 384), f32),
            jax.ShapeDtypeStruct((3, 2, 1, EZ), f32),
        ),
        scratch_shapes=[pltpu.VMEM((2, 128, 128), f32), pltpu.VMEM((384, 128), f32)],
        compiler_params=limit,
    )
    everyone = ("gy", "gx")

    def from_device(block, distance):
        place = {k: m % rows_of * columns_of + m // rows_of for m, k in enumerate(order)}
        route = [(place[(k + distance) % devices], place[k]) for k in range(devices)]
        return lax.ppermute(block, ("gx", "gy"), route)

    def body(initial, forcing, modulus, solid_list):
        sent = pack(initial, forcing, modulus, solid_list, jnp.asarray(pack_table()))
        sent = sent.reshape(devices, SENT // 128, 4, 128)
        arrived = lax.all_to_all(sent, everyone, 0, 0, tiled=True).reshape(devices * 12, 128)
        message, edge, load = first(
            *[from_device(arrived, n) if n else arrived for n in near],
            jnp.asarray(spread),
            jnp.asarray(collect),
            jnp.asarray(transfer),
        )
        messages = [from_device(message, n) if n else message for n in whole]
        edges = [from_device(edge, n) for n in outer]
        result = second(
            *messages,
            *edges,
            load,
            jnp.asarray(spread),
            jnp.asarray(collect),
            jnp.asarray(transfer_back),
        )
        back = lax.all_to_all(result.reshape(devices, 8, 128), everyone, 0, 0, tiled=True)
        return unpack(back, jnp.asarray(unpack_table()))

    placed = (
        P(None, "gx", "gy", None),
        P(None, "gx", "gy", None),
        P("gx", "gy", None),
        P("gx", "gy", None),
    )
    return jax.shard_map(
        body,
        mesh=mesh,
        in_specs=placed,
        out_specs=(P(None, "gx", "gy", None), P(None, "gx", "gy", None)),
        check_vma=False,
    )
```

```python
import functools
import math

import jax
import jax.numpy as jnp
import numpy as np
from jax import lax
from jax.experimental import pallas as pl
from jax.experimental.pallas import tpu as pltpu
from jax.sharding import PartitionSpec as P

CHEB = 3
EZ = 128

element_span = 20.0
lame_ratio = 4.0
rest_ratio = 1.25
modulus_top = 2.0
spectrum_floor = 0.05
interval_centre = (1.0 + spectrum_floor) / 2.0
interval_radius = (1.0 - spectrum_floor) / 2.0
interval_ratio = interval_centre / interval_radius
inner_anchors = (0.5 - 0.5 / math.sqrt(5.0), 0.5 + 0.5 / math.sqrt(5.0))

BEFORE = 4
PAIRS = 6
BEFORE_B = 6
PAIRS_B = 8
BLOCK = 84
SENT = 384

SLOTS = [
    (0, 0, 0), (1, 0, 0), (2, 0, 0), (0, 1, 0), (0, 2, 0), (0, 0, 1), (0, 0, 2), None,
    (0, 1, 1), (0, 1, 2), (0, 2, 1), (0, 2, 2), (1, 0, 1), (1, 0, 2), (2, 0, 1), (2, 0, 2),
    (1, 1, 0), (1, 2, 0), (2, 1, 0), (2, 2, 0), (1, 1, 1), (1, 1, 2), (1, 2, 1), (1, 2, 2),
    None, None, None, None, (2, 1, 1), (2, 1, 2), (2, 2, 1), (2, 2, 2),
]
TWIN = 7
NEXT_SLOTS = [0, 1, 2, 3, 4, 5, 6, 7, 16, 17, 18, 19]
NEXT_COLUMN = 4 * BLOCK
RESTRICTED_SLOT = 24
STIFF_SLOT = 25
OWN_SHIFT, SHIFT_X, SHIFT_Y, SHIFT_Z = (0, 0, 0), (1, 0, 0), (0, 1, 0), (0, 0, 1)
ELEMENT_ROWS = (
    [(slot, OWN_SHIFT) for slot in range(24)]
    + [(slot, SHIFT_Z) for slot in range(16, 20)]
    + [(slot, OWN_SHIFT) for slot in range(28, 32)]
    + [(slot, SHIFT_X) for slot in range(7)] + [None]
    + [(slot, SHIFT_Y) for slot in range(7)] + [(0, (0, 1, 1))]
    + [(slot, SHIFT_Z) for slot in range(7)] + [(0, (1, 0, 1))]
    + [(slot, SHIFT_X) for slot in range(8, 12)] + [(slot, SHIFT_Y) for slot in range(12, 16)]
    + [(0, (1, 1, 1)), (1, (0, 1, 1)), (2, (0, 1, 1)), (3, (1, 0, 1)), (4, (1, 0, 1))]
    + [(5, (1, 1, 0)), (6, (1, 1, 0)), (0, (1, 1, 0))]
)
ROWS = len(ELEMENT_ROWS)
DEPTH = 80
CORNERS = [(a, b, c) for a in range(2) for b in range(2) for c in range(2)]


def gauss_rule(point_count):
    if point_count == 2:
        offset = 1.0 / math.sqrt(3.0)
        points = [-offset, offset]
        weights = [1.0, 1.0]
    else:
        inner = math.sqrt(3.0 / 7.0 - 2.0 / 7.0 * math.sqrt(6.0 / 5.0))
        outer = math.sqrt(3.0 / 7.0 + 2.0 / 7.0 * math.sqrt(6.0 / 5.0))
        heavy = (18.0 + math.sqrt(30.0)) / 36.0
        light = (18.0 - math.sqrt(30.0)) / 36.0
        points = [-outer, -inner, inner, outer]
        weights = [light, heavy, heavy, light]
    return (np.array(points), np.array(weights))


def lagrange_tables(anchors, samples):
    values = np.zeros((len(samples), len(anchors)))
    slopes = np.zeros((len(samples), len(anchors)))
    for sample_index, sample in enumerate(samples):
        for anchor_index, anchor in enumerate(anchors):
            others = [
                location
                for location_index, location in enumerate(anchors)
                if location_index != anchor_index
            ]
            product = 1.0
            for location in others:
                product = product * (sample - location) / (anchor - location)
            values[sample_index, anchor_index] = product
            derivative = 0.0
            for skipped in range(len(others)):
                summand = 1.0 / (anchor - others[skipped])
                for kept_index in range(len(others)):
                    if kept_index != skipped:
                        summand = (
                            summand * (sample - others[kept_index]) / (anchor - others[kept_index])
                        )
                derivative = derivative + summand
            slopes[sample_index, anchor_index] = derivative
    return (values, slopes)


def outer_three(first, second, third):
    return (
        first[:, None, None, :, None, None]
        * second[None, :, None, None, :, None]
        * third[None, None, :, None, None, :]
    )


def build_tables(anchors, point_count):
    raw_points, raw_weights = gauss_rule(point_count)
    samples = (raw_points + 1.0) / 2.0
    weights = raw_weights / 2.0
    basis_values, slopes = lagrange_tables(anchors, samples)
    quad_total = point_count**3
    nodal_count = len(anchors) ** 3
    derivative_one = outer_three(slopes, basis_values, basis_values).reshape(
        quad_total, nodal_count
    )
    derivative_two = outer_three(basis_values, slopes, basis_values).reshape(
        quad_total, nodal_count
    )
    derivative_three = outer_three(basis_values, basis_values, slopes).reshape(
        quad_total, nodal_count
    )
    stacked = np.stack([derivative_one, derivative_two, derivative_three]) / element_span
    volume = (weights[:, None, None] * weights[None, :, None] * weights[None, None, :]).reshape(
        -1
    ) * element_span**3
    forward = stacked.reshape(3 * quad_total, nodal_count)
    backward = (stacked * volume[None, :, None]).reshape(3 * quad_total, nodal_count).T
    weighted = stacked * volume[None, :, None]
    laplace = weighted[0].T @ stacked[0] + weighted[1].T @ stacked[1] + weighted[2].T @ stacked[2]
    matrix = np.zeros((nodal_count, 3, nodal_count, 3))
    for first in range(3):
        for second in range(3):
            block = weighted[second].T @ stacked[first] + (lame_ratio - 1.0) * (
                weighted[first].T @ stacked[second]
            )
            if first == second:
                block = block + laplace
            matrix[:, first, :, second] = block
    matrix = matrix.reshape(3 * nodal_count, 3 * nodal_count)
    vector = 1.5 + np.cos(1.3 * np.arange(3 * nodal_count))
    for repeat in range(200):
        vector = matrix @ vector
        vector = vector / np.sqrt(vector @ vector)
    largest = vector @ (matrix @ vector)
    return (forward, backward, float(4.0 * modulus_top * 1.1 * largest))


def row_nodes():
    nodes = []
    for entry in ELEMENT_ROWS:
        slot = SLOTS[entry[0]] if entry else None
        if slot is None or any(s and n for s, n in zip(entry[1], slot)):
            nodes.append(None)
        else:
            a, b, c = (3 * s + n for s, n in zip(entry[1], slot))
            nodes.append(16 * a + 4 * b + c)
    return nodes


def halves(matrix):
    whole = np.asarray(matrix, np.float32)
    high = whole.astype(jnp.bfloat16)
    low = (whole - high.astype(np.float32)).astype(jnp.bfloat16)
    return high, low


def element_tables():
    forward, backward, bound = build_tables([0.0, inner_anchors[0], inner_anchors[1], 1.0], 4)
    spread = np.zeros((forward.shape[0], DEPTH))
    collect = np.zeros((ROWS, backward.shape[1]))
    for row, node in enumerate(row_nodes()):
        if node is not None:
            spread[:, row] = forward[:, node]
            collect[row, :] = backward[node, :]
    spread_high, spread_low = halves(spread)
    collect_high, collect_low = halves(collect)
    return (
        np.concatenate([spread_high, spread_high, spread_low], 1),
        np.concatenate([collect_high, collect_low], 0),
        bound,
    )


def transfer_table():
    table = np.zeros((8, 32))
    reach = (0.0, inner_anchors[0], inner_anchors[1])
    for row, corner in enumerate(CORNERS):
        for column, slot in enumerate(SLOTS):
            if slot is not None:
                weight = 1.0
                for side, node in zip(corner, slot):
                    weight = weight * (reach[node] if side else 1.0 - reach[node])
                table[row, column] = weight
    back = table.T.copy()
    back[TWIN] = back[0]
    return table.T.astype(np.float32), back.astype(np.float32)


def chebyshev_steps():
    steps = [(0.0, 1.0 / interval_centre)]
    ratio_now = 1.0 / interval_ratio
    for sweep in range(1, CHEB):
        ratio_next = 1.0 / (2.0 * interval_ratio - ratio_now)
        steps.append((ratio_next * ratio_now, 2.0 * ratio_next / interval_radius))
        ratio_now = ratio_next
    return steps


def stack_row(field, component, layer, b):
    return field * 54 + component * 18 + layer * 3 + b


def block_column(component, slot):
    return 72 + 4 * component + slot - 28 if slot >= 24 else 24 * component + slot


def pack_table():
    table = np.zeros((3, 128, 2, 2, 128), np.float32)
    for field in range(2):
        for x in range(2):
            for component in range(3):
                for column, slot in enumerate(SLOTS):
                    if slot is not None:
                        a, b, c = slot
                        row = stack_row(field, component, 3 * x + a, b)
                        table[c, row, field, x, block_column(component, column)] = 1.0
                        if field == 0 and column in NEXT_SLOTS:
                            at = BLOCK + 12 * component + NEXT_SLOTS.index(column)
                            table[c, row, 1, x, at] = 1.0
            table[0, 108 + x, 0, x, TWIN] = 1.0
    return table.reshape(384, 512).astype(jnp.bfloat16)


def unpack_table():
    table = np.zeros((2, 128, 4, 128), np.float32)
    for x in range(2):
        for component in range(3):
            for column, slot in enumerate(SLOTS):
                if slot is not None:
                    a, b, c = slot
                    row = stack_row(0, component, 3 * x + a, b)
                    table[x, component * 32 + column, c, row] = 1.0
                    if column < 5:
                        table[x, 96 + 8 * component + column, 3, row] = 1.0
                    if column == 0:
                        table[x, 96 + 8 * component + TWIN, 3, row] = 1.0
                    if 16 <= column < 20:
                        table[x, component * 32 + column + 8, 3, row] = 1.0
            table[x, 120 + component, 0, 54 + 2 * component + x] = 1.0
    return table.reshape(256, 512).astype(jnp.bfloat16)


def pick(values, table):
    count = values.shape[0]
    parts = jnp.dot(
        jnp.concatenate(high_low(values), 0), table, preferred_element_type=jnp.float32
    )
    return parts[:count] + parts[count:]


def ring_order(rows_of, columns_of):
    if (rows_of, columns_of) != (4, 8):
        return list(range(rows_of * columns_of))
    order = []
    for z in range(4):
        for x in range(2):
            for y in range(2):
                chip = (z, 7 - z, 15 - z, 8 + z)[2 * x + y]
                order += [2 * chip, 2 * chip + 1]
    return order


def pack_kernel(
    order,
    initial_at, forcing_at, modulus_at, listing_at, table_at, out,
    initial, forcing, modulus, listing, table, rows, turned, places, ready,
):
    own_layers = EZ // len(order)
    sources = (listing_at, modulus_at, initial_at, forcing_at, table_at)
    copies = [
        pltpu.make_async_copy(source, here, ready.at[n])
        for n, (source, here) in enumerate(
            zip(sources, (listing, modulus, initial, forcing, table))
        )
    ]
    for copy in copies:
        copy.start()
    rows[108:128, :] = jnp.zeros((20, 384), jnp.float32)
    copies[0].wait()
    copies[1].wait()
    listed = listing[0].astype(jnp.float32)
    listed = jnp.concatenate([listed, jnp.full((1, 64), 256.0, jnp.float32)], 1)
    listed = jnp.broadcast_to(listed, (128, 256)).T
    lanes = lax.broadcasted_iota(jnp.int32, (256, 128), 1).astype(jnp.float32)
    row_at = lax.broadcasted_iota(jnp.int32, (128, 128), 0)
    stiff = jnp.zeros((128, 128), jnp.float32)
    for x in range(2):
        hit = jnp.max(jnp.where(listed == lanes + 128.0 * x, 1.0, 0.0), axis=0, keepdims=True)
        stiff = jnp.where(row_at == 108 + x, hit * modulus[x], stiff)
    copies[2].wait()
    copies[3].wait()
    for field, source in enumerate((initial, forcing)):
        for component in range(3):
            for layer in range(6):
                at = stack_row(field, component, layer, 0)
                rows[at : at + 3, :] = source[component, layer]
    for part in range(3):
        span = slice(128 * part, 128 * part + 128)
        turned[span, :] = rows[:, span].T
    picked = [turned[pl.ds(c, 128, stride=3), :] for c in range(3)]
    picked[0] = picked[0] + stiff.T
    copies[4].wait()
    wide = pick(jnp.concatenate(picked, 1), table[...])
    lane = lax.broadcasted_iota(jnp.int32, (128, 128), 1)
    for x in range(2):
        tiles = [None] * (SENT // 128)
        for n in range(4):
            pair, field = n // 2, n % 2
            moved = wide[:, 128 * (2 * field + x) : 128 * (2 * field + x) + 128]
            first = BLOCK * n
            if pair:
                moved = pltpu.roll(moved, 128 - 2 * pair, 0)
            if first % 128:
                moved = pltpu.roll(moved, first % 128, 1)
            for tile in range(first // 128, (first + BLOCK - 1) // 128 + 1):
                before = tiles[tile]
                if before is None:
                    tiles[tile] = moved
                else:
                    tiles[tile] = jnp.where(lane >= first - 128 * tile, moved, before)
        above = wide[:, 128 * (2 + x) : 128 * (2 + x) + 128]
        above = pltpu.roll(pltpu.roll(above, 128 - own_layers, 0), (NEXT_COLUMN - BLOCK) % 128, 1)
        tiles[-1] = jnp.where(lane >= NEXT_COLUMN % 128, above, tiles[-1])
        for tile in range(SENT // 128):
            places[3 * x + tile, 0:128, :] = tiles[tile]
            places[3 * x + tile, 128:136, :] = jnp.zeros((8, 128), jnp.float32)
    for device, k in enumerate(order):
        for tile in range(SENT // 128):
            for x in range(2):
                at = 12 * device + 4 * tile + 2 * x
                out[at : at + 2, :] = places[
                    3 * x + tile, own_layers * k : own_layers * k + 2, :
                ]


def unpack_kernel(order, arrived, table, out, coarse_out, layers, turned):
    devices = arrived.shape[0]
    own_layers = EZ // devices
    for x in range(2):
        for layer in range(own_layers):
            row = (layer // 2) * 4 + x * 2 + layer % 2
            if order == sorted(order):
                layers[x, pl.ds(layer, devices, stride=own_layers), :] = arrived[:, row, :]
                continue
            for device, k in enumerate(order):
                at = own_layers * k + layer
                layers[x, at : at + 1, :] = arrived[device, row : row + 1, :]
    wide = pick(jnp.concatenate([layers[0], layers[1]], 1), table[...])
    shares = pltpu.roll(wide[:, 384:512], own_layers, 0)
    turned[pl.ds(0, 128, stride=3), :] = wide[:, 0:128] + shares
    for c in range(1, 3):
        turned[pl.ds(c, 128, stride=3), :] = wide[:, 128 * c : 128 * c + 128]
    for part in range(3):
        span = slice(128 * part, 128 * part + 128)
        back = turned[span, :].T
        for component in range(3):
            for layer in range(6):
                at = stack_row(0, component, layer, 0)
                out[component, layer, :, span] = back[at : at + 3, :]
    back = wide[:, 0:128].T
    for component in range(3):
        for x in range(2):
            at = 54 + 2 * component + x
            coarse_out[component, x] = back[at : at + 1, :]


def cofactor_rows(deform):
    return [
        [
            deform[(row_at + 1) % 3][(column + 1) % 3] * deform[(row_at + 2) % 3][(column + 2) % 3]
            - deform[(row_at + 1) % 3][(column + 2) % 3]
            * deform[(row_at + 2) % 3][(column + 1) % 3]
            for column in range(3)
        ]
        for row_at in range(3)
    ]


def point_stress(deform, stiffness, stiffness_four):
    cofactors = cofactor_rows(deform)
    jacobian = (
        deform[0][0] * cofactors[0][0]
        + deform[0][1] * cofactors[0][1]
        + deform[0][2] * cofactors[0][2]
    )
    pressure = stiffness_four * (jacobian - rest_ratio)
    return [
        [stiffness * deform[i][d] + pressure * cofactors[i][d] for d in range(3)] for i in range(3)
    ]


coarse_samples = [0.5 - 0.5 / math.sqrt(3.0), 0.5 + 0.5 / math.sqrt(3.0)]
two = range(2)


def at_points(low, high):
    change = high - low
    return [low + s * change for s in coarse_samples], change * (1.0 / element_span)


def ends_of(first, second):
    high = coarse_samples[0] * first + coarse_samples[1] * second
    return [first + second - high, high]


def high_low(values):
    high = values.astype(jnp.bfloat16)
    return high, (values - high.astype(jnp.float32)).astype(jnp.bfloat16)


def reads(pairs):
    return set(range(pairs[0], pairs[-1] + 2))


def plan_steps(spans):
    plan = []
    for first, count in spans:
        pairs = list(range(first, first + count))
        plan.append([pairs[n : n + 2] for n in range(0, count, 2)])
    for now, later in zip(plan, plan[1:]):
        if reads(later[0]) & set(now[-1]) and len(now[-1]) == 2:
            now[-1:] = [now[-1][:1], now[-1][1:]]
        if reads(later[0]) & set(now[-1]) and len(later[0]) == 2:
            later[:1] = [later[0][:1], later[0][1:]]
    return plan


class Slab:
    def __init__(self, width, across):
        self.width = width
        self.y_step = 2 * across
        lane = lax.broadcasted_iota(jnp.int32, (8, width), 1)
        x = (lane // 2) % across
        self.bottom, self.top, self.even = x == 0, x == across - 1, lane % 2 == 0
        self.row = lax.broadcasted_iota(jnp.int32, (8, width), 0)
        row = lax.broadcasted_iota(jnp.int32, (32, width), 0)
        lane = lax.broadcasted_iota(jnp.int32, (32, width), 1)
        on_face = (row == 0) | ((row >= 3) & (row <= 11))
        self.keep = jnp.where(on_face & ((lane // 2) % across == 0), 0.0, 1.0)

    def lanes(self, v, step):
        return pltpu.roll(v, step % self.width, 1)

    def from_next(self, v, x, y):
        if x or y:
            v = self.lanes(v, -2 * x - self.y_step * y)
        return jnp.where(self.top, 0.0, v) if x else v

    def from_next_z(self, v, ahead, x, y):
        step = -2 * x - self.y_step * y
        v = jnp.where(self.even, self.lanes(v, step - 1), self.lanes(ahead, step + 1))
        return jnp.where(self.top, 0.0, v) if x else v

    def onto_next(self, v, x, y, z=0):
        if x or y or z:
            v = self.lanes(v, 2 * x + self.y_step * y + z)
        return jnp.where(self.bottom, 0.0, v) if x else v

    def gather(self, here, ahead):
        row = self.row
        g0, g1, g2, g3 = here[0:8], here[8:16], here[16:24], here[24:32]
        a0 = ahead[0:8]
        z0, xz = self.from_next_z(g0, a0, 0, 0), self.from_next_z(g0, a0, 1, 0)
        yz, xyz = self.from_next_z(g0, a0, 0, 1), self.from_next_z(g0, a0, 1, 1)
        z2 = self.from_next_z(g2, ahead[16:24], 0, 0)
        edges = jnp.where(row <= 4, xz, self.from_next(g0, 1, 1))
        edges = jnp.where(row == 0, xyz, jnp.where(row <= 2, yz, edges))
        return jnp.concatenate(
            [
                g0,
                g1,
                g2,
                jnp.where(row < 4, z2, g3),
                self.from_next(g0, 1, 0),
                jnp.where(row == 7, yz, self.from_next(g0, 0, 1)),
                jnp.where(row == 7, xz, z0),
                jnp.where(row < 4, self.from_next(g1, 1, 0), self.from_next(g1, 0, 1)),
                edges,
                jnp.zeros_like(g0),
            ],
            0,
        )

    def scatter(self, part, behind):
        row = self.row
        g0, g1, g2, g3, x0, y0, z0, sides, edges = (part[8 * n : 8 * n + 8] for n in range(9))
        last = row == 7
        for_z = jnp.where(last, 0.0, z0)
        for_xz = jnp.where(last, z0, jnp.where((row == 3) | (row == 4), edges, 0.0))
        for_yz = jnp.where(last, y0, jnp.where((row == 1) | (row == 2), edges, 0.0))
        for_xyz = jnp.where(row == 0, edges, 0.0)
        for_xy = jnp.where(row >= 5, edges, 0.0)

        def above(z):
            return (
                self.onto_next(for_z, 0, 0, z)
                + self.onto_next(for_yz, 0, 1, z)
                + self.onto_next(for_xz, 1, 0, z)
                + self.onto_next(for_xyz, 1, 1, z)
            )

        own0 = g0 + self.onto_next(x0, 1, 0) + self.onto_next(jnp.where(last, 0.0, y0), 0, 1)
        own0 = own0 + self.onto_next(for_xy, 1, 1)
        own0 = own0 + jnp.where(self.even, behind[0], above(1))
        own1 = g1 + jnp.where(row < 4, self.onto_next(sides, 1, 0), self.onto_next(sides, 0, 1))
        share2 = jnp.where(self.even, behind[1], self.onto_next(g3, 0, 0, 1))
        own2 = g2 + jnp.where(row < 4, share2, 0.0)
        own3 = jnp.where(row < 4, 0.0, g3)
        moved = (above(-1), self.onto_next(g3, 0, 0, -1))
        return jnp.concatenate([self.twinned(own0), own1, own2, own3], 0), moved

    def twinned(self, v):
        twins = jnp.where(self.row == 7, pltpu.roll(v, 7, 0), 0.0)
        return v + jnp.where(self.row == 0, pltpu.roll(v, 1, 0), twins)

    def absorb(self, total, behind):
        low = self.twinned(jnp.where(self.even, behind[0], 0.0))
        high = jnp.where(self.even & (self.row < 4), behind[1], 0.0)
        return jnp.concatenate(
            [total[0:8] + low, total[8:16], total[16:24] + high, total[24:32]], 0
        )

    def gradient(self, u, spread, pairs):
        blocks = [self.gather(u[i, pair], u[i, pair + 1]) for i in range(3) for pair in pairs]
        high, low = high_low(jnp.concatenate(blocks, 1))
        return jnp.dot(
            spread[...],
            jnp.concatenate([high, low, high], 0),
            preferred_element_type=jnp.float32,
        )

    def force(self, gradient, stiff, collect, pairs):
        width = len(pairs) * self.width
        stiffness = jnp.concatenate([stiff[pair : pair + 1, :] for pair in pairs], 1)
        deform = [
            [
                gradient[64 * e : 64 * e + 64, width * i : width * (i + 1)]
                + (1.0 if i == e else 0.0)
                for e in range(3)
            ]
            for i in range(3)
        ]
        stress = point_stress(deform, stiffness, lame_ratio * stiffness)
        stress = jnp.concatenate(
            [jnp.concatenate([stress[i][e] for i in range(3)], 1) for e in range(3)], 0
        )
        high, low = high_low(stress)
        force = jnp.dot(collect[...], high, preferred_element_type=jnp.float32)
        return force[0:ROWS] + (
            force[ROWS:] + jnp.dot(collect[0:ROWS], low, preferred_element_type=jnp.float32)
        )

    def run(self, u, stiff, spread, collect, jobs, given=None):
        plan = plan_steps([job[:2] for job in jobs])
        steps = [(pairs, n) for n, chunks in enumerate(plan) for pairs in chunks]
        none = jnp.zeros((8, self.width), jnp.float32)
        ahead, carry, job = None, None, None
        for at, (pairs, n) in enumerate(steps):
            ready = given is not None and n == 0 and pairs == given[0]
            gradient = ahead
            if ahead is None and not ready:
                gradient = self.gradient(u, spread, pairs)
            if not ready:
                ahead = None
            if ahead is None and at + 1 < len(steps):
                later, later_job = steps[at + 1]
                if given is not None and later_job == 0 and later == given[0]:
                    later, later_job = steps[at + 2]
                if later_job == n or not reads(later) & set(pairs):
                    ahead = self.gradient(u, spread, later)
            if job != n:
                carry, job = [(none, none) for i in range(3)], n
            if ready:
                for q, pair in enumerate(pairs):
                    total = given[1][q]
                    if q == 0:
                        total = [self.absorb(total[i], carry[i]) for i in range(3)]
                    jobs[n][2](pair, total)
                carry = list(given[2])
                continue
            force = self.force(gradient, stiff, collect, pairs)
            totals = [[] for pair in pairs]
            for q in range(len(pairs)):
                for i in range(3):
                    lane = (len(pairs) * i + q) * self.width
                    total, carry[i] = self.scatter(force[:, lane : lane + self.width], carry[i])
                    totals[q].append(total)
            for pair, total in zip(pairs, totals):
                jobs[n][2](pair, total)
        return carry

    def smoothing(self, u, f, f_shift, d, spans, bound):
        jobs = []
        for (first, count), (held, added) in zip(spans, chebyshev_steps()):

            def finish(pair, forces, held=held, added=added):
                for i in range(3):
                    z = (added / bound) * self.keep * (f[i, pair + f_shift] - forces[i])
                    move = held * d[i, pair] + z if held else z
                    d[i, pair] = move
                    u[i, pair] = u[i, pair] + move

            jobs.append((first, count, finish))
        return jobs

    def owed(self, carry, bound):
        scale = -chebyshev_steps()[-1][1] / bound
        return [
            (
                scale * jnp.where(self.even, low, 0.0) * self.keep[0:8],
                scale * jnp.where(self.even, high, 0.0) * self.keep[16:24],
            )
            for low, high in carry
        ]

    def corners_of(self, v):
        ahead = pltpu.roll(v, 7, 0)
        found = {}
        for a in range(2):
            for b in range(2):
                found[a, b, 0] = self.from_next(v, a, b)
                found[a, b, 1] = self.from_next_z(v, ahead, a, b)
        return found

    def assemble(self, part):
        here, odd, even = 0.0, 0.0, 0.0
        for a in range(2):
            for b in range(2):
                here = here + self.onto_next(part[a, b, 0], a, b)
                odd = odd + self.onto_next(part[a, b, 1], a, b, 1)
                even = even + self.onto_next(part[a, b, 1], a, b, -1)
        return here + jnp.where(self.even, pltpu.roll(even, 1, 0), odd)

    def coarse_force(self, values, stiffness):
        grads = []
        for i in range(3):
            v = self.corners_of(values[i])
            vz, sz = {}, {}
            for a in two:
                for b in two:
                    vz[a, b], sz[a, b] = at_points(v[a, b, 0], v[a, b, 1])
            vv, vs, sv = {}, {}, {}
            for a in two:
                for k in two:
                    vv[a, k], vs[a, k] = at_points(vz[a, 0][k], vz[a, 1][k])
                sv[a], unused = at_points(sz[a, 0], sz[a, 1])
            dx, dy, dz = {}, {}, {}
            for k in two:
                for j in two:
                    dx[j, k] = (vv[1, k][j] - vv[0, k][j]) * (1.0 / element_span)
                line, unused = at_points(vs[0, k], vs[1, k])
                for h in two:
                    dy[h, k] = line[h]
            for j in two:
                line, unused = at_points(sv[0][j], sv[1][j])
                for h in two:
                    dz[h, j] = line[h]
            grads.append((dx, dy, dz))
        weight = element_span**2 / 8.0
        scaled = weight * stiffness
        scaled_four = lame_ratio * scaled
        sums = [({}, {}, {}) for i in range(3)]

        def add(table, key, value):
            table[key] = table[key] + value if key in table else value

        for h in two:
            for j in two:
                for k in two:
                    deform = [
                        [grads[i][0][j, k], grads[i][1][h, k], grads[i][2][h, j]]
                        for i in range(3)
                    ]
                    for i in range(3):
                        deform[i][i] = deform[i][i] + 1.0
                    stress = point_stress(deform, scaled, scaled_four)
                    for i in range(3):
                        add(sums[i][0], (j, k), stress[i][0])
                        add(sums[i][1], (h, k), stress[i][1])
                        add(sums[i][2], (h, j), stress[i][2])

        forces = []
        for i in range(3):
            part = {}
            qx, qy, qz = sums[i]
            along_z = [ends_of(qx[j, 0], qx[j, 1]) for j in two]
            for c in two:
                line = ends_of(along_z[0][c], along_z[1][c])
                for b in two:
                    part[0, b, c] = -line[b]
                    part[1, b, c] = line[b]
            along_z = [ends_of(qy[h, 0], qy[h, 1]) for h in two]
            for c in two:
                line = ends_of(along_z[0][c], along_z[1][c])
                for a in two:
                    part[a, 0, c] = part[a, 0, c] - line[a]
                    part[a, 1, c] = part[a, 1, c] + line[a]
            along_y = [ends_of(qz[h, 0], qz[h, 1]) for h in two]
            for b in two:
                line = ends_of(along_y[0][b], along_y[1][b])
                for a in two:
                    part[a, b, 0] = part[a, b, 0] - line[a]
                    part[a, b, 1] = part[a, b, 1] + line[a]
            forces.append(self.assemble(part))
        return forces


def window_pair(slab, first_layer, own_layers, fetch):
    found = []
    for parity in range(2):
        layer = first_layer + parity
        device = layer // own_layers
        layer = layer - device * own_layers
        found.append((device, layer // 2, layer % 2))
    values = [fetch(device, q) for device, q, parity in found]
    if found[0][:2] == found[1][:2] or (values[0] is None and values[1] is None):
        return values[0]
    for parity in range(2):
        if values[parity] is None:
            values[parity] = jnp.zeros_like(values[1 - parity])
        elif found[parity][2] != parity:
            values[parity] = slab.lanes(values[parity], 2 * parity - 1)
    lane = lax.broadcasted_iota(jnp.int32, values[0].shape, 1)
    return jnp.where(lane % 2 == 0, values[0], values[1])


def first_sources(own_layers):
    return list(range(-BEFORE // own_layers, (own_layers + BEFORE - 1) // own_layers + 1))


def turn_rows(block, mixed, turned, width, at):
    for tile in range(SENT // 128):
        n = at * (SENT // 128) + tile
        for m in range(width // 4):
            first = 12 * m + 4 * tile
            mixed[n, 4 * m : 4 * m + 4, :] = block[first : first + 4, :]
        turned[at, 128 * tile : 128 * tile + 128, :] = mixed[n].T


def regroup(slab, field, rows):
    values, hard = [], None
    for i in range(3):
        parts = [rows(24 * i + 8 * n) for n in range(3)]
        if field == 0 and i == 0:
            hard = parts[0][TWIN : TWIN + 1]
        parts[0] = jnp.where(slab.row == TWIN, pltpu.roll(parts[0], TWIN, 0), parts[0])
        parts.append(jnp.where(slab.row < 4, 0.0, rows(68 + 4 * i)))
        whole = jnp.concatenate(parts, 0)
        values.append(whole * slab.keep if field == 0 else whole)
    return values, hard


def make_own_kernel(width, across, own_layers):
    own_pairs = own_layers // 2
    pairs = list(range(own_pairs))

    def own_kernel(block, spread, collect, u, f, stiff, forces, moved, mixed, turned):
        slab = Slab(width, across)
        turn_rows(block, mixed, turned, width, 0)
        for pair in pairs:
            for field, target in enumerate((u, f)):

                def rows(start, field=field, pair=pair):
                    at = BLOCK * (2 * pair + field) + start
                    return turned[0, at : at + 8, :]

                values, hard = regroup(slab, field, rows)
                for i in range(3):
                    target[i, pair] = values[i]
                if field == 0:
                    stiff[pair : pair + 1, :] = hard
        for i in range(3):
            low = turned[0, NEXT_COLUMN + 12 * i : NEXT_COLUMN + 12 * i + 8, :]
            high = turned[0, NEXT_COLUMN + 12 * i + 4 : NEXT_COLUMN + 12 * i + 12, :]
            high = jnp.where(slab.row < 4, pltpu.roll(high, 4, 0), 0.0)
            low = jnp.where(slab.row == TWIN, pltpu.roll(low, TWIN, 0), low)
            nothing = jnp.zeros((8, width), jnp.float32)
            u[i, own_pairs] = jnp.concatenate([low, nothing, high, nothing], 0) * slab.keep

        def finish(pair, total):
            for i in range(3):
                forces[i, pair] = total[i]

        carry = slab.run(u, stiff, spread, collect, [(0, own_pairs, finish)])
        for i in range(3):
            moved[i, 0] = carry[i][0]
            moved[i, 1] = carry[i][1]

    return own_kernel


def make_first_kernel(width, across, own_layers, fine_bound):
    own = BEFORE // 2
    own_pairs = (own_layers + 1) // 2
    spans = []
    for n in (4, 3, 2, 1):
        low, high = BEFORE - n, BEFORE + own_layers + n - 1
        spans.append((low // 2, (high + 1) // 2 - low // 2))
    prepared = own_layers == 4
    sources = [n for n in first_sources(own_layers) if n or not prepared]

    def first_kernel(*refs):
        arrived = refs[: len(sources)]
        refs = refs[len(sources) :]
        if prepared:
            own_u, own_f, own_stiff, own_forces, own_moved = refs[:5]
            refs = refs[5:]
        spread, collect, transfer, message, edge, f, u, d, stiff, shares, mixed, turned = refs
        slab = Slab(width, across)
        u[...] = jnp.zeros(u.shape, jnp.float32)
        if not prepared:
            f[...] = jnp.zeros(f.shape, jnp.float32)
        shares[...] = jnp.zeros(shares.shape, jnp.float32)
        stiff[...] = jnp.zeros(stiff.shape, jnp.float32)
        for n in range(len(sources)):
            turn_rows(arrived[n], mixed, turned, width, n)
        for pair in range(PAIRS):
            if prepared and own <= pair < own + own_pairs:
                for i in range(3):
                    u[i, pair] = own_u[i, pair - own]
                    f[i, pair] = own_f[i, pair - own]
                stiff[pair : pair + 1, :] = own_stiff[pair - own : pair - own + 1, :]
                continue
            for field, target in enumerate((u, f)):

                def rows(start, field=field, pair=pair):
                    def fetch(device, q):
                        if device not in sources:
                            return None
                        at = BLOCK * (2 * q + field) + start
                        return turned[sources.index(device), at : at + 8, :]

                    value = window_pair(slab, 2 * pair - BEFORE, own_layers, fetch)
                    return jnp.zeros((8, width), jnp.float32) if value is None else value

                values, hard = regroup(slab, field, rows)
                for i in range(3):
                    target[i, pair] = values[i]
                if field == 0:
                    stiff[pair : pair + 1, :] = hard
        given = None
        if prepared:
            given = (
                list(range(own, own + own_pairs)),
                [[own_forces[i, q] for i in range(3)] for q in range(own_pairs)],
                [(own_moved[i, 0], own_moved[i, 1]) for i in range(3)],
            )

        weights = [jnp.broadcast_to(transfer[:, n : n + 1], (32, width)) for n in range(8)]

        def restrict(pair, forces):
            for i in range(3):
                rest = slab.keep * (f[i, pair] - forces[i])
                for n in range(8):
                    part = rest * weights[n]
                    part = (part[0:8] + part[8:16]) + (part[16:24] + part[24:32])
                    shares[i, n, pl.ds(pair, 1), :] = jnp.sum(part, axis=0, keepdims=True)

        jobs = slab.smoothing(u, f, 0, d, spans[0:3], fine_bound)
        slab.run(u, stiff, spread, collect, jobs + [(*spans[3], restrict)], given)

        restricted = [
            slab.assemble({corner: shares[i, n] for n, corner in enumerate(CORNERS)})
            for i in range(3)
        ]
        for q in range(own_pairs):
            hard = stiff[own + q : own + q + 1, :]
            for i in range(3):
                message[i, q] = u[i, own + q]
                message[i, q, RESTRICTED_SLOT : RESTRICTED_SLOT + 1, :] = restricted[i][
                    own + q : own + q + 1
                ]
                edge[q, i : i + 1, :] = u[i, own + q, 0:1, :]
                edge[q, 3 + i : 4 + i, :] = restricted[i][own + q : own + q + 1]
            message[0, q, STIFF_SLOT : STIFF_SLOT + 1, :] = hard
            edge[q, 6:8, :] = jnp.broadcast_to(hard, (2, width))

    return first_kernel


def shares_sent(own_layers):
    return own_layers % 2 == 0


def sources_of(own_layers):
    below = 2 if shares_sent(own_layers) else 3
    whole = range(-below // own_layers, (own_layers + 2) // own_layers + 1)
    coarse = range(-(below + 2) // own_layers, (own_layers + 4) // own_layers + 1)
    return list(whole), [n for n in coarse if n not in whole]


def make_second_kernel(width, across, own_layers, fine_bound, coarse_bound):
    own = BEFORE_B // 2
    own_pairs = (own_layers + 1) // 2
    shift = (BEFORE - BEFORE_B) // 2
    whole, outer = sources_of(own_layers)
    steps = chebyshev_steps()
    spans = []
    for n in (3, 2, 1):
        low, high = BEFORE_B - n + shares_sent(own_layers), BEFORE_B + own_layers + n - 1
        spans.append((low // 2, (high + 1) // 2 - low // 2))

    def second_kernel(*refs):
        messages = dict(zip(whole, refs))
        refs = refs[len(whole) :]
        edges = dict(zip(outer, refs))
        f, spread, collect, transfer_back, out, u, d, stiff, coarse = refs[len(outer) :]
        slab = Slab(width, across)

        def pair_of(pair, fetch):
            return window_pair(slab, 2 * pair - BEFORE_B, own_layers, fetch)

        u[...] = jnp.zeros(u.shape, jnp.float32)
        coarse[...] = jnp.zeros(coarse.shape, jnp.float32)
        d[...] = jnp.zeros(d.shape, jnp.float32)
        for pair in range(PAIRS_B):
            for i in range(3):
                block = pair_of(pair, lambda n, q: messages[n][i, q] if n in messages else None)
                if block is not None:
                    u[i, pair] = block
            for n in range(7):

                def fetch(device, q, n=n):
                    if device in messages:
                        i, slot = ((n, 0), (n - 3, RESTRICTED_SLOT), (0, STIFF_SLOT))[n // 3]
                        return messages[device][i, q, slot : slot + 1, :]
                    return edges[device][q, n : n + 1, :] if device in edges else None

                line = pair_of(pair, fetch)
                if line is not None:
                    coarse[n, pair : pair + 1, :] = line
        stiff[...] = coarse[6]

        stiffness = coarse[6]
        keep_coarse = jnp.where(slab.bottom, 0.0, 1.0)
        start = [coarse[i] for i in range(3)]
        restricted = [coarse[3 + i] for i in range(3)]
        before = slab.coarse_force(start, stiffness)
        move = [(steps[0][1] / coarse_bound) * keep_coarse * restricted[i] for i in range(3)]
        level = [start[i] + move[i] for i in range(3)]
        for held, added in steps[1:]:
            force = slab.coarse_force(level, stiffness)
            for i in range(3):
                z = keep_coarse * (restricted[i] + before[i] - force[i])
                move[i] = held * move[i] + (added / coarse_bound) * z
                level[i] = level[i] + move[i]

        weights = [jnp.broadcast_to(transfer_back[:, n : n + 1], (32, width)) for n in range(8)]
        for i in range(3):
            change = slab.corners_of(level[i] - start[i])
            for pair in range(spans[0][0], min(spans[0][0] + spans[0][1] + 1, PAIRS_B)):
                lift = u[i, pair]
                for n, corner in enumerate(CORNERS):
                    lift = lift + weights[n] * change[corner][pair : pair + 1]
                u[i, pair] = lift

        jobs = slab.smoothing(u, f, shift, d, spans, fine_bound)
        owed = slab.owed(slab.run(u, stiff, spread, collect, jobs), fine_bound)

        lower = lax.broadcasted_iota(jnp.int32, (width // 8, 8, 128), 1) < 4
        nothing = jnp.zeros((8, width), jnp.float32)
        sides = []
        for q in range(2):
            if q or not shares_sent(own_layers):
                owed = [(nothing, nothing)] * 3
            rows = []
            for i in range(3):
                value = u[i, own + q]
                rows += [value[0:24], jnp.where(slab.row < 4, owed[i][1], value[24:32])]
            rows += [owed[i][0] for i in range(3)]
            rows += [level[i][own + q : own + q + 1] for i in range(3)] + [nothing[0:5]]
            sides.append(jnp.concatenate(rows, 0).T.reshape(width // 8, 8, 128))
        out[:, 0] = jnp.where(lower, sides[0], pltpu.roll(sides[1], 4, 1))
        out[:, 1] = jnp.where(lower, pltpu.roll(sides[0], 4, 1), sides[1])

    return second_kernel


def solution(mesh):
    rows_of, columns_of = mesh.shape["gx"], mesh.shape["gy"]
    devices = rows_of * columns_of
    order = ring_order(rows_of, columns_of)
    own_layers = EZ // devices
    own_pairs = (own_layers + 1) // 2
    width = 4 * devices
    across = 2 * rows_of
    near = first_sources(own_layers)
    prepared = own_layers == 4
    whole, outer = sources_of(own_layers)
    spread, collect, fine_bound = element_tables()
    coarse_bound = build_tables([0.0, 1.0], 2)[2]
    transfer, transfer_back = transfer_table()
    wide = pltpu.CompilerParams(vmem_limit_bytes=60 * 1024 * 1024)
    limit = pltpu.CompilerParams(vmem_limit_bytes=48 * 1024 * 1024)
    f32 = jnp.float32

    pack = pl.pallas_call(
        functools.partial(pack_kernel, order),
        out_shape=jax.ShapeDtypeStruct((devices * 12, 128), f32),
        in_specs=[pl.BlockSpec(memory_space=pl.ANY)] * 5,
        out_specs=pl.BlockSpec(memory_space=pltpu.VMEM),
        scratch_shapes=[
            pltpu.VMEM((3, 6, 3, 384), f32),
            pltpu.VMEM((3, 6, 3, 384), f32),
            pltpu.VMEM((2, 1, EZ), f32),
            pltpu.VMEM((1, 1, 192), jnp.int32),
            pltpu.VMEM((384, 512), jnp.bfloat16),
            pltpu.VMEM((128, 384), f32),
            pltpu.VMEM((384, 128), f32),
            pltpu.VMEM((6, 136, 128), f32),
            pltpu.SemaphoreType.DMA((5,)),
        ],
        compiler_params=wide,
    )
    own = pl.pallas_call(
        make_own_kernel(width, across, own_layers),
        out_shape=(
            jax.ShapeDtypeStruct((3, own_pairs + 1, 32, width), f32),
            jax.ShapeDtypeStruct((3, own_pairs, 32, width), f32),
            jax.ShapeDtypeStruct((own_pairs, width), f32),
            jax.ShapeDtypeStruct((3, own_pairs, 32, width), f32),
            jax.ShapeDtypeStruct((3, 2, 8, width), f32),
        ),
        scratch_shapes=[
            pltpu.VMEM((SENT // 128, width, 128), f32),
            pltpu.VMEM((1, SENT, width), f32),
        ],
        compiler_params=limit,
        cost_estimate=pl.CostEstimate(flops=400_000_000, bytes_accessed=1_000_000, transcendentals=0),
    )
    first = pl.pallas_call(
        make_first_kernel(width, across, own_layers, fine_bound),
        out_shape=(
            jax.ShapeDtypeStruct((3, own_pairs, 32, width), f32),
            jax.ShapeDtypeStruct((own_pairs, 8, width), f32),
            jax.ShapeDtypeStruct((3, PAIRS, 32, width), f32),
        ),
        scratch_shapes=[
            pltpu.VMEM((3, 8, 32, width), f32),
            pltpu.VMEM((3, 8, 32, width), f32),
            pltpu.VMEM((8, width), f32),
            pltpu.VMEM((3, 8, 8, width), f32),
            pltpu.VMEM((len(near) * (SENT // 128), width, 128), f32),
            pltpu.VMEM((len(near), SENT, width), f32),
        ],
        compiler_params=limit,
    )
    second = pl.pallas_call(
        make_second_kernel(width, across, own_layers, fine_bound, coarse_bound),
        out_shape=jax.ShapeDtypeStruct((devices // 2, 2, 8, 128), f32),
        scratch_shapes=[
            pltpu.VMEM((3, PAIRS_B + 2, 32, width), f32),
            pltpu.VMEM((3, PAIRS_B, 32, width), f32),
            pltpu.VMEM((PAIRS_B, width), f32),
            pltpu.VMEM((7, PAIRS_B, width), f32),
        ],
        compiler_params=limit,
    )
    unpack = pl.pallas_call(
        functools.partial(unpack_kernel, order),
        out_shape=(
            jax.ShapeDtypeStruct((3, 6, 3, 384), f32),
            jax.ShapeDtypeStruct((3, 2, 1, EZ), f32),
        ),
        scratch_shapes=[pltpu.VMEM((2, 128, 128), f32), pltpu.VMEM((384, 128), f32)],
        compiler_params=limit,
    )
    everyone = ("gy", "gx")

    def from_device(block, distance):
        place = {k: m % rows_of * columns_of + m // rows_of for m, k in enumerate(order)}
        route = [(place[(k + distance) % devices], place[k]) for k in range(devices)]
        return lax.ppermute(block, ("gx", "gy"), route)

    def body(initial, forcing, modulus, solid_list):
        sent = pack(initial, forcing, modulus, solid_list, jnp.asarray(pack_table()))
        sent = sent.reshape(devices, SENT // 128, 4, 128)
        arrived = lax.all_to_all(sent, everyone, 0, 0, tiled=True).reshape(devices * 12, 128)
        blocks = [from_device(arrived, n) if n else arrived for n in near]
        if prepared:
            blocks = [block for n, block in zip(near, blocks) if n]
            blocks += own(arrived, jnp.asarray(spread), jnp.asarray(collect))
        message, edge, load = first(
            *blocks,
            jnp.asarray(spread),
            jnp.asarray(collect),
            jnp.asarray(transfer),
        )
        messages = [from_device(message, n) if n else message for n in whole]
        edges = [from_device(edge, n) for n in outer]
        result = second(
            *messages,
            *edges,
            load,
            jnp.asarray(spread),
            jnp.asarray(collect),
            jnp.asarray(transfer_back),
        )
        back = lax.all_to_all(result.reshape(devices, 8, 128), everyone, 0, 0, tiled=True)
        return unpack(back, jnp.asarray(unpack_table()))

    placed = (
        P(None, "gx", "gy", None),
        P(None, "gx", "gy", None),
        P("gx", "gy", None),
        P("gx", "gy", None),
    )
    return jax.shard_map(
        body,
        mesh=mesh,
        in_specs=placed,
        out_specs=(P(None, "gx", "gy", None), P(None, "gx", "gy", None)),
        check_vma=False,
    )
```

```python
import functools
import math

import jax
import jax.numpy as jnp
import numpy as np
from jax import lax
from jax.experimental import pallas as pl
from jax.experimental.pallas import tpu as pltpu
from jax.sharding import PartitionSpec as P

CHEB = 3
EZ = 128

element_span = 20.0
lame_ratio = 4.0
rest_ratio = 1.25
modulus_top = 2.0
spectrum_floor = 0.05
interval_centre = (1.0 + spectrum_floor) / 2.0
interval_radius = (1.0 - spectrum_floor) / 2.0
interval_ratio = interval_centre / interval_radius
inner_anchors = (0.5 - 0.5 / math.sqrt(5.0), 0.5 + 0.5 / math.sqrt(5.0))

BEFORE = 4
PAIRS = 6
BEFORE_B = 6
PAIRS_B = 8
BLOCK = 84
SENT = 384

SLOTS = [
    (0, 0, 0), (1, 0, 0), (2, 0, 0), (0, 1, 0), (0, 2, 0), (0, 0, 1), (0, 0, 2), None,
    (0, 1, 1), (0, 1, 2), (0, 2, 1), (0, 2, 2), (1, 0, 1), (1, 0, 2), (2, 0, 1), (2, 0, 2),
    (1, 1, 0), (1, 2, 0), (2, 1, 0), (2, 2, 0), (1, 1, 1), (1, 1, 2), (1, 2, 1), (1, 2, 2),
    None, None, None, None, (2, 1, 1), (2, 1, 2), (2, 2, 1), (2, 2, 2),
]
TWIN = 7
NEXT_SLOTS = [0, 1, 2, 3, 4, 5, 6, 7, 16, 17, 18, 19]
NEXT_COLUMN = 4 * BLOCK
RESTRICTED_SLOT = 24
STIFF_SLOT = 25
OWN_SHIFT, SHIFT_X, SHIFT_Y, SHIFT_Z = (0, 0, 0), (1, 0, 0), (0, 1, 0), (0, 0, 1)
ELEMENT_ROWS = (
    [(slot, OWN_SHIFT) for slot in range(24)]
    + [(slot, SHIFT_Z) for slot in range(16, 20)]
    + [(slot, OWN_SHIFT) for slot in range(28, 32)]
    + [(slot, SHIFT_X) for slot in range(7)] + [None]
    + [(slot, SHIFT_Y) for slot in range(7)] + [(0, (0, 1, 1))]
    + [(slot, SHIFT_Z) for slot in range(7)] + [(0, (1, 0, 1))]
    + [(slot, SHIFT_X) for slot in range(8, 12)] + [(slot, SHIFT_Y) for slot in range(12, 16)]
    + [(0, (1, 1, 1)), (1, (0, 1, 1)), (2, (0, 1, 1)), (3, (1, 0, 1)), (4, (1, 0, 1))]
    + [(5, (1, 1, 0)), (6, (1, 1, 0)), (0, (1, 1, 0))]
)
ROWS = len(ELEMENT_ROWS)
DEPTH = 80
CORNERS = [(a, b, c) for a in range(2) for b in range(2) for c in range(2)]


def gauss_rule(point_count):
    if point_count == 2:
        offset = 1.0 / math.sqrt(3.0)
        points = [-offset, offset]
        weights = [1.0, 1.0]
    else:
        inner = math.sqrt(3.0 / 7.0 - 2.0 / 7.0 * math.sqrt(6.0 / 5.0))
        outer = math.sqrt(3.0 / 7.0 + 2.0 / 7.0 * math.sqrt(6.0 / 5.0))
        heavy = (18.0 + math.sqrt(30.0)) / 36.0
        light = (18.0 - math.sqrt(30.0)) / 36.0
        points = [-outer, -inner, inner, outer]
        weights = [light, heavy, heavy, light]
    return (np.array(points), np.array(weights))


def lagrange_tables(anchors, samples):
    values = np.zeros((len(samples), len(anchors)))
    slopes = np.zeros((len(samples), len(anchors)))
    for sample_index, sample in enumerate(samples):
        for anchor_index, anchor in enumerate(anchors):
            others = [
                location
                for location_index, location in enumerate(anchors)
                if location_index != anchor_index
            ]
            product = 1.0
            for location in others:
                product = product * (sample - location) / (anchor - location)
            values[sample_index, anchor_index] = product
            derivative = 0.0
            for skipped in range(len(others)):
                summand = 1.0 / (anchor - others[skipped])
                for kept_index in range(len(others)):
                    if kept_index != skipped:
                        summand = (
                            summand * (sample - others[kept_index]) / (anchor - others[kept_index])
                        )
                derivative = derivative + summand
            slopes[sample_index, anchor_index] = derivative
    return (values, slopes)


def outer_three(first, second, third):
    return (
        first[:, None, None, :, None, None]
        * second[None, :, None, None, :, None]
        * third[None, None, :, None, None, :]
    )


def build_tables(anchors, point_count):
    raw_points, raw_weights = gauss_rule(point_count)
    samples = (raw_points + 1.0) / 2.0
    weights = raw_weights / 2.0
    basis_values, slopes = lagrange_tables(anchors, samples)
    quad_total = point_count**3
    nodal_count = len(anchors) ** 3
    derivative_one = outer_three(slopes, basis_values, basis_values).reshape(
        quad_total, nodal_count
    )
    derivative_two = outer_three(basis_values, slopes, basis_values).reshape(
        quad_total, nodal_count
    )
    derivative_three = outer_three(basis_values, basis_values, slopes).reshape(
        quad_total, nodal_count
    )
    stacked = np.stack([derivative_one, derivative_two, derivative_three]) / element_span
    volume = (weights[:, None, None] * weights[None, :, None] * weights[None, None, :]).reshape(
        -1
    ) * element_span**3
    forward = stacked.reshape(3 * quad_total, nodal_count)
    backward = (stacked * volume[None, :, None]).reshape(3 * quad_total, nodal_count).T
    weighted = stacked * volume[None, :, None]
    laplace = weighted[0].T @ stacked[0] + weighted[1].T @ stacked[1] + weighted[2].T @ stacked[2]
    matrix = np.zeros((nodal_count, 3, nodal_count, 3))
    for first in range(3):
        for second in range(3):
            block = weighted[second].T @ stacked[first] + (lame_ratio - 1.0) * (
                weighted[first].T @ stacked[second]
            )
            if first == second:
                block = block + laplace
            matrix[:, first, :, second] = block
    matrix = matrix.reshape(3 * nodal_count, 3 * nodal_count)
    vector = 1.5 + np.cos(1.3 * np.arange(3 * nodal_count))
    for repeat in range(200):
        vector = matrix @ vector
        vector = vector / np.sqrt(vector @ vector)
    largest = vector @ (matrix @ vector)
    return (forward, backward, float(4.0 * modulus_top * 1.1 * largest))


def row_nodes():
    nodes = []
    for entry in ELEMENT_ROWS:
        slot = SLOTS[entry[0]] if entry else None
        if slot is None or any(s and n for s, n in zip(entry[1], slot)):
            nodes.append(None)
        else:
            a, b, c = (3 * s + n for s, n in zip(entry[1], slot))
            nodes.append(16 * a + 4 * b + c)
    return nodes


def halves(matrix):
    whole = np.asarray(matrix, np.float32)
    high = whole.astype(jnp.bfloat16)
    low = (whole - high.astype(np.float32)).astype(jnp.bfloat16)
    return high, low


def element_tables():
    forward, backward, bound = build_tables([0.0, inner_anchors[0], inner_anchors[1], 1.0], 4)
    spread = np.zeros((forward.shape[0], DEPTH))
    collect = np.zeros((ROWS, backward.shape[1]))
    for row, node in enumerate(row_nodes()):
        if node is not None:
            spread[:, row] = forward[:, node]
            collect[row, :] = backward[node, :]
    spread_high, spread_low = halves(spread)
    collect_high, collect_low = halves(collect)
    return (
        np.concatenate([spread_high, spread_high, spread_low], 1),
        np.concatenate([collect_high, collect_low], 0),
        bound,
    )


def transfer_table():
    table = np.zeros((8, 32))
    reach = (0.0, inner_anchors[0], inner_anchors[1])
    for row, corner in enumerate(CORNERS):
        for column, slot in enumerate(SLOTS):
            if slot is not None:
                weight = 1.0
                for side, node in zip(corner, slot):
                    weight = weight * (reach[node] if side else 1.0 - reach[node])
                table[row, column] = weight
    back = table.T.copy()
    back[TWIN] = back[0]
    return table.T.astype(np.float32), back.astype(np.float32)


def chebyshev_steps():
    steps = [(0.0, 1.0 / interval_centre)]
    ratio_now = 1.0 / interval_ratio
    for sweep in range(1, CHEB):
        ratio_next = 1.0 / (2.0 * interval_ratio - ratio_now)
        steps.append((ratio_next * ratio_now, 2.0 * ratio_next / interval_radius))
        ratio_now = ratio_next
    return steps


def stack_row(field, component, layer, b):
    return field * 54 + component * 18 + layer * 3 + b


def block_column(component, slot):
    return 72 + 4 * component + slot - 28 if slot >= 24 else 24 * component + slot


def pack_table():
    table = np.zeros((3, 128, 2, 2, 128), np.float32)
    for field in range(2):
        for x in range(2):
            for component in range(3):
                for column, slot in enumerate(SLOTS):
                    if slot is not None:
                        a, b, c = slot
                        row = stack_row(field, component, 3 * x + a, b)
                        table[c, row, field, x, block_column(component, column)] = 1.0
                        if field == 0 and column in NEXT_SLOTS:
                            at = BLOCK + 12 * component + NEXT_SLOTS.index(column)
                            table[c, row, 1, x, at] = 1.0
            table[0, 108 + x, 0, x, TWIN] = 1.0
    return table.reshape(384, 512).astype(jnp.bfloat16)


def unpack_table():
    table = np.zeros((2, 128, 4, 128), np.float32)
    for x in range(2):
        for component in range(3):
            for column, slot in enumerate(SLOTS):
                if slot is not None:
                    a, b, c = slot
                    row = stack_row(0, component, 3 * x + a, b)
                    table[x, component * 32 + column, c, row] = 1.0
                    if column < 5:
                        table[x, 96 + 8 * component + column, 3, row] = 1.0
                    if column == 0:
                        table[x, 96 + 8 * component + TWIN, 3, row] = 1.0
                    if 16 <= column < 20:
                        table[x, component * 32 + column + 8, 3, row] = 1.0
            table[x, 120 + component, 0, 54 + 2 * component + x] = 1.0
    return table.reshape(256, 512).astype(jnp.bfloat16)


def pick(values, table):
    count = values.shape[0]
    parts = jnp.dot(
        jnp.concatenate(high_low(values), 0), table, preferred_element_type=jnp.float32
    )
    return parts[:count] + parts[count:]


def ring_order(rows_of, columns_of):
    if (rows_of, columns_of) != (4, 8):
        return list(range(rows_of * columns_of))
    order = []
    for z in range(4):
        for x in range(2):
            for y in range(2):
                chip = (z, 7 - z, 15 - z, 8 + z)[2 * x + y]
                order += [2 * chip, 2 * chip + 1]
    return order


def pack_kernel(
    order,
    initial_at, forcing_at, modulus_at, listing_at, table_at, out,
    initial, forcing, modulus, listing, table, rows, turned, places, ready,
):
    own_layers = EZ // len(order)
    sources = (listing_at, modulus_at, initial_at, forcing_at, table_at)
    copies = [
        pltpu.make_async_copy(source, here, ready.at[n])
        for n, (source, here) in enumerate(
            zip(sources, (listing, modulus, initial, forcing, table))
        )
    ]
    for copy in copies:
        copy.start()
    rows[108:128, :] = jnp.zeros((20, 384), jnp.float32)
    copies[0].wait()
    copies[1].wait()
    listed = listing[0].astype(jnp.float32)
    listed = jnp.concatenate([listed, jnp.full((1, 64), 256.0, jnp.float32)], 1)
    listed = jnp.broadcast_to(listed, (128, 256)).T
    lanes = lax.broadcasted_iota(jnp.int32, (256, 128), 1).astype(jnp.float32)
    row_at = lax.broadcasted_iota(jnp.int32, (128, 128), 0)
    stiff = jnp.zeros((128, 128), jnp.float32)
    for x in range(2):
        hit = jnp.max(jnp.where(listed == lanes + 128.0 * x, 1.0, 0.0), axis=0, keepdims=True)
        stiff = jnp.where(row_at == 108 + x, hit * modulus[x], stiff)
    copies[2].wait()
    copies[3].wait()
    for field, source in enumerate((initial, forcing)):
        for component in range(3):
            for layer in range(6):
                at = stack_row(field, component, layer, 0)
                rows[at : at + 3, :] = source[component, layer]
    for part in range(3):
        span = slice(128 * part, 128 * part + 128)
        turned[span, :] = rows[:, span].T
    picked = [turned[pl.ds(c, 128, stride=3), :] for c in range(3)]
    picked[0] = picked[0] + stiff.T
    copies[4].wait()
    wide = pick(jnp.concatenate(picked, 1), table[...])
    lane = lax.broadcasted_iota(jnp.int32, (128, 128), 1)
    for x in range(2):
        tiles = [None] * (SENT // 128)
        for n in range(4):
            pair, field = n // 2, n % 2
            moved = wide[:, 128 * (2 * field + x) : 128 * (2 * field + x) + 128]
            first = BLOCK * n
            if pair:
                moved = pltpu.roll(moved, 128 - 2 * pair, 0)
            if first % 128:
                moved = pltpu.roll(moved, first % 128, 1)
            for tile in range(first // 128, (first + BLOCK - 1) // 128 + 1):
                before = tiles[tile]
                if before is None:
                    tiles[tile] = moved
                else:
                    tiles[tile] = jnp.where(lane >= first - 128 * tile, moved, before)
        above = wide[:, 128 * (2 + x) : 128 * (2 + x) + 128]
        above = pltpu.roll(pltpu.roll(above, 128 - own_layers, 0), (NEXT_COLUMN - BLOCK) % 128, 1)
        tiles[-1] = jnp.where(lane >= NEXT_COLUMN % 128, above, tiles[-1])
        for tile in range(SENT // 128):
            places[3 * x + tile, 0:128, :] = tiles[tile]
            places[3 * x + tile, 128:136, :] = jnp.zeros((8, 128), jnp.float32)
    for device, k in enumerate(order):
        for tile in range(SENT // 128):
            for x in range(2):
                at = 12 * device + 4 * tile + 2 * x
                out[at : at + 2, :] = places[
                    3 * x + tile, own_layers * k : own_layers * k + 2, :
                ]


def unpack_kernel(order, arrived, table, out, coarse_out, layers, turned):
    devices = arrived.shape[0]
    own_layers = EZ // devices
    for x in range(2):
        for layer in range(own_layers):
            row = (layer // 2) * 4 + x * 2 + layer % 2
            if order == sorted(order):
                layers[x, pl.ds(layer, devices, stride=own_layers), :] = arrived[:, row, :]
                continue
            for device, k in enumerate(order):
                at = own_layers * k + layer
                layers[x, at : at + 1, :] = arrived[device, row : row + 1, :]
    wide = pick(jnp.concatenate([layers[0], layers[1]], 1), table[...])
    shares = pltpu.roll(wide[:, 384:512], own_layers, 0)
    turned[pl.ds(0, 128, stride=3), :] = wide[:, 0:128] + shares
    for c in range(1, 3):
        turned[pl.ds(c, 128, stride=3), :] = wide[:, 128 * c : 128 * c + 128]
    for part in range(3):
        span = slice(128 * part, 128 * part + 128)
        back = turned[span, :].T
        for component in range(3):
            for layer in range(6):
                at = stack_row(0, component, layer, 0)
                out[component, layer, :, span] = back[at : at + 3, :]
    back = wide[:, 0:128].T
    for component in range(3):
        for x in range(2):
            at = 54 + 2 * component + x
            coarse_out[component, x] = back[at : at + 1, :]


def cofactor_rows(deform):
    return [
        [
            deform[(row_at + 1) % 3][(column + 1) % 3] * deform[(row_at + 2) % 3][(column + 2) % 3]
            - deform[(row_at + 1) % 3][(column + 2) % 3]
            * deform[(row_at + 2) % 3][(column + 1) % 3]
            for column in range(3)
        ]
        for row_at in range(3)
    ]


def point_stress(deform, stiffness, stiffness_four):
    cofactors = cofactor_rows(deform)
    jacobian = (
        deform[0][0] * cofactors[0][0]
        + deform[0][1] * cofactors[0][1]
        + deform[0][2] * cofactors[0][2]
    )
    pressure = stiffness_four * (jacobian - rest_ratio)
    return [
        [stiffness * deform[i][d] + pressure * cofactors[i][d] for d in range(3)] for i in range(3)
    ]


coarse_samples = [0.5 - 0.5 / math.sqrt(3.0), 0.5 + 0.5 / math.sqrt(3.0)]
two = range(2)


def at_points(low, high):
    change = high - low
    return [low + s * change for s in coarse_samples], change * (1.0 / element_span)


def ends_of(first, second):
    high = coarse_samples[0] * first + coarse_samples[1] * second
    return [first + second - high, high]


def high_low(values):
    high = values.astype(jnp.bfloat16)
    return high, (values - high.astype(jnp.float32)).astype(jnp.bfloat16)


def reads(pairs):
    return set(range(pairs[0], pairs[-1] + 2))


def plan_steps(spans):
    plan = []
    for first, count in spans:
        pairs = list(range(first, first + count))
        plan.append([pairs[n : n + 2] for n in range(0, count, 2)])
    for now, later in zip(plan, plan[1:]):
        if reads(later[0]) & set(now[-1]) and len(now[-1]) == 2:
            now[-1:] = [now[-1][:1], now[-1][1:]]
        if reads(later[0]) & set(now[-1]) and len(later[0]) == 2:
            later[:1] = [later[0][:1], later[0][1:]]
    return plan


class Slab:
    def __init__(self, width, across):
        self.width = width
        self.y_step = 2 * across
        lane = lax.broadcasted_iota(jnp.int32, (8, width), 1)
        x = (lane // 2) % across
        self.bottom, self.top, self.even = x == 0, x == across - 1, lane % 2 == 0
        self.row = lax.broadcasted_iota(jnp.int32, (8, width), 0)
        row = lax.broadcasted_iota(jnp.int32, (32, width), 0)
        lane = lax.broadcasted_iota(jnp.int32, (32, width), 1)
        on_face = (row == 0) | ((row >= 3) & (row <= 11))
        self.keep = jnp.where(on_face & ((lane // 2) % across == 0), 0.0, 1.0)

    def lanes(self, v, step):
        return pltpu.roll(v, step % self.width, 1)

    def from_next(self, v, x, y):
        if x or y:
            v = self.lanes(v, -2 * x - self.y_step * y)
        return jnp.where(self.top, 0.0, v) if x else v

    def from_next_z(self, v, ahead, x, y):
        step = -2 * x - self.y_step * y
        v = jnp.where(self.even, self.lanes(v, step - 1), self.lanes(ahead, step + 1))
        return jnp.where(self.top, 0.0, v) if x else v

    def onto_next(self, v, x, y, z=0):
        if x or y or z:
            v = self.lanes(v, 2 * x + self.y_step * y + z)
        return jnp.where(self.bottom, 0.0, v) if x else v

    def gather(self, here, ahead):
        row = self.row
        g0, g1, g2, g3 = here[0:8], here[8:16], here[16:24], here[24:32]
        a0 = ahead[0:8]
        z0, xz = self.from_next_z(g0, a0, 0, 0), self.from_next_z(g0, a0, 1, 0)
        yz, xyz = self.from_next_z(g0, a0, 0, 1), self.from_next_z(g0, a0, 1, 1)
        z2 = self.from_next_z(g2, ahead[16:24], 0, 0)
        edges = jnp.where(row <= 4, xz, self.from_next(g0, 1, 1))
        edges = jnp.where(row == 0, xyz, jnp.where(row <= 2, yz, edges))
        return jnp.concatenate(
            [
                g0,
                g1,
                g2,
                jnp.where(row < 4, z2, g3),
                self.from_next(g0, 1, 0),
                jnp.where(row == 7, yz, self.from_next(g0, 0, 1)),
                jnp.where(row == 7, xz, z0),
                jnp.where(row < 4, self.from_next(g1, 1, 0), self.from_next(g1, 0, 1)),
                edges,
                jnp.zeros_like(g0),
            ],
            0,
        )

    def scatter(self, part, behind):
        row = self.row
        g0, g1, g2, g3, x0, y0, z0, sides, edges = (part[8 * n : 8 * n + 8] for n in range(9))
        last = row == 7
        for_z = jnp.where(last, 0.0, z0)
        for_xz = jnp.where(last, z0, jnp.where((row == 3) | (row == 4), edges, 0.0))
        for_yz = jnp.where(last, y0, jnp.where((row == 1) | (row == 2), edges, 0.0))
        for_xyz = jnp.where(row == 0, edges, 0.0)
        for_xy = jnp.where(row >= 5, edges, 0.0)

        def above(z):
            return (
                self.onto_next(for_z, 0, 0, z)
                + self.onto_next(for_yz, 0, 1, z)
                + self.onto_next(for_xz, 1, 0, z)
                + self.onto_next(for_xyz, 1, 1, z)
            )

        own0 = g0 + self.onto_next(x0, 1, 0) + self.onto_next(jnp.where(last, 0.0, y0), 0, 1)
        own0 = own0 + self.onto_next(for_xy, 1, 1)
        own0 = own0 + jnp.where(self.even, behind[0], above(1))
        own1 = g1 + jnp.where(row < 4, self.onto_next(sides, 1, 0), self.onto_next(sides, 0, 1))
        share2 = jnp.where(self.even, behind[1], self.onto_next(g3, 0, 0, 1))
        own2 = g2 + jnp.where(row < 4, share2, 0.0)
        own3 = jnp.where(row < 4, 0.0, g3)
        moved = (above(-1), self.onto_next(g3, 0, 0, -1))
        return jnp.concatenate([self.twinned(own0), own1, own2, own3], 0), moved

    def twinned(self, v):
        twins = jnp.where(self.row == 7, pltpu.roll(v, 7, 0), 0.0)
        return v + jnp.where(self.row == 0, pltpu.roll(v, 1, 0), twins)

    def absorb(self, total, behind):
        low = self.twinned(jnp.where(self.even, behind[0], 0.0))
        high = jnp.where(self.even & (self.row < 4), behind[1], 0.0)
        return jnp.concatenate(
            [total[0:8] + low, total[8:16], total[16:24] + high, total[24:32]], 0
        )

    def gradient(self, u, spread, pairs):
        blocks = [self.gather(u[i, pair], u[i, pair + 1]) for i in range(3) for pair in pairs]
        high, low = high_low(jnp.concatenate(blocks, 1))
        return jnp.dot(
            spread[...],
            jnp.concatenate([high, low, high], 0),
            preferred_element_type=jnp.float32,
        )

    def force(self, gradient, stiff, collect, pairs):
        width = len(pairs) * self.width
        stiffness = jnp.concatenate([stiff[pair : pair + 1, :] for pair in pairs], 1)
        deform = [
            [
                gradient[64 * e : 64 * e + 64, width * i : width * (i + 1)]
                + (1.0 if i == e else 0.0)
                for e in range(3)
            ]
            for i in range(3)
        ]
        stress = point_stress(deform, stiffness, lame_ratio * stiffness)
        stress = jnp.concatenate(
            [jnp.concatenate([stress[i][e] for i in range(3)], 1) for e in range(3)], 0
        )
        high, low = high_low(stress)
        force = jnp.dot(collect[...], high, preferred_element_type=jnp.float32)
        return force[0:ROWS] + (
            force[ROWS:] + jnp.dot(collect[0:ROWS], low, preferred_element_type=jnp.float32)
        )

    def run(self, u, stiff, spread, collect, jobs, given=None):
        plan = plan_steps([job[:2] for job in jobs])
        steps = [(pairs, n) for n, chunks in enumerate(plan) for pairs in chunks]
        none = jnp.zeros((8, self.width), jnp.float32)
        ahead, carry, job = None, None, None
        for at, (pairs, n) in enumerate(steps):
            ready = given is not None and n == 0 and pairs == given[0]
            gradient = ahead
            if ahead is None and not ready:
                gradient = self.gradient(u, spread, pairs)
            if not ready:
                ahead = None
            if ahead is None and at + 1 < len(steps):
                later, later_job = steps[at + 1]
                if given is not None and later_job == 0 and later == given[0]:
                    later, later_job = steps[at + 2]
                if later_job == n or not reads(later) & set(pairs):
                    ahead = self.gradient(u, spread, later)
            if job != n:
                carry, job = [(none, none) for i in range(3)], n
            if ready:
                for q, pair in enumerate(pairs):
                    total = given[1][q]
                    if q == 0:
                        total = [self.absorb(total[i], carry[i]) for i in range(3)]
                    jobs[n][2](pair, total)
                carry = list(given[2])
                continue
            force = self.force(gradient, stiff, collect, pairs)
            totals = [[] for pair in pairs]
            for q in range(len(pairs)):
                for i in range(3):
                    lane = (len(pairs) * i + q) * self.width
                    total, carry[i] = self.scatter(force[:, lane : lane + self.width], carry[i])
                    totals[q].append(total)
            for pair, total in zip(pairs, totals):
                jobs[n][2](pair, total)
        return carry

    def smoothing(self, u, f, f_shift, d, spans, bound):
        jobs = []
        for (first, count), (held, added) in zip(spans, chebyshev_steps()):

            def finish(pair, forces, held=held, added=added):
                for i in range(3):
                    z = (added / bound) * self.keep * (f[i, pair + f_shift] - forces[i])
                    move = held * d[i, pair] + z if held else z
                    d[i, pair] = move
                    u[i, pair] = u[i, pair] + move

            jobs.append((first, count, finish))
        return jobs

    def owed(self, carry, bound):
        scale = -chebyshev_steps()[-1][1] / bound
        return [
            (
                scale * jnp.where(self.even, low, 0.0) * self.keep[0:8],
                scale * jnp.where(self.even, high, 0.0) * self.keep[16:24],
            )
            for low, high in carry
        ]

    def corners_of(self, v):
        ahead = pltpu.roll(v, 7, 0)
        found = {}
        for a in range(2):
            for b in range(2):
                found[a, b, 0] = self.from_next(v, a, b)
                found[a, b, 1] = self.from_next_z(v, ahead, a, b)
        return found

    def assemble(self, part):
        here, odd, even = 0.0, 0.0, 0.0
        for a in range(2):
            for b in range(2):
                here = here + self.onto_next(part[a, b, 0], a, b)
                odd = odd + self.onto_next(part[a, b, 1], a, b, 1)
                even = even + self.onto_next(part[a, b, 1], a, b, -1)
        return here + jnp.where(self.even, pltpu.roll(even, 1, 0), odd)

    def coarse_force(self, values, stiffness):
        grads = []
        for i in range(3):
            v = self.corners_of(values[i])
            vz, sz = {}, {}
            for a in two:
                for b in two:
                    vz[a, b], sz[a, b] = at_points(v[a, b, 0], v[a, b, 1])
            vv, vs, sv = {}, {}, {}
            for a in two:
                for k in two:
                    vv[a, k], vs[a, k] = at_points(vz[a, 0][k], vz[a, 1][k])
                sv[a], unused = at_points(sz[a, 0], sz[a, 1])
            dx, dy, dz = {}, {}, {}
            for k in two:
                for j in two:
                    dx[j, k] = (vv[1, k][j] - vv[0, k][j]) * (1.0 / element_span)
                line, unused = at_points(vs[0, k], vs[1, k])
                for h in two:
                    dy[h, k] = line[h]
            for j in two:
                line, unused = at_points(sv[0][j], sv[1][j])
                for h in two:
                    dz[h, j] = line[h]
            grads.append((dx, dy, dz))
        weight = element_span**2 / 8.0
        scaled = weight * stiffness
        scaled_four = lame_ratio * scaled
        sums = [({}, {}, {}) for i in range(3)]

        def add(table, key, value):
            table[key] = table[key] + value if key in table else value

        for h in two:
            for j in two:
                for k in two:
                    deform = [
                        [grads[i][0][j, k], grads[i][1][h, k], grads[i][2][h, j]]
                        for i in range(3)
                    ]
                    for i in range(3):
                        deform[i][i] = deform[i][i] + 1.0
                    stress = point_stress(deform, scaled, scaled_four)
                    for i in range(3):
                        add(sums[i][0], (j, k), stress[i][0])
                        add(sums[i][1], (h, k), stress[i][1])
                        add(sums[i][2], (h, j), stress[i][2])

        forces = []
        for i in range(3):
            part = {}
            qx, qy, qz = sums[i]
            along_z = [ends_of(qx[j, 0], qx[j, 1]) for j in two]
            for c in two:
                line = ends_of(along_z[0][c], along_z[1][c])
                for b in two:
                    part[0, b, c] = -line[b]
                    part[1, b, c] = line[b]
            along_z = [ends_of(qy[h, 0], qy[h, 1]) for h in two]
            for c in two:
                line = ends_of(along_z[0][c], along_z[1][c])
                for a in two:
                    part[a, 0, c] = part[a, 0, c] - line[a]
                    part[a, 1, c] = part[a, 1, c] + line[a]
            along_y = [ends_of(qz[h, 0], qz[h, 1]) for h in two]
            for b in two:
                line = ends_of(along_y[0][b], along_y[1][b])
                for a in two:
                    part[a, b, 0] = part[a, b, 0] - line[a]
                    part[a, b, 1] = part[a, b, 1] + line[a]
            forces.append(self.assemble(part))
        return forces


def window_pair(slab, first_layer, own_layers, fetch):
    found = []
    for parity in range(2):
        layer = first_layer + parity
        device = layer // own_layers
        layer = layer - device * own_layers
        found.append((device, layer // 2, layer % 2))
    values = [fetch(device, q) for device, q, parity in found]
    if found[0][:2] == found[1][:2] or (values[0] is None and values[1] is None):
        return values[0]
    for parity in range(2):
        if values[parity] is None:
            values[parity] = jnp.zeros_like(values[1 - parity])
        elif found[parity][2] != parity:
            values[parity] = slab.lanes(values[parity], 2 * parity - 1)
    lane = lax.broadcasted_iota(jnp.int32, values[0].shape, 1)
    return jnp.where(lane % 2 == 0, values[0], values[1])


def first_sources(own_layers):
    return list(range(-BEFORE // own_layers, (own_layers + BEFORE - 1) // own_layers + 1))


def whole_pairs(own_layers):
    return own_layers == 4


def turn_rows(block, mixed, turned, width, at):
    for tile in range(SENT // 128):
        n = at * (SENT // 128) + tile
        for m in range(width // 4):
            first = 12 * m + 4 * tile
            mixed[n, 4 * m : 4 * m + 4, :] = block[first : first + 4, :]
        turned[at, 128 * tile : 128 * tile + 128, :] = mixed[n].T


def regroup(slab, field, rows):
    values, hard = [], None
    for i in range(3):
        parts = [rows(24 * i + 8 * n) for n in range(3)]
        if field == 0 and i == 0:
            hard = parts[0][TWIN : TWIN + 1]
        parts[0] = jnp.where(slab.row == TWIN, pltpu.roll(parts[0], TWIN, 0), parts[0])
        parts.append(jnp.where(slab.row < 4, 0.0, rows(68 + 4 * i)))
        whole = jnp.concatenate(parts, 0)
        values.append(whole * slab.keep if field == 0 else whole)
    return values, hard


def layer_above(slab, turned, at, i):
    first = NEXT_COLUMN + 12 * i
    low, high = turned[at, first : first + 8, :], turned[at, first + 4 : first + 12, :]
    high = jnp.where(slab.row < 4, pltpu.roll(high, 4, 0), 0.0)
    low = jnp.where(slab.row == TWIN, pltpu.roll(low, TWIN, 0), low)
    nothing = jnp.zeros_like(low)
    return jnp.concatenate([low, nothing, high, nothing], 0) * slab.keep


def make_own_kernel(width, across, own_layers):
    own_pairs = own_layers // 2
    pairs = list(range(own_pairs))

    def own_kernel(block, spread, collect, u, f, stiff, forces, moved, mixed, turned):
        slab = Slab(width, across)
        turn_rows(block, mixed, turned, width, 0)
        for pair in pairs:
            for field, target in enumerate((u, f)):

                def rows(start, field=field, pair=pair):
                    at = BLOCK * (2 * pair + field) + start
                    return turned[0, at : at + 8, :]

                values, hard = regroup(slab, field, rows)
                for i in range(3):
                    target[i, pair] = values[i]
                if field == 0:
                    stiff[pair : pair + 1, :] = hard
        for i in range(3):
            u[i, own_pairs] = layer_above(slab, turned, 0, i)

        def finish(pair, total):
            for i in range(3):
                forces[i, pair] = total[i]

        carry = slab.run(u, stiff, spread, collect, [(0, own_pairs, finish)])
        for i in range(3):
            moved[i, 0] = carry[i][0]
            moved[i, 1] = carry[i][1]

    return own_kernel


def make_first_kernel(width, across, own_layers, fine_bound):
    own = BEFORE // 2
    own_pairs = (own_layers + 1) // 2
    spans = []
    prepared = whole_pairs(own_layers)
    for n in (4, 3, 2, 1):
        low, high = BEFORE - n, BEFORE + own_layers + n - 1 + prepared
        spans.append((low // 2, (high + 1) // 2 - low // 2))
    sources = [n for n in first_sources(own_layers) if n or not prepared]

    def first_kernel(*refs):
        arrived = refs[: len(sources)]
        refs = refs[len(sources) :]
        if prepared:
            own_u, own_f, own_stiff, own_forces, own_moved = refs[:5]
            refs = refs[5:]
        spread, collect, transfer, message, *sent, f, u, d, stiff, shares, mixed, turned = refs
        slab = Slab(width, across)
        u[...] = jnp.zeros(u.shape, jnp.float32)
        if not prepared:
            f[...] = jnp.zeros(f.shape, jnp.float32)
        shares[...] = jnp.zeros(shares.shape, jnp.float32)
        stiff[...] = jnp.zeros(stiff.shape, jnp.float32)
        for n in range(len(sources)):
            turn_rows(arrived[n], mixed, turned, width, n)
        for pair in range(PAIRS):
            if prepared and own <= pair < own + own_pairs:
                for i in range(3):
                    u[i, pair] = own_u[i, pair - own]
                    f[i, pair] = own_f[i, pair - own]
                stiff[pair : pair + 1, :] = own_stiff[pair - own : pair - own + 1, :]
                continue
            for field, target in enumerate((u, f)):

                def rows(start, field=field, pair=pair):
                    def fetch(device, q):
                        if device not in sources:
                            return None
                        at = BLOCK * (2 * q + field) + start
                        return turned[sources.index(device), at : at + 8, :]

                    value = window_pair(slab, 2 * pair - BEFORE, own_layers, fetch)
                    return jnp.zeros((8, width), jnp.float32) if value is None else value

                values, hard = regroup(slab, field, rows)
                for i in range(3):
                    target[i, pair] = values[i]
                if field == 0:
                    stiff[pair : pair + 1, :] = hard
        given = None
        if prepared:
            for i in range(3):
                u[i, PAIRS] = layer_above(slab, turned, sources.index(1), i)
            given = (
                list(range(own, own + own_pairs)),
                [[own_forces[i, q] for i in range(3)] for q in range(own_pairs)],
                [(own_moved[i, 0], own_moved[i, 1]) for i in range(3)],
            )

        weights = [jnp.broadcast_to(transfer[:, n : n + 1], (32, width)) for n in range(8)]

        def restrict(pair, forces):
            for i in range(3):
                rest = slab.keep * (f[i, pair] - forces[i])
                for n in range(8):
                    part = rest * weights[n]
                    part = (part[0:8] + part[8:16]) + (part[16:24] + part[24:32])
                    shares[i, n, pl.ds(pair, 1), :] = jnp.sum(part, axis=0, keepdims=True)

        jobs = slab.smoothing(u, f, 0, d, spans[0:3], fine_bound)
        slab.run(u, stiff, spread, collect, jobs + [(*spans[3], restrict)], given)

        restricted = [
            slab.assemble({corner: shares[i, n] for n, corner in enumerate(CORNERS)})
            for i in range(3)
        ]
        def line(rows, q):
            return rows[own + q : own + q + 1]

        for q in range(own_pairs):
            for i in range(3):
                message[i, q] = u[i, own + q]
                message[i, q, RESTRICTED_SLOT : RESTRICTED_SLOT + 1, :] = line(restricted[i], q)
            message[0, q, STIFF_SLOT : STIFF_SLOT + 1, :] = line(stiff, q)
        if prepared:
            down, up = sent
            for i in range(3):
                down[i, 0:32] = u[i, own]
                down[i, 32:40] = u[i, own + 1, 0:8, :]
                down[i, 40:48] = u[i, own + 1, 16:24, :]
                up[i] = u[i, own + 1]
                for n, row in enumerate(
                    (line(restricted[i], 0), line(restricted[i], 1), u[i, own + 2, 0:1, :])
                    + (line(restricted[i], 2),)
                ):
                    down[i, 24 + n : 25 + n, :] = row
                for n, row in enumerate(
                    (line(restricted[i], 1), line(restricted[i], 0), u[i, own, 0:1, :])
                ):
                    up[i, 24 + n : 25 + n, :] = row
            for q in range(own_pairs):
                down[q, 32 + TWIN : 33 + TWIN, :] = line(stiff, q)
                up[q, TWIN : TWIN + 1, :] = line(stiff, q)
            return
        edge = sent[0]
        for q in range(own_pairs):
            for i in range(3):
                edge[q, i : i + 1, :] = u[i, own + q, 0:1, :]
                edge[q, 3 + i : 4 + i, :] = line(restricted[i], q)
            edge[q, 6:8, :] = jnp.broadcast_to(line(stiff, q), (2, width))

    return first_kernel


def shares_sent(own_layers):
    return own_layers % 2 == 0


def sources_of(own_layers):
    below = 2 if shares_sent(own_layers) else 3
    whole = range(-below // own_layers, (own_layers + 2) // own_layers + 1)
    coarse = range(-(below + 2) // own_layers, (own_layers + 4) // own_layers + 1)
    return list(whole), [n for n in coarse if n not in whole]


def message_line(message, q, n):
    i, slot = ((n, 0), (n - 3, RESTRICTED_SLOT), (0, STIFF_SLOT))[n // 3]
    return message[i, q, slot : slot + 1, :]


def sent_readers(slab, up, message, down):
    def block_of(device, q, i):
        if device == 0:
            return message[i, q]
        if (device, q) == (1, 0):
            whole = down[i, 0:32]
        elif (device, q) == (1, 1):
            low, high = down[i, 32:40], down[i, 40:48]
            low = jnp.where(slab.row == TWIN, pltpu.roll(low, TWIN, 0), low)
            whole = jnp.concatenate([low, jnp.zeros_like(low), high, jnp.zeros_like(low)], 0)
        elif (device, q) == (-1, 1):
            low = up[i, 0:8]
            low = jnp.where(slab.row == TWIN, pltpu.roll(low, TWIN, 0), low)
            whole = jnp.concatenate([low, up[i, 8:32]], 0)
        else:
            return None
        return whole

    def line_of(device, q, n):
        if device == 0:
            return message_line(message, q, n)
        kind, i = n // 3, n % 3
        if device == 1:
            row = ((0, 24), (32, 25))[q][kind] if kind < 2 else 32 + TWIN
            i = i if kind < 2 else q
            return down[i, row : row + 1, :]
        if device == -1:
            row = ((26, 25), (0, 24))[q][kind] if kind < 2 else TWIN
            i = i if kind < 2 else q
            return up[i, row : row + 1, :]
        if (device, q) == (2, 0) and kind < 2:
            return down[i, 26 + kind : 27 + kind, :]
        return None

    return block_of, line_of


def make_second_kernel(width, across, own_layers, fine_bound, coarse_bound):
    own = BEFORE_B // 2
    own_pairs = (own_layers + 1) // 2
    shift = (BEFORE - BEFORE_B) // 2
    whole, outer = sources_of(own_layers)
    steps = chebyshev_steps()
    spans = []
    for n in (3, 2, 1):
        low, high = BEFORE_B - n + shares_sent(own_layers), BEFORE_B + own_layers + n - 1
        spans.append((low // 2, (high + 1) // 2 - low // 2))

    def second_kernel(*refs):
        slab = Slab(width, across)
        if whole_pairs(own_layers):
            up, message, down = refs[:3]
            refs = refs[3:]
            block_of, line_of = sent_readers(slab, up, message, down)
        else:
            messages = dict(zip(whole, refs))
            edges = dict(zip(outer, refs[len(whole) :]))
            refs = refs[len(whole) + len(outer) :]

            def block_of(device, q, i):
                return messages[device][i, q] if device in messages else None

            def line_of(device, q, n):
                if device in messages:
                    return message_line(messages[device], q, n)
                return edges[device][q, n : n + 1, :] if device in edges else None

        f, spread, collect, transfer_back, out, u, d, stiff, coarse = refs

        def pair_of(pair, fetch):
            return window_pair(slab, 2 * pair - BEFORE_B, own_layers, fetch)

        u[...] = jnp.zeros(u.shape, jnp.float32)
        coarse[...] = jnp.zeros(coarse.shape, jnp.float32)
        d[...] = jnp.zeros(d.shape, jnp.float32)
        for pair in range(PAIRS_B):
            for i in range(3):
                block = pair_of(pair, lambda device, q: block_of(device, q, i))
                if block is not None:
                    u[i, pair] = block
            for n in range(7):
                line = pair_of(pair, lambda device, q: line_of(device, q, n))
                if line is not None:
                    coarse[n, pair : pair + 1, :] = line
        stiff[...] = coarse[6]

        stiffness = coarse[6]
        keep_coarse = jnp.where(slab.bottom, 0.0, 1.0)
        start = [coarse[i] for i in range(3)]
        restricted = [coarse[3 + i] for i in range(3)]
        before = slab.coarse_force(start, stiffness)
        move = [(steps[0][1] / coarse_bound) * keep_coarse * restricted[i] for i in range(3)]
        level = [start[i] + move[i] for i in range(3)]
        for held, added in steps[1:]:
            force = slab.coarse_force(level, stiffness)
            for i in range(3):
                z = keep_coarse * (restricted[i] + before[i] - force[i])
                move[i] = held * move[i] + (added / coarse_bound) * z
                level[i] = level[i] + move[i]

        weights = [jnp.broadcast_to(transfer_back[:, n : n + 1], (32, width)) for n in range(8)]
        for i in range(3):
            change = slab.corners_of(level[i] - start[i])
            for pair in range(spans[0][0], min(spans[0][0] + spans[0][1] + 1, PAIRS_B)):
                lift = u[i, pair]
                for n, corner in enumerate(CORNERS):
                    lift = lift + weights[n] * change[corner][pair : pair + 1]
                u[i, pair] = lift

        jobs = slab.smoothing(u, f, shift, d, spans, fine_bound)
        owed = slab.owed(slab.run(u, stiff, spread, collect, jobs), fine_bound)

        lower = lax.broadcasted_iota(jnp.int32, (width // 8, 8, 128), 1) < 4
        nothing = jnp.zeros((8, width), jnp.float32)
        sides = []
        for q in range(2):
            if q or not shares_sent(own_layers):
                owed = [(nothing, nothing)] * 3
            rows = []
            for i in range(3):
                value = u[i, own + q]
                rows += [value[0:24], jnp.where(slab.row < 4, owed[i][1], value[24:32])]
            rows += [owed[i][0] for i in range(3)]
            rows += [level[i][own + q : own + q + 1] for i in range(3)] + [nothing[0:5]]
            sides.append(jnp.concatenate(rows, 0).T.reshape(width // 8, 8, 128))
        out[:, 0] = jnp.where(lower, sides[0], pltpu.roll(sides[1], 4, 1))
        out[:, 1] = jnp.where(lower, pltpu.roll(sides[0], 4, 1), sides[1])

    return second_kernel


def solution(mesh):
    rows_of, columns_of = mesh.shape["gx"], mesh.shape["gy"]
    devices = rows_of * columns_of
    order = ring_order(rows_of, columns_of)
    own_layers = EZ // devices
    own_pairs = (own_layers + 1) // 2
    width = 4 * devices
    across = 2 * rows_of
    near = first_sources(own_layers)
    prepared = whole_pairs(own_layers)
    whole, outer = sources_of(own_layers)
    spread, collect, fine_bound = element_tables()
    coarse_bound = build_tables([0.0, 1.0], 2)[2]
    transfer, transfer_back = transfer_table()
    wide = pltpu.CompilerParams(vmem_limit_bytes=60 * 1024 * 1024)
    limit = pltpu.CompilerParams(vmem_limit_bytes=48 * 1024 * 1024)
    f32 = jnp.float32

    pack = pl.pallas_call(
        functools.partial(pack_kernel, order),
        out_shape=jax.ShapeDtypeStruct((devices * 12, 128), f32),
        in_specs=[pl.BlockSpec(memory_space=pl.ANY)] * 5,
        out_specs=pl.BlockSpec(memory_space=pltpu.VMEM),
        scratch_shapes=[
            pltpu.VMEM((3, 6, 3, 384), f32),
            pltpu.VMEM((3, 6, 3, 384), f32),
            pltpu.VMEM((2, 1, EZ), f32),
            pltpu.VMEM((1, 1, 192), jnp.int32),
            pltpu.VMEM((384, 512), jnp.bfloat16),
            pltpu.VMEM((128, 384), f32),
            pltpu.VMEM((384, 128), f32),
            pltpu.VMEM((6, 136, 128), f32),
            pltpu.SemaphoreType.DMA((5,)),
        ],
        compiler_params=wide,
    )
    own = pl.pallas_call(
        make_own_kernel(width, across, own_layers),
        out_shape=(
            jax.ShapeDtypeStruct((3, own_pairs + 1, 32, width), f32),
            jax.ShapeDtypeStruct((3, own_pairs, 32, width), f32),
            jax.ShapeDtypeStruct((own_pairs, width), f32),
            jax.ShapeDtypeStruct((3, own_pairs, 32, width), f32),
            jax.ShapeDtypeStruct((3, 2, 8, width), f32),
        ),
        scratch_shapes=[
            pltpu.VMEM((SENT // 128, width, 128), f32),
            pltpu.VMEM((1, SENT, width), f32),
        ],
        compiler_params=limit,
        cost_estimate=pl.CostEstimate(flops=400_000_000, bytes_accessed=1_000_000, transcendentals=0),
    )
    sent = [jax.ShapeDtypeStruct((own_pairs, 8, width), f32)]
    if prepared:
        sent = [jax.ShapeDtypeStruct((3, rows, width), f32) for rows in (48, 32)]
    first = pl.pallas_call(
        make_first_kernel(width, across, own_layers, fine_bound),
        out_shape=(
            jax.ShapeDtypeStruct((3, own_pairs, 32, width), f32),
            *sent,
            jax.ShapeDtypeStruct((3, PAIRS, 32, width), f32),
        ),
        scratch_shapes=[
            pltpu.VMEM((3, 8, 32, width), f32),
            pltpu.VMEM((3, 8, 32, width), f32),
            pltpu.VMEM((8, width), f32),
            pltpu.VMEM((3, 8, 8, width), f32),
            pltpu.VMEM((len(near) * (SENT // 128), width, 128), f32),
            pltpu.VMEM((len(near), SENT, width), f32),
        ],
        compiler_params=limit,
    )
    second = pl.pallas_call(
        make_second_kernel(width, across, own_layers, fine_bound, coarse_bound),
        out_shape=jax.ShapeDtypeStruct((devices // 2, 2, 8, 128), f32),
        scratch_shapes=[
            pltpu.VMEM((3, PAIRS_B + 2, 32, width), f32),
            pltpu.VMEM((3, PAIRS_B, 32, width), f32),
            pltpu.VMEM((PAIRS_B, width), f32),
            pltpu.VMEM((7, PAIRS_B, width), f32),
        ],
        compiler_params=limit,
    )
    unpack = pl.pallas_call(
        functools.partial(unpack_kernel, order),
        out_shape=(
            jax.ShapeDtypeStruct((3, 6, 3, 384), f32),
            jax.ShapeDtypeStruct((3, 2, 1, EZ), f32),
        ),
        scratch_shapes=[pltpu.VMEM((2, 128, 128), f32), pltpu.VMEM((384, 128), f32)],
        compiler_params=limit,
    )
    everyone = ("gy", "gx")

    def from_device(block, distance):
        place = {k: m % rows_of * columns_of + m // rows_of for m, k in enumerate(order)}
        route = [(place[(k + distance) % devices], place[k]) for k in range(devices)]
        return lax.ppermute(block, ("gx", "gy"), route)

    def body(initial, forcing, modulus, solid_list):
        sent = pack(initial, forcing, modulus, solid_list, jnp.asarray(pack_table()))
        sent = sent.reshape(devices, SENT // 128, 4, 128)
        arrived = lax.all_to_all(sent, everyone, 0, 0, tiled=True).reshape(devices * 12, 128)
        blocks = [from_device(arrived, n) if n else arrived for n in near]
        if prepared:
            blocks = [block for n, block in zip(near, blocks) if n]
            blocks += own(arrived, jnp.asarray(spread), jnp.asarray(collect))
        message, *edges, load = first(
            *blocks,
            jnp.asarray(spread),
            jnp.asarray(collect),
            jnp.asarray(transfer),
        )
        if prepared:
            down, up = edges
            messages = [from_device(up, -1), message, from_device(down, 1)]
        else:
            messages = [from_device(message, n) if n else message for n in whole]
            messages += [from_device(edges[0], n) for n in outer]
        result = second(
            *messages,
            load,
            jnp.asarray(spread),
            jnp.asarray(collect),
            jnp.asarray(transfer_back),
        )
        back = lax.all_to_all(result.reshape(devices, 8, 128), everyone, 0, 0, tiled=True)
        return unpack(back, jnp.asarray(unpack_table()))

    placed = (
        P(None, "gx", "gy", None),
        P(None, "gx", "gy", None),
        P("gx", "gy", None),
        P("gx", "gy", None),
    )
    return jax.shard_map(
        body,
        mesh=mesh,
        in_specs=placed,
        out_specs=(P(None, "gx", "gy", None), P(None, "gx", "gy", None)),
        check_vma=False,
    )
```

```python
import functools
import math

import jax
import jax.numpy as jnp
import numpy as np
from jax import lax
from jax.experimental import pallas as pl
from jax.experimental.pallas import tpu as pltpu
from jax.sharding import PartitionSpec as P

CHEB = 3
EZ = 128

element_span = 20.0
lame_ratio = 4.0
rest_ratio = 1.25
modulus_top = 2.0
spectrum_floor = 0.05
interval_centre = (1.0 + spectrum_floor) / 2.0
interval_radius = (1.0 - spectrum_floor) / 2.0
interval_ratio = interval_centre / interval_radius
inner_anchors = (0.5 - 0.5 / math.sqrt(5.0), 0.5 + 0.5 / math.sqrt(5.0))

BEFORE = 4
PAIRS = 6
BEFORE_B = 6
PAIRS_B = 8
BLOCK = 84
SENT = 384

SLOTS = [
    (0, 0, 0), (1, 0, 0), (2, 0, 0), (0, 1, 0), (0, 2, 0), (0, 0, 1), (0, 0, 2), None,
    (0, 1, 1), (0, 1, 2), (0, 2, 1), (0, 2, 2), (1, 0, 1), (1, 0, 2), (2, 0, 1), (2, 0, 2),
    (1, 1, 0), (1, 2, 0), (2, 1, 0), (2, 2, 0), (1, 1, 1), (1, 1, 2), (1, 2, 1), (1, 2, 2),
    None, None, None, None, (2, 1, 1), (2, 1, 2), (2, 2, 1), (2, 2, 2),
]
TWIN = 7
NEXT_SLOTS = [0, 1, 2, 3, 4, 5, 6, 7, 16, 17, 18, 19]
NEXT_COLUMN = 4 * BLOCK
RESTRICTED_SLOT = 24
STIFF_SLOT = 25
OWN_SHIFT, SHIFT_X, SHIFT_Y, SHIFT_Z = (0, 0, 0), (1, 0, 0), (0, 1, 0), (0, 0, 1)
ELEMENT_ROWS = (
    [(slot, OWN_SHIFT) for slot in range(24)]
    + [(slot, SHIFT_Z) for slot in range(16, 20)]
    + [(slot, OWN_SHIFT) for slot in range(28, 32)]
    + [(slot, SHIFT_X) for slot in range(7)] + [None]
    + [(slot, SHIFT_Y) for slot in range(7)] + [(0, (0, 1, 1))]
    + [(slot, SHIFT_Z) for slot in range(7)] + [(0, (1, 0, 1))]
    + [(slot, SHIFT_X) for slot in range(8, 12)] + [(slot, SHIFT_Y) for slot in range(12, 16)]
    + [(0, (1, 1, 1)), (1, (0, 1, 1)), (2, (0, 1, 1)), (3, (1, 0, 1)), (4, (1, 0, 1))]
    + [(5, (1, 1, 0)), (6, (1, 1, 0)), (0, (1, 1, 0))]
)
ROWS = len(ELEMENT_ROWS)
DEPTH = 80
CORNERS = [(a, b, c) for a in range(2) for b in range(2) for c in range(2)]


def gauss_rule(point_count):
    if point_count == 2:
        offset = 1.0 / math.sqrt(3.0)
        points = [-offset, offset]
        weights = [1.0, 1.0]
    else:
        inner = math.sqrt(3.0 / 7.0 - 2.0 / 7.0 * math.sqrt(6.0 / 5.0))
        outer = math.sqrt(3.0 / 7.0 + 2.0 / 7.0 * math.sqrt(6.0 / 5.0))
        heavy = (18.0 + math.sqrt(30.0)) / 36.0
        light = (18.0 - math.sqrt(30.0)) / 36.0
        points = [-outer, -inner, inner, outer]
        weights = [light, heavy, heavy, light]
    return (np.array(points), np.array(weights))


def lagrange_tables(anchors, samples):
    values = np.zeros((len(samples), len(anchors)))
    slopes = np.zeros((len(samples), len(anchors)))
    for sample_index, sample in enumerate(samples):
        for anchor_index, anchor in enumerate(anchors):
            others = [
                location
                for location_index, location in enumerate(anchors)
                if location_index != anchor_index
            ]
            product = 1.0
            for location in others:
                product = product * (sample - location) / (anchor - location)
            values[sample_index, anchor_index] = product
            derivative = 0.0
            for skipped in range(len(others)):
                summand = 1.0 / (anchor - others[skipped])
                for kept_index in range(len(others)):
                    if kept_index != skipped:
                        summand = (
                            summand * (sample - others[kept_index]) / (anchor - others[kept_index])
                        )
                derivative = derivative + summand
            slopes[sample_index, anchor_index] = derivative
    return (values, slopes)


def outer_three(first, second, third):
    return (
        first[:, None, None, :, None, None]
        * second[None, :, None, None, :, None]
        * third[None, None, :, None, None, :]
    )


def build_tables(anchors, point_count):
    raw_points, raw_weights = gauss_rule(point_count)
    samples = (raw_points + 1.0) / 2.0
    weights = raw_weights / 2.0
    basis_values, slopes = lagrange_tables(anchors, samples)
    quad_total = point_count**3
    nodal_count = len(anchors) ** 3
    derivative_one = outer_three(slopes, basis_values, basis_values).reshape(
        quad_total, nodal_count
    )
    derivative_two = outer_three(basis_values, slopes, basis_values).reshape(
        quad_total, nodal_count
    )
    derivative_three = outer_three(basis_values, basis_values, slopes).reshape(
        quad_total, nodal_count
    )
    stacked = np.stack([derivative_one, derivative_two, derivative_three]) / element_span
    volume = (weights[:, None, None] * weights[None, :, None] * weights[None, None, :]).reshape(
        -1
    ) * element_span**3
    forward = stacked.reshape(3 * quad_total, nodal_count)
    backward = (stacked * volume[None, :, None]).reshape(3 * quad_total, nodal_count).T
    weighted = stacked * volume[None, :, None]
    laplace = weighted[0].T @ stacked[0] + weighted[1].T @ stacked[1] + weighted[2].T @ stacked[2]
    matrix = np.zeros((nodal_count, 3, nodal_count, 3))
    for first in range(3):
        for second in range(3):
            block = weighted[second].T @ stacked[first] + (lame_ratio - 1.0) * (
                weighted[first].T @ stacked[second]
            )
            if first == second:
                block = block + laplace
            matrix[:, first, :, second] = block
    matrix = matrix.reshape(3 * nodal_count, 3 * nodal_count)
    vector = 1.5 + np.cos(1.3 * np.arange(3 * nodal_count))
    for repeat in range(200):
        vector = matrix @ vector
        vector = vector / np.sqrt(vector @ vector)
    largest = vector @ (matrix @ vector)
    return (forward, backward, float(4.0 * modulus_top * 1.1 * largest))


def row_nodes():
    nodes = []
    for entry in ELEMENT_ROWS:
        slot = SLOTS[entry[0]] if entry else None
        if slot is None or any(s and n for s, n in zip(entry[1], slot)):
            nodes.append(None)
        else:
            a, b, c = (3 * s + n for s, n in zip(entry[1], slot))
            nodes.append(16 * a + 4 * b + c)
    return nodes


def halves(matrix):
    whole = np.asarray(matrix, np.float32)
    high = whole.astype(jnp.bfloat16)
    low = (whole - high.astype(np.float32)).astype(jnp.bfloat16)
    return high, low


def element_tables():
    anchors = [0.0, inner_anchors[0], inner_anchors[1], 1.0]
    bound = build_tables(anchors, 4)[2]
    raw_points, raw_weights = gauss_rule(4)
    weights = raw_weights / 2.0
    values, slopes = lagrange_tables(anchors, (raw_points + 1.0) / 2.0)
    both = [outer_three(values, values, each).reshape(64, 64) for each in (values, slopes)]
    forward = np.concatenate([both[0], both[1] / element_span], 0)
    volume = (weights[:, None, None] * weights[None, :, None] * weights[None, None, :]).reshape(
        -1
    ) * element_span**3
    backward = (forward * np.concatenate([volume, volume])[:, None]).T
    spread = np.zeros((forward.shape[0], DEPTH))
    collect = np.zeros((ROWS, backward.shape[1]))
    for row, node in enumerate(row_nodes()):
        if node is not None:
            spread[:, row] = forward[:, node]
            collect[row, :] = backward[node, :]
    spread_high, spread_low = halves(spread)
    collect_high, collect_low = halves(collect)
    return (
        np.concatenate([spread_high, spread_high, spread_low], 1),
        np.concatenate(
            [
                np.concatenate([collect_high, collect_high], 1),
                np.concatenate([collect_low, np.zeros_like(collect_low)], 1),
            ],
            0,
        ),
        bound,
    )


def slope_tables(transposed):
    raw_points, weights = gauss_rule(4)
    samples = (raw_points + 1.0) / 2.0
    slopes = lagrange_tables(list(samples), samples)[1] / element_span
    if transposed:
        slopes = slopes.T * weights[None, :] / weights[:, None]
    from_even = [[(slopes[i, j] + slopes[i, 3 - j]) / 2.0 for j in range(2)] for i in range(2)]
    from_odd = [[(slopes[i, j] - slopes[i, 3 - j]) / 2.0 for j in range(2)] for i in range(2)]
    return (
        [[float(c) for c in row] for row in from_even],
        [[float(c) for c in row] for row in from_odd],
    )


def slopes_x(v, tables):
    from_even, from_odd = tables
    v = [v[16 * n : 16 * n + 16] for n in range(4)]
    even, odd = [v[0] + v[3], v[1] + v[2]], [v[0] - v[3], v[1] - v[2]]
    t = [from_even[i][0] * even[0] + from_even[i][1] * even[1] for i in range(2)]
    s = [from_odd[i][0] * odd[0] + from_odd[i][1] * odd[1] for i in range(2)]
    return jnp.concatenate([s[0] + t[0], s[1] + t[1], s[1] - t[1], s[0] - t[0]], 0)


def slopes_y(v, tables):
    lower = lax.broadcasted_iota(jnp.int32, (8, v.shape[1]), 0) < 4

    def both(first, second):
        return jnp.where(lower, first, second)

    (e, o) = tables
    parts = []
    for n in range(4):
        here, there = v[16 * n : 16 * n + 8], pltpu.roll(v[16 * n + 8 : 16 * n + 16], 4, 0)
        even, odd = here + there, here - there
        t = both(e[0][0], e[1][1]) * even + both(e[0][1], e[1][0]) * pltpu.roll(even, 4, 0)
        s = both(o[0][0], o[1][1]) * odd + both(o[0][1], o[1][0]) * pltpu.roll(odd, 4, 0)
        parts += [s + t, pltpu.roll(s - t, 4, 0)]
    return jnp.concatenate(parts, 0)


def transfer_table():
    table = np.zeros((8, 32))
    reach = (0.0, inner_anchors[0], inner_anchors[1])
    for row, corner in enumerate(CORNERS):
        for column, slot in enumerate(SLOTS):
            if slot is not None:
                weight = 1.0
                for side, node in zip(corner, slot):
                    weight = weight * (reach[node] if side else 1.0 - reach[node])
                table[row, column] = weight
    back = table.T.copy()
    back[TWIN] = back[0]
    return table.T.astype(np.float32), back.astype(np.float32)


def chebyshev_steps():
    steps = [(0.0, 1.0 / interval_centre)]
    ratio_now = 1.0 / interval_ratio
    for sweep in range(1, CHEB):
        ratio_next = 1.0 / (2.0 * interval_ratio - ratio_now)
        steps.append((ratio_next * ratio_now, 2.0 * ratio_next / interval_radius))
        ratio_now = ratio_next
    return steps


def stack_row(field, component, layer, b):
    return field * 54 + component * 18 + layer * 3 + b


def block_column(component, slot):
    return 72 + 4 * component + slot - 28 if slot >= 24 else 24 * component + slot


def pack_table():
    table = np.zeros((3, 128, 2, 2, 128), np.float32)
    for field in range(2):
        for x in range(2):
            for component in range(3):
                for column, slot in enumerate(SLOTS):
                    if slot is not None:
                        a, b, c = slot
                        row = stack_row(field, component, 3 * x + a, b)
                        table[c, row, field, x, block_column(component, column)] = 1.0
                        if field == 0 and column in NEXT_SLOTS:
                            at = BLOCK + 12 * component + NEXT_SLOTS.index(column)
                            table[c, row, 1, x, at] = 1.0
            table[0, 108 + x, 0, x, TWIN] = 1.0
    return table.reshape(384, 512).astype(jnp.bfloat16)


def unpack_table():
    table = np.zeros((2, 128, 4, 128), np.float32)
    for x in range(2):
        for component in range(3):
            for column, slot in enumerate(SLOTS):
                if slot is not None:
                    a, b, c = slot
                    row = stack_row(0, component, 3 * x + a, b)
                    table[x, component * 32 + column, c, row] = 1.0
                    if column < 5:
                        table[x, 96 + 8 * component + column, 3, row] = 1.0
                    if column == 0:
                        table[x, 96 + 8 * component + TWIN, 3, row] = 1.0
                    if 16 <= column < 20:
                        table[x, component * 32 + column + 8, 3, row] = 1.0
            table[x, 120 + component, 0, 54 + 2 * component + x] = 1.0
    return table.reshape(256, 512).astype(jnp.bfloat16)


def pick(values, table):
    count = values.shape[0]
    parts = jnp.dot(
        jnp.concatenate(high_low(values), 0), table, preferred_element_type=jnp.float32
    )
    return parts[:count] + parts[count:]


def ring_order(rows_of, columns_of):
    if (rows_of, columns_of) != (4, 8):
        return list(range(rows_of * columns_of))
    order = []
    for z in range(4):
        for x in range(2):
            for y in range(2):
                chip = (z, 7 - z, 15 - z, 8 + z)[2 * x + y]
                order += [2 * chip, 2 * chip + 1]
    return order


def pack_kernel(
    order,
    initial_at, forcing_at, modulus_at, listing_at, table_at, out,
    initial, forcing, modulus, listing, table, rows, turned, places, ready,
):
    own_layers = EZ // len(order)
    sources = (listing_at, modulus_at, initial_at, forcing_at, table_at)
    copies = [
        pltpu.make_async_copy(source, here, ready.at[n])
        for n, (source, here) in enumerate(
            zip(sources, (listing, modulus, initial, forcing, table))
        )
    ]
    for copy in copies:
        copy.start()
    rows[108:128, :] = jnp.zeros((20, 384), jnp.float32)
    copies[0].wait()
    copies[1].wait()
    listed = listing[0].astype(jnp.float32)
    listed = jnp.concatenate([listed, jnp.full((1, 64), 256.0, jnp.float32)], 1)
    listed = jnp.broadcast_to(listed, (128, 256)).T
    lanes = lax.broadcasted_iota(jnp.int32, (256, 128), 1).astype(jnp.float32)
    row_at = lax.broadcasted_iota(jnp.int32, (128, 128), 0)
    stiff = jnp.zeros((128, 128), jnp.float32)
    for x in range(2):
        hit = jnp.max(jnp.where(listed == lanes + 128.0 * x, 1.0, 0.0), axis=0, keepdims=True)
        stiff = jnp.where(row_at == 108 + x, hit * modulus[x], stiff)
    copies[2].wait()
    copies[3].wait()
    for field, source in enumerate((initial, forcing)):
        for component in range(3):
            for layer in range(6):
                at = stack_row(field, component, layer, 0)
                rows[at : at + 3, :] = source[component, layer]
    for part in range(3):
        span = slice(128 * part, 128 * part + 128)
        turned[span, :] = rows[:, span].T
    picked = [turned[pl.ds(c, 128, stride=3), :] for c in range(3)]
    picked[0] = picked[0] + stiff.T
    copies[4].wait()
    wide = pick(jnp.concatenate(picked, 1), table[...])
    lane = lax.broadcasted_iota(jnp.int32, (128, 128), 1)
    for x in range(2):
        tiles = [None] * (SENT // 128)
        for n in range(4):
            pair, field = n // 2, n % 2
            moved = wide[:, 128 * (2 * field + x) : 128 * (2 * field + x) + 128]
            first = BLOCK * n
            if pair:
                moved = pltpu.roll(moved, 128 - 2 * pair, 0)
            if first % 128:
                moved = pltpu.roll(moved, first % 128, 1)
            for tile in range(first // 128, (first + BLOCK - 1) // 128 + 1):
                before = tiles[tile]
                if before is None:
                    tiles[tile] = moved
                else:
                    tiles[tile] = jnp.where(lane >= first - 128 * tile, moved, before)
        above = wide[:, 128 * (2 + x) : 128 * (2 + x) + 128]
        above = pltpu.roll(pltpu.roll(above, 128 - own_layers, 0), (NEXT_COLUMN - BLOCK) % 128, 1)
        tiles[-1] = jnp.where(lane >= NEXT_COLUMN % 128, above, tiles[-1])
        for tile in range(SENT // 128):
            places[3 * x + tile, 0:128, :] = tiles[tile]
            places[3 * x + tile, 128:136, :] = jnp.zeros((8, 128), jnp.float32)
    for device, k in enumerate(order):
        for tile in range(SENT // 128):
            for x in range(2):
                at = 12 * device + 4 * tile + 2 * x
                out[at : at + 2, :] = places[
                    3 * x + tile, own_layers * k : own_layers * k + 2, :
                ]


def unpack_kernel(order, arrived, table, out, coarse_out, layers, turned):
    devices = arrived.shape[0]
    own_layers = EZ // devices
    for x in range(2):
        for layer in range(own_layers):
            row = (layer // 2) * 4 + x * 2 + layer % 2
            if order == sorted(order):
                layers[x, pl.ds(layer, devices, stride=own_layers), :] = arrived[:, row, :]
                continue
            for device, k in enumerate(order):
                at = own_layers * k + layer
                layers[x, at : at + 1, :] = arrived[device, row : row + 1, :]
    wide = pick(jnp.concatenate([layers[0], layers[1]], 1), table[...])
    shares = pltpu.roll(wide[:, 384:512], own_layers, 0)
    turned[pl.ds(0, 128, stride=3), :] = wide[:, 0:128] + shares
    for c in range(1, 3):
        turned[pl.ds(c, 128, stride=3), :] = wide[:, 128 * c : 128 * c + 128]
    for part in range(3):
        span = slice(128 * part, 128 * part + 128)
        back = turned[span, :].T
        for component in range(3):
            for layer in range(6):
                at = stack_row(0, component, layer, 0)
                out[component, layer, :, span] = back[at : at + 3, :]
    back = wide[:, 0:128].T
    for component in range(3):
        for x in range(2):
            at = 54 + 2 * component + x
            coarse_out[component, x] = back[at : at + 1, :]


def cofactor_rows(deform):
    return [
        [
            deform[(row_at + 1) % 3][(column + 1) % 3] * deform[(row_at + 2) % 3][(column + 2) % 3]
            - deform[(row_at + 1) % 3][(column + 2) % 3]
            * deform[(row_at + 2) % 3][(column + 1) % 3]
            for column in range(3)
        ]
        for row_at in range(3)
    ]


def point_stress(deform, stiffness, stiffness_four):
    cofactors = cofactor_rows(deform)
    jacobian = (
        deform[0][0] * cofactors[0][0]
        + deform[0][1] * cofactors[0][1]
        + deform[0][2] * cofactors[0][2]
    )
    pressure = stiffness_four * (jacobian - rest_ratio)
    return [
        [stiffness * deform[i][d] + pressure * cofactors[i][d] for d in range(3)] for i in range(3)
    ]


coarse_samples = [0.5 - 0.5 / math.sqrt(3.0), 0.5 + 0.5 / math.sqrt(3.0)]
two = range(2)


def at_points(low, high):
    change = high - low
    return [low + s * change for s in coarse_samples], change * (1.0 / element_span)


def ends_of(first, second):
    high = coarse_samples[0] * first + coarse_samples[1] * second
    return [first + second - high, high]


def high_low(values):
    high = values.astype(jnp.bfloat16)
    return high, (values - high.astype(jnp.float32)).astype(jnp.bfloat16)


def reads(pairs):
    return set(range(pairs[0], pairs[-1] + 2))


def plan_steps(spans):
    plan = []
    for first, count in spans:
        pairs = list(range(first, first + count))
        plan.append([pairs[n : n + 2] for n in range(0, count, 2)])
    for now, later in zip(plan, plan[1:]):
        if reads(later[0]) & set(now[-1]) and len(now[-1]) == 2:
            now[-1:] = [now[-1][:1], now[-1][1:]]
        if reads(later[0]) & set(now[-1]) and len(later[0]) == 2:
            later[:1] = [later[0][:1], later[0][1:]]
    return plan


class Slab:
    def __init__(self, width, across):
        self.width = width
        self.y_step = 2 * across
        lane = lax.broadcasted_iota(jnp.int32, (8, width), 1)
        x = (lane // 2) % across
        self.bottom, self.top, self.even = x == 0, x == across - 1, lane % 2 == 0
        self.row = lax.broadcasted_iota(jnp.int32, (8, width), 0)
        row = lax.broadcasted_iota(jnp.int32, (32, width), 0)
        lane = lax.broadcasted_iota(jnp.int32, (32, width), 1)
        on_face = (row == 0) | ((row >= 3) & (row <= 11))
        self.keep = jnp.where(on_face & ((lane // 2) % across == 0), 0.0, 1.0)

    def lanes(self, v, step):
        return pltpu.roll(v, step % self.width, 1)

    def from_next(self, v, x, y):
        if x or y:
            v = self.lanes(v, -2 * x - self.y_step * y)
        return jnp.where(self.top, 0.0, v) if x else v

    def from_next_z(self, v, ahead, x, y):
        step = -2 * x - self.y_step * y
        v = jnp.where(self.even, self.lanes(v, step - 1), self.lanes(ahead, step + 1))
        return jnp.where(self.top, 0.0, v) if x else v

    def onto_next(self, v, x, y, z=0):
        if x or y or z:
            v = self.lanes(v, 2 * x + self.y_step * y + z)
        return jnp.where(self.bottom, 0.0, v) if x else v

    def gather(self, here, ahead):
        row = self.row
        g0, g1, g2, g3 = here[0:8], here[8:16], here[16:24], here[24:32]
        a0 = ahead[0:8]
        z0, xz = self.from_next_z(g0, a0, 0, 0), self.from_next_z(g0, a0, 1, 0)
        yz, xyz = self.from_next_z(g0, a0, 0, 1), self.from_next_z(g0, a0, 1, 1)
        z2 = self.from_next_z(g2, ahead[16:24], 0, 0)
        edges = jnp.where(row <= 4, xz, self.from_next(g0, 1, 1))
        edges = jnp.where(row == 0, xyz, jnp.where(row <= 2, yz, edges))
        return jnp.concatenate(
            [
                g0,
                g1,
                g2,
                jnp.where(row < 4, z2, g3),
                self.from_next(g0, 1, 0),
                jnp.where(row == 7, yz, self.from_next(g0, 0, 1)),
                jnp.where(row == 7, xz, z0),
                jnp.where(row < 4, self.from_next(g1, 1, 0), self.from_next(g1, 0, 1)),
                edges,
                jnp.zeros_like(g0),
            ],
            0,
        )

    def scatter(self, part, behind):
        row = self.row
        g0, g1, g2, g3, x0, y0, z0, sides, edges = (part[8 * n : 8 * n + 8] for n in range(9))
        last = row == 7
        for_z = jnp.where(last, 0.0, z0)
        for_xz = jnp.where(last, z0, jnp.where((row == 3) | (row == 4), edges, 0.0))
        for_yz = jnp.where(last, y0, jnp.where((row == 1) | (row == 2), edges, 0.0))
        for_xyz = jnp.where(row == 0, edges, 0.0)
        for_xy = jnp.where(row >= 5, edges, 0.0)

        def above(z):
            return (
                self.onto_next(for_z, 0, 0, z)
                + self.onto_next(for_yz, 0, 1, z)
                + self.onto_next(for_xz, 1, 0, z)
                + self.onto_next(for_xyz, 1, 1, z)
            )

        own0 = g0 + self.onto_next(x0, 1, 0) + self.onto_next(jnp.where(last, 0.0, y0), 0, 1)
        own0 = own0 + self.onto_next(for_xy, 1, 1)
        own0 = own0 + jnp.where(self.even, behind[0], above(1))
        own1 = g1 + jnp.where(row < 4, self.onto_next(sides, 1, 0), self.onto_next(sides, 0, 1))
        share2 = jnp.where(self.even, behind[1], self.onto_next(g3, 0, 0, 1))
        own2 = g2 + jnp.where(row < 4, share2, 0.0)
        own3 = jnp.where(row < 4, 0.0, g3)
        moved = (above(-1), self.onto_next(g3, 0, 0, -1))
        return jnp.concatenate([self.twinned(own0), own1, own2, own3], 0), moved

    def twinned(self, v):
        twins = jnp.where(self.row == 7, pltpu.roll(v, 7, 0), 0.0)
        return v + jnp.where(self.row == 0, pltpu.roll(v, 1, 0), twins)

    def absorb(self, total, behind):
        low = self.twinned(jnp.where(self.even, behind[0], 0.0))
        high = jnp.where(self.even & (self.row < 4), behind[1], 0.0)
        return jnp.concatenate(
            [total[0:8] + low, total[8:16], total[16:24] + high, total[24:32]], 0
        )

    def gradient(self, u, spread, pairs):
        blocks = [self.gather(u[i, pair], u[i, pair + 1]) for i in range(3) for pair in pairs]
        high, low = high_low(jnp.concatenate(blocks, 1))
        return jnp.dot(
            spread[...],
            jnp.concatenate([high, low, high], 0),
            preferred_element_type=jnp.float32,
        )

    def force(self, gradient, stiff, collect, pairs):
        width = len(pairs) * self.width
        stiffness = jnp.concatenate([stiff[pair : pair + 1, :] for pair in pairs], 1)
        tables, tables_back = slope_tables(False), slope_tables(True)
        deform = []
        for i in range(3):
            span = slice(width * i, width * (i + 1))
            values = gradient[0:64, span]
            deform.append([slopes_x(values, tables), slopes_y(values, tables), gradient[64:, span]])
            deform[i][i] = deform[i][i] + 1.0
        stress = point_stress(deform, stiffness, lame_ratio * stiffness)
        parts = []
        for i in range(3):
            plane = slopes_x(stress[i][0], tables_back) + slopes_y(stress[i][1], tables_back)
            parts.append(jnp.concatenate([plane, stress[i][2]], 0))
        high, low = high_low(jnp.concatenate(parts, 1))
        force = jnp.dot(
            collect[...], jnp.concatenate([high, low], 0), preferred_element_type=jnp.float32
        )
        return force[0:ROWS] + force[ROWS:]

    def run(self, u, stiff, spread, collect, jobs, given=None):
        plan = plan_steps([job[:2] for job in jobs])
        steps = [(pairs, n) for n, chunks in enumerate(plan) for pairs in chunks]
        none = jnp.zeros((8, self.width), jnp.float32)
        ahead, carry, job = None, None, None
        for at, (pairs, n) in enumerate(steps):
            ready = given is not None and n == 0 and pairs == given[0]
            gradient = ahead
            if ahead is None and not ready:
                gradient = self.gradient(u, spread, pairs)
            if not ready:
                ahead = None
            if ahead is None and at + 1 < len(steps):
                later, later_job = steps[at + 1]
                if given is not None and later_job == 0 and later == given[0]:
                    later, later_job = steps[at + 2]
                if later_job == n or not reads(later) & set(pairs):
                    ahead = self.gradient(u, spread, later)
            if job != n:
                carry, job = [(none, none) for i in range(3)], n
            if ready:
                for q, pair in enumerate(pairs):
                    total = given[1][q]
                    if q == 0:
                        total = [self.absorb(total[i], carry[i]) for i in range(3)]
                    jobs[n][2](pair, total)
                carry = list(given[2])
                continue
            force = self.force(gradient, stiff, collect, pairs)
            totals = [[] for pair in pairs]
            for q in range(len(pairs)):
                for i in range(3):
                    lane = (len(pairs) * i + q) * self.width
                    total, carry[i] = self.scatter(force[:, lane : lane + self.width], carry[i])
                    totals[q].append(total)
            for pair, total in zip(pairs, totals):
                jobs[n][2](pair, total)
        return carry

    def smoothing(self, u, f, f_shift, d, spans, bound):
        jobs = []
        for (first, count), (held, added) in zip(spans, chebyshev_steps()):

            def finish(pair, forces, held=held, added=added):
                for i in range(3):
                    z = (added / bound) * self.keep * (f[i, pair + f_shift] - forces[i])
                    move = held * d[i, pair] + z if held else z
                    d[i, pair] = move
                    u[i, pair] = u[i, pair] + move

            jobs.append((first, count, finish))
        return jobs

    def owed(self, carry, bound):
        scale = -chebyshev_steps()[-1][1] / bound
        return [
            (
                scale * jnp.where(self.even, low, 0.0) * self.keep[0:8],
                scale * jnp.where(self.even, high, 0.0) * self.keep[16:24],
            )
            for low, high in carry
        ]

    def corners_of(self, v):
        ahead = pltpu.roll(v, 7, 0)
        found = {}
        for a in range(2):
            for b in range(2):
                found[a, b, 0] = self.from_next(v, a, b)
                found[a, b, 1] = self.from_next_z(v, ahead, a, b)
        return found

    def assemble(self, part):
        here, odd, even = 0.0, 0.0, 0.0
        for a in range(2):
            for b in range(2):
                here = here + self.onto_next(part[a, b, 0], a, b)
                odd = odd + self.onto_next(part[a, b, 1], a, b, 1)
                even = even + self.onto_next(part[a, b, 1], a, b, -1)
        return here + jnp.where(self.even, pltpu.roll(even, 1, 0), odd)

    def coarse_force(self, values, stiffness):
        grads = []
        for i in range(3):
            v = self.corners_of(values[i])
            vz, sz = {}, {}
            for a in two:
                for b in two:
                    vz[a, b], sz[a, b] = at_points(v[a, b, 0], v[a, b, 1])
            vv, vs, sv = {}, {}, {}
            for a in two:
                for k in two:
                    vv[a, k], vs[a, k] = at_points(vz[a, 0][k], vz[a, 1][k])
                sv[a], unused = at_points(sz[a, 0], sz[a, 1])
            dx, dy, dz = {}, {}, {}
            for k in two:
                for j in two:
                    dx[j, k] = (vv[1, k][j] - vv[0, k][j]) * (1.0 / element_span)
                line, unused = at_points(vs[0, k], vs[1, k])
                for h in two:
                    dy[h, k] = line[h]
            for j in two:
                line, unused = at_points(sv[0][j], sv[1][j])
                for h in two:
                    dz[h, j] = line[h]
            grads.append((dx, dy, dz))
        weight = element_span**2 / 8.0
        scaled = weight * stiffness
        scaled_four = lame_ratio * scaled
        sums = [({}, {}, {}) for i in range(3)]

        def add(table, key, value):
            table[key] = table[key] + value if key in table else value

        for h in two:
            for j in two:
                for k in two:
                    deform = [
                        [grads[i][0][j, k], grads[i][1][h, k], grads[i][2][h, j]]
                        for i in range(3)
                    ]
                    for i in range(3):
                        deform[i][i] = deform[i][i] + 1.0
                    stress = point_stress(deform, scaled, scaled_four)
                    for i in range(3):
                        add(sums[i][0], (j, k), stress[i][0])
                        add(sums[i][1], (h, k), stress[i][1])
                        add(sums[i][2], (h, j), stress[i][2])

        forces = []
        for i in range(3):
            part = {}
            qx, qy, qz = sums[i]
            along_z = [ends_of(qx[j, 0], qx[j, 1]) for j in two]
            for c in two:
                line = ends_of(along_z[0][c], along_z[1][c])
                for b in two:
                    part[0, b, c] = -line[b]
                    part[1, b, c] = line[b]
            along_z = [ends_of(qy[h, 0], qy[h, 1]) for h in two]
            for c in two:
                line = ends_of(along_z[0][c], along_z[1][c])
                for a in two:
                    part[a, 0, c] = part[a, 0, c] - line[a]
                    part[a, 1, c] = part[a, 1, c] + line[a]
            along_y = [ends_of(qz[h, 0], qz[h, 1]) for h in two]
            for b in two:
                line = ends_of(along_y[0][b], along_y[1][b])
                for a in two:
                    part[a, b, 0] = part[a, b, 0] - line[a]
                    part[a, b, 1] = part[a, b, 1] + line[a]
            forces.append(self.assemble(part))
        return forces


def window_pair(slab, first_layer, own_layers, fetch):
    found = []
    for parity in range(2):
        layer = first_layer + parity
        device = layer // own_layers
        layer = layer - device * own_layers
        found.append((device, layer // 2, layer % 2))
    values = [fetch(device, q) for device, q, parity in found]
    if found[0][:2] == found[1][:2] or (values[0] is None and values[1] is None):
        return values[0]
    for parity in range(2):
        if values[parity] is None:
            values[parity] = jnp.zeros_like(values[1 - parity])
        elif found[parity][2] != parity:
            values[parity] = slab.lanes(values[parity], 2 * parity - 1)
    lane = lax.broadcasted_iota(jnp.int32, values[0].shape, 1)
    return jnp.where(lane % 2 == 0, values[0], values[1])


def first_sources(own_layers):
    return list(range(-BEFORE // own_layers, (own_layers + BEFORE - 1) // own_layers + 1))


def whole_pairs(own_layers):
    return own_layers == 4


def turn_rows(block, mixed, turned, width, at):
    for tile in range(SENT // 128):
        n = at * (SENT // 128) + tile
        for m in range(width // 4):
            first = 12 * m + 4 * tile
            mixed[n, 4 * m : 4 * m + 4, :] = block[first : first + 4, :]
        turned[at, 128 * tile : 128 * tile + 128, :] = mixed[n].T


def regroup(slab, field, rows):
    values, hard = [], None
    for i in range(3):
        parts = [rows(24 * i + 8 * n) for n in range(3)]
        if field == 0 and i == 0:
            hard = parts[0][TWIN : TWIN + 1]
        parts[0] = jnp.where(slab.row == TWIN, pltpu.roll(parts[0], TWIN, 0), parts[0])
        parts.append(jnp.where(slab.row < 4, 0.0, rows(68 + 4 * i)))
        whole = jnp.concatenate(parts, 0)
        values.append(whole * slab.keep if field == 0 else whole)
    return values, hard


def layer_above(slab, turned, at, i):
    first = NEXT_COLUMN + 12 * i
    low, high = turned[at, first : first + 8, :], turned[at, first + 4 : first + 12, :]
    high = jnp.where(slab.row < 4, pltpu.roll(high, 4, 0), 0.0)
    low = jnp.where(slab.row == TWIN, pltpu.roll(low, TWIN, 0), low)
    nothing = jnp.zeros_like(low)
    return jnp.concatenate([low, nothing, high, nothing], 0) * slab.keep


def make_own_kernel(width, across, own_layers):
    own_pairs = own_layers // 2
    pairs = list(range(own_pairs))

    def own_kernel(block, spread, collect, u, f, stiff, forces, moved, mixed, turned):
        slab = Slab(width, across)
        turn_rows(block, mixed, turned, width, 0)
        for pair in pairs:
            for field, target in enumerate((u, f)):

                def rows(start, field=field, pair=pair):
                    at = BLOCK * (2 * pair + field) + start
                    return turned[0, at : at + 8, :]

                values, hard = regroup(slab, field, rows)
                for i in range(3):
                    target[i, pair] = values[i]
                if field == 0:
                    stiff[pair : pair + 1, :] = hard
        for i in range(3):
            u[i, own_pairs] = layer_above(slab, turned, 0, i)

        def finish(pair, total):
            for i in range(3):
                forces[i, pair] = total[i]

        carry = slab.run(u, stiff, spread, collect, [(0, own_pairs, finish)])
        for i in range(3):
            moved[i, 0] = carry[i][0]
            moved[i, 1] = carry[i][1]

    return own_kernel


def make_first_kernel(width, across, own_layers, fine_bound):
    own = BEFORE // 2
    own_pairs = (own_layers + 1) // 2
    spans = []
    prepared = whole_pairs(own_layers)
    for n in (4, 3, 2, 1):
        low, high = BEFORE - n, BEFORE + own_layers + n - 1 + prepared
        spans.append((low // 2, (high + 1) // 2 - low // 2))
    sources = [n for n in first_sources(own_layers) if n or not prepared]

    def first_kernel(*refs):
        arrived = refs[: len(sources)]
        refs = refs[len(sources) :]
        if prepared:
            own_u, own_f, own_stiff, own_forces, own_moved = refs[:5]
            refs = refs[5:]
        spread, collect, transfer, message, *sent, f, u, d, stiff, shares, mixed, turned = refs
        slab = Slab(width, across)
        u[...] = jnp.zeros(u.shape, jnp.float32)
        if not prepared:
            f[...] = jnp.zeros(f.shape, jnp.float32)
        shares[...] = jnp.zeros(shares.shape, jnp.float32)
        stiff[...] = jnp.zeros(stiff.shape, jnp.float32)
        for n in range(len(sources)):
            turn_rows(arrived[n], mixed, turned, width, n)
        for pair in range(PAIRS):
            if prepared and own <= pair < own + own_pairs:
                for i in range(3):
                    u[i, pair] = own_u[i, pair - own]
                    f[i, pair] = own_f[i, pair - own]
                stiff[pair : pair + 1, :] = own_stiff[pair - own : pair - own + 1, :]
                continue
            for field, target in enumerate((u, f)):

                def rows(start, field=field, pair=pair):
                    def fetch(device, q):
                        if device not in sources:
                            return None
                        at = BLOCK * (2 * q + field) + start
                        return turned[sources.index(device), at : at + 8, :]

                    value = window_pair(slab, 2 * pair - BEFORE, own_layers, fetch)
                    return jnp.zeros((8, width), jnp.float32) if value is None else value

                values, hard = regroup(slab, field, rows)
                for i in range(3):
                    target[i, pair] = values[i]
                if field == 0:
                    stiff[pair : pair + 1, :] = hard
        given = None
        if prepared:
            for i in range(3):
                u[i, PAIRS] = layer_above(slab, turned, sources.index(1), i)
            given = (
                list(range(own, own + own_pairs)),
                [[own_forces[i, q] for i in range(3)] for q in range(own_pairs)],
                [(own_moved[i, 0], own_moved[i, 1]) for i in range(3)],
            )

        weights = [jnp.broadcast_to(transfer[:, n : n + 1], (32, width)) for n in range(8)]

        def restrict(pair, forces):
            for i in range(3):
                rest = slab.keep * (f[i, pair] - forces[i])
                for n in range(8):
                    part = rest * weights[n]
                    part = (part[0:8] + part[8:16]) + (part[16:24] + part[24:32])
                    shares[i, n, pl.ds(pair, 1), :] = jnp.sum(part, axis=0, keepdims=True)

        jobs = slab.smoothing(u, f, 0, d, spans[0:3], fine_bound)
        slab.run(u, stiff, spread, collect, jobs + [(*spans[3], restrict)], given)

        restricted = [
            slab.assemble({corner: shares[i, n] for n, corner in enumerate(CORNERS)})
            for i in range(3)
        ]
        def line(rows, q):
            return rows[own + q : own + q + 1]

        for q in range(own_pairs):
            for i in range(3):
                message[i, q] = u[i, own + q]
                message[i, q, RESTRICTED_SLOT : RESTRICTED_SLOT + 1, :] = line(restricted[i], q)
            message[0, q, STIFF_SLOT : STIFF_SLOT + 1, :] = line(stiff, q)
        if prepared:
            down, up = sent
            for i in range(3):
                down[i, 0:32] = u[i, own]
                down[i, 32:40] = u[i, own + 1, 0:8, :]
                down[i, 40:48] = u[i, own + 1, 16:24, :]
                up[i] = u[i, own + 1]
                for n, row in enumerate(
                    (line(restricted[i], 0), line(restricted[i], 1), u[i, own + 2, 0:1, :])
                    + (line(restricted[i], 2),)
                ):
                    down[i, 24 + n : 25 + n, :] = row
                for n, row in enumerate(
                    (line(restricted[i], 1), line(restricted[i], 0), u[i, own, 0:1, :])
                ):
                    up[i, 24 + n : 25 + n, :] = row
            for q in range(own_pairs):
                down[q, 32 + TWIN : 33 + TWIN, :] = line(stiff, q)
                up[q, TWIN : TWIN + 1, :] = line(stiff, q)
            return
        edge = sent[0]
        for q in range(own_pairs):
            for i in range(3):
                edge[q, i : i + 1, :] = u[i, own + q, 0:1, :]
                edge[q, 3 + i : 4 + i, :] = line(restricted[i], q)
            edge[q, 6:8, :] = jnp.broadcast_to(line(stiff, q), (2, width))

    return first_kernel


def shares_sent(own_layers):
    return own_layers % 2 == 0


def sources_of(own_layers):
    below = 2 if shares_sent(own_layers) else 3
    whole = range(-below // own_layers, (own_layers + 2) // own_layers + 1)
    coarse = range(-(below + 2) // own_layers, (own_layers + 4) // own_layers + 1)
    return list(whole), [n for n in coarse if n not in whole]


def message_line(message, q, n):
    i, slot = ((n, 0), (n - 3, RESTRICTED_SLOT), (0, STIFF_SLOT))[n // 3]
    return message[i, q, slot : slot + 1, :]


def sent_readers(slab, up, message, down):
    def block_of(device, q, i):
        if device == 0:
            return message[i, q]
        if (device, q) == (1, 0):
            whole = down[i, 0:32]
        elif (device, q) == (1, 1):
            low, high = down[i, 32:40], down[i, 40:48]
            low = jnp.where(slab.row == TWIN, pltpu.roll(low, TWIN, 0), low)
            whole = jnp.concatenate([low, jnp.zeros_like(low), high, jnp.zeros_like(low)], 0)
        elif (device, q) == (-1, 1):
            low = up[i, 0:8]
            low = jnp.where(slab.row == TWIN, pltpu.roll(low, TWIN, 0), low)
            whole = jnp.concatenate([low, up[i, 8:32]], 0)
        else:
            return None
        return whole

    def line_of(device, q, n):
        if device == 0:
            return message_line(message, q, n)
        kind, i = n // 3, n % 3
        if device == 1:
            row = ((0, 24), (32, 25))[q][kind] if kind < 2 else 32 + TWIN
            i = i if kind < 2 else q
            return down[i, row : row + 1, :]
        if device == -1:
            row = ((26, 25), (0, 24))[q][kind] if kind < 2 else TWIN
            i = i if kind < 2 else q
            return up[i, row : row + 1, :]
        if (device, q) == (2, 0) and kind < 2:
            return down[i, 26 + kind : 27 + kind, :]
        return None

    return block_of, line_of


def make_second_kernel(width, across, own_layers, fine_bound, coarse_bound):
    own = BEFORE_B // 2
    own_pairs = (own_layers + 1) // 2
    shift = (BEFORE - BEFORE_B) // 2
    whole, outer = sources_of(own_layers)
    steps = chebyshev_steps()
    spans = []
    for n in (3, 2, 1):
        low, high = BEFORE_B - n + shares_sent(own_layers), BEFORE_B + own_layers + n - 1
        spans.append((low // 2, (high + 1) // 2 - low // 2))

    def second_kernel(*refs):
        slab = Slab(width, across)
        if whole_pairs(own_layers):
            up, message, down = refs[:3]
            refs = refs[3:]
            block_of, line_of = sent_readers(slab, up, message, down)
        else:
            messages = dict(zip(whole, refs))
            edges = dict(zip(outer, refs[len(whole) :]))
            refs = refs[len(whole) + len(outer) :]

            def block_of(device, q, i):
                return messages[device][i, q] if device in messages else None

            def line_of(device, q, n):
                if device in messages:
                    return message_line(messages[device], q, n)
                return edges[device][q, n : n + 1, :] if device in edges else None

        f, spread, collect, transfer_back, out, u, d, stiff, coarse = refs

        def pair_of(pair, fetch):
            return window_pair(slab, 2 * pair - BEFORE_B, own_layers, fetch)

        u[...] = jnp.zeros(u.shape, jnp.float32)
        coarse[...] = jnp.zeros(coarse.shape, jnp.float32)
        d[...] = jnp.zeros(d.shape, jnp.float32)
        for pair in range(PAIRS_B):
            for i in range(3):
                block = pair_of(pair, lambda device, q: block_of(device, q, i))
                if block is not None:
                    u[i, pair] = block
            for n in range(7):
                line = pair_of(pair, lambda device, q: line_of(device, q, n))
                if line is not None:
                    coarse[n, pair : pair + 1, :] = line
        stiff[...] = coarse[6]

        stiffness = coarse[6]
        keep_coarse = jnp.where(slab.bottom, 0.0, 1.0)
        start = [coarse[i] for i in range(3)]
        restricted = [coarse[3 + i] for i in range(3)]
        before = slab.coarse_force(start, stiffness)
        move = [(steps[0][1] / coarse_bound) * keep_coarse * restricted[i] for i in range(3)]
        level = [start[i] + move[i] for i in range(3)]
        for held, added in steps[1:]:
            force = slab.coarse_force(level, stiffness)
            for i in range(3):
                z = keep_coarse * (restricted[i] + before[i] - force[i])
                move[i] = held * move[i] + (added / coarse_bound) * z
                level[i] = level[i] + move[i]

        weights = [jnp.broadcast_to(transfer_back[:, n : n + 1], (32, width)) for n in range(8)]
        for i in range(3):
            change = slab.corners_of(level[i] - start[i])
            for pair in range(spans[0][0], min(spans[0][0] + spans[0][1] + 1, PAIRS_B)):
                lift = u[i, pair]
                for n, corner in enumerate(CORNERS):
                    lift = lift + weights[n] * change[corner][pair : pair + 1]
                u[i, pair] = lift

        jobs = slab.smoothing(u, f, shift, d, spans, fine_bound)
        owed = slab.owed(slab.run(u, stiff, spread, collect, jobs), fine_bound)

        lower = lax.broadcasted_iota(jnp.int32, (width // 8, 8, 128), 1) < 4
        nothing = jnp.zeros((8, width), jnp.float32)
        sides = []
        for q in range(2):
            if q or not shares_sent(own_layers):
                owed = [(nothing, nothing)] * 3
            rows = []
            for i in range(3):
                value = u[i, own + q]
                rows += [value[0:24], jnp.where(slab.row < 4, owed[i][1], value[24:32])]
            rows += [owed[i][0] for i in range(3)]
            rows += [level[i][own + q : own + q + 1] for i in range(3)] + [nothing[0:5]]
            sides.append(jnp.concatenate(rows, 0).T.reshape(width // 8, 8, 128))
        out[:, 0] = jnp.where(lower, sides[0], pltpu.roll(sides[1], 4, 1))
        out[:, 1] = jnp.where(lower, pltpu.roll(sides[0], 4, 1), sides[1])

    return second_kernel


def solution(mesh):
    rows_of, columns_of = mesh.shape["gx"], mesh.shape["gy"]
    devices = rows_of * columns_of
    order = ring_order(rows_of, columns_of)
    own_layers = EZ // devices
    own_pairs = (own_layers + 1) // 2
    width = 4 * devices
    across = 2 * rows_of
    near = first_sources(own_layers)
    prepared = whole_pairs(own_layers)
    whole, outer = sources_of(own_layers)
    spread, collect, fine_bound = element_tables()
    coarse_bound = build_tables([0.0, 1.0], 2)[2]
    transfer, transfer_back = transfer_table()
    wide = pltpu.CompilerParams(vmem_limit_bytes=60 * 1024 * 1024)
    limit = pltpu.CompilerParams(vmem_limit_bytes=48 * 1024 * 1024)
    f32 = jnp.float32

    pack = pl.pallas_call(
        functools.partial(pack_kernel, order),
        out_shape=jax.ShapeDtypeStruct((devices * 12, 128), f32),
        in_specs=[pl.BlockSpec(memory_space=pl.ANY)] * 5,
        out_specs=pl.BlockSpec(memory_space=pltpu.VMEM),
        scratch_shapes=[
            pltpu.VMEM((3, 6, 3, 384), f32),
            pltpu.VMEM((3, 6, 3, 384), f32),
            pltpu.VMEM((2, 1, EZ), f32),
            pltpu.VMEM((1, 1, 192), jnp.int32),
            pltpu.VMEM((384, 512), jnp.bfloat16),
            pltpu.VMEM((128, 384), f32),
            pltpu.VMEM((384, 128), f32),
            pltpu.VMEM((6, 136, 128), f32),
            pltpu.SemaphoreType.DMA((5,)),
        ],
        compiler_params=wide,
    )
    own = pl.pallas_call(
        make_own_kernel(width, across, own_layers),
        out_shape=(
            jax.ShapeDtypeStruct((3, own_pairs + 1, 32, width), f32),
            jax.ShapeDtypeStruct((3, own_pairs, 32, width), f32),
            jax.ShapeDtypeStruct((own_pairs, width), f32),
            jax.ShapeDtypeStruct((3, own_pairs, 32, width), f32),
            jax.ShapeDtypeStruct((3, 2, 8, width), f32),
        ),
        scratch_shapes=[
            pltpu.VMEM((SENT // 128, width, 128), f32),
            pltpu.VMEM((1, SENT, width), f32),
        ],
        compiler_params=limit,
        cost_estimate=pl.CostEstimate(flops=400_000_000, bytes_accessed=1_000_000, transcendentals=0),
    )
    sent = [jax.ShapeDtypeStruct((own_pairs, 8, width), f32)]
    if prepared:
        sent = [jax.ShapeDtypeStruct((3, rows, width), f32) for rows in (48, 32)]
    first = pl.pallas_call(
        make_first_kernel(width, across, own_layers, fine_bound),
        out_shape=(
            jax.ShapeDtypeStruct((3, own_pairs, 32, width), f32),
            *sent,
            jax.ShapeDtypeStruct((3, PAIRS, 32, width), f32),
        ),
        scratch_shapes=[
            pltpu.VMEM((3, 8, 32, width), f32),
            pltpu.VMEM((3, 8, 32, width), f32),
            pltpu.VMEM((8, width), f32),
            pltpu.VMEM((3, 8, 8, width), f32),
            pltpu.VMEM((len(near) * (SENT // 128), width, 128), f32),
            pltpu.VMEM((len(near), SENT, width), f32),
        ],
        compiler_params=limit,
    )
    second = pl.pallas_call(
        make_second_kernel(width, across, own_layers, fine_bound, coarse_bound),
        out_shape=jax.ShapeDtypeStruct((devices // 2, 2, 8, 128), f32),
        scratch_shapes=[
            pltpu.VMEM((3, PAIRS_B + 2, 32, width), f32),
            pltpu.VMEM((3, PAIRS_B, 32, width), f32),
            pltpu.VMEM((PAIRS_B, width), f32),
            pltpu.VMEM((7, PAIRS_B, width), f32),
        ],
        compiler_params=limit,
    )
    unpack = pl.pallas_call(
        functools.partial(unpack_kernel, order),
        out_shape=(
            jax.ShapeDtypeStruct((3, 6, 3, 384), f32),
            jax.ShapeDtypeStruct((3, 2, 1, EZ), f32),
        ),
        scratch_shapes=[pltpu.VMEM((2, 128, 128), f32), pltpu.VMEM((384, 128), f32)],
        compiler_params=limit,
    )
    everyone = ("gy", "gx")

    def from_device(block, distance):
        place = {k: m % rows_of * columns_of + m // rows_of for m, k in enumerate(order)}
        route = [(place[(k + distance) % devices], place[k]) for k in range(devices)]
        return lax.ppermute(block, ("gx", "gy"), route)

    def body(initial, forcing, modulus, solid_list):
        sent = pack(initial, forcing, modulus, solid_list, jnp.asarray(pack_table()))
        sent = sent.reshape(devices, SENT // 128, 4, 128)
        arrived = lax.all_to_all(sent, everyone, 0, 0, tiled=True).reshape(devices * 12, 128)
        blocks = [from_device(arrived, n) if n else arrived for n in near]
        if prepared:
            blocks = [block for n, block in zip(near, blocks) if n]
            blocks += own(arrived, jnp.asarray(spread), jnp.asarray(collect))
        message, *edges, load = first(
            *blocks,
            jnp.asarray(spread),
            jnp.asarray(collect),
            jnp.asarray(transfer),
        )
        if prepared:
            down, up = edges
            messages = [from_device(up, -1), message, from_device(down, 1)]
        else:
            messages = [from_device(message, n) if n else message for n in whole]
            messages += [from_device(edges[0], n) for n in outer]
        result = second(
            *messages,
            load,
            jnp.asarray(spread),
            jnp.asarray(collect),
            jnp.asarray(transfer_back),
        )
        back = lax.all_to_all(result.reshape(devices, 8, 128), everyone, 0, 0, tiled=True)
        return unpack(back, jnp.asarray(unpack_table()))

    placed = (
        P(None, "gx", "gy", None),
        P(None, "gx", "gy", None),
        P("gx", "gy", None),
        P("gx", "gy", None),
    )
    return jax.shard_map(
        body,
        mesh=mesh,
        in_specs=placed,
        out_specs=(P(None, "gx", "gy", None), P(None, "gx", "gy", None)),
        check_vma=False,
    )
```

```python
import functools
import math

import jax
import jax.numpy as jnp
import numpy as np
from jax import lax
from jax.experimental import pallas as pl
from jax.experimental.pallas import tpu as pltpu
from jax.sharding import PartitionSpec as P

CHEB = 3
EZ = 128

element_span = 20.0
lame_ratio = 4.0
rest_ratio = 1.25
modulus_top = 2.0
spectrum_floor = 0.05
interval_centre = (1.0 + spectrum_floor) / 2.0
interval_radius = (1.0 - spectrum_floor) / 2.0
interval_ratio = interval_centre / interval_radius
inner_anchors = (0.5 - 0.5 / math.sqrt(5.0), 0.5 + 0.5 / math.sqrt(5.0))

BEFORE = 4
PAIRS = 6
BEFORE_B = 6
PAIRS_B = 8
BLOCK = 84
SENT = 384

SLOTS = [
    (0, 0, 0), (1, 0, 0), (2, 0, 0), (0, 1, 0), (0, 2, 0), (0, 0, 1), (0, 0, 2), None,
    (0, 1, 1), (0, 1, 2), (0, 2, 1), (0, 2, 2), (1, 0, 1), (1, 0, 2), (2, 0, 1), (2, 0, 2),
    (1, 1, 0), (1, 2, 0), (2, 1, 0), (2, 2, 0), (1, 1, 1), (1, 1, 2), (1, 2, 1), (1, 2, 2),
    None, None, None, None, (2, 1, 1), (2, 1, 2), (2, 2, 1), (2, 2, 2),
]
TWIN = 7
NEXT_SLOTS = [0, 1, 2, 3, 4, 5, 6, 7, 16, 17, 18, 19]
NEXT_COLUMN = 4 * BLOCK
RESTRICTED_SLOT = 24
STIFF_SLOT = 25
OWN_SHIFT, SHIFT_X, SHIFT_Y, SHIFT_Z = (0, 0, 0), (1, 0, 0), (0, 1, 0), (0, 0, 1)
ELEMENT_ROWS = (
    [(slot, OWN_SHIFT) for slot in range(24)]
    + [(slot, SHIFT_Z) for slot in range(16, 20)]
    + [(slot, OWN_SHIFT) for slot in range(28, 32)]
    + [(slot, SHIFT_X) for slot in range(7)] + [None]
    + [(slot, SHIFT_Y) for slot in range(7)] + [(0, (0, 1, 1))]
    + [(slot, SHIFT_Z) for slot in range(7)] + [(0, (1, 0, 1))]
    + [(slot, SHIFT_X) for slot in range(8, 12)] + [(slot, SHIFT_Y) for slot in range(12, 16)]
    + [(0, (1, 1, 1)), (1, (0, 1, 1)), (2, (0, 1, 1)), (3, (1, 0, 1)), (4, (1, 0, 1))]
    + [(5, (1, 1, 0)), (6, (1, 1, 0)), (0, (1, 1, 0))]
)
ROWS = len(ELEMENT_ROWS)
DEPTH = 80
CORNERS = [(a, b, c) for a in range(2) for b in range(2) for c in range(2)]


def gauss_rule(point_count):
    if point_count == 2:
        offset = 1.0 / math.sqrt(3.0)
        points = [-offset, offset]
        weights = [1.0, 1.0]
    else:
        inner = math.sqrt(3.0 / 7.0 - 2.0 / 7.0 * math.sqrt(6.0 / 5.0))
        outer = math.sqrt(3.0 / 7.0 + 2.0 / 7.0 * math.sqrt(6.0 / 5.0))
        heavy = (18.0 + math.sqrt(30.0)) / 36.0
        light = (18.0 - math.sqrt(30.0)) / 36.0
        points = [-outer, -inner, inner, outer]
        weights = [light, heavy, heavy, light]
    return (np.array(points), np.array(weights))


def lagrange_tables(anchors, samples):
    values = np.zeros((len(samples), len(anchors)))
    slopes = np.zeros((len(samples), len(anchors)))
    for sample_index, sample in enumerate(samples):
        for anchor_index, anchor in enumerate(anchors):
            others = [
                location
                for location_index, location in enumerate(anchors)
                if location_index != anchor_index
            ]
            product = 1.0
            for location in others:
                product = product * (sample - location) / (anchor - location)
            values[sample_index, anchor_index] = product
            derivative = 0.0
            for skipped in range(len(others)):
                summand = 1.0 / (anchor - others[skipped])
                for kept_index in range(len(others)):
                    if kept_index != skipped:
                        summand = (
                            summand * (sample - others[kept_index]) / (anchor - others[kept_index])
                        )
                derivative = derivative + summand
            slopes[sample_index, anchor_index] = derivative
    return (values, slopes)


def outer_three(first, second, third):
    return (
        first[:, None, None, :, None, None]
        * second[None, :, None, None, :, None]
        * third[None, None, :, None, None, :]
    )


def build_tables(anchors, point_count):
    raw_points, raw_weights = gauss_rule(point_count)
    samples = (raw_points + 1.0) / 2.0
    weights = raw_weights / 2.0
    basis_values, slopes = lagrange_tables(anchors, samples)
    quad_total = point_count**3
    nodal_count = len(anchors) ** 3
    derivative_one = outer_three(slopes, basis_values, basis_values).reshape(
        quad_total, nodal_count
    )
    derivative_two = outer_three(basis_values, slopes, basis_values).reshape(
        quad_total, nodal_count
    )
    derivative_three = outer_three(basis_values, basis_values, slopes).reshape(
        quad_total, nodal_count
    )
    stacked = np.stack([derivative_one, derivative_two, derivative_three]) / element_span
    volume = (weights[:, None, None] * weights[None, :, None] * weights[None, None, :]).reshape(
        -1
    ) * element_span**3
    forward = stacked.reshape(3 * quad_total, nodal_count)
    backward = (stacked * volume[None, :, None]).reshape(3 * quad_total, nodal_count).T
    weighted = stacked * volume[None, :, None]
    laplace = weighted[0].T @ stacked[0] + weighted[1].T @ stacked[1] + weighted[2].T @ stacked[2]
    matrix = np.zeros((nodal_count, 3, nodal_count, 3))
    for first in range(3):
        for second in range(3):
            block = weighted[second].T @ stacked[first] + (lame_ratio - 1.0) * (
                weighted[first].T @ stacked[second]
            )
            if first == second:
                block = block + laplace
            matrix[:, first, :, second] = block
    matrix = matrix.reshape(3 * nodal_count, 3 * nodal_count)
    vector = 1.5 + np.cos(1.3 * np.arange(3 * nodal_count))
    for repeat in range(200):
        vector = matrix @ vector
        vector = vector / np.sqrt(vector @ vector)
    largest = vector @ (matrix @ vector)
    return (forward, backward, float(4.0 * modulus_top * 1.1 * largest))


def row_nodes():
    nodes = []
    for entry in ELEMENT_ROWS:
        slot = SLOTS[entry[0]] if entry else None
        if slot is None or any(s and n for s, n in zip(entry[1], slot)):
            nodes.append(None)
        else:
            a, b, c = (3 * s + n for s, n in zip(entry[1], slot))
            nodes.append(16 * a + 4 * b + c)
    return nodes


def halves(matrix):
    whole = np.asarray(matrix, np.float32)
    high = whole.astype(jnp.bfloat16)
    low = (whole - high.astype(np.float32)).astype(jnp.bfloat16)
    return high, low


def element_tables():
    forward, backward, bound = build_tables([0.0, inner_anchors[0], inner_anchors[1], 1.0], 4)
    spread = np.zeros((forward.shape[0], DEPTH))
    collect = np.zeros((ROWS, backward.shape[1]))
    for row, node in enumerate(row_nodes()):
        if node is not None:
            spread[:, row] = forward[:, node]
            collect[row, :] = backward[node, :]
    spread_high, spread_low = halves(spread)
    collect_high, collect_low = halves(collect)
    return (
        np.concatenate([spread_high, spread_high, spread_low], 1),
        np.concatenate([collect_high, collect_low], 0),
        bound,
    )


def transfer_table():
    table = np.zeros((8, 32))
    reach = (0.0, inner_anchors[0], inner_anchors[1])
    for row, corner in enumerate(CORNERS):
        for column, slot in enumerate(SLOTS):
            if slot is not None:
                weight = 1.0
                for side, node in zip(corner, slot):
                    weight = weight * (reach[node] if side else 1.0 - reach[node])
                table[row, column] = weight
    back = table.T.copy()
    back[TWIN] = back[0]
    return table.T.astype(np.float32), back.astype(np.float32)


def chebyshev_steps():
    steps = [(0.0, 1.0 / interval_centre)]
    ratio_now = 1.0 / interval_ratio
    for sweep in range(1, CHEB):
        ratio_next = 1.0 / (2.0 * interval_ratio - ratio_now)
        steps.append((ratio_next * ratio_now, 2.0 * ratio_next / interval_radius))
        ratio_now = ratio_next
    return steps


def stack_row(field, component, layer, b):
    return field * 54 + component * 18 + layer * 3 + b


def block_column(component, slot):
    return 72 + 4 * component + slot - 28 if slot >= 24 else 24 * component + slot


def pack_table():
    table = np.zeros((3, 128, 2, 2, 128), np.float32)
    for field in range(2):
        for x in range(2):
            for component in range(3):
                for column, slot in enumerate(SLOTS):
                    if slot is not None:
                        a, b, c = slot
                        row = stack_row(field, component, 3 * x + a, b)
                        table[c, row, field, x, block_column(component, column)] = 1.0
                        if field == 0 and column in NEXT_SLOTS:
                            at = BLOCK + 12 * component + NEXT_SLOTS.index(column)
                            table[c, row, 1, x, at] = 1.0
            table[0, 108 + x, 0, x, TWIN] = 1.0
    return table.reshape(384, 512).astype(jnp.bfloat16)


def unpack_table():
    table = np.zeros((2, 128, 4, 128), np.float32)
    for x in range(2):
        for component in range(3):
            for column, slot in enumerate(SLOTS):
                if slot is not None:
                    a, b, c = slot
                    row = stack_row(0, component, 3 * x + a, b)
                    table[x, component * 32 + column, c, row] = 1.0
                    if column < 5:
                        table[x, 96 + 8 * component + column, 3, row] = 1.0
                    if column == 0:
                        table[x, 96 + 8 * component + TWIN, 3, row] = 1.0
                    if 16 <= column < 20:
                        table[x, component * 32 + column + 8, 3, row] = 1.0
            table[x, 120 + component, 0, 54 + 2 * component + x] = 1.0
    return table.reshape(256, 512).astype(jnp.bfloat16)


def pick(values, table):
    count = values.shape[0]
    parts = jnp.dot(
        jnp.concatenate(high_low(values), 0), table, preferred_element_type=jnp.float32
    )
    return parts[:count] + parts[count:]


def ring_order(rows_of, columns_of):
    if (rows_of, columns_of) != (4, 8):
        return list(range(rows_of * columns_of))
    order = []
    for z in range(4):
        for x in range(2):
            for y in range(2):
                chip = (z, 7 - z, 15 - z, 8 + z)[2 * x + y]
                order += [2 * chip, 2 * chip + 1]
    return order


def pack_kernel(
    order,
    initial_at, forcing_at, modulus_at, listing_at, table_at, out,
    initial, forcing, modulus, listing, table, rows, turned, places, ready,
):
    own_layers = EZ // len(order)
    sources = (listing_at, modulus_at, initial_at, forcing_at, table_at)
    copies = [
        pltpu.make_async_copy(source, here, ready.at[n])
        for n, (source, here) in enumerate(
            zip(sources, (listing, modulus, initial, forcing, table))
        )
    ]
    for copy in copies:
        copy.start()
    rows[108:128, :] = jnp.zeros((20, 384), jnp.float32)
    copies[0].wait()
    copies[1].wait()
    listed = listing[0].astype(jnp.float32)
    listed = jnp.concatenate([listed, jnp.full((1, 64), 256.0, jnp.float32)], 1)
    listed = jnp.broadcast_to(listed, (128, 256)).T
    lanes = lax.broadcasted_iota(jnp.int32, (256, 128), 1).astype(jnp.float32)
    row_at = lax.broadcasted_iota(jnp.int32, (128, 128), 0)
    stiff = jnp.zeros((128, 128), jnp.float32)
    for x in range(2):
        hit = jnp.max(jnp.where(listed == lanes + 128.0 * x, 1.0, 0.0), axis=0, keepdims=True)
        stiff = jnp.where(row_at == 108 + x, hit * modulus[x], stiff)
    copies[2].wait()
    copies[3].wait()
    for field, source in enumerate((initial, forcing)):
        for component in range(3):
            for layer in range(6):
                at = stack_row(field, component, layer, 0)
                rows[at : at + 3, :] = source[component, layer]
    for part in range(3):
        span = slice(128 * part, 128 * part + 128)
        turned[span, :] = rows[:, span].T
    picked = [turned[pl.ds(c, 128, stride=3), :] for c in range(3)]
    picked[0] = picked[0] + stiff.T
    copies[4].wait()
    wide = pick(jnp.concatenate(picked, 1), table[...])
    lane = lax.broadcasted_iota(jnp.int32, (128, 128), 1)
    for x in range(2):
        tiles = [None] * (SENT // 128)
        for n in range(4):
            pair, field = n // 2, n % 2
            moved = wide[:, 128 * (2 * field + x) : 128 * (2 * field + x) + 128]
            first = BLOCK * n
            if pair:
                moved = pltpu.roll(moved, 128 - 2 * pair, 0)
            if first % 128:
                moved = pltpu.roll(moved, first % 128, 1)
            for tile in range(first // 128, (first + BLOCK - 1) // 128 + 1):
                before = tiles[tile]
                if before is None:
                    tiles[tile] = moved
                else:
                    tiles[tile] = jnp.where(lane >= first - 128 * tile, moved, before)
        above = wide[:, 128 * (2 + x) : 128 * (2 + x) + 128]
        above = pltpu.roll(pltpu.roll(above, 128 - own_layers, 0), (NEXT_COLUMN - BLOCK) % 128, 1)
        tiles[-1] = jnp.where(lane >= NEXT_COLUMN % 128, above, tiles[-1])
        for tile in range(SENT // 128):
            places[3 * x + tile, 0:128, :] = tiles[tile]
            places[3 * x + tile, 128:136, :] = jnp.zeros((8, 128), jnp.float32)
    for device, k in enumerate(order):
        for tile in range(SENT // 128):
            for x in range(2):
                at = 12 * device + 4 * tile + 2 * x
                out[at : at + 2, :] = places[
                    3 * x + tile, own_layers * k : own_layers * k + 2, :
                ]


def unpack_kernel(order, arrived, table, out, coarse_out, layers, turned):
    devices = arrived.shape[0]
    own_layers = EZ // devices
    for x in range(2):
        for layer in range(own_layers):
            row = (layer // 2) * 4 + x * 2 + layer % 2
            if order == sorted(order):
                layers[x, pl.ds(layer, devices, stride=own_layers), :] = arrived[:, row, :]
                continue
            for device, k in enumerate(order):
                at = own_layers * k + layer
                layers[x, at : at + 1, :] = arrived[device, row : row + 1, :]
    wide = pick(jnp.concatenate([layers[0], layers[1]], 1), table[...])
    shares = pltpu.roll(wide[:, 384:512], own_layers, 0)
    turned[pl.ds(0, 128, stride=3), :] = wide[:, 0:128] + shares
    for c in range(1, 3):
        turned[pl.ds(c, 128, stride=3), :] = wide[:, 128 * c : 128 * c + 128]
    for part in range(3):
        span = slice(128 * part, 128 * part + 128)
        back = turned[span, :].T
        for component in range(3):
            for layer in range(6):
                at = stack_row(0, component, layer, 0)
                out[component, layer, :, span] = back[at : at + 3, :]
    back = wide[:, 0:128].T
    for component in range(3):
        for x in range(2):
            at = 54 + 2 * component + x
            coarse_out[component, x] = back[at : at + 1, :]


def cofactor_rows(deform):
    return [
        [
            deform[(row_at + 1) % 3][(column + 1) % 3] * deform[(row_at + 2) % 3][(column + 2) % 3]
            - deform[(row_at + 1) % 3][(column + 2) % 3]
            * deform[(row_at + 2) % 3][(column + 1) % 3]
            for column in range(3)
        ]
        for row_at in range(3)
    ]


def point_stress(deform):
    cofactors = cofactor_rows(deform)
    jacobian = (
        deform[0][0] * cofactors[0][0]
        + deform[0][1] * cofactors[0][1]
        + deform[0][2] * cofactors[0][2]
    )
    pressure = lame_ratio * (jacobian - rest_ratio)
    return [
        [deform[i][d] + pressure * cofactors[i][d] for d in range(3)] for i in range(3)
    ]


coarse_samples = [0.5 - 0.5 / math.sqrt(3.0), 0.5 + 0.5 / math.sqrt(3.0)]
two = range(2)


def at_points(low, high):
    change = high - low
    return [low + s * change for s in coarse_samples], change * (1.0 / element_span)


def ends_of(first, second):
    high = coarse_samples[0] * first + coarse_samples[1] * second
    return [first + second - high, high]


def high_low(values):
    high = values.astype(jnp.bfloat16)
    return high, (values - high.astype(jnp.float32)).astype(jnp.bfloat16)


def reads(pairs):
    return set(range(pairs[0], pairs[-1] + 2))


def plan_steps(spans):
    plan = []
    for first, count in spans:
        pairs = list(range(first, first + count))
        plan.append([pairs[n : n + 2] for n in range(0, count, 2)])
    for now, later in zip(plan, plan[1:]):
        if reads(later[0]) & set(now[-1]) and len(now[-1]) == 2:
            now[-1:] = [now[-1][:1], now[-1][1:]]
        if reads(later[0]) & set(now[-1]) and len(later[0]) == 2:
            later[:1] = [later[0][:1], later[0][1:]]
    return plan


class Slab:
    def __init__(self, width, across):
        self.width = width
        self.y_step = 2 * across
        lane = lax.broadcasted_iota(jnp.int32, (8, width), 1)
        x = (lane // 2) % across
        self.bottom, self.top, self.even = x == 0, x == across - 1, lane % 2 == 0
        self.row = lax.broadcasted_iota(jnp.int32, (8, width), 0)
        row = lax.broadcasted_iota(jnp.int32, (32, width), 0)
        lane = lax.broadcasted_iota(jnp.int32, (32, width), 1)
        on_face = (row == 0) | ((row >= 3) & (row <= 11))
        self.keep = jnp.where(on_face & ((lane // 2) % across == 0), 0.0, 1.0)

    def lanes(self, v, step):
        return pltpu.roll(v, step % self.width, 1)

    def from_next(self, v, x, y):
        if x or y:
            v = self.lanes(v, -2 * x - self.y_step * y)
        return jnp.where(self.top, 0.0, v) if x else v

    def from_next_z(self, v, ahead, x, y):
        step = -2 * x - self.y_step * y
        v = jnp.where(self.even, self.lanes(v, step - 1), self.lanes(ahead, step + 1))
        return jnp.where(self.top, 0.0, v) if x else v

    def onto_next(self, v, x, y, z=0):
        if x or y or z:
            v = self.lanes(v, 2 * x + self.y_step * y + z)
        return jnp.where(self.bottom, 0.0, v) if x else v

    def gather(self, here, ahead):
        row = self.row
        g0, g1, g2, g3 = here[0:8], here[8:16], here[16:24], here[24:32]
        a0 = ahead[0:8]
        z0, xz = self.from_next_z(g0, a0, 0, 0), self.from_next_z(g0, a0, 1, 0)
        yz, xyz = self.from_next_z(g0, a0, 0, 1), self.from_next_z(g0, a0, 1, 1)
        z2 = self.from_next_z(g2, ahead[16:24], 0, 0)
        edges = jnp.where(row <= 4, xz, self.from_next(g0, 1, 1))
        edges = jnp.where(row == 0, xyz, jnp.where(row <= 2, yz, edges))
        return jnp.concatenate(
            [
                g0,
                g1,
                g2,
                jnp.where(row < 4, z2, g3),
                self.from_next(g0, 1, 0),
                jnp.where(row == 7, yz, self.from_next(g0, 0, 1)),
                jnp.where(row == 7, xz, z0),
                jnp.where(row < 4, self.from_next(g1, 1, 0), self.from_next(g1, 0, 1)),
                edges,
                jnp.zeros_like(g0),
            ],
            0,
        )

    def scatter(self, part, behind):
        row = self.row
        g0, g1, g2, g3, x0, y0, z0, sides, edges = (part[8 * n : 8 * n + 8] for n in range(9))
        last = row == 7
        for_z = jnp.where(last, 0.0, z0)
        for_xz = jnp.where(last, z0, jnp.where((row == 3) | (row == 4), edges, 0.0))
        for_yz = jnp.where(last, y0, jnp.where((row == 1) | (row == 2), edges, 0.0))
        for_xyz = jnp.where(row == 0, edges, 0.0)
        for_xy = jnp.where(row >= 5, edges, 0.0)

        def above(z):
            return (
                self.onto_next(for_z, 0, 0, z)
                + self.onto_next(for_yz, 0, 1, z)
                + self.onto_next(for_xz, 1, 0, z)
                + self.onto_next(for_xyz, 1, 1, z)
            )

        own0 = g0 + self.onto_next(x0, 1, 0) + self.onto_next(jnp.where(last, 0.0, y0), 0, 1)
        own0 = own0 + self.onto_next(for_xy, 1, 1)
        own0 = own0 + jnp.where(self.even, behind[0], above(1))
        own1 = g1 + jnp.where(row < 4, self.onto_next(sides, 1, 0), self.onto_next(sides, 0, 1))
        share2 = jnp.where(self.even, behind[1], self.onto_next(g3, 0, 0, 1))
        own2 = g2 + jnp.where(row < 4, share2, 0.0)
        own3 = jnp.where(row < 4, 0.0, g3)
        moved = (above(-1), self.onto_next(g3, 0, 0, -1))
        return jnp.concatenate([self.twinned(own0), own1, own2, own3], 0), moved

    def twinned(self, v):
        twins = jnp.where(self.row == 7, pltpu.roll(v, 7, 0), 0.0)
        return v + jnp.where(self.row == 0, pltpu.roll(v, 1, 0), twins)

    def absorb(self, total, behind):
        low = self.twinned(jnp.where(self.even, behind[0], 0.0))
        high = jnp.where(self.even & (self.row < 4), behind[1], 0.0)
        return jnp.concatenate(
            [total[0:8] + low, total[8:16], total[16:24] + high, total[24:32]], 0
        )

    def gradient(self, u, spread, pairs):
        parts = [
            high_low(self.gather(u[i, pair], u[i, pair + 1])) for i in range(3) for pair in pairs
        ]
        return jnp.dot(
            spread[...],
            jnp.concatenate([jnp.concatenate([h, l, h], 0) for h, l in parts], 1),
            preferred_element_type=jnp.float32,
        )

    def force(self, gradient, stiff, collect, pairs):
        width, count = self.width, len(pairs)
        rows = 16
        high, low = {}, {}
        for q in range(count):
            for r in range(64 // rows):
                deform = [
                    [
                        gradient[
                            64 * e + rows * r : 64 * e + rows * (r + 1),
                            width * (count * i + q) : width * (count * i + q + 1),
                        ]
                        + (1.0 if i == e else 0.0)
                        for e in range(3)
                    ]
                    for i in range(3)
                ]
                stress = point_stress(deform)
                for i in range(3):
                    for e in range(3):
                        high[e, r, i, q], low[e, r, i, q] = high_low(stress[i][e])

        def whole(part):
            return jnp.concatenate(
                [
                    jnp.concatenate([part[e, r, i, q] for i in range(3) for q in range(count)], 1)
                    for e in range(3)
                    for r in range(64 // rows)
                ],
                0,
            )

        force = jnp.dot(collect[...], whole(high), preferred_element_type=jnp.float32)
        force = force[0:ROWS] + (
            force[ROWS:]
            + jnp.dot(collect[0:ROWS], whole(low), preferred_element_type=jnp.float32)
        )
        stiffness = [stiff[pair : pair + 1, :] for pair in pairs]
        return force * jnp.concatenate(stiffness * 3, 1)

    def run(self, u, stiff, spread, collect, jobs, given=None):
        plan = plan_steps([job[:2] for job in jobs])
        steps = [(pairs, n) for n, chunks in enumerate(plan) for pairs in chunks]
        none = jnp.zeros((8, self.width), jnp.float32)
        ahead, carry, job = None, None, None
        for at, (pairs, n) in enumerate(steps):
            ready = given is not None and n == 0 and pairs == given[0]
            gradient = ahead
            if ahead is None and not ready:
                gradient = self.gradient(u, spread, pairs)
            if not ready:
                ahead = None
            if ahead is None and at + 1 < len(steps):
                later, later_job = steps[at + 1]
                if given is not None and later_job == 0 and later == given[0]:
                    later, later_job = steps[at + 2]
                if later_job == n or not reads(later) & set(pairs):
                    ahead = self.gradient(u, spread, later)
            if job != n:
                carry, job = [(none, none) for i in range(3)], n
            if ready:
                for q, pair in enumerate(pairs):
                    total = given[1][q]
                    if q == 0:
                        total = [self.absorb(total[i], carry[i]) for i in range(3)]
                    jobs[n][2](pair, total)
                carry = list(given[2])
                continue
            force = self.force(gradient, stiff, collect, pairs)
            totals = [[] for pair in pairs]
            for q in range(len(pairs)):
                for i in range(3):
                    lane = (len(pairs) * i + q) * self.width
                    total, carry[i] = self.scatter(force[:, lane : lane + self.width], carry[i])
                    totals[q].append(total)
            for pair, total in zip(pairs, totals):
                jobs[n][2](pair, total)
        return carry

    def smoothing(self, u, f, f_shift, d, spans, bound):
        jobs = []
        for (first, count), (held, added) in zip(spans, chebyshev_steps()):

            def finish(pair, forces, held=held, added=added):
                for i in range(3):
                    z = (added / bound) * self.keep * (f[i, pair + f_shift] - forces[i])
                    move = held * d[i, pair] + z if held else z
                    d[i, pair] = move
                    u[i, pair] = u[i, pair] + move

            jobs.append((first, count, finish))
        return jobs

    def owed(self, carry, bound):
        scale = -chebyshev_steps()[-1][1] / bound
        return [
            (
                scale * jnp.where(self.even, low, 0.0) * self.keep[0:8],
                scale * jnp.where(self.even, high, 0.0) * self.keep[16:24],
            )
            for low, high in carry
        ]

    def corners_of(self, v):
        ahead = pltpu.roll(v, 7, 0)
        found = {}
        for a in range(2):
            for b in range(2):
                found[a, b, 0] = self.from_next(v, a, b)
                found[a, b, 1] = self.from_next_z(v, ahead, a, b)
        return found

    def assemble(self, part):
        here, odd, even = 0.0, 0.0, 0.0
        for a in range(2):
            for b in range(2):
                here = here + self.onto_next(part[a, b, 0], a, b)
                odd = odd + self.onto_next(part[a, b, 1], a, b, 1)
                even = even + self.onto_next(part[a, b, 1], a, b, -1)
        return here + jnp.where(self.even, pltpu.roll(even, 1, 0), odd)

    def coarse_force(self, values, stiffness):
        grads = []
        for i in range(3):
            v = self.corners_of(values[i])
            vz, sz = {}, {}
            for a in two:
                for b in two:
                    vz[a, b], sz[a, b] = at_points(v[a, b, 0], v[a, b, 1])
            vv, vs, sv = {}, {}, {}
            for a in two:
                for k in two:
                    vv[a, k], vs[a, k] = at_points(vz[a, 0][k], vz[a, 1][k])
                sv[a], unused = at_points(sz[a, 0], sz[a, 1])
            dx, dy, dz = {}, {}, {}
            for k in two:
                for j in two:
                    dx[j, k] = (vv[1, k][j] - vv[0, k][j]) * (1.0 / element_span)
                line, unused = at_points(vs[0, k], vs[1, k])
                for h in two:
                    dy[h, k] = line[h]
            for j in two:
                line, unused = at_points(sv[0][j], sv[1][j])
                for h in two:
                    dz[h, j] = line[h]
            grads.append((dx, dy, dz))
        weight = element_span**2 / 8.0
        scaled = weight * stiffness
        sums = [({}, {}, {}) for i in range(3)]

        def add(table, key, value):
            table[key] = table[key] + value if key in table else value

        for h in two:
            for j in two:
                for k in two:
                    deform = [
                        [grads[i][0][j, k], grads[i][1][h, k], grads[i][2][h, j]]
                        for i in range(3)
                    ]
                    for i in range(3):
                        deform[i][i] = deform[i][i] + 1.0
                    stress = point_stress(deform)
                    for i in range(3):
                        add(sums[i][0], (j, k), stress[i][0])
                        add(sums[i][1], (h, k), stress[i][1])
                        add(sums[i][2], (h, j), stress[i][2])

        forces = []
        for i in range(3):
            part = {}
            qx, qy, qz = sums[i]
            along_z = [ends_of(qx[j, 0], qx[j, 1]) for j in two]
            for c in two:
                line = ends_of(along_z[0][c], along_z[1][c])
                for b in two:
                    part[0, b, c] = -line[b]
                    part[1, b, c] = line[b]
            along_z = [ends_of(qy[h, 0], qy[h, 1]) for h in two]
            for c in two:
                line = ends_of(along_z[0][c], along_z[1][c])
                for a in two:
                    part[a, 0, c] = part[a, 0, c] - line[a]
                    part[a, 1, c] = part[a, 1, c] + line[a]
            along_y = [ends_of(qz[h, 0], qz[h, 1]) for h in two]
            for b in two:
                line = ends_of(along_y[0][b], along_y[1][b])
                for a in two:
                    part[a, b, 0] = part[a, b, 0] - line[a]
                    part[a, b, 1] = part[a, b, 1] + line[a]
            forces.append(self.assemble({key: scaled * value for key, value in part.items()}))
        return forces


def window_pair(slab, first_layer, own_layers, fetch):
    found = []
    for parity in range(2):
        layer = first_layer + parity
        device = layer // own_layers
        layer = layer - device * own_layers
        found.append((device, layer // 2, layer % 2))
    values = [fetch(device, q) for device, q, parity in found]
    if found[0][:2] == found[1][:2] or (values[0] is None and values[1] is None):
        return values[0]
    for parity in range(2):
        if values[parity] is None:
            values[parity] = jnp.zeros_like(values[1 - parity])
        elif found[parity][2] != parity:
            values[parity] = slab.lanes(values[parity], 2 * parity - 1)
    lane = lax.broadcasted_iota(jnp.int32, values[0].shape, 1)
    return jnp.where(lane % 2 == 0, values[0], values[1])


def first_sources(own_layers):
    return list(range(-BEFORE // own_layers, (own_layers + BEFORE - 1) // own_layers + 1))


def whole_pairs(own_layers):
    return own_layers == 4


def turn_rows(block, mixed, turned, width, at):
    for tile in range(SENT // 128):
        n = at * (SENT // 128) + tile
        for m in range(width // 4):
            first = 12 * m + 4 * tile
            mixed[n, 4 * m : 4 * m + 4, :] = block[first : first + 4, :]
        turned[at, 128 * tile : 128 * tile + 128, :] = mixed[n].T


def regroup(slab, field, rows):
    values, hard = [], None
    for i in range(3):
        parts = [rows(24 * i + 8 * n) for n in range(3)]
        if field == 0 and i == 0:
            hard = parts[0][TWIN : TWIN + 1]
        parts[0] = jnp.where(slab.row == TWIN, pltpu.roll(parts[0], TWIN, 0), parts[0])
        parts.append(jnp.where(slab.row < 4, 0.0, rows(68 + 4 * i)))
        whole = jnp.concatenate(parts, 0)
        values.append(whole * slab.keep if field == 0 else whole)
    return values, hard


def layer_above(slab, turned, at, i):
    first = NEXT_COLUMN + 12 * i
    low, high = turned[at, first : first + 8, :], turned[at, first + 4 : first + 12, :]
    high = jnp.where(slab.row < 4, pltpu.roll(high, 4, 0), 0.0)
    low = jnp.where(slab.row == TWIN, pltpu.roll(low, TWIN, 0), low)
    nothing = jnp.zeros_like(low)
    return jnp.concatenate([low, nothing, high, nothing], 0) * slab.keep


def make_own_kernel(width, across, own_layers):
    own_pairs = own_layers // 2
    pairs = list(range(own_pairs))

    def own_kernel(block, spread, collect, u, f, stiff, forces, moved, mixed, turned):
        slab = Slab(width, across)
        turn_rows(block, mixed, turned, width, 0)
        for pair in pairs:
            for field, target in enumerate((u, f)):

                def rows(start, field=field, pair=pair):
                    at = BLOCK * (2 * pair + field) + start
                    return turned[0, at : at + 8, :]

                values, hard = regroup(slab, field, rows)
                for i in range(3):
                    target[i, pair] = values[i]
                if field == 0:
                    stiff[pair : pair + 1, :] = hard
        for i in range(3):
            u[i, own_pairs] = layer_above(slab, turned, 0, i)

        def finish(pair, total):
            for i in range(3):
                forces[i, pair] = total[i]

        carry = slab.run(u, stiff, spread, collect, [(0, own_pairs, finish)])
        for i in range(3):
            moved[i, 0] = carry[i][0]
            moved[i, 1] = carry[i][1]

    return own_kernel


def make_first_kernel(width, across, own_layers, fine_bound):
    own = BEFORE // 2
    own_pairs = (own_layers + 1) // 2
    spans = []
    prepared = whole_pairs(own_layers)
    for n in (4, 3, 2, 1):
        low, high = BEFORE - n, BEFORE + own_layers + n - 1 + prepared
        spans.append((low // 2, (high + 1) // 2 - low // 2))
    sources = [n for n in first_sources(own_layers) if n or not prepared]

    def first_kernel(*refs):
        arrived = refs[: len(sources)]
        refs = refs[len(sources) :]
        if prepared:
            own_u, own_f, own_stiff, own_forces, own_moved = refs[:5]
            refs = refs[5:]
        spread, collect, transfer, message, *sent, f, u, d, stiff, shares, mixed, turned = refs
        slab = Slab(width, across)
        u[...] = jnp.zeros(u.shape, jnp.float32)
        if not prepared:
            f[...] = jnp.zeros(f.shape, jnp.float32)
        shares[...] = jnp.zeros(shares.shape, jnp.float32)
        stiff[...] = jnp.zeros(stiff.shape, jnp.float32)
        for n in range(len(sources)):
            turn_rows(arrived[n], mixed, turned, width, n)
        for pair in range(PAIRS):
            if prepared and own <= pair < own + own_pairs:
                for i in range(3):
                    u[i, pair] = own_u[i, pair - own]
                    f[i, pair] = own_f[i, pair - own]
                stiff[pair : pair + 1, :] = own_stiff[pair - own : pair - own + 1, :]
                continue
            for field, target in enumerate((u, f)):

                def rows(start, field=field, pair=pair):
                    def fetch(device, q):
                        if device not in sources:
                            return None
                        at = BLOCK * (2 * q + field) + start
                        return turned[sources.index(device), at : at + 8, :]

                    value = window_pair(slab, 2 * pair - BEFORE, own_layers, fetch)
                    return jnp.zeros((8, width), jnp.float32) if value is None else value

                values, hard = regroup(slab, field, rows)
                for i in range(3):
                    target[i, pair] = values[i]
                if field == 0:
                    stiff[pair : pair + 1, :] = hard
        given = None
        if prepared:
            for i in range(3):
                u[i, PAIRS] = layer_above(slab, turned, sources.index(1), i)
            given = (
                list(range(own, own + own_pairs)),
                [[own_forces[i, q] for i in range(3)] for q in range(own_pairs)],
                [(own_moved[i, 0], own_moved[i, 1]) for i in range(3)],
            )

        weights = [jnp.broadcast_to(transfer[:, n : n + 1], (32, width)) for n in range(8)]

        def restrict(pair, forces):
            for i in range(3):
                rest = slab.keep * (f[i, pair] - forces[i])
                for n in range(8):
                    part = rest * weights[n]
                    part = (part[0:8] + part[8:16]) + (part[16:24] + part[24:32])
                    shares[i, n, pl.ds(pair, 1), :] = jnp.sum(part, axis=0, keepdims=True)

        jobs = slab.smoothing(u, f, 0, d, spans[0:3], fine_bound)
        slab.run(u, stiff, spread, collect, jobs + [(*spans[3], restrict)], given)

        restricted = [
            slab.assemble({corner: shares[i, n] for n, corner in enumerate(CORNERS)})
            for i in range(3)
        ]
        def line(rows, q):
            return rows[own + q : own + q + 1]

        for q in range(own_pairs):
            for i in range(3):
                message[i, q] = u[i, own + q]
                message[i, q, RESTRICTED_SLOT : RESTRICTED_SLOT + 1, :] = line(restricted[i], q)
            message[0, q, STIFF_SLOT : STIFF_SLOT + 1, :] = line(stiff, q)
        if prepared:
            down, up = sent
            for i in range(3):
                down[i, 0:32] = u[i, own]
                down[i, 32:40] = u[i, own + 1, 0:8, :]
                down[i, 40:48] = u[i, own + 1, 16:24, :]
                up[i] = u[i, own + 1]
                for n, row in enumerate(
                    (line(restricted[i], 0), line(restricted[i], 1), u[i, own + 2, 0:1, :])
                    + (line(restricted[i], 2),)
                ):
                    down[i, 24 + n : 25 + n, :] = row
                for n, row in enumerate(
                    (line(restricted[i], 1), line(restricted[i], 0), u[i, own, 0:1, :])
                ):
                    up[i, 24 + n : 25 + n, :] = row
            for q in range(own_pairs):
                down[q, 32 + TWIN : 33 + TWIN, :] = line(stiff, q)
                up[q, TWIN : TWIN + 1, :] = line(stiff, q)
            return
        edge = sent[0]
        for q in range(own_pairs):
            for i in range(3):
                edge[q, i : i + 1, :] = u[i, own + q, 0:1, :]
                edge[q, 3 + i : 4 + i, :] = line(restricted[i], q)
            edge[q, 6:8, :] = jnp.broadcast_to(line(stiff, q), (2, width))

    return first_kernel


def shares_sent(own_layers):
    return own_layers % 2 == 0


def sources_of(own_layers):
    below = 2 if shares_sent(own_layers) else 3
    whole = range(-below // own_layers, (own_layers + 2) // own_layers + 1)
    coarse = range(-(below + 2) // own_layers, (own_layers + 4) // own_layers + 1)
    return list(whole), [n for n in coarse if n not in whole]


def message_line(message, q, n):
    i, slot = ((n, 0), (n - 3, RESTRICTED_SLOT), (0, STIFF_SLOT))[n // 3]
    return message[i, q, slot : slot + 1, :]


def sent_readers(slab, up, message, down):
    def block_of(device, q, i):
        if device == 0:
            return message[i, q]
        if (device, q) == (1, 0):
            whole = down[i, 0:32]
        elif (device, q) == (1, 1):
            low, high = down[i, 32:40], down[i, 40:48]
            low = jnp.where(slab.row == TWIN, pltpu.roll(low, TWIN, 0), low)
            whole = jnp.concatenate([low, jnp.zeros_like(low), high, jnp.zeros_like(low)], 0)
        elif (device, q) == (-1, 1):
            low = up[i, 0:8]
            low = jnp.where(slab.row == TWIN, pltpu.roll(low, TWIN, 0), low)
            whole = jnp.concatenate([low, up[i, 8:32]], 0)
        else:
            return None
        return whole

    def line_of(device, q, n):
        if device == 0:
            return message_line(message, q, n)
        kind, i = n // 3, n % 3
        if device == 1:
            row = ((0, 24), (32, 25))[q][kind] if kind < 2 else 32 + TWIN
            i = i if kind < 2 else q
            return down[i, row : row + 1, :]
        if device == -1:
            row = ((26, 25), (0, 24))[q][kind] if kind < 2 else TWIN
            i = i if kind < 2 else q
            return up[i, row : row + 1, :]
        if (device, q) == (2, 0) and kind < 2:
            return down[i, 26 + kind : 27 + kind, :]
        return None

    return block_of, line_of


def make_second_kernel(width, across, own_layers, fine_bound, coarse_bound):
    own = BEFORE_B // 2
    own_pairs = (own_layers + 1) // 2
    shift = (BEFORE - BEFORE_B) // 2
    whole, outer = sources_of(own_layers)
    steps = chebyshev_steps()
    spans = []
    for n in (3, 2, 1):
        low, high = BEFORE_B - n + shares_sent(own_layers), BEFORE_B + own_layers + n - 1
        spans.append((low // 2, (high + 1) // 2 - low // 2))

    def second_kernel(*refs):
        slab = Slab(width, across)
        if whole_pairs(own_layers):
            up, message, down = refs[:3]
            refs = refs[3:]
            block_of, line_of = sent_readers(slab, up, message, down)
        else:
            messages = dict(zip(whole, refs))
            edges = dict(zip(outer, refs[len(whole) :]))
            refs = refs[len(whole) + len(outer) :]

            def block_of(device, q, i):
                return messages[device][i, q] if device in messages else None

            def line_of(device, q, n):
                if device in messages:
                    return message_line(messages[device], q, n)
                return edges[device][q, n : n + 1, :] if device in edges else None

        f, spread, collect, transfer_back, out, u, d, stiff, coarse = refs

        def pair_of(pair, fetch):
            return window_pair(slab, 2 * pair - BEFORE_B, own_layers, fetch)

        u[...] = jnp.zeros(u.shape, jnp.float32)
        coarse[...] = jnp.zeros(coarse.shape, jnp.float32)
        d[...] = jnp.zeros(d.shape, jnp.float32)
        for pair in range(PAIRS_B):
            for i in range(3):
                block = pair_of(pair, lambda device, q: block_of(device, q, i))
                if block is not None:
                    u[i, pair] = block
            for n in range(7):
                line = pair_of(pair, lambda device, q: line_of(device, q, n))
                if line is not None:
                    coarse[n, pair : pair + 1, :] = line
        stiff[...] = coarse[6]

        stiffness = coarse[6]
        keep_coarse = jnp.where(slab.bottom, 0.0, 1.0)
        start = [coarse[i] for i in range(3)]
        restricted = [coarse[3 + i] for i in range(3)]
        before = slab.coarse_force(start, stiffness)
        move = [(steps[0][1] / coarse_bound) * keep_coarse * restricted[i] for i in range(3)]
        level = [start[i] + move[i] for i in range(3)]
        for held, added in steps[1:]:
            force = slab.coarse_force(level, stiffness)
            for i in range(3):
                z = keep_coarse * (restricted[i] + before[i] - force[i])
                move[i] = held * move[i] + (added / coarse_bound) * z
                level[i] = level[i] + move[i]

        weights = [jnp.broadcast_to(transfer_back[:, n : n + 1], (32, width)) for n in range(8)]
        for i in range(3):
            change = slab.corners_of(level[i] - start[i])
            for pair in range(spans[0][0], min(spans[0][0] + spans[0][1] + 1, PAIRS_B)):
                lift = u[i, pair]
                for n, corner in enumerate(CORNERS):
                    lift = lift + weights[n] * change[corner][pair : pair + 1]
                u[i, pair] = lift

        jobs = slab.smoothing(u, f, shift, d, spans, fine_bound)
        owed = slab.owed(slab.run(u, stiff, spread, collect, jobs), fine_bound)

        lower = lax.broadcasted_iota(jnp.int32, (width // 8, 8, 128), 1) < 4
        nothing = jnp.zeros((8, width), jnp.float32)
        sides = []
        for q in range(2):
            if q or not shares_sent(own_layers):
                owed = [(nothing, nothing)] * 3
            rows = []
            for i in range(3):
                value = u[i, own + q]
                rows += [value[0:24], jnp.where(slab.row < 4, owed[i][1], value[24:32])]
            rows += [owed[i][0] for i in range(3)]
            rows += [level[i][own + q : own + q + 1] for i in range(3)] + [nothing[0:5]]
            sides.append(jnp.concatenate(rows, 0).T.reshape(width // 8, 8, 128))
        out[:, 0] = jnp.where(lower, sides[0], pltpu.roll(sides[1], 4, 1))
        out[:, 1] = jnp.where(lower, pltpu.roll(sides[0], 4, 1), sides[1])

    return second_kernel


def solution(mesh):
    rows_of, columns_of = mesh.shape["gx"], mesh.shape["gy"]
    devices = rows_of * columns_of
    order = ring_order(rows_of, columns_of)
    own_layers = EZ // devices
    own_pairs = (own_layers + 1) // 2
    width = 4 * devices
    across = 2 * rows_of
    near = first_sources(own_layers)
    prepared = whole_pairs(own_layers)
    whole, outer = sources_of(own_layers)
    spread, collect, fine_bound = element_tables()
    coarse_bound = build_tables([0.0, 1.0], 2)[2]
    transfer, transfer_back = transfer_table()
    wide = pltpu.CompilerParams(vmem_limit_bytes=60 * 1024 * 1024)
    limit = pltpu.CompilerParams(vmem_limit_bytes=48 * 1024 * 1024)
    f32 = jnp.float32

    pack = pl.pallas_call(
        functools.partial(pack_kernel, order),
        out_shape=jax.ShapeDtypeStruct((devices * 12, 128), f32),
        in_specs=[pl.BlockSpec(memory_space=pl.ANY)] * 5,
        out_specs=pl.BlockSpec(memory_space=pltpu.VMEM),
        scratch_shapes=[
            pltpu.VMEM((3, 6, 3, 384), f32),
            pltpu.VMEM((3, 6, 3, 384), f32),
            pltpu.VMEM((2, 1, EZ), f32),
            pltpu.VMEM((1, 1, 192), jnp.int32),
            pltpu.VMEM((384, 512), jnp.bfloat16),
            pltpu.VMEM((128, 384), f32),
            pltpu.VMEM((384, 128), f32),
            pltpu.VMEM((6, 136, 128), f32),
            pltpu.SemaphoreType.DMA((5,)),
        ],
        compiler_params=wide,
    )
    own = pl.pallas_call(
        make_own_kernel(width, across, own_layers),
        out_shape=(
            jax.ShapeDtypeStruct((3, own_pairs + 1, 32, width), f32),
            jax.ShapeDtypeStruct((3, own_pairs, 32, width), f32),
            jax.ShapeDtypeStruct((own_pairs, width), f32),
            jax.ShapeDtypeStruct((3, own_pairs, 32, width), f32),
            jax.ShapeDtypeStruct((3, 2, 8, width), f32),
        ),
        scratch_shapes=[
            pltpu.VMEM((SENT // 128, width, 128), f32),
            pltpu.VMEM((1, SENT, width), f32),
        ],
        compiler_params=limit,
        cost_estimate=pl.CostEstimate(flops=400_000_000, bytes_accessed=1_000_000, transcendentals=0),
    )
    sent = [jax.ShapeDtypeStruct((own_pairs, 8, width), f32)]
    if prepared:
        sent = [jax.ShapeDtypeStruct((3, rows, width), f32) for rows in (48, 32)]
    first = pl.pallas_call(
        make_first_kernel(width, across, own_layers, fine_bound),
        out_shape=(
            jax.ShapeDtypeStruct((3, own_pairs, 32, width), f32),
            *sent,
            jax.ShapeDtypeStruct((3, PAIRS, 32, width), f32),
        ),
        scratch_shapes=[
            pltpu.VMEM((3, 8, 32, width), f32),
            pltpu.VMEM((3, 8, 32, width), f32),
            pltpu.VMEM((8, width), f32),
            pltpu.VMEM((3, 8, 8, width), f32),
            pltpu.VMEM((len(near) * (SENT // 128), width, 128), f32),
            pltpu.VMEM((len(near), SENT, width), f32),
        ],
        compiler_params=limit,
    )
    second = pl.pallas_call(
        make_second_kernel(width, across, own_layers, fine_bound, coarse_bound),
        out_shape=jax.ShapeDtypeStruct((devices // 2, 2, 8, 128), f32),
        scratch_shapes=[
            pltpu.VMEM((3, PAIRS_B + 2, 32, width), f32),
            pltpu.VMEM((3, PAIRS_B, 32, width), f32),
            pltpu.VMEM((PAIRS_B, width), f32),
            pltpu.VMEM((7, PAIRS_B, width), f32),
        ],
        compiler_params=limit,
    )
    unpack = pl.pallas_call(
        functools.partial(unpack_kernel, order),
        out_shape=(
            jax.ShapeDtypeStruct((3, 6, 3, 384), f32),
            jax.ShapeDtypeStruct((3, 2, 1, EZ), f32),
        ),
        scratch_shapes=[pltpu.VMEM((2, 128, 128), f32), pltpu.VMEM((384, 128), f32)],
        compiler_params=limit,
    )
    everyone = ("gy", "gx")

    def from_device(block, distance):
        place = {k: m % rows_of * columns_of + m // rows_of for m, k in enumerate(order)}
        route = [(place[(k + distance) % devices], place[k]) for k in range(devices)]
        return lax.ppermute(block, ("gx", "gy"), route)

    def body(initial, forcing, modulus, solid_list):
        sent = pack(initial, forcing, modulus, solid_list, jnp.asarray(pack_table()))
        sent = sent.reshape(devices, SENT // 128, 4, 128)
        arrived = lax.all_to_all(sent, everyone, 0, 0, tiled=True).reshape(devices * 12, 128)
        blocks = [from_device(arrived, n) if n else arrived for n in near]
        if prepared:
            blocks = [block for n, block in zip(near, blocks) if n]
            blocks += own(arrived, jnp.asarray(spread), jnp.asarray(collect))
        message, *edges, load = first(
            *blocks,
            jnp.asarray(spread),
            jnp.asarray(collect),
            jnp.asarray(transfer),
        )
        if prepared:
            down, up = edges
            messages = [from_device(up, -1), message, from_device(down, 1)]
        else:
            messages = [from_device(message, n) if n else message for n in whole]
            messages += [from_device(edges[0], n) for n in outer]
        result = second(
            *messages,
            load,
            jnp.asarray(spread),
            jnp.asarray(collect),
            jnp.asarray(transfer_back),
        )
        back = lax.all_to_all(result.reshape(devices, 8, 128), everyone, 0, 0, tiled=True)
        return unpack(back, jnp.asarray(unpack_table()))

    placed = (
        P(None, "gx", "gy", None),
        P(None, "gx", "gy", None),
        P("gx", "gy", None),
        P("gx", "gy", None),
    )
    return jax.shard_map(
        body,
        mesh=mesh,
        in_specs=placed,
        out_specs=(P(None, "gx", "gy", None), P(None, "gx", "gy", None)),
        check_vma=False,
    )
```

```python
import functools
import math

import jax
import jax.numpy as jnp
import numpy as np
from jax import lax
from jax.experimental import pallas as pl
from jax.experimental.pallas import tpu as pltpu
from jax.sharding import PartitionSpec as P

CHEB = 3
EZ = 128

element_span = 20.0
lame_ratio = 4.0
rest_ratio = 1.25
modulus_top = 2.0
spectrum_floor = 0.05
interval_centre = (1.0 + spectrum_floor) / 2.0
interval_radius = (1.0 - spectrum_floor) / 2.0
interval_ratio = interval_centre / interval_radius
inner_anchors = (0.5 - 0.5 / math.sqrt(5.0), 0.5 + 0.5 / math.sqrt(5.0))

BEFORE = 4
PAIRS = 6
BEFORE_B = 6
PAIRS_B = 8
BLOCK = 84
SENT = 384

SLOTS = [
    (0, 0, 0), (1, 0, 0), (2, 0, 0), (0, 1, 0), (0, 2, 0), (0, 0, 1), (0, 0, 2), None,
    (0, 1, 1), (0, 1, 2), (0, 2, 1), (0, 2, 2), (1, 0, 1), (1, 0, 2), (2, 0, 1), (2, 0, 2),
    (1, 1, 0), (1, 2, 0), (2, 1, 0), (2, 2, 0), (1, 1, 1), (1, 1, 2), (1, 2, 1), (1, 2, 2),
    None, None, None, None, (2, 1, 1), (2, 1, 2), (2, 2, 1), (2, 2, 2),
]
TWIN = 7
NEXT_SLOTS = [0, 1, 2, 3, 4, 5, 6, 7, 16, 17, 18, 19]
NEXT_COLUMN = 4 * BLOCK
RESTRICTED_SLOT = 24
STIFF_SLOT = 25
OWN_SHIFT, SHIFT_X, SHIFT_Y, SHIFT_Z = (0, 0, 0), (1, 0, 0), (0, 1, 0), (0, 0, 1)
ELEMENT_ROWS = (
    [(slot, OWN_SHIFT) for slot in range(24)]
    + [(slot, SHIFT_Z) for slot in range(16, 20)]
    + [(slot, OWN_SHIFT) for slot in range(28, 32)]
    + [(slot, SHIFT_X) for slot in range(7)] + [None]
    + [(slot, SHIFT_Y) for slot in range(7)] + [(0, (0, 1, 1))]
    + [(slot, SHIFT_Z) for slot in range(7)] + [(0, (1, 0, 1))]
    + [(slot, SHIFT_X) for slot in range(8, 12)] + [(slot, SHIFT_Y) for slot in range(12, 16)]
    + [(0, (1, 1, 1)), (1, (0, 1, 1)), (2, (0, 1, 1)), (3, (1, 0, 1)), (4, (1, 0, 1))]
    + [(5, (1, 1, 0)), (6, (1, 1, 0)), (0, (1, 1, 0))]
)
ROWS = len(ELEMENT_ROWS)
DEPTH = 80
CORNERS = [(a, b, c) for a in range(2) for b in range(2) for c in range(2)]


def gauss_rule(point_count):
    if point_count == 2:
        offset = 1.0 / math.sqrt(3.0)
        points = [-offset, offset]
        weights = [1.0, 1.0]
    else:
        inner = math.sqrt(3.0 / 7.0 - 2.0 / 7.0 * math.sqrt(6.0 / 5.0))
        outer = math.sqrt(3.0 / 7.0 + 2.0 / 7.0 * math.sqrt(6.0 / 5.0))
        heavy = (18.0 + math.sqrt(30.0)) / 36.0
        light = (18.0 - math.sqrt(30.0)) / 36.0
        points = [-outer, -inner, inner, outer]
        weights = [light, heavy, heavy, light]
    return (np.array(points), np.array(weights))


def lagrange_tables(anchors, samples):
    values = np.zeros((len(samples), len(anchors)))
    slopes = np.zeros((len(samples), len(anchors)))
    for sample_index, sample in enumerate(samples):
        for anchor_index, anchor in enumerate(anchors):
            others = [
                location
                for location_index, location in enumerate(anchors)
                if location_index != anchor_index
            ]
            product = 1.0
            for location in others:
                product = product * (sample - location) / (anchor - location)
            values[sample_index, anchor_index] = product
            derivative = 0.0
            for skipped in range(len(others)):
                summand = 1.0 / (anchor - others[skipped])
                for kept_index in range(len(others)):
                    if kept_index != skipped:
                        summand = (
                            summand * (sample - others[kept_index]) / (anchor - others[kept_index])
                        )
                derivative = derivative + summand
            slopes[sample_index, anchor_index] = derivative
    return (values, slopes)


def outer_three(first, second, third):
    return (
        first[:, None, None, :, None, None]
        * second[None, :, None, None, :, None]
        * third[None, None, :, None, None, :]
    )


def build_tables(anchors, point_count):
    raw_points, raw_weights = gauss_rule(point_count)
    samples = (raw_points + 1.0) / 2.0
    weights = raw_weights / 2.0
    basis_values, slopes = lagrange_tables(anchors, samples)
    quad_total = point_count**3
    nodal_count = len(anchors) ** 3
    derivative_one = outer_three(slopes, basis_values, basis_values).reshape(
        quad_total, nodal_count
    )
    derivative_two = outer_three(basis_values, slopes, basis_values).reshape(
        quad_total, nodal_count
    )
    derivative_three = outer_three(basis_values, basis_values, slopes).reshape(
        quad_total, nodal_count
    )
    stacked = np.stack([derivative_one, derivative_two, derivative_three]) / element_span
    volume = (weights[:, None, None] * weights[None, :, None] * weights[None, None, :]).reshape(
        -1
    ) * element_span**3
    forward = stacked.reshape(3 * quad_total, nodal_count)
    backward = (stacked * volume[None, :, None]).reshape(3 * quad_total, nodal_count).T
    weighted = stacked * volume[None, :, None]
    laplace = weighted[0].T @ stacked[0] + weighted[1].T @ stacked[1] + weighted[2].T @ stacked[2]
    matrix = np.zeros((nodal_count, 3, nodal_count, 3))
    for first in range(3):
        for second in range(3):
            block = weighted[second].T @ stacked[first] + (lame_ratio - 1.0) * (
                weighted[first].T @ stacked[second]
            )
            if first == second:
                block = block + laplace
            matrix[:, first, :, second] = block
    matrix = matrix.reshape(3 * nodal_count, 3 * nodal_count)
    vector = 1.5 + np.cos(1.3 * np.arange(3 * nodal_count))
    for repeat in range(200):
        vector = matrix @ vector
        vector = vector / np.sqrt(vector @ vector)
    largest = vector @ (matrix @ vector)
    return (forward, backward, float(4.0 * modulus_top * 1.1 * largest))


def row_nodes():
    nodes = []
    for entry in ELEMENT_ROWS:
        slot = SLOTS[entry[0]] if entry else None
        if slot is None or any(s and n for s, n in zip(entry[1], slot)):
            nodes.append(None)
        else:
            a, b, c = (3 * s + n for s, n in zip(entry[1], slot))
            nodes.append(16 * a + 4 * b + c)
    return nodes


def halves(matrix):
    whole = np.asarray(matrix, np.float32)
    high = whole.astype(jnp.bfloat16)
    low = (whole - high.astype(np.float32)).astype(jnp.bfloat16)
    return high, low


def element_tables():
    forward, backward, bound = build_tables([0.0, inner_anchors[0], inner_anchors[1], 1.0], 4)
    spread = np.zeros((forward.shape[0], DEPTH))
    collect = np.zeros((ROWS, backward.shape[1]))
    for row, node in enumerate(row_nodes()):
        if node is not None:
            spread[:, row] = forward[:, node]
            collect[row, :] = backward[node, :]
    spread_high, spread_low = halves(spread)
    collect_high, collect_low = halves(collect)
    return (
        np.concatenate([spread_high, spread_high, spread_low], 1),
        np.concatenate([collect_high, collect_low], 0),
        bound,
    )


def transfer_table():
    table = np.zeros((8, 32))
    reach = (0.0, inner_anchors[0], inner_anchors[1])
    for row, corner in enumerate(CORNERS):
        for column, slot in enumerate(SLOTS):
            if slot is not None:
                weight = 1.0
                for side, node in zip(corner, slot):
                    weight = weight * (reach[node] if side else 1.0 - reach[node])
                table[row, column] = weight
    back = table.T.copy()
    back[TWIN] = back[0]
    return table.T.astype(np.float32), back.astype(np.float32)


def chebyshev_steps():
    steps = [(0.0, 1.0 / interval_centre)]
    ratio_now = 1.0 / interval_ratio
    for sweep in range(1, CHEB):
        ratio_next = 1.0 / (2.0 * interval_ratio - ratio_now)
        steps.append((ratio_next * ratio_now, 2.0 * ratio_next / interval_radius))
        ratio_now = ratio_next
    return steps


def stack_row(field, component, layer, b):
    return field * 54 + component * 18 + layer * 3 + b


def block_column(component, slot):
    return 72 + 4 * component + slot - 28 if slot >= 24 else 24 * component + slot


def pack_table():
    table = np.zeros((3, 128, 2, 2, 128), np.float32)
    for field in range(2):
        for x in range(2):
            for component in range(3):
                for column, slot in enumerate(SLOTS):
                    if slot is not None:
                        a, b, c = slot
                        row = stack_row(field, component, 3 * x + a, b)
                        table[c, row, field, x, block_column(component, column)] = 1.0
                        if field == 0 and column in NEXT_SLOTS:
                            at = BLOCK + 12 * component + NEXT_SLOTS.index(column)
                            table[c, row, 1, x, at] = 1.0
            table[0, 108 + x, 0, x, TWIN] = 1.0
    return table.reshape(384, 512).astype(jnp.bfloat16)


def unpack_table():
    table = np.zeros((2, 128, 4, 128), np.float32)
    for x in range(2):
        for component in range(3):
            for column, slot in enumerate(SLOTS):
                if slot is not None:
                    a, b, c = slot
                    row = stack_row(0, component, 3 * x + a, b)
                    table[x, component * 32 + column, c, row] = 1.0
                    if column < 5:
                        table[x, 96 + 8 * component + column, 3, row] = 1.0
                    if column == 0:
                        table[x, 96 + 8 * component + TWIN, 3, row] = 1.0
                    if 16 <= column < 20:
                        table[x, component * 32 + column + 8, 3, row] = 1.0
            table[x, 120 + component, 0, 54 + 2 * component + x] = 1.0
    return table.reshape(256, 512).astype(jnp.bfloat16)


def pick(values, table):
    count = values.shape[0]
    parts = jnp.dot(
        jnp.concatenate(high_low(values), 0), table, preferred_element_type=jnp.float32
    )
    return parts[:count] + parts[count:]


def ring_order(rows_of, columns_of):
    if (rows_of, columns_of) != (4, 8):
        return list(range(rows_of * columns_of))
    order = []
    for z in range(4):
        for x in range(2):
            for y in range(2):
                chip = (z, 7 - z, 15 - z, 8 + z)[2 * x + y]
                order += [2 * chip, 2 * chip + 1]
    return order


def pack_kernel(
    order,
    initial_at, forcing_at, modulus_at, listing_at, table_at, out,
    initial, forcing, modulus, listing, table, rows, turned, places, ready,
):
    own_layers = EZ // len(order)
    sources = (listing_at, modulus_at, initial_at, forcing_at, table_at)
    copies = [
        pltpu.make_async_copy(source, here, ready.at[n])
        for n, (source, here) in enumerate(
            zip(sources, (listing, modulus, initial, forcing, table))
        )
    ]
    for copy in copies:
        copy.start()
    rows[108:128, :] = jnp.zeros((20, 384), jnp.float32)
    copies[0].wait()
    copies[1].wait()
    listed = listing[0].astype(jnp.float32)
    listed = jnp.concatenate([listed, jnp.full((1, 64), 256.0, jnp.float32)], 1)
    listed = jnp.broadcast_to(listed, (128, 256)).T
    lanes = lax.broadcasted_iota(jnp.int32, (256, 128), 1).astype(jnp.float32)
    row_at = lax.broadcasted_iota(jnp.int32, (128, 128), 0)
    stiff = jnp.zeros((128, 128), jnp.float32)
    for x in range(2):
        hit = jnp.max(jnp.where(listed == lanes + 128.0 * x, 1.0, 0.0), axis=0, keepdims=True)
        stiff = jnp.where(row_at == 108 + x, hit * modulus[x], stiff)
    copies[2].wait()
    copies[3].wait()
    for field, source in enumerate((initial, forcing)):
        for component in range(3):
            for layer in range(6):
                at = stack_row(field, component, layer, 0)
                rows[at : at + 3, :] = source[component, layer]
    for part in range(3):
        span = slice(128 * part, 128 * part + 128)
        turned[span, :] = rows[:, span].T
    picked = [turned[pl.ds(c, 128, stride=3), :] for c in range(3)]
    picked[0] = picked[0] + stiff.T
    copies[4].wait()
    wide = pick(jnp.concatenate(picked, 1), table[...])
    lane = lax.broadcasted_iota(jnp.int32, (128, 128), 1)
    for x in range(2):
        tiles = [None] * (SENT // 128)
        for n in range(4):
            pair, field = n // 2, n % 2
            moved = wide[:, 128 * (2 * field + x) : 128 * (2 * field + x) + 128]
            first = BLOCK * n
            if pair:
                moved = pltpu.roll(moved, 128 - 2 * pair, 0)
            if first % 128:
                moved = pltpu.roll(moved, first % 128, 1)
            for tile in range(first // 128, (first + BLOCK - 1) // 128 + 1):
                before = tiles[tile]
                if before is None:
                    tiles[tile] = moved
                else:
                    tiles[tile] = jnp.where(lane >= first - 128 * tile, moved, before)
        above = wide[:, 128 * (2 + x) : 128 * (2 + x) + 128]
        above = pltpu.roll(pltpu.roll(above, 128 - own_layers, 0), (NEXT_COLUMN - BLOCK) % 128, 1)
        tiles[-1] = jnp.where(lane >= NEXT_COLUMN % 128, above, tiles[-1])
        for tile in range(SENT // 128):
            places[3 * x + tile, 0:128, :] = tiles[tile]
            places[3 * x + tile, 128:136, :] = jnp.zeros((8, 128), jnp.float32)
    for device, k in enumerate(order):
        for tile in range(SENT // 128):
            for x in range(2):
                at = 12 * device + 4 * tile + 2 * x
                out[at : at + 2, :] = places[
                    3 * x + tile, own_layers * k : own_layers * k + 2, :
                ]


def unpack_kernel(order, arrived, table, out, coarse_out, layers, turned):
    devices = arrived.shape[0]
    own_layers = EZ // devices
    for x in range(2):
        for layer in range(own_layers):
            row = (layer // 2) * 4 + x * 2 + layer % 2
            if order == sorted(order):
                layers[x, pl.ds(layer, devices, stride=own_layers), :] = arrived[:, row, :]
                continue
            for device, k in enumerate(order):
                at = own_layers * k + layer
                layers[x, at : at + 1, :] = arrived[device, row : row + 1, :]
    wide = pick(jnp.concatenate([layers[0], layers[1]], 1), table[...])
    shares = pltpu.roll(wide[:, 384:512], own_layers, 0)
    turned[pl.ds(0, 128, stride=3), :] = wide[:, 0:128] + shares
    for c in range(1, 3):
        turned[pl.ds(c, 128, stride=3), :] = wide[:, 128 * c : 128 * c + 128]
    for part in range(3):
        span = slice(128 * part, 128 * part + 128)
        back = turned[span, :].T
        for component in range(3):
            for layer in range(6):
                at = stack_row(0, component, layer, 0)
                out[component, layer, :, span] = back[at : at + 3, :]
    back = wide[:, 0:128].T
    for component in range(3):
        for x in range(2):
            at = 54 + 2 * component + x
            coarse_out[component, x] = back[at : at + 1, :]


def cofactor_rows(deform):
    return [
        [
            deform[(row_at + 1) % 3][(column + 1) % 3] * deform[(row_at + 2) % 3][(column + 2) % 3]
            - deform[(row_at + 1) % 3][(column + 2) % 3]
            * deform[(row_at + 2) % 3][(column + 1) % 3]
            for column in range(3)
        ]
        for row_at in range(3)
    ]


def point_stress(deform):
    cofactors = cofactor_rows(deform)
    jacobian = (
        deform[0][0] * cofactors[0][0]
        + deform[0][1] * cofactors[0][1]
        + deform[0][2] * cofactors[0][2]
    )
    pressure = lame_ratio * (jacobian - rest_ratio)
    return [
        [deform[i][d] + pressure * cofactors[i][d] for d in range(3)] for i in range(3)
    ]


coarse_samples = [0.5 - 0.5 / math.sqrt(3.0), 0.5 + 0.5 / math.sqrt(3.0)]
two = range(2)


def at_points(low, high):
    change = high - low
    return [low + s * change for s in coarse_samples], change * (1.0 / element_span)


def ends_of(first, second):
    high = coarse_samples[0] * first + coarse_samples[1] * second
    return [first + second - high, high]


def high_low(values):
    high = values.astype(jnp.bfloat16)
    return high, (values - high.astype(jnp.float32)).astype(jnp.bfloat16)


def reads(pairs):
    return set(range(pairs[0], pairs[-1] + 2))


def plan_steps(spans):
    plan = []
    for first, count in spans:
        pairs = list(range(first, first + count))
        plan.append([pairs[n : n + 2] for n in range(0, count, 2)])
    for now, later in zip(plan, plan[1:]):
        if reads(later[0]) & set(now[-1]) and len(now[-1]) == 2:
            now[-1:] = [now[-1][:1], now[-1][1:]]
        if reads(later[0]) & set(now[-1]) and len(later[0]) == 2:
            later[:1] = [later[0][:1], later[0][1:]]
    return plan


class Slab:
    def __init__(self, width, across):
        self.width = width
        self.y_step = 2 * across
        lane = lax.broadcasted_iota(jnp.int32, (8, width), 1)
        x = (lane // 2) % across
        self.bottom, self.top, self.even = x == 0, x == across - 1, lane % 2 == 0
        self.row = lax.broadcasted_iota(jnp.int32, (8, width), 0)
        row = lax.broadcasted_iota(jnp.int32, (32, width), 0)
        lane = lax.broadcasted_iota(jnp.int32, (32, width), 1)
        on_face = (row == 0) | ((row >= 3) & (row <= 11))
        self.keep = jnp.where(on_face & ((lane // 2) % across == 0), 0.0, 1.0)

    def lanes(self, v, step):
        return pltpu.roll(v, step % self.width, 1)

    def from_next(self, v, x, y):
        if x or y:
            v = self.lanes(v, -2 * x - self.y_step * y)
        return jnp.where(self.top, 0.0, v) if x else v

    def from_next_z(self, v, ahead, x, y):
        step = -2 * x - self.y_step * y
        v = jnp.where(self.even, self.lanes(v, step - 1), self.lanes(ahead, step + 1))
        return jnp.where(self.top, 0.0, v) if x else v

    def onto_next(self, v, x, y, z=0):
        if x or y or z:
            v = self.lanes(v, 2 * x + self.y_step * y + z)
        return jnp.where(self.bottom, 0.0, v) if x else v

    def gather(self, here, ahead):
        row = self.row
        g0, g1, g2, g3 = here[0:8], here[8:16], here[16:24], here[24:32]
        a0 = ahead[0:8]
        z0, xz = self.from_next_z(g0, a0, 0, 0), self.from_next_z(g0, a0, 1, 0)
        yz, xyz = self.from_next_z(g0, a0, 0, 1), self.from_next_z(g0, a0, 1, 1)
        z2 = self.from_next_z(g2, ahead[16:24], 0, 0)
        edges = jnp.where(row <= 4, xz, self.from_next(g0, 1, 1))
        edges = jnp.where(row == 0, xyz, jnp.where(row <= 2, yz, edges))
        return jnp.concatenate(
            [
                g0,
                g1,
                g2,
                jnp.where(row < 4, z2, g3),
                self.from_next(g0, 1, 0),
                jnp.where(row == 7, yz, self.from_next(g0, 0, 1)),
                jnp.where(row == 7, xz, z0),
                jnp.where(row < 4, self.from_next(g1, 1, 0), self.from_next(g1, 0, 1)),
                edges,
                jnp.zeros_like(g0),
            ],
            0,
        )

    def scatter(self, part, behind):
        row = self.row
        g0, g1, g2, g3, x0, y0, z0, sides, edges = (part[8 * n : 8 * n + 8] for n in range(9))
        last = row == 7
        for_z = jnp.where(last, 0.0, z0)
        for_xz = jnp.where(last, z0, jnp.where((row == 3) | (row == 4), edges, 0.0))
        for_yz = jnp.where(last, y0, jnp.where((row == 1) | (row == 2), edges, 0.0))
        for_xyz = jnp.where(row == 0, edges, 0.0)
        for_xy = jnp.where(row >= 5, edges, 0.0)

        def above(z):
            return (
                self.onto_next(for_z, 0, 0, z)
                + self.onto_next(for_yz, 0, 1, z)
                + self.onto_next(for_xz, 1, 0, z)
                + self.onto_next(for_xyz, 1, 1, z)
            )

        own0 = g0 + self.onto_next(x0, 1, 0) + self.onto_next(jnp.where(last, 0.0, y0), 0, 1)
        own0 = own0 + self.onto_next(for_xy, 1, 1)
        own0 = own0 + jnp.where(self.even, behind[0], above(1))
        own1 = g1 + jnp.where(row < 4, self.onto_next(sides, 1, 0), self.onto_next(sides, 0, 1))
        share2 = jnp.where(self.even, behind[1], self.onto_next(g3, 0, 0, 1))
        own2 = g2 + jnp.where(row < 4, share2, 0.0)
        own3 = jnp.where(row < 4, 0.0, g3)
        moved = (above(-1), self.onto_next(g3, 0, 0, -1))
        return jnp.concatenate([self.twinned(own0), own1, own2, own3], 0), moved

    def twinned(self, v):
        twins = jnp.where(self.row == 7, pltpu.roll(v, 7, 0), 0.0)
        return v + jnp.where(self.row == 0, pltpu.roll(v, 1, 0), twins)

    def absorb(self, total, behind):
        low = self.twinned(jnp.where(self.even, behind[0], 0.0))
        high = jnp.where(self.even & (self.row < 4), behind[1], 0.0)
        return jnp.concatenate(
            [total[0:8] + low, total[8:16], total[16:24] + high, total[24:32]], 0
        )

    def gradient(self, u, spread, pairs):
        parts = [
            high_low(self.gather(u[i, pair], u[i, pair + 1])) for i in range(3) for pair in pairs
        ]
        return jnp.dot(
            spread[...],
            jnp.concatenate([jnp.concatenate([h, l, h], 0) for h, l in parts], 1),
            preferred_element_type=jnp.float32,
        )

    def force(self, gradient, stiff, collect, pairs):
        width, count = self.width, len(pairs)
        rows = 16
        high, low = {}, {}
        for q in range(count):
            for r in range(64 // rows):
                deform = [
                    [
                        gradient[
                            64 * e + rows * r : 64 * e + rows * (r + 1),
                            width * (count * i + q) : width * (count * i + q + 1),
                        ]
                        + (1.0 if i == e else 0.0)
                        for e in range(3)
                    ]
                    for i in range(3)
                ]
                stress = point_stress(deform)
                for i in range(3):
                    for e in range(3):
                        high[e, r, i, q], low[e, r, i, q] = high_low(stress[i][e])

        def whole(part):
            return jnp.concatenate(
                [
                    jnp.concatenate([part[e, r, i, q] for i in range(3) for q in range(count)], 1)
                    for e in range(3)
                    for r in range(64 // rows)
                ],
                0,
            )

        force = jnp.dot(collect[...], whole(high), preferred_element_type=jnp.float32)
        force = force[0:ROWS] + (
            force[ROWS:]
            + jnp.dot(collect[0:ROWS], whole(low), preferred_element_type=jnp.float32)
        )
        stiffness = [stiff[pair : pair + 1, :] for pair in pairs]
        return force * jnp.concatenate(stiffness * 3, 1)

    def run(self, u, stiff, spread, collect, jobs, given=None):
        plan = plan_steps([job[:2] for job in jobs])
        steps = [(pairs, n) for n, chunks in enumerate(plan) for pairs in chunks]
        none = jnp.zeros((8, self.width), jnp.float32)
        ahead, carry, job = None, None, None
        for at, (pairs, n) in enumerate(steps):
            ready = given is not None and n == 0 and pairs == given[0]
            gradient = ahead
            if ahead is None and not ready:
                gradient = self.gradient(u, spread, pairs)
            if not ready:
                ahead = None
            if ahead is None and at + 1 < len(steps):
                later, later_job = steps[at + 1]
                if given is not None and later_job == 0 and later == given[0]:
                    later, later_job = steps[at + 2]
                if later_job == n or not reads(later) & set(pairs):
                    ahead = self.gradient(u, spread, later)
            if job != n:
                carry, job = [(none, none) for i in range(3)], n
            if ready:
                for q, pair in enumerate(pairs):
                    total = given[1][q]
                    if q == 0:
                        total = [self.absorb(total[i], carry[i]) for i in range(3)]
                    jobs[n][2](pair, total)
                carry = list(given[2])
                continue
            force = self.force(gradient, stiff, collect, pairs)
            totals = [[] for pair in pairs]
            for q in range(len(pairs)):
                for i in range(3):
                    lane = (len(pairs) * i + q) * self.width
                    total, carry[i] = self.scatter(force[:, lane : lane + self.width], carry[i])
                    totals[q].append(total)
            for pair, total in zip(pairs, totals):
                jobs[n][2](pair, total)
        return carry

    def smoothing(self, u, f, f_shift, d, spans, bound):
        jobs = []
        for (first, count), (held, added) in zip(spans, chebyshev_steps()):

            def finish(pair, forces, held=held, added=added):
                for i in range(3):
                    z = (added / bound) * self.keep * (f[i, pair + f_shift] - forces[i])
                    move = held * d[i, pair] + z if held else z
                    d[i, pair] = move
                    u[i, pair] = u[i, pair] + move

            jobs.append((first, count, finish))
        return jobs

    def owed(self, carry, bound):
        scale = -chebyshev_steps()[-1][1] / bound
        return [
            (
                scale * jnp.where(self.even, low, 0.0) * self.keep[0:8],
                scale * jnp.where(self.even, high, 0.0) * self.keep[16:24],
            )
            for low, high in carry
        ]

    def corners_of(self, v):
        ahead = pltpu.roll(v, 7, 0)
        found = {}
        for a in range(2):
            for b in range(2):
                found[a, b, 0] = self.from_next(v, a, b)
                found[a, b, 1] = self.from_next_z(v, ahead, a, b)
        return found

    def assemble(self, part):
        here, odd, even = 0.0, 0.0, 0.0
        for a in range(2):
            for b in range(2):
                here = here + self.onto_next(part[a, b, 0], a, b)
                odd = odd + self.onto_next(part[a, b, 1], a, b, 1)
                even = even + self.onto_next(part[a, b, 1], a, b, -1)
        return here + jnp.where(self.even, pltpu.roll(even, 1, 0), odd)

    def coarse_force(self, values, stiffness):
        grads = []
        for i in range(3):
            v = self.corners_of(values[i])
            vz, sz = {}, {}
            for a in two:
                for b in two:
                    vz[a, b], sz[a, b] = at_points(v[a, b, 0], v[a, b, 1])
            vv, vs, sv = {}, {}, {}
            for a in two:
                for k in two:
                    vv[a, k], vs[a, k] = at_points(vz[a, 0][k], vz[a, 1][k])
                sv[a], unused = at_points(sz[a, 0], sz[a, 1])
            dx, dy, dz = {}, {}, {}
            for k in two:
                for j in two:
                    dx[j, k] = (vv[1, k][j] - vv[0, k][j]) * (1.0 / element_span)
                line, unused = at_points(vs[0, k], vs[1, k])
                for h in two:
                    dy[h, k] = line[h]
            for j in two:
                line, unused = at_points(sv[0][j], sv[1][j])
                for h in two:
                    dz[h, j] = line[h]
            grads.append((dx, dy, dz))
        weight = element_span**2 / 8.0
        scaled = weight * stiffness
        sums = [({}, {}, {}) for i in range(3)]

        def add(table, key, value):
            table[key] = table[key] + value if key in table else value

        for h in two:
            for j in two:
                for k in two:
                    deform = [
                        [grads[i][0][j, k], grads[i][1][h, k], grads[i][2][h, j]]
                        for i in range(3)
                    ]
                    for i in range(3):
                        deform[i][i] = deform[i][i] + 1.0
                    stress = point_stress(deform)
                    for i in range(3):
                        add(sums[i][0], (j, k), stress[i][0])
                        add(sums[i][1], (h, k), stress[i][1])
                        add(sums[i][2], (h, j), stress[i][2])

        forces = []
        for i in range(3):
            part = {}
            qx, qy, qz = sums[i]
            along_z = [ends_of(qx[j, 0], qx[j, 1]) for j in two]
            for c in two:
                line = ends_of(along_z[0][c], along_z[1][c])
                for b in two:
                    part[0, b, c] = -line[b]
                    part[1, b, c] = line[b]
            along_z = [ends_of(qy[h, 0], qy[h, 1]) for h in two]
            for c in two:
                line = ends_of(along_z[0][c], along_z[1][c])
                for a in two:
                    part[a, 0, c] = part[a, 0, c] - line[a]
                    part[a, 1, c] = part[a, 1, c] + line[a]
            along_y = [ends_of(qz[h, 0], qz[h, 1]) for h in two]
            for b in two:
                line = ends_of(along_y[0][b], along_y[1][b])
                for a in two:
                    part[a, b, 0] = part[a, b, 0] - line[a]
                    part[a, b, 1] = part[a, b, 1] + line[a]
            forces.append(self.assemble({key: scaled * value for key, value in part.items()}))
        return forces


def window_pair(slab, first_layer, own_layers, fetch):
    found = []
    for parity in range(2):
        layer = first_layer + parity
        device = layer // own_layers
        layer = layer - device * own_layers
        found.append((device, layer // 2, layer % 2))
    values = [fetch(device, q) for device, q, parity in found]
    if found[0][:2] == found[1][:2] or (values[0] is None and values[1] is None):
        return values[0]
    for parity in range(2):
        if values[parity] is None:
            values[parity] = jnp.zeros_like(values[1 - parity])
        elif found[parity][2] != parity:
            values[parity] = slab.lanes(values[parity], 2 * parity - 1)
    lane = lax.broadcasted_iota(jnp.int32, values[0].shape, 1)
    return jnp.where(lane % 2 == 0, values[0], values[1])


def first_sources(own_layers):
    return list(range(-BEFORE // own_layers, (own_layers + BEFORE - 1) // own_layers + 1))


def whole_pairs(own_layers):
    return own_layers == 4


def turn_rows(block, mixed, turned, width, at):
    for tile in range(SENT // 128):
        n = at * (SENT // 128) + tile
        for m in range(width // 4):
            first = 12 * m + 4 * tile
            mixed[n, 4 * m : 4 * m + 4, :] = block[first : first + 4, :]
        turned[at, 128 * tile : 128 * tile + 128, :] = mixed[n].T


def regroup(slab, field, rows):
    values, hard = [], None
    for i in range(3):
        parts = [rows(24 * i + 8 * n) for n in range(3)]
        if field == 0 and i == 0:
            hard = parts[0][TWIN : TWIN + 1]
        parts[0] = jnp.where(slab.row == TWIN, pltpu.roll(parts[0], TWIN, 0), parts[0])
        parts.append(jnp.where(slab.row < 4, 0.0, rows(68 + 4 * i)))
        whole = jnp.concatenate(parts, 0)
        values.append(whole * slab.keep if field == 0 else whole)
    return values, hard


def layer_above(slab, turned, at, i):
    first = NEXT_COLUMN + 12 * i
    low, high = turned[at, first : first + 8, :], turned[at, first + 4 : first + 12, :]
    high = jnp.where(slab.row < 4, pltpu.roll(high, 4, 0), 0.0)
    low = jnp.where(slab.row == TWIN, pltpu.roll(low, TWIN, 0), low)
    nothing = jnp.zeros_like(low)
    return jnp.concatenate([low, nothing, high, nothing], 0) * slab.keep


def make_own_kernel(width, across, own_layers):
    own_pairs = own_layers // 2
    pairs = list(range(own_pairs))

    def own_kernel(block, spread, collect, u, f, stiff, forces, moved, mixed, turned):
        slab = Slab(width, across)
        turn_rows(block, mixed, turned, width, 0)
        for pair in pairs:
            for field, target in enumerate((u, f)):

                def rows(start, field=field, pair=pair):
                    at = BLOCK * (2 * pair + field) + start
                    return turned[0, at : at + 8, :]

                values, hard = regroup(slab, field, rows)
                for i in range(3):
                    target[i, pair] = values[i]
                if field == 0:
                    stiff[pair : pair + 1, :] = hard
        for i in range(3):
            u[i, own_pairs] = layer_above(slab, turned, 0, i)

        def finish(pair, total):
            for i in range(3):
                forces[i, pair] = total[i]

        carry = slab.run(u, stiff, spread, collect, [(0, own_pairs, finish)])
        for i in range(3):
            moved[i, 0] = carry[i][0]
            moved[i, 1] = carry[i][1]

    return own_kernel


def make_first_kernel(width, across, own_layers, fine_bound):
    own = BEFORE // 2
    own_pairs = (own_layers + 1) // 2
    spans = []
    prepared = whole_pairs(own_layers)
    for n in (4, 3, 2, 1):
        low, high = BEFORE - n, BEFORE + own_layers + n - 1 + prepared
        spans.append((low // 2, (high + 1) // 2 - low // 2))
    sources = [n for n in first_sources(own_layers) if n or not prepared]

    def first_kernel(*refs):
        arrived = refs[: len(sources)]
        refs = refs[len(sources) :]
        if prepared:
            own_u, own_f, own_stiff, own_forces, own_moved = refs[:5]
            refs = refs[5:]
        spread, collect, transfer, message, *sent, f, u, d, stiff, shares, mixed, turned = refs
        slab = Slab(width, across)
        u[...] = jnp.zeros(u.shape, jnp.float32)
        if not prepared:
            f[...] = jnp.zeros(f.shape, jnp.float32)
        shares[...] = jnp.zeros(shares.shape, jnp.float32)
        stiff[...] = jnp.zeros(stiff.shape, jnp.float32)
        for n in range(len(sources)):
            turn_rows(arrived[n], mixed, turned, width, n)
        for pair in range(PAIRS):
            if prepared and own <= pair < own + own_pairs:
                for i in range(3):
                    u[i, pair] = own_u[i, pair - own]
                    f[i, pair] = own_f[i, pair - own]
                stiff[pair : pair + 1, :] = own_stiff[pair - own : pair - own + 1, :]
                continue
            for field, target in enumerate((u, f)):

                def rows(start, field=field, pair=pair):
                    def fetch(device, q):
                        if device not in sources:
                            return None
                        at = BLOCK * (2 * q + field) + start
                        return turned[sources.index(device), at : at + 8, :]

                    value = window_pair(slab, 2 * pair - BEFORE, own_layers, fetch)
                    return jnp.zeros((8, width), jnp.float32) if value is None else value

                values, hard = regroup(slab, field, rows)
                for i in range(3):
                    target[i, pair] = values[i]
                if field == 0:
                    stiff[pair : pair + 1, :] = hard
        given = None
        if prepared:
            for i in range(3):
                u[i, PAIRS] = layer_above(slab, turned, sources.index(1), i)
            given = (
                list(range(own, own + own_pairs)),
                [[own_forces[i, q] for i in range(3)] for q in range(own_pairs)],
                [(own_moved[i, 0], own_moved[i, 1]) for i in range(3)],
            )

        weights = [jnp.broadcast_to(transfer[:, n : n + 1], (32, width)) for n in range(8)]

        def restrict(pair, forces):
            for i in range(3):
                rest = slab.keep * (f[i, pair] - forces[i])
                for n in range(8):
                    part = rest * weights[n]
                    part = (part[0:8] + part[8:16]) + (part[16:24] + part[24:32])
                    shares[i, n, pl.ds(pair, 1), :] = jnp.sum(part, axis=0, keepdims=True)

        jobs = slab.smoothing(u, f, 0, d, spans[0:3], fine_bound)
        slab.run(u, stiff, spread, collect, jobs + [(*spans[3], restrict)], given)

        restricted = [
            slab.assemble({corner: shares[i, n] for n, corner in enumerate(CORNERS)})
            for i in range(3)
        ]
        def line(rows, q):
            return rows[own + q : own + q + 1]

        for q in range(own_pairs):
            for i in range(3):
                message[i, q] = u[i, own + q]
                message[i, q, RESTRICTED_SLOT : RESTRICTED_SLOT + 1, :] = line(restricted[i], q)
            message[0, q, STIFF_SLOT : STIFF_SLOT + 1, :] = line(stiff, q)
        if prepared:
            down, up = sent
            for i in range(3):
                down[i, 0:32] = u[i, own]
                down[i, 32:40] = u[i, own + 1, 0:8, :]
                down[i, 40:48] = u[i, own + 1, 16:24, :]
                up[i] = u[i, own + 1]
                for n, row in enumerate(
                    (line(restricted[i], 0), line(restricted[i], 1), u[i, own + 2, 0:1, :])
                    + (line(restricted[i], 2),)
                ):
                    down[i, 24 + n : 25 + n, :] = row
                for n, row in enumerate(
                    (line(restricted[i], 1), line(restricted[i], 0), u[i, own, 0:1, :])
                ):
                    up[i, 24 + n : 25 + n, :] = row
            for q in range(own_pairs):
                down[q, 32 + TWIN : 33 + TWIN, :] = line(stiff, q)
                up[q, TWIN : TWIN + 1, :] = line(stiff, q)
            return
        edge = sent[0]
        for q in range(own_pairs):
            for i in range(3):
                edge[q, i : i + 1, :] = u[i, own + q, 0:1, :]
                edge[q, 3 + i : 4 + i, :] = line(restricted[i], q)
            edge[q, 6:8, :] = jnp.broadcast_to(line(stiff, q), (2, width))

    return first_kernel


def shares_sent(own_layers):
    return own_layers % 2 == 0


def sources_of(own_layers):
    below = 2 if shares_sent(own_layers) else 3
    whole = range(-below // own_layers, (own_layers + 2) // own_layers + 1)
    coarse = range(-(below + 2) // own_layers, (own_layers + 4) // own_layers + 1)
    return list(whole), [n for n in coarse if n not in whole]


def message_line(message, q, n):
    i, slot = ((n, 0), (n - 3, RESTRICTED_SLOT), (0, STIFF_SLOT))[n // 3]
    return message[i, q, slot : slot + 1, :]


def sent_readers(slab, up, message, down):
    def block_of(device, q, i):
        if device == 0:
            return message[i, q]
        if (device, q) == (1, 0):
            whole = down[i, 0:32]
        elif (device, q) == (1, 1):
            low, high = down[i, 32:40], down[i, 40:48]
            low = jnp.where(slab.row == TWIN, pltpu.roll(low, TWIN, 0), low)
            whole = jnp.concatenate([low, jnp.zeros_like(low), high, jnp.zeros_like(low)], 0)
        elif (device, q) == (-1, 1):
            low = up[i, 0:8]
            low = jnp.where(slab.row == TWIN, pltpu.roll(low, TWIN, 0), low)
            whole = jnp.concatenate([low, up[i, 8:32]], 0)
        else:
            return None
        return whole

    def line_of(device, q, n):
        if device == 0:
            return message_line(message, q, n)
        kind, i = n // 3, n % 3
        if device == 1:
            row = ((0, 24), (32, 25))[q][kind] if kind < 2 else 32 + TWIN
            i = i if kind < 2 else q
            return down[i, row : row + 1, :]
        if device == -1:
            row = ((26, 25), (0, 24))[q][kind] if kind < 2 else TWIN
            i = i if kind < 2 else q
            return up[i, row : row + 1, :]
        if (device, q) == (2, 0) and kind < 2:
            return down[i, 26 + kind : 27 + kind, :]
        return None

    return block_of, line_of


def make_second_kernel(width, across, own_layers, fine_bound, coarse_bound):
    own = BEFORE_B // 2
    own_pairs = (own_layers + 1) // 2
    shift = (BEFORE - BEFORE_B) // 2
    whole, outer = sources_of(own_layers)
    steps = chebyshev_steps()
    spans = []
    for n in (3, 2, 1):
        low, high = BEFORE_B - n + shares_sent(own_layers), BEFORE_B + own_layers + n - 1
        spans.append((low // 2, (high + 1) // 2 - low // 2))

    def second_kernel(*refs):
        slab = Slab(width, across)
        if whole_pairs(own_layers):
            up, message, down = refs[:3]
            refs = refs[3:]
            block_of, line_of = sent_readers(slab, up, message, down)
        else:
            messages = dict(zip(whole, refs))
            edges = dict(zip(outer, refs[len(whole) :]))
            refs = refs[len(whole) + len(outer) :]

            def block_of(device, q, i):
                return messages[device][i, q] if device in messages else None

            def line_of(device, q, n):
                if device in messages:
                    return message_line(messages[device], q, n)
                return edges[device][q, n : n + 1, :] if device in edges else None

        f, spread, collect, transfer_back, out, u, d, stiff, coarse = refs

        def pair_of(pair, fetch):
            return window_pair(slab, 2 * pair - BEFORE_B, own_layers, fetch)

        u[...] = jnp.zeros(u.shape, jnp.float32)
        coarse[...] = jnp.zeros(coarse.shape, jnp.float32)
        d[...] = jnp.zeros(d.shape, jnp.float32)
        for pair in range(PAIRS_B):
            for i in range(3):
                block = pair_of(pair, lambda device, q: block_of(device, q, i))
                if block is not None:
                    u[i, pair] = block
            for n in range(7):
                line = pair_of(pair, lambda device, q: line_of(device, q, n))
                if line is not None:
                    coarse[n, pair : pair + 1, :] = line
        stiff[...] = coarse[6]

        stiffness = coarse[6]
        keep_coarse = jnp.where(slab.bottom, 0.0, 1.0)
        start = [coarse[i] for i in range(3)]
        restricted = [coarse[3 + i] for i in range(3)]
        before = slab.coarse_force(start, stiffness)
        move = [(steps[0][1] / coarse_bound) * keep_coarse * restricted[i] for i in range(3)]
        level = [start[i] + move[i] for i in range(3)]
        for held, added in steps[1:]:
            force = slab.coarse_force(level, stiffness)
            for i in range(3):
                z = keep_coarse * (restricted[i] + before[i] - force[i])
                move[i] = held * move[i] + (added / coarse_bound) * z
                level[i] = level[i] + move[i]

        weights = [jnp.broadcast_to(transfer_back[:, n : n + 1], (32, width)) for n in range(8)]
        for i in range(3):
            change = slab.corners_of(level[i] - start[i])
            for pair in range(spans[0][0], min(spans[0][0] + spans[0][1] + 1, PAIRS_B)):
                lift = u[i, pair]
                for n, corner in enumerate(CORNERS):
                    lift = lift + weights[n] * change[corner][pair : pair + 1]
                u[i, pair] = lift

        jobs = slab.smoothing(u, f, shift, d, spans, fine_bound)
        owed = slab.owed(slab.run(u, stiff, spread, collect, jobs), fine_bound)

        lower = lax.broadcasted_iota(jnp.int32, (width // 8, 8, 128), 1) < 4
        nothing = jnp.zeros((8, width), jnp.float32)
        sides = []
        for q in range(2):
            if q or not shares_sent(own_layers):
                owed = [(nothing, nothing)] * 3
            rows = []
            for i in range(3):
                value = u[i, own + q]
                rows += [value[0:24], jnp.where(slab.row < 4, owed[i][1], value[24:32])]
            rows += [owed[i][0] for i in range(3)]
            rows += [level[i][own + q : own + q + 1] for i in range(3)] + [nothing[0:5]]
            sides.append(jnp.concatenate(rows, 0).T.reshape(width // 8, 8, 128))
        out[:, 0] = jnp.where(lower, sides[0], pltpu.roll(sides[1], 4, 1))
        out[:, 1] = jnp.where(lower, pltpu.roll(sides[0], 4, 1), sides[1])

    return second_kernel


def solution(mesh):
    rows_of, columns_of = mesh.shape["gx"], mesh.shape["gy"]
    devices = rows_of * columns_of
    order = ring_order(rows_of, columns_of)
    own_layers = EZ // devices
    own_pairs = (own_layers + 1) // 2
    width = 4 * devices
    across = 2 * rows_of
    near = first_sources(own_layers)
    prepared = whole_pairs(own_layers)
    whole, outer = sources_of(own_layers)
    spread, collect, fine_bound = element_tables()
    coarse_bound = build_tables([0.0, 1.0], 2)[2]
    transfer, transfer_back = transfer_table()
    wide = pltpu.CompilerParams(vmem_limit_bytes=60 * 1024 * 1024)
    limit = pltpu.CompilerParams(vmem_limit_bytes=48 * 1024 * 1024)
    f32 = jnp.float32

    pack = pl.pallas_call(
        functools.partial(pack_kernel, order),
        out_shape=pltpu.VMEM((devices * 12, 128), f32),
        in_specs=[pl.BlockSpec(memory_space=pl.ANY)] * 5,
        out_specs=pl.BlockSpec(memory_space=pltpu.VMEM),
        scratch_shapes=[
            pltpu.VMEM((3, 6, 3, 384), f32),
            pltpu.VMEM((3, 6, 3, 384), f32),
            pltpu.VMEM((2, 1, EZ), f32),
            pltpu.VMEM((1, 1, 192), jnp.int32),
            pltpu.VMEM((384, 512), jnp.bfloat16),
            pltpu.VMEM((128, 384), f32),
            pltpu.VMEM((384, 128), f32),
            pltpu.VMEM((6, 136, 128), f32),
            pltpu.SemaphoreType.DMA((5,)),
        ],
        compiler_params=wide,
    )
    own = pl.pallas_call(
        make_own_kernel(width, across, own_layers),
        out_shape=(
            jax.ShapeDtypeStruct((3, own_pairs + 1, 32, width), f32),
            jax.ShapeDtypeStruct((3, own_pairs, 32, width), f32),
            jax.ShapeDtypeStruct((own_pairs, width), f32),
            jax.ShapeDtypeStruct((3, own_pairs, 32, width), f32),
            jax.ShapeDtypeStruct((3, 2, 8, width), f32),
        ),
        scratch_shapes=[
            pltpu.VMEM((SENT // 128, width, 128), f32),
            pltpu.VMEM((1, SENT, width), f32),
        ],
        compiler_params=limit,
        cost_estimate=pl.CostEstimate(flops=400_000_000, bytes_accessed=1_000_000, transcendentals=0),
    )
    sent = [jax.ShapeDtypeStruct((own_pairs, 8, width), f32)]
    if prepared:
        sent = [jax.ShapeDtypeStruct((3, rows, width), f32) for rows in (48, 32)]
    first = pl.pallas_call(
        make_first_kernel(width, across, own_layers, fine_bound),
        out_shape=(
            jax.ShapeDtypeStruct((3, own_pairs, 32, width), f32),
            *sent,
            jax.ShapeDtypeStruct((3, PAIRS, 32, width), f32),
        ),
        scratch_shapes=[
            pltpu.VMEM((3, 8, 32, width), f32),
            pltpu.VMEM((3, 8, 32, width), f32),
            pltpu.VMEM((8, width), f32),
            pltpu.VMEM((3, 8, 8, width), f32),
            pltpu.VMEM((len(near) * (SENT // 128), width, 128), f32),
            pltpu.VMEM((len(near), SENT, width), f32),
        ],
        compiler_params=limit,
    )
    second = pl.pallas_call(
        make_second_kernel(width, across, own_layers, fine_bound, coarse_bound),
        out_shape=jax.ShapeDtypeStruct((devices // 2, 2, 8, 128), f32),
        scratch_shapes=[
            pltpu.VMEM((3, PAIRS_B + 2, 32, width), f32),
            pltpu.VMEM((3, PAIRS_B, 32, width), f32),
            pltpu.VMEM((PAIRS_B, width), f32),
            pltpu.VMEM((7, PAIRS_B, width), f32),
        ],
        compiler_params=limit,
    )
    unpack = pl.pallas_call(
        functools.partial(unpack_kernel, order),
        out_shape=(
            jax.ShapeDtypeStruct((3, 6, 3, 384), f32),
            jax.ShapeDtypeStruct((3, 2, 1, EZ), f32),
        ),
        scratch_shapes=[pltpu.VMEM((2, 128, 128), f32), pltpu.VMEM((384, 128), f32)],
        compiler_params=limit,
    )
    everyone = ("gy", "gx")

    def from_device(block, distance):
        place = {k: m % rows_of * columns_of + m // rows_of for m, k in enumerate(order)}
        route = [(place[(k + distance) % devices], place[k]) for k in range(devices)]
        return lax.ppermute(block, ("gx", "gy"), route)

    def body(initial, forcing, modulus, solid_list):
        sent = pack(initial, forcing, modulus, solid_list, jnp.asarray(pack_table()))
        sent = sent.reshape(devices, SENT // 128, 4, 128)
        arrived = lax.all_to_all(sent, everyone, 0, 0, tiled=True).reshape(devices * 12, 128)
        blocks = [from_device(arrived, n) if n else arrived for n in near]
        if prepared:
            blocks = [block for n, block in zip(near, blocks) if n]
            blocks += own(arrived, jnp.asarray(spread), jnp.asarray(collect))
        message, *edges, load = first(
            *blocks,
            jnp.asarray(spread),
            jnp.asarray(collect),
            jnp.asarray(transfer),
        )
        if prepared:
            down, up = edges
            messages = [from_device(up, -1), message, from_device(down, 1)]
        else:
            messages = [from_device(message, n) if n else message for n in whole]
            messages += [from_device(edges[0], n) for n in outer]
        result = second(
            *messages,
            load,
            jnp.asarray(spread),
            jnp.asarray(collect),
            jnp.asarray(transfer_back),
        )
        back = lax.all_to_all(result.reshape(devices, 8, 128), everyone, 0, 0, tiled=True)
        return unpack(back, jnp.asarray(unpack_table()))

    placed = (
        P(None, "gx", "gy", None),
        P(None, "gx", "gy", None),
        P("gx", "gy", None),
        P("gx", "gy", None),
    )
    return jax.shard_map(
        body,
        mesh=mesh,
        in_specs=placed,
        out_specs=(P(None, "gx", "gy", None), P(None, "gx", "gy", None)),
        check_vma=False,
    )
```

```python
import functools
import math

import jax
import jax.numpy as jnp
import numpy as np
from jax import lax
from jax.experimental import pallas as pl
from jax.experimental.pallas import tpu as pltpu
from jax.sharding import PartitionSpec as P

CHEB = 3
EZ = 128

element_span = 20.0
lame_ratio = 4.0
rest_ratio = 1.25
modulus_top = 2.0
spectrum_floor = 0.05
interval_centre = (1.0 + spectrum_floor) / 2.0
interval_radius = (1.0 - spectrum_floor) / 2.0
interval_ratio = interval_centre / interval_radius
inner_anchors = (0.5 - 0.5 / math.sqrt(5.0), 0.5 + 0.5 / math.sqrt(5.0))

BEFORE = 4
PAIRS = 6
BEFORE_B = 6
PAIRS_B = 8
BLOCK = 84
SENT = 384

SLOTS = [
    (0, 0, 0), (1, 0, 0), (2, 0, 0), (0, 1, 0), (0, 2, 0), (0, 0, 1), (0, 0, 2), None,
    (0, 1, 1), (0, 1, 2), (0, 2, 1), (0, 2, 2), (1, 0, 1), (1, 0, 2), (2, 0, 1), (2, 0, 2),
    (1, 1, 0), (1, 2, 0), (2, 1, 0), (2, 2, 0), (1, 1, 1), (1, 1, 2), (1, 2, 1), (1, 2, 2),
    None, None, None, None, (2, 1, 1), (2, 1, 2), (2, 2, 1), (2, 2, 2),
]
TWIN = 7
NEXT_SLOTS = [0, 1, 2, 3, 4, 5, 6, 7, 16, 17, 18, 19]
NEXT_COLUMN = 4 * BLOCK
RESTRICTED_SLOT = 24
STIFF_SLOT = 25
OWN_SHIFT, SHIFT_X, SHIFT_Y, SHIFT_Z = (0, 0, 0), (1, 0, 0), (0, 1, 0), (0, 0, 1)
ELEMENT_ROWS = (
    [(slot, OWN_SHIFT) for slot in range(24)]
    + [(slot, SHIFT_Z) for slot in range(16, 20)]
    + [(slot, OWN_SHIFT) for slot in range(28, 32)]
    + [(slot, SHIFT_X) for slot in range(7)] + [None]
    + [(slot, SHIFT_Y) for slot in range(7)] + [(0, (0, 1, 1))]
    + [(slot, SHIFT_Z) for slot in range(7)] + [(0, (1, 0, 1))]
    + [(slot, SHIFT_X) for slot in range(8, 12)] + [(slot, SHIFT_Y) for slot in range(12, 16)]
    + [(0, (1, 1, 1)), (1, (0, 1, 1)), (2, (0, 1, 1)), (3, (1, 0, 1)), (4, (1, 0, 1))]
    + [(5, (1, 1, 0)), (6, (1, 1, 0)), (0, (1, 1, 0))]
)
ROWS = len(ELEMENT_ROWS)
DEPTH = 80
CORNERS = [(a, b, c) for a in range(2) for b in range(2) for c in range(2)]


def gauss_rule(point_count):
    if point_count == 2:
        offset = 1.0 / math.sqrt(3.0)
        points = [-offset, offset]
        weights = [1.0, 1.0]
    else:
        inner = math.sqrt(3.0 / 7.0 - 2.0 / 7.0 * math.sqrt(6.0 / 5.0))
        outer = math.sqrt(3.0 / 7.0 + 2.0 / 7.0 * math.sqrt(6.0 / 5.0))
        heavy = (18.0 + math.sqrt(30.0)) / 36.0
        light = (18.0 - math.sqrt(30.0)) / 36.0
        points = [-outer, -inner, inner, outer]
        weights = [light, heavy, heavy, light]
    return (np.array(points), np.array(weights))


def lagrange_tables(anchors, samples):
    values = np.zeros((len(samples), len(anchors)))
    slopes = np.zeros((len(samples), len(anchors)))
    for sample_index, sample in enumerate(samples):
        for anchor_index, anchor in enumerate(anchors):
            others = [
                location
                for location_index, location in enumerate(anchors)
                if location_index != anchor_index
            ]
            product = 1.0
            for location in others:
                product = product * (sample - location) / (anchor - location)
            values[sample_index, anchor_index] = product
            derivative = 0.0
            for skipped in range(len(others)):
                summand = 1.0 / (anchor - others[skipped])
                for kept_index in range(len(others)):
                    if kept_index != skipped:
                        summand = (
                            summand * (sample - others[kept_index]) / (anchor - others[kept_index])
                        )
                derivative = derivative + summand
            slopes[sample_index, anchor_index] = derivative
    return (values, slopes)


def outer_three(first, second, third):
    return (
        first[:, None, None, :, None, None]
        * second[None, :, None, None, :, None]
        * third[None, None, :, None, None, :]
    )


def build_tables(anchors, point_count):
    raw_points, raw_weights = gauss_rule(point_count)
    samples = (raw_points + 1.0) / 2.0
    weights = raw_weights / 2.0
    basis_values, slopes = lagrange_tables(anchors, samples)
    quad_total = point_count**3
    nodal_count = len(anchors) ** 3
    derivative_one = outer_three(slopes, basis_values, basis_values).reshape(
        quad_total, nodal_count
    )
    derivative_two = outer_three(basis_values, slopes, basis_values).reshape(
        quad_total, nodal_count
    )
    derivative_three = outer_three(basis_values, basis_values, slopes).reshape(
        quad_total, nodal_count
    )
    stacked = np.stack([derivative_one, derivative_two, derivative_three]) / element_span
    volume = (weights[:, None, None] * weights[None, :, None] * weights[None, None, :]).reshape(
        -1
    ) * element_span**3
    forward = stacked.reshape(3 * quad_total, nodal_count)
    backward = (stacked * volume[None, :, None]).reshape(3 * quad_total, nodal_count).T
    weighted = stacked * volume[None, :, None]
    laplace = weighted[0].T @ stacked[0] + weighted[1].T @ stacked[1] + weighted[2].T @ stacked[2]
    matrix = np.zeros((nodal_count, 3, nodal_count, 3))
    for first in range(3):
        for second in range(3):
            block = weighted[second].T @ stacked[first] + (lame_ratio - 1.0) * (
                weighted[first].T @ stacked[second]
            )
            if first == second:
                block = block + laplace
            matrix[:, first, :, second] = block
    matrix = matrix.reshape(3 * nodal_count, 3 * nodal_count)
    vector = 1.5 + np.cos(1.3 * np.arange(3 * nodal_count))
    for repeat in range(200):
        vector = matrix @ vector
        vector = vector / np.sqrt(vector @ vector)
    largest = vector @ (matrix @ vector)
    return (forward, backward, float(4.0 * modulus_top * 1.1 * largest))


def row_nodes():
    nodes = []
    for entry in ELEMENT_ROWS:
        slot = SLOTS[entry[0]] if entry else None
        if slot is None or any(s and n for s, n in zip(entry[1], slot)):
            nodes.append(None)
        else:
            a, b, c = (3 * s + n for s, n in zip(entry[1], slot))
            nodes.append(16 * a + 4 * b + c)
    return nodes


def halves(matrix):
    whole = np.asarray(matrix, np.float32)
    high = whole.astype(jnp.bfloat16)
    low = (whole - high.astype(np.float32)).astype(jnp.bfloat16)
    return high, low


def element_tables():
    forward, backward, bound = build_tables([0.0, inner_anchors[0], inner_anchors[1], 1.0], 4)
    spread = np.zeros((forward.shape[0], DEPTH))
    collect = np.zeros((ROWS, backward.shape[1]))
    for row, node in enumerate(row_nodes()):
        if node is not None:
            spread[:, row] = forward[:, node]
            collect[row, :] = backward[node, :]
    spread_high, spread_low = halves(spread)
    collect_high, collect_low = halves(collect)
    return (
        np.concatenate([spread_high, spread_high, spread_low], 1),
        np.concatenate([collect_high, collect_low], 0),
        bound,
    )


def transfer_table():
    table = np.zeros((8, 32))
    reach = (0.0, inner_anchors[0], inner_anchors[1])
    for row, corner in enumerate(CORNERS):
        for column, slot in enumerate(SLOTS):
            if slot is not None:
                weight = 1.0
                for side, node in zip(corner, slot):
                    weight = weight * (reach[node] if side else 1.0 - reach[node])
                table[row, column] = weight
    back = table.T.copy()
    back[TWIN] = back[0]
    return table.T.astype(np.float32), back.astype(np.float32)


def chebyshev_steps():
    steps = [(0.0, 1.0 / interval_centre)]
    ratio_now = 1.0 / interval_ratio
    for sweep in range(1, CHEB):
        ratio_next = 1.0 / (2.0 * interval_ratio - ratio_now)
        steps.append((ratio_next * ratio_now, 2.0 * ratio_next / interval_radius))
        ratio_now = ratio_next
    return steps


def stack_row(field, component, layer, b):
    return field * 54 + component * 18 + layer * 3 + b


def block_column(component, slot):
    return 72 + 4 * component + slot - 28 if slot >= 24 else 24 * component + slot


def pack_table():
    table = np.zeros((3, 128, 2, 2, 128), np.float32)
    for field in range(2):
        for x in range(2):
            for component in range(3):
                for column, slot in enumerate(SLOTS):
                    if slot is not None:
                        a, b, c = slot
                        row = stack_row(field, component, 3 * x + a, b)
                        table[c, row, field, x, block_column(component, column)] = 1.0
                        if field == 0 and column in NEXT_SLOTS:
                            at = BLOCK + 12 * component + NEXT_SLOTS.index(column)
                            table[c, row, 1, x, at] = 1.0
            table[0, 108 + x, 0, x, TWIN] = 1.0
    return table.reshape(384, 512).astype(jnp.bfloat16)


def unpack_table():
    table = np.zeros((2, 128, 4, 128), np.float32)
    for x in range(2):
        for component in range(3):
            for column, slot in enumerate(SLOTS):
                if slot is not None:
                    a, b, c = slot
                    row = stack_row(0, component, 3 * x + a, b)
                    table[x, component * 32 + column, c, row] = 1.0
                    if column < 5:
                        table[x, 96 + 8 * component + column, 3, row] = 1.0
                    if column == 0:
                        table[x, 96 + 8 * component + TWIN, 3, row] = 1.0
                    if 16 <= column < 20:
                        table[x, component * 32 + column + 8, 3, row] = 1.0
            table[x, 120 + component, 0, 54 + 2 * component + x] = 1.0
    return table.reshape(256, 512).astype(jnp.bfloat16)


def pick(values, table):
    count = values.shape[0]
    parts = jnp.dot(
        jnp.concatenate(high_low(values), 0), table, preferred_element_type=jnp.float32
    )
    return parts[:count] + parts[count:]


def ring_order(rows_of, columns_of):
    if (rows_of, columns_of) != (4, 8):
        return list(range(rows_of * columns_of))
    order = []
    for z in range(4):
        for x in range(2):
            for y in range(2):
                chip = (z, 7 - z, 15 - z, 8 + z)[2 * x + y]
                order += [2 * chip, 2 * chip + 1]
    return order


def pack_kernel(
    order,
    initial_at, forcing_at, modulus_at, listing_at, table_at, out,
    initial, forcing, modulus, listing, table, rows, turned, places, ready,
):
    own_layers = EZ // len(order)
    sources = (listing_at, modulus_at, initial_at, forcing_at, table_at)
    copies = [
        pltpu.make_async_copy(source, here, ready.at[n])
        for n, (source, here) in enumerate(
            zip(sources, (listing, modulus, initial, forcing, table))
        )
    ]
    for copy in copies:
        copy.start()
    rows[108:128, :] = jnp.zeros((20, 384), jnp.float32)
    copies[0].wait()
    copies[1].wait()
    listed = listing[0].astype(jnp.float32)
    listed = jnp.concatenate([listed, jnp.full((1, 64), 256.0, jnp.float32)], 1)
    listed = jnp.broadcast_to(listed, (128, 256)).T
    lanes = lax.broadcasted_iota(jnp.int32, (256, 128), 1).astype(jnp.float32)
    row_at = lax.broadcasted_iota(jnp.int32, (128, 128), 0)
    stiff = jnp.zeros((128, 128), jnp.float32)
    for x in range(2):
        hit = jnp.max(jnp.where(listed == lanes + 128.0 * x, 1.0, 0.0), axis=0, keepdims=True)
        stiff = jnp.where(row_at == 108 + x, hit * modulus[x], stiff)
    copies[2].wait()
    copies[3].wait()
    for field, source in enumerate((initial, forcing)):
        for component in range(3):
            for layer in range(6):
                at = stack_row(field, component, layer, 0)
                rows[at : at + 3, :] = source[component, layer]
    for part in range(3):
        span = slice(128 * part, 128 * part + 128)
        turned[span, :] = rows[:, span].T
    picked = [turned[pl.ds(c, 128, stride=3), :] for c in range(3)]
    picked[0] = picked[0] + stiff.T
    copies[4].wait()
    wide = pick(jnp.concatenate(picked, 1), table[...])
    lane = lax.broadcasted_iota(jnp.int32, (128, 128), 1)
    for x in range(2):
        tiles = [None] * (SENT // 128)
        for n in range(4):
            pair, field = n // 2, n % 2
            moved = wide[:, 128 * (2 * field + x) : 128 * (2 * field + x) + 128]
            first = BLOCK * n
            if pair:
                moved = pltpu.roll(moved, 128 - 2 * pair, 0)
            if first % 128:
                moved = pltpu.roll(moved, first % 128, 1)
            for tile in range(first // 128, (first + BLOCK - 1) // 128 + 1):
                before = tiles[tile]
                if before is None:
                    tiles[tile] = moved
                else:
                    tiles[tile] = jnp.where(lane >= first - 128 * tile, moved, before)
        above = wide[:, 128 * (2 + x) : 128 * (2 + x) + 128]
        above = pltpu.roll(pltpu.roll(above, 128 - own_layers, 0), (NEXT_COLUMN - BLOCK) % 128, 1)
        tiles[-1] = jnp.where(lane >= NEXT_COLUMN % 128, above, tiles[-1])
        for tile in range(SENT // 128):
            places[3 * x + tile, 0:128, :] = tiles[tile]
            places[3 * x + tile, 128:136, :] = jnp.zeros((8, 128), jnp.float32)
    for device, k in enumerate(order):
        for tile in range(SENT // 128):
            for x in range(2):
                at = 12 * device + 4 * tile + 2 * x
                out[at : at + 2, :] = places[
                    3 * x + tile, own_layers * k : own_layers * k + 2, :
                ]


def unpack_kernel(order, arrived, table, out, coarse_out, layers, turned):
    devices = arrived.shape[0]
    own_layers = EZ // devices
    for x in range(2):
        for layer in range(own_layers):
            row = (layer // 2) * 4 + x * 2 + layer % 2
            if order == sorted(order):
                layers[x, pl.ds(layer, devices, stride=own_layers), :] = arrived[:, row, :]
                continue
            for device, k in enumerate(order):
                at = own_layers * k + layer
                layers[x, at : at + 1, :] = arrived[device, row : row + 1, :]
    wide = pick(jnp.concatenate([layers[0], layers[1]], 1), table[...])
    shares = pltpu.roll(wide[:, 384:512], own_layers, 0)
    turned[pl.ds(0, 128, stride=3), :] = wide[:, 0:128] + shares
    for c in range(1, 3):
        turned[pl.ds(c, 128, stride=3), :] = wide[:, 128 * c : 128 * c + 128]
    for part in range(3):
        span = slice(128 * part, 128 * part + 128)
        back = turned[span, :].T
        for component in range(3):
            for layer in range(6):
                at = stack_row(0, component, layer, 0)
                out[component, layer, :, span] = back[at : at + 3, :]
    back = wide[:, 0:128].T
    for component in range(3):
        for x in range(2):
            at = 54 + 2 * component + x
            coarse_out[component, x] = back[at : at + 1, :]


def cofactor_rows(deform):
    return [
        [
            deform[(row_at + 1) % 3][(column + 1) % 3] * deform[(row_at + 2) % 3][(column + 2) % 3]
            - deform[(row_at + 1) % 3][(column + 2) % 3]
            * deform[(row_at + 2) % 3][(column + 1) % 3]
            for column in range(3)
        ]
        for row_at in range(3)
    ]


def point_stress(deform):
    cofactors = cofactor_rows(deform)
    jacobian = (
        deform[0][0] * cofactors[0][0]
        + deform[0][1] * cofactors[0][1]
        + deform[0][2] * cofactors[0][2]
    )
    pressure = lame_ratio * (jacobian - rest_ratio)
    return [
        [deform[i][d] + pressure * cofactors[i][d] for d in range(3)] for i in range(3)
    ]


coarse_samples = [0.5 - 0.5 / math.sqrt(3.0), 0.5 + 0.5 / math.sqrt(3.0)]
two = range(2)


def at_points(low, high):
    change = high - low
    return [low + s * change for s in coarse_samples], change * (1.0 / element_span)


def ends_of(first, second):
    high = coarse_samples[0] * first + coarse_samples[1] * second
    return [first + second - high, high]


def high_low(values):
    high = values.astype(jnp.bfloat16)
    return high, (values - high.astype(jnp.float32)).astype(jnp.bfloat16)


def reads(pairs):
    return set(range(pairs[0], pairs[-1] + 2))


def plan_steps(spans):
    plan = []
    for first, count in spans:
        pairs = list(range(first, first + count))
        plan.append([pairs[n : n + 2] for n in range(0, count, 2)])
    return plan


class Slab:
    def __init__(self, width, across):
        self.width = width
        self.y_step = 2 * across
        lane = lax.broadcasted_iota(jnp.int32, (8, width), 1)
        x = (lane // 2) % across
        self.bottom, self.top, self.even = x == 0, x == across - 1, lane % 2 == 0
        self.row = lax.broadcasted_iota(jnp.int32, (8, width), 0)
        row = lax.broadcasted_iota(jnp.int32, (32, width), 0)
        lane = lax.broadcasted_iota(jnp.int32, (32, width), 1)
        on_face = (row == 0) | ((row >= 3) & (row <= 11))
        self.keep = jnp.where(on_face & ((lane // 2) % across == 0), 0.0, 1.0)

    def lanes(self, v, step):
        return pltpu.roll(v, step % self.width, 1)

    def from_next(self, v, x, y):
        if x or y:
            v = self.lanes(v, -2 * x - self.y_step * y)
        return jnp.where(self.top, 0.0, v) if x else v

    def from_next_z(self, v, ahead, x, y):
        step = -2 * x - self.y_step * y
        v = jnp.where(self.even, self.lanes(v, step - 1), self.lanes(ahead, step + 1))
        return jnp.where(self.top, 0.0, v) if x else v

    def onto_next(self, v, x, y, z=0):
        if x or y or z:
            v = self.lanes(v, 2 * x + self.y_step * y + z)
        return jnp.where(self.bottom, 0.0, v) if x else v

    def gather(self, here, ahead):
        row = self.row
        g0, g1, g2, g3 = here[0:8], here[8:16], here[16:24], here[24:32]
        a0 = ahead[0:8]
        z0, xz = self.from_next_z(g0, a0, 0, 0), self.from_next_z(g0, a0, 1, 0)
        yz, xyz = self.from_next_z(g0, a0, 0, 1), self.from_next_z(g0, a0, 1, 1)
        z2 = self.from_next_z(g2, ahead[16:24], 0, 0)
        edges = jnp.where(row <= 4, xz, self.from_next(g0, 1, 1))
        edges = jnp.where(row == 0, xyz, jnp.where(row <= 2, yz, edges))
        return jnp.concatenate(
            [
                g0,
                g1,
                g2,
                jnp.where(row < 4, z2, g3),
                self.from_next(g0, 1, 0),
                jnp.where(row == 7, yz, self.from_next(g0, 0, 1)),
                jnp.where(row == 7, xz, z0),
                jnp.where(row < 4, self.from_next(g1, 1, 0), self.from_next(g1, 0, 1)),
                edges,
                jnp.zeros_like(g0),
            ],
            0,
        )

    def scatter(self, part, behind):
        row = self.row
        g0, g1, g2, g3, x0, y0, z0, sides, edges = (part[8 * n : 8 * n + 8] for n in range(9))
        last = row == 7
        for_z = jnp.where(last, 0.0, z0)
        for_xz = jnp.where(last, z0, jnp.where((row == 3) | (row == 4), edges, 0.0))
        for_yz = jnp.where(last, y0, jnp.where((row == 1) | (row == 2), edges, 0.0))
        for_xyz = jnp.where(row == 0, edges, 0.0)
        for_xy = jnp.where(row >= 5, edges, 0.0)

        def above(z):
            return (
                self.onto_next(for_z, 0, 0, z)
                + self.onto_next(for_yz, 0, 1, z)
                + self.onto_next(for_xz, 1, 0, z)
                + self.onto_next(for_xyz, 1, 1, z)
            )

        own0 = g0 + self.onto_next(x0, 1, 0) + self.onto_next(jnp.where(last, 0.0, y0), 0, 1)
        own0 = own0 + self.onto_next(for_xy, 1, 1)
        own0 = own0 + jnp.where(self.even, behind[0], above(1))
        own1 = g1 + jnp.where(row < 4, self.onto_next(sides, 1, 0), self.onto_next(sides, 0, 1))
        share2 = jnp.where(self.even, behind[1], self.onto_next(g3, 0, 0, 1))
        own2 = g2 + jnp.where(row < 4, share2, 0.0)
        own3 = jnp.where(row < 4, 0.0, g3)
        moved = (above(-1), self.onto_next(g3, 0, 0, -1))
        return jnp.concatenate([self.twinned(own0), own1, own2, own3], 0), moved

    def twinned(self, v):
        twins = jnp.where(self.row == 7, pltpu.roll(v, 7, 0), 0.0)
        return v + jnp.where(self.row == 0, pltpu.roll(v, 1, 0), twins)

    def absorb(self, total, behind):
        low = self.twinned(jnp.where(self.even, behind[0], 0.0))
        high = jnp.where(self.even & (self.row < 4), behind[1], 0.0)
        return jnp.concatenate(
            [total[0:8] + low, total[8:16], total[16:24] + high, total[24:32]], 0
        )

    def gradient(self, u, spread, pairs):
        parts = [
            high_low(self.gather(u[i, pair], u[i, pair + 1])) for i in range(3) for pair in pairs
        ]
        return jnp.dot(
            spread[...],
            jnp.concatenate([jnp.concatenate([h, l, h], 0) for h, l in parts], 1),
            preferred_element_type=jnp.float32,
        )

    def force(self, gradient, stiff, collect, pairs):
        width, count = self.width, len(pairs)
        rows = 16
        high, low = {}, {}
        for q in range(count):
            for r in range(64 // rows):
                deform = [
                    [
                        gradient[
                            64 * e + rows * r : 64 * e + rows * (r + 1),
                            width * (count * i + q) : width * (count * i + q + 1),
                        ]
                        + (1.0 if i == e else 0.0)
                        for e in range(3)
                    ]
                    for i in range(3)
                ]
                stress = point_stress(deform)
                for i in range(3):
                    for e in range(3):
                        high[e, r, i, q], low[e, r, i, q] = high_low(stress[i][e])

        def whole(part):
            return jnp.concatenate(
                [
                    jnp.concatenate([part[e, r, i, q] for i in range(3) for q in range(count)], 1)
                    for e in range(3)
                    for r in range(64 // rows)
                ],
                0,
            )

        force = jnp.dot(collect[...], whole(high), preferred_element_type=jnp.float32)
        force = force[0:ROWS] + (
            force[ROWS:]
            + jnp.dot(collect[0:ROWS], whole(low), preferred_element_type=jnp.float32)
        )
        stiffness = [stiff[pair : pair + 1, :] for pair in pairs]
        return force * jnp.concatenate(stiffness * 3, 1)

    def run(self, u, stiff, spread, collect, jobs, given=None):
        plan = plan_steps([job[:2] for job in jobs])
        steps = [(pairs, n) for n, chunks in enumerate(plan) for pairs in chunks]
        none = jnp.zeros((8, self.width), jnp.float32)
        ahead, carry, job = None, None, None
        for at, (pairs, n) in enumerate(steps):
            ready = given is not None and n == 0 and pairs == given[0]
            gradient = ahead
            if ahead is None and not ready:
                gradient = self.gradient(u, spread, pairs)
            if not ready:
                ahead = None
            if ahead is None and at + 1 < len(steps):
                later, later_job = steps[at + 1]
                if given is not None and later_job == 0 and later == given[0]:
                    later, later_job = steps[at + 2]
                if later_job == n or not reads(later) & set(pairs):
                    ahead = self.gradient(u, spread, later)
            if job != n:
                carry, job = [(none, none) for i in range(3)], n
            if ready:
                for q, pair in enumerate(pairs):
                    total = given[1][q]
                    if q == 0:
                        total = [self.absorb(total[i], carry[i]) for i in range(3)]
                    jobs[n][2](pair, total)
                carry = list(given[2])
                continue
            force = self.force(gradient, stiff, collect, pairs)
            totals = [[] for pair in pairs]
            for q in range(len(pairs)):
                for i in range(3):
                    lane = (len(pairs) * i + q) * self.width
                    total, carry[i] = self.scatter(force[:, lane : lane + self.width], carry[i])
                    totals[q].append(total)
            for pair, total in zip(pairs, totals):
                jobs[n][2](pair, total)
        return carry

    def smoothing(self, u, f, f_shift, d, spans, bound):
        jobs = []
        for (first, count), (held, added) in zip(spans, chebyshev_steps()):

            def finish(pair, forces, held=held, added=added):
                for i in range(3):
                    z = (added / bound) * self.keep * (f[i, pair + f_shift] - forces[i])
                    move = held * d[i, pair] + z if held else z
                    d[i, pair] = move
                    u[i, pair] = u[i, pair] + move

            jobs.append((first, count, finish))
        return jobs

    def owed(self, carry, bound):
        scale = -chebyshev_steps()[-1][1] / bound
        return [
            (
                scale * jnp.where(self.even, low, 0.0) * self.keep[0:8],
                scale * jnp.where(self.even, high, 0.0) * self.keep[16:24],
            )
            for low, high in carry
        ]

    def corners_of(self, v):
        ahead = pltpu.roll(v, 7, 0)
        found = {}
        for a in range(2):
            for b in range(2):
                found[a, b, 0] = self.from_next(v, a, b)
                found[a, b, 1] = self.from_next_z(v, ahead, a, b)
        return found

    def assemble(self, part):
        here, odd, even = 0.0, 0.0, 0.0
        for a in range(2):
            for b in range(2):
                here = here + self.onto_next(part[a, b, 0], a, b)
                odd = odd + self.onto_next(part[a, b, 1], a, b, 1)
                even = even + self.onto_next(part[a, b, 1], a, b, -1)
        return here + jnp.where(self.even, pltpu.roll(even, 1, 0), odd)

    def coarse_force(self, values, stiffness):
        grads = []
        for i in range(3):
            v = self.corners_of(values[i])
            vz, sz = {}, {}
            for a in two:
                for b in two:
                    vz[a, b], sz[a, b] = at_points(v[a, b, 0], v[a, b, 1])
            vv, vs, sv = {}, {}, {}
            for a in two:
                for k in two:
                    vv[a, k], vs[a, k] = at_points(vz[a, 0][k], vz[a, 1][k])
                sv[a], unused = at_points(sz[a, 0], sz[a, 1])
            dx, dy, dz = {}, {}, {}
            for k in two:
                for j in two:
                    dx[j, k] = (vv[1, k][j] - vv[0, k][j]) * (1.0 / element_span)
                line, unused = at_points(vs[0, k], vs[1, k])
                for h in two:
                    dy[h, k] = line[h]
            for j in two:
                line, unused = at_points(sv[0][j], sv[1][j])
                for h in two:
                    dz[h, j] = line[h]
            grads.append((dx, dy, dz))
        weight = element_span**2 / 8.0
        scaled = weight * stiffness
        sums = [({}, {}, {}) for i in range(3)]

        def add(table, key, value):
            table[key] = table[key] + value if key in table else value

        for h in two:
            for j in two:
                for k in two:
                    deform = [
                        [grads[i][0][j, k], grads[i][1][h, k], grads[i][2][h, j]]
                        for i in range(3)
                    ]
                    for i in range(3):
                        deform[i][i] = deform[i][i] + 1.0
                    stress = point_stress(deform)
                    for i in range(3):
                        add(sums[i][0], (j, k), stress[i][0])
                        add(sums[i][1], (h, k), stress[i][1])
                        add(sums[i][2], (h, j), stress[i][2])

        forces = []
        for i in range(3):
            part = {}
            qx, qy, qz = sums[i]
            along_z = [ends_of(qx[j, 0], qx[j, 1]) for j in two]
            for c in two:
                line = ends_of(along_z[0][c], along_z[1][c])
                for b in two:
                    part[0, b, c] = -line[b]
                    part[1, b, c] = line[b]
            along_z = [ends_of(qy[h, 0], qy[h, 1]) for h in two]
            for c in two:
                line = ends_of(along_z[0][c], along_z[1][c])
                for a in two:
                    part[a, 0, c] = part[a, 0, c] - line[a]
                    part[a, 1, c] = part[a, 1, c] + line[a]
            along_y = [ends_of(qz[h, 0], qz[h, 1]) for h in two]
            for b in two:
                line = ends_of(along_y[0][b], along_y[1][b])
                for a in two:
                    part[a, b, 0] = part[a, b, 0] - line[a]
                    part[a, b, 1] = part[a, b, 1] + line[a]
            forces.append(self.assemble({key: scaled * value for key, value in part.items()}))
        return forces


def window_pair(slab, first_layer, own_layers, fetch):
    found = []
    for parity in range(2):
        layer = first_layer + parity
        device = layer // own_layers
        layer = layer - device * own_layers
        found.append((device, layer // 2, layer % 2))
    values = [fetch(device, q) for device, q, parity in found]
    if found[0][:2] == found[1][:2] or (values[0] is None and values[1] is None):
        return values[0]
    for parity in range(2):
        if values[parity] is None:
            values[parity] = jnp.zeros_like(values[1 - parity])
        elif found[parity][2] != parity:
            values[parity] = slab.lanes(values[parity], 2 * parity - 1)
    lane = lax.broadcasted_iota(jnp.int32, values[0].shape, 1)
    return jnp.where(lane % 2 == 0, values[0], values[1])


def first_sources(own_layers):
    return list(range(-BEFORE // own_layers, (own_layers + BEFORE - 1) // own_layers + 1))


def whole_pairs(own_layers):
    return own_layers == 4


def turn_rows(block, mixed, turned, width, at):
    for tile in range(SENT // 128):
        n = at * (SENT // 128) + tile
        for m in range(width // 4):
            first = 12 * m + 4 * tile
            mixed[n, 4 * m : 4 * m + 4, :] = block[first : first + 4, :]
        turned[at, 128 * tile : 128 * tile + 128, :] = mixed[n].T


def regroup(slab, field, rows):
    values, hard = [], None
    for i in range(3):
        parts = [rows(24 * i + 8 * n) for n in range(3)]
        if field == 0 and i == 0:
            hard = parts[0][TWIN : TWIN + 1]
        parts[0] = jnp.where(slab.row == TWIN, pltpu.roll(parts[0], TWIN, 0), parts[0])
        parts.append(jnp.where(slab.row < 4, 0.0, rows(68 + 4 * i)))
        whole = jnp.concatenate(parts, 0)
        values.append(whole * slab.keep if field == 0 else whole)
    return values, hard


def layer_above(slab, turned, at, i):
    first = NEXT_COLUMN + 12 * i
    low, high = turned[at, first : first + 8, :], turned[at, first + 4 : first + 12, :]
    high = jnp.where(slab.row < 4, pltpu.roll(high, 4, 0), 0.0)
    low = jnp.where(slab.row == TWIN, pltpu.roll(low, TWIN, 0), low)
    nothing = jnp.zeros_like(low)
    return jnp.concatenate([low, nothing, high, nothing], 0) * slab.keep


def make_own_kernel(width, across, own_layers):
    own_pairs = own_layers // 2
    pairs = list(range(own_pairs))

    def own_kernel(block, spread, collect, u, f, stiff, forces, moved, mixed, turned):
        slab = Slab(width, across)
        turn_rows(block, mixed, turned, width, 0)
        for pair in pairs:
            for field, target in enumerate((u, f)):

                def rows(start, field=field, pair=pair):
                    at = BLOCK * (2 * pair + field) + start
                    return turned[0, at : at + 8, :]

                values, hard = regroup(slab, field, rows)
                for i in range(3):
                    target[i, pair] = values[i]
                if field == 0:
                    stiff[pair : pair + 1, :] = hard
        for i in range(3):
            u[i, own_pairs] = layer_above(slab, turned, 0, i)

        def finish(pair, total):
            for i in range(3):
                forces[i, pair] = total[i]

        carry = slab.run(u, stiff, spread, collect, [(0, own_pairs, finish)])
        for i in range(3):
            moved[i, 0] = carry[i][0]
            moved[i, 1] = carry[i][1]

    return own_kernel


def make_first_kernel(width, across, own_layers, fine_bound):
    own = BEFORE // 2
    own_pairs = (own_layers + 1) // 2
    spans = []
    prepared = whole_pairs(own_layers)
    for n in (4, 3, 2, 1):
        low, high = BEFORE - n, BEFORE + own_layers + n - 1 + prepared
        spans.append((low // 2, (high + 1) // 2 - low // 2))
    sources = [n for n in first_sources(own_layers) if n or not prepared]

    def first_kernel(*refs):
        arrived = refs[: len(sources)]
        refs = refs[len(sources) :]
        if prepared:
            own_u, own_f, own_stiff, own_forces, own_moved = refs[:5]
            refs = refs[5:]
        spread, collect, transfer, message, *sent, f, u, d, stiff, shares, mixed, turned = refs
        slab = Slab(width, across)
        if not prepared:
            u[...] = jnp.zeros(u.shape, jnp.float32)
            f[...] = jnp.zeros(f.shape, jnp.float32)
        shares[...] = jnp.zeros(shares.shape, jnp.float32)
        stiff[...] = jnp.zeros(stiff.shape, jnp.float32)
        for n in range(len(sources)):
            turn_rows(arrived[n], mixed, turned, width, n)
        for pair in range(PAIRS):
            if prepared and own <= pair < own + own_pairs:
                for i in range(3):
                    u[i, pair] = own_u[i, pair - own]
                    f[i, pair] = own_f[i, pair - own]
                stiff[pair : pair + 1, :] = own_stiff[pair - own : pair - own + 1, :]
                continue
            for field, target in enumerate((u, f)):

                def rows(start, field=field, pair=pair):
                    def fetch(device, q):
                        if device not in sources:
                            return None
                        at = BLOCK * (2 * q + field) + start
                        return turned[sources.index(device), at : at + 8, :]

                    value = window_pair(slab, 2 * pair - BEFORE, own_layers, fetch)
                    return jnp.zeros((8, width), jnp.float32) if value is None else value

                values, hard = regroup(slab, field, rows)
                for i in range(3):
                    target[i, pair] = values[i]
                if field == 0:
                    stiff[pair : pair + 1, :] = hard
        given = None
        if prepared:
            for i in range(3):
                u[i, PAIRS] = layer_above(slab, turned, sources.index(1), i)
            given = (
                list(range(own, own + own_pairs)),
                [[own_forces[i, q] for i in range(3)] for q in range(own_pairs)],
                [(own_moved[i, 0], own_moved[i, 1]) for i in range(3)],
            )

        weights = [jnp.broadcast_to(transfer[:, n : n + 1], (32, width)) for n in range(8)]

        def restrict(pair, forces):
            for i in range(3):
                rest = slab.keep * (f[i, pair] - forces[i])
                for n in range(8):
                    part = rest * weights[n]
                    part = (part[0:8] + part[8:16]) + (part[16:24] + part[24:32])
                    shares[i, n, pl.ds(pair, 1), :] = jnp.sum(part, axis=0, keepdims=True)

        jobs = slab.smoothing(u, f, 0, d, spans[0:3], fine_bound)
        slab.run(u, stiff, spread, collect, jobs + [(*spans[3], restrict)], given)

        restricted = [
            slab.assemble({corner: shares[i, n] for n, corner in enumerate(CORNERS)})
            for i in range(3)
        ]
        def line(rows, q):
            return rows[own + q : own + q + 1]

        for q in range(own_pairs):
            for i in range(3):
                message[i, q] = u[i, own + q]
                message[i, q, RESTRICTED_SLOT : RESTRICTED_SLOT + 1, :] = line(restricted[i], q)
            message[0, q, STIFF_SLOT : STIFF_SLOT + 1, :] = line(stiff, q)
        if prepared:
            down, up = sent
            for i in range(3):
                down[i, 0:32] = u[i, own]
                down[i, 32:40] = u[i, own + 1, 0:8, :]
                down[i, 40:48] = u[i, own + 1, 16:24, :]
                up[i] = u[i, own + 1]
                for n, row in enumerate(
                    (line(restricted[i], 0), line(restricted[i], 1), u[i, own + 2, 0:1, :])
                    + (line(restricted[i], 2),)
                ):
                    down[i, 24 + n : 25 + n, :] = row
                for n, row in enumerate(
                    (line(restricted[i], 1), line(restricted[i], 0), u[i, own, 0:1, :])
                ):
                    up[i, 24 + n : 25 + n, :] = row
            for q in range(own_pairs):
                down[q, 32 + TWIN : 33 + TWIN, :] = line(stiff, q)
                up[q, TWIN : TWIN + 1, :] = line(stiff, q)
            return
        edge = sent[0]
        for q in range(own_pairs):
            for i in range(3):
                edge[q, i : i + 1, :] = u[i, own + q, 0:1, :]
                edge[q, 3 + i : 4 + i, :] = line(restricted[i], q)
            edge[q, 6:8, :] = jnp.broadcast_to(line(stiff, q), (2, width))

    return first_kernel


def shares_sent(own_layers):
    return own_layers % 2 == 0


def sources_of(own_layers):
    below = 2 if shares_sent(own_layers) else 3
    whole = range(-below // own_layers, (own_layers + 2) // own_layers + 1)
    coarse = range(-(below + 2) // own_layers, (own_layers + 4) // own_layers + 1)
    return list(whole), [n for n in coarse if n not in whole]


def message_line(message, q, n):
    i, slot = ((n, 0), (n - 3, RESTRICTED_SLOT), (0, STIFF_SLOT))[n // 3]
    return message[i, q, slot : slot + 1, :]


def sent_readers(slab, up, message, down):
    def block_of(device, q, i):
        if device == 0:
            return message[i, q]
        if (device, q) == (1, 0):
            whole = down[i, 0:32]
        elif (device, q) == (1, 1):
            low, high = down[i, 32:40], down[i, 40:48]
            low = jnp.where(slab.row == TWIN, pltpu.roll(low, TWIN, 0), low)
            whole = jnp.concatenate([low, jnp.zeros_like(low), high, jnp.zeros_like(low)], 0)
        elif (device, q) == (-1, 1):
            low = up[i, 0:8]
            low = jnp.where(slab.row == TWIN, pltpu.roll(low, TWIN, 0), low)
            whole = jnp.concatenate([low, up[i, 8:32]], 0)
        else:
            return None
        return whole

    def line_of(device, q, n):
        if device == 0:
            return message_line(message, q, n)
        kind, i = n // 3, n % 3
        if device == 1:
            row = ((0, 24), (32, 25))[q][kind] if kind < 2 else 32 + TWIN
            i = i if kind < 2 else q
            return down[i, row : row + 1, :]
        if device == -1:
            row = ((26, 25), (0, 24))[q][kind] if kind < 2 else TWIN
            i = i if kind < 2 else q
            return up[i, row : row + 1, :]
        if (device, q) == (2, 0) and kind < 2:
            return down[i, 26 + kind : 27 + kind, :]
        return None

    return block_of, line_of


def make_second_kernel(width, across, own_layers, fine_bound, coarse_bound):
    own = BEFORE_B // 2
    own_pairs = (own_layers + 1) // 2
    shift = (BEFORE - BEFORE_B) // 2
    whole, outer = sources_of(own_layers)
    steps = chebyshev_steps()
    spans = []
    for n in (3, 2, 1):
        low, high = BEFORE_B - n + shares_sent(own_layers), BEFORE_B + own_layers + n - 1
        spans.append((low // 2, (high + 1) // 2 - low // 2))

    def second_kernel(*refs):
        slab = Slab(width, across)
        if whole_pairs(own_layers):
            up, message, down = refs[:3]
            refs = refs[3:]
            block_of, line_of = sent_readers(slab, up, message, down)
        else:
            messages = dict(zip(whole, refs))
            edges = dict(zip(outer, refs[len(whole) :]))
            refs = refs[len(whole) + len(outer) :]

            def block_of(device, q, i):
                return messages[device][i, q] if device in messages else None

            def line_of(device, q, n):
                if device in messages:
                    return message_line(messages[device], q, n)
                return edges[device][q, n : n + 1, :] if device in edges else None

        f, spread, collect, transfer_back, out, u, d, stiff, coarse = refs

        def pair_of(pair, fetch):
            return window_pair(slab, 2 * pair - BEFORE_B, own_layers, fetch)

        coarse[...] = jnp.zeros(coarse.shape, jnp.float32)
        for pair in range(PAIRS_B):
            for i in range(3):
                block = pair_of(pair, lambda device, q: block_of(device, q, i))
                u[i, pair] = jnp.zeros((32, width), jnp.float32) if block is None else block
            for n in range(7):
                line = pair_of(pair, lambda device, q: line_of(device, q, n))
                if line is not None:
                    coarse[n, pair : pair + 1, :] = line
        stiff[...] = coarse[6]

        stiffness = coarse[6]
        keep_coarse = jnp.where(slab.bottom, 0.0, 1.0)
        start = [coarse[i] for i in range(3)]
        restricted = [coarse[3 + i] for i in range(3)]
        before = slab.coarse_force(start, stiffness)
        move = [(steps[0][1] / coarse_bound) * keep_coarse * restricted[i] for i in range(3)]
        level = [start[i] + move[i] for i in range(3)]
        for held, added in steps[1:]:
            force = slab.coarse_force(level, stiffness)
            for i in range(3):
                z = keep_coarse * (restricted[i] + before[i] - force[i])
                move[i] = held * move[i] + (added / coarse_bound) * z
                level[i] = level[i] + move[i]

        weights = [jnp.broadcast_to(transfer_back[:, n : n + 1], (32, width)) for n in range(8)]
        for i in range(3):
            change = slab.corners_of(level[i] - start[i])
            for pair in range(spans[0][0], min(spans[0][0] + spans[0][1] + 1, PAIRS_B)):
                lift = u[i, pair]
                for n, corner in enumerate(CORNERS):
                    lift = lift + weights[n] * change[corner][pair : pair + 1]
                u[i, pair] = lift

        jobs = slab.smoothing(u, f, shift, d, spans, fine_bound)
        owed = slab.owed(slab.run(u, stiff, spread, collect, jobs), fine_bound)

        lower = lax.broadcasted_iota(jnp.int32, (width // 8, 8, 128), 1) < 4
        nothing = jnp.zeros((8, width), jnp.float32)
        sides = []
        for q in range(2):
            if q or not shares_sent(own_layers):
                owed = [(nothing, nothing)] * 3
            rows = []
            for i in range(3):
                value = u[i, own + q]
                rows += [value[0:24], jnp.where(slab.row < 4, owed[i][1], value[24:32])]
            rows += [owed[i][0] for i in range(3)]
            rows += [level[i][own + q : own + q + 1] for i in range(3)] + [nothing[0:5]]
            sides.append(jnp.concatenate(rows, 0).T.reshape(width // 8, 8, 128))
        out[:, 0] = jnp.where(lower, sides[0], pltpu.roll(sides[1], 4, 1))
        out[:, 1] = jnp.where(lower, pltpu.roll(sides[0], 4, 1), sides[1])

    return second_kernel


def solution(mesh):
    rows_of, columns_of = mesh.shape["gx"], mesh.shape["gy"]
    devices = rows_of * columns_of
    order = ring_order(rows_of, columns_of)
    own_layers = EZ // devices
    own_pairs = (own_layers + 1) // 2
    width = 4 * devices
    across = 2 * rows_of
    near = first_sources(own_layers)
    prepared = whole_pairs(own_layers)
    whole, outer = sources_of(own_layers)
    spread, collect, fine_bound = element_tables()
    coarse_bound = build_tables([0.0, 1.0], 2)[2]
    transfer, transfer_back = transfer_table()
    wide = pltpu.CompilerParams(vmem_limit_bytes=60 * 1024 * 1024)
    limit = pltpu.CompilerParams(vmem_limit_bytes=48 * 1024 * 1024)
    f32 = jnp.float32

    pack = pl.pallas_call(
        functools.partial(pack_kernel, order),
        out_shape=pltpu.VMEM((devices * 12, 128), f32),
        in_specs=[pl.BlockSpec(memory_space=pl.ANY)] * 5,
        out_specs=pl.BlockSpec(memory_space=pltpu.VMEM),
        scratch_shapes=[
            pltpu.VMEM((3, 6, 3, 384), f32),
            pltpu.VMEM((3, 6, 3, 384), f32),
            pltpu.VMEM((2, 1, EZ), f32),
            pltpu.VMEM((1, 1, 192), jnp.int32),
            pltpu.VMEM((384, 512), jnp.bfloat16),
            pltpu.VMEM((128, 384), f32),
            pltpu.VMEM((384, 128), f32),
            pltpu.VMEM((6, 136, 128), f32),
            pltpu.SemaphoreType.DMA((5,)),
        ],
        compiler_params=wide,
    )
    own = pl.pallas_call(
        make_own_kernel(width, across, own_layers),
        out_shape=(
            jax.ShapeDtypeStruct((3, own_pairs + 1, 32, width), f32),
            jax.ShapeDtypeStruct((3, own_pairs, 32, width), f32),
            jax.ShapeDtypeStruct((own_pairs, width), f32),
            jax.ShapeDtypeStruct((3, own_pairs, 32, width), f32),
            jax.ShapeDtypeStruct((3, 2, 8, width), f32),
        ),
        scratch_shapes=[
            pltpu.VMEM((SENT // 128, width, 128), f32),
            pltpu.VMEM((1, SENT, width), f32),
        ],
        compiler_params=limit,
        cost_estimate=pl.CostEstimate(flops=400_000_000, bytes_accessed=1_000_000, transcendentals=0),
    )
    sent = [jax.ShapeDtypeStruct((own_pairs, 8, width), f32)]
    if prepared:
        sent = [jax.ShapeDtypeStruct((3, rows, width), f32) for rows in (48, 32)]
    first = pl.pallas_call(
        make_first_kernel(width, across, own_layers, fine_bound),
        out_shape=(
            jax.ShapeDtypeStruct((3, own_pairs, 32, width), f32),
            *sent,
            jax.ShapeDtypeStruct((3, PAIRS, 32, width), f32),
        ),
        scratch_shapes=[
            pltpu.VMEM((3, 8, 32, width), f32),
            pltpu.VMEM((3, 8, 32, width), f32),
            pltpu.VMEM((8, width), f32),
            pltpu.VMEM((3, 8, 8, width), f32),
            pltpu.VMEM((len(near) * (SENT // 128), width, 128), f32),
            pltpu.VMEM((len(near), SENT, width), f32),
        ],
        compiler_params=limit,
    )
    second = pl.pallas_call(
        make_second_kernel(width, across, own_layers, fine_bound, coarse_bound),
        out_shape=jax.ShapeDtypeStruct((devices // 2, 2, 8, 128), f32),
        scratch_shapes=[
            pltpu.VMEM((3, PAIRS_B, 32, width), f32),
            pltpu.VMEM((3, PAIRS_B, 32, width), f32),
            pltpu.VMEM((PAIRS_B, width), f32),
            pltpu.VMEM((7, PAIRS_B, width), f32),
        ],
        compiler_params=limit,
    )
    unpack = pl.pallas_call(
        functools.partial(unpack_kernel, order),
        out_shape=(
            jax.ShapeDtypeStruct((3, 6, 3, 384), f32),
            jax.ShapeDtypeStruct((3, 2, 1, EZ), f32),
        ),
        scratch_shapes=[pltpu.VMEM((2, 128, 128), f32), pltpu.VMEM((384, 128), f32)],
        compiler_params=limit,
    )
    everyone = ("gy", "gx")

    def from_device(block, distance):
        place = {k: m % rows_of * columns_of + m // rows_of for m, k in enumerate(order)}
        route = [(place[(k + distance) % devices], place[k]) for k in range(devices)]
        return lax.ppermute(block, ("gx", "gy"), route)

    def body(initial, forcing, modulus, solid_list):
        sent = pack(initial, forcing, modulus, solid_list, jnp.asarray(pack_table()))
        sent = sent.reshape(devices, SENT // 128, 4, 128)
        arrived = lax.all_to_all(sent, everyone, 0, 0, tiled=True).reshape(devices * 12, 128)
        blocks = [from_device(arrived, n) if n else arrived for n in near]
        if prepared:
            blocks = [block for n, block in zip(near, blocks) if n]
            blocks += own(arrived, jnp.asarray(spread), jnp.asarray(collect))
        message, *edges, load = first(
            *blocks,
            jnp.asarray(spread),
            jnp.asarray(collect),
            jnp.asarray(transfer),
        )
        if prepared:
            down, up = edges
            messages = [from_device(up, -1), message, from_device(down, 1)]
        else:
            messages = [from_device(message, n) if n else message for n in whole]
            messages += [from_device(edges[0], n) for n in outer]
        result = second(
            *messages,
            load,
            jnp.asarray(spread),
            jnp.asarray(collect),
            jnp.asarray(transfer_back),
        )
        back = lax.all_to_all(result.reshape(devices, 8, 128), everyone, 0, 0, tiled=True)
        return unpack(back, jnp.asarray(unpack_table()))

    placed = (
        P(None, "gx", "gy", None),
        P(None, "gx", "gy", None),
        P("gx", "gy", None),
        P("gx", "gy", None),
    )
    return jax.shard_map(
        body,
        mesh=mesh,
        in_specs=placed,
        out_specs=(P(None, "gx", "gy", None), P(None, "gx", "gy", None)),
        check_vma=False,
    )
```

```python
import functools
import math

import jax
import jax.numpy as jnp
import numpy as np
from jax import lax
from jax.experimental import pallas as pl
from jax.experimental.pallas import tpu as pltpu
from jax.sharding import PartitionSpec as P

CHEB = 3
EZ = 128

element_span = 20.0
lame_ratio = 4.0
rest_ratio = 1.25
modulus_top = 2.0
spectrum_floor = 0.05
interval_centre = (1.0 + spectrum_floor) / 2.0
interval_radius = (1.0 - spectrum_floor) / 2.0
interval_ratio = interval_centre / interval_radius
inner_anchors = (0.5 - 0.5 / math.sqrt(5.0), 0.5 + 0.5 / math.sqrt(5.0))

BEFORE = 4
PAIRS = 6
BEFORE_B = 6
PAIRS_B = 8
BLOCK = 84
SENT = 384

SLOTS = [
    (0, 0, 0), (1, 0, 0), (2, 0, 0), (0, 1, 0), (0, 2, 0), (0, 0, 1), (0, 0, 2), None,
    (0, 1, 1), (0, 1, 2), (0, 2, 1), (0, 2, 2), (1, 0, 1), (1, 0, 2), (2, 0, 1), (2, 0, 2),
    (1, 1, 0), (1, 2, 0), (2, 1, 0), (2, 2, 0), (1, 1, 1), (1, 1, 2), (1, 2, 1), (1, 2, 2),
    None, None, None, None, (2, 1, 1), (2, 1, 2), (2, 2, 1), (2, 2, 2),
]
TWIN = 7
NEXT_SLOTS = [0, 1, 2, 3, 4, 5, 6, 7, 16, 17, 18, 19]
NEXT_COLUMN = 4 * BLOCK
RESTRICTED_SLOT = 24
STIFF_SLOT = 25
OWN_SHIFT, SHIFT_X, SHIFT_Y, SHIFT_Z = (0, 0, 0), (1, 0, 0), (0, 1, 0), (0, 0, 1)
ELEMENT_ROWS = (
    [(slot, OWN_SHIFT) for slot in range(24)]
    + [(slot, SHIFT_Z) for slot in range(16, 20)]
    + [(slot, OWN_SHIFT) for slot in range(28, 32)]
    + [(slot, SHIFT_X) for slot in range(7)] + [None]
    + [(slot, SHIFT_Y) for slot in range(7)] + [(0, (0, 1, 1))]
    + [(slot, SHIFT_Z) for slot in range(7)] + [(0, (1, 0, 1))]
    + [(slot, SHIFT_X) for slot in range(8, 12)] + [(slot, SHIFT_Y) for slot in range(12, 16)]
    + [(0, (1, 1, 1)), (1, (0, 1, 1)), (2, (0, 1, 1)), (3, (1, 0, 1)), (4, (1, 0, 1))]
    + [(5, (1, 1, 0)), (6, (1, 1, 0)), (0, (1, 1, 0))]
)
ROWS = len(ELEMENT_ROWS)
DEPTH = 80
CORNERS = [(a, b, c) for a in range(2) for b in range(2) for c in range(2)]


def gauss_rule(point_count):
    if point_count == 2:
        offset = 1.0 / math.sqrt(3.0)
        points = [-offset, offset]
        weights = [1.0, 1.0]
    else:
        inner = math.sqrt(3.0 / 7.0 - 2.0 / 7.0 * math.sqrt(6.0 / 5.0))
        outer = math.sqrt(3.0 / 7.0 + 2.0 / 7.0 * math.sqrt(6.0 / 5.0))
        heavy = (18.0 + math.sqrt(30.0)) / 36.0
        light = (18.0 - math.sqrt(30.0)) / 36.0
        points = [-outer, -inner, inner, outer]
        weights = [light, heavy, heavy, light]
    return (np.array(points), np.array(weights))


def lagrange_tables(anchors, samples):
    values = np.zeros((len(samples), len(anchors)))
    slopes = np.zeros((len(samples), len(anchors)))
    for sample_index, sample in enumerate(samples):
        for anchor_index, anchor in enumerate(anchors):
            others = [
                location
                for location_index, location in enumerate(anchors)
                if location_index != anchor_index
            ]
            product = 1.0
            for location in others:
                product = product * (sample - location) / (anchor - location)
            values[sample_index, anchor_index] = product
            derivative = 0.0
            for skipped in range(len(others)):
                summand = 1.0 / (anchor - others[skipped])
                for kept_index in range(len(others)):
                    if kept_index != skipped:
                        summand = (
                            summand * (sample - others[kept_index]) / (anchor - others[kept_index])
                        )
                derivative = derivative + summand
            slopes[sample_index, anchor_index] = derivative
    return (values, slopes)


def outer_three(first, second, third):
    return (
        first[:, None, None, :, None, None]
        * second[None, :, None, None, :, None]
        * third[None, None, :, None, None, :]
    )


def build_tables(anchors, point_count):
    raw_points, raw_weights = gauss_rule(point_count)
    samples = (raw_points + 1.0) / 2.0
    weights = raw_weights / 2.0
    basis_values, slopes = lagrange_tables(anchors, samples)
    quad_total = point_count**3
    nodal_count = len(anchors) ** 3
    derivative_one = outer_three(slopes, basis_values, basis_values).reshape(
        quad_total, nodal_count
    )
    derivative_two = outer_three(basis_values, slopes, basis_values).reshape(
        quad_total, nodal_count
    )
    derivative_three = outer_three(basis_values, basis_values, slopes).reshape(
        quad_total, nodal_count
    )
    stacked = np.stack([derivative_one, derivative_two, derivative_three]) / element_span
    volume = (weights[:, None, None] * weights[None, :, None] * weights[None, None, :]).reshape(
        -1
    ) * element_span**3
    forward = stacked.reshape(3 * quad_total, nodal_count)
    backward = (stacked * volume[None, :, None]).reshape(3 * quad_total, nodal_count).T
    weighted = stacked * volume[None, :, None]
    laplace = weighted[0].T @ stacked[0] + weighted[1].T @ stacked[1] + weighted[2].T @ stacked[2]
    matrix = np.zeros((nodal_count, 3, nodal_count, 3))
    for first in range(3):
        for second in range(3):
            block = weighted[second].T @ stacked[first] + (lame_ratio - 1.0) * (
                weighted[first].T @ stacked[second]
            )
            if first == second:
                block = block + laplace
            matrix[:, first, :, second] = block
    matrix = matrix.reshape(3 * nodal_count, 3 * nodal_count)
    vector = 1.5 + np.cos(1.3 * np.arange(3 * nodal_count))
    for repeat in range(200):
        vector = matrix @ vector
        vector = vector / np.sqrt(vector @ vector)
    largest = vector @ (matrix @ vector)
    return (forward, backward, float(4.0 * modulus_top * 1.1 * largest))


def row_nodes():
    nodes = []
    for entry in ELEMENT_ROWS:
        slot = SLOTS[entry[0]] if entry else None
        if slot is None or any(s and n for s, n in zip(entry[1], slot)):
            nodes.append(None)
        else:
            a, b, c = (3 * s + n for s, n in zip(entry[1], slot))
            nodes.append(16 * a + 4 * b + c)
    return nodes


def halves(matrix):
    whole = np.asarray(matrix, np.float32)
    high = whole.astype(jnp.bfloat16)
    low = (whole - high.astype(np.float32)).astype(jnp.bfloat16)
    return high, low


def element_tables():
    forward, backward, bound = build_tables([0.0, inner_anchors[0], inner_anchors[1], 1.0], 4)
    spread = np.zeros((forward.shape[0], DEPTH))
    collect = np.zeros((ROWS, backward.shape[1]))
    for row, node in enumerate(row_nodes()):
        if node is not None:
            spread[:, row] = forward[:, node]
            collect[row, :] = backward[node, :]
    for column in range(3):
        spread[64 * column : 64 * column + 64, ROWS + column] = 1.0
    spread_high, spread_low = halves(spread)
    collect_high, collect_low = halves(collect)
    return (
        np.concatenate([spread_high, spread_high, spread_low], 1),
        np.concatenate([collect_high, collect_low], 0),
        bound,
    )


def transfer_table():
    table = np.zeros((8, 32))
    reach = (0.0, inner_anchors[0], inner_anchors[1])
    for row, corner in enumerate(CORNERS):
        for column, slot in enumerate(SLOTS):
            if slot is not None:
                weight = 1.0
                for side, node in zip(corner, slot):
                    weight = weight * (reach[node] if side else 1.0 - reach[node])
                table[row, column] = weight
    back = table.T.copy()
    back[TWIN] = back[0]
    return table.T.astype(np.float32), back.astype(np.float32)


def chebyshev_steps():
    steps = [(0.0, 1.0 / interval_centre)]
    ratio_now = 1.0 / interval_ratio
    for sweep in range(1, CHEB):
        ratio_next = 1.0 / (2.0 * interval_ratio - ratio_now)
        steps.append((ratio_next * ratio_now, 2.0 * ratio_next / interval_radius))
        ratio_now = ratio_next
    return steps


def stack_row(field, component, layer, b):
    return field * 54 + component * 18 + layer * 3 + b


def block_column(component, slot):
    return 72 + 4 * component + slot - 28 if slot >= 24 else 24 * component + slot


def pack_table():
    table = np.zeros((3, 128, 2, 2, 128), np.float32)
    for field in range(2):
        for x in range(2):
            for component in range(3):
                for column, slot in enumerate(SLOTS):
                    if slot is not None:
                        a, b, c = slot
                        row = stack_row(field, component, 3 * x + a, b)
                        table[c, row, field, x, block_column(component, column)] = 1.0
                        if field == 0 and column in NEXT_SLOTS:
                            at = BLOCK + 12 * component + NEXT_SLOTS.index(column)
                            table[c, row, 1, x, at] = 1.0
            table[0, 108 + x, 0, x, TWIN] = 1.0
    return table.reshape(384, 512).astype(jnp.bfloat16)


def unpack_table():
    table = np.zeros((2, 128, 4, 128), np.float32)
    for x in range(2):
        for component in range(3):
            for column, slot in enumerate(SLOTS):
                if slot is not None:
                    a, b, c = slot
                    row = stack_row(0, component, 3 * x + a, b)
                    table[x, component * 32 + column, c, row] = 1.0
                    if column < 5:
                        table[x, 96 + 8 * component + column, 3, row] = 1.0
                    if column == 0:
                        table[x, 96 + 8 * component + TWIN, 3, row] = 1.0
                    if 16 <= column < 20:
                        table[x, component * 32 + column + 8, 3, row] = 1.0
            table[x, 120 + component, 0, 54 + 2 * component + x] = 1.0
    return table.reshape(256, 512).astype(jnp.bfloat16)


def pick(values, table):
    count = values.shape[0]
    parts = jnp.dot(
        jnp.concatenate(high_low(values), 0), table, preferred_element_type=jnp.float32
    )
    return parts[:count] + parts[count:]


def ring_order(rows_of, columns_of):
    if (rows_of, columns_of) != (4, 8):
        return list(range(rows_of * columns_of))
    order = []
    for z in range(4):
        for x in range(2):
            for y in range(2):
                chip = (z, 7 - z, 15 - z, 8 + z)[2 * x + y]
                order += [2 * chip, 2 * chip + 1]
    return order


def pack_kernel(
    order,
    initial_at, forcing_at, modulus_at, listing_at, table_at, out,
    initial, forcing, modulus, listing, table, rows, turned, places, ready,
):
    own_layers = EZ // len(order)
    sources = (listing_at, modulus_at, initial_at, forcing_at, table_at)
    copies = [
        pltpu.make_async_copy(source, here, ready.at[n])
        for n, (source, here) in enumerate(
            zip(sources, (listing, modulus, initial, forcing, table))
        )
    ]
    for copy in copies:
        copy.start()
    rows[108:128, :] = jnp.zeros((20, 384), jnp.float32)
    copies[0].wait()
    copies[1].wait()
    listed = listing[0].astype(jnp.float32)
    listed = jnp.concatenate([listed, jnp.full((1, 64), 256.0, jnp.float32)], 1)
    listed = jnp.broadcast_to(listed, (128, 256)).T
    lanes = lax.broadcasted_iota(jnp.int32, (256, 128), 1).astype(jnp.float32)
    row_at = lax.broadcasted_iota(jnp.int32, (128, 128), 0)
    stiff = jnp.zeros((128, 128), jnp.float32)
    for x in range(2):
        hit = jnp.max(jnp.where(listed == lanes + 128.0 * x, 1.0, 0.0), axis=0, keepdims=True)
        stiff = jnp.where(row_at == 108 + x, hit * modulus[x], stiff)
    copies[2].wait()
    copies[3].wait()
    for field, source in enumerate((initial, forcing)):
        for component in range(3):
            for layer in range(6):
                at = stack_row(field, component, layer, 0)
                rows[at : at + 3, :] = source[component, layer]
    for part in range(3):
        span = slice(128 * part, 128 * part + 128)
        turned[span, :] = rows[:, span].T
    picked = [turned[pl.ds(c, 128, stride=3), :] for c in range(3)]
    picked[0] = picked[0] + stiff.T
    copies[4].wait()
    wide = pick(jnp.concatenate(picked, 1), table[...])
    lane = lax.broadcasted_iota(jnp.int32, (128, 128), 1)
    for x in range(2):
        tiles = [None] * (SENT // 128)
        for n in range(4):
            pair, field = n // 2, n % 2
            moved = wide[:, 128 * (2 * field + x) : 128 * (2 * field + x) + 128]
            first = BLOCK * n
            if pair:
                moved = pltpu.roll(moved, 128 - 2 * pair, 0)
            if first % 128:
                moved = pltpu.roll(moved, first % 128, 1)
            for tile in range(first // 128, (first + BLOCK - 1) // 128 + 1):
                before = tiles[tile]
                if before is None:
                    tiles[tile] = moved
                else:
                    tiles[tile] = jnp.where(lane >= first - 128 * tile, moved, before)
        above = wide[:, 128 * (2 + x) : 128 * (2 + x) + 128]
        above = pltpu.roll(pltpu.roll(above, 128 - own_layers, 0), (NEXT_COLUMN - BLOCK) % 128, 1)
        tiles[-1] = jnp.where(lane >= NEXT_COLUMN % 128, above, tiles[-1])
        for tile in range(SENT // 128):
            places[3 * x + tile, 0:128, :] = tiles[tile]
            places[3 * x + tile, 128:136, :] = jnp.zeros((8, 128), jnp.float32)
    for device, k in enumerate(order):
        for tile in range(SENT // 128):
            for x in range(2):
                at = 12 * device + 4 * tile + 2 * x
                out[at : at + 2, :] = places[
                    3 * x + tile, own_layers * k : own_layers * k + 2, :
                ]


def unpack_kernel(order, arrived, table, out, coarse_out, layers, turned):
    devices = arrived.shape[0]
    own_layers = EZ // devices
    together = min(own_layers, 2)
    for x in range(2):
        for layer in range(0, own_layers, 2):
            row = (layer // 2) * 4 + x * 2
            if order == sorted(order):
                layers[x, pl.ds(layer, devices, stride=own_layers), :] = arrived[:, row, :]
                continue
            for device, k in enumerate(order):
                at = own_layers * k + layer
                layers[x, at : at + together, :] = arrived[device, row : row + together, :]
    wide = pick(jnp.concatenate([layers[0], layers[1]], 1), table[...])
    shares = pltpu.roll(wide[:, 384:512], own_layers, 0)
    turned[pl.ds(0, 128, stride=3), :] = wide[:, 0:128] + shares
    for c in range(1, 3):
        turned[pl.ds(c, 128, stride=3), :] = wide[:, 128 * c : 128 * c + 128]
    for part in range(3):
        span = slice(128 * part, 128 * part + 128)
        back = turned[span, :].T
        for component in range(3):
            for layer in range(6):
                at = stack_row(0, component, layer, 0)
                out[component, layer, :, span] = back[at : at + 3, :]
    back = wide[:, 0:128].T
    for component in range(3):
        for x in range(2):
            at = 54 + 2 * component + x
            coarse_out[component, x] = back[at : at + 1, :]


def cofactor_rows(deform):
    return [
        [
            deform[(row_at + 1) % 3][(column + 1) % 3] * deform[(row_at + 2) % 3][(column + 2) % 3]
            - deform[(row_at + 1) % 3][(column + 2) % 3]
            * deform[(row_at + 2) % 3][(column + 1) % 3]
            for column in range(3)
        ]
        for row_at in range(3)
    ]


def point_stress(deform):
    cofactors = cofactor_rows(deform)
    jacobian = (
        deform[0][0] * cofactors[0][0]
        + deform[0][1] * cofactors[0][1]
        + deform[0][2] * cofactors[0][2]
    )
    pressure = lame_ratio * (jacobian - rest_ratio)
    return [
        [deform[i][d] + pressure * cofactors[i][d] for d in range(3)] for i in range(3)
    ]


coarse_samples = [0.5 - 0.5 / math.sqrt(3.0), 0.5 + 0.5 / math.sqrt(3.0)]
two = range(2)


def at_points(low, high):
    change = high - low
    return [low + s * change for s in coarse_samples], change * (1.0 / element_span)


def ends_of(first, second):
    high = coarse_samples[0] * first + coarse_samples[1] * second
    return [first + second - high, high]


def high_low(values):
    high = values.astype(jnp.bfloat16)
    return high, (values - high.astype(jnp.float32)).astype(jnp.bfloat16)


def reads(pairs):
    return set(range(pairs[0], pairs[-1] + 2))


def plan_steps(spans):
    plan = []
    for first, count in spans:
        pairs = list(range(first, first + count))
        plan.append([pairs[n : n + 2] for n in range(0, count, 2)])
    return plan


class Slab:
    def __init__(self, width, across):
        self.width = width
        self.y_step = 2 * across
        lane = lax.broadcasted_iota(jnp.int32, (8, width), 1)
        x = (lane // 2) % across
        self.bottom, self.top, self.even = x == 0, x == across - 1, lane % 2 == 0
        self.row = lax.broadcasted_iota(jnp.int32, (8, width), 0)
        row = lax.broadcasted_iota(jnp.int32, (32, width), 0)
        lane = lax.broadcasted_iota(jnp.int32, (32, width), 1)
        on_face = (row == 0) | ((row >= 3) & (row <= 11))
        self.keep = jnp.where(on_face & ((lane // 2) % across == 0), 0.0, 1.0)

    def lanes(self, v, step):
        return pltpu.roll(v, step % self.width, 1)

    def from_next(self, v, x, y):
        if x or y:
            v = self.lanes(v, -2 * x - self.y_step * y)
        return jnp.where(self.top, 0.0, v) if x else v

    def from_next_z(self, v, ahead, x, y):
        step = -2 * x - self.y_step * y
        v = jnp.where(self.even, self.lanes(v, step - 1), self.lanes(ahead, step + 1))
        return jnp.where(self.top, 0.0, v) if x else v

    def onto_next(self, v, x, y, z=0):
        if x or y or z:
            v = self.lanes(v, 2 * x + self.y_step * y + z)
        return jnp.where(self.bottom, 0.0, v) if x else v

    def gather(self, component, here, ahead):
        row = self.row
        g0, g1, g2, g3 = here[0:8], here[8:16], here[16:24], here[24:32]
        a0 = ahead[0:8]
        z0, xz = self.from_next_z(g0, a0, 0, 0), self.from_next_z(g0, a0, 1, 0)
        yz, xyz = self.from_next_z(g0, a0, 0, 1), self.from_next_z(g0, a0, 1, 1)
        z2 = self.from_next_z(g2, ahead[16:24], 0, 0)
        edges = jnp.where(row <= 4, xz, self.from_next(g0, 1, 1))
        edges = jnp.where(row == 0, xyz, jnp.where(row <= 2, yz, edges))
        return jnp.concatenate(
            [
                g0,
                g1,
                g2,
                jnp.where(row < 4, z2, g3),
                self.from_next(g0, 1, 0),
                jnp.where(row == 7, yz, self.from_next(g0, 0, 1)),
                jnp.where(row == 7, xz, z0),
                jnp.where(row < 4, self.from_next(g1, 1, 0), self.from_next(g1, 0, 1)),
                edges,
                jnp.where(row == component, 1.0, 0.0),
            ],
            0,
        )

    def scatter(self, part, behind):
        row = self.row
        g0, g1, g2, g3, x0, y0, z0, sides, edges = (part[8 * n : 8 * n + 8] for n in range(9))
        last = row == 7
        for_z = jnp.where(last, 0.0, z0)
        for_xz = jnp.where(last, z0, jnp.where((row == 3) | (row == 4), edges, 0.0))
        for_yz = jnp.where(last, y0, jnp.where((row == 1) | (row == 2), edges, 0.0))
        for_xyz = jnp.where(row == 0, edges, 0.0)
        for_xy = jnp.where(row >= 5, edges, 0.0)

        def above(z):
            return (
                self.onto_next(for_z, 0, 0, z)
                + self.onto_next(for_yz, 0, 1, z)
                + self.onto_next(for_xz, 1, 0, z)
                + self.onto_next(for_xyz, 1, 1, z)
            )

        own0 = g0 + self.onto_next(x0, 1, 0) + self.onto_next(jnp.where(last, 0.0, y0), 0, 1)
        own0 = own0 + self.onto_next(for_xy, 1, 1)
        own0 = own0 + jnp.where(self.even, behind[0], above(1))
        own1 = g1 + jnp.where(row < 4, self.onto_next(sides, 1, 0), self.onto_next(sides, 0, 1))
        share2 = jnp.where(self.even, behind[1], self.onto_next(g3, 0, 0, 1))
        own2 = g2 + jnp.where(row < 4, share2, 0.0)
        moved = (above(-1), self.onto_next(g3, 0, 0, -1))
        return jnp.concatenate([self.twinned(own0), own1, own2, g3], 0), moved

    def twinned(self, v):
        twins = jnp.where(self.row == 7, pltpu.roll(v, 7, 0), 0.0)
        return v + jnp.where(self.row == 0, pltpu.roll(v, 1, 0), twins)

    def absorb(self, total, behind):
        low = self.twinned(jnp.where(self.even, behind[0], 0.0))
        high = jnp.where(self.even & (self.row < 4), behind[1], 0.0)
        return jnp.concatenate(
            [total[0:8] + low, total[8:16], total[16:24] + high, total[24:32]], 0
        )

    def gradient(self, u, spread, pairs):
        parts = [
            high_low(self.gather(i, u[i, pair], u[i, pair + 1]))
            for i in range(3)
            for pair in pairs
        ]
        return jnp.dot(
            spread[...],
            jnp.concatenate([jnp.concatenate([h, l, h], 0) for h, l in parts], 1),
            preferred_element_type=jnp.float32,
        )

    def force(self, gradient, stiff, collect, pairs):
        width, count = self.width, len(pairs)
        rows = 16
        high, low = {}, {}
        for q in range(count):
            for r in range(64 // rows):
                deform = [
                    [
                        gradient[
                            64 * e + rows * r : 64 * e + rows * (r + 1),
                            width * (count * i + q) : width * (count * i + q + 1),
                        ]
                        for e in range(3)
                    ]
                    for i in range(3)
                ]
                stress = point_stress(deform)
                for i in range(3):
                    for e in range(3):
                        high[e, r, i, q], low[e, r, i, q] = high_low(stress[i][e])

        def whole(part):
            return jnp.concatenate(
                [
                    jnp.concatenate([part[e, r, i, q] for i in range(3) for q in range(count)], 1)
                    for e in range(3)
                    for r in range(64 // rows)
                ],
                0,
            )

        force = jnp.dot(collect[...], whole(high), preferred_element_type=jnp.float32)
        force = force[0:ROWS] + (
            force[ROWS:]
            + jnp.dot(collect[0:ROWS], whole(low), preferred_element_type=jnp.float32)
        )
        stiffness = [stiff[pair : pair + 1, :] for pair in pairs]
        return force * jnp.concatenate(stiffness * 3, 1)

    def run(self, u, stiff, spread, collect, jobs, given=None):
        plan = plan_steps([job[:2] for job in jobs])
        steps = [(pairs, n) for n, chunks in enumerate(plan) for pairs in chunks]
        none = jnp.zeros((8, self.width), jnp.float32)
        ahead, carry, job = None, None, None
        for at, (pairs, n) in enumerate(steps):
            ready = given is not None and n == 0 and pairs == given[0]
            gradient = ahead
            if ahead is None and not ready:
                gradient = self.gradient(u, spread, pairs)
            if not ready:
                ahead = None
            if ahead is None and at + 1 < len(steps):
                later, later_job = steps[at + 1]
                if given is not None and later_job == 0 and later == given[0]:
                    later, later_job = steps[at + 2]
                if later_job == n or not reads(later) & set(pairs):
                    ahead = self.gradient(u, spread, later)
            if job != n:
                carry, job = [(none, none) for i in range(3)], n
            if ready:
                for q, pair in enumerate(pairs):
                    total = given[1][q]
                    if q == 0:
                        total = [self.absorb(total[i], carry[i]) for i in range(3)]
                    jobs[n][2](pair, total)
                carry = list(given[2])
                continue
            force = self.force(gradient, stiff, collect, pairs)
            totals = [[] for pair in pairs]
            for q in range(len(pairs)):
                for i in range(3):
                    lane = (len(pairs) * i + q) * self.width
                    total, carry[i] = self.scatter(force[:, lane : lane + self.width], carry[i])
                    totals[q].append(total)
            for pair, total in zip(pairs, totals):
                jobs[n][2](pair, total)
        return carry

    def smoothing(self, u, f, f_shift, d, spans, bound):
        jobs = []
        for (first, count), (held, added) in zip(spans, chebyshev_steps()):

            def finish(pair, forces, held=held, added=added):
                for i in range(3):
                    z = (added / bound) * self.keep * (f[i, pair + f_shift] - forces[i])
                    move = held * d[i, pair] + z if held else z
                    d[i, pair] = move
                    u[i, pair] = u[i, pair] + move

            jobs.append((first, count, finish))
        return jobs

    def owed(self, carry, bound):
        scale = -chebyshev_steps()[-1][1] / bound
        return [
            (
                scale * jnp.where(self.even, low, 0.0) * self.keep[0:8],
                scale * jnp.where(self.even, high, 0.0) * self.keep[16:24],
            )
            for low, high in carry
        ]

    def corners_of(self, v):
        ahead = pltpu.roll(v, 7, 0)
        found = {}
        for a in range(2):
            for b in range(2):
                found[a, b, 0] = self.from_next(v, a, b)
                found[a, b, 1] = self.from_next_z(v, ahead, a, b)
        return found

    def assemble(self, part):
        here, odd, even = 0.0, 0.0, 0.0
        for a in range(2):
            for b in range(2):
                here = here + self.onto_next(part[a, b, 0], a, b)
                odd = odd + self.onto_next(part[a, b, 1], a, b, 1)
                even = even + self.onto_next(part[a, b, 1], a, b, -1)
        return here + jnp.where(self.even, pltpu.roll(even, 1, 0), odd)

    def coarse_force(self, values, stiffness):
        grads = []
        for i in range(3):
            v = self.corners_of(values[i])
            vz, sz = {}, {}
            for a in two:
                for b in two:
                    vz[a, b], sz[a, b] = at_points(v[a, b, 0], v[a, b, 1])
            vv, vs, sv = {}, {}, {}
            for a in two:
                for k in two:
                    vv[a, k], vs[a, k] = at_points(vz[a, 0][k], vz[a, 1][k])
                sv[a], unused = at_points(sz[a, 0], sz[a, 1])
            dx, dy, dz = {}, {}, {}
            for k in two:
                for j in two:
                    dx[j, k] = (vv[1, k][j] - vv[0, k][j]) * (1.0 / element_span)
                line, unused = at_points(vs[0, k], vs[1, k])
                for h in two:
                    dy[h, k] = line[h]
            for j in two:
                line, unused = at_points(sv[0][j], sv[1][j])
                for h in two:
                    dz[h, j] = line[h]
            grads.append((dx, dy, dz))
        weight = element_span**2 / 8.0
        scaled = weight * stiffness
        sums = [({}, {}, {}) for i in range(3)]

        def add(table, key, value):
            table[key] = table[key] + value if key in table else value

        for h in two:
            for j in two:
                for k in two:
                    deform = [
                        [grads[i][0][j, k], grads[i][1][h, k], grads[i][2][h, j]]
                        for i in range(3)
                    ]
                    for i in range(3):
                        deform[i][i] = deform[i][i] + 1.0
                    stress = point_stress(deform)
                    for i in range(3):
                        add(sums[i][0], (j, k), stress[i][0])
                        add(sums[i][1], (h, k), stress[i][1])
                        add(sums[i][2], (h, j), stress[i][2])

        forces = []
        for i in range(3):
            part = {}
            qx, qy, qz = sums[i]
            along_z = [ends_of(qx[j, 0], qx[j, 1]) for j in two]
            for c in two:
                line = ends_of(along_z[0][c], along_z[1][c])
                for b in two:
                    part[0, b, c] = -line[b]
                    part[1, b, c] = line[b]
            along_z = [ends_of(qy[h, 0], qy[h, 1]) for h in two]
            for c in two:
                line = ends_of(along_z[0][c], along_z[1][c])
                for a in two:
                    part[a, 0, c] = part[a, 0, c] - line[a]
                    part[a, 1, c] = part[a, 1, c] + line[a]
            along_y = [ends_of(qz[h, 0], qz[h, 1]) for h in two]
            for b in two:
                line = ends_of(along_y[0][b], along_y[1][b])
                for a in two:
                    part[a, b, 0] = part[a, b, 0] - line[a]
                    part[a, b, 1] = part[a, b, 1] + line[a]
            forces.append(self.assemble({key: scaled * value for key, value in part.items()}))
        return forces


def window_pair(slab, first_layer, own_layers, fetch):
    found = []
    for parity in range(2):
        layer = first_layer + parity
        device = layer // own_layers
        layer = layer - device * own_layers
        found.append((device, layer // 2, layer % 2))
    values = [fetch(device, q) for device, q, parity in found]
    if found[0][:2] == found[1][:2] or (values[0] is None and values[1] is None):
        return values[0]
    for parity in range(2):
        if values[parity] is None:
            values[parity] = jnp.zeros_like(values[1 - parity])
        elif found[parity][2] != parity:
            values[parity] = slab.lanes(values[parity], 2 * parity - 1)
    lane = lax.broadcasted_iota(jnp.int32, values[0].shape, 1)
    return jnp.where(lane % 2 == 0, values[0], values[1])


def first_sources(own_layers):
    return list(range(-BEFORE // own_layers, (own_layers + BEFORE - 1) // own_layers + 1))


def whole_pairs(own_layers):
    return own_layers == 4


def turn_rows(block, mixed, turned, width, at):
    for tile in range(SENT // 128):
        n = at * (SENT // 128) + tile
        for m in range(width // 4):
            first = 12 * m + 4 * tile
            mixed[n, 4 * m : 4 * m + 4, :] = block[first : first + 4, :]
        turned[at, 128 * tile : 128 * tile + 128, :] = mixed[n].T


def regroup(slab, field, rows):
    values, hard = [], None
    for i in range(3):
        parts = [rows(24 * i + 8 * n) for n in range(3)]
        if field == 0 and i == 0:
            hard = parts[0][TWIN : TWIN + 1]
        parts[0] = jnp.where(slab.row == TWIN, pltpu.roll(parts[0], TWIN, 0), parts[0])
        parts.append(jnp.where(slab.row < 4, 0.0, rows(68 + 4 * i)))
        whole = jnp.concatenate(parts, 0)
        values.append(whole * slab.keep if field == 0 else whole)
    return values, hard


def layer_above(slab, turned, at, i):
    first = NEXT_COLUMN + 12 * i
    low, high = turned[at, first : first + 8, :], turned[at, first + 4 : first + 12, :]
    high = jnp.where(slab.row < 4, pltpu.roll(high, 4, 0), 0.0)
    low = jnp.where(slab.row == TWIN, pltpu.roll(low, TWIN, 0), low)
    nothing = jnp.zeros_like(low)
    return jnp.concatenate([low, nothing, high, nothing], 0) * slab.keep


def make_own_kernel(width, across, own_layers):
    own_pairs = own_layers // 2
    pairs = list(range(own_pairs))

    def own_kernel(block, spread, collect, u, f, stiff, forces, moved, mixed, turned):
        slab = Slab(width, across)
        turn_rows(block, mixed, turned, width, 0)
        for pair in pairs:
            for field, target in enumerate((u, f)):

                def rows(start, field=field, pair=pair):
                    at = BLOCK * (2 * pair + field) + start
                    return turned[0, at : at + 8, :]

                values, hard = regroup(slab, field, rows)
                for i in range(3):
                    target[i, pair] = values[i]
                if field == 0:
                    stiff[pair : pair + 1, :] = hard
        for i in range(3):
            u[i, own_pairs] = layer_above(slab, turned, 0, i)

        def finish(pair, total):
            for i in range(3):
                forces[i, pair] = total[i]

        carry = slab.run(u, stiff, spread, collect, [(0, own_pairs, finish)])
        for i in range(3):
            moved[i, 0] = carry[i][0]
            moved[i, 1] = carry[i][1]

    return own_kernel


def make_first_kernel(width, across, own_layers, fine_bound):
    own = BEFORE // 2
    own_pairs = (own_layers + 1) // 2
    spans = []
    prepared = whole_pairs(own_layers)
    for n in (4, 3, 2, 1):
        low, high = BEFORE - n, BEFORE + own_layers + n - 1 + prepared
        spans.append((low // 2, (high + 1) // 2 - low // 2))
    sources = [n for n in first_sources(own_layers) if n or not prepared]

    def first_kernel(*refs):
        arrived = refs[: len(sources)]
        refs = refs[len(sources) :]
        if prepared:
            own_u, own_f, own_stiff, own_forces, own_moved = refs[:5]
            refs = refs[5:]
        spread, collect, transfer, message, *sent, f, u, d, stiff, shares, mixed, turned = refs
        slab = Slab(width, across)
        if not prepared:
            u[...] = jnp.zeros(u.shape, jnp.float32)
            f[...] = jnp.zeros(f.shape, jnp.float32)
        shares[...] = jnp.zeros(shares.shape, jnp.float32)
        stiff[...] = jnp.zeros(stiff.shape, jnp.float32)
        for n in range(len(sources)):
            turn_rows(arrived[n], mixed, turned, width, n)
        for pair in range(PAIRS):
            if prepared and own <= pair < own + own_pairs:
                for i in range(3):
                    u[i, pair] = own_u[i, pair - own]
                    f[i, pair] = own_f[i, pair - own]
                stiff[pair : pair + 1, :] = own_stiff[pair - own : pair - own + 1, :]
                continue
            for field, target in enumerate((u, f)):

                def rows(start, field=field, pair=pair):
                    def fetch(device, q):
                        if device not in sources:
                            return None
                        at = BLOCK * (2 * q + field) + start
                        return turned[sources.index(device), at : at + 8, :]

                    value = window_pair(slab, 2 * pair - BEFORE, own_layers, fetch)
                    return jnp.zeros((8, width), jnp.float32) if value is None else value

                values, hard = regroup(slab, field, rows)
                for i in range(3):
                    target[i, pair] = values[i]
                if field == 0:
                    stiff[pair : pair + 1, :] = hard
        given = None
        if prepared:
            for i in range(3):
                u[i, PAIRS] = layer_above(slab, turned, sources.index(1), i)
            given = (
                list(range(own, own + own_pairs)),
                [[own_forces[i, q] for i in range(3)] for q in range(own_pairs)],
                [(own_moved[i, 0], own_moved[i, 1]) for i in range(3)],
            )

        weights = [jnp.broadcast_to(transfer[:, n : n + 1], (32, width)) for n in range(8)]

        def restrict(pair, forces):
            for i in range(3):
                rest = slab.keep * (f[i, pair] - forces[i])
                for n in range(8):
                    part = rest * weights[n]
                    part = (part[0:8] + part[8:16]) + (part[16:24] + part[24:32])
                    shares[i, n, pl.ds(pair, 1), :] = jnp.sum(part, axis=0, keepdims=True)

        jobs = slab.smoothing(u, f, 0, d, spans[0:3], fine_bound)
        slab.run(u, stiff, spread, collect, jobs + [(*spans[3], restrict)], given)

        restricted = [
            slab.assemble({corner: shares[i, n] for n, corner in enumerate(CORNERS)})
            for i in range(3)
        ]
        def line(rows, q):
            return rows[own + q : own + q + 1]

        for q in range(own_pairs):
            for i in range(3):
                message[i, q] = u[i, own + q]
                message[i, q, RESTRICTED_SLOT : RESTRICTED_SLOT + 1, :] = line(restricted[i], q)
            message[0, q, STIFF_SLOT : STIFF_SLOT + 1, :] = line(stiff, q)
        if prepared:
            down, up = sent
            for i in range(3):
                down[i, 0:32] = u[i, own]
                down[i, 32:40] = u[i, own + 1, 0:8, :]
                down[i, 40:48] = u[i, own + 1, 16:24, :]
                up[i] = u[i, own + 1]
                for n, row in enumerate(
                    (line(restricted[i], 0), line(restricted[i], 1), u[i, own + 2, 0:1, :])
                    + (line(restricted[i], 2),)
                ):
                    down[i, 24 + n : 25 + n, :] = row
                for n, row in enumerate(
                    (line(restricted[i], 1), line(restricted[i], 0), u[i, own, 0:1, :])
                ):
                    up[i, 24 + n : 25 + n, :] = row
            for q in range(own_pairs):
                down[q, 32 + TWIN : 33 + TWIN, :] = line(stiff, q)
                up[q, TWIN : TWIN + 1, :] = line(stiff, q)
            return
        edge = sent[0]
        for q in range(own_pairs):
            for i in range(3):
                edge[q, i : i + 1, :] = u[i, own + q, 0:1, :]
                edge[q, 3 + i : 4 + i, :] = line(restricted[i], q)
            edge[q, 6:8, :] = jnp.broadcast_to(line(stiff, q), (2, width))

    return first_kernel


def shares_sent(own_layers):
    return own_layers % 2 == 0


def sources_of(own_layers):
    below = 2 if shares_sent(own_layers) else 3
    whole = range(-below // own_layers, (own_layers + 2) // own_layers + 1)
    coarse = range(-(below + 2) // own_layers, (own_layers + 4) // own_layers + 1)
    return list(whole), [n for n in coarse if n not in whole]


def message_line(message, q, n):
    i, slot = ((n, 0), (n - 3, RESTRICTED_SLOT), (0, STIFF_SLOT))[n // 3]
    return message[i, q, slot : slot + 1, :]


def sent_readers(slab, up, message, down):
    def block_of(device, q, i):
        if device == 0:
            return message[i, q]
        if (device, q) == (1, 0):
            whole = down[i, 0:32]
        elif (device, q) == (1, 1):
            low, high = down[i, 32:40], down[i, 40:48]
            low = jnp.where(slab.row == TWIN, pltpu.roll(low, TWIN, 0), low)
            whole = jnp.concatenate([low, jnp.zeros_like(low), high, jnp.zeros_like(low)], 0)
        elif (device, q) == (-1, 1):
            low = up[i, 0:8]
            low = jnp.where(slab.row == TWIN, pltpu.roll(low, TWIN, 0), low)
            whole = jnp.concatenate([low, up[i, 8:32]], 0)
        else:
            return None
        return whole

    def line_of(device, q, n):
        if device == 0:
            return message_line(message, q, n)
        kind, i = n // 3, n % 3
        if device == 1:
            row = ((0, 24), (32, 25))[q][kind] if kind < 2 else 32 + TWIN
            i = i if kind < 2 else q
            return down[i, row : row + 1, :]
        if device == -1:
            row = ((26, 25), (0, 24))[q][kind] if kind < 2 else TWIN
            i = i if kind < 2 else q
            return up[i, row : row + 1, :]
        if (device, q) == (2, 0) and kind < 2:
            return down[i, 26 + kind : 27 + kind, :]
        return None

    return block_of, line_of


def make_second_kernel(width, across, own_layers, fine_bound, coarse_bound):
    own = BEFORE_B // 2
    own_pairs = (own_layers + 1) // 2
    shift = (BEFORE - BEFORE_B) // 2
    whole, outer = sources_of(own_layers)
    steps = chebyshev_steps()
    spans = []
    for n in (3, 2, 1):
        low, high = BEFORE_B - n + shares_sent(own_layers), BEFORE_B + own_layers + n - 1
        spans.append((low // 2, (high + 1) // 2 - low // 2))

    def second_kernel(*refs):
        slab = Slab(width, across)
        if whole_pairs(own_layers):
            up, message, down = refs[:3]
            refs = refs[3:]
            block_of, line_of = sent_readers(slab, up, message, down)
        else:
            messages = dict(zip(whole, refs))
            edges = dict(zip(outer, refs[len(whole) :]))
            refs = refs[len(whole) + len(outer) :]

            def block_of(device, q, i):
                return messages[device][i, q] if device in messages else None

            def line_of(device, q, n):
                if device in messages:
                    return message_line(messages[device], q, n)
                return edges[device][q, n : n + 1, :] if device in edges else None

        f, spread, collect, transfer_back, out, u, d, stiff, coarse = refs

        def pair_of(pair, fetch):
            return window_pair(slab, 2 * pair - BEFORE_B, own_layers, fetch)

        coarse[...] = jnp.zeros(coarse.shape, jnp.float32)
        for pair in range(PAIRS_B):
            for i in range(3):
                block = pair_of(pair, lambda device, q: block_of(device, q, i))
                u[i, pair] = jnp.zeros((32, width), jnp.float32) if block is None else block
            for n in range(7):
                line = pair_of(pair, lambda device, q: line_of(device, q, n))
                if line is not None:
                    coarse[n, pair : pair + 1, :] = line
        stiff[...] = coarse[6]

        stiffness = coarse[6]
        keep_coarse = jnp.where(slab.bottom, 0.0, 1.0)
        start = [coarse[i] for i in range(3)]
        restricted = [coarse[3 + i] for i in range(3)]
        before = slab.coarse_force(start, stiffness)
        move = [(steps[0][1] / coarse_bound) * keep_coarse * restricted[i] for i in range(3)]
        level = [start[i] + move[i] for i in range(3)]
        for held, added in steps[1:]:
            force = slab.coarse_force(level, stiffness)
            for i in range(3):
                z = keep_coarse * (restricted[i] + before[i] - force[i])
                move[i] = held * move[i] + (added / coarse_bound) * z
                level[i] = level[i] + move[i]

        weights = [jnp.broadcast_to(transfer_back[:, n : n + 1], (32, width)) for n in range(8)]
        for i in range(3):
            change = slab.corners_of(level[i] - start[i])
            for pair in range(spans[0][0], min(spans[0][0] + spans[0][1] + 1, PAIRS_B)):
                lift = u[i, pair]
                for n, corner in enumerate(CORNERS):
                    lift = lift + weights[n] * change[corner][pair : pair + 1]
                u[i, pair] = lift

        jobs = slab.smoothing(u, f, shift, d, spans, fine_bound)
        owed = slab.owed(slab.run(u, stiff, spread, collect, jobs), fine_bound)

        lower = lax.broadcasted_iota(jnp.int32, (width // 8, 8, 128), 1) < 4
        nothing = jnp.zeros((8, width), jnp.float32)
        sides = []
        for q in range(2):
            if q or not shares_sent(own_layers):
                owed = [(nothing, nothing)] * 3
            rows = []
            for i in range(3):
                value = u[i, own + q]
                rows += [value[0:24], jnp.where(slab.row < 4, owed[i][1], value[24:32])]
            rows += [owed[i][0] for i in range(3)]
            rows += [level[i][own + q : own + q + 1] for i in range(3)] + [nothing[0:5]]
            sides.append(jnp.concatenate(rows, 0).T.reshape(width // 8, 8, 128))
        out[:, 0] = jnp.where(lower, sides[0], pltpu.roll(sides[1], 4, 1))
        out[:, 1] = jnp.where(lower, pltpu.roll(sides[0], 4, 1), sides[1])

    return second_kernel


def solution(mesh):
    rows_of, columns_of = mesh.shape["gx"], mesh.shape["gy"]
    devices = rows_of * columns_of
    order = ring_order(rows_of, columns_of)
    own_layers = EZ // devices
    own_pairs = (own_layers + 1) // 2
    width = 4 * devices
    across = 2 * rows_of
    near = first_sources(own_layers)
    prepared = whole_pairs(own_layers)
    whole, outer = sources_of(own_layers)
    spread, collect, fine_bound = element_tables()
    coarse_bound = build_tables([0.0, 1.0], 2)[2]
    transfer, transfer_back = transfer_table()
    wide = pltpu.CompilerParams(vmem_limit_bytes=60 * 1024 * 1024)
    limit = pltpu.CompilerParams(vmem_limit_bytes=48 * 1024 * 1024)
    f32 = jnp.float32

    pack = pl.pallas_call(
        functools.partial(pack_kernel, order),
        out_shape=pltpu.VMEM((devices * 12, 128), f32),
        in_specs=[pl.BlockSpec(memory_space=pl.ANY)] * 5,
        out_specs=pl.BlockSpec(memory_space=pltpu.VMEM),
        scratch_shapes=[
            pltpu.VMEM((3, 6, 3, 384), f32),
            pltpu.VMEM((3, 6, 3, 384), f32),
            pltpu.VMEM((2, 1, EZ), f32),
            pltpu.VMEM((1, 1, 192), jnp.int32),
            pltpu.VMEM((384, 512), jnp.bfloat16),
            pltpu.VMEM((128, 384), f32),
            pltpu.VMEM((384, 128), f32),
            pltpu.VMEM((6, 136, 128), f32),
            pltpu.SemaphoreType.DMA((5,)),
        ],
        compiler_params=wide,
    )
    own = pl.pallas_call(
        make_own_kernel(width, across, own_layers),
        out_shape=(
            jax.ShapeDtypeStruct((3, own_pairs + 1, 32, width), f32),
            jax.ShapeDtypeStruct((3, own_pairs, 32, width), f32),
            jax.ShapeDtypeStruct((own_pairs, width), f32),
            jax.ShapeDtypeStruct((3, own_pairs, 32, width), f32),
            jax.ShapeDtypeStruct((3, 2, 8, width), f32),
        ),
        scratch_shapes=[
            pltpu.VMEM((SENT // 128, width, 128), f32),
            pltpu.VMEM((1, SENT, width), f32),
        ],
        compiler_params=limit,
        cost_estimate=pl.CostEstimate(flops=400_000_000, bytes_accessed=1_000_000, transcendentals=0),
    )
    sent = [jax.ShapeDtypeStruct((own_pairs, 8, width), f32)]
    if prepared:
        sent = [jax.ShapeDtypeStruct((3, rows, width), f32) for rows in (48, 32)]
    first = pl.pallas_call(
        make_first_kernel(width, across, own_layers, fine_bound),
        out_shape=(
            jax.ShapeDtypeStruct((3, own_pairs, 32, width), f32),
            *sent,
            jax.ShapeDtypeStruct((3, PAIRS, 32, width), f32),
        ),
        scratch_shapes=[
            pltpu.VMEM((3, 8, 32, width), f32),
            pltpu.VMEM((3, 8, 32, width), f32),
            pltpu.VMEM((8, width), f32),
            pltpu.VMEM((3, 8, 8, width), f32),
            pltpu.VMEM((len(near) * (SENT // 128), width, 128), f32),
            pltpu.VMEM((len(near), SENT, width), f32),
        ],
        compiler_params=limit,
    )
    second = pl.pallas_call(
        make_second_kernel(width, across, own_layers, fine_bound, coarse_bound),
        out_shape=jax.ShapeDtypeStruct((devices // 2, 2, 8, 128), f32),
        scratch_shapes=[
            pltpu.VMEM((3, PAIRS_B, 32, width), f32),
            pltpu.VMEM((3, PAIRS_B, 32, width), f32),
            pltpu.VMEM((PAIRS_B, width), f32),
            pltpu.VMEM((7, PAIRS_B, width), f32),
        ],
        compiler_params=limit,
    )
    unpack = pl.pallas_call(
        functools.partial(unpack_kernel, order),
        out_shape=(
            jax.ShapeDtypeStruct((3, 6, 3, 384), f32),
            jax.ShapeDtypeStruct((3, 2, 1, EZ), f32),
        ),
        scratch_shapes=[pltpu.VMEM((2, 128, 128), f32), pltpu.VMEM((384, 128), f32)],
        compiler_params=limit,
    )
    everyone = ("gy", "gx")

    def from_device(block, distance):
        place = {k: m % rows_of * columns_of + m // rows_of for m, k in enumerate(order)}
        route = [(place[(k + distance) % devices], place[k]) for k in range(devices)]
        return lax.ppermute(block, ("gx", "gy"), route)

    def body(initial, forcing, modulus, solid_list):
        sent = pack(initial, forcing, modulus, solid_list, jnp.asarray(pack_table()))
        sent = sent.reshape(devices, SENT // 128, 4, 128)
        arrived = lax.all_to_all(sent, everyone, 0, 0, tiled=True).reshape(devices * 12, 128)
        blocks = [from_device(arrived, n) if n else arrived for n in near]
        if prepared:
            blocks = [block for n, block in zip(near, blocks) if n]
            blocks += own(arrived, jnp.asarray(spread), jnp.asarray(collect))
        message, *edges, load = first(
            *blocks,
            jnp.asarray(spread),
            jnp.asarray(collect),
            jnp.asarray(transfer),
        )
        if prepared:
            down, up = edges
            messages = [from_device(up, -1), message, from_device(down, 1)]
        else:
            messages = [from_device(message, n) if n else message for n in whole]
            messages += [from_device(edges[0], n) for n in outer]
        result = second(
            *messages,
            load,
            jnp.asarray(spread),
            jnp.asarray(collect),
            jnp.asarray(transfer_back),
        )
        back = lax.all_to_all(result.reshape(devices, 8, 128), everyone, 0, 0, tiled=True)
        return unpack(back, jnp.asarray(unpack_table()))

    placed = (
        P(None, "gx", "gy", None),
        P(None, "gx", "gy", None),
        P("gx", "gy", None),
        P("gx", "gy", None),
    )
    return jax.shard_map(
        body,
        mesh=mesh,
        in_specs=placed,
        out_specs=(P(None, "gx", "gy", None), P(None, "gx", "gy", None)),
        check_vma=False,
    )
```

```python
import functools
import math

import jax
import jax.numpy as jnp
import numpy as np
from jax import lax
from jax.experimental import pallas as pl
from jax.experimental.pallas import tpu as pltpu
from jax.sharding import PartitionSpec as P

CHEB = 3
EZ = 128

element_span = 20.0
lame_ratio = 4.0
rest_ratio = 1.25
modulus_top = 2.0
spectrum_floor = 0.05
interval_centre = (1.0 + spectrum_floor) / 2.0
interval_radius = (1.0 - spectrum_floor) / 2.0
interval_ratio = interval_centre / interval_radius
inner_anchors = (0.5 - 0.5 / math.sqrt(5.0), 0.5 + 0.5 / math.sqrt(5.0))

BEFORE = 4
PAIRS = 6
BEFORE_B = 6
PAIRS_B = 8
BLOCK = 84
SENT = 384

SLOTS = [
    (0, 0, 0), (1, 0, 0), (2, 0, 0), (0, 1, 0), (0, 2, 0), (0, 0, 1), (0, 0, 2), None,
    (0, 1, 1), (0, 1, 2), (0, 2, 1), (0, 2, 2), (1, 0, 1), (1, 0, 2), (2, 0, 1), (2, 0, 2),
    (1, 1, 0), (1, 2, 0), (2, 1, 0), (2, 2, 0), (1, 1, 1), (1, 1, 2), (1, 2, 1), (1, 2, 2),
    None, None, None, None, (2, 1, 1), (2, 1, 2), (2, 2, 1), (2, 2, 2),
]
TWIN = 7
NEXT_SLOTS = [0, 1, 2, 3, 4, 5, 6, 7, 16, 17, 18, 19]
NEXT_COLUMN = 4 * BLOCK
RESTRICTED_SLOT = 24
STIFF_SLOT = 25
OWN_SHIFT, SHIFT_X, SHIFT_Y, SHIFT_Z = (0, 0, 0), (1, 0, 0), (0, 1, 0), (0, 0, 1)
ELEMENT_ROWS = (
    [(slot, OWN_SHIFT) for slot in range(24)]
    + [(slot, SHIFT_Z) for slot in range(16, 20)]
    + [(slot, OWN_SHIFT) for slot in range(28, 32)]
    + [(slot, SHIFT_X) for slot in range(7)] + [None]
    + [(slot, SHIFT_Y) for slot in range(7)] + [(0, (0, 1, 1))]
    + [(slot, SHIFT_Z) for slot in range(7)] + [(0, (1, 0, 1))]
    + [(slot, SHIFT_X) for slot in range(8, 12)] + [(slot, SHIFT_Y) for slot in range(12, 16)]
    + [(0, (1, 1, 1)), (1, (0, 1, 1)), (2, (0, 1, 1)), (3, (1, 0, 1)), (4, (1, 0, 1))]
    + [(5, (1, 1, 0)), (6, (1, 1, 0)), (0, (1, 1, 0))]
)
ROWS = len(ELEMENT_ROWS)
DEPTH = 80
CORNERS = [(a, b, c) for a in range(2) for b in range(2) for c in range(2)]


def gauss_rule(point_count):
    if point_count == 2:
        offset = 1.0 / math.sqrt(3.0)
        points = [-offset, offset]
        weights = [1.0, 1.0]
    else:
        inner = math.sqrt(3.0 / 7.0 - 2.0 / 7.0 * math.sqrt(6.0 / 5.0))
        outer = math.sqrt(3.0 / 7.0 + 2.0 / 7.0 * math.sqrt(6.0 / 5.0))
        heavy = (18.0 + math.sqrt(30.0)) / 36.0
        light = (18.0 - math.sqrt(30.0)) / 36.0
        points = [-outer, -inner, inner, outer]
        weights = [light, heavy, heavy, light]
    return (np.array(points), np.array(weights))


def lagrange_tables(anchors, samples):
    values = np.zeros((len(samples), len(anchors)))
    slopes = np.zeros((len(samples), len(anchors)))
    for sample_index, sample in enumerate(samples):
        for anchor_index, anchor in enumerate(anchors):
            others = [
                location
                for location_index, location in enumerate(anchors)
                if location_index != anchor_index
            ]
            product = 1.0
            for location in others:
                product = product * (sample - location) / (anchor - location)
            values[sample_index, anchor_index] = product
            derivative = 0.0
            for skipped in range(len(others)):
                summand = 1.0 / (anchor - others[skipped])
                for kept_index in range(len(others)):
                    if kept_index != skipped:
                        summand = (
                            summand * (sample - others[kept_index]) / (anchor - others[kept_index])
                        )
                derivative = derivative + summand
            slopes[sample_index, anchor_index] = derivative
    return (values, slopes)


def outer_three(first, second, third):
    return (
        first[:, None, None, :, None, None]
        * second[None, :, None, None, :, None]
        * third[None, None, :, None, None, :]
    )


def build_tables(anchors, point_count):
    raw_points, raw_weights = gauss_rule(point_count)
    samples = (raw_points + 1.0) / 2.0
    weights = raw_weights / 2.0
    basis_values, slopes = lagrange_tables(anchors, samples)
    quad_total = point_count**3
    nodal_count = len(anchors) ** 3
    derivative_one = outer_three(slopes, basis_values, basis_values).reshape(
        quad_total, nodal_count
    )
    derivative_two = outer_three(basis_values, slopes, basis_values).reshape(
        quad_total, nodal_count
    )
    derivative_three = outer_three(basis_values, basis_values, slopes).reshape(
        quad_total, nodal_count
    )
    stacked = np.stack([derivative_one, derivative_two, derivative_three]) / element_span
    volume = (weights[:, None, None] * weights[None, :, None] * weights[None, None, :]).reshape(
        -1
    ) * element_span**3
    forward = stacked.reshape(3 * quad_total, nodal_count)
    backward = (stacked * volume[None, :, None]).reshape(3 * quad_total, nodal_count).T
    weighted = stacked * volume[None, :, None]
    laplace = weighted[0].T @ stacked[0] + weighted[1].T @ stacked[1] + weighted[2].T @ stacked[2]
    matrix = np.zeros((nodal_count, 3, nodal_count, 3))
    for first in range(3):
        for second in range(3):
            block = weighted[second].T @ stacked[first] + (lame_ratio - 1.0) * (
                weighted[first].T @ stacked[second]
            )
            if first == second:
                block = block + laplace
            matrix[:, first, :, second] = block
    matrix = matrix.reshape(3 * nodal_count, 3 * nodal_count)
    vector = 1.5 + np.cos(1.3 * np.arange(3 * nodal_count))
    for repeat in range(200):
        vector = matrix @ vector
        vector = vector / np.sqrt(vector @ vector)
    largest = vector @ (matrix @ vector)
    return (forward, backward, float(4.0 * modulus_top * 1.1 * largest))


def row_nodes():
    nodes = []
    for entry in ELEMENT_ROWS:
        slot = SLOTS[entry[0]] if entry else None
        if slot is None or any(s and n for s, n in zip(entry[1], slot)):
            nodes.append(None)
        else:
            a, b, c = (3 * s + n for s, n in zip(entry[1], slot))
            nodes.append(16 * a + 4 * b + c)
    return nodes


def halves(matrix):
    whole = np.asarray(matrix, np.float32)
    high = whole.astype(jnp.bfloat16)
    low = (whole - high.astype(np.float32)).astype(jnp.bfloat16)
    return high, low


def element_tables():
    forward, backward, bound = build_tables([0.0, inner_anchors[0], inner_anchors[1], 1.0], 4)
    spread = np.zeros((forward.shape[0], DEPTH))
    collect = np.zeros((ROWS, backward.shape[1]))
    for row, node in enumerate(row_nodes()):
        if node is not None:
            spread[:, row] = forward[:, node]
            collect[row, :] = backward[node, :]
    for column in range(3):
        spread[64 * column : 64 * column + 64, ROWS + column] = 1.0
    spread_high, spread_low = halves(spread)
    collect_high, collect_low = halves(collect)
    return (
        np.concatenate([spread_high, spread_high, spread_low], 1),
        np.concatenate([collect_high, collect_low], 0),
        bound,
    )


def corner_tables():
    anchors = [0.0, inner_anchors[0], inner_anchors[1], 1.0]
    backward = build_tables(anchors, 4)[1]
    reach = np.stack([1.0 - np.array(anchors), np.array(anchors)])
    weights = outer_three(reach, reach, reach).reshape(8, 64)
    held = np.arange(64) < 16
    from_stress = np.concatenate([weights @ backward, np.where(held, 0.0, weights) @ backward], 0)
    from_loads = np.zeros((16, 32))
    from_loads[:8] = transfer_table()[0].T
    loads_high, loads_low = halves(from_loads)
    return (
        np.concatenate(halves(from_stress), 0),
        np.concatenate([loads_high, loads_high, loads_low], 1),
    )


def transfer_table():
    table = np.zeros((8, 32))
    reach = (0.0, inner_anchors[0], inner_anchors[1])
    for row, corner in enumerate(CORNERS):
        for column, slot in enumerate(SLOTS):
            if slot is not None:
                weight = 1.0
                for side, node in zip(corner, slot):
                    weight = weight * (reach[node] if side else 1.0 - reach[node])
                table[row, column] = weight
    back = table.T.copy()
    back[TWIN] = back[0]
    return table.T.astype(np.float32), back.astype(np.float32)


def chebyshev_steps():
    steps = [(0.0, 1.0 / interval_centre)]
    ratio_now = 1.0 / interval_ratio
    for sweep in range(1, CHEB):
        ratio_next = 1.0 / (2.0 * interval_ratio - ratio_now)
        steps.append((ratio_next * ratio_now, 2.0 * ratio_next / interval_radius))
        ratio_now = ratio_next
    return steps


def stack_row(field, component, layer, b):
    return field * 54 + component * 18 + layer * 3 + b


def block_column(component, slot):
    return 72 + 4 * component + slot - 28 if slot >= 24 else 24 * component + slot


def pack_table():
    table = np.zeros((3, 128, 2, 2, 128), np.float32)
    for field in range(2):
        for x in range(2):
            for component in range(3):
                for column, slot in enumerate(SLOTS):
                    if slot is not None:
                        a, b, c = slot
                        row = stack_row(field, component, 3 * x + a, b)
                        table[c, row, field, x, block_column(component, column)] = 1.0
                        if field == 0 and column in NEXT_SLOTS:
                            at = BLOCK + 12 * component + NEXT_SLOTS.index(column)
                            table[c, row, 1, x, at] = 1.0
            table[0, 108 + x, 0, x, TWIN] = 1.0
    return table.reshape(384, 512).astype(jnp.bfloat16)


def unpack_table():
    table = np.zeros((2, 128, 4, 128), np.float32)
    for x in range(2):
        for component in range(3):
            for column, slot in enumerate(SLOTS):
                if slot is not None:
                    a, b, c = slot
                    row = stack_row(0, component, 3 * x + a, b)
                    table[x, component * 32 + column, c, row] = 1.0
                    if column < 5:
                        table[x, 96 + 8 * component + column, 3, row] = 1.0
                    if column == 0:
                        table[x, 96 + 8 * component + TWIN, 3, row] = 1.0
                    if 16 <= column < 20:
                        table[x, component * 32 + column + 8, 3, row] = 1.0
            table[x, 120 + component, 0, 54 + 2 * component + x] = 1.0
    return table.reshape(256, 512).astype(jnp.bfloat16)


def pick(values, table):
    count = values.shape[0]
    parts = jnp.dot(
        jnp.concatenate(high_low(values), 0), table, preferred_element_type=jnp.float32
    )
    return parts[:count] + parts[count:]


def ring_order(rows_of, columns_of):
    if (rows_of, columns_of) != (4, 8):
        return list(range(rows_of * columns_of))
    order = []
    for z in range(4):
        for x in range(2):
            for y in range(2):
                chip = (z, 7 - z, 15 - z, 8 + z)[2 * x + y]
                order += [2 * chip, 2 * chip + 1]
    return order


def pack_kernel(
    order,
    initial_at, forcing_at, modulus_at, listing_at, table_at, out,
    initial, forcing, modulus, listing, table, rows, turned, places, ready,
):
    own_layers = EZ // len(order)
    sources = (listing_at, modulus_at, initial_at, forcing_at, table_at)
    copies = [
        pltpu.make_async_copy(source, here, ready.at[n])
        for n, (source, here) in enumerate(
            zip(sources, (listing, modulus, initial, forcing, table))
        )
    ]
    for copy in copies:
        copy.start()
    rows[108:128, :] = jnp.zeros((20, 384), jnp.float32)
    copies[0].wait()
    copies[1].wait()
    listed = listing[0].astype(jnp.float32)
    listed = jnp.concatenate([listed, jnp.full((1, 64), 256.0, jnp.float32)], 1)
    listed = jnp.broadcast_to(listed, (128, 256)).T
    lanes = lax.broadcasted_iota(jnp.int32, (256, 128), 1).astype(jnp.float32)
    row_at = lax.broadcasted_iota(jnp.int32, (128, 128), 0)
    stiff = jnp.zeros((128, 128), jnp.float32)
    for x in range(2):
        hit = jnp.max(jnp.where(listed == lanes + 128.0 * x, 1.0, 0.0), axis=0, keepdims=True)
        stiff = jnp.where(row_at == 108 + x, hit * modulus[x], stiff)
    copies[2].wait()
    copies[3].wait()
    for field, source in enumerate((initial, forcing)):
        for component in range(3):
            for layer in range(6):
                at = stack_row(field, component, layer, 0)
                rows[at : at + 3, :] = source[component, layer]
    for part in range(3):
        span = slice(128 * part, 128 * part + 128)
        turned[span, :] = rows[:, span].T
    picked = [turned[pl.ds(c, 128, stride=3), :] for c in range(3)]
    picked[0] = picked[0] + stiff.T
    copies[4].wait()
    wide = pick(jnp.concatenate(picked, 1), table[...])
    lane = lax.broadcasted_iota(jnp.int32, (128, 128), 1)
    for x in range(2):
        tiles = [None] * (SENT // 128)
        for n in range(4):
            pair, field = n // 2, n % 2
            moved = wide[:, 128 * (2 * field + x) : 128 * (2 * field + x) + 128]
            first = BLOCK * n
            if pair:
                moved = pltpu.roll(moved, 128 - 2 * pair, 0)
            if first % 128:
                moved = pltpu.roll(moved, first % 128, 1)
            for tile in range(first // 128, (first + BLOCK - 1) // 128 + 1):
                before = tiles[tile]
                if before is None:
                    tiles[tile] = moved
                else:
                    tiles[tile] = jnp.where(lane >= first - 128 * tile, moved, before)
        above = wide[:, 128 * (2 + x) : 128 * (2 + x) + 128]
        above = pltpu.roll(pltpu.roll(above, 128 - own_layers, 0), (NEXT_COLUMN - BLOCK) % 128, 1)
        tiles[-1] = jnp.where(lane >= NEXT_COLUMN % 128, above, tiles[-1])
        for tile in range(SENT // 128):
            places[3 * x + tile, 0:128, :] = tiles[tile]
            places[3 * x + tile, 128:136, :] = jnp.zeros((8, 128), jnp.float32)
    for device, k in enumerate(order):
        for tile in range(SENT // 128):
            for x in range(2):
                at = 12 * device + 4 * tile + 2 * x
                out[at : at + 2, :] = places[
                    3 * x + tile, own_layers * k : own_layers * k + 2, :
                ]


def unpack_kernel(order, arrived, table, out, coarse_out, layers, turned):
    devices = arrived.shape[0]
    own_layers = EZ // devices
    together = min(own_layers, 2)
    for x in range(2):
        for layer in range(0, own_layers, 2):
            row = (layer // 2) * 4 + x * 2
            if order == sorted(order):
                for n in range(together):
                    at = pl.ds(layer + n, devices, stride=own_layers)
                    layers[x, at, :] = arrived[:, row + n, :]
                continue
            for device, k in enumerate(order):
                at = own_layers * k + layer
                layers[x, at : at + together, :] = arrived[device, row : row + together, :]
    wide = pick(jnp.concatenate([layers[0], layers[1]], 1), table[...])
    shares = pltpu.roll(wide[:, 384:512], own_layers, 0)
    turned[pl.ds(0, 128, stride=3), :] = wide[:, 0:128] + shares
    for c in range(1, 3):
        turned[pl.ds(c, 128, stride=3), :] = wide[:, 128 * c : 128 * c + 128]
    for part in range(3):
        span = slice(128 * part, 128 * part + 128)
        back = turned[span, :].T
        for component in range(3):
            for layer in range(6):
                at = stack_row(0, component, layer, 0)
                out[component, layer, :, span] = back[at : at + 3, :]
    back = wide[:, 0:128].T
    for component in range(3):
        for x in range(2):
            at = 54 + 2 * component + x
            coarse_out[component, x] = back[at : at + 1, :]


def cofactor_rows(deform):
    return [
        [
            deform[(row_at + 1) % 3][(column + 1) % 3] * deform[(row_at + 2) % 3][(column + 2) % 3]
            - deform[(row_at + 1) % 3][(column + 2) % 3]
            * deform[(row_at + 2) % 3][(column + 1) % 3]
            for column in range(3)
        ]
        for row_at in range(3)
    ]


def point_stress(deform):
    cofactors = cofactor_rows(deform)
    jacobian = (
        deform[0][0] * cofactors[0][0]
        + deform[0][1] * cofactors[0][1]
        + deform[0][2] * cofactors[0][2]
    )
    pressure = lame_ratio * (jacobian - rest_ratio)
    return [
        [deform[i][d] + pressure * cofactors[i][d] for d in range(3)] for i in range(3)
    ]


coarse_samples = [0.5 - 0.5 / math.sqrt(3.0), 0.5 + 0.5 / math.sqrt(3.0)]
two = range(2)


def at_points(low, high):
    change = high - low
    return [low + s * change for s in coarse_samples], change * (1.0 / element_span)


def ends_of(first, second):
    high = coarse_samples[0] * first + coarse_samples[1] * second
    return [first + second - high, high]


def high_low(values):
    high = values.astype(jnp.bfloat16)
    return high, (values - high.astype(jnp.float32)).astype(jnp.bfloat16)


def reads(pairs):
    return set(range(pairs[0], pairs[-1] + 2))


def plan_steps(spans):
    plan = []
    for first, count in spans:
        pairs = list(range(first, first + count))
        plan.append([pairs[n : n + 2] for n in range(0, count, 2)])
    return plan


class Slab:
    def __init__(self, width, across):
        self.width = width
        self.y_step = 2 * across
        lane = lax.broadcasted_iota(jnp.int32, (8, width), 1)
        x = (lane // 2) % across
        self.bottom, self.top, self.even = x == 0, x == across - 1, lane % 2 == 0
        self.row = lax.broadcasted_iota(jnp.int32, (8, width), 0)
        row = lax.broadcasted_iota(jnp.int32, (32, width), 0)
        lane = lax.broadcasted_iota(jnp.int32, (32, width), 1)
        on_face = (row == 0) | ((row >= 3) & (row <= 11))
        self.keep = jnp.where(on_face & ((lane // 2) % across == 0), 0.0, 1.0)

    def lanes(self, v, step):
        return pltpu.roll(v, step % self.width, 1)

    def from_next(self, v, x, y):
        if x or y:
            v = self.lanes(v, -2 * x - self.y_step * y)
        return jnp.where(self.top, 0.0, v) if x else v

    def from_next_z(self, v, ahead, x, y):
        step = -2 * x - self.y_step * y
        v = jnp.where(self.even, self.lanes(v, step - 1), self.lanes(ahead, step + 1))
        return jnp.where(self.top, 0.0, v) if x else v

    def onto_next(self, v, x, y, z=0):
        if x or y or z:
            v = self.lanes(v, 2 * x + self.y_step * y + z)
        return jnp.where(self.bottom, 0.0, v) if x else v

    def gather(self, component, here, ahead):
        row = self.row
        g0, g1, g2, g3 = here[0:8], here[8:16], here[16:24], here[24:32]
        a0 = ahead[0:8]
        z0, xz = self.from_next_z(g0, a0, 0, 0), self.from_next_z(g0, a0, 1, 0)
        yz, xyz = self.from_next_z(g0, a0, 0, 1), self.from_next_z(g0, a0, 1, 1)
        z2 = self.from_next_z(g2, ahead[16:24], 0, 0)
        edges = jnp.where(row <= 4, xz, self.from_next(g0, 1, 1))
        edges = jnp.where(row == 0, xyz, jnp.where(row <= 2, yz, edges))
        return jnp.concatenate(
            [
                g0,
                g1,
                g2,
                jnp.where(row < 4, z2, g3),
                self.from_next(g0, 1, 0),
                jnp.where(row == 7, yz, self.from_next(g0, 0, 1)),
                jnp.where(row == 7, xz, z0),
                jnp.where(row < 4, self.from_next(g1, 1, 0), self.from_next(g1, 0, 1)),
                edges,
                jnp.where(row == component, 1.0, 0.0),
            ],
            0,
        )

    def scatter(self, part, behind):
        row = self.row
        g0, g1, g2, g3, x0, y0, z0, sides, edges = (part[8 * n : 8 * n + 8] for n in range(9))
        last = row == 7
        for_z = jnp.where(last, 0.0, z0)
        for_xz = jnp.where(last, z0, jnp.where((row == 3) | (row == 4), edges, 0.0))
        for_yz = jnp.where(last, y0, jnp.where((row == 1) | (row == 2), edges, 0.0))
        for_xyz = jnp.where(row == 0, edges, 0.0)
        for_xy = jnp.where(row >= 5, edges, 0.0)

        def above(z):
            return (
                self.onto_next(for_z, 0, 0, z)
                + self.onto_next(for_yz, 0, 1, z)
                + self.onto_next(for_xz, 1, 0, z)
                + self.onto_next(for_xyz, 1, 1, z)
            )

        own0 = g0 + self.onto_next(x0, 1, 0) + self.onto_next(jnp.where(last, 0.0, y0), 0, 1)
        own0 = own0 + self.onto_next(for_xy, 1, 1)
        own0 = own0 + jnp.where(self.even, behind[0], above(1))
        own1 = g1 + jnp.where(row < 4, self.onto_next(sides, 1, 0), self.onto_next(sides, 0, 1))
        share2 = jnp.where(self.even, behind[1], self.onto_next(g3, 0, 0, 1))
        own2 = g2 + jnp.where(row < 4, share2, 0.0)
        moved = (above(-1), self.onto_next(g3, 0, 0, -1))
        return jnp.concatenate([self.twinned(own0), own1, own2, g3], 0), moved

    def twinned(self, v):
        twins = jnp.where(self.row == 7, pltpu.roll(v, 7, 0), 0.0)
        return v + jnp.where(self.row == 0, pltpu.roll(v, 1, 0), twins)

    def absorb(self, total, behind):
        low = self.twinned(jnp.where(self.even, behind[0], 0.0))
        high = jnp.where(self.even & (self.row < 4), behind[1], 0.0)
        return jnp.concatenate(
            [total[0:8] + low, total[8:16], total[16:24] + high, total[24:32]], 0
        )

    def gradient(self, u, spread, pairs):
        parts = [
            high_low(self.gather(i, u[i, pair], u[i, pair + 1]))
            for i in range(3)
            for pair in pairs
        ]
        return jnp.dot(
            spread[...],
            jnp.concatenate([jnp.concatenate([h, l, h], 0) for h, l in parts], 1),
            preferred_element_type=jnp.float32,
        )

    def stresses(self, gradient, count):
        width = self.width
        rows = 16
        high, low = {}, {}
        for q in range(count):
            for r in range(64 // rows):
                deform = [
                    [
                        gradient[
                            64 * e + rows * r : 64 * e + rows * (r + 1),
                            width * (count * i + q) : width * (count * i + q + 1),
                        ]
                        for e in range(3)
                    ]
                    for i in range(3)
                ]
                stress = point_stress(deform)
                for i in range(3):
                    for e in range(3):
                        high[e, r, i, q], low[e, r, i, q] = high_low(stress[i][e])

        def whole(part):
            return jnp.concatenate(
                [
                    jnp.concatenate([part[e, r, i, q] for i in range(3) for q in range(count)], 1)
                    for e in range(3)
                    for r in range(64 // rows)
                ],
                0,
            )

        return whole(high), whole(low)

    def force(self, gradient, stiff, collect, pairs):
        high, low = self.stresses(gradient, len(pairs))
        rows = collect.shape[0] // 2
        force = jnp.dot(collect[...], high, preferred_element_type=jnp.float32)
        force = force[0:rows] + (
            force[rows:] + jnp.dot(collect[0:rows], low, preferred_element_type=jnp.float32)
        )
        stiffness = [stiff[pair : pair + 1, :] for pair in pairs]
        return force * jnp.concatenate(stiffness * 3, 1)

    def run(self, u, stiff, spread, collect, jobs, given=None):
        plan = plan_steps([job[:2] for job in jobs])
        steps = [(pairs, n) for n, chunks in enumerate(plan) for pairs in chunks]
        none = jnp.zeros((8, self.width), jnp.float32)
        ahead, carry, job = None, None, None
        for at, (pairs, n) in enumerate(steps):
            ready = given is not None and n == 0 and pairs == given[0]
            gradient = ahead
            if ahead is None and not ready:
                gradient = self.gradient(u, spread, pairs)
            if not ready:
                ahead = None
            if ahead is None and at + 1 < len(steps):
                later, later_job = steps[at + 1]
                if given is not None and later_job == 0 and later == given[0]:
                    later, later_job = steps[at + 2]
                if later_job == n or not reads(later) & set(pairs):
                    ahead = self.gradient(u, spread, later)
            if job != n:
                carry, job = [(none, none) for i in range(3)], n
            if ready:
                for q, pair in enumerate(pairs):
                    total = given[1][q]
                    if q == 0:
                        total = [self.absorb(total[i], carry[i]) for i in range(3)]
                    jobs[n][2](pair, total)
                carry = list(given[2])
                continue
            force = self.force(gradient, stiff, collect, pairs)
            totals = [[] for pair in pairs]
            for q in range(len(pairs)):
                for i in range(3):
                    lane = (len(pairs) * i + q) * self.width
                    total, carry[i] = self.scatter(force[:, lane : lane + self.width], carry[i])
                    totals[q].append(total)
            for pair, total in zip(pairs, totals):
                jobs[n][2](pair, total)
        return carry

    def smoothing(self, u, f, f_shift, d, spans, bound):
        jobs = []
        for (first, count), (held, added) in zip(spans, chebyshev_steps()):

            def finish(pair, forces, held=held, added=added):
                for i in range(3):
                    z = (added / bound) * self.keep * (f[i, pair + f_shift] - forces[i])
                    move = held * d[i, pair] + z if held else z
                    d[i, pair] = move
                    u[i, pair] = u[i, pair] + move

            jobs.append((first, count, finish))
        return jobs

    def owed(self, carry, bound):
        scale = -chebyshev_steps()[-1][1] / bound
        return [
            (
                scale * jnp.where(self.even, low, 0.0) * self.keep[0:8],
                scale * jnp.where(self.even, high, 0.0) * self.keep[16:24],
            )
            for low, high in carry
        ]

    def corners_of(self, v):
        ahead = pltpu.roll(v, 7, 0)
        found = {}
        for a in range(2):
            for b in range(2):
                found[a, b, 0] = self.from_next(v, a, b)
                found[a, b, 1] = self.from_next_z(v, ahead, a, b)
        return found

    def assemble(self, part):
        here, odd, even = 0.0, 0.0, 0.0
        for a in range(2):
            for b in range(2):
                here = here + self.onto_next(part[a, b, 0], a, b)
                odd = odd + self.onto_next(part[a, b, 1], a, b, 1)
                even = even + self.onto_next(part[a, b, 1], a, b, -1)
        return here + jnp.where(self.even, pltpu.roll(even, 1, 0), odd)

    def coarse_force(self, values, stiffness):
        grads = []
        for i in range(3):
            v = self.corners_of(values[i])
            vz, sz = {}, {}
            for a in two:
                for b in two:
                    vz[a, b], sz[a, b] = at_points(v[a, b, 0], v[a, b, 1])
            vv, vs, sv = {}, {}, {}
            for a in two:
                for k in two:
                    vv[a, k], vs[a, k] = at_points(vz[a, 0][k], vz[a, 1][k])
                sv[a], unused = at_points(sz[a, 0], sz[a, 1])
            dx, dy, dz = {}, {}, {}
            for k in two:
                for j in two:
                    dx[j, k] = (vv[1, k][j] - vv[0, k][j]) * (1.0 / element_span)
                line, unused = at_points(vs[0, k], vs[1, k])
                for h in two:
                    dy[h, k] = line[h]
            for j in two:
                line, unused = at_points(sv[0][j], sv[1][j])
                for h in two:
                    dz[h, j] = line[h]
            grads.append((dx, dy, dz))
        weight = element_span**2 / 8.0
        scaled = weight * stiffness
        sums = [({}, {}, {}) for i in range(3)]

        def add(table, key, value):
            table[key] = table[key] + value if key in table else value

        for h in two:
            for j in two:
                for k in two:
                    deform = [
                        [grads[i][0][j, k], grads[i][1][h, k], grads[i][2][h, j]]
                        for i in range(3)
                    ]
                    for i in range(3):
                        deform[i][i] = deform[i][i] + 1.0
                    stress = point_stress(deform)
                    for i in range(3):
                        add(sums[i][0], (j, k), stress[i][0])
                        add(sums[i][1], (h, k), stress[i][1])
                        add(sums[i][2], (h, j), stress[i][2])

        forces = []
        for i in range(3):
            part = {}
            qx, qy, qz = sums[i]
            along_z = [ends_of(qx[j, 0], qx[j, 1]) for j in two]
            for c in two:
                line = ends_of(along_z[0][c], along_z[1][c])
                for b in two:
                    part[0, b, c] = -line[b]
                    part[1, b, c] = line[b]
            along_z = [ends_of(qy[h, 0], qy[h, 1]) for h in two]
            for c in two:
                line = ends_of(along_z[0][c], along_z[1][c])
                for a in two:
                    part[a, 0, c] = part[a, 0, c] - line[a]
                    part[a, 1, c] = part[a, 1, c] + line[a]
            along_y = [ends_of(qz[h, 0], qz[h, 1]) for h in two]
            for b in two:
                line = ends_of(along_y[0][b], along_y[1][b])
                for a in two:
                    part[a, b, 0] = part[a, b, 0] - line[a]
                    part[a, b, 1] = part[a, b, 1] + line[a]
            forces.append(self.assemble({key: scaled * value for key, value in part.items()}))
        return forces


def window_pair(slab, first_layer, own_layers, fetch):
    found = []
    for parity in range(2):
        layer = first_layer + parity
        device = layer // own_layers
        layer = layer - device * own_layers
        found.append((device, layer // 2, layer % 2))
    values = [fetch(device, q) for device, q, parity in found]
    if found[0][:2] == found[1][:2] or (values[0] is None and values[1] is None):
        return values[0]
    for parity in range(2):
        if values[parity] is None:
            values[parity] = jnp.zeros_like(values[1 - parity])
        elif found[parity][2] != parity:
            values[parity] = slab.lanes(values[parity], 2 * parity - 1)
    lane = lax.broadcasted_iota(jnp.int32, values[0].shape, 1)
    return jnp.where(lane % 2 == 0, values[0], values[1])


def first_sources(own_layers):
    return list(range(-BEFORE // own_layers, (own_layers + BEFORE - 1) // own_layers + 1))


def whole_pairs(own_layers):
    return own_layers == 4


def turn_rows(block, mixed, turned, width, at):
    for tile in range(SENT // 128):
        n = at * (SENT // 128) + tile
        for m in range(width // 4):
            first = 12 * m + 4 * tile
            mixed[n, 4 * m : 4 * m + 4, :] = block[first : first + 4, :]
        turned[at, 128 * tile : 128 * tile + 128, :] = mixed[n].T


def regroup(slab, field, rows):
    values, hard = [], None
    for i in range(3):
        parts = [rows(24 * i + 8 * n) for n in range(3)]
        if field == 0 and i == 0:
            hard = parts[0][TWIN : TWIN + 1]
        parts[0] = jnp.where(slab.row == TWIN, pltpu.roll(parts[0], TWIN, 0), parts[0])
        parts.append(jnp.where(slab.row < 4, 0.0, rows(68 + 4 * i)))
        whole = jnp.concatenate(parts, 0)
        values.append(whole * slab.keep if field == 0 else whole)
    return values, hard


def layer_above(slab, turned, at, i):
    first = NEXT_COLUMN + 12 * i
    low, high = turned[at, first : first + 8, :], turned[at, first + 4 : first + 12, :]
    high = jnp.where(slab.row < 4, pltpu.roll(high, 4, 0), 0.0)
    low = jnp.where(slab.row == TWIN, pltpu.roll(low, TWIN, 0), low)
    nothing = jnp.zeros_like(low)
    return jnp.concatenate([low, nothing, high, nothing], 0) * slab.keep


def make_own_kernel(width, across, own_layers):
    own_pairs = own_layers // 2
    pairs = list(range(own_pairs))

    def own_kernel(block, spread, collect, u, f, stiff, forces, moved, mixed, turned):
        slab = Slab(width, across)
        turn_rows(block, mixed, turned, width, 0)
        for pair in pairs:
            for field, target in enumerate((u, f)):

                def rows(start, field=field, pair=pair):
                    at = BLOCK * (2 * pair + field) + start
                    return turned[0, at : at + 8, :]

                values, hard = regroup(slab, field, rows)
                for i in range(3):
                    target[i, pair] = values[i]
                if field == 0:
                    stiff[pair : pair + 1, :] = hard
        for i in range(3):
            u[i, own_pairs] = layer_above(slab, turned, 0, i)

        def finish(pair, total):
            for i in range(3):
                forces[i, pair] = total[i]

        carry = slab.run(u, stiff, spread, collect, [(0, own_pairs, finish)])
        for i in range(3):
            moved[i, 0] = carry[i][0]
            moved[i, 1] = carry[i][1]

    return own_kernel


def make_first_kernel(width, across, own_layers, fine_bound):
    own = BEFORE // 2
    own_pairs = (own_layers + 1) // 2
    spans = []
    prepared = whole_pairs(own_layers)
    for n in (4, 3, 2, 1):
        low, high = BEFORE - n, BEFORE + own_layers + n - 1 + prepared
        spans.append((low // 2, (high + 1) // 2 - low // 2))
    sources = [n for n in first_sources(own_layers) if n or not prepared]

    def first_kernel(*refs):
        arrived = refs[: len(sources)]
        refs = refs[len(sources) :]
        if prepared:
            own_u, own_f, own_stiff, own_forces, own_moved = refs[:5]
            refs = refs[5:]
        spread, collect, corners, from_loads, message, *sent, f = refs[: -6]
        u, d, stiff, shares, mixed, turned = refs[-6:]
        slab = Slab(width, across)
        if not prepared:
            u[...] = jnp.zeros(u.shape, jnp.float32)
            f[...] = jnp.zeros(f.shape, jnp.float32)
        shares[...] = jnp.zeros(shares.shape, jnp.float32)
        stiff[...] = jnp.zeros(stiff.shape, jnp.float32)
        for n in range(len(sources)):
            turn_rows(arrived[n], mixed, turned, width, n)
        for pair in range(PAIRS):
            if prepared and own <= pair < own + own_pairs:
                for i in range(3):
                    u[i, pair] = own_u[i, pair - own]
                    f[i, pair] = own_f[i, pair - own]
                stiff[pair : pair + 1, :] = own_stiff[pair - own : pair - own + 1, :]
                continue
            for field, target in enumerate((u, f)):

                def rows(start, field=field, pair=pair):
                    def fetch(device, q):
                        if device not in sources:
                            return None
                        at = BLOCK * (2 * q + field) + start
                        return turned[sources.index(device), at : at + 8, :]

                    value = window_pair(slab, 2 * pair - BEFORE, own_layers, fetch)
                    return jnp.zeros((8, width), jnp.float32) if value is None else value

                values, hard = regroup(slab, field, rows)
                for i in range(3):
                    target[i, pair] = values[i]
                if field == 0:
                    stiff[pair : pair + 1, :] = hard
        given = None
        if prepared:
            for i in range(3):
                u[i, PAIRS] = layer_above(slab, turned, sources.index(1), i)
            given = (
                list(range(own, own + own_pairs)),
                [[own_forces[i, q] for i in range(3)] for q in range(own_pairs)],
                [(own_moved[i, 0], own_moved[i, 1]) for i in range(3)],
            )

        first, count = spans[3]
        blocks = [
            high_low(slab.keep * f[i, pair]) for pair in range(first, first + count) for i in range(3)
        ]
        loads = jnp.dot(
            from_loads[...],
            jnp.concatenate([jnp.concatenate([h, l, h], 0) for h, l in blocks], 1),
            preferred_element_type=jnp.float32,
        )
        jobs = slab.smoothing(u, f, 0, d, spans[0:3], fine_bound)
        slab.run(u, stiff, spread, collect, jobs, given)
        steps = plan_steps([spans[3]])[0]
        gradients = [slab.gradient(u, spread, pairs) for pairs in steps]
        for pairs, gradient in zip(steps, gradients):
            force = slab.force(gradient, stiff, corners, pairs)
            for q, pair in enumerate(pairs):
                for i in range(3):
                    at = (len(pairs) * i + q) * width
                    load_at = (3 * (pair - first) + i) * width
                    part = force[:, at : at + width]
                    part = jnp.where(slab.bottom, part[8:16], part[0:8])
                    shares[i, pair] = loads[0:8, load_at : load_at + width] - part

        restricted = [
            slab.assemble({corner: shares[i, :, n, :] for n, corner in enumerate(CORNERS)})
            for i in range(3)
        ]
        def line(rows, q):
            return rows[own + q : own + q + 1]

        for q in range(own_pairs):
            for i in range(3):
                message[i, q] = u[i, own + q]
                message[i, q, RESTRICTED_SLOT : RESTRICTED_SLOT + 1, :] = line(restricted[i], q)
            message[0, q, STIFF_SLOT : STIFF_SLOT + 1, :] = line(stiff, q)
        if prepared:
            down, up = sent
            for i in range(3):
                down[i, 0:32] = u[i, own]
                down[i, 32:40] = u[i, own + 1, 0:8, :]
                down[i, 40:48] = u[i, own + 1, 16:24, :]
                up[i] = u[i, own + 1]
                for n, row in enumerate(
                    (line(restricted[i], 0), line(restricted[i], 1), u[i, own + 2, 0:1, :])
                    + (line(restricted[i], 2),)
                ):
                    down[i, 24 + n : 25 + n, :] = row
                for n, row in enumerate(
                    (line(restricted[i], 1), line(restricted[i], 0), u[i, own, 0:1, :])
                ):
                    up[i, 24 + n : 25 + n, :] = row
            for q in range(own_pairs):
                down[q, 32 + TWIN : 33 + TWIN, :] = line(stiff, q)
                up[q, TWIN : TWIN + 1, :] = line(stiff, q)
            return
        edge = sent[0]
        for q in range(own_pairs):
            for i in range(3):
                edge[q, i : i + 1, :] = u[i, own + q, 0:1, :]
                edge[q, 3 + i : 4 + i, :] = line(restricted[i], q)
            edge[q, 6:8, :] = jnp.broadcast_to(line(stiff, q), (2, width))

    return first_kernel


def shares_sent(own_layers):
    return own_layers % 2 == 0


def sources_of(own_layers):
    below = 2 if shares_sent(own_layers) else 3
    whole = range(-below // own_layers, (own_layers + 2) // own_layers + 1)
    coarse = range(-(below + 2) // own_layers, (own_layers + 4) // own_layers + 1)
    return list(whole), [n for n in coarse if n not in whole]


def message_line(message, q, n):
    i, slot = ((n, 0), (n - 3, RESTRICTED_SLOT), (0, STIFF_SLOT))[n // 3]
    return message[i, q, slot : slot + 1, :]


def sent_readers(slab, up, message, down):
    def block_of(device, q, i):
        if device == 0:
            return message[i, q]
        if (device, q) == (1, 0):
            whole = down[i, 0:32]
        elif (device, q) == (1, 1):
            low, high = down[i, 32:40], down[i, 40:48]
            low = jnp.where(slab.row == TWIN, pltpu.roll(low, TWIN, 0), low)
            whole = jnp.concatenate([low, jnp.zeros_like(low), high, jnp.zeros_like(low)], 0)
        elif (device, q) == (-1, 1):
            low = up[i, 0:8]
            low = jnp.where(slab.row == TWIN, pltpu.roll(low, TWIN, 0), low)
            whole = jnp.concatenate([low, up[i, 8:32]], 0)
        else:
            return None
        return whole

    def line_of(device, q, n):
        if device == 0:
            return message_line(message, q, n)
        kind, i = n // 3, n % 3
        if device == 1:
            row = ((0, 24), (32, 25))[q][kind] if kind < 2 else 32 + TWIN
            i = i if kind < 2 else q
            return down[i, row : row + 1, :]
        if device == -1:
            row = ((26, 25), (0, 24))[q][kind] if kind < 2 else TWIN
            i = i if kind < 2 else q
            return up[i, row : row + 1, :]
        if (device, q) == (2, 0) and kind < 2:
            return down[i, 26 + kind : 27 + kind, :]
        return None

    return block_of, line_of


def make_second_kernel(width, across, own_layers, fine_bound, coarse_bound):
    own = BEFORE_B // 2
    own_pairs = (own_layers + 1) // 2
    shift = (BEFORE - BEFORE_B) // 2
    whole, outer = sources_of(own_layers)
    steps = chebyshev_steps()
    spans = []
    for n in (3, 2, 1):
        low, high = BEFORE_B - n + shares_sent(own_layers), BEFORE_B + own_layers + n - 1
        spans.append((low // 2, (high + 1) // 2 - low // 2))

    def second_kernel(*refs):
        slab = Slab(width, across)
        if whole_pairs(own_layers):
            up, message, down = refs[:3]
            refs = refs[3:]
            block_of, line_of = sent_readers(slab, up, message, down)
        else:
            messages = dict(zip(whole, refs))
            edges = dict(zip(outer, refs[len(whole) :]))
            refs = refs[len(whole) + len(outer) :]

            def block_of(device, q, i):
                return messages[device][i, q] if device in messages else None

            def line_of(device, q, n):
                if device in messages:
                    return message_line(messages[device], q, n)
                return edges[device][q, n : n + 1, :] if device in edges else None

        f, spread, collect, transfer_back, out, u, d, stiff, coarse = refs

        def pair_of(pair, fetch):
            return window_pair(slab, 2 * pair - BEFORE_B, own_layers, fetch)

        coarse[...] = jnp.zeros(coarse.shape, jnp.float32)
        for pair in range(PAIRS_B):
            for i in range(3):
                block = pair_of(pair, lambda device, q: block_of(device, q, i))
                u[i, pair] = jnp.zeros((32, width), jnp.float32) if block is None else block
            for n in range(7):
                line = pair_of(pair, lambda device, q: line_of(device, q, n))
                if line is not None:
                    coarse[n, pair : pair + 1, :] = line
        stiff[...] = coarse[6]

        stiffness = coarse[6]
        keep_coarse = jnp.where(slab.bottom, 0.0, 1.0)
        start = [coarse[i] for i in range(3)]
        restricted = [coarse[3 + i] for i in range(3)]
        before = slab.coarse_force(start, stiffness)
        move = [(steps[0][1] / coarse_bound) * keep_coarse * restricted[i] for i in range(3)]
        level = [start[i] + move[i] for i in range(3)]
        for held, added in steps[1:]:
            force = slab.coarse_force(level, stiffness)
            for i in range(3):
                z = keep_coarse * (restricted[i] + before[i] - force[i])
                move[i] = held * move[i] + (added / coarse_bound) * z
                level[i] = level[i] + move[i]

        weights = [jnp.broadcast_to(transfer_back[:, n : n + 1], (32, width)) for n in range(8)]
        for i in range(3):
            change = slab.corners_of(level[i] - start[i])
            for pair in range(spans[0][0], min(spans[0][0] + spans[0][1] + 1, PAIRS_B)):
                lift = u[i, pair]
                for n, corner in enumerate(CORNERS):
                    lift = lift + weights[n] * change[corner][pair : pair + 1]
                u[i, pair] = lift

        jobs = slab.smoothing(u, f, shift, d, spans, fine_bound)
        owed = slab.owed(slab.run(u, stiff, spread, collect, jobs), fine_bound)

        lower = lax.broadcasted_iota(jnp.int32, (width // 8, 8, 128), 1) < 4
        nothing = jnp.zeros((8, width), jnp.float32)
        sides = []
        for q in range(2):
            if q or not shares_sent(own_layers):
                owed = [(nothing, nothing)] * 3
            rows = []
            for i in range(3):
                value = u[i, own + q]
                rows += [value[0:24], jnp.where(slab.row < 4, owed[i][1], value[24:32])]
            rows += [owed[i][0] for i in range(3)]
            rows += [level[i][own + q : own + q + 1] for i in range(3)] + [nothing[0:5]]
            sides.append(jnp.concatenate(rows, 0).T.reshape(width // 8, 8, 128))
        out[:, 0] = jnp.where(lower, sides[0], pltpu.roll(sides[1], 4, 1))
        out[:, 1] = jnp.where(lower, pltpu.roll(sides[0], 4, 1), sides[1])

    return second_kernel


def solution(mesh):
    rows_of, columns_of = mesh.shape["gx"], mesh.shape["gy"]
    devices = rows_of * columns_of
    order = ring_order(rows_of, columns_of)
    own_layers = EZ // devices
    own_pairs = (own_layers + 1) // 2
    width = 4 * devices
    across = 2 * rows_of
    near = first_sources(own_layers)
    prepared = whole_pairs(own_layers)
    whole, outer = sources_of(own_layers)
    spread, collect, fine_bound = element_tables()
    coarse_bound = build_tables([0.0, 1.0], 2)[2]
    transfer_back = transfer_table()[1]
    corners, from_loads = corner_tables()
    wide = pltpu.CompilerParams(vmem_limit_bytes=60 * 1024 * 1024)
    limit = pltpu.CompilerParams(vmem_limit_bytes=48 * 1024 * 1024)
    f32 = jnp.float32

    pack = pl.pallas_call(
        functools.partial(pack_kernel, order),
        out_shape=pltpu.VMEM((devices * 12, 128), f32),
        in_specs=[pl.BlockSpec(memory_space=pl.ANY)] * 5,
        out_specs=pl.BlockSpec(memory_space=pltpu.VMEM),
        scratch_shapes=[
            pltpu.VMEM((3, 6, 3, 384), f32),
            pltpu.VMEM((3, 6, 3, 384), f32),
            pltpu.VMEM((2, 1, EZ), f32),
            pltpu.VMEM((1, 1, 192), jnp.int32),
            pltpu.VMEM((384, 512), jnp.bfloat16),
            pltpu.VMEM((128, 384), f32),
            pltpu.VMEM((384, 128), f32),
            pltpu.VMEM((6, 136, 128), f32),
            pltpu.SemaphoreType.DMA((5,)),
        ],
        compiler_params=wide,
    )
    own = pl.pallas_call(
        make_own_kernel(width, across, own_layers),
        out_shape=(
            jax.ShapeDtypeStruct((3, own_pairs + 1, 32, width), f32),
            jax.ShapeDtypeStruct((3, own_pairs, 32, width), f32),
            jax.ShapeDtypeStruct((own_pairs, width), f32),
            jax.ShapeDtypeStruct((3, own_pairs, 32, width), f32),
            jax.ShapeDtypeStruct((3, 2, 8, width), f32),
        ),
        scratch_shapes=[
            pltpu.VMEM((SENT // 128, width, 128), f32),
            pltpu.VMEM((1, SENT, width), f32),
        ],
        compiler_params=limit,
        cost_estimate=pl.CostEstimate(flops=400_000_000, bytes_accessed=1_000_000, transcendentals=0),
    )
    sent = [jax.ShapeDtypeStruct((own_pairs, 8, width), f32)]
    if prepared:
        sent = [jax.ShapeDtypeStruct((3, rows, width), f32) for rows in (48, 32)]
    first = pl.pallas_call(
        make_first_kernel(width, across, own_layers, fine_bound),
        out_shape=(
            jax.ShapeDtypeStruct((3, own_pairs, 32, width), f32),
            *sent,
            jax.ShapeDtypeStruct((3, PAIRS, 32, width), f32),
        ),
        scratch_shapes=[
            pltpu.VMEM((3, 8, 32, width), f32),
            pltpu.VMEM((3, 8, 32, width), f32),
            pltpu.VMEM((8, width), f32),
            pltpu.VMEM((3, 8, 8, width), f32),
            pltpu.VMEM((len(near) * (SENT // 128), width, 128), f32),
            pltpu.VMEM((len(near), SENT, width), f32),
        ],
        compiler_params=limit,
    )
    second = pl.pallas_call(
        make_second_kernel(width, across, own_layers, fine_bound, coarse_bound),
        out_shape=jax.ShapeDtypeStruct((devices // 2, 2, 8, 128), f32),
        scratch_shapes=[
            pltpu.VMEM((3, PAIRS_B, 32, width), f32),
            pltpu.VMEM((3, PAIRS_B, 32, width), f32),
            pltpu.VMEM((PAIRS_B, width), f32),
            pltpu.VMEM((7, PAIRS_B, width), f32),
        ],
        compiler_params=limit,
    )
    unpack = pl.pallas_call(
        functools.partial(unpack_kernel, order),
        out_shape=(
            jax.ShapeDtypeStruct((3, 6, 3, 384), f32),
            jax.ShapeDtypeStruct((3, 2, 1, EZ), f32),
        ),
        scratch_shapes=[pltpu.VMEM((2, 128, 128), f32), pltpu.VMEM((384, 128), f32)],
        compiler_params=limit,
    )
    everyone = ("gy", "gx")

    def from_device(block, distance):
        place = {k: m % rows_of * columns_of + m // rows_of for m, k in enumerate(order)}
        route = [(place[(k + distance) % devices], place[k]) for k in range(devices)]
        return lax.ppermute(block, ("gx", "gy"), route)

    def body(initial, forcing, modulus, solid_list):
        sent = pack(initial, forcing, modulus, solid_list, jnp.asarray(pack_table()))
        sent = sent.reshape(devices, SENT // 128, 4, 128)
        arrived = lax.all_to_all(sent, everyone, 0, 0, tiled=True).reshape(devices * 12, 128)
        blocks = [from_device(arrived, n) if n else arrived for n in near]
        if prepared:
            blocks = [block for n, block in zip(near, blocks) if n]
            blocks += own(arrived, jnp.asarray(spread), jnp.asarray(collect))
        message, *edges, load = first(
            *blocks,
            jnp.asarray(spread),
            jnp.asarray(collect),
            jnp.asarray(corners),
            jnp.asarray(from_loads),
        )
        if prepared:
            down, up = edges
            messages = [from_device(up, -1), message, from_device(down, 1)]
        else:
            messages = [from_device(message, n) if n else message for n in whole]
            messages += [from_device(edges[0], n) for n in outer]
        result = second(
            *messages,
            load,
            jnp.asarray(spread),
            jnp.asarray(collect),
            jnp.asarray(transfer_back),
        )
        back = lax.all_to_all(result.reshape(devices, 8, 128), everyone, 0, 0, tiled=True)
        return unpack(back, jnp.asarray(unpack_table()))

    placed = (
        P(None, "gx", "gy", None),
        P(None, "gx", "gy", None),
        P("gx", "gy", None),
        P("gx", "gy", None),
    )
    return jax.shard_map(
        body,
        mesh=mesh,
        in_specs=placed,
        out_specs=(P(None, "gx", "gy", None), P(None, "gx", "gy", None)),
        check_vma=False,
    )
```

```python
import functools
import math

import jax
import jax.numpy as jnp
import numpy as np
from jax import lax
from jax.experimental import pallas as pl
from jax.experimental.pallas import tpu as pltpu
from jax.sharding import PartitionSpec as P

CHEB = 3
EZ = 128

element_span = 20.0
lame_ratio = 4.0
rest_ratio = 1.25
modulus_top = 2.0
spectrum_floor = 0.05
interval_centre = (1.0 + spectrum_floor) / 2.0
interval_radius = (1.0 - spectrum_floor) / 2.0
interval_ratio = interval_centre / interval_radius
inner_anchors = (0.5 - 0.5 / math.sqrt(5.0), 0.5 + 0.5 / math.sqrt(5.0))

BEFORE = 4
PAIRS = 6
BEFORE_B = 6
PAIRS_B = 8
BLOCK = 84
SENT = 384

SLOTS = [
    (0, 0, 0), (1, 0, 0), (2, 0, 0), (0, 1, 0), (0, 2, 0), (0, 0, 1), (0, 0, 2), None,
    (0, 1, 1), (0, 1, 2), (0, 2, 1), (0, 2, 2), (1, 0, 1), (1, 0, 2), (2, 0, 1), (2, 0, 2),
    (1, 1, 0), (1, 2, 0), (2, 1, 0), (2, 2, 0), (1, 1, 1), (1, 1, 2), (1, 2, 1), (1, 2, 2),
    None, None, None, None, (2, 1, 1), (2, 1, 2), (2, 2, 1), (2, 2, 2),
]
TWIN = 7
NEXT_SLOTS = [0, 1, 2, 3, 4, 5, 6, 7, 16, 17, 18, 19]
NEXT_COLUMN = 4 * BLOCK
RESTRICTED_SLOT = 24
STIFF_SLOT = 25
OWN_SHIFT, SHIFT_X, SHIFT_Y, SHIFT_Z = (0, 0, 0), (1, 0, 0), (0, 1, 0), (0, 0, 1)
ELEMENT_ROWS = (
    [(slot, OWN_SHIFT) for slot in range(24)]
    + [(slot, SHIFT_Z) for slot in range(16, 20)]
    + [(slot, OWN_SHIFT) for slot in range(28, 32)]
    + [(slot, SHIFT_X) for slot in range(7)] + [None]
    + [(slot, SHIFT_Y) for slot in range(7)] + [(0, (0, 1, 1))]
    + [(slot, SHIFT_Z) for slot in range(7)] + [(0, (1, 0, 1))]
    + [(slot, SHIFT_X) for slot in range(8, 12)] + [(slot, SHIFT_Y) for slot in range(12, 16)]
    + [(0, (1, 1, 1)), (1, (0, 1, 1)), (2, (0, 1, 1)), (3, (1, 0, 1)), (4, (1, 0, 1))]
    + [(5, (1, 1, 0)), (6, (1, 1, 0)), (0, (1, 1, 0))]
)
ROWS = len(ELEMENT_ROWS)
DEPTH = 80
POINT_ROWS = 192
CORNERS = [(a, b, c) for a in range(2) for b in range(2) for c in range(2)]


def gauss_rule(point_count):
    if point_count == 2:
        offset = 1.0 / math.sqrt(3.0)
        points = [-offset, offset]
        weights = [1.0, 1.0]
    else:
        inner = math.sqrt(3.0 / 7.0 - 2.0 / 7.0 * math.sqrt(6.0 / 5.0))
        outer = math.sqrt(3.0 / 7.0 + 2.0 / 7.0 * math.sqrt(6.0 / 5.0))
        heavy = (18.0 + math.sqrt(30.0)) / 36.0
        light = (18.0 - math.sqrt(30.0)) / 36.0
        points = [-outer, -inner, inner, outer]
        weights = [light, heavy, heavy, light]
    return (np.array(points), np.array(weights))


def lagrange_tables(anchors, samples):
    values = np.zeros((len(samples), len(anchors)))
    slopes = np.zeros((len(samples), len(anchors)))
    for sample_index, sample in enumerate(samples):
        for anchor_index, anchor in enumerate(anchors):
            others = [
                location
                for location_index, location in enumerate(anchors)
                if location_index != anchor_index
            ]
            product = 1.0
            for location in others:
                product = product * (sample - location) / (anchor - location)
            values[sample_index, anchor_index] = product
            derivative = 0.0
            for skipped in range(len(others)):
                summand = 1.0 / (anchor - others[skipped])
                for kept_index in range(len(others)):
                    if kept_index != skipped:
                        summand = (
                            summand * (sample - others[kept_index]) / (anchor - others[kept_index])
                        )
                derivative = derivative + summand
            slopes[sample_index, anchor_index] = derivative
    return (values, slopes)


def outer_three(first, second, third):
    return (
        first[:, None, None, :, None, None]
        * second[None, :, None, None, :, None]
        * third[None, None, :, None, None, :]
    )


def build_tables(anchors, point_count):
    raw_points, raw_weights = gauss_rule(point_count)
    samples = (raw_points + 1.0) / 2.0
    weights = raw_weights / 2.0
    basis_values, slopes = lagrange_tables(anchors, samples)
    quad_total = point_count**3
    nodal_count = len(anchors) ** 3
    derivative_one = outer_three(slopes, basis_values, basis_values).reshape(
        quad_total, nodal_count
    )
    derivative_two = outer_three(basis_values, slopes, basis_values).reshape(
        quad_total, nodal_count
    )
    derivative_three = outer_three(basis_values, basis_values, slopes).reshape(
        quad_total, nodal_count
    )
    stacked = np.stack([derivative_one, derivative_two, derivative_three]) / element_span
    volume = (weights[:, None, None] * weights[None, :, None] * weights[None, None, :]).reshape(
        -1
    ) * element_span**3
    forward = stacked.reshape(3 * quad_total, nodal_count)
    backward = (stacked * volume[None, :, None]).reshape(3 * quad_total, nodal_count).T
    weighted = stacked * volume[None, :, None]
    laplace = weighted[0].T @ stacked[0] + weighted[1].T @ stacked[1] + weighted[2].T @ stacked[2]
    matrix = np.zeros((nodal_count, 3, nodal_count, 3))
    for first in range(3):
        for second in range(3):
            block = weighted[second].T @ stacked[first] + (lame_ratio - 1.0) * (
                weighted[first].T @ stacked[second]
            )
            if first == second:
                block = block + laplace
            matrix[:, first, :, second] = block
    matrix = matrix.reshape(3 * nodal_count, 3 * nodal_count)
    vector = 1.5 + np.cos(1.3 * np.arange(3 * nodal_count))
    for repeat in range(200):
        vector = matrix @ vector
        vector = vector / np.sqrt(vector @ vector)
    largest = vector @ (matrix @ vector)
    return (forward, backward, float(4.0 * modulus_top * 1.1 * largest))


def row_nodes():
    nodes = []
    for entry in ELEMENT_ROWS:
        slot = SLOTS[entry[0]] if entry else None
        if slot is None or any(s and n for s, n in zip(entry[1], slot)):
            nodes.append(None)
        else:
            a, b, c = (3 * s + n for s, n in zip(entry[1], slot))
            nodes.append(16 * a + 4 * b + c)
    return nodes


def halves(matrix):
    whole = np.asarray(matrix, np.float32)
    high = whole.astype(jnp.bfloat16)
    low = (whole - high.astype(np.float32)).astype(jnp.bfloat16)
    return high, low


def element_tables():
    forward, backward, bound = build_tables([0.0, inner_anchors[0], inner_anchors[1], 1.0], 4)
    spread = np.zeros((forward.shape[0], DEPTH))
    collect = np.zeros((ROWS, backward.shape[1]))
    for row, node in enumerate(row_nodes()):
        if node is not None:
            spread[:, row] = forward[:, node]
            collect[row, :] = backward[node, :]
    for column in range(3):
        spread[64 * column : 64 * column + 64, ROWS + column] = 1.0
    spread_high, spread_low = halves(spread)
    collect_high, collect_low = halves(collect)
    return (
        np.concatenate([spread_high, spread_high, spread_low], 1),
        np.concatenate([collect_high, collect_low], 0),
        bound,
    )


def corner_tables():
    anchors = [0.0, inner_anchors[0], inner_anchors[1], 1.0]
    backward = build_tables(anchors, 4)[1]
    reach = np.stack([1.0 - np.array(anchors), np.array(anchors)])
    weights = outer_three(reach, reach, reach).reshape(8, 64)
    held = np.arange(64) < 16
    from_stress = np.concatenate([weights @ backward, np.where(held, 0.0, weights) @ backward], 0)
    from_loads = np.zeros((16, 32))
    from_loads[:8] = transfer_table()[0].T
    loads_high, loads_low = halves(from_loads)
    return (
        np.concatenate(halves(from_stress), 0),
        np.concatenate([loads_high, loads_high, loads_low], 1),
    )


def transfer_table():
    table = np.zeros((8, 32))
    reach = (0.0, inner_anchors[0], inner_anchors[1])
    for row, corner in enumerate(CORNERS):
        for column, slot in enumerate(SLOTS):
            if slot is not None:
                weight = 1.0
                for side, node in zip(corner, slot):
                    weight = weight * (reach[node] if side else 1.0 - reach[node])
                table[row, column] = weight
    back = table.T.copy()
    back[TWIN] = back[0]
    return table.T.astype(np.float32), back.astype(np.float32)


def chebyshev_steps():
    steps = [(0.0, 1.0 / interval_centre)]
    ratio_now = 1.0 / interval_ratio
    for sweep in range(1, CHEB):
        ratio_next = 1.0 / (2.0 * interval_ratio - ratio_now)
        steps.append((ratio_next * ratio_now, 2.0 * ratio_next / interval_radius))
        ratio_now = ratio_next
    return steps


def stack_row(field, component, layer, b):
    return field * 54 + component * 18 + layer * 3 + b


def block_column(component, slot):
    return 72 + 4 * component + slot - 28 if slot >= 24 else 24 * component + slot


def pack_table():
    table = np.zeros((3, 128, 2, 2, 128), np.float32)
    for field in range(2):
        for x in range(2):
            for component in range(3):
                for column, slot in enumerate(SLOTS):
                    if slot is not None:
                        a, b, c = slot
                        row = stack_row(field, component, 3 * x + a, b)
                        table[c, row, field, x, block_column(component, column)] = 1.0
                        if field == 0 and column in NEXT_SLOTS:
                            at = BLOCK + 12 * component + NEXT_SLOTS.index(column)
                            table[c, row, 1, x, at] = 1.0
            table[0, 108 + x, 0, x, TWIN] = 1.0
    return table.reshape(384, 512).astype(jnp.bfloat16)


def unpack_table():
    table = np.zeros((2, 128, 4, 128), np.float32)
    for x in range(2):
        for component in range(3):
            for column, slot in enumerate(SLOTS):
                if slot is not None:
                    a, b, c = slot
                    row = stack_row(0, component, 3 * x + a, b)
                    table[x, component * 32 + column, c, row] = 1.0
                    if column < 5:
                        table[x, 96 + 8 * component + column, 3, row] = 1.0
                    if column == 0:
                        table[x, 96 + 8 * component + TWIN, 3, row] = 1.0
                    if 16 <= column < 20:
                        table[x, component * 32 + column + 8, 3, row] = 1.0
            table[x, 120 + component, 0, 54 + 2 * component + x] = 1.0
    return table.reshape(256, 512).astype(jnp.bfloat16)


def pick(values, table):
    count = values.shape[0]
    parts = jnp.dot(
        jnp.concatenate(high_low(values), 0), table, preferred_element_type=jnp.float32
    )
    return parts[:count] + parts[count:]


def ring_order(rows_of, columns_of):
    if (rows_of, columns_of) != (4, 8):
        return list(range(rows_of * columns_of))
    order = []
    for z in range(4):
        for x in range(2):
            for y in range(2):
                chip = (z, 7 - z, 15 - z, 8 + z)[2 * x + y]
                order += [2 * chip, 2 * chip + 1]
    return order


def pack_kernel(
    order,
    initial_at, forcing_at, modulus_at, listing_at, table_at, out,
    initial, forcing, modulus, listing, table, rows, turned, places, ready,
):
    own_layers = EZ // len(order)
    sources = (listing_at, modulus_at, initial_at, forcing_at, table_at)
    copies = [
        pltpu.make_async_copy(source, here, ready.at[n])
        for n, (source, here) in enumerate(
            zip(sources, (listing, modulus, initial, forcing, table))
        )
    ]
    for copy in copies:
        copy.start()
    rows[108:128, :] = jnp.zeros((20, 384), jnp.float32)
    copies[0].wait()
    copies[1].wait()
    listed = listing[0].astype(jnp.float32)
    listed = jnp.concatenate([listed, jnp.full((1, 64), 256.0, jnp.float32)], 1)
    listed = jnp.broadcast_to(listed, (128, 256)).T
    lanes = lax.broadcasted_iota(jnp.int32, (256, 128), 1).astype(jnp.float32)
    row_at = lax.broadcasted_iota(jnp.int32, (128, 128), 0)
    stiff = jnp.zeros((128, 128), jnp.float32)
    for x in range(2):
        hit = jnp.max(jnp.where(listed == lanes + 128.0 * x, 1.0, 0.0), axis=0, keepdims=True)
        stiff = jnp.where(row_at == 108 + x, hit * modulus[x], stiff)
    copies[2].wait()
    copies[3].wait()
    for field, source in enumerate((initial, forcing)):
        for component in range(3):
            for layer in range(6):
                at = stack_row(field, component, layer, 0)
                rows[at : at + 3, :] = source[component, layer]
    for part in range(3):
        span = slice(128 * part, 128 * part + 128)
        turned[span, :] = rows[:, span].T
    picked = [turned[pl.ds(c, 128, stride=3), :] for c in range(3)]
    picked[0] = picked[0] + stiff.T
    copies[4].wait()
    wide = pick(jnp.concatenate(picked, 1), table[...])
    lane = lax.broadcasted_iota(jnp.int32, (128, 128), 1)
    for x in range(2):
        tiles = [None] * (SENT // 128)
        for n in range(4):
            pair, field = n // 2, n % 2
            moved = wide[:, 128 * (2 * field + x) : 128 * (2 * field + x) + 128]
            first = BLOCK * n
            if pair:
                moved = pltpu.roll(moved, 128 - 2 * pair, 0)
            if first % 128:
                moved = pltpu.roll(moved, first % 128, 1)
            for tile in range(first // 128, (first + BLOCK - 1) // 128 + 1):
                before = tiles[tile]
                if before is None:
                    tiles[tile] = moved
                else:
                    tiles[tile] = jnp.where(lane >= first - 128 * tile, moved, before)
        above = wide[:, 128 * (2 + x) : 128 * (2 + x) + 128]
        above = pltpu.roll(pltpu.roll(above, 128 - own_layers, 0), (NEXT_COLUMN - BLOCK) % 128, 1)
        tiles[-1] = jnp.where(lane >= NEXT_COLUMN % 128, above, tiles[-1])
        for tile in range(SENT // 128):
            places[3 * x + tile, 0:128, :] = tiles[tile]
            places[3 * x + tile, 128:136, :] = jnp.zeros((8, 128), jnp.float32)
    for device, k in enumerate(order):
        for tile in range(SENT // 128):
            for x in range(2):
                at = 12 * device + 4 * tile + 2 * x
                out[at : at + 2, :] = places[
                    3 * x + tile, own_layers * k : own_layers * k + 2, :
                ]


def unpack_kernel(order, arrived, table, out, coarse_out, layers, turned):
    devices = arrived.shape[0]
    own_layers = EZ // devices
    together = min(own_layers, 2)
    for x in range(2):
        for layer in range(0, own_layers, 2):
            row = (layer // 2) * 4 + x * 2
            if order == sorted(order):
                for n in range(together):
                    at = pl.ds(layer + n, devices, stride=own_layers)
                    layers[x, at, :] = arrived[:, row + n, :]
                continue
            for device, k in enumerate(order):
                at = own_layers * k + layer
                layers[x, at : at + together, :] = arrived[device, row : row + together, :]
    wide = pick(jnp.concatenate([layers[0], layers[1]], 1), table[...])
    shares = pltpu.roll(wide[:, 384:512], own_layers, 0)
    turned[pl.ds(0, 128, stride=3), :] = wide[:, 0:128] + shares
    for c in range(1, 3):
        turned[pl.ds(c, 128, stride=3), :] = wide[:, 128 * c : 128 * c + 128]
    for part in range(3):
        span = slice(128 * part, 128 * part + 128)
        back = turned[span, :].T
        for component in range(3):
            for layer in range(6):
                at = stack_row(0, component, layer, 0)
                out[component, layer, :, span] = back[at : at + 3, :]
    back = wide[:, 0:128].T
    for component in range(3):
        for x in range(2):
            at = 54 + 2 * component + x
            coarse_out[component, x] = back[at : at + 1, :]


def cofactor_rows(deform):
    return [
        [
            deform[(row_at + 1) % 3][(column + 1) % 3] * deform[(row_at + 2) % 3][(column + 2) % 3]
            - deform[(row_at + 1) % 3][(column + 2) % 3]
            * deform[(row_at + 2) % 3][(column + 1) % 3]
            for column in range(3)
        ]
        for row_at in range(3)
    ]


def point_stress(deform):
    cofactors = cofactor_rows(deform)
    jacobian = (
        deform[0][0] * cofactors[0][0]
        + deform[0][1] * cofactors[0][1]
        + deform[0][2] * cofactors[0][2]
    )
    pressure = lame_ratio * (jacobian - rest_ratio)
    return [
        [deform[i][d] + pressure * cofactors[i][d] for d in range(3)] for i in range(3)
    ]


coarse_samples = [0.5 - 0.5 / math.sqrt(3.0), 0.5 + 0.5 / math.sqrt(3.0)]
two = range(2)


def at_points(low, high):
    change = high - low
    return [low + s * change for s in coarse_samples], change * (1.0 / element_span)


def ends_of(first, second):
    high = coarse_samples[0] * first + coarse_samples[1] * second
    return [first + second - high, high]


def high_low(values):
    high = values.astype(jnp.bfloat16)
    return high, (values - high.astype(jnp.float32)).astype(jnp.bfloat16)


def reads(pairs):
    return set(range(pairs[0], pairs[-1] + 2))


def plan_steps(spans):
    plan = []
    for first, count in spans:
        pairs = list(range(first, first + count))
        plan.append([pairs[n : n + 2] for n in range(0, count, 2)])
    return plan


class Slab:
    def __init__(self, width, across):
        self.width = width
        self.y_step = 2 * across
        lane = lax.broadcasted_iota(jnp.int32, (8, width), 1)
        x = (lane // 2) % across
        self.bottom, self.top, self.even = x == 0, x == across - 1, lane % 2 == 0
        self.row = lax.broadcasted_iota(jnp.int32, (8, width), 0)
        row = lax.broadcasted_iota(jnp.int32, (32, width), 0)
        lane = lax.broadcasted_iota(jnp.int32, (32, width), 1)
        on_face = (row == 0) | ((row >= 3) & (row <= 11))
        self.keep = jnp.where(on_face & ((lane // 2) % across == 0), 0.0, 1.0)

    def lanes(self, v, step):
        return pltpu.roll(v, step % self.width, 1)

    def from_next(self, v, x, y):
        if x or y:
            v = self.lanes(v, -2 * x - self.y_step * y)
        return jnp.where(self.top, 0.0, v) if x else v

    def from_next_z(self, v, ahead, x, y):
        step = -2 * x - self.y_step * y
        v = jnp.where(self.even, self.lanes(v, step - 1), self.lanes(ahead, step + 1))
        return jnp.where(self.top, 0.0, v) if x else v

    def onto_next(self, v, x, y, z=0):
        if x or y or z:
            v = self.lanes(v, 2 * x + self.y_step * y + z)
        return jnp.where(self.bottom, 0.0, v) if x else v

    def gather(self, component, here, ahead):
        row = self.row
        g0, g1, g2, g3 = here[0:8], here[8:16], here[16:24], here[24:32]
        a0 = ahead[0:8]
        z0, xz = self.from_next_z(g0, a0, 0, 0), self.from_next_z(g0, a0, 1, 0)
        yz, xyz = self.from_next_z(g0, a0, 0, 1), self.from_next_z(g0, a0, 1, 1)
        z2 = self.from_next_z(g2, ahead[16:24], 0, 0)
        edges = jnp.where(row <= 4, xz, self.from_next(g0, 1, 1))
        edges = jnp.where(row == 0, xyz, jnp.where(row <= 2, yz, edges))
        return jnp.concatenate(
            [
                g0,
                g1,
                g2,
                jnp.where(row < 4, z2, g3),
                self.from_next(g0, 1, 0),
                jnp.where(row == 7, yz, self.from_next(g0, 0, 1)),
                jnp.where(row == 7, xz, z0),
                jnp.where(row < 4, self.from_next(g1, 1, 0), self.from_next(g1, 0, 1)),
                edges,
                jnp.where(row == component, 1.0, 0.0),
            ],
            0,
        )

    def scatter(self, part, behind):
        row = self.row
        g0, g1, g2, g3, x0, y0, z0, sides, edges = (part[8 * n : 8 * n + 8] for n in range(9))
        last = row == 7
        for_z = jnp.where(last, 0.0, z0)
        for_xz = jnp.where(last, z0, jnp.where((row == 3) | (row == 4), edges, 0.0))
        for_yz = jnp.where(last, y0, jnp.where((row == 1) | (row == 2), edges, 0.0))
        for_xyz = jnp.where(row == 0, edges, 0.0)
        for_xy = jnp.where(row >= 5, edges, 0.0)

        def above(z):
            return (
                self.onto_next(for_z, 0, 0, z)
                + self.onto_next(for_yz, 0, 1, z)
                + self.onto_next(for_xz, 1, 0, z)
                + self.onto_next(for_xyz, 1, 1, z)
            )

        own0 = g0 + self.onto_next(x0, 1, 0) + self.onto_next(jnp.where(last, 0.0, y0), 0, 1)
        own0 = own0 + self.onto_next(for_xy, 1, 1)
        own0 = own0 + jnp.where(self.even, behind[0], above(1))
        own1 = g1 + jnp.where(row < 4, self.onto_next(sides, 1, 0), self.onto_next(sides, 0, 1))
        share2 = jnp.where(self.even, behind[1], self.onto_next(g3, 0, 0, 1))
        own2 = g2 + jnp.where(row < 4, share2, 0.0)
        moved = (above(-1), self.onto_next(g3, 0, 0, -1))
        return jnp.concatenate([self.twinned(own0), own1, own2, g3], 0), moved

    def twinned(self, v):
        twins = jnp.where(self.row == 7, pltpu.roll(v, 7, 0), 0.0)
        return v + jnp.where(self.row == 0, pltpu.roll(v, 1, 0), twins)

    def absorb(self, total, behind):
        low = self.twinned(jnp.where(self.even, behind[0], 0.0))
        high = jnp.where(self.even & (self.row < 4), behind[1], 0.0)
        return jnp.concatenate(
            [total[0:8] + low, total[8:16], total[16:24] + high, total[24:32]], 0
        )

    def gradient(self, u, spread, pairs):
        parts = [
            high_low(self.gather(i, u[i, pair], u[i, pair + 1]))
            for i in range(3)
            for pair in pairs
        ]
        return jnp.dot(
            spread[0:POINT_ROWS, :],
            jnp.concatenate([jnp.concatenate([h, l, h], 0) for h, l in parts], 1),
            preferred_element_type=jnp.float32,
        )

    def stresses(self, gradient, count):
        width = self.width
        rows = 16
        high, low = {}, {}
        for q in range(count):
            for r in range(64 // rows):
                deform = [
                    [
                        gradient[
                            64 * e + rows * r : 64 * e + rows * (r + 1),
                            width * (count * i + q) : width * (count * i + q + 1),
                        ]
                        for e in range(3)
                    ]
                    for i in range(3)
                ]
                stress = point_stress(deform)
                for i in range(3):
                    for e in range(3):
                        high[e, r, i, q], low[e, r, i, q] = high_low(stress[i][e])

        def whole(part):
            return jnp.concatenate(
                [
                    jnp.concatenate([part[e, r, i, q] for i in range(3) for q in range(count)], 1)
                    for e in range(3)
                    for r in range(64 // rows)
                ],
                0,
            )

        return whole(high), whole(low)

    def force(self, gradient, stiff, collect, pairs, first=0, rows=ROWS):
        high, low = self.stresses(gradient, len(pairs))
        both = collect[first : first + 2 * rows, :]
        force = jnp.dot(both, high, preferred_element_type=jnp.float32)
        force = force[0:rows] + (
            force[rows:] + jnp.dot(both[0:rows], low, preferred_element_type=jnp.float32)
        )
        stiffness = [stiff[pair : pair + 1, :] for pair in pairs]
        return force * jnp.concatenate(stiffness * 3, 1)

    def run(self, u, stiff, spread, collect, jobs, given=None):
        plan = plan_steps([job[:2] for job in jobs])
        steps = [(pairs, n) for n, chunks in enumerate(plan) for pairs in chunks]
        none = jnp.zeros((8, self.width), jnp.float32)
        ahead, carry, job = None, None, None
        for at, (pairs, n) in enumerate(steps):
            ready = given is not None and n == 0 and pairs == given[0]
            gradient = ahead
            if ahead is None and not ready:
                gradient = self.gradient(u, spread, pairs)
            if not ready:
                ahead = None
            if ahead is None and at + 1 < len(steps):
                later, later_job = steps[at + 1]
                if given is not None and later_job == 0 and later == given[0]:
                    later, later_job = steps[at + 2]
                if later_job == n or not reads(later) & set(pairs):
                    ahead = self.gradient(u, spread, later)
            if job != n:
                carry, job = [(none, none) for i in range(3)], n
            if ready:
                for q, pair in enumerate(pairs):
                    total = given[1][q]
                    if q == 0:
                        total = [self.absorb(total[i], carry[i]) for i in range(3)]
                    jobs[n][2](pair, total)
                carry = list(given[2])
                continue
            force = self.force(gradient, stiff, collect, pairs)
            totals = [[] for pair in pairs]
            for q in range(len(pairs)):
                for i in range(3):
                    lane = (len(pairs) * i + q) * self.width
                    total, carry[i] = self.scatter(force[:, lane : lane + self.width], carry[i])
                    totals[q].append(total)
            for pair, total in zip(pairs, totals):
                jobs[n][2](pair, total)
        return carry

    def smoothing(self, u, f, f_shift, d, spans, bound):
        jobs = []
        for (first, count), (held, added) in zip(spans, chebyshev_steps()):

            def finish(pair, forces, held=held, added=added):
                for i in range(3):
                    z = (added / bound) * self.keep * (f[i, pair + f_shift] - forces[i])
                    move = held * d[i, pair] + z if held else z
                    d[i, pair] = move
                    u[i, pair] = u[i, pair] + move

            jobs.append((first, count, finish))
        return jobs

    def owed(self, carry, bound):
        scale = -chebyshev_steps()[-1][1] / bound
        return [
            (
                scale * jnp.where(self.even, low, 0.0) * self.keep[0:8],
                scale * jnp.where(self.even, high, 0.0) * self.keep[16:24],
            )
            for low, high in carry
        ]

    def corners_of(self, v):
        ahead = pltpu.roll(v, 7, 0)
        found = {}
        for a in range(2):
            for b in range(2):
                found[a, b, 0] = self.from_next(v, a, b)
                found[a, b, 1] = self.from_next_z(v, ahead, a, b)
        return found

    def assemble(self, part):
        here, odd, even = 0.0, 0.0, 0.0
        for a in range(2):
            for b in range(2):
                here = here + self.onto_next(part[a, b, 0], a, b)
                odd = odd + self.onto_next(part[a, b, 1], a, b, 1)
                even = even + self.onto_next(part[a, b, 1], a, b, -1)
        return here + jnp.where(self.even, pltpu.roll(even, 1, 0), odd)

    def coarse_force(self, values, stiffness):
        grads = []
        for i in range(3):
            v = self.corners_of(values[i])
            vz, sz = {}, {}
            for a in two:
                for b in two:
                    vz[a, b], sz[a, b] = at_points(v[a, b, 0], v[a, b, 1])
            vv, vs, sv = {}, {}, {}
            for a in two:
                for k in two:
                    vv[a, k], vs[a, k] = at_points(vz[a, 0][k], vz[a, 1][k])
                sv[a], unused = at_points(sz[a, 0], sz[a, 1])
            dx, dy, dz = {}, {}, {}
            for k in two:
                for j in two:
                    dx[j, k] = (vv[1, k][j] - vv[0, k][j]) * (1.0 / element_span)
                line, unused = at_points(vs[0, k], vs[1, k])
                for h in two:
                    dy[h, k] = line[h]
            for j in two:
                line, unused = at_points(sv[0][j], sv[1][j])
                for h in two:
                    dz[h, j] = line[h]
            grads.append((dx, dy, dz))
        weight = element_span**2 / 8.0
        scaled = weight * stiffness
        sums = [({}, {}, {}) for i in range(3)]

        def add(table, key, value):
            table[key] = table[key] + value if key in table else value

        for h in two:
            for j in two:
                for k in two:
                    deform = [
                        [grads[i][0][j, k], grads[i][1][h, k], grads[i][2][h, j]]
                        for i in range(3)
                    ]
                    for i in range(3):
                        deform[i][i] = deform[i][i] + 1.0
                    stress = point_stress(deform)
                    for i in range(3):
                        add(sums[i][0], (j, k), stress[i][0])
                        add(sums[i][1], (h, k), stress[i][1])
                        add(sums[i][2], (h, j), stress[i][2])

        forces = []
        for i in range(3):
            part = {}
            qx, qy, qz = sums[i]
            along_z = [ends_of(qx[j, 0], qx[j, 1]) for j in two]
            for c in two:
                line = ends_of(along_z[0][c], along_z[1][c])
                for b in two:
                    part[0, b, c] = -line[b]
                    part[1, b, c] = line[b]
            along_z = [ends_of(qy[h, 0], qy[h, 1]) for h in two]
            for c in two:
                line = ends_of(along_z[0][c], along_z[1][c])
                for a in two:
                    part[a, 0, c] = part[a, 0, c] - line[a]
                    part[a, 1, c] = part[a, 1, c] + line[a]
            along_y = [ends_of(qz[h, 0], qz[h, 1]) for h in two]
            for b in two:
                line = ends_of(along_y[0][b], along_y[1][b])
                for a in two:
                    part[a, b, 0] = part[a, b, 0] - line[a]
                    part[a, b, 1] = part[a, b, 1] + line[a]
            forces.append(self.assemble({key: scaled * value for key, value in part.items()}))
        return forces


def window_pair(slab, first_layer, own_layers, fetch):
    found = []
    for parity in range(2):
        layer = first_layer + parity
        device = layer // own_layers
        layer = layer - device * own_layers
        found.append((device, layer // 2, layer % 2))
    values = [fetch(device, q) for device, q, parity in found]
    if found[0][:2] == found[1][:2] or (values[0] is None and values[1] is None):
        return values[0]
    for parity in range(2):
        if values[parity] is None:
            values[parity] = jnp.zeros_like(values[1 - parity])
        elif found[parity][2] != parity:
            values[parity] = slab.lanes(values[parity], 2 * parity - 1)
    lane = lax.broadcasted_iota(jnp.int32, values[0].shape, 1)
    return jnp.where(lane % 2 == 0, values[0], values[1])


def first_sources(own_layers):
    return list(range(-BEFORE // own_layers, (own_layers + BEFORE - 1) // own_layers + 1))


def whole_pairs(own_layers):
    return own_layers == 4


def turn_rows(block, mixed, turned, width, at):
    for tile in range(SENT // 128):
        n = at * (SENT // 128) + tile
        for m in range(width // 4):
            first = 12 * m + 4 * tile
            mixed[n, 4 * m : 4 * m + 4, :] = block[first : first + 4, :]
        turned[at, 128 * tile : 128 * tile + 128, :] = mixed[n].T


def regroup(slab, field, rows):
    values, hard = [], None
    for i in range(3):
        parts = [rows(24 * i + 8 * n) for n in range(3)]
        if field == 0 and i == 0:
            hard = parts[0][TWIN : TWIN + 1]
        parts[0] = jnp.where(slab.row == TWIN, pltpu.roll(parts[0], TWIN, 0), parts[0])
        parts.append(jnp.where(slab.row < 4, 0.0, rows(68 + 4 * i)))
        whole = jnp.concatenate(parts, 0)
        values.append(whole * slab.keep if field == 0 else whole)
    return values, hard


def layer_above(slab, turned, at, i):
    first = NEXT_COLUMN + 12 * i
    low, high = turned[at, first : first + 8, :], turned[at, first + 4 : first + 12, :]
    high = jnp.where(slab.row < 4, pltpu.roll(high, 4, 0), 0.0)
    low = jnp.where(slab.row == TWIN, pltpu.roll(low, TWIN, 0), low)
    nothing = jnp.zeros_like(low)
    return jnp.concatenate([low, nothing, high, nothing], 0) * slab.keep


def make_own_kernel(width, across, own_layers):
    own_pairs = own_layers // 2
    pairs = list(range(own_pairs))

    def own_kernel(block, spread, collect, u, f, stiff, forces, moved, mixed, turned):
        slab = Slab(width, across)
        turn_rows(block, mixed, turned, width, 0)
        for pair in pairs:
            for field, target in enumerate((u, f)):

                def rows(start, field=field, pair=pair):
                    at = BLOCK * (2 * pair + field) + start
                    return turned[0, at : at + 8, :]

                values, hard = regroup(slab, field, rows)
                for i in range(3):
                    target[i, pair] = values[i]
                if field == 0:
                    stiff[pair : pair + 1, :] = hard
        for i in range(3):
            u[i, own_pairs] = layer_above(slab, turned, 0, i)

        def finish(pair, total):
            for i in range(3):
                forces[i, pair] = total[i]

        carry = slab.run(u, stiff, spread, collect, [(0, own_pairs, finish)])
        for i in range(3):
            moved[i, 0] = carry[i][0]
            moved[i, 1] = carry[i][1]

    return own_kernel


def make_first_kernel(width, across, own_layers, fine_bound):
    own = BEFORE // 2
    own_pairs = (own_layers + 1) // 2
    spans = []
    prepared = whole_pairs(own_layers)
    for n in (4, 3, 2, 1):
        low, high = BEFORE - n, BEFORE + own_layers + n - 1 + prepared
        spans.append((low // 2, (high + 1) // 2 - low // 2))
    sources = [n for n in first_sources(own_layers) if n or not prepared]

    def first_kernel(*refs):
        arrived = refs[: len(sources)]
        refs = refs[len(sources) :]
        if prepared:
            own_u, own_f, own_stiff, own_forces, own_moved = refs[:5]
            refs = refs[5:]
        spread, collect, message, *sent, f = refs[:-6]
        u, d, stiff, shares, mixed, turned = refs[-6:]
        slab = Slab(width, across)
        if not prepared:
            u[...] = jnp.zeros(u.shape, jnp.float32)
            f[...] = jnp.zeros(f.shape, jnp.float32)
        shares[...] = jnp.zeros(shares.shape, jnp.float32)
        stiff[...] = jnp.zeros(stiff.shape, jnp.float32)
        for n in range(len(sources)):
            turn_rows(arrived[n], mixed, turned, width, n)
        for pair in range(PAIRS):
            if prepared and own <= pair < own + own_pairs:
                for i in range(3):
                    u[i, pair] = own_u[i, pair - own]
                    f[i, pair] = own_f[i, pair - own]
                stiff[pair : pair + 1, :] = own_stiff[pair - own : pair - own + 1, :]
                continue
            for field, target in enumerate((u, f)):

                def rows(start, field=field, pair=pair):
                    def fetch(device, q):
                        if device not in sources:
                            return None
                        at = BLOCK * (2 * q + field) + start
                        return turned[sources.index(device), at : at + 8, :]

                    value = window_pair(slab, 2 * pair - BEFORE, own_layers, fetch)
                    return jnp.zeros((8, width), jnp.float32) if value is None else value

                values, hard = regroup(slab, field, rows)
                for i in range(3):
                    target[i, pair] = values[i]
                if field == 0:
                    stiff[pair : pair + 1, :] = hard
        given = None
        if prepared:
            for i in range(3):
                u[i, PAIRS] = layer_above(slab, turned, sources.index(1), i)
            given = (
                list(range(own, own + own_pairs)),
                [[own_forces[i, q] for i in range(3)] for q in range(own_pairs)],
                [(own_moved[i, 0], own_moved[i, 1]) for i in range(3)],
            )

        first, count = spans[3]
        blocks = [
            high_low(slab.keep * f[i, pair]) for pair in range(first, first + count) for i in range(3)
        ]
        loads = jnp.dot(
            spread[POINT_ROWS:, 0:96],
            jnp.concatenate([jnp.concatenate([h, l, h], 0) for h, l in blocks], 1),
            preferred_element_type=jnp.float32,
        )
        jobs = slab.smoothing(u, f, 0, d, spans[0:3], fine_bound)
        slab.run(u, stiff, spread, collect, jobs, given)
        steps = plan_steps([spans[3]])[0]
        gradients = [slab.gradient(u, spread, pairs) for pairs in steps]
        for pairs, gradient in zip(steps, gradients):
            force = slab.force(gradient, stiff, collect, pairs, 2 * ROWS, 16)
            for q, pair in enumerate(pairs):
                for i in range(3):
                    at = (len(pairs) * i + q) * width
                    load_at = (3 * (pair - first) + i) * width
                    part = force[:, at : at + width]
                    part = jnp.where(slab.bottom, part[8:16], part[0:8])
                    shares[i, pair] = loads[0:8, load_at : load_at + width] - part

        restricted = [
            slab.assemble({corner: shares[i, :, n, :] for n, corner in enumerate(CORNERS)})
            for i in range(3)
        ]
        def line(rows, q):
            return rows[own + q : own + q + 1]

        for q in range(own_pairs):
            for i in range(3):
                message[i, q] = u[i, own + q]
                message[i, q, RESTRICTED_SLOT : RESTRICTED_SLOT + 1, :] = line(restricted[i], q)
            message[0, q, STIFF_SLOT : STIFF_SLOT + 1, :] = line(stiff, q)
        if prepared:
            down, up = sent
            for i in range(3):
                down[i, 0:32] = u[i, own]
                down[i, 32:40] = u[i, own + 1, 0:8, :]
                down[i, 40:48] = u[i, own + 1, 16:24, :]
                up[i] = u[i, own + 1]
                for n, row in enumerate(
                    (line(restricted[i], 0), line(restricted[i], 1), u[i, own + 2, 0:1, :])
                    + (line(restricted[i], 2),)
                ):
                    down[i, 24 + n : 25 + n, :] = row
                for n, row in enumerate(
                    (line(restricted[i], 1), line(restricted[i], 0), u[i, own, 0:1, :])
                ):
                    up[i, 24 + n : 25 + n, :] = row
            for q in range(own_pairs):
                down[q, 32 + TWIN : 33 + TWIN, :] = line(stiff, q)
                up[q, TWIN : TWIN + 1, :] = line(stiff, q)
            return
        edge = sent[0]
        for q in range(own_pairs):
            for i in range(3):
                edge[q, i : i + 1, :] = u[i, own + q, 0:1, :]
                edge[q, 3 + i : 4 + i, :] = line(restricted[i], q)
            edge[q, 6:8, :] = jnp.broadcast_to(line(stiff, q), (2, width))

    return first_kernel


def shares_sent(own_layers):
    return own_layers % 2 == 0


def sources_of(own_layers):
    below = 2 if shares_sent(own_layers) else 3
    whole = range(-below // own_layers, (own_layers + 2) // own_layers + 1)
    coarse = range(-(below + 2) // own_layers, (own_layers + 4) // own_layers + 1)
    return list(whole), [n for n in coarse if n not in whole]


def message_line(message, q, n):
    i, slot = ((n, 0), (n - 3, RESTRICTED_SLOT), (0, STIFF_SLOT))[n // 3]
    return message[i, q, slot : slot + 1, :]


def sent_readers(slab, up, message, down):
    def block_of(device, q, i):
        if device == 0:
            return message[i, q]
        if (device, q) == (1, 0):
            whole = down[i, 0:32]
        elif (device, q) == (1, 1):
            low, high = down[i, 32:40], down[i, 40:48]
            low = jnp.where(slab.row == TWIN, pltpu.roll(low, TWIN, 0), low)
            whole = jnp.concatenate([low, jnp.zeros_like(low), high, jnp.zeros_like(low)], 0)
        elif (device, q) == (-1, 1):
            low = up[i, 0:8]
            low = jnp.where(slab.row == TWIN, pltpu.roll(low, TWIN, 0), low)
            whole = jnp.concatenate([low, up[i, 8:32]], 0)
        else:
            return None
        return whole

    def line_of(device, q, n):
        if device == 0:
            return message_line(message, q, n)
        kind, i = n // 3, n % 3
        if device == 1:
            row = ((0, 24), (32, 25))[q][kind] if kind < 2 else 32 + TWIN
            i = i if kind < 2 else q
            return down[i, row : row + 1, :]
        if device == -1:
            row = ((26, 25), (0, 24))[q][kind] if kind < 2 else TWIN
            i = i if kind < 2 else q
            return up[i, row : row + 1, :]
        if (device, q) == (2, 0) and kind < 2:
            return down[i, 26 + kind : 27 + kind, :]
        return None

    return block_of, line_of


def make_second_kernel(width, across, own_layers, fine_bound, coarse_bound):
    own = BEFORE_B // 2
    own_pairs = (own_layers + 1) // 2
    shift = (BEFORE - BEFORE_B) // 2
    whole, outer = sources_of(own_layers)
    steps = chebyshev_steps()
    spans = []
    for n in (3, 2, 1):
        low, high = BEFORE_B - n + shares_sent(own_layers), BEFORE_B + own_layers + n - 1
        spans.append((low // 2, (high + 1) // 2 - low // 2))

    def second_kernel(*refs):
        slab = Slab(width, across)
        if whole_pairs(own_layers):
            up, message, down = refs[:3]
            refs = refs[3:]
            block_of, line_of = sent_readers(slab, up, message, down)
        else:
            messages = dict(zip(whole, refs))
            edges = dict(zip(outer, refs[len(whole) :]))
            refs = refs[len(whole) + len(outer) :]

            def block_of(device, q, i):
                return messages[device][i, q] if device in messages else None

            def line_of(device, q, n):
                if device in messages:
                    return message_line(messages[device], q, n)
                return edges[device][q, n : n + 1, :] if device in edges else None

        f, spread, collect, transfer_back, out, u, d, stiff, coarse = refs

        def pair_of(pair, fetch):
            return window_pair(slab, 2 * pair - BEFORE_B, own_layers, fetch)

        coarse[...] = jnp.zeros(coarse.shape, jnp.float32)
        for pair in range(PAIRS_B):
            for i in range(3):
                block = pair_of(pair, lambda device, q: block_of(device, q, i))
                u[i, pair] = jnp.zeros((32, width), jnp.float32) if block is None else block
            for n in range(7):
                line = pair_of(pair, lambda device, q: line_of(device, q, n))
                if line is not None:
                    coarse[n, pair : pair + 1, :] = line
        stiff[...] = coarse[6]

        stiffness = coarse[6]
        keep_coarse = jnp.where(slab.bottom, 0.0, 1.0)
        start = [coarse[i] for i in range(3)]
        restricted = [coarse[3 + i] for i in range(3)]
        before = slab.coarse_force(start, stiffness)
        move = [(steps[0][1] / coarse_bound) * keep_coarse * restricted[i] for i in range(3)]
        level = [start[i] + move[i] for i in range(3)]
        for held, added in steps[1:]:
            force = slab.coarse_force(level, stiffness)
            for i in range(3):
                z = keep_coarse * (restricted[i] + before[i] - force[i])
                move[i] = held * move[i] + (added / coarse_bound) * z
                level[i] = level[i] + move[i]

        weights = [jnp.broadcast_to(transfer_back[:, n : n + 1], (32, width)) for n in range(8)]
        for i in range(3):
            change = slab.corners_of(level[i] - start[i])
            for pair in range(spans[0][0], min(spans[0][0] + spans[0][1] + 1, PAIRS_B)):
                lift = u[i, pair]
                for n, corner in enumerate(CORNERS):
                    lift = lift + weights[n] * change[corner][pair : pair + 1]
                u[i, pair] = lift

        jobs = slab.smoothing(u, f, shift, d, spans, fine_bound)
        owed = slab.owed(slab.run(u, stiff, spread, collect, jobs), fine_bound)

        lower = lax.broadcasted_iota(jnp.int32, (width // 8, 8, 128), 1) < 4
        nothing = jnp.zeros((8, width), jnp.float32)
        sides = []
        for q in range(2):
            if q or not shares_sent(own_layers):
                owed = [(nothing, nothing)] * 3
            rows = []
            for i in range(3):
                value = u[i, own + q]
                rows += [value[0:24], jnp.where(slab.row < 4, owed[i][1], value[24:32])]
            rows += [owed[i][0] for i in range(3)]
            rows += [level[i][own + q : own + q + 1] for i in range(3)] + [nothing[0:5]]
            sides.append(jnp.concatenate(rows, 0).T.reshape(width // 8, 8, 128))
        out[:, 0] = jnp.where(lower, sides[0], pltpu.roll(sides[1], 4, 1))
        out[:, 1] = jnp.where(lower, pltpu.roll(sides[0], 4, 1), sides[1])

    return second_kernel


def solution(mesh):
    rows_of, columns_of = mesh.shape["gx"], mesh.shape["gy"]
    devices = rows_of * columns_of
    order = ring_order(rows_of, columns_of)
    own_layers = EZ // devices
    own_pairs = (own_layers + 1) // 2
    width = 4 * devices
    across = 2 * rows_of
    near = first_sources(own_layers)
    prepared = whole_pairs(own_layers)
    whole, outer = sources_of(own_layers)
    spread, collect, fine_bound = element_tables()
    coarse_bound = build_tables([0.0, 1.0], 2)[2]
    transfer_back = transfer_table()[1]
    corners, from_loads = corner_tables()
    from_loads = np.pad(from_loads, ((0, 0), (0, spread.shape[1] - from_loads.shape[1])))
    spread = np.concatenate([spread, from_loads], 0)
    collect = np.concatenate([collect, corners], 0)
    wide = pltpu.CompilerParams(vmem_limit_bytes=60 * 1024 * 1024)
    limit = pltpu.CompilerParams(vmem_limit_bytes=48 * 1024 * 1024)
    f32 = jnp.float32

    pack = pl.pallas_call(
        functools.partial(pack_kernel, order),
        out_shape=pltpu.VMEM((devices * 12, 128), f32),
        in_specs=[pl.BlockSpec(memory_space=pl.ANY)] * 5,
        out_specs=pl.BlockSpec(memory_space=pltpu.VMEM),
        scratch_shapes=[
            pltpu.VMEM((3, 6, 3, 384), f32),
            pltpu.VMEM((3, 6, 3, 384), f32),
            pltpu.VMEM((2, 1, EZ), f32),
            pltpu.VMEM((1, 1, 192), jnp.int32),
            pltpu.VMEM((384, 512), jnp.bfloat16),
            pltpu.VMEM((128, 384), f32),
            pltpu.VMEM((384, 128), f32),
            pltpu.VMEM((6, 136, 128), f32),
            pltpu.SemaphoreType.DMA((5,)),
        ],
        compiler_params=wide,
    )
    own = pl.pallas_call(
        make_own_kernel(width, across, own_layers),
        out_shape=(
            jax.ShapeDtypeStruct((3, own_pairs + 1, 32, width), f32),
            jax.ShapeDtypeStruct((3, own_pairs, 32, width), f32),
            jax.ShapeDtypeStruct((own_pairs, width), f32),
            jax.ShapeDtypeStruct((3, own_pairs, 32, width), f32),
            jax.ShapeDtypeStruct((3, 2, 8, width), f32),
        ),
        scratch_shapes=[
            pltpu.VMEM((SENT // 128, width, 128), f32),
            pltpu.VMEM((1, SENT, width), f32),
        ],
        compiler_params=limit,
        cost_estimate=pl.CostEstimate(flops=400_000_000, bytes_accessed=1_000_000, transcendentals=0),
    )
    sent = [jax.ShapeDtypeStruct((own_pairs, 8, width), f32)]
    if prepared:
        sent = [jax.ShapeDtypeStruct((3, rows, width), f32) for rows in (48, 32)]
    first = pl.pallas_call(
        make_first_kernel(width, across, own_layers, fine_bound),
        out_shape=(
            jax.ShapeDtypeStruct((3, own_pairs, 32, width), f32),
            *sent,
            jax.ShapeDtypeStruct((3, PAIRS, 32, width), f32),
        ),
        scratch_shapes=[
            pltpu.VMEM((3, 8, 32, width), f32),
            pltpu.VMEM((3, 8, 32, width), f32),
            pltpu.VMEM((8, width), f32),
            pltpu.VMEM((3, 8, 8, width), f32),
            pltpu.VMEM((len(near) * (SENT // 128), width, 128), f32),
            pltpu.VMEM((len(near), SENT, width), f32),
        ],
        compiler_params=limit,
    )
    second = pl.pallas_call(
        make_second_kernel(width, across, own_layers, fine_bound, coarse_bound),
        out_shape=jax.ShapeDtypeStruct((devices // 2, 2, 8, 128), f32),
        scratch_shapes=[
            pltpu.VMEM((3, PAIRS_B, 32, width), f32),
            pltpu.VMEM((3, PAIRS_B, 32, width), f32),
            pltpu.VMEM((PAIRS_B, width), f32),
            pltpu.VMEM((7, PAIRS_B, width), f32),
        ],
        compiler_params=limit,
    )
    unpack = pl.pallas_call(
        functools.partial(unpack_kernel, order),
        out_shape=(
            jax.ShapeDtypeStruct((3, 6, 3, 384), f32),
            jax.ShapeDtypeStruct((3, 2, 1, EZ), f32),
        ),
        scratch_shapes=[pltpu.VMEM((2, 128, 128), f32), pltpu.VMEM((384, 128), f32)],
        compiler_params=limit,
    )
    everyone = ("gy", "gx")

    def from_device(block, distance):
        place = {k: m % rows_of * columns_of + m // rows_of for m, k in enumerate(order)}
        route = [(place[(k + distance) % devices], place[k]) for k in range(devices)]
        return lax.ppermute(block, ("gx", "gy"), route)

    def body(initial, forcing, modulus, solid_list):
        sent = pack(initial, forcing, modulus, solid_list, jnp.asarray(pack_table()))
        sent = sent.reshape(devices, SENT // 128, 4, 128)
        arrived = lax.all_to_all(sent, everyone, 0, 0, tiled=True).reshape(devices * 12, 128)
        blocks = [from_device(arrived, n) if n else arrived for n in near]
        if prepared:
            blocks = [block for n, block in zip(near, blocks) if n]
            blocks += own(arrived, jnp.asarray(spread), jnp.asarray(collect))
        message, *edges, load = first(
            *blocks,
            jnp.asarray(spread),
            jnp.asarray(collect),
        )
        if prepared:
            down, up = edges
            messages = [from_device(up, -1), message, from_device(down, 1)]
        else:
            messages = [from_device(message, n) if n else message for n in whole]
            messages += [from_device(edges[0], n) for n in outer]
        result = second(
            *messages,
            load,
            jnp.asarray(spread),
            jnp.asarray(collect),
            jnp.asarray(transfer_back),
        )
        back = lax.all_to_all(result.reshape(devices, 8, 128), everyone, 0, 0, tiled=True)
        return unpack(back, jnp.asarray(unpack_table()))

    placed = (
        P(None, "gx", "gy", None),
        P(None, "gx", "gy", None),
        P("gx", "gy", None),
        P("gx", "gy", None),
    )
    return jax.shard_map(
        body,
        mesh=mesh,
        in_specs=placed,
        out_specs=(P(None, "gx", "gy", None), P(None, "gx", "gy", None)),
        check_vma=False,
    )
```

```python
import functools
import math

import jax
import jax.numpy as jnp
import numpy as np
from jax import lax
from jax.experimental import pallas as pl
from jax.experimental.pallas import tpu as pltpu
from jax.sharding import PartitionSpec as P

CHEB = 3
EZ = 128

element_span = 20.0
lame_ratio = 4.0
rest_ratio = 1.25
modulus_top = 2.0
spectrum_floor = 0.05
interval_centre = (1.0 + spectrum_floor) / 2.0
interval_radius = (1.0 - spectrum_floor) / 2.0
interval_ratio = interval_centre / interval_radius
inner_anchors = (0.5 - 0.5 / math.sqrt(5.0), 0.5 + 0.5 / math.sqrt(5.0))

BEFORE = 4
PAIRS = 6
BEFORE_B = 6
PAIRS_B = 8
BLOCK = 84
SENT = 384

SLOTS = [
    (0, 0, 0), (1, 0, 0), (2, 0, 0), (0, 1, 0), (0, 2, 0), (0, 0, 1), (0, 0, 2), None,
    (0, 1, 1), (0, 1, 2), (0, 2, 1), (0, 2, 2), (1, 0, 1), (1, 0, 2), (2, 0, 1), (2, 0, 2),
    (1, 1, 0), (1, 2, 0), (2, 1, 0), (2, 2, 0), (1, 1, 1), (1, 1, 2), (1, 2, 1), (1, 2, 2),
    None, None, None, None, (2, 1, 1), (2, 1, 2), (2, 2, 1), (2, 2, 2),
]
TWIN = 7
NEXT_SLOTS = [0, 1, 2, 3, 4, 5, 6, 7, 16, 17, 18, 19]
NEXT_COLUMN = 4 * BLOCK
RESTRICTED_SLOT = 24
STIFF_SLOT = 25
OWN_SHIFT, SHIFT_X, SHIFT_Y, SHIFT_Z = (0, 0, 0), (1, 0, 0), (0, 1, 0), (0, 0, 1)
ELEMENT_ROWS = (
    [(slot, OWN_SHIFT) for slot in range(24)]
    + [(slot, SHIFT_Z) for slot in range(16, 20)]
    + [(slot, OWN_SHIFT) for slot in range(28, 32)]
    + [(slot, SHIFT_X) for slot in range(7)] + [None]
    + [(slot, SHIFT_Y) for slot in range(7)] + [(0, (0, 1, 1))]
    + [(slot, SHIFT_Z) for slot in range(7)] + [(0, (1, 0, 1))]
    + [(slot, SHIFT_X) for slot in range(8, 12)] + [(slot, SHIFT_Y) for slot in range(12, 16)]
    + [(0, (1, 1, 1)), (1, (0, 1, 1)), (2, (0, 1, 1)), (3, (1, 0, 1)), (4, (1, 0, 1))]
    + [(5, (1, 1, 0)), (6, (1, 1, 0)), (0, (1, 1, 0))]
)
ROWS = len(ELEMENT_ROWS)
DEPTH = 80
POINT_ROWS = 192
CORNERS = [(a, b, c) for a in range(2) for b in range(2) for c in range(2)]


def gauss_rule(point_count):
    if point_count == 2:
        offset = 1.0 / math.sqrt(3.0)
        points = [-offset, offset]
        weights = [1.0, 1.0]
    else:
        inner = math.sqrt(3.0 / 7.0 - 2.0 / 7.0 * math.sqrt(6.0 / 5.0))
        outer = math.sqrt(3.0 / 7.0 + 2.0 / 7.0 * math.sqrt(6.0 / 5.0))
        heavy = (18.0 + math.sqrt(30.0)) / 36.0
        light = (18.0 - math.sqrt(30.0)) / 36.0
        points = [-outer, -inner, inner, outer]
        weights = [light, heavy, heavy, light]
    return (np.array(points), np.array(weights))


def lagrange_tables(anchors, samples):
    values = np.zeros((len(samples), len(anchors)))
    slopes = np.zeros((len(samples), len(anchors)))
    for sample_index, sample in enumerate(samples):
        for anchor_index, anchor in enumerate(anchors):
            others = [
                location
                for location_index, location in enumerate(anchors)
                if location_index != anchor_index
            ]
            product = 1.0
            for location in others:
                product = product * (sample - location) / (anchor - location)
            values[sample_index, anchor_index] = product
            derivative = 0.0
            for skipped in range(len(others)):
                summand = 1.0 / (anchor - others[skipped])
                for kept_index in range(len(others)):
                    if kept_index != skipped:
                        summand = (
                            summand * (sample - others[kept_index]) / (anchor - others[kept_index])
                        )
                derivative = derivative + summand
            slopes[sample_index, anchor_index] = derivative
    return (values, slopes)


def outer_three(first, second, third):
    return (
        first[:, None, None, :, None, None]
        * second[None, :, None, None, :, None]
        * third[None, None, :, None, None, :]
    )


def build_tables(anchors, point_count):
    raw_points, raw_weights = gauss_rule(point_count)
    samples = (raw_points + 1.0) / 2.0
    weights = raw_weights / 2.0
    basis_values, slopes = lagrange_tables(anchors, samples)
    quad_total = point_count**3
    nodal_count = len(anchors) ** 3
    derivative_one = outer_three(slopes, basis_values, basis_values).reshape(
        quad_total, nodal_count
    )
    derivative_two = outer_three(basis_values, slopes, basis_values).reshape(
        quad_total, nodal_count
    )
    derivative_three = outer_three(basis_values, basis_values, slopes).reshape(
        quad_total, nodal_count
    )
    stacked = np.stack([derivative_one, derivative_two, derivative_three]) / element_span
    volume = (weights[:, None, None] * weights[None, :, None] * weights[None, None, :]).reshape(
        -1
    ) * element_span**3
    forward = stacked.reshape(3 * quad_total, nodal_count)
    backward = (stacked * volume[None, :, None]).reshape(3 * quad_total, nodal_count).T
    weighted = stacked * volume[None, :, None]
    laplace = weighted[0].T @ stacked[0] + weighted[1].T @ stacked[1] + weighted[2].T @ stacked[2]
    matrix = np.zeros((nodal_count, 3, nodal_count, 3))
    for first in range(3):
        for second in range(3):
            block = weighted[second].T @ stacked[first] + (lame_ratio - 1.0) * (
                weighted[first].T @ stacked[second]
            )
            if first == second:
                block = block + laplace
            matrix[:, first, :, second] = block
    matrix = matrix.reshape(3 * nodal_count, 3 * nodal_count)
    vector = 1.5 + np.cos(1.3 * np.arange(3 * nodal_count))
    for repeat in range(200):
        vector = matrix @ vector
        vector = vector / np.sqrt(vector @ vector)
    largest = vector @ (matrix @ vector)
    return (forward, backward, float(4.0 * modulus_top * 1.1 * largest))


def row_nodes():
    nodes = []
    for entry in ELEMENT_ROWS:
        slot = SLOTS[entry[0]] if entry else None
        if slot is None or any(s and n for s, n in zip(entry[1], slot)):
            nodes.append(None)
        else:
            a, b, c = (3 * s + n for s, n in zip(entry[1], slot))
            nodes.append(16 * a + 4 * b + c)
    return nodes


def halves(matrix):
    whole = np.asarray(matrix, np.float32)
    high = whole.astype(jnp.bfloat16)
    low = (whole - high.astype(np.float32)).astype(jnp.bfloat16)
    return high, low


def element_tables():
    forward, backward, bound = build_tables([0.0, inner_anchors[0], inner_anchors[1], 1.0], 4)
    spread = np.zeros((forward.shape[0], DEPTH))
    collect = np.zeros((ROWS, backward.shape[1]))
    for row, node in enumerate(row_nodes()):
        if node is not None:
            spread[:, row] = forward[:, node]
            collect[row, :] = backward[node, :]
    for column in range(3):
        spread[64 * column : 64 * column + 64, ROWS + column] = 1.0
    spread_high, spread_low = halves(spread)
    collect_high, collect_low = halves(collect)
    return (
        np.concatenate([spread_high, spread_high, spread_low], 1),
        np.concatenate([collect_high, collect_low], 0),
        bound,
    )


def corner_tables():
    anchors = [0.0, inner_anchors[0], inner_anchors[1], 1.0]
    backward = build_tables(anchors, 4)[1]
    reach = np.stack([1.0 - np.array(anchors), np.array(anchors)])
    weights = outer_three(reach, reach, reach).reshape(8, 64)
    held = np.arange(64) < 16
    from_stress = np.concatenate([weights @ backward, np.where(held, 0.0, weights) @ backward], 0)
    from_loads = np.zeros((16, 32))
    from_loads[:8] = transfer_table()[0].T
    loads_high, loads_low = halves(from_loads)
    return (
        np.concatenate(halves(from_stress), 0),
        np.concatenate([loads_high, loads_high, loads_low], 1),
    )


def transfer_table():
    table = np.zeros((8, 32))
    reach = (0.0, inner_anchors[0], inner_anchors[1])
    for row, corner in enumerate(CORNERS):
        for column, slot in enumerate(SLOTS):
            if slot is not None:
                weight = 1.0
                for side, node in zip(corner, slot):
                    weight = weight * (reach[node] if side else 1.0 - reach[node])
                table[row, column] = weight
    back = table.T.copy()
    back[TWIN] = back[0]
    return table.T.astype(np.float32), back.astype(np.float32)


def chebyshev_steps():
    steps = [(0.0, 1.0 / interval_centre)]
    ratio_now = 1.0 / interval_ratio
    for sweep in range(1, CHEB):
        ratio_next = 1.0 / (2.0 * interval_ratio - ratio_now)
        steps.append((ratio_next * ratio_now, 2.0 * ratio_next / interval_radius))
        ratio_now = ratio_next
    return steps


def stack_row(field, component, layer, b):
    return field * 54 + component * 18 + layer * 3 + b


def block_column(component, slot):
    return 72 + 4 * component + slot - 28 if slot >= 24 else 24 * component + slot


def pack_table():
    table = np.zeros((3, 128, 2, 2, 128), np.float32)
    for field in range(2):
        for x in range(2):
            for component in range(3):
                for column, slot in enumerate(SLOTS):
                    if slot is not None:
                        a, b, c = slot
                        row = stack_row(field, component, 3 * x + a, b)
                        table[c, row, field, x, block_column(component, column)] = 1.0
                        if field == 0 and column in NEXT_SLOTS:
                            at = BLOCK + 12 * component + NEXT_SLOTS.index(column)
                            table[c, row, 1, x, at] = 1.0
            table[0, 108 + x, 0, x, TWIN] = 1.0
    return table.reshape(384, 512).astype(jnp.bfloat16)


def unpack_table():
    table = np.zeros((2, 128, 4, 128), np.float32)
    for x in range(2):
        for component in range(3):
            for column, slot in enumerate(SLOTS):
                if slot is not None:
                    a, b, c = slot
                    row = stack_row(0, component, 3 * x + a, b)
                    table[x, component * 32 + column, c, row] = 1.0
                    if column < 5:
                        table[x, 96 + 8 * component + column, 3, row] = 1.0
                    if column == 0:
                        table[x, 96 + 8 * component + TWIN, 3, row] = 1.0
                    if 16 <= column < 20:
                        table[x, component * 32 + column + 8, 3, row] = 1.0
            table[x, 120 + component, 0, 54 + 2 * component + x] = 1.0
    return table.reshape(256, 512).astype(jnp.bfloat16)


def pick(values, table):
    count = values.shape[0]
    parts = jnp.dot(
        jnp.concatenate(high_low(values), 0), table, preferred_element_type=jnp.float32
    )
    return parts[:count] + parts[count:]


def ring_order(rows_of, columns_of):
    if (rows_of, columns_of) != (4, 8):
        return list(range(rows_of * columns_of))
    order = []
    for z in range(4):
        for x in range(2):
            for y in range(2):
                chip = (z, 7 - z, 15 - z, 8 + z)[2 * x + y]
                order += [2 * chip, 2 * chip + 1]
    return order


def pack_kernel(
    order,
    initial_at, forcing_at, modulus_at, listing_at, table_at, out,
    initial, forcing, modulus, listing, table, rows, turned, places, ready,
):
    own_layers = EZ // len(order)
    sources = (listing_at, modulus_at, initial_at, forcing_at, table_at)
    copies = [
        pltpu.make_async_copy(source, here, ready.at[n])
        for n, (source, here) in enumerate(
            zip(sources, (listing, modulus, initial, forcing, table))
        )
    ]
    for copy in copies:
        copy.start()
    rows[108:128, :] = jnp.zeros((20, 384), jnp.float32)
    copies[0].wait()
    copies[1].wait()
    listed = listing[0].astype(jnp.float32)
    listed = jnp.concatenate([listed, jnp.full((1, 64), 256.0, jnp.float32)], 1)
    listed = jnp.broadcast_to(listed, (128, 256)).T
    lanes = lax.broadcasted_iota(jnp.int32, (256, 128), 1).astype(jnp.float32)
    row_at = lax.broadcasted_iota(jnp.int32, (128, 128), 0)
    stiff = jnp.zeros((128, 128), jnp.float32)
    for x in range(2):
        hit = jnp.max(jnp.where(listed == lanes + 128.0 * x, 1.0, 0.0), axis=0, keepdims=True)
        stiff = jnp.where(row_at == 108 + x, hit * modulus[x], stiff)
    copies[2].wait()
    copies[3].wait()
    for field, source in enumerate((initial, forcing)):
        for component in range(3):
            for layer in range(6):
                at = stack_row(field, component, layer, 0)
                rows[at : at + 3, :] = source[component, layer]
    for part in range(3):
        span = slice(128 * part, 128 * part + 128)
        turned[span, :] = rows[:, span].T
    picked = [turned[pl.ds(c, 128, stride=3), :] for c in range(3)]
    picked[0] = picked[0] + stiff.T
    copies[4].wait()
    wide = pick(jnp.concatenate(picked, 1), table[...])
    lane = lax.broadcasted_iota(jnp.int32, (128, 128), 1)
    for x in range(2):
        tiles = [None] * (SENT // 128)
        for n in range(4):
            pair, field = n // 2, n % 2
            moved = wide[:, 128 * (2 * field + x) : 128 * (2 * field + x) + 128]
            first = BLOCK * n
            if pair:
                moved = pltpu.roll(moved, 128 - 2 * pair, 0)
            if first % 128:
                moved = pltpu.roll(moved, first % 128, 1)
            for tile in range(first // 128, (first + BLOCK - 1) // 128 + 1):
                before = tiles[tile]
                if before is None:
                    tiles[tile] = moved
                else:
                    tiles[tile] = jnp.where(lane >= first - 128 * tile, moved, before)
        above = wide[:, 128 * (2 + x) : 128 * (2 + x) + 128]
        above = pltpu.roll(pltpu.roll(above, 128 - own_layers, 0), (NEXT_COLUMN - BLOCK) % 128, 1)
        tiles[-1] = jnp.where(lane >= NEXT_COLUMN % 128, above, tiles[-1])
        for tile in range(SENT // 128):
            places[3 * x + tile, 0:128, :] = tiles[tile]
            places[3 * x + tile, 128:136, :] = jnp.zeros((8, 128), jnp.float32)
    for device, k in enumerate(order):
        for tile in range(SENT // 128):
            for x in range(2):
                at = 12 * device + 4 * tile + 2 * x
                out[at : at + 2, :] = places[
                    3 * x + tile, own_layers * k : own_layers * k + 2, :
                ]


def unpack_kernel(order, arrived, table, out, coarse_out, layers, turned):
    devices = arrived.shape[0]
    own_layers = EZ // devices
    together = min(own_layers, 2)
    for x in range(2):
        for layer in range(0, own_layers, 2):
            row = (layer // 2) * 4 + x * 2
            if order == sorted(order):
                for n in range(together):
                    at = pl.ds(layer + n, devices, stride=own_layers)
                    layers[x, at, :] = arrived[:, row + n, :]
                continue
            for device, k in enumerate(order):
                at = own_layers * k + layer
                layers[x, at : at + together, :] = arrived[device, row : row + together, :]
    wide = pick(jnp.concatenate([layers[0], layers[1]], 1), table[...])
    shares = pltpu.roll(wide[:, 384:512], own_layers, 0)
    turned[pl.ds(0, 128, stride=3), :] = wide[:, 0:128] + shares
    for c in range(1, 3):
        turned[pl.ds(c, 128, stride=3), :] = wide[:, 128 * c : 128 * c + 128]
    for part in range(3):
        span = slice(128 * part, 128 * part + 128)
        back = turned[span, :].T
        for component in range(3):
            for layer in range(6):
                at = stack_row(0, component, layer, 0)
                out[component, layer, :, span] = back[at : at + 3, :]
    back = wide[:, 0:128].T
    for component in range(3):
        for x in range(2):
            at = 54 + 2 * component + x
            coarse_out[component, x] = back[at : at + 1, :]


def cofactor_rows(deform):
    return [
        [
            deform[(row_at + 1) % 3][(column + 1) % 3] * deform[(row_at + 2) % 3][(column + 2) % 3]
            - deform[(row_at + 1) % 3][(column + 2) % 3]
            * deform[(row_at + 2) % 3][(column + 1) % 3]
            for column in range(3)
        ]
        for row_at in range(3)
    ]


def point_stress(deform):
    cofactors = cofactor_rows(deform)
    jacobian = (
        deform[0][0] * cofactors[0][0]
        + deform[0][1] * cofactors[0][1]
        + deform[0][2] * cofactors[0][2]
    )
    pressure = lame_ratio * (jacobian - rest_ratio)
    return [
        [deform[i][d] + pressure * cofactors[i][d] for d in range(3)] for i in range(3)
    ]


coarse_samples = [0.5 - 0.5 / math.sqrt(3.0), 0.5 + 0.5 / math.sqrt(3.0)]
two = range(2)


def at_points(low, high):
    change = high - low
    return [low + s * change for s in coarse_samples], change * (1.0 / element_span)


def ends_of(first, second):
    high = coarse_samples[0] * first + coarse_samples[1] * second
    return [first + second - high, high]


def high_low(values):
    high = values.astype(jnp.bfloat16)
    return high, (values - high.astype(jnp.float32)).astype(jnp.bfloat16)


def reads(pairs):
    return set(range(pairs[0], pairs[-1] + 2))


def plan_steps(spans):
    plan = []
    for first, count in spans:
        pairs = list(range(first, first + count))
        plan.append([pairs[n : n + 2] for n in range(0, count, 2)])
    return plan


class Slab:
    def __init__(self, width, across):
        self.width = width
        self.y_step = 2 * across
        lane = lax.broadcasted_iota(jnp.int32, (8, width), 1)
        x = (lane // 2) % across
        self.bottom, self.top, self.even = x == 0, x == across - 1, lane % 2 == 0
        self.row = lax.broadcasted_iota(jnp.int32, (8, width), 0)
        row = lax.broadcasted_iota(jnp.int32, (32, width), 0)
        lane = lax.broadcasted_iota(jnp.int32, (32, width), 1)
        on_face = (row == 0) | ((row >= 3) & (row <= 11))
        self.keep = jnp.where(on_face & ((lane // 2) % across == 0), 0.0, 1.0)

    def lanes(self, v, step):
        return pltpu.roll(v, step % self.width, 1)

    def from_next(self, v, x, y):
        if x or y:
            v = self.lanes(v, -2 * x - self.y_step * y)
        return jnp.where(self.top, 0.0, v) if x else v

    def from_next_z(self, v, ahead, x, y):
        step = -2 * x - self.y_step * y
        v = jnp.where(self.even, self.lanes(v, step - 1), self.lanes(ahead, step + 1))
        return jnp.where(self.top, 0.0, v) if x else v

    def onto_next(self, v, x, y, z=0):
        if x or y or z:
            v = self.lanes(v, 2 * x + self.y_step * y + z)
        return jnp.where(self.bottom, 0.0, v) if x else v

    def gather(self, component, here, ahead):
        row = self.row
        g0, g1, g2, g3 = here[0:8], here[8:16], here[16:24], here[24:32]
        a0 = ahead[0:8]
        z0, xz = self.from_next_z(g0, a0, 0, 0), self.from_next_z(g0, a0, 1, 0)
        yz, xyz = self.from_next_z(g0, a0, 0, 1), self.from_next_z(g0, a0, 1, 1)
        z2 = self.from_next_z(g2, ahead[16:24], 0, 0)
        edges = jnp.where(row <= 4, xz, self.from_next(g0, 1, 1))
        edges = jnp.where(row == 0, xyz, jnp.where(row <= 2, yz, edges))
        return jnp.concatenate(
            [
                g0,
                g1,
                g2,
                jnp.where(row < 4, z2, g3),
                self.from_next(g0, 1, 0),
                jnp.where(row == 7, yz, self.from_next(g0, 0, 1)),
                jnp.where(row == 7, xz, z0),
                jnp.where(row < 4, self.from_next(g1, 1, 0), self.from_next(g1, 0, 1)),
                edges,
                jnp.where(row == component, 1.0, 0.0),
            ],
            0,
        )

    def scatter(self, part, behind):
        row = self.row
        g0, g1, g2, g3, x0, y0, z0, sides, edges = (part[8 * n : 8 * n + 8] for n in range(9))
        last = row == 7
        for_z = jnp.where(last, 0.0, z0)
        for_xz = jnp.where(last, z0, jnp.where((row == 3) | (row == 4), edges, 0.0))
        for_yz = jnp.where(last, y0, jnp.where((row == 1) | (row == 2), edges, 0.0))
        for_xyz = jnp.where(row == 0, edges, 0.0)
        for_xy = jnp.where(row >= 5, edges, 0.0)

        def above(z):
            return (
                self.onto_next(for_z, 0, 0, z)
                + self.onto_next(for_yz, 0, 1, z)
                + self.onto_next(for_xz, 1, 0, z)
                + self.onto_next(for_xyz, 1, 1, z)
            )

        own0 = g0 + self.onto_next(x0, 1, 0) + self.onto_next(jnp.where(last, 0.0, y0), 0, 1)
        own0 = own0 + self.onto_next(for_xy, 1, 1)
        own0 = own0 + jnp.where(self.even, behind[0], above(1))
        own1 = g1 + jnp.where(row < 4, self.onto_next(sides, 1, 0), self.onto_next(sides, 0, 1))
        share2 = jnp.where(self.even, behind[1], self.onto_next(g3, 0, 0, 1))
        own2 = g2 + jnp.where(row < 4, share2, 0.0)
        moved = (above(-1), self.onto_next(g3, 0, 0, -1))
        return jnp.concatenate([self.twinned(own0), own1, own2, g3], 0), moved

    def twinned(self, v):
        twins = jnp.where(self.row == 7, pltpu.roll(v, 7, 0), 0.0)
        return v + jnp.where(self.row == 0, pltpu.roll(v, 1, 0), twins)

    def absorb(self, total, behind):
        low = self.twinned(jnp.where(self.even, behind[0], 0.0))
        high = jnp.where(self.even & (self.row < 4), behind[1], 0.0)
        return jnp.concatenate(
            [total[0:8] + low, total[8:16], total[16:24] + high, total[24:32]], 0
        )

    def gradient(self, u, spread, pairs):
        def block(i, pair):
            if isinstance(pair, tuple):
                halves_of = [block(i, each) for each in pair]
                lane = lax.broadcasted_iota(jnp.int32, halves_of[0].shape, 1)
                return jnp.where(lane % 2 == 0, *halves_of)
            return self.gather(i, u[i, pair], u[i, pair + 1])

        parts = [high_low(block(i, pair)) for i in range(3) for pair in pairs]
        return jnp.dot(
            spread[0:POINT_ROWS, :],
            jnp.concatenate([jnp.concatenate([h, l, h], 0) for h, l in parts], 1),
            preferred_element_type=jnp.float32,
        )

    def stresses(self, gradient, count):
        width = self.width
        rows = 16
        high, low = {}, {}
        for q in range(count):
            for r in range(64 // rows):
                deform = [
                    [
                        gradient[
                            64 * e + rows * r : 64 * e + rows * (r + 1),
                            width * (count * i + q) : width * (count * i + q + 1),
                        ]
                        for e in range(3)
                    ]
                    for i in range(3)
                ]
                stress = point_stress(deform)
                for i in range(3):
                    for e in range(3):
                        high[e, r, i, q], low[e, r, i, q] = high_low(stress[i][e])

        def whole(part):
            return jnp.concatenate(
                [
                    jnp.concatenate([part[e, r, i, q] for i in range(3) for q in range(count)], 1)
                    for e in range(3)
                    for r in range(64 // rows)
                ],
                0,
            )

        return whole(high), whole(low)

    def force(self, gradient, stiff, collect, pairs, first=0, rows=ROWS):
        high, low = self.stresses(gradient, len(pairs))
        both = collect[first : first + 2 * rows, :]
        force = jnp.dot(both, high, preferred_element_type=jnp.float32)
        force = force[0:rows] + (
            force[rows:] + jnp.dot(both[0:rows], low, preferred_element_type=jnp.float32)
        )
        stiffness = []
        for pair in pairs:
            if isinstance(pair, tuple):
                rows = [stiff[each : each + 1, :] for each in pair]
                stiffness.append(jnp.where(self.even[0:1], *rows))
            else:
                stiffness.append(stiff[pair : pair + 1, :])
        return force * jnp.concatenate(stiffness * 3, 1)

    def run(self, u, stiff, spread, collect, jobs, given=None):
        plan = plan_steps([job[:2] for job in jobs])
        steps = [(pairs, n) for n, chunks in enumerate(plan) for pairs in chunks]
        none = jnp.zeros((8, self.width), jnp.float32)
        ahead, carry, job = None, None, None
        for at, (pairs, n) in enumerate(steps):
            ready = given is not None and n == 0 and pairs == given[0]
            gradient = ahead
            if ahead is None and not ready:
                gradient = self.gradient(u, spread, pairs)
            if not ready:
                ahead = None
            if ahead is None and at + 1 < len(steps):
                later, later_job = steps[at + 1]
                if given is not None and later_job == 0 and later == given[0]:
                    later, later_job = steps[at + 2]
                if later_job == n or not reads(later) & set(pairs):
                    ahead = self.gradient(u, spread, later)
            if job != n:
                carry, job = [(none, none) for i in range(3)], n
            if ready:
                for q, pair in enumerate(pairs):
                    total = given[1][q]
                    if q == 0:
                        total = [self.absorb(total[i], carry[i]) for i in range(3)]
                    jobs[n][2](pair, total)
                carry = list(given[2])
                continue
            force = self.force(gradient, stiff, collect, pairs)
            totals = [[] for pair in pairs]
            for q in range(len(pairs)):
                for i in range(3):
                    lane = (len(pairs) * i + q) * self.width
                    total, carry[i] = self.scatter(force[:, lane : lane + self.width], carry[i])
                    totals[q].append(total)
            for pair, total in zip(pairs, totals):
                jobs[n][2](pair, total)
        return carry

    def smoothing(self, u, f, f_shift, d, spans, bound):
        jobs = []
        for (first, count), (held, added) in zip(spans, chebyshev_steps()):

            def finish(pair, forces, held=held, added=added):
                for i in range(3):
                    z = (added / bound) * self.keep * (f[i, pair + f_shift] - forces[i])
                    move = held * d[i, pair] + z if held else z
                    d[i, pair] = move
                    u[i, pair] = u[i, pair] + move

            jobs.append((first, count, finish))
        return jobs

    def owed(self, carry, bound):
        scale = -chebyshev_steps()[-1][1] / bound
        return [
            (
                scale * jnp.where(self.even, low, 0.0) * self.keep[0:8],
                scale * jnp.where(self.even, high, 0.0) * self.keep[16:24],
            )
            for low, high in carry
        ]

    def corners_of(self, v):
        ahead = pltpu.roll(v, 7, 0)
        found = {}
        for a in range(2):
            for b in range(2):
                found[a, b, 0] = self.from_next(v, a, b)
                found[a, b, 1] = self.from_next_z(v, ahead, a, b)
        return found

    def assemble(self, part):
        here, odd, even = 0.0, 0.0, 0.0
        for a in range(2):
            for b in range(2):
                here = here + self.onto_next(part[a, b, 0], a, b)
                odd = odd + self.onto_next(part[a, b, 1], a, b, 1)
                even = even + self.onto_next(part[a, b, 1], a, b, -1)
        return here + jnp.where(self.even, pltpu.roll(even, 1, 0), odd)

    def coarse_force(self, values, stiffness):
        grads = []
        for i in range(3):
            v = self.corners_of(values[i])
            vz, sz = {}, {}
            for a in two:
                for b in two:
                    vz[a, b], sz[a, b] = at_points(v[a, b, 0], v[a, b, 1])
            vv, vs, sv = {}, {}, {}
            for a in two:
                for k in two:
                    vv[a, k], vs[a, k] = at_points(vz[a, 0][k], vz[a, 1][k])
                sv[a], unused = at_points(sz[a, 0], sz[a, 1])
            dx, dy, dz = {}, {}, {}
            for k in two:
                for j in two:
                    dx[j, k] = (vv[1, k][j] - vv[0, k][j]) * (1.0 / element_span)
                line, unused = at_points(vs[0, k], vs[1, k])
                for h in two:
                    dy[h, k] = line[h]
            for j in two:
                line, unused = at_points(sv[0][j], sv[1][j])
                for h in two:
                    dz[h, j] = line[h]
            grads.append((dx, dy, dz))
        weight = element_span**2 / 8.0
        scaled = weight * stiffness
        sums = [({}, {}, {}) for i in range(3)]

        def add(table, key, value):
            table[key] = table[key] + value if key in table else value

        for h in two:
            for j in two:
                for k in two:
                    deform = [
                        [grads[i][0][j, k], grads[i][1][h, k], grads[i][2][h, j]]
                        for i in range(3)
                    ]
                    for i in range(3):
                        deform[i][i] = deform[i][i] + 1.0
                    stress = point_stress(deform)
                    for i in range(3):
                        add(sums[i][0], (j, k), stress[i][0])
                        add(sums[i][1], (h, k), stress[i][1])
                        add(sums[i][2], (h, j), stress[i][2])

        forces = []
        for i in range(3):
            part = {}
            qx, qy, qz = sums[i]
            along_z = [ends_of(qx[j, 0], qx[j, 1]) for j in two]
            for c in two:
                line = ends_of(along_z[0][c], along_z[1][c])
                for b in two:
                    part[0, b, c] = -line[b]
                    part[1, b, c] = line[b]
            along_z = [ends_of(qy[h, 0], qy[h, 1]) for h in two]
            for c in two:
                line = ends_of(along_z[0][c], along_z[1][c])
                for a in two:
                    part[a, 0, c] = part[a, 0, c] - line[a]
                    part[a, 1, c] = part[a, 1, c] + line[a]
            along_y = [ends_of(qz[h, 0], qz[h, 1]) for h in two]
            for b in two:
                line = ends_of(along_y[0][b], along_y[1][b])
                for a in two:
                    part[a, b, 0] = part[a, b, 0] - line[a]
                    part[a, b, 1] = part[a, b, 1] + line[a]
            forces.append(self.assemble({key: scaled * value for key, value in part.items()}))
        return forces


def window_pair(slab, first_layer, own_layers, fetch):
    found = []
    for parity in range(2):
        layer = first_layer + parity
        device = layer // own_layers
        layer = layer - device * own_layers
        found.append((device, layer // 2, layer % 2))
    values = [fetch(device, q) for device, q, parity in found]
    if found[0][:2] == found[1][:2] or (values[0] is None and values[1] is None):
        return values[0]
    for parity in range(2):
        if values[parity] is None:
            values[parity] = jnp.zeros_like(values[1 - parity])
        elif found[parity][2] != parity:
            values[parity] = slab.lanes(values[parity], 2 * parity - 1)
    lane = lax.broadcasted_iota(jnp.int32, values[0].shape, 1)
    return jnp.where(lane % 2 == 0, values[0], values[1])


def first_sources(own_layers):
    return list(range(-BEFORE // own_layers, (own_layers + BEFORE - 1) // own_layers + 1))


def whole_pairs(own_layers):
    return own_layers == 4


def turn_rows(block, mixed, turned, width, at):
    for tile in range(SENT // 128):
        n = at * (SENT // 128) + tile
        for m in range(width // 4):
            first = 12 * m + 4 * tile
            mixed[n, 4 * m : 4 * m + 4, :] = block[first : first + 4, :]
        turned[at, 128 * tile : 128 * tile + 128, :] = mixed[n].T


def regroup(slab, field, rows):
    values, hard = [], None
    for i in range(3):
        parts = [rows(24 * i + 8 * n) for n in range(3)]
        if field == 0 and i == 0:
            hard = parts[0][TWIN : TWIN + 1]
        parts[0] = jnp.where(slab.row == TWIN, pltpu.roll(parts[0], TWIN, 0), parts[0])
        parts.append(jnp.where(slab.row < 4, 0.0, rows(68 + 4 * i)))
        whole = jnp.concatenate(parts, 0)
        values.append(whole * slab.keep if field == 0 else whole)
    return values, hard


def layer_above(slab, turned, at, i):
    first = NEXT_COLUMN + 12 * i
    low, high = turned[at, first : first + 8, :], turned[at, first + 4 : first + 12, :]
    high = jnp.where(slab.row < 4, pltpu.roll(high, 4, 0), 0.0)
    low = jnp.where(slab.row == TWIN, pltpu.roll(low, TWIN, 0), low)
    nothing = jnp.zeros_like(low)
    return jnp.concatenate([low, nothing, high, nothing], 0) * slab.keep


def make_own_kernel(width, across, own_layers):
    own_pairs = own_layers // 2
    pairs = list(range(own_pairs))

    def own_kernel(block, spread, collect, u, f, stiff, forces, moved, mixed, turned):
        slab = Slab(width, across)
        turn_rows(block, mixed, turned, width, 0)
        for pair in pairs:
            for field, target in enumerate((u, f)):

                def rows(start, field=field, pair=pair):
                    at = BLOCK * (2 * pair + field) + start
                    return turned[0, at : at + 8, :]

                values, hard = regroup(slab, field, rows)
                for i in range(3):
                    target[i, pair] = values[i]
                if field == 0:
                    stiff[pair : pair + 1, :] = hard
        for i in range(3):
            u[i, own_pairs] = layer_above(slab, turned, 0, i)

        def finish(pair, total):
            for i in range(3):
                forces[i, pair] = total[i]

        carry = slab.run(u, stiff, spread, collect, [(0, own_pairs, finish)])
        for i in range(3):
            moved[i, 0] = carry[i][0]
            moved[i, 1] = carry[i][1]

    return own_kernel


def make_first_kernel(width, across, own_layers, fine_bound):
    own = BEFORE // 2
    own_pairs = (own_layers + 1) // 2
    spans = []
    prepared = whole_pairs(own_layers)
    for n in (4, 3, 2, 1):
        low, high = BEFORE - n, BEFORE + own_layers + n - 1 + prepared
        spans.append((low // 2, (high + 1) // 2 - low // 2))
    sources = [n for n in first_sources(own_layers) if n or not prepared]

    def first_kernel(*refs):
        arrived = refs[: len(sources)]
        refs = refs[len(sources) :]
        if prepared:
            own_u, own_f, own_stiff, own_forces, own_moved = refs[:5]
            refs = refs[5:]
        spread, collect, message, *sent, f = refs[:-6]
        u, d, stiff, shares, mixed, turned = refs[-6:]
        slab = Slab(width, across)
        if not prepared:
            u[...] = jnp.zeros(u.shape, jnp.float32)
            f[...] = jnp.zeros(f.shape, jnp.float32)
        shares[...] = jnp.zeros(shares.shape, jnp.float32)
        stiff[...] = jnp.zeros(stiff.shape, jnp.float32)
        for n in range(len(sources)):
            turn_rows(arrived[n], mixed, turned, width, n)
        for pair in range(PAIRS):
            if prepared and own <= pair < own + own_pairs:
                for i in range(3):
                    u[i, pair] = own_u[i, pair - own]
                    f[i, pair] = own_f[i, pair - own]
                stiff[pair : pair + 1, :] = own_stiff[pair - own : pair - own + 1, :]
                continue
            for field, target in enumerate((u, f)):

                def rows(start, field=field, pair=pair):
                    def fetch(device, q):
                        if device not in sources:
                            return None
                        at = BLOCK * (2 * q + field) + start
                        return turned[sources.index(device), at : at + 8, :]

                    value = window_pair(slab, 2 * pair - BEFORE, own_layers, fetch)
                    return jnp.zeros((8, width), jnp.float32) if value is None else value

                values, hard = regroup(slab, field, rows)
                for i in range(3):
                    target[i, pair] = values[i]
                if field == 0:
                    stiff[pair : pair + 1, :] = hard
        given = None
        if prepared:
            for i in range(3):
                u[i, PAIRS] = layer_above(slab, turned, sources.index(1), i)
            given = (
                list(range(own, own + own_pairs)),
                [[own_forces[i, q] for i in range(3)] for q in range(own_pairs)],
                [(own_moved[i, 0], own_moved[i, 1]) for i in range(3)],
            )

        first, count = spans[3]
        blocks = [
            high_low(slab.keep * f[i, pair]) for pair in range(first, first + count) for i in range(3)
        ]
        loads = jnp.dot(
            spread[POINT_ROWS:, 0:96],
            jnp.concatenate([jnp.concatenate([h, l, h], 0) for h, l in blocks], 1),
            preferred_element_type=jnp.float32,
        )
        jobs = slab.smoothing(u, f, 0, d, spans[0:3], fine_bound)
        slab.run(u, stiff, spread, collect, jobs, given)
        steps = plan_steps([spans[3]])[0]
        if prepared:
            steps = [list(range(own, own + own_pairs)), [(own + own_pairs, own - 1)]]
        gradients = [slab.gradient(u, spread, pairs) for pairs in steps]
        for pairs, gradient in zip(steps, gradients):
            force = slab.force(gradient, stiff, collect, pairs, 2 * ROWS, 16)
            for q, pair in enumerate(pairs):
                for i in range(3):
                    at = (len(pairs) * i + q) * width
                    part = force[:, at : at + width]
                    part = jnp.where(slab.bottom, part[8:16], part[0:8])
                    owners = {pair: part}
                    if isinstance(pair, tuple):
                        owners = {
                            pair[0]: jnp.where(slab.even, part, 0.0),
                            pair[1]: jnp.where(slab.even, 0.0, part),
                        }
                    for each, share in owners.items():
                        load_at = (3 * (each - first) + i) * width
                        shares[i, each] = loads[0:8, load_at : load_at + width] - share

        restricted = [
            slab.assemble({corner: shares[i, :, n, :] for n, corner in enumerate(CORNERS)})
            for i in range(3)
        ]
        def line(rows, q):
            return rows[own + q : own + q + 1]

        for q in range(own_pairs):
            for i in range(3):
                message[i, q] = u[i, own + q]
                message[i, q, RESTRICTED_SLOT : RESTRICTED_SLOT + 1, :] = line(restricted[i], q)
            message[0, q, STIFF_SLOT : STIFF_SLOT + 1, :] = line(stiff, q)
        if prepared:
            down, up = sent
            for i in range(3):
                down[i, 0:32] = u[i, own]
                down[i, 32:40] = u[i, own + 1, 0:8, :]
                down[i, 40:48] = u[i, own + 1, 16:24, :]
                up[i] = u[i, own + 1]
                for n, row in enumerate(
                    (line(restricted[i], 0), line(restricted[i], 1), u[i, own + 2, 0:1, :])
                    + (line(restricted[i], 2),)
                ):
                    down[i, 24 + n : 25 + n, :] = row
                for n, row in enumerate(
                    (line(restricted[i], 1), line(restricted[i], 0), u[i, own, 0:1, :])
                ):
                    up[i, 24 + n : 25 + n, :] = row
            for q in range(own_pairs):
                down[q, 32 + TWIN : 33 + TWIN, :] = line(stiff, q)
                up[q, TWIN : TWIN + 1, :] = line(stiff, q)
            return
        edge = sent[0]
        for q in range(own_pairs):
            for i in range(3):
                edge[q, i : i + 1, :] = u[i, own + q, 0:1, :]
                edge[q, 3 + i : 4 + i, :] = line(restricted[i], q)
            edge[q, 6:8, :] = jnp.broadcast_to(line(stiff, q), (2, width))

    return first_kernel


def shares_sent(own_layers):
    return own_layers % 2 == 0


def sources_of(own_layers):
    below = 2 if shares_sent(own_layers) else 3
    whole = range(-below // own_layers, (own_layers + 2) // own_layers + 1)
    coarse = range(-(below + 2) // own_layers, (own_layers + 4) // own_layers + 1)
    return list(whole), [n for n in coarse if n not in whole]


def message_line(message, q, n):
    i, slot = ((n, 0), (n - 3, RESTRICTED_SLOT), (0, STIFF_SLOT))[n // 3]
    return message[i, q, slot : slot + 1, :]


def sent_readers(slab, up, message, down):
    def block_of(device, q, i):
        if device == 0:
            return message[i, q]
        if (device, q) == (1, 0):
            whole = down[i, 0:32]
        elif (device, q) == (1, 1):
            low, high = down[i, 32:40], down[i, 40:48]
            low = jnp.where(slab.row == TWIN, pltpu.roll(low, TWIN, 0), low)
            whole = jnp.concatenate([low, jnp.zeros_like(low), high, jnp.zeros_like(low)], 0)
        elif (device, q) == (-1, 1):
            low = up[i, 0:8]
            low = jnp.where(slab.row == TWIN, pltpu.roll(low, TWIN, 0), low)
            whole = jnp.concatenate([low, up[i, 8:32]], 0)
        else:
            return None
        return whole

    def line_of(device, q, n):
        if device == 0:
            return message_line(message, q, n)
        kind, i = n // 3, n % 3
        if device == 1:
            row = ((0, 24), (32, 25))[q][kind] if kind < 2 else 32 + TWIN
            i = i if kind < 2 else q
            return down[i, row : row + 1, :]
        if device == -1:
            row = ((26, 25), (0, 24))[q][kind] if kind < 2 else TWIN
            i = i if kind < 2 else q
            return up[i, row : row + 1, :]
        if (device, q) == (2, 0) and kind < 2:
            return down[i, 26 + kind : 27 + kind, :]
        return None

    return block_of, line_of


def make_second_kernel(width, across, own_layers, fine_bound, coarse_bound):
    own = BEFORE_B // 2
    own_pairs = (own_layers + 1) // 2
    shift = (BEFORE - BEFORE_B) // 2
    whole, outer = sources_of(own_layers)
    steps = chebyshev_steps()
    spans = []
    for n in (3, 2, 1):
        low, high = BEFORE_B - n + shares_sent(own_layers), BEFORE_B + own_layers + n - 1
        spans.append((low // 2, (high + 1) // 2 - low // 2))

    def second_kernel(*refs):
        slab = Slab(width, across)
        if whole_pairs(own_layers):
            up, message, down = refs[:3]
            refs = refs[3:]
            block_of, line_of = sent_readers(slab, up, message, down)
        else:
            messages = dict(zip(whole, refs))
            edges = dict(zip(outer, refs[len(whole) :]))
            refs = refs[len(whole) + len(outer) :]

            def block_of(device, q, i):
                return messages[device][i, q] if device in messages else None

            def line_of(device, q, n):
                if device in messages:
                    return message_line(messages[device], q, n)
                return edges[device][q, n : n + 1, :] if device in edges else None

        f, spread, collect, transfer_back, out, u, d, stiff, coarse = refs

        def pair_of(pair, fetch):
            return window_pair(slab, 2 * pair - BEFORE_B, own_layers, fetch)

        coarse[...] = jnp.zeros(coarse.shape, jnp.float32)
        for pair in range(PAIRS_B):
            for i in range(3):
                block = pair_of(pair, lambda device, q: block_of(device, q, i))
                u[i, pair] = jnp.zeros((32, width), jnp.float32) if block is None else block
            for n in range(7):
                line = pair_of(pair, lambda device, q: line_of(device, q, n))
                if line is not None:
                    coarse[n, pair : pair + 1, :] = line
        stiff[...] = coarse[6]

        stiffness = coarse[6]
        keep_coarse = jnp.where(slab.bottom, 0.0, 1.0)
        start = [coarse[i] for i in range(3)]
        restricted = [coarse[3 + i] for i in range(3)]
        before = slab.coarse_force(start, stiffness)
        move = [(steps[0][1] / coarse_bound) * keep_coarse * restricted[i] for i in range(3)]
        level = [start[i] + move[i] for i in range(3)]
        for held, added in steps[1:]:
            force = slab.coarse_force(level, stiffness)
            for i in range(3):
                z = keep_coarse * (restricted[i] + before[i] - force[i])
                move[i] = held * move[i] + (added / coarse_bound) * z
                level[i] = level[i] + move[i]

        weights = [jnp.broadcast_to(transfer_back[:, n : n + 1], (32, width)) for n in range(8)]
        for i in range(3):
            change = slab.corners_of(level[i] - start[i])
            for pair in range(spans[0][0], min(spans[0][0] + spans[0][1] + 1, PAIRS_B)):
                lift = u[i, pair]
                for n, corner in enumerate(CORNERS):
                    lift = lift + weights[n] * change[corner][pair : pair + 1]
                u[i, pair] = lift

        jobs = slab.smoothing(u, f, shift, d, spans, fine_bound)
        owed = slab.owed(slab.run(u, stiff, spread, collect, jobs), fine_bound)

        lower = lax.broadcasted_iota(jnp.int32, (width // 8, 8, 128), 1) < 4
        nothing = jnp.zeros((8, width), jnp.float32)
        sides = []
        for q in range(2):
            if q or not shares_sent(own_layers):
                owed = [(nothing, nothing)] * 3
            rows = []
            for i in range(3):
                value = u[i, own + q]
                rows += [value[0:24], jnp.where(slab.row < 4, owed[i][1], value[24:32])]
            rows += [owed[i][0] for i in range(3)]
            rows += [level[i][own + q : own + q + 1] for i in range(3)] + [nothing[0:5]]
            sides.append(jnp.concatenate(rows, 0).T.reshape(width // 8, 8, 128))
        out[:, 0] = jnp.where(lower, sides[0], pltpu.roll(sides[1], 4, 1))
        out[:, 1] = jnp.where(lower, pltpu.roll(sides[0], 4, 1), sides[1])

    return second_kernel


def solution(mesh):
    rows_of, columns_of = mesh.shape["gx"], mesh.shape["gy"]
    devices = rows_of * columns_of
    order = ring_order(rows_of, columns_of)
    own_layers = EZ // devices
    own_pairs = (own_layers + 1) // 2
    width = 4 * devices
    across = 2 * rows_of
    near = first_sources(own_layers)
    prepared = whole_pairs(own_layers)
    whole, outer = sources_of(own_layers)
    spread, collect, fine_bound = element_tables()
    coarse_bound = build_tables([0.0, 1.0], 2)[2]
    transfer_back = transfer_table()[1]
    corners, from_loads = corner_tables()
    from_loads = np.pad(from_loads, ((0, 0), (0, spread.shape[1] - from_loads.shape[1])))
    spread = np.concatenate([spread, from_loads], 0)
    collect = np.concatenate([collect, corners], 0)
    wide = pltpu.CompilerParams(vmem_limit_bytes=60 * 1024 * 1024)
    limit = pltpu.CompilerParams(vmem_limit_bytes=48 * 1024 * 1024)
    f32 = jnp.float32

    pack = pl.pallas_call(
        functools.partial(pack_kernel, order),
        out_shape=pltpu.VMEM((devices * 12, 128), f32),
        in_specs=[pl.BlockSpec(memory_space=pl.ANY)] * 5,
        out_specs=pl.BlockSpec(memory_space=pltpu.VMEM),
        scratch_shapes=[
            pltpu.VMEM((3, 6, 3, 384), f32),
            pltpu.VMEM((3, 6, 3, 384), f32),
            pltpu.VMEM((2, 1, EZ), f32),
            pltpu.VMEM((1, 1, 192), jnp.int32),
            pltpu.VMEM((384, 512), jnp.bfloat16),
            pltpu.VMEM((128, 384), f32),
            pltpu.VMEM((384, 128), f32),
            pltpu.VMEM((6, 136, 128), f32),
            pltpu.SemaphoreType.DMA((5,)),
        ],
        compiler_params=wide,
    )
    own = pl.pallas_call(
        make_own_kernel(width, across, own_layers),
        out_shape=(
            jax.ShapeDtypeStruct((3, own_pairs + 1, 32, width), f32),
            jax.ShapeDtypeStruct((3, own_pairs, 32, width), f32),
            jax.ShapeDtypeStruct((own_pairs, width), f32),
            jax.ShapeDtypeStruct((3, own_pairs, 32, width), f32),
            jax.ShapeDtypeStruct((3, 2, 8, width), f32),
        ),
        scratch_shapes=[
            pltpu.VMEM((SENT // 128, width, 128), f32),
            pltpu.VMEM((1, SENT, width), f32),
        ],
        compiler_params=limit,
        cost_estimate=pl.CostEstimate(flops=400_000_000, bytes_accessed=1_000_000, transcendentals=0),
    )
    sent = [jax.ShapeDtypeStruct((own_pairs, 8, width), f32)]
    if prepared:
        sent = [jax.ShapeDtypeStruct((3, rows, width), f32) for rows in (48, 32)]
    first = pl.pallas_call(
        make_first_kernel(width, across, own_layers, fine_bound),
        out_shape=(
            jax.ShapeDtypeStruct((3, own_pairs, 32, width), f32),
            *sent,
            jax.ShapeDtypeStruct((3, PAIRS, 32, width), f32),
        ),
        scratch_shapes=[
            pltpu.VMEM((3, 8, 32, width), f32),
            pltpu.VMEM((3, 8, 32, width), f32),
            pltpu.VMEM((8, width), f32),
            pltpu.VMEM((3, 8, 8, width), f32),
            pltpu.VMEM((len(near) * (SENT // 128), width, 128), f32),
            pltpu.VMEM((len(near), SENT, width), f32),
        ],
        compiler_params=limit,
    )
    second = pl.pallas_call(
        make_second_kernel(width, across, own_layers, fine_bound, coarse_bound),
        out_shape=jax.ShapeDtypeStruct((devices // 2, 2, 8, 128), f32),
        scratch_shapes=[
            pltpu.VMEM((3, PAIRS_B, 32, width), f32),
            pltpu.VMEM((3, PAIRS_B, 32, width), f32),
            pltpu.VMEM((PAIRS_B, width), f32),
            pltpu.VMEM((7, PAIRS_B, width), f32),
        ],
        compiler_params=limit,
    )
    unpack = pl.pallas_call(
        functools.partial(unpack_kernel, order),
        out_shape=(
            jax.ShapeDtypeStruct((3, 6, 3, 384), f32),
            jax.ShapeDtypeStruct((3, 2, 1, EZ), f32),
        ),
        scratch_shapes=[pltpu.VMEM((2, 128, 128), f32), pltpu.VMEM((384, 128), f32)],
        compiler_params=limit,
    )
    everyone = ("gy", "gx")

    def from_device(block, distance):
        place = {k: m % rows_of * columns_of + m // rows_of for m, k in enumerate(order)}
        route = [(place[(k + distance) % devices], place[k]) for k in range(devices)]
        return lax.ppermute(block, ("gx", "gy"), route)

    def body(initial, forcing, modulus, solid_list):
        sent = pack(initial, forcing, modulus, solid_list, jnp.asarray(pack_table()))
        sent = sent.reshape(devices, SENT // 128, 4, 128)
        arrived = lax.all_to_all(sent, everyone, 0, 0, tiled=True).reshape(devices * 12, 128)
        blocks = [from_device(arrived, n) if n else arrived for n in near]
        if prepared:
            blocks = [block for n, block in zip(near, blocks) if n]
            blocks += own(arrived, jnp.asarray(spread), jnp.asarray(collect))
        message, *edges, load = first(
            *blocks,
            jnp.asarray(spread),
            jnp.asarray(collect),
        )
        if prepared:
            down, up = edges
            messages = [from_device(up, -1), message, from_device(down, 1)]
        else:
            messages = [from_device(message, n) if n else message for n in whole]
            messages += [from_device(edges[0], n) for n in outer]
        result = second(
            *messages,
            load,
            jnp.asarray(spread),
            jnp.asarray(collect),
            jnp.asarray(transfer_back),
        )
        back = lax.all_to_all(result.reshape(devices, 8, 128), everyone, 0, 0, tiled=True)
        return unpack(back, jnp.asarray(unpack_table()))

    placed = (
        P(None, "gx", "gy", None),
        P(None, "gx", "gy", None),
        P("gx", "gy", None),
        P("gx", "gy", None),
    )
    return jax.shard_map(
        body,
        mesh=mesh,
        in_specs=placed,
        out_specs=(P(None, "gx", "gy", None), P(None, "gx", "gy", None)),
        check_vma=False,
    )
```

```python
import functools
import math

import jax
import jax.numpy as jnp
import numpy as np
from jax import lax
from jax.experimental import pallas as pl
from jax.experimental.pallas import tpu as pltpu
from jax.sharding import PartitionSpec as P

CHEB = 3
EZ = 128

element_span = 20.0
lame_ratio = 4.0
rest_ratio = 1.25
modulus_top = 2.0
spectrum_floor = 0.05
interval_centre = (1.0 + spectrum_floor) / 2.0
interval_radius = (1.0 - spectrum_floor) / 2.0
interval_ratio = interval_centre / interval_radius
inner_anchors = (0.5 - 0.5 / math.sqrt(5.0), 0.5 + 0.5 / math.sqrt(5.0))

BEFORE = 4
PAIRS = 6
BEFORE_B = 6
PAIRS_B = 8
BLOCK = 84
SENT = 384

SLOTS = [
    (0, 0, 0), (1, 0, 0), (2, 0, 0), (0, 1, 0), (0, 2, 0), (0, 0, 1), (0, 0, 2), None,
    (0, 1, 1), (0, 1, 2), (0, 2, 1), (0, 2, 2), (1, 0, 1), (1, 0, 2), (2, 0, 1), (2, 0, 2),
    (1, 1, 0), (1, 2, 0), (2, 1, 0), (2, 2, 0), (1, 1, 1), (1, 1, 2), (1, 2, 1), (1, 2, 2),
    None, None, None, None, (2, 1, 1), (2, 1, 2), (2, 2, 1), (2, 2, 2),
]
TWIN = 7
NEXT_SLOTS = [0, 1, 2, 3, 4, 5, 6, 7, 16, 17, 18, 19]
NEXT_COLUMN = 4 * BLOCK
RESTRICTED_SLOT = 24
STIFF_SLOT = 25
OWN_SHIFT, SHIFT_X, SHIFT_Y, SHIFT_Z = (0, 0, 0), (1, 0, 0), (0, 1, 0), (0, 0, 1)
ELEMENT_ROWS = (
    [(slot, OWN_SHIFT) for slot in range(24)]
    + [(slot, SHIFT_Z) for slot in range(16, 20)]
    + [(slot, OWN_SHIFT) for slot in range(28, 32)]
    + [(slot, SHIFT_X) for slot in range(7)] + [None]
    + [(slot, SHIFT_Y) for slot in range(7)] + [(0, (0, 1, 1))]
    + [(slot, SHIFT_Z) for slot in range(7)] + [(0, (1, 0, 1))]
    + [(slot, SHIFT_X) for slot in range(8, 12)] + [(slot, SHIFT_Y) for slot in range(12, 16)]
    + [(0, (1, 1, 1)), (1, (0, 1, 1)), (2, (0, 1, 1)), (3, (1, 0, 1)), (4, (1, 0, 1))]
    + [(5, (1, 1, 0)), (6, (1, 1, 0)), (0, (1, 1, 0))]
)
ROWS = len(ELEMENT_ROWS)
DEPTH = 80
POINT_ROWS = 192
CORNERS = [(a, b, c) for a in range(2) for b in range(2) for c in range(2)]


def gauss_rule(point_count):
    if point_count == 2:
        offset = 1.0 / math.sqrt(3.0)
        points = [-offset, offset]
        weights = [1.0, 1.0]
    else:
        inner = math.sqrt(3.0 / 7.0 - 2.0 / 7.0 * math.sqrt(6.0 / 5.0))
        outer = math.sqrt(3.0 / 7.0 + 2.0 / 7.0 * math.sqrt(6.0 / 5.0))
        heavy = (18.0 + math.sqrt(30.0)) / 36.0
        light = (18.0 - math.sqrt(30.0)) / 36.0
        points = [-outer, -inner, inner, outer]
        weights = [light, heavy, heavy, light]
    return (np.array(points), np.array(weights))


def lagrange_tables(anchors, samples):
    values = np.zeros((len(samples), len(anchors)))
    slopes = np.zeros((len(samples), len(anchors)))
    for sample_index, sample in enumerate(samples):
        for anchor_index, anchor in enumerate(anchors):
            others = [
                location
                for location_index, location in enumerate(anchors)
                if location_index != anchor_index
            ]
            product = 1.0
            for location in others:
                product = product * (sample - location) / (anchor - location)
            values[sample_index, anchor_index] = product
            derivative = 0.0
            for skipped in range(len(others)):
                summand = 1.0 / (anchor - others[skipped])
                for kept_index in range(len(others)):
                    if kept_index != skipped:
                        summand = (
                            summand * (sample - others[kept_index]) / (anchor - others[kept_index])
                        )
                derivative = derivative + summand
            slopes[sample_index, anchor_index] = derivative
    return (values, slopes)


def outer_three(first, second, third):
    return (
        first[:, None, None, :, None, None]
        * second[None, :, None, None, :, None]
        * third[None, None, :, None, None, :]
    )


def build_tables(anchors, point_count):
    raw_points, raw_weights = gauss_rule(point_count)
    samples = (raw_points + 1.0) / 2.0
    weights = raw_weights / 2.0
    basis_values, slopes = lagrange_tables(anchors, samples)
    quad_total = point_count**3
    nodal_count = len(anchors) ** 3
    derivative_one = outer_three(slopes, basis_values, basis_values).reshape(
        quad_total, nodal_count
    )
    derivative_two = outer_three(basis_values, slopes, basis_values).reshape(
        quad_total, nodal_count
    )
    derivative_three = outer_three(basis_values, basis_values, slopes).reshape(
        quad_total, nodal_count
    )
    stacked = np.stack([derivative_one, derivative_two, derivative_three]) / element_span
    volume = (weights[:, None, None] * weights[None, :, None] * weights[None, None, :]).reshape(
        -1
    ) * element_span**3
    forward = stacked.reshape(3 * quad_total, nodal_count)
    backward = (stacked * volume[None, :, None]).reshape(3 * quad_total, nodal_count).T
    weighted = stacked * volume[None, :, None]
    laplace = weighted[0].T @ stacked[0] + weighted[1].T @ stacked[1] + weighted[2].T @ stacked[2]
    matrix = np.zeros((nodal_count, 3, nodal_count, 3))
    for first in range(3):
        for second in range(3):
            block = weighted[second].T @ stacked[first] + (lame_ratio - 1.0) * (
                weighted[first].T @ stacked[second]
            )
            if first == second:
                block = block + laplace
            matrix[:, first, :, second] = block
    matrix = matrix.reshape(3 * nodal_count, 3 * nodal_count)
    vector = 1.5 + np.cos(1.3 * np.arange(3 * nodal_count))
    for repeat in range(200):
        vector = matrix @ vector
        vector = vector / np.sqrt(vector @ vector)
    largest = vector @ (matrix @ vector)
    return (forward, backward, float(4.0 * modulus_top * 1.1 * largest))


def row_nodes():
    nodes = []
    for entry in ELEMENT_ROWS:
        slot = SLOTS[entry[0]] if entry else None
        if slot is None or any(s and n for s, n in zip(entry[1], slot)):
            nodes.append(None)
        else:
            a, b, c = (3 * s + n for s, n in zip(entry[1], slot))
            nodes.append(16 * a + 4 * b + c)
    return nodes


def halves(matrix):
    whole = np.asarray(matrix, np.float32)
    high = whole.astype(jnp.bfloat16)
    low = (whole - high.astype(np.float32)).astype(jnp.bfloat16)
    return high, low


def element_tables():
    forward, backward, bound = build_tables([0.0, inner_anchors[0], inner_anchors[1], 1.0], 4)
    spread = np.zeros((forward.shape[0], DEPTH))
    collect = np.zeros((ROWS, backward.shape[1]))
    for row, node in enumerate(row_nodes()):
        if node is not None:
            spread[:, row] = forward[:, node]
            collect[row, :] = backward[node, :]
    for column in range(3):
        spread[64 * column : 64 * column + 64, ROWS + column] = 1.0
    spread_high, spread_low = halves(spread)
    collect_high, collect_low = halves(collect)
    return (
        np.concatenate([spread_high, spread_high, spread_low], 1),
        np.concatenate([collect_high, collect_low], 0),
        bound,
    )


def corner_tables():
    anchors = [0.0, inner_anchors[0], inner_anchors[1], 1.0]
    backward = build_tables(anchors, 4)[1]
    reach = np.stack([1.0 - np.array(anchors), np.array(anchors)])
    weights = outer_three(reach, reach, reach).reshape(8, 64)
    held = np.arange(64) < 16
    from_stress = np.concatenate([weights @ backward, np.where(held, 0.0, weights) @ backward], 0)
    from_loads = np.zeros((16, 32))
    from_loads[:8] = transfer_table()[0].T
    loads_high, loads_low = halves(from_loads)
    return (
        np.concatenate(halves(from_stress), 0),
        np.concatenate([loads_high, loads_high, loads_low], 1),
    )


def transfer_table():
    table = np.zeros((8, 32))
    reach = (0.0, inner_anchors[0], inner_anchors[1])
    for row, corner in enumerate(CORNERS):
        for column, slot in enumerate(SLOTS):
            if slot is not None:
                weight = 1.0
                for side, node in zip(corner, slot):
                    weight = weight * (reach[node] if side else 1.0 - reach[node])
                table[row, column] = weight
    back = table.T.copy()
    back[TWIN] = back[0]
    return table.T.astype(np.float32), back.astype(np.float32)


def chebyshev_steps():
    steps = [(0.0, 1.0 / interval_centre)]
    ratio_now = 1.0 / interval_ratio
    for sweep in range(1, CHEB):
        ratio_next = 1.0 / (2.0 * interval_ratio - ratio_now)
        steps.append((ratio_next * ratio_now, 2.0 * ratio_next / interval_radius))
        ratio_now = ratio_next
    return steps


def stack_row(field, component, layer, b):
    return field * 54 + component * 18 + layer * 3 + b


def block_column(component, slot):
    return 72 + 4 * component + slot - 28 if slot >= 24 else 24 * component + slot


def pack_table():
    table = np.zeros((3, 128, 2, 2, 128), np.float32)
    for field in range(2):
        for x in range(2):
            for component in range(3):
                for column, slot in enumerate(SLOTS):
                    if slot is not None:
                        a, b, c = slot
                        row = stack_row(field, component, 3 * x + a, b)
                        table[c, row, field, x, block_column(component, column)] = 1.0
                        if field == 0 and column in NEXT_SLOTS:
                            at = BLOCK + 12 * component + NEXT_SLOTS.index(column)
                            table[c, row, 1, x, at] = 1.0
            table[0, 108 + x, 0, x, TWIN] = 1.0
    return table.reshape(384, 512).astype(jnp.bfloat16)


def unpack_table():
    table = np.zeros((2, 128, 4, 128), np.float32)
    for x in range(2):
        for component in range(3):
            for column, slot in enumerate(SLOTS):
                if slot is not None:
                    a, b, c = slot
                    row = stack_row(0, component, 3 * x + a, b)
                    table[x, component * 32 + column, c, row] = 1.0
                    if column < 5:
                        table[x, 96 + 8 * component + column, 3, row] = 1.0
                    if column == 0:
                        table[x, 96 + 8 * component + TWIN, 3, row] = 1.0
                    if 16 <= column < 20:
                        table[x, component * 32 + column + 8, 3, row] = 1.0
            table[x, 120 + component, 0, 54 + 2 * component + x] = 1.0
    return table.reshape(256, 512).astype(jnp.bfloat16)


def pick(values, table):
    count = values.shape[0]
    parts = jnp.dot(
        jnp.concatenate(high_low(values), 0), table, preferred_element_type=jnp.float32
    )
    return parts[:count] + parts[count:]


def ring_order(rows_of, columns_of):
    if (rows_of, columns_of) != (4, 8):
        return list(range(rows_of * columns_of))
    order = []
    for z in range(4):
        for x in range(2):
            for y in range(2):
                chip = (z, 7 - z, 15 - z, 8 + z)[2 * x + y]
                order += [2 * chip, 2 * chip + 1]
    return order


def pack_kernel(
    order,
    initial_at, forcing_at, modulus_at, listing_at, table_at, out,
    initial, forcing, modulus, listing, table, rows, turned, places, ready,
):
    own_layers = EZ // len(order)
    sources = (initial_at, forcing_at, listing_at, modulus_at, table_at)
    copies = [
        pltpu.make_async_copy(source, here, ready.at[n])
        for n, (source, here) in enumerate(
            zip(sources, (initial, forcing, listing, modulus, table))
        )
    ]
    for copy in copies:
        copy.start()
    rows[108:128, :] = jnp.zeros((20, 384), jnp.float32)
    copies[2].wait()
    copies[3].wait()
    listed = listing[0].astype(jnp.float32)
    listed = jnp.concatenate([listed, jnp.full((1, 64), 256.0, jnp.float32)], 1)
    listed = jnp.broadcast_to(listed, (128, 256)).T
    lanes = lax.broadcasted_iota(jnp.int32, (256, 128), 1).astype(jnp.float32)
    row_at = lax.broadcasted_iota(jnp.int32, (128, 128), 0)
    stiff = jnp.zeros((128, 128), jnp.float32)
    for x in range(2):
        hit = jnp.max(jnp.where(listed == lanes + 128.0 * x, 1.0, 0.0), axis=0, keepdims=True)
        stiff = jnp.where(row_at == 108 + x, hit * modulus[x], stiff)
    for field, source in enumerate((initial, forcing)):
        copies[field].wait()
        for component in range(3):
            for layer in range(6):
                at = stack_row(field, component, layer, 0)
                rows[at : at + 3, :] = source[component, layer]
    for part in range(3):
        span = slice(128 * part, 128 * part + 128)
        turned[span, :] = rows[:, span].T
    picked = [turned[pl.ds(c, 128, stride=3), :] for c in range(3)]
    picked[0] = picked[0] + stiff.T
    copies[4].wait()
    wide = pick(jnp.concatenate(picked, 1), table[...])
    lane = lax.broadcasted_iota(jnp.int32, (128, 128), 1)
    for x in range(2):
        tiles = [None] * (SENT // 128)
        for n in range(4):
            pair, field = n // 2, n % 2
            moved = wide[:, 128 * (2 * field + x) : 128 * (2 * field + x) + 128]
            first = BLOCK * n
            if pair:
                moved = pltpu.roll(moved, 128 - 2 * pair, 0)
            if first % 128:
                moved = pltpu.roll(moved, first % 128, 1)
            for tile in range(first // 128, (first + BLOCK - 1) // 128 + 1):
                before = tiles[tile]
                if before is None:
                    tiles[tile] = moved
                else:
                    tiles[tile] = jnp.where(lane >= first - 128 * tile, moved, before)
        above = wide[:, 128 * (2 + x) : 128 * (2 + x) + 128]
        above = pltpu.roll(pltpu.roll(above, 128 - own_layers, 0), (NEXT_COLUMN - BLOCK) % 128, 1)
        tiles[-1] = jnp.where(lane >= NEXT_COLUMN % 128, above, tiles[-1])
        for tile in range(SENT // 128):
            places[3 * x + tile, 0:128, :] = tiles[tile]
            places[3 * x + tile, 128:136, :] = jnp.zeros((8, 128), jnp.float32)
    for device, k in enumerate(order):
        for tile in range(SENT // 128):
            for x in range(2):
                at = 12 * device + 4 * tile + 2 * x
                out[at : at + 2, :] = places[
                    3 * x + tile, own_layers * k : own_layers * k + 2, :
                ]


def unpack_kernel(order, arrived, table, out, coarse_out, layers, turned):
    devices = arrived.shape[0]
    own_layers = EZ // devices
    together = min(own_layers, 2)
    for x in range(2):
        for layer in range(0, own_layers, 2):
            row = (layer // 2) * 4 + x * 2
            if order == sorted(order):
                for n in range(together):
                    at = pl.ds(layer + n, devices, stride=own_layers)
                    layers[x, at, :] = arrived[:, row + n, :]
                continue
            for device, k in enumerate(order):
                at = own_layers * k + layer
                layers[x, at : at + together, :] = arrived[device, row : row + together, :]
    wide = pick(jnp.concatenate([layers[0], layers[1]], 1), table[...])
    shares = pltpu.roll(wide[:, 384:512], own_layers, 0)
    turned[pl.ds(0, 128, stride=3), :] = wide[:, 0:128] + shares
    for c in range(1, 3):
        turned[pl.ds(c, 128, stride=3), :] = wide[:, 128 * c : 128 * c + 128]
    for part in range(3):
        span = slice(128 * part, 128 * part + 128)
        back = turned[span, :].T
        for component in range(3):
            for layer in range(6):
                at = stack_row(0, component, layer, 0)
                out[component, layer, :, span] = back[at : at + 3, :]
    back = wide[:, 0:128].T
    for component in range(3):
        for x in range(2):
            at = 54 + 2 * component + x
            coarse_out[component, x] = back[at : at + 1, :]


def cofactor_rows(deform):
    return [
        [
            deform[(row_at + 1) % 3][(column + 1) % 3] * deform[(row_at + 2) % 3][(column + 2) % 3]
            - deform[(row_at + 1) % 3][(column + 2) % 3]
            * deform[(row_at + 2) % 3][(column + 1) % 3]
            for column in range(3)
        ]
        for row_at in range(3)
    ]


def point_stress(deform):
    cofactors = cofactor_rows(deform)
    jacobian = (
        deform[0][0] * cofactors[0][0]
        + deform[0][1] * cofactors[0][1]
        + deform[0][2] * cofactors[0][2]
    )
    pressure = lame_ratio * (jacobian - rest_ratio)
    return [
        [deform[i][d] + pressure * cofactors[i][d] for d in range(3)] for i in range(3)
    ]


coarse_samples = [0.5 - 0.5 / math.sqrt(3.0), 0.5 + 0.5 / math.sqrt(3.0)]
two = range(2)


def at_points(low, high):
    change = high - low
    return [low + s * change for s in coarse_samples], change * (1.0 / element_span)


def ends_of(first, second):
    high = coarse_samples[0] * first + coarse_samples[1] * second
    return [first + second - high, high]


def high_low(values):
    high = values.astype(jnp.bfloat16)
    return high, (values - high.astype(jnp.float32)).astype(jnp.bfloat16)


def reads(pairs):
    return set(range(pairs[0], pairs[-1] + 2))


def plan_steps(spans):
    plan = []
    for first, count in spans:
        pairs = list(range(first, first + count))
        plan.append([pairs[n : n + 2] for n in range(0, count, 2)])
    return plan


class Slab:
    def __init__(self, width, across):
        self.width = width
        self.y_step = 2 * across
        lane = lax.broadcasted_iota(jnp.int32, (8, width), 1)
        x = (lane // 2) % across
        self.bottom, self.top, self.even = x == 0, x == across - 1, lane % 2 == 0
        self.row = lax.broadcasted_iota(jnp.int32, (8, width), 0)
        row = lax.broadcasted_iota(jnp.int32, (32, width), 0)
        lane = lax.broadcasted_iota(jnp.int32, (32, width), 1)
        on_face = (row == 0) | ((row >= 3) & (row <= 11))
        self.keep = jnp.where(on_face & ((lane // 2) % across == 0), 0.0, 1.0)

    def lanes(self, v, step):
        return pltpu.roll(v, step % self.width, 1)

    def from_next(self, v, x, y):
        if x or y:
            v = self.lanes(v, -2 * x - self.y_step * y)
        return jnp.where(self.top, 0.0, v) if x else v

    def from_next_z(self, v, ahead, x, y):
        step = -2 * x - self.y_step * y
        v = jnp.where(self.even, self.lanes(v, step - 1), self.lanes(ahead, step + 1))
        return jnp.where(self.top, 0.0, v) if x else v

    def onto_next(self, v, x, y, z=0):
        if x or y or z:
            v = self.lanes(v, 2 * x + self.y_step * y + z)
        return jnp.where(self.bottom, 0.0, v) if x else v

    def gather(self, component, here, ahead):
        row = self.row
        g0, g1, g2, g3 = here[0:8], here[8:16], here[16:24], here[24:32]
        a0 = ahead[0:8]
        z0, xz = self.from_next_z(g0, a0, 0, 0), self.from_next_z(g0, a0, 1, 0)
        yz, xyz = self.from_next_z(g0, a0, 0, 1), self.from_next_z(g0, a0, 1, 1)
        z2 = self.from_next_z(g2, ahead[16:24], 0, 0)
        edges = jnp.where(row <= 4, xz, self.from_next(g0, 1, 1))
        edges = jnp.where(row == 0, xyz, jnp.where(row <= 2, yz, edges))
        return jnp.concatenate(
            [
                g0,
                g1,
                g2,
                jnp.where(row < 4, z2, g3),
                self.from_next(g0, 1, 0),
                jnp.where(row == 7, yz, self.from_next(g0, 0, 1)),
                jnp.where(row == 7, xz, z0),
                jnp.where(row < 4, self.from_next(g1, 1, 0), self.from_next(g1, 0, 1)),
                edges,
                jnp.where(row == component, 1.0, 0.0),
            ],
            0,
        )

    def scatter(self, part, behind):
        row = self.row
        g0, g1, g2, g3, x0, y0, z0, sides, edges = (part[8 * n : 8 * n + 8] for n in range(9))
        last = row == 7
        for_z = jnp.where(last, 0.0, z0)
        for_xz = jnp.where(last, z0, jnp.where((row == 3) | (row == 4), edges, 0.0))
        for_yz = jnp.where(last, y0, jnp.where((row == 1) | (row == 2), edges, 0.0))
        for_xyz = jnp.where(row == 0, edges, 0.0)
        for_xy = jnp.where(row >= 5, edges, 0.0)

        def above(z):
            return (
                self.onto_next(for_z, 0, 0, z)
                + self.onto_next(for_yz, 0, 1, z)
                + self.onto_next(for_xz, 1, 0, z)
                + self.onto_next(for_xyz, 1, 1, z)
            )

        own0 = g0 + self.onto_next(x0, 1, 0) + self.onto_next(jnp.where(last, 0.0, y0), 0, 1)
        own0 = own0 + self.onto_next(for_xy, 1, 1)
        own0 = own0 + jnp.where(self.even, behind[0], above(1))
        own1 = g1 + jnp.where(row < 4, self.onto_next(sides, 1, 0), self.onto_next(sides, 0, 1))
        share2 = jnp.where(self.even, behind[1], self.onto_next(g3, 0, 0, 1))
        own2 = g2 + jnp.where(row < 4, share2, 0.0)
        moved = (above(-1), self.onto_next(g3, 0, 0, -1))
        return jnp.concatenate([self.twinned(own0), own1, own2, g3], 0), moved

    def twinned(self, v):
        twins = jnp.where(self.row == 7, pltpu.roll(v, 7, 0), 0.0)
        return v + jnp.where(self.row == 0, pltpu.roll(v, 1, 0), twins)

    def absorb(self, total, behind):
        low = self.twinned(jnp.where(self.even, behind[0], 0.0))
        high = jnp.where(self.even & (self.row < 4), behind[1], 0.0)
        return jnp.concatenate(
            [total[0:8] + low, total[8:16], total[16:24] + high, total[24:32]], 0
        )

    def gradient(self, u, spread, pairs):
        def block(i, pair):
            if isinstance(pair, tuple):
                halves_of = [block(i, each) for each in pair]
                lane = lax.broadcasted_iota(jnp.int32, halves_of[0].shape, 1)
                return jnp.where(lane % 2 == 0, *halves_of)
            return self.gather(i, u[i, pair], u[i, pair + 1])

        parts = [high_low(block(i, pair)) for i in range(3) for pair in pairs]
        return jnp.dot(
            spread[0:POINT_ROWS, :],
            jnp.concatenate([jnp.concatenate([h, l, h], 0) for h, l in parts], 1),
            preferred_element_type=jnp.float32,
        )

    def stresses(self, gradient, count):
        width = self.width
        rows = 16
        high, low = {}, {}
        for q in range(count):
            for r in range(64 // rows):
                deform = [
                    [
                        gradient[
                            64 * e + rows * r : 64 * e + rows * (r + 1),
                            width * (count * i + q) : width * (count * i + q + 1),
                        ]
                        for e in range(3)
                    ]
                    for i in range(3)
                ]
                stress = point_stress(deform)
                for i in range(3):
                    for e in range(3):
                        high[e, r, i, q], low[e, r, i, q] = high_low(stress[i][e])

        def whole(part):
            return jnp.concatenate(
                [
                    jnp.concatenate([part[e, r, i, q] for i in range(3) for q in range(count)], 1)
                    for e in range(3)
                    for r in range(64 // rows)
                ],
                0,
            )

        return whole(high), whole(low)

    def force(self, gradient, stiff, collect, pairs, first=0, rows=ROWS):
        high, low = self.stresses(gradient, len(pairs))
        both = collect[first : first + 2 * rows, :]
        force = jnp.dot(both, high, preferred_element_type=jnp.float32)
        force = force[0:rows] + (
            force[rows:] + jnp.dot(both[0:rows], low, preferred_element_type=jnp.float32)
        )
        stiffness = []
        for pair in pairs:
            if isinstance(pair, tuple):
                rows = [stiff[each : each + 1, :] for each in pair]
                stiffness.append(jnp.where(self.even[0:1], *rows))
            else:
                stiffness.append(stiff[pair : pair + 1, :])
        return force * jnp.concatenate(stiffness * 3, 1)

    def run(self, u, stiff, spread, collect, jobs, given=None):
        plan = plan_steps([job[:2] for job in jobs])
        steps = [(pairs, n) for n, chunks in enumerate(plan) for pairs in chunks]
        none = jnp.zeros((8, self.width), jnp.float32)
        ahead, carry, job = None, None, None
        for at, (pairs, n) in enumerate(steps):
            ready = given is not None and n == 0 and pairs == given[0]
            gradient = ahead
            if ahead is None and not ready:
                gradient = self.gradient(u, spread, pairs)
            if not ready:
                ahead = None
            if ahead is None and at + 1 < len(steps):
                later, later_job = steps[at + 1]
                if given is not None and later_job == 0 and later == given[0]:
                    later, later_job = steps[at + 2]
                if later_job == n or not reads(later) & set(pairs):
                    ahead = self.gradient(u, spread, later)
            if job != n:
                carry, job = [(none, none) for i in range(3)], n
            if ready:
                for q, pair in enumerate(pairs):
                    total = given[1][q]
                    if q == 0:
                        total = [self.absorb(total[i], carry[i]) for i in range(3)]
                    jobs[n][2](pair, total)
                carry = list(given[2])
                continue
            force = self.force(gradient, stiff, collect, pairs)
            totals = [[] for pair in pairs]
            for q in range(len(pairs)):
                for i in range(3):
                    lane = (len(pairs) * i + q) * self.width
                    total, carry[i] = self.scatter(force[:, lane : lane + self.width], carry[i])
                    totals[q].append(total)
            for pair, total in zip(pairs, totals):
                jobs[n][2](pair, total)
        return carry

    def smoothing(self, u, f, f_shift, d, spans, bound):
        jobs = []
        for (first, count), (held, added) in zip(spans, chebyshev_steps()):

            def finish(pair, forces, held=held, added=added):
                for i in range(3):
                    z = (added / bound) * self.keep * (f[i, pair + f_shift] - forces[i])
                    move = held * d[i, pair] + z if held else z
                    d[i, pair] = move
                    u[i, pair] = u[i, pair] + move

            jobs.append((first, count, finish))
        return jobs

    def owed(self, carry, bound):
        scale = -chebyshev_steps()[-1][1] / bound
        return [
            (
                scale * jnp.where(self.even, low, 0.0) * self.keep[0:8],
                scale * jnp.where(self.even, high, 0.0) * self.keep[16:24],
            )
            for low, high in carry
        ]

    def corners_of(self, v):
        ahead = pltpu.roll(v, 7, 0)
        found = {}
        for a in range(2):
            for b in range(2):
                found[a, b, 0] = self.from_next(v, a, b)
                found[a, b, 1] = self.from_next_z(v, ahead, a, b)
        return found

    def assemble(self, part):
        here, odd, even = 0.0, 0.0, 0.0
        for a in range(2):
            for b in range(2):
                here = here + self.onto_next(part[a, b, 0], a, b)
                odd = odd + self.onto_next(part[a, b, 1], a, b, 1)
                even = even + self.onto_next(part[a, b, 1], a, b, -1)
        return here + jnp.where(self.even, pltpu.roll(even, 1, 0), odd)

    def coarse_force(self, values, stiffness):
        grads = []
        for i in range(3):
            v = self.corners_of(values[i])
            vz, sz = {}, {}
            for a in two:
                for b in two:
                    vz[a, b], sz[a, b] = at_points(v[a, b, 0], v[a, b, 1])
            vv, vs, sv = {}, {}, {}
            for a in two:
                for k in two:
                    vv[a, k], vs[a, k] = at_points(vz[a, 0][k], vz[a, 1][k])
                sv[a], unused = at_points(sz[a, 0], sz[a, 1])
            dx, dy, dz = {}, {}, {}
            for k in two:
                for j in two:
                    dx[j, k] = (vv[1, k][j] - vv[0, k][j]) * (1.0 / element_span)
                line, unused = at_points(vs[0, k], vs[1, k])
                for h in two:
                    dy[h, k] = line[h]
            for j in two:
                line, unused = at_points(sv[0][j], sv[1][j])
                for h in two:
                    dz[h, j] = line[h]
            grads.append((dx, dy, dz))
        weight = element_span**2 / 8.0
        scaled = weight * stiffness
        sums = [({}, {}, {}) for i in range(3)]

        def add(table, key, value):
            table[key] = table[key] + value if key in table else value

        for h in two:
            for j in two:
                for k in two:
                    deform = [
                        [grads[i][0][j, k], grads[i][1][h, k], grads[i][2][h, j]]
                        for i in range(3)
                    ]
                    for i in range(3):
                        deform[i][i] = deform[i][i] + 1.0
                    stress = point_stress(deform)
                    for i in range(3):
                        add(sums[i][0], (j, k), stress[i][0])
                        add(sums[i][1], (h, k), stress[i][1])
                        add(sums[i][2], (h, j), stress[i][2])

        forces = []
        for i in range(3):
            part = {}
            qx, qy, qz = sums[i]
            along_z = [ends_of(qx[j, 0], qx[j, 1]) for j in two]
            for c in two:
                line = ends_of(along_z[0][c], along_z[1][c])
                for b in two:
                    part[0, b, c] = -line[b]
                    part[1, b, c] = line[b]
            along_z = [ends_of(qy[h, 0], qy[h, 1]) for h in two]
            for c in two:
                line = ends_of(along_z[0][c], along_z[1][c])
                for a in two:
                    part[a, 0, c] = part[a, 0, c] - line[a]
                    part[a, 1, c] = part[a, 1, c] + line[a]
            along_y = [ends_of(qz[h, 0], qz[h, 1]) for h in two]
            for b in two:
                line = ends_of(along_y[0][b], along_y[1][b])
                for a in two:
                    part[a, b, 0] = part[a, b, 0] - line[a]
                    part[a, b, 1] = part[a, b, 1] + line[a]
            forces.append(self.assemble({key: scaled * value for key, value in part.items()}))
        return forces


def window_pair(slab, first_layer, own_layers, fetch):
    found = []
    for parity in range(2):
        layer = first_layer + parity
        device = layer // own_layers
        layer = layer - device * own_layers
        found.append((device, layer // 2, layer % 2))
    values = [fetch(device, q) for device, q, parity in found]
    if found[0][:2] == found[1][:2] or (values[0] is None and values[1] is None):
        return values[0]
    for parity in range(2):
        if values[parity] is None:
            values[parity] = jnp.zeros_like(values[1 - parity])
        elif found[parity][2] != parity:
            values[parity] = slab.lanes(values[parity], 2 * parity - 1)
    lane = lax.broadcasted_iota(jnp.int32, values[0].shape, 1)
    return jnp.where(lane % 2 == 0, values[0], values[1])


def first_sources(own_layers):
    return list(range(-BEFORE // own_layers, (own_layers + BEFORE - 1) // own_layers + 1))


def whole_pairs(own_layers):
    return own_layers == 4


def turn_rows(block, mixed, turned, width, at):
    for tile in range(SENT // 128):
        n = at * (SENT // 128) + tile
        for m in range(width // 4):
            first = 12 * m + 4 * tile
            mixed[n, 4 * m : 4 * m + 4, :] = block[first : first + 4, :]
        turned[at, 128 * tile : 128 * tile + 128, :] = mixed[n].T


def regroup(slab, field, rows):
    values, hard = [], None
    for i in range(3):
        parts = [rows(24 * i + 8 * n) for n in range(3)]
        if field == 0 and i == 0:
            hard = parts[0][TWIN : TWIN + 1]
        parts[0] = jnp.where(slab.row == TWIN, pltpu.roll(parts[0], TWIN, 0), parts[0])
        parts.append(jnp.where(slab.row < 4, 0.0, rows(68 + 4 * i)))
        whole = jnp.concatenate(parts, 0)
        values.append(whole * slab.keep if field == 0 else whole)
    return values, hard


def layer_above(slab, turned, at, i):
    first = NEXT_COLUMN + 12 * i
    low, high = turned[at, first : first + 8, :], turned[at, first + 4 : first + 12, :]
    high = jnp.where(slab.row < 4, pltpu.roll(high, 4, 0), 0.0)
    low = jnp.where(slab.row == TWIN, pltpu.roll(low, TWIN, 0), low)
    nothing = jnp.zeros_like(low)
    return jnp.concatenate([low, nothing, high, nothing], 0) * slab.keep


def make_own_kernel(width, across, own_layers):
    own_pairs = own_layers // 2
    pairs = list(range(own_pairs))

    def own_kernel(block, spread, collect, u, f, stiff, forces, moved, mixed, turned):
        slab = Slab(width, across)
        turn_rows(block, mixed, turned, width, 0)
        for pair in pairs:
            for field, target in enumerate((u, f)):

                def rows(start, field=field, pair=pair):
                    at = BLOCK * (2 * pair + field) + start
                    return turned[0, at : at + 8, :]

                values, hard = regroup(slab, field, rows)
                for i in range(3):
                    target[i, pair] = values[i]
                if field == 0:
                    stiff[pair : pair + 1, :] = hard
        for i in range(3):
            u[i, own_pairs] = layer_above(slab, turned, 0, i)

        def finish(pair, total):
            for i in range(3):
                forces[i, pair] = total[i]

        carry = slab.run(u, stiff, spread, collect, [(0, own_pairs, finish)])
        for i in range(3):
            moved[i, 0] = carry[i][0]
            moved[i, 1] = carry[i][1]

    return own_kernel


def make_first_kernel(width, across, own_layers, fine_bound):
    own = BEFORE // 2
    own_pairs = (own_layers + 1) // 2
    spans = []
    prepared = whole_pairs(own_layers)
    for n in (4, 3, 2, 1):
        low, high = BEFORE - n, BEFORE + own_layers + n - 1 + prepared
        spans.append((low // 2, (high + 1) // 2 - low // 2))
    sources = [n for n in first_sources(own_layers) if n or not prepared]

    def first_kernel(*refs):
        arrived = refs[: len(sources)]
        refs = refs[len(sources) :]
        if prepared:
            own_u, own_f, own_stiff, own_forces, own_moved = refs[:5]
            refs = refs[5:]
        spread, collect, message, *sent, f = refs[:-6]
        u, d, stiff, shares, mixed, turned = refs[-6:]
        slab = Slab(width, across)
        if not prepared:
            u[...] = jnp.zeros(u.shape, jnp.float32)
            f[...] = jnp.zeros(f.shape, jnp.float32)
        shares[...] = jnp.zeros(shares.shape, jnp.float32)
        stiff[...] = jnp.zeros(stiff.shape, jnp.float32)
        for n in range(len(sources)):
            turn_rows(arrived[n], mixed, turned, width, n)
        for pair in range(PAIRS):
            if prepared and own <= pair < own + own_pairs:
                for i in range(3):
                    u[i, pair] = own_u[i, pair - own]
                    f[i, pair] = own_f[i, pair - own]
                stiff[pair : pair + 1, :] = own_stiff[pair - own : pair - own + 1, :]
                continue
            for field, target in enumerate((u, f)):

                def rows(start, field=field, pair=pair):
                    def fetch(device, q):
                        if device not in sources:
                            return None
                        at = BLOCK * (2 * q + field) + start
                        return turned[sources.index(device), at : at + 8, :]

                    value = window_pair(slab, 2 * pair - BEFORE, own_layers, fetch)
                    return jnp.zeros((8, width), jnp.float32) if value is None else value

                values, hard = regroup(slab, field, rows)
                for i in range(3):
                    target[i, pair] = values[i]
                if field == 0:
                    stiff[pair : pair + 1, :] = hard
        given = None
        if prepared:
            for i in range(3):
                u[i, PAIRS] = layer_above(slab, turned, sources.index(1), i)
            given = (
                list(range(own, own + own_pairs)),
                [[own_forces[i, q] for i in range(3)] for q in range(own_pairs)],
                [(own_moved[i, 0], own_moved[i, 1]) for i in range(3)],
            )

        first, count = spans[3]
        blocks = [
            high_low(slab.keep * f[i, pair]) for pair in range(first, first + count) for i in range(3)
        ]
        loads = jnp.dot(
            spread[POINT_ROWS:, 0:96],
            jnp.concatenate([jnp.concatenate([h, l, h], 0) for h, l in blocks], 1),
            preferred_element_type=jnp.float32,
        )
        jobs = slab.smoothing(u, f, 0, d, spans[0:3], fine_bound)
        slab.run(u, stiff, spread, collect, jobs, given)
        steps = plan_steps([spans[3]])[0]
        if prepared:
            steps = [list(range(own, own + own_pairs)), [(own + own_pairs, own - 1)]]
        gradients = [slab.gradient(u, spread, pairs) for pairs in steps]
        for pairs, gradient in zip(steps, gradients):
            force = slab.force(gradient, stiff, collect, pairs, 2 * ROWS, 16)
            for q, pair in enumerate(pairs):
                for i in range(3):
                    at = (len(pairs) * i + q) * width
                    part = force[:, at : at + width]
                    part = jnp.where(slab.bottom, part[8:16], part[0:8])
                    owners = {pair: part}
                    if isinstance(pair, tuple):
                        owners = {
                            pair[0]: jnp.where(slab.even, part, 0.0),
                            pair[1]: jnp.where(slab.even, 0.0, part),
                        }
                    for each, share in owners.items():
                        load_at = (3 * (each - first) + i) * width
                        shares[i, each] = loads[0:8, load_at : load_at + width] - share

        restricted = [
            slab.assemble({corner: shares[i, :, n, :] for n, corner in enumerate(CORNERS)})
            for i in range(3)
        ]
        def line(rows, q):
            return rows[own + q : own + q + 1]

        for q in range(own_pairs):
            for i in range(3):
                message[i, q] = u[i, own + q]
                message[i, q, RESTRICTED_SLOT : RESTRICTED_SLOT + 1, :] = line(restricted[i], q)
            message[0, q, STIFF_SLOT : STIFF_SLOT + 1, :] = line(stiff, q)
        if prepared:
            down, up = sent
            for i in range(3):
                down[i, 0:32] = u[i, own]
                down[i, 32:40] = u[i, own + 1, 0:8, :]
                down[i, 40:48] = u[i, own + 1, 16:24, :]
                up[i] = u[i, own + 1]
                for n, row in enumerate(
                    (line(restricted[i], 0), line(restricted[i], 1), u[i, own + 2, 0:1, :])
                    + (line(restricted[i], 2),)
                ):
                    down[i, 24 + n : 25 + n, :] = row
                for n, row in enumerate(
                    (line(restricted[i], 1), line(restricted[i], 0), u[i, own, 0:1, :])
                ):
                    up[i, 24 + n : 25 + n, :] = row
            for q in range(own_pairs):
                down[q, 32 + TWIN : 33 + TWIN, :] = line(stiff, q)
                up[q, TWIN : TWIN + 1, :] = line(stiff, q)
            return
        edge = sent[0]
        for q in range(own_pairs):
            for i in range(3):
                edge[q, i : i + 1, :] = u[i, own + q, 0:1, :]
                edge[q, 3 + i : 4 + i, :] = line(restricted[i], q)
            edge[q, 6:8, :] = jnp.broadcast_to(line(stiff, q), (2, width))

    return first_kernel


def shares_sent(own_layers):
    return own_layers % 2 == 0


def sources_of(own_layers):
    below = 2 if shares_sent(own_layers) else 3
    whole = range(-below // own_layers, (own_layers + 2) // own_layers + 1)
    coarse = range(-(below + 2) // own_layers, (own_layers + 4) // own_layers + 1)
    return list(whole), [n for n in coarse if n not in whole]


def message_line(message, q, n):
    i, slot = ((n, 0), (n - 3, RESTRICTED_SLOT), (0, STIFF_SLOT))[n // 3]
    return message[i, q, slot : slot + 1, :]


def sent_readers(slab, up, message, down):
    def block_of(device, q, i):
        if device == 0:
            return message[i, q]
        if (device, q) == (1, 0):
            whole = down[i, 0:32]
        elif (device, q) == (1, 1):
            low, high = down[i, 32:40], down[i, 40:48]
            low = jnp.where(slab.row == TWIN, pltpu.roll(low, TWIN, 0), low)
            whole = jnp.concatenate([low, jnp.zeros_like(low), high, jnp.zeros_like(low)], 0)
        elif (device, q) == (-1, 1):
            low = up[i, 0:8]
            low = jnp.where(slab.row == TWIN, pltpu.roll(low, TWIN, 0), low)
            whole = jnp.concatenate([low, up[i, 8:32]], 0)
        else:
            return None
        return whole

    def line_of(device, q, n):
        if device == 0:
            return message_line(message, q, n)
        kind, i = n // 3, n % 3
        if device == 1:
            row = ((0, 24), (32, 25))[q][kind] if kind < 2 else 32 + TWIN
            i = i if kind < 2 else q
            return down[i, row : row + 1, :]
        if device == -1:
            row = ((26, 25), (0, 24))[q][kind] if kind < 2 else TWIN
            i = i if kind < 2 else q
            return up[i, row : row + 1, :]
        if (device, q) == (2, 0) and kind < 2:
            return down[i, 26 + kind : 27 + kind, :]
        return None

    return block_of, line_of


def make_second_kernel(width, across, own_layers, fine_bound, coarse_bound):
    own = BEFORE_B // 2
    own_pairs = (own_layers + 1) // 2
    shift = (BEFORE - BEFORE_B) // 2
    whole, outer = sources_of(own_layers)
    steps = chebyshev_steps()
    spans = []
    for n in (3, 2, 1):
        low, high = BEFORE_B - n + shares_sent(own_layers), BEFORE_B + own_layers + n - 1
        spans.append((low // 2, (high + 1) // 2 - low // 2))

    def second_kernel(*refs):
        slab = Slab(width, across)
        if whole_pairs(own_layers):
            up, message, down = refs[:3]
            refs = refs[3:]
            block_of, line_of = sent_readers(slab, up, message, down)
        else:
            messages = dict(zip(whole, refs))
            edges = dict(zip(outer, refs[len(whole) :]))
            refs = refs[len(whole) + len(outer) :]

            def block_of(device, q, i):
                return messages[device][i, q] if device in messages else None

            def line_of(device, q, n):
                if device in messages:
                    return message_line(messages[device], q, n)
                return edges[device][q, n : n + 1, :] if device in edges else None

        f, spread, collect, transfer_back, out, u, d, stiff, coarse = refs

        def pair_of(pair, fetch):
            return window_pair(slab, 2 * pair - BEFORE_B, own_layers, fetch)

        coarse[...] = jnp.zeros(coarse.shape, jnp.float32)
        for pair in range(PAIRS_B):
            for i in range(3):
                block = pair_of(pair, lambda device, q: block_of(device, q, i))
                u[i, pair] = jnp.zeros((32, width), jnp.float32) if block is None else block
            for n in range(7):
                line = pair_of(pair, lambda device, q: line_of(device, q, n))
                if line is not None:
                    coarse[n, pair : pair + 1, :] = line
        stiff[...] = coarse[6]

        stiffness = coarse[6]
        keep_coarse = jnp.where(slab.bottom, 0.0, 1.0)
        start = [coarse[i] for i in range(3)]
        restricted = [coarse[3 + i] for i in range(3)]
        before = slab.coarse_force(start, stiffness)
        move = [(steps[0][1] / coarse_bound) * keep_coarse * restricted[i] for i in range(3)]
        level = [start[i] + move[i] for i in range(3)]
        for held, added in steps[1:]:
            force = slab.coarse_force(level, stiffness)
            for i in range(3):
                z = keep_coarse * (restricted[i] + before[i] - force[i])
                move[i] = held * move[i] + (added / coarse_bound) * z
                level[i] = level[i] + move[i]

        weights = [jnp.broadcast_to(transfer_back[:, n : n + 1], (32, width)) for n in range(8)]
        for i in range(3):
            change = slab.corners_of(level[i] - start[i])
            for pair in range(spans[0][0], min(spans[0][0] + spans[0][1] + 1, PAIRS_B)):
                lift = u[i, pair]
                for n, corner in enumerate(CORNERS):
                    lift = lift + weights[n] * change[corner][pair : pair + 1]
                u[i, pair] = lift

        jobs = slab.smoothing(u, f, shift, d, spans, fine_bound)
        owed = slab.owed(slab.run(u, stiff, spread, collect, jobs), fine_bound)

        lower = lax.broadcasted_iota(jnp.int32, (width // 8, 8, 128), 1) < 4
        nothing = jnp.zeros((8, width), jnp.float32)
        sides = []
        for q in range(2):
            if q or not shares_sent(own_layers):
                owed = [(nothing, nothing)] * 3
            rows = []
            for i in range(3):
                value = u[i, own + q]
                rows += [value[0:24], jnp.where(slab.row < 4, owed[i][1], value[24:32])]
            rows += [owed[i][0] for i in range(3)]
            rows += [level[i][own + q : own + q + 1] for i in range(3)] + [nothing[0:5]]
            sides.append(jnp.concatenate(rows, 0).T.reshape(width // 8, 8, 128))
        out[:, 0] = jnp.where(lower, sides[0], pltpu.roll(sides[1], 4, 1))
        out[:, 1] = jnp.where(lower, pltpu.roll(sides[0], 4, 1), sides[1])

    return second_kernel


def solution(mesh):
    rows_of, columns_of = mesh.shape["gx"], mesh.shape["gy"]
    devices = rows_of * columns_of
    order = ring_order(rows_of, columns_of)
    own_layers = EZ // devices
    own_pairs = (own_layers + 1) // 2
    width = 4 * devices
    across = 2 * rows_of
    near = first_sources(own_layers)
    prepared = whole_pairs(own_layers)
    whole, outer = sources_of(own_layers)
    spread, collect, fine_bound = element_tables()
    coarse_bound = build_tables([0.0, 1.0], 2)[2]
    transfer_back = transfer_table()[1]
    corners, from_loads = corner_tables()
    from_loads = np.pad(from_loads, ((0, 0), (0, spread.shape[1] - from_loads.shape[1])))
    spread = np.concatenate([spread, from_loads], 0)
    collect = np.concatenate([collect, corners], 0)
    wide = pltpu.CompilerParams(vmem_limit_bytes=60 * 1024 * 1024)
    limit = pltpu.CompilerParams(vmem_limit_bytes=48 * 1024 * 1024)
    f32 = jnp.float32

    pack = pl.pallas_call(
        functools.partial(pack_kernel, order),
        out_shape=pltpu.VMEM((devices * 12, 128), f32),
        in_specs=[pl.BlockSpec(memory_space=pl.ANY)] * 5,
        out_specs=pl.BlockSpec(memory_space=pltpu.VMEM),
        scratch_shapes=[
            pltpu.VMEM((3, 6, 3, 384), f32),
            pltpu.VMEM((3, 6, 3, 384), f32),
            pltpu.VMEM((2, 1, EZ), f32),
            pltpu.VMEM((1, 1, 192), jnp.int32),
            pltpu.VMEM((384, 512), jnp.bfloat16),
            pltpu.VMEM((128, 384), f32),
            pltpu.VMEM((384, 128), f32),
            pltpu.VMEM((6, 136, 128), f32),
            pltpu.SemaphoreType.DMA((5,)),
        ],
        compiler_params=wide,
    )
    own = pl.pallas_call(
        make_own_kernel(width, across, own_layers),
        out_shape=(
            jax.ShapeDtypeStruct((3, own_pairs + 1, 32, width), f32),
            jax.ShapeDtypeStruct((3, own_pairs, 32, width), f32),
            jax.ShapeDtypeStruct((own_pairs, width), f32),
            jax.ShapeDtypeStruct((3, own_pairs, 32, width), f32),
            jax.ShapeDtypeStruct((3, 2, 8, width), f32),
        ),
        scratch_shapes=[
            pltpu.VMEM((SENT // 128, width, 128), f32),
            pltpu.VMEM((1, SENT, width), f32),
        ],
        compiler_params=limit,
        cost_estimate=pl.CostEstimate(flops=400_000_000, bytes_accessed=1_000_000, transcendentals=0),
    )
    sent = [jax.ShapeDtypeStruct((own_pairs, 8, width), f32)]
    if prepared:
        sent = [jax.ShapeDtypeStruct((3, rows, width), f32) for rows in (48, 32)]
    first = pl.pallas_call(
        make_first_kernel(width, across, own_layers, fine_bound),
        out_shape=(
            jax.ShapeDtypeStruct((3, own_pairs, 32, width), f32),
            *sent,
            jax.ShapeDtypeStruct((3, PAIRS, 32, width), f32),
        ),
        scratch_shapes=[
            pltpu.VMEM((3, 8, 32, width), f32),
            pltpu.VMEM((3, 8, 32, width), f32),
            pltpu.VMEM((8, width), f32),
            pltpu.VMEM((3, 8, 8, width), f32),
            pltpu.VMEM((len(near) * (SENT // 128), width, 128), f32),
            pltpu.VMEM((len(near), SENT, width), f32),
        ],
        compiler_params=limit,
    )
    second = pl.pallas_call(
        make_second_kernel(width, across, own_layers, fine_bound, coarse_bound),
        out_shape=jax.ShapeDtypeStruct((devices // 2, 2, 8, 128), f32),
        scratch_shapes=[
            pltpu.VMEM((3, PAIRS_B, 32, width), f32),
            pltpu.VMEM((3, PAIRS_B, 32, width), f32),
            pltpu.VMEM((PAIRS_B, width), f32),
            pltpu.VMEM((7, PAIRS_B, width), f32),
        ],
        compiler_params=limit,
    )
    unpack = pl.pallas_call(
        functools.partial(unpack_kernel, order),
        out_shape=(
            jax.ShapeDtypeStruct((3, 6, 3, 384), f32),
            jax.ShapeDtypeStruct((3, 2, 1, EZ), f32),
        ),
        scratch_shapes=[pltpu.VMEM((2, 128, 128), f32), pltpu.VMEM((384, 128), f32)],
        compiler_params=limit,
    )
    everyone = ("gy", "gx")

    def from_device(block, distance):
        place = {k: m % rows_of * columns_of + m // rows_of for m, k in enumerate(order)}
        route = [(place[(k + distance) % devices], place[k]) for k in range(devices)]
        return lax.ppermute(block, ("gx", "gy"), route)

    def body(initial, forcing, modulus, solid_list):
        sent = pack(initial, forcing, modulus, solid_list, jnp.asarray(pack_table()))
        sent = sent.reshape(devices, SENT // 128, 4, 128)
        arrived = lax.all_to_all(sent, everyone, 0, 0, tiled=True).reshape(devices * 12, 128)
        blocks = [from_device(arrived, n) if n else arrived for n in near]
        if prepared:
            blocks = [block for n, block in zip(near, blocks) if n]
            blocks += own(arrived, jnp.asarray(spread), jnp.asarray(collect))
        message, *edges, load = first(
            *blocks,
            jnp.asarray(spread),
            jnp.asarray(collect),
        )
        if prepared:
            down, up = edges
            messages = [from_device(up, -1), message, from_device(down, 1)]
        else:
            messages = [from_device(message, n) if n else message for n in whole]
            messages += [from_device(edges[0], n) for n in outer]
        result = second(
            *messages,
            load,
            jnp.asarray(spread),
            jnp.asarray(collect),
            jnp.asarray(transfer_back),
        )
        back = lax.all_to_all(result.reshape(devices, 8, 128), everyone, 0, 0, tiled=True)
        return unpack(back, jnp.asarray(unpack_table()))

    placed = (
        P(None, "gx", "gy", None),
        P(None, "gx", "gy", None),
        P("gx", "gy", None),
        P("gx", "gy", None),
    )
    return jax.shard_map(
        body,
        mesh=mesh,
        in_specs=placed,
        out_specs=(P(None, "gx", "gy", None), P(None, "gx", "gy", None)),
        check_vma=False,
    )
```
